32 devices in a mesh: section: 2 (over core), seq: 4 (over z), head: 4 (over y, x).
Axes of the slice: x: 2, y: 2, z: 4, core: 2. Of those that a mesh axis runs over, the one named last changes fastest.
Arguments:
- tokens: bfloat16 [4, 1024, 1024], P(None, 'seq'), may hold values from -6 to 6
- slot_order: int32 [4], replicated, may hold values from 0 to 3, each once
- log_decay: float32 [2, 4, 32, 1024], P('section', None, 'head', 'seq'), may hold values from -0.6 to 0, as said below
- grad_out: bfloat16 [4, 1024, 1024], P(None, 'seq'), may hold values from -6 to 6
- in_gain: float32 [2, 1024], P('section'), may hold values from 0.1 to 1.9
- w_gate: bfloat16 [2, 1024, 2048], P('section', None, 'head'), may hold values from -0.1875 to 0.1875
- w_inner: bfloat16 [2, 1024, 2048], P('section', None, 'head'), may hold values from -0.1875 to 0.1875
- w_shared: bfloat16 [2, 1024, 256], P('section'), may hold values from -0.1875 to 0.1875
- conv_inner: float32 [2, 4, 2048], P('section', None, 'head'), may hold values from -3 to 3
- conv_shared: float32 [2, 4, 256], P('section'), may hold values from -3 to 3
- d_skip: float32 [2, 32], P('section', 'head'), may hold values from 0.1 to 1
- norm_gain: float32 [2, 2048], P('section', 'head'), may hold values from 0.1 to 1.9
- w_out: bfloat16 [2, 2048, 1024], P('section'), may hold values from -0.125 to 0.125
Outputs:
- section_out: float32 [2, 4, 1024, 1024], P('section', None, 'seq', 'head')
- input_grad: float32 [2, 4, 1024, 1024], P('section', None, 'seq', 'head')
- grad_in_gain: float32 [2, 1024], P('section', ('seq', 'head'))
- grad_w_gate: float32 [2, 1024, 2048], P('section', 'seq', 'head')
- grad_w_inner: float32 [2, 1024, 2048], P('section', 'seq', 'head')
- grad_w_shared: float32 [2, 1024, 256], P('section', ('seq', 'head'))
- grad_conv_inner: float32 [2, 4, 2048], P('section', None, 'head')
- grad_conv_shared: float32 [2, 4, 256], P('section', None, ('seq', 'head'))
- grad_d_skip: float32 [2, 32], P('section', 'head')
- grad_norm_gain: float32 [2, 2048], P('section', 'head')
- grad_w_out: float32 [2, 2048, 1024], P('section', 'head', 'seq')
The draws below stay inside these ranges and needn't reach their ends.
Inputs may be any that keep to these rules, and one draw needn't show every extreme that they name: `log_decay`: every value is below zero. `slot_order`: names every micro-batch once.
All inputs are finite; a program needn't handle non-finite values.
Results may differ from the reference program's by a relative error of at most 0.03.
Values may be sent and summed in bfloat16 or wider, within the bound.
No kernel may reach another device: no remote copies, remote signals or barrier semaphores. Data moves between devices by JAX's collectives and lax.ppermute only.
A program may use at most 128 MiB of HBM per device.

```python
import math
import jax
import jax.numpy as jnp
from jax import lax

D = 1024
STATE_HEADS = 32
STATE = 128
CONV = 4
BLOCK = 256
MICRO_BATCHES = 4
TOK_DEV = 256
INNER = 2048
SEQUENCE_LENGTH = 1024
LAYER_TOTAL = 2


def draw_log_decay(key, part):
    key = jax.random.fold_in(key, 7)
    random_keys = jax.random.split(key, 7)
    fast_share = 0.5
    head_draw = jax.random.uniform(random_keys[0], (LAYER_TOTAL, 1, STATE_HEADS, 1))
    fast_rate = jnp.exp(jax.random.uniform(random_keys[1], (LAYER_TOTAL, 1, STATE_HEADS, 1), minval=jnp.log(1.0 / 50.0), maxval=jnp.log(1.0 / 30.0)))
    slow_rate = jnp.exp(jax.random.uniform(random_keys[2], (LAYER_TOTAL, 1, STATE_HEADS, 1), minval=jnp.log(0.2), maxval=jnp.log(0.5))) / SEQUENCE_LENGTH
    baseline_rate = jnp.where(head_draw < fast_share, fast_rate, slow_rate)
    span_count = SEQUENCE_LENGTH // TOK_DEV
    extent_factor = jnp.exp(jax.random.uniform(random_keys[3], (LAYER_TOTAL, MICRO_BATCHES, STATE_HEADS, span_count, 1), minval=jnp.log(0.5), maxval=jnp.log(1.5)))
    extent_factor = jnp.broadcast_to(extent_factor, (LAYER_TOTAL, MICRO_BATCHES, STATE_HEADS, span_count, TOK_DEV)).reshape(LAYER_TOTAL, MICRO_BATCHES, STATE_HEADS, SEQUENCE_LENGTH)
    random_wobble = jax.random.uniform(random_keys[4], (LAYER_TOTAL, MICRO_BATCHES, STATE_HEADS, SEQUENCE_LENGTH), minval=0.5, maxval=1.5)
    surge_position = jax.random.randint(random_keys[5], (LAYER_TOTAL, MICRO_BATCHES, 1, 3, 1), 0, SEQUENCE_LENGTH)
    surge_depth = jax.random.uniform(random_keys[6], (LAYER_TOTAL, MICRO_BATCHES, STATE_HEADS, 3, 1), minval=0.22, maxval=0.51)
    placement_list = jnp.arange(SEQUENCE_LENGTH)[None, None, None, None, :]
    surge_list = jnp.sum(jnp.where(placement_list == surge_position, surge_depth, 0.0), axis=3)
    return -(baseline_rate * extent_factor * random_wobble + surge_list)


def block_levels(own_key, extent, shards, low, largest):
    factor_of = 1.0
    for axis_at, blocks in shards:
        draws = jax.random.uniform(jax.random.fold_in(jax.random.fold_in(own_key, 6), axis_at), (blocks,), jnp.float32, low / len(shards), largest / len(shards))
        factor_of = factor_of * jnp.repeat(jnp.exp(draws), extent[axis_at] // blocks).reshape((-1,) + (1,) * (len(extent) - 1 - axis_at))
    return factor_of


def gaussian(rng, extent, scale, limit, pieces=(), dtype=jnp.bfloat16):
    drawn = scale * jax.random.normal(rng, extent, jnp.float32)
    if pieces:
        drawn = drawn * block_levels(rng, extent, pieces, -0.22, 0.18)
    return jnp.clip(drawn, -limit, limit).astype(dtype)


def setup_inputs(seed: int = 0) -> dict:
    splits = jax.random.split(jax.random.key(seed), 14)
    tokens = gaussian(splits[0], (MICRO_BATCHES, SEQUENCE_LENGTH, D), 1.0, 6.0, ((1, 4),))
    slot_order = jax.random.permutation(splits[1], MICRO_BATCHES).astype(jnp.int32)
    log_decay = draw_log_decay(jax.random.fold_in(splits[13], 71), 0)
    grad_out = gaussian(splits[3], (MICRO_BATCHES, SEQUENCE_LENGTH, D), 1.0, 6.0, ((1, 4),))
    in_gain = jnp.clip(1.0 + 0.18 * jax.random.normal(splits[4], (LAYER_TOTAL, D), jnp.float32), 0.1, 1.9)
    w_gate = gaussian(splits[5], (LAYER_TOTAL, D, INNER), D ** -0.5, 0.1875, ((0, 2), (2, 4)))
    w_inner = gaussian(splits[6], (LAYER_TOTAL, D, INNER), D ** -0.5, 0.1875, ((0, 2), (2, 4)))
    w_shared = gaussian(splits[7], (LAYER_TOTAL, D, 2 * STATE), D ** -0.5, 0.1875, ((0, 2),))
    conv_inner = gaussian(splits[8], (LAYER_TOTAL, CONV, INNER), CONV ** -0.5, 3.0, ((0, 2), (2, 4)), jnp.float32)
    conv_shared = gaussian(splits[9], (LAYER_TOTAL, CONV, 2 * STATE), CONV ** -0.5, 3.0, ((0, 2),), jnp.float32)
    d_skip = jnp.clip(jnp.exp(math.log(1.0) - 2.3025851 * jax.random.uniform(splits[10], (LAYER_TOTAL, STATE_HEADS), jnp.float32) ** block_levels(splits[10], (LAYER_TOTAL, STATE_HEADS), ((0, 2), (1, 4)), -0.2, 0.2)), 0.1, 1.0)
    norm_gain = jnp.clip(1.0 + 0.18 * jax.random.normal(splits[11], (LAYER_TOTAL, INNER), jnp.float32), 0.1, 1.9)
    w_out = gaussian(splits[12], (LAYER_TOTAL, INNER, D), INNER ** -0.5, 0.125, ((0, 2),))
    return {"tokens": tokens, "slot_order": slot_order, "log_decay": log_decay, "grad_out": grad_out, "in_gain": in_gain, "w_gate": w_gate, "w_inner": w_inner, "w_shared": w_shared, "conv_inner": conv_inner, "conv_shared": conv_shared, "d_skip": d_skip, "norm_gain": norm_gain, "w_out": w_out}


EPS = 1e-05
HIGH = lax.Precision.HIGHEST

@jax.custom_vjp
def low(v):
    return lax.optimization_barrier(v.astype(jnp.bfloat16)).astype(jnp.float32)

@jax.custom_vjp
def low_back(v):
    return v

def low_keep(v):
    return (low(v), None)

def low_pass(kept, grad):
    return (grad,)

def back_keep(v):
    return (v, None)

def back_low(kept, grad):
    return (low(grad),)
low.defvjp(low_keep, low_pass)
low_back.defvjp(back_keep, back_low)

def causal_conv(values, kernel):
    kernel_len = kernel.shape[0]
    padded = jnp.pad(values, ((kernel_len - 1, 0), (0, 0)))
    summed = jnp.zeros(values.shape, jnp.float32)
    for offset in range(kernel_len):
        summed = summed + kernel[offset] * padded[offset:offset + values.shape[0]]
    return summed

def state_space(inner_act, b_rows, c_rows, rate_rows, skip_gain):
    blocks = inner_act.shape[0] // BLOCK
    head_count = rate_rows.shape[0]
    head_dim = inner_act.shape[1] // head_count
    values = inner_act.reshape(blocks, BLOCK, head_count, head_dim)
    b_blocks = b_rows.reshape(blocks, BLOCK, b_rows.shape[1])
    c_blocks = c_rows.reshape(blocks, BLOCK, c_rows.shape[1])
    rate_blocks = jnp.transpose(rate_rows.reshape(head_count, blocks, BLOCK), (1, 0, 2))
    step_dt = -rate_blocks
    cum_rates = jnp.cumsum(rate_blocks, axis=-1)
    gram_blocks = jnp.einsum('cqn,ckn->cqk', c_blocks, b_blocks, precision=HIGH)
    lower_mask = jnp.arange(BLOCK)[:, None] >= jnp.arange(BLOCK)[None, :]
    spread = cum_rates[:, :, :, None] - cum_rates[:, :, None, :]
    decay_mask = jnp.where(lower_mask, jnp.exp(jnp.where(lower_mask, spread, 0.0)), 0.0) * step_dt[:, :, None, :]
    mixing = low(gram_blocks[:, None] * decay_mask)
    intra_part = jnp.einsum('chqk,ckhp->cqhp', mixing, values, precision=HIGH)
    to_end = jnp.exp(cum_rates[:, :, -1:] - cum_rates) * step_dt
    carried = low(values * jnp.transpose(to_end, (0, 2, 1))[..., None])
    local_state = jnp.einsum('cqhp,cqn->chpn', carried, b_blocks, precision=HIGH)
    block_decay = jnp.exp(cum_rates[:, :, -1])

    def advance(running, slot_item):
        factor, addend = slot_item
        return (factor[:, None, None] * running + addend, running)
    initial = jnp.zeros((head_count, head_dim, b_rows.shape[1]), jnp.float32)
    unused, incoming = lax.scan(advance, initial, (block_decay, local_state))
    inter_part = jnp.einsum('cqn,chpn->cqhp', c_blocks, incoming, precision=HIGH)
    inter_part = inter_part * jnp.transpose(jnp.exp(cum_rates), (0, 2, 1))[..., None]
    result = intra_part + inter_part + skip_gain[None, None, :, None] * values
    return result.reshape(inner_act.shape)

def section_forward(residual, params, rate_rows):
    gain_in, gate_w, inner_w, shared_w, conv_in, conv_sh, skip_gain, gain_norm, out_w = params
    inv_in = lax.rsqrt(lax.optimization_barrier(jnp.mean(residual * residual, axis=-1, keepdims=True)) + EPS)
    normed = low(residual * inv_in * gain_in)
    gate_lin = low_back(jnp.dot(normed, gate_w, precision=HIGH))
    inner_lin = low(low_back(jnp.dot(normed, inner_w, precision=HIGH)))
    shared_lin = low(jnp.dot(normed, shared_w, precision=HIGH))
    inner_act = low(jax.nn.silu(causal_conv(inner_lin, conv_in)))
    shared_act = low(jax.nn.silu(causal_conv(shared_lin, conv_sh)))
    state_dim = shared_act.shape[1] // 2
    ssd_out = low_back(state_space(inner_act, shared_act[:, :state_dim], shared_act[:, state_dim:], rate_rows, skip_gain))
    gated_out = ssd_out * jax.nn.silu(gate_lin)
    inv_norm = lax.rsqrt(lax.optimization_barrier(jnp.mean(gated_out * gated_out, axis=-1, keepdims=True)) + EPS)
    scaled = low(gated_out * inv_norm * gain_norm)
    mixed_out = low_back(jnp.dot(scaled, out_w, precision=HIGH))
    return residual + mixed_out

def bound_section(rate_rows):

    def apply_section(residual, params):
        return section_forward(residual, params, rate_rows)
    return apply_section

def reference(tokens, slot_order, log_decay, grad_out, in_gain, w_gate, w_inner, w_shared, conv_inner, conv_shared, d_skip, norm_gain, w_out):
    weights = (in_gain.astype(jnp.float32), w_gate.astype(jnp.float32), w_inner.astype(jnp.float32), w_shared.astype(jnp.float32), conv_inner.astype(jnp.float32), conv_shared.astype(jnp.float32), d_skip.astype(jnp.float32), norm_gain.astype(jnp.float32), w_out.astype(jnp.float32))
    firsts = tokens.astype(jnp.float32)[slot_order]
    cotangents = grad_out.astype(jnp.float32)[slot_order]
    slot_rates = jnp.transpose(log_decay[:, slot_order], (1, 0, 2, 3))
    layer_count = log_decay.shape[0]

    def one_slot(grad_sums, slot_item):
        first_in, cotangent, rate_slot = slot_item
        residual = first_in
        outputs = []
        pullbacks = []
        for layer_idx in range(layer_count):
            level_params = tuple((weight[layer_idx] for weight in weights))
            residual, pullback = jax.vjp(bound_section(rate_slot[layer_idx]), residual, level_params)
            outputs.append(residual)
            pullbacks.append(pullback)
        flowing = cotangent
        in_grads = [flowing] * layer_count
        grad_list = list(grad_sums)
        for layer_idx in range(layer_count - 1, -1, -1):
            flowing, level_grads = pullbacks[layer_idx](flowing)
            in_grads[layer_idx] = flowing
            for position in range(len(grad_list)):
                grad_list[position] = grad_list[position].at[layer_idx].add(level_grads[position])
        return (tuple(grad_list), (jnp.stack(outputs), jnp.stack(in_grads)))
    initial = tuple((jnp.zeros(weight.shape, jnp.float32) for weight in weights))
    grad_sums, (section_rows, grad_rows) = lax.scan(one_slot, initial, (firsts, cotangents, slot_rates))
    section_out = jnp.transpose(section_rows, (1, 0, 2, 3))
    input_grad = jnp.transpose(grad_rows, (1, 0, 2, 3))
    return (section_out, input_grad, grad_sums[0], grad_sums[1], grad_sums[2], grad_sums[3], grad_sums[4], grad_sums[5], grad_sums[6], grad_sums[7], grad_sums[8])
```

```python
import functools

import jax
import jax.numpy as jnp
from jax import lax
from jax.experimental import pallas as pl
from jax.experimental.pallas import tpu as pltpu
from jax.sharding import PartitionSpec as P

BLOCK = 256
HALF = BLOCK // 2
PAD = 16
EPS = 1e-05
F32 = jnp.float32
LOW = jnp.bfloat16
HIDDEN = -1e30
NN = ((1,), (0,))
NT = ((1,), (1,))
TN = ((0,), (0,))
VMEM_BYTES = 50 * 1024 * 1024


def dot(a, b, dims):
    return lax.dot_general(a, b, (dims, ((), ())), preferred_element_type=F32)


def aligned(start, size):
    return pl.ds(pl.multiple_of(start, size), size)


def spread(cols, first, count, width):
    rows = cols.shape[0]
    lane = lax.broadcasted_iota(jnp.int32, (rows, count * width), 1)
    out = jnp.broadcast_to(cols[:, first : first + 1], (rows, count * width))
    for h in range(1, count):
        out = jnp.where(lane >= h * width, cols[:, first + h : first + h + 1], out)
    return out


def per_head(array, h, width):
    lane = lax.broadcasted_iota(jnp.int32, array.shape, 1)
    inside = (lane >= h * width) & (lane < (h + 1) * width)
    return jnp.where(inside, array, jnp.zeros_like(array))


def split_low(value):
    high = value.astype(LOW).astype(F32)
    return high, value - high


def column_of(row, size):
    return jnp.transpose(jnp.broadcast_to(row, (128, size)))


def sigmoid(v):
    return 1.0 / (1.0 + jnp.exp(-v))


def pick(flag, a, b):
    return jnp.where(flag, a, b)


class Sizes:
    def __init__(self, blocks, width, channels, heads, states, taps, head_axis, inner):
        self.blocks = blocks
        self.width = width
        self.channels = channels
        self.heads = heads
        self.head_width = channels // heads
        self.states = states
        self.lin = channels + 2 * states
        self.taps = taps
        self.head_axis = head_axis
        self.chunk = width // head_axis
        self.rows = blocks * HALF
        self.tokens = blocks * BLOCK
        self.inner = inner


def load_weights(sz, layer, c, wown, wrecv, oown, orecv, wv, ov):
    @pl.when(c == layer)
    def _():
        pltpu.sync_copy(wown, wv)
        pltpu.sync_copy(oown, ov)

    @pl.when(c != layer)
    def _():
        pltpu.sync_copy(wrecv, wv)
        pltpu.sync_copy(orecv, ov)


def put_pair(dst, c, own, other):
    dst[aligned(c * HALF, HALF), :] = own
    dst[aligned((1 - c) * HALF, HALF), :] = other


def put_pieces(sz, dst, c, h, own, other):
    for d in range(sz.head_axis):
        cols = aligned((h ^ d) * sz.chunk, sz.chunk)
        dst[aligned(c * HALF, HALF), cols] = own[d]
        dst[aligned((1 - c) * HALF, HALF), cols] = other[d]


def put_parts(sz, b, c, h, part, keep, send):
    for d in range(sz.head_axis):
        cols = aligned((h ^ d) * sz.chunk, sz.chunk)
        keep[d, aligned(b * HALF, HALF), :] = part[aligned(c * HALF, HALF), cols]
        send[d, aligned(b * HALF, HALF), :] = part[aligned((1 - c) * HALF, HALF), cols]


def put_scalars(b, c, row, kept, sent):
    for scratch, flag in ((kept, c == 0), (sent, c != 0)):
        high, low = split_low(pick(flag, row[:, :HALF], row[:, HALF:]))
        line = lax.broadcasted_iota(jnp.int32, scratch.shape, 0)
        lower = jnp.where(line == 8 + b, low, scratch[...])
        scratch[...] = jnp.where(line == b, high, lower)


def line_of(table, at):
    line = lax.broadcasted_iota(jnp.int32, table.shape, 0)
    return jnp.sum(jnp.where(line == at, table, 0.0), axis=0, keepdims=True)


def close_parts(sz, keep, send, kept, sent):
    for scratch, out in ((kept, keep), (sent, send)):
        extra = jnp.concatenate([scratch[...]] * (sz.chunk // HALF), axis=1).astype(LOW)
        for d in range(sz.head_axis):
            out[d, sz.rows :, :] = extra


def conv_forward(sz, ext, taps):
    pre = taps[0:1] * ext[5 : 5 + BLOCK, :]
    for j in range(1, sz.taps):
        pre = pre + taps[j : j + 1] * ext[5 + j : 5 + j + BLOCK, :]
    return pre


def decay_of(sz, cols, rowp, h, mask):
    rows = cols[:, h : h + 1] + rowp[12 + h : 13 + h, :]
    return jnp.exp(jnp.where(mask, rows, HIDDEN))


def lower_mask():
    t = lax.broadcasted_iota(jnp.int32, (BLOCK, BLOCK), 0)
    s = lax.broadcasted_iota(jnp.int32, (BLOCK, BLOCK), 1)
    return t >= s


def forward_kernel(sz, layer, sc, *refs):
    sources = 2 if layer == 0 else 2 * sz.head_axis + 2
    src, refs = refs[:sources], refs[sources:]
    rowp, pv, wown, wrecv, oown, orecv, halo, begin = refs[:8]
    normed_o, gl_o, lin_o, ssd_o, inc_o, inv_o, part_o, keep, send, fin_o = refs[8:18]
    xs, ms, wv, ov, ext, state, kept, sent, part = refs[18:]
    b = pl.program_id(0)
    c, h = sc[0], sc[1]
    ch, st = sz.channels, sz.states

    @pl.when(b == 0)
    def _():
        load_weights(sz, layer, c, wown, wrecv, oown, orecv, wv, ov)
        ext[0:8, :] = halo[...]
        state[...] = begin[...]
        kept[...] = jnp.zeros_like(kept)
        sent[...] = jnp.zeros_like(sent)

    if layer == 0:
        put_pair(xs, c, src[0][0], src[1][0])
    else:
        n = sz.head_axis
        put_pieces(sz, xs, c, h, [r[...] for r in src[:n]], [r[...] for r in src[n : 2 * n]])
        put_pair(ms, c, src[2 * n][0], src[2 * n + 1][0])

    x = xs[...].astype(F32)
    inv_in = lax.rsqrt(jnp.mean(x * x, axis=1, keepdims=True) + EPS)
    normed = (x * inv_in * pv[0:1, : sz.width]).astype(LOW)
    normed_o[...] = normed
    proj = dot(normed, wv[...], NN)
    gl = proj[:, :ch]
    gl_o[...] = gl
    lin = proj[:, ch:].astype(LOW)
    lin_o[...] = lin
    ext[8 : 8 + BLOCK, :] = lin.astype(F32)
    pre = conv_forward(sz, ext, pv[1:5, : sz.lin])
    ext[0:8, :] = ext[BLOCK : BLOCK + 8, :]
    act = (pre * sigmoid(pre)).astype(LOW)
    values, bm, cm = act[:, :ch], act[:, ch : ch + st], act[:, ch + st :]

    rp = rowp[...]
    cols = jnp.transpose(rp)
    mask = lower_mask()
    gram = dot(cm, bm, NT)
    mixes, parts = [], []
    for i in range(sz.heads):
        mixes.append((gram * decay_of(sz, cols, rp, i, mask)).astype(LOW))
        parts.append(per_head(values, i, sz.head_width))
    intra = dot(jnp.concatenate(mixes, axis=1), jnp.concatenate(parts, axis=0), NN)

    low_state = state[...].astype(LOW)
    inc_o[0] = low_state
    ecum = spread(cols, sz.heads, sz.heads, sz.head_width)
    inter = dot(cm, low_state, NT) * ecum
    vf = values.astype(F32)
    carried = (vf * spread(cols, 2 * sz.heads, sz.heads, sz.head_width)).astype(LOW)
    local = dot(carried, bm, TN)
    for i in range(sz.heads):
        rows = slice(i * sz.head_width, (i + 1) * sz.head_width)
        total = cols[BLOCK - 1 : BLOCK, sz.heads + i : sz.heads + i + 1]
        state[rows, :] = total * state[rows, :] + local[rows]
    ssd = intra + inter + pv[6:7, :ch] * vf
    ssd_o[...] = ssd
    gated = ssd * (gl * sigmoid(gl))
    weighty = gated * pv[5:6, :ch]
    part[...] = dot(weighty.astype(LOW), ov[...], NN).astype(LOW)

    lane = lax.broadcasted_iota(jnp.int32, (BLOCK, 128), 1)
    square = jnp.sum(gated * gated, axis=1, keepdims=True)
    if layer == 0:
        project = jnp.zeros_like(square)
    else:
        scaled_grad = dot(ms[...], ov[...], NT)
        project = jnp.sum(scaled_grad * weighty, axis=1, keepdims=True)
    stats = jnp.where(lane == 0, square, jnp.where(lane == 1, project, inv_in))
    stats = jnp.transpose(stats)
    part_o[...] = stats[0:2, :]
    inv_o[...] = stats[2:3, :]
    put_scalars(b, c, stats[0:1, :], kept, sent)
    put_parts(sz, b, c, h, part, keep, send)

    @pl.when(b == sz.blocks - 1)
    def _():
        close_parts(sz, keep, send, kept, sent)
        fin_o[...] = state[...]


def backward_kernel(sz, layer, sc, *refs):
    n = sz.head_axis
    sources = 2 * n + 2 if layer == 0 else 3
    src, refs = refs[:sources], refs[sources:]
    normed_r, gl_r, lin_r, ssd_r, inc_r, rowp, pv = refs[:7]
    wown, wrecv, oown, orecv, halo, halo_grad, begin = refs[7:14]
    keep, send, cat_o, scaled_o, mixed_o, small, fin_o, rim_o = refs[14:22]
    ms, wv, ov, ext, back, state, kept, sent, part, heads_p = refs[22:]
    i_step = pl.program_id(0)
    b = sz.blocks - 1 - i_step
    c, h = sc[0], sc[1]
    ch, st = sz.channels, sz.states

    @pl.when(i_step == 0)
    def _():
        load_weights(sz, layer, c, wown, wrecv, oown, orecv, wv, ov)
        back[BLOCK : BLOCK + 8, :] = halo_grad[...]
        state[...] = begin[...]
        kept[...] = jnp.zeros_like(kept)
        sent[...] = jnp.zeros_like(sent)
        small[...] = jnp.zeros_like(small)
        if layer == 0:
            for k in range(2):
                extra = src[k * n][sz.rows :, :].astype(F32)
                for d in range(1, n):
                    extra = extra + src[k * n + d][sz.rows :, :].astype(F32)
                heads_p[8 * k : 8 * k + 8, :] = extra[0:8, :HALF] + extra[8:16, :HALF]

    if layer == 0:
        rows = aligned(b * HALF, HALF)
        put_pieces(
            sz, ms, c, h, [r[rows, :] for r in src[:n]], [r[rows, :] for r in src[n : 2 * n]]
        )
        halves = []
        for k in range(2):
            alpha = lax.rsqrt(line_of(src[2 * n + k][...], b) / sz.inner + EPS)
            beta = alpha * alpha * line_of(heads_p[...], 8 * k + b) / sz.inner
            halves.append((alpha, beta))
        alpha, beta = (
            pick(
                c == 0,
                jnp.concatenate([halves[0][q], halves[1][q]], axis=1),
                jnp.concatenate([halves[1][q], halves[0][q]], axis=1),
            )
            for q in range(2)
        )
    else:
        put_pair(ms, c, src[0][0], src[1][0])
        alpha = lax.rsqrt(src[2][0:1, :] / sz.inner + EPS)
        beta = alpha * alpha * alpha * src[2][1:2, :] / sz.inner

    rp = rowp[...]
    sub = lax.broadcasted_iota(jnp.int32, rp.shape, 0)
    cols = jnp.transpose(jnp.where(sub == 12, alpha, jnp.where(sub == 13, beta, rp)))
    alpha, beta = cols[:, 12:13], cols[:, 13:14]

    gl = gl_r[...]
    ssd = ssd_r[...]
    sig = sigmoid(gl)
    swish = gl * sig
    slope = sig * (1.0 + gl * (1.0 - sig))
    gated = ssd * swish
    mixed_grad = ms[...]
    mixed_o[...] = mixed_grad
    scaled_grad = dot(mixed_grad, ov[...], NT)
    gain = pv[5:6, :ch]
    normal = gated * alpha
    small[4:5, :ch] += jnp.sum(scaled_grad * normal, axis=0, keepdims=True)
    scaled_o[...] = (normal * gain).astype(LOW)
    gated_grad = alpha * (scaled_grad * gain) - beta * gated
    ssd_grad = (gated_grad * swish).astype(LOW)
    gate_grad = (gated_grad * ssd * slope).astype(LOW)
    sgf = ssd_grad.astype(F32)

    before = lin_r[pl.ds(pl.multiple_of(jnp.maximum(b * BLOCK - 16, 0), 16), 16), :]
    ext[0:8, :] = pick(b > 0, before[8:16, :].astype(F32), halo[...])
    ext[8 : 8 + BLOCK, :] = lin_r[aligned(b * BLOCK, BLOCK), :].astype(F32)
    taps = pv[1:5, : sz.lin]
    pre = conv_forward(sz, ext, taps)
    psig = sigmoid(pre)
    pact = pre * psig
    pslope = psig * (1.0 + pre * (1.0 - psig))
    act = pact.astype(LOW)
    values, bm, cm = act[:, :ch], act[:, ch : ch + st], act[:, ch + st :]
    vf = values.astype(F32)
    small[5:6, :ch] += jnp.sum(sgf * vf, axis=0, keepdims=True)

    mask = lower_mask()
    gram = dot(cm, bm, NT)
    gram_grad = jnp.zeros((BLOCK, BLOCK), F32)
    mixes, parts = [], []
    for i in range(sz.heads):
        decay = decay_of(sz, cols, rp, i, mask)
        mixes.append((gram * decay).astype(LOW))
        parts.append(per_head(ssd_grad, i, sz.head_width))
        gram_grad = gram_grad + dot(parts[-1], values, NT) * decay
    intra_grad = dot(jnp.concatenate(mixes, axis=0), jnp.concatenate(parts, axis=0), TN)

    ecum = spread(cols, sz.heads, sz.heads, sz.head_width)
    to_end = spread(cols, 2 * sz.heads, sz.heads, sz.head_width)
    inter_grad = (sgf * ecum).astype(LOW)
    low_state = state[...].astype(LOW)
    carried = (vf * to_end).astype(LOW)
    carried_grad = dot(bm, low_state, NT)
    gram_low = gram_grad.astype(LOW)
    b_grad = dot(gram_low, cm, TN) + dot(carried, low_state, NN)
    c_grad = dot(gram_low, bm, NN) + dot(inter_grad, inc_r[0], NN)
    value_grad = intra_grad + pv[6:7, :ch] * sgf + carried_grad * to_end
    entry = dot(inter_grad, cm, TN)
    for i in range(sz.heads):
        rows = slice(i * sz.head_width, (i + 1) * sz.head_width)
        total = cols[BLOCK - 1 : BLOCK, sz.heads + i : sz.heads + i + 1]
        state[rows, :] = total * state[rows, :] + entry[rows]

    pre_grad = jnp.concatenate([value_grad, b_grad, c_grad], axis=1) * pslope
    back[0:BLOCK, :] = pre_grad
    lin_grad = taps[0:1] * back[sz.taps - 1 : sz.taps - 1 + BLOCK, :]
    for j in range(1, sz.taps):
        at = sz.taps - 1 - j
        lin_grad = lin_grad + taps[j : j + 1] * back[at : at + BLOCK, :]
    for j in range(sz.taps):
        small[j : j + 1, :] += jnp.sum(pre_grad * ext[5 + j : 5 + j + BLOCK, :], axis=0, keepdims=True)
    back[BLOCK : BLOCK + 8, :] = back[0:8, :]
    cat = jnp.concatenate([gate_grad, lin_grad.astype(LOW)], axis=1)
    cat_o[...] = cat
    normed_grad = dot(cat, wv[...], NT)
    part[...] = normed_grad.astype(LOW)
    along = jnp.sum(normed_grad * normed_r[...].astype(F32), axis=1, keepdims=True)
    along = jnp.transpose(jnp.broadcast_to(along, (BLOCK, 128)))
    put_scalars(b, c, along[0:1, :], kept, sent)
    put_parts(sz, b, c, h, part, keep, send)

    @pl.when(i_step == sz.blocks - 1)
    def _():
        close_parts(sz, keep, send, kept, sent)
        fin_o[...] = state[...]
        rim_o[...] = back[0:8, :]


def weights_kernel(sz, sc, normed, cat, mixed, scaled, *outs):
    outs, full = outs[:-1], outs[-1]
    wide = cat.shape[1]
    step = sz.chunk
    for q in range(sz.head_axis):
        at = slice(q * step, (q + 1) * step)
        full[at, :wide] = dot(normed[:, at], cat[...], TN).astype(LOW)
        full[at, wide:] = dot(mixed[:, at], scaled[...], TN).astype(LOW)
    rows = sz.width // len(outs)
    for r, out in enumerate(outs):
        to = lax.rem(sc[2] + r, len(outs))
        out[...] = full[aligned(to * rows, rows), :]


def join_kernel(sz, keep, recv, own, *sends):
    rows = sz.rows
    extra = keep[0, rows:, :].astype(F32) + recv[0, rows:, :].astype(F32)
    high, low = split_low(extra[0:8, :] + extra[8:16, :])
    extra = jnp.concatenate([high, low], axis=0)
    for d, out in enumerate((own,) + sends):
        out[:rows, :] = (keep[d, :rows, :].astype(F32) + recv[d, :rows, :].astype(F32)).astype(out.dtype)
        out[rows:, :] = extra.astype(out.dtype)


def total_of(parts, rows):
    total = parts[0][rows, :].astype(F32)
    for p in parts[1:]:
        total = total + p[rows, :].astype(F32)
    return total


def output_kernel(sz, layer, sc, *refs):
    n = sz.head_axis
    parts, refs = refs[:n], refs[n:]
    resid, res_o, low_o, mixed_o, square_o = refs
    h = sc[1]
    extra = total_of(parts, slice(sz.rows, sz.rows + PAD))
    square = extra[0:8, :HALF] + extra[8:16, :HALF]
    square_o[...] = square
    inv = lax.rsqrt(square / sz.inner + EPS)
    for b in range(sz.blocks):
        rows = slice(b * HALF, (b + 1) * HALF)
        col = column_of(inv[b : b + 1, :], HALF)[:, 0:1]
        mixed = total_of(parts, rows) * col
        if layer == 0:
            base = resid[b, :, aligned(h * sz.chunk, sz.chunk)].astype(F32)
        else:
            base = resid[rows, :]
        res = base + mixed
        res_o[rows, :] = res
        low_o[rows, :] = res.astype(LOW)
        mixed_o[rows, :] = mixed


def input_kernel(sz, layer, sc, *refs):
    n = sz.head_axis
    parts, refs = refs[:n], refs[n:]
    resid, outg, inv_r, pv = refs[:4]
    refs = refs[4:]
    if layer == 1:
        mixed, refs = refs[0], refs[1:]
    grad_o, low_o, gain_o = refs
    c, h = sc[0], sc[1]
    mine = aligned(h * sz.chunk, sz.chunk)
    gain = pv[0:1, mine]
    extra = total_of(parts, slice(sz.rows, sz.rows + PAD))
    along = extra[0:8, :HALF] + extra[8:16, :HALF]
    gain_sum = jnp.zeros((1, sz.chunk), F32)
    tops, lows = [], []
    for b in range(sz.blocks):
        rows = slice(b * HALF, (b + 1) * HALF)
        at = b * BLOCK
        inv_row = pick(c == 0, inv_r[:, at : at + HALF], inv_r[:, at + HALF : at + BLOCK])
        inv = column_of(inv_row, HALF)[:, 0:1]
        share = column_of(along[b : b + 1, :] / sz.width, HALF)[:, 0:1]
        total = total_of(parts, rows)
        if layer == 0:
            base = resid[b, :, mine].astype(F32)
            out_grad = outg[rows, :]
        else:
            base = resid[rows, :]
            out_grad = outg[b, :, mine].astype(F32)
        unit = base * inv
        gain_sum = gain_sum + jnp.sum(total * unit, axis=0, keepdims=True)
        grad = out_grad + inv * (total * gain - unit * share)
        grad_o[rows, :] = grad
        low = grad.astype(LOW)
        low_o[rows, :] = low
        if layer == 1:
            dots = jnp.sum(low.astype(F32) * mixed[rows, :], axis=1, keepdims=True)
            row = jnp.transpose(jnp.broadcast_to(dots, (HALF, 128)))[0:1, :]
            high, rest = split_low(row)
            tops.append(high)
            lows.append(rest)
    gain_o[...] = jnp.broadcast_to(gain_sum, (8, sz.chunk))
    if layer == 1:
        fill = [jnp.zeros((8 - sz.blocks, HALF), F32)] if sz.blocks < 8 else []
        extra = jnp.concatenate(tops + fill + lows + fill, axis=0)
        extra = jnp.concatenate([extra] * (sz.chunk // HALF), axis=1)
        low_o[sz.rows :, :] = extra.astype(LOW)
    else:
        low_o[sz.rows :, :] = jnp.zeros((PAD, sz.chunk), LOW)


def sum_kernel(sz, count, sc, *refs):
    same, other = refs[:count], refs[count : 2 * count]
    gate_o, inner_o, shared_o, out_o = refs[2 * count :]
    c = sc[0]
    ch, st = sz.channels, sz.states
    a = total_of(same, slice(None))
    b = total_of(other, slice(None))
    mine, theirs = aligned(c * ch, ch), aligned((1 - c) * ch, ch)
    for at, out in ((0, gate_o), (ch, inner_o), (2 * ch + 2 * st, out_o)):
        out[:, mine] = a[:, at : at + ch]
        out[:, theirs] = b[:, at : at + ch]
    shared_o[...] = a[:, 2 * ch : 2 * ch + 2 * st] + b[:, 2 * ch : 2 * ch + 2 * st]


def whole(shape):
    return pl.BlockSpec(shape, lambda *_: (0,) * len(shape))


def per_device(
    tokens,
    slot_order,
    log_decay,
    grad_out,
    in_gain,
    w_gate,
    w_inner,
    w_shared,
    conv_inner,
    conv_shared,
    d_skip,
    norm_gain,
    w_out,
):
    slots = tokens.shape[0]
    span = tokens.shape[1]
    width = tokens.shape[2]
    seq = lax.axis_size("seq")
    head_axis = lax.axis_size("head")
    cores = lax.axis_size("section")
    spans = seq // slots
    c = lax.axis_index("section")
    z = lax.axis_index("seq")
    h = lax.axis_index("head")
    k = lax.rem(z, slots)
    g = z // slots
    inner_dev = w_gate.shape[2]
    channels = inner_dev // cores
    shared = w_shared.shape[2]
    heads_dev = d_skip.shape[1]
    heads = heads_dev // cores
    taps = conv_inner.shape[1]
    sz = Sizes(
        slots * span // BLOCK,
        width,
        channels,
        heads,
        shared // 2,
        taps,
        head_axis,
        inner_dev * head_axis,
    )
    first = c == 0
    swap = [(0, 1), (1, 0)]
    sc = jnp.stack([c, h, z]).astype(jnp.int32)
    nb, tok, rows, chunk = sz.blocks, sz.tokens, sz.rows, sz.chunk

    def cross(x):
        return lax.ppermute(x, "section", swap)

    def turn(x, r):
        pairs = [(i, i // slots * slots + (i % slots + r) % slots) for i in range(seq)]
        return lax.ppermute(x, "seq", pairs)

    def over_heads(x, d):
        return lax.ppermute(x, "head", [(i, i ^ d) for i in range(head_axis)])

    def next_span(x, way):
        pairs = [(i, i + way * slots) for i in range(seq) if 0 <= i + way * slots < seq]
        return lax.ppermute(x, "seq", pairs)

    def exchange(item, shape, dtype):
        out = lax.dynamic_update_index_in_dim(jnp.zeros((slots,) + shape, dtype), item(k), k, 0)
        for r in range(1, slots):
            got = turn(item(lax.rem(k + r, slots)), r)
            out = lax.dynamic_update_index_in_dim(out, got, lax.rem(k + slots - r, slots), 0)
        return out

    def rows_of(source):
        def item(j):
            piece = lax.dynamic_slice(source, (slot_order[j], c * HALF, 0), (1, HALF, width))
            return piece[0]

        own = exchange(item, (HALF, width), LOW)
        return own, cross(own)

    def half(w, which):
        return lax.dynamic_slice_in_dim(w[0], which * channels, channels, w.ndim - 2)

    def side(which):
        return jnp.concatenate([half(w_gate, which), half(w_inner, which), w_shared[0]], axis=1)

    def out_side(which):
        return lax.dynamic_slice_in_dim(w_out[0], h * inner_dev + which * channels, channels, 0)

    def gains(which):
        def line(row):
            return jnp.pad(row, ((0, 0), (0, width - row.shape[1])))

        skip = jnp.repeat(
            lax.dynamic_slice_in_dim(d_skip[0], which * heads, heads, 0), sz.head_width
        )
        conv = jnp.concatenate([half(conv_inner, which), conv_shared[0]], axis=1)
        lines = [
            line(in_gain),
            line(conv),
            line(lax.dynamic_slice_in_dim(norm_gain, which * channels, channels, 1)),
            line(skip[None]),
        ]
        table = jnp.concatenate(lines, axis=0)
        return jnp.pad(table, ((0, 16 - table.shape[0]), (0, 0)))

    tok_own, tok_other = rows_of(tokens)
    w_mine, o_mine = side(c), out_side(c)
    w_got, o_got = cross(side(1 - c)), cross(out_side(1 - c))
    pv_mine, pv_got = gains(c), cross(gains(1 - c))
    pvs = (pick(first, pv_mine, pv_got), pick(first, pv_got, pv_mine))

    rates = lax.all_gather(log_decay[0][slot_order], ("section", "seq"))
    rates = rates.reshape(cores, seq, slots, heads_dev, span)
    rates = lax.dynamic_slice(
        rates, (0, g * slots, k, c * heads, 0), (cores, slots, 1, heads, span)
    )[:, :, 0]
    rates = jnp.transpose(rates, (0, 2, 1, 3)).reshape(cores, heads, nb, BLOCK)
    cum = jnp.cumsum(rates, axis=-1)
    end = cum[..., -1:]
    tables = jnp.concatenate(
        [cum, jnp.exp(cum), jnp.exp(end - cum) * -rates, jnp.log(-rates) - cum], axis=1
    ).reshape(cores, 4 * heads, tok)
    tables = jnp.pad(tables, ((0, 0), (0, 16 - 4 * heads), (0, 0)))
    span_total = jnp.exp(jnp.sum(end[..., 0], axis=-1))
    span_total = jnp.repeat(span_total, sz.head_width, axis=1)[:, :, None]

    out_own, out_other = rows_of(grad_out)

    prefetch = functools.partial(pltpu.PrefetchScalarGridSpec, num_scalar_prefetch=1)
    options = pltpu.CompilerParams(vmem_limit_bytes=VMEM_BYTES)
    anywhere = pl.BlockSpec(memory_space=pl.ANY)

    def shape(dims, dtype):
        return jax.ShapeDtypeStruct(dims, dtype)

    parts_shape = shape((head_axis, rows + PAD, chunk), LOW)

    def forward(layer, sources):
        def at(b, _):
            return (b, 0)

        pair = pl.BlockSpec((1, HALF, width), lambda b, _: (b, 0, 0))
        piece = pl.BlockSpec((HALF, chunk), at)
        src_specs = [pair] * 2 if layer == 0 else [piece] * (2 * head_axis) + [pair] * 2

        def call(halo, begin):
            return pl.pallas_call(
                functools.partial(forward_kernel, sz, layer),
                grid_spec=prefetch(
                    grid=(nb,),
                    in_specs=src_specs
                    + [
                        pl.BlockSpec((16, BLOCK), lambda b, _: (0, b)),
                        whole((16, width)),
                        anywhere,
                        anywhere,
                        anywhere,
                        anywhere,
                        whole((8, sz.lin)),
                        whole((channels, sz.states)),
                    ],
                    out_specs=[
                        pl.BlockSpec((BLOCK, width), at),
                        pl.BlockSpec((BLOCK, channels), at),
                        pl.BlockSpec((BLOCK, sz.lin), at),
                        pl.BlockSpec((BLOCK, channels), at),
                        pl.BlockSpec((1, channels, sz.states), lambda b, _: (b, 0, 0)),
                        pl.BlockSpec((1, BLOCK), lambda b, _: (0, b)),
                        pl.BlockSpec((2, BLOCK), lambda b, _: (0, b)),
                        whole(parts_shape.shape),
                        whole(parts_shape.shape),
                        whole((channels, sz.states)),
                    ],
                    scratch_shapes=[
                        pltpu.VMEM((BLOCK, width), LOW),
                        pltpu.VMEM((BLOCK, width), LOW),
                        pltpu.VMEM(w_mine.shape, LOW),
                        pltpu.VMEM(o_mine.shape, LOW),
                        pltpu.VMEM((BLOCK + 8, sz.lin), F32),
                        pltpu.VMEM((channels, sz.states), F32),
                        pltpu.VMEM((PAD, HALF), F32),
                        pltpu.VMEM((PAD, HALF), F32),
                        pltpu.VMEM((BLOCK, width), LOW),
                    ],
                ),
                out_shape=[
                    shape((tok, width), LOW),
                    shape((tok, channels), F32),
                    shape((tok, sz.lin), LOW),
                    shape((tok, channels), F32),
                    shape((nb, channels, sz.states), LOW),
                    shape((1, tok), F32),
                    shape((2, tok), F32),
                    parts_shape,
                    parts_shape,
                    shape((channels, sz.states), F32),
                ],
                compiler_params=options,
            )(sc, *sources, tables[layer], pvs[layer], w_mine, w_got, o_mine, o_got, halo, begin)

        halo = jnp.zeros((8, sz.lin), F32)
        begin = jnp.zeros((channels, sz.states), F32)
        if spans == 1:
            return call(halo, begin), halo
        halo = next_span(call(halo, begin)[2][tok - 8 :].astype(F32), 1)
        local = call(halo, begin)[9]
        for _ in range(spans - 1):
            begin = next_span(span_total[layer] * begin + local, 1)
        return call(halo, begin), halo

    def backward(layer, sources, saved, halo):
        def at(i, _):
            return (nb - 1 - i, 0)

        pair = pl.BlockSpec((1, HALF, width), lambda i, _: (nb - 1 - i, 0, 0))
        if layer == 0:
            src_specs = [whole(s.shape) for s in sources]
        else:
            src_specs = [pair, pair, pl.BlockSpec((2, BLOCK), lambda i, _: (0, nb - 1 - i))]
        normed, gl, lin, ssd, inc = saved

        def call(halo_grad, begin):
            return pl.pallas_call(
                functools.partial(backward_kernel, sz, layer),
                grid_spec=prefetch(
                    grid=(nb,),
                    in_specs=src_specs
                    + [
                        pl.BlockSpec((BLOCK, width), at),
                        pl.BlockSpec((BLOCK, channels), at),
                        whole(lin.shape),
                        pl.BlockSpec((BLOCK, channels), at),
                        pl.BlockSpec((1, channels, sz.states), lambda i, _: (nb - 1 - i, 0, 0)),
                        pl.BlockSpec((16, BLOCK), lambda i, _: (0, nb - 1 - i)),
                        whole((16, width)),
                        anywhere,
                        anywhere,
                        anywhere,
                        anywhere,
                        whole((8, sz.lin)),
                        whole((8, sz.lin)),
                        whole((channels, sz.states)),
                    ],
                    out_specs=[
                        whole(parts_shape.shape),
                        whole(parts_shape.shape),
                        pl.BlockSpec((BLOCK, w_mine.shape[1]), at),
                        pl.BlockSpec((BLOCK, channels), at),
                        pl.BlockSpec((BLOCK, width), at),
                        whole((16, sz.lin)),
                        whole((channels, sz.states)),
                        whole((8, sz.lin)),
                    ],
                    scratch_shapes=[
                        pltpu.VMEM((BLOCK, width), LOW),
                        pltpu.VMEM(w_mine.shape, LOW),
                        pltpu.VMEM(o_mine.shape, LOW),
                        pltpu.VMEM((BLOCK + 8, sz.lin), F32),
                        pltpu.VMEM((BLOCK + 8, sz.lin), F32),
                        pltpu.VMEM((channels, sz.states), F32),
                        pltpu.VMEM((PAD, HALF), F32),
                        pltpu.VMEM((PAD, HALF), F32),
                        pltpu.VMEM((BLOCK, width), LOW),
                        pltpu.VMEM((PAD, HALF), F32),
                    ],
                ),
                out_shape=[
                    parts_shape,
                    parts_shape,
                    shape((tok, w_mine.shape[1]), LOW),
                    shape((tok, channels), LOW),
                    shape((tok, width), LOW),
                    shape((16, sz.lin), F32),
                    shape((channels, sz.states), F32),
                    shape((8, sz.lin), F32),
                ],
                compiler_params=options,
            )(
                sc, *sources, normed, gl, lin, ssd, inc, tables[layer], pvs[layer],
                w_mine, w_got, o_mine, o_got, halo, halo_grad, begin,
            )

        halo_grad = jnp.zeros((8, sz.lin), F32)
        begin = jnp.zeros((channels, sz.states), F32)
        if spans == 1:
            return call(halo_grad, begin)
        local = call(halo_grad, begin)[6]
        for _ in range(spans - 1):
            begin = next_span(span_total[layer] * begin + local, -1)
        halo_grad = next_span(call(halo_grad, begin)[7], -1)
        return call(halo_grad, begin)

    def scatter(keep, send):
        joined = pl.pallas_call(
            functools.partial(join_kernel, sz),
            out_shape=[shape((rows + PAD, chunk), F32)]
            + [shape((rows + PAD, chunk), LOW)] * (head_axis - 1),
            compiler_params=options,
        )(keep, cross(send))
        return [joined[0]] + [over_heads(joined[d], d) for d in range(1, head_axis)]

    def gather(low):
        own = [low] + [over_heads(low, d) for d in range(1, head_axis)]
        return own + [cross(x) for x in own]

    smem = pl.BlockSpec(memory_space=pltpu.SMEM)
    vmem = pl.BlockSpec(memory_space=pltpu.VMEM)

    def section_output(layer, parts, resid):
        return pl.pallas_call(
            functools.partial(output_kernel, sz, layer),
            in_specs=[smem] + [vmem] * (head_axis + 1),
            out_shape=[
                shape((rows, chunk), F32),
                shape((rows, chunk), LOW),
                shape((rows, chunk), F32),
                shape((8, HALF), F32),
            ],
            compiler_params=options,
        )(sc, *parts, resid)

    def section_input(layer, parts, *others):
        return pl.pallas_call(
            functools.partial(input_kernel, sz, layer),
            in_specs=[smem] + [vmem] * (head_axis + len(others)),
            out_shape=[
                shape((rows, chunk), F32),
                shape((rows + PAD, chunk), LOW),
                shape((8, chunk), F32),
            ],
            compiler_params=options,
        )(sc, *parts, *others)

    def weight_grads(layer, normed, cat, mixed, scaled):
        part = width // seq
        chunks = pl.pallas_call(
            functools.partial(weights_kernel, sz),
            in_specs=[smem] + [vmem] * 4,
            out_shape=[shape((part, cat.shape[1] + channels), LOW)] * seq,
            scratch_shapes=[pltpu.VMEM((width, cat.shape[1] + channels), LOW)],
            compiler_params=options,
        )(sc, normed, cat, mixed, scaled)
        same, other = [chunks[0]], []
        for r in range(seq):
            for source in range(cores):
                if source == layer and r == 0:
                    continue
                pairs = [(source * seq + i, layer * seq + (i + r) % seq) for i in range(seq)]
                got = lax.ppermute(chunks[r], ("section", "seq"), pairs)
                (same if source == layer else other).append(got)
        return pl.pallas_call(
            functools.partial(sum_kernel, sz, seq),
            in_specs=[smem] + [vmem] * (2 * seq),
            out_shape=[
                shape((part, inner_dev), F32),
                shape((part, inner_dev), F32),
                shape((part, shared), F32),
                shape((part, inner_dev), F32),
            ],
            compiler_params=options,
        )(sc, *same, *other)

    def to_home(one, two):
        one = one[:rows].reshape(nb, HALF, chunk)
        two = two[:rows].reshape(nb, HALF, chunk)
        mine = pick(first, one, two)
        got = cross(pick(first, two, one))
        full = jnp.concatenate([pick(first, mine, got), pick(first, got, mine)], axis=1)
        back = exchange(
            lambda j: lax.dynamic_index_in_dim(full, j, 0, False), (BLOCK, chunk), LOW
        )
        return back.astype(F32)[None]

    fw0, halo0 = forward(0, [tok_own, tok_other])
    res1, low1, mixed0, square0 = section_output(0, scatter(fw0[7], fw0[8]), tok_own)
    pieces1 = gather(low1)
    square_other = cross(square0)

    fw1, halo1 = forward(1, pieces1 + [out_own, out_other])
    stats = lax.psum(fw1[6], ("section", "head"))
    bw1 = backward(1, [out_own, out_other, stats], fw1[:5], halo1)
    igrad1, glow1, gain1 = section_input(
        1, scatter(bw1[0], bw1[1]), res1, out_own, fw1[5], pvs[1], mixed0
    )
    piecesg = gather(glow1)

    bw0 = backward(0, piecesg + [square0, square_other], fw0[:5], halo0)
    igrad0, glow0, gain0 = section_input(
        0, scatter(bw0[0], bw0[1]), tok_own, igrad1, fw0[5], pvs[0]
    )

    unused, low2, unused_mixed, unused_square = section_output(1, scatter(fw1[7], fw1[8]), res1)
    sums1 = weight_grads(1, fw1[0], bw1[2], bw1[4], bw1[3])
    sums0 = weight_grads(0, fw0[0], bw0[2], bw0[4], bw0[3])
    section_out = to_home(low1, low2)
    input_grad = to_home(glow0, glow1)

    gate_g, inner_g, shared_g, out_g = (pick(first, a, b) for a, b in zip(sums0, sums1))
    part = shared_g.shape[0] // head_axis
    shared_sum = lax.dynamic_slice_in_dim(shared_g, h * part, part, 0)
    for d in range(1, head_axis):
        piece = lax.dynamic_slice_in_dim(shared_g, (h ^ d) * part, part, 0).astype(LOW)
        shared_sum = shared_sum + over_heads(piece, d).astype(F32)

    def placed(small):
        lines = small[: taps + 2, :channels]
        wide = jnp.zeros((taps + 2, inner_dev), F32)
        return lax.dynamic_update_slice(wide, lines, (0, c * channels))

    by_channel = lax.psum(jnp.stack([placed(bw0[5]), placed(bw1[5])]), ("section", "seq"))
    by_channel = pick(first, by_channel[0], by_channel[1])

    def common(small, gain):
        lines = jnp.zeros((head_axis, chunk), F32)
        lines = lax.dynamic_update_slice(lines, gain[0:1], (h, 0))
        return jnp.concatenate([small[:taps, channels:].reshape(-1), lines.reshape(-1)])

    by_all = lax.psum(
        jnp.stack([common(bw0[5], gain0), common(bw1[5], gain1)]), ("section", "seq", "head")
    )
    by_all = pick(first, by_all[0], by_all[1])
    place = z * head_axis + h
    conv_g = by_all[: taps * shared].reshape(taps, shared)
    conv_part = shared // (seq * head_axis)
    gain_part = width // (seq * head_axis)
    return (
        section_out,
        input_grad,
        lax.dynamic_slice_in_dim(by_all[taps * shared :], place * gain_part, gain_part, 0)[None],
        gate_g[None],
        inner_g[None],
        shared_sum[None],
        by_channel[:taps][None],
        lax.dynamic_slice_in_dim(conv_g, place * conv_part, conv_part, 1)[None],
        jnp.sum(by_channel[taps + 1].reshape(heads_dev, sz.head_width), axis=1)[None],
        by_channel[taps][None],
        jnp.transpose(out_g)[None],
    )


def solution(mesh):
    placed = (
        P(None, "seq", None),
        P(),
        P("section", None, "head", "seq"),
        P(None, "seq", None),
        P("section", None),
        P("section", None, "head"),
        P("section", None, "head"),
        P("section", None, None),
        P("section", None, "head"),
        P("section", None, None),
        P("section", "head"),
        P("section", "head"),
        P("section", None, None),
    )
    return jax.shard_map(
        per_device,
        mesh=mesh,
        in_specs=placed,
        out_specs=(
            P("section", None, "seq", "head"),
            P("section", None, "seq", "head"),
            P("section", ("seq", "head")),
            P("section", "seq", "head"),
            P("section", "seq", "head"),
            P("section", ("seq", "head"), None),
            P("section", None, "head"),
            P("section", None, ("seq", "head")),
            P("section", "head"),
            P("section", "head"),
            P("section", "head", "seq"),
        ),
        check_vma=False,
    )
```

```python
import functools

import jax
import jax.numpy as jnp
from jax import lax
from jax.experimental import pallas as pl
from jax.experimental.pallas import tpu as pltpu
from jax.sharding import PartitionSpec as P

BLOCK = 256
HALF = BLOCK // 2
PAD = 16
EPS = 1e-05
F32 = jnp.float32
LOW = jnp.bfloat16
HIDDEN = -1e30
NN = ((1,), (0,))
NT = ((1,), (1,))
TN = ((0,), (0,))
VMEM_BYTES = 50 * 1024 * 1024


def dot(a, b, dims):
    return lax.dot_general(a, b, (dims, ((), ())), preferred_element_type=F32)


def aligned(start, size):
    return pl.ds(pl.multiple_of(start, size), size)


def spread(cols, first, count, width):
    rows = cols.shape[0]
    lane = lax.broadcasted_iota(jnp.int32, (rows, count * width), 1)
    out = jnp.broadcast_to(cols[:, first : first + 1], (rows, count * width))
    for h in range(1, count):
        out = jnp.where(lane >= h * width, cols[:, first + h : first + h + 1], out)
    return out


def per_head(array, h, width):
    lane = lax.broadcasted_iota(jnp.int32, array.shape, 1)
    inside = (lane >= h * width) & (lane < (h + 1) * width)
    return jnp.where(inside, array, jnp.zeros_like(array))


def split_low(value):
    high = value.astype(LOW).astype(F32)
    return high, value - high


def column_of(row, size):
    return jnp.transpose(jnp.broadcast_to(row, (128, size)))


def sigmoid(v):
    return 0.5 * jnp.tanh(0.5 * v) + 0.5


def pick(flag, a, b):
    return jnp.where(flag, a, b)


class Sizes:
    def __init__(self, blocks, width, channels, heads, states, taps, head_axis, inner):
        self.blocks = blocks
        self.width = width
        self.channels = channels
        self.heads = heads
        self.head_width = channels // heads
        self.states = states
        self.lin = channels + 2 * states
        self.taps = taps
        self.head_axis = head_axis
        self.chunk = width // head_axis
        self.rows = blocks * HALF
        self.tokens = blocks * BLOCK
        self.inner = inner


def weight_copies(sz, layer, c, h, raw, got, wv, ov, sems):
    gate, inner, shared, out = raw
    ch = sz.channels
    cols = aligned(c * ch, ch)
    rows = aligned((h * 2 + c) * ch, ch)
    own = [
        (gate.at[0, :, cols], wv.at[:, :ch]),
        (inner.at[0, :, cols], wv.at[:, ch : 2 * ch]),
        (shared.at[0], wv.at[:, 2 * ch :]),
        (out.at[0, rows, :], ov),
    ]
    sent = [(got[0], wv), (got[1], ov)]
    return [
        (c == layer, [pltpu.make_async_copy(p, q, sems.at[i]) for i, (p, q) in enumerate(own)]),
        (c != layer, [pltpu.make_async_copy(p, q, sems.at[i]) for i, (p, q) in enumerate(sent)]),
    ]


def run_copies(choices, start, wait):
    for flag, copies in choices:

        @pl.when(flag)
        def _(copies=copies):
            if start:
                for copy in copies:
                    copy.start()
            if wait:
                for copy in copies:
                    copy.wait()


def put_ordered(sz, dst, c, k, b, own, other):
    for r in range(len(own)):

        @pl.when(lax.rem(k - b + len(own), len(own)) == r)
        def _(r=r):
            put_pair(dst, c, own[r][...], other[r][...])


def put_pair(dst, c, own, other):
    dst[aligned(c * HALF, HALF), :] = own
    dst[aligned((1 - c) * HALF, HALF), :] = other


def put_pieces(sz, dst, c, h, own, other):
    for d in range(sz.head_axis):
        cols = aligned((h ^ d) * sz.chunk, sz.chunk)
        dst[aligned(c * HALF, HALF), cols] = own[d]
        dst[aligned((1 - c) * HALF, HALF), cols] = other[d]


def put_parts(sz, b, c, h, part, keep, send):
    for d in range(sz.head_axis):
        cols = aligned((h ^ d) * sz.chunk, sz.chunk)
        keep[d, aligned(b * HALF, HALF), :] = part[aligned(c * HALF, HALF), cols]
        send[d, aligned(b * HALF, HALF), :] = part[aligned((1 - c) * HALF, HALF), cols]


def put_scalars(b, c, row, kept, sent):
    for scratch, flag in ((kept, c == 0), (sent, c != 0)):
        high, low = split_low(pick(flag, row[:, :HALF], row[:, HALF:]))
        line = lax.broadcasted_iota(jnp.int32, scratch.shape, 0)
        lower = jnp.where(line == 8 + b, low, scratch[...])
        scratch[...] = jnp.where(line == b, high, lower)


def line_of(table, at):
    line = lax.broadcasted_iota(jnp.int32, table.shape, 0)
    return jnp.sum(jnp.where(line == at, table, 0.0), axis=0, keepdims=True)


def close_parts(sz, keep, send, kept, sent):
    for scratch, out in ((kept, keep), (sent, send)):
        extra = jnp.concatenate([scratch[...]] * (sz.chunk // HALF), axis=1).astype(LOW)
        for d in range(sz.head_axis):
            out[d, sz.rows :, :] = extra


def conv_forward(sz, ext, taps):
    pre = taps[0:1] * ext[5 : 5 + BLOCK, :]
    for j in range(1, sz.taps):
        pre = pre + taps[j : j + 1] * ext[5 + j : 5 + j + BLOCK, :]
    return pre


def decay_of(sz, cols, rp, h, mask):
    rows = cols[:, h : h + 1] + rp[12 + h : 13 + h, :]
    return jnp.exp(jnp.where(mask, rows, HIDDEN))


def lower_mask():
    t = lax.broadcasted_iota(jnp.int32, (BLOCK, BLOCK), 0)
    s = lax.broadcasted_iota(jnp.int32, (BLOCK, BLOCK), 1)
    return t >= s


def forward_kernel(sz, layer, slots, sc, *refs):
    n = sz.head_axis
    sources = 2 * slots if layer == 0 else 2 * n + 2 * slots
    src, refs = refs[:sources], refs[sources:]
    tables, gains, raw, got, halo, begin = (
        refs[0:2], refs[2:4], refs[4:8], refs[8:10], refs[10], refs[11],
    )
    normed_o, gl_o, lin_o, ssd_o, inc_o, inv_o, part_o, keep, send, fin_o, sc_o, base_o = refs[12:24]
    refs = refs[24:]
    if layer == 1:
        mixed_o, refs = refs[0], refs[1:]
    xs, ms, wv, ov, ext, state, kept, sent, part, sems = refs
    b = pl.program_id(0)
    c, h, k = sc[0], sc[1], sc[3]
    ch, st = sz.channels, sz.states
    copies = weight_copies(sz, layer, c, h, raw, got, wv, ov, sems)

    @pl.when(b == 0)
    def _():
        run_copies(copies, True, False)
        ext[0:8, :] = halo[...]
        state[...] = begin[...]
        kept[...] = jnp.zeros_like(kept)
        sent[...] = jnp.zeros_like(sent)
        for i in range(4):
            sc_o[i] = sc[i]

    mine = aligned(c * HALF, HALF)
    cols = aligned(h * sz.chunk, sz.chunk)
    if layer == 0:
        put_ordered(sz, xs, c, k, b, src[:slots], src[slots:])
        base_o[...] = xs[mine, cols]
    else:
        put_pieces(sz, xs, c, h, [r[...] for r in src[:n]], [r[...] for r in src[n : 2 * n]])
        put_ordered(sz, ms, c, k, b, src[2 * n : 2 * n + slots], src[2 * n + slots :])
        base_o[...] = ms[mine, cols]
        mixed_o[...] = ms[...]

    pv = pick(c == layer, gains[0][...], gains[1][...])
    rp = pick(c == layer, tables[0][...], tables[1][...])
    x = xs[...].astype(F32)
    inv_in = lax.rsqrt(jnp.mean(x * x, axis=1, keepdims=True) + EPS)
    normed = (x * inv_in * pv[0:1, : sz.width]).astype(LOW)
    normed_o[...] = normed

    @pl.when(b == 0)
    def _():
        run_copies(copies, False, True)

    proj = dot(normed, wv[...], NN)
    gl = proj[:, :ch]
    gl_o[...] = gl
    lin = proj[:, ch:].astype(LOW)
    lin_o[...] = lin
    ext[8 : 8 + BLOCK, :] = lin.astype(F32)
    pre = conv_forward(sz, ext, pv[1:5, : sz.lin])
    ext[0:8, :] = ext[BLOCK : BLOCK + 8, :]
    act = (pre * sigmoid(pre)).astype(LOW)
    values, bm, cm = act[:, :ch], act[:, ch : ch + st], act[:, ch + st :]

    cols = jnp.transpose(rp)
    mask = lower_mask()
    gram = dot(cm, bm, NT)
    mixes, parts = [], []
    for i in range(sz.heads):
        mixes.append((gram * decay_of(sz, cols, rp, i, mask)).astype(LOW))
        parts.append(per_head(values, i, sz.head_width))
    intra = dot(jnp.concatenate(mixes, axis=1), jnp.concatenate(parts, axis=0), NN)

    low_state = state[...].astype(LOW)
    inc_o[0] = low_state
    ecum = spread(cols, sz.heads, sz.heads, sz.head_width)
    inter = dot(cm, low_state, NT) * ecum
    vf = values.astype(F32)
    carried = (vf * spread(cols, 2 * sz.heads, sz.heads, sz.head_width)).astype(LOW)
    local = dot(carried, bm, TN)
    for i in range(sz.heads):
        rows = slice(i * sz.head_width, (i + 1) * sz.head_width)
        total = cols[BLOCK - 1 : BLOCK, sz.heads + i : sz.heads + i + 1]
        state[rows, :] = total * state[rows, :] + local[rows]
    ssd = intra + inter + pv[6:7, :ch] * vf
    ssd_o[...] = ssd
    gated = ssd * (gl * sigmoid(gl))
    weighty = gated * pv[5:6, :ch]
    part[...] = dot(weighty.astype(LOW), ov[...], NN).astype(LOW)

    lane = lax.broadcasted_iota(jnp.int32, (BLOCK, 128), 1)
    square = jnp.sum(gated * gated, axis=1, keepdims=True)
    if layer == 0:
        project = jnp.zeros_like(square)
    else:
        scaled_grad = dot(ms[...], ov[...], NT)
        project = jnp.sum(scaled_grad * weighty, axis=1, keepdims=True)
    stats = jnp.where(lane == 0, square, jnp.where(lane == 1, project, inv_in))
    stats = jnp.transpose(stats)
    part_o[...] = stats[0:2, :]
    inv_o[...] = stats[2:3, :]
    put_scalars(b, c, stats[0:1, :], kept, sent)
    put_parts(sz, b, c, h, part, keep, send)

    @pl.when(b == sz.blocks - 1)
    def _():
        close_parts(sz, keep, send, kept, sent)
        fin_o[...] = state[...]


def backward_kernel(sz, layer, sc, *refs):
    n = sz.head_axis
    sources = 2 * n + 2 if layer == 0 else 1 + n
    src, refs = refs[:sources], refs[sources:]
    normed_r, gl_r, lin_r, ssd_r, inc_r = refs[:5]
    tables, gains, raw, got, halo, halo_grad, begin = (
        refs[5:7], refs[7:9], refs[9:13], refs[13:15], refs[15], refs[16], refs[17],
    )
    keep, send, cat_o, scaled_o, small_o, fin_o, rim_o = refs[18:25]
    refs = refs[25:]
    if layer == 0:
        mixed_o, refs = refs[0], refs[1:]
    ms, wv, ov, ext, back, state, kept, sent, part, heads_p, small, wide, sems = refs
    i_step = pl.program_id(0)
    b = sz.blocks - 1 - i_step
    c, h = sc[0], sc[1]
    ch, st = sz.channels, sz.states
    copies = weight_copies(sz, layer, c, h, raw, got, wv, ov, sems)
    pv = pick(c == layer, gains[0][...], gains[1][...])
    rp = pick(c == layer, tables[0][...], tables[1][...])

    @pl.when(i_step == 0)
    def _():
        run_copies(copies, True, True)
        back[BLOCK : BLOCK + 8, :] = halo_grad[...]
        state[...] = begin[...]
        kept[...] = jnp.zeros_like(kept)
        sent[...] = jnp.zeros_like(sent)
        small[...] = jnp.zeros_like(small)
        wide[...] = jnp.zeros_like(wide)
        if layer == 0:
            for i in range(2):
                extra = src[i * n][sz.rows :, :].astype(F32)
                for d in range(1, n):
                    extra = extra + src[i * n + d][sz.rows :, :].astype(F32)
                heads_p[8 * i : 8 * i + 8, :] = extra[0:8, :HALF] + extra[8:16, :HALF]

    if layer == 0:
        rows = aligned(b * HALF, HALF)
        put_pieces(
            sz, ms, c, h, [r[rows, :] for r in src[:n]], [r[rows, :] for r in src[n : 2 * n]]
        )
        halves = []
        for k in range(2):
            alpha = lax.rsqrt(line_of(src[2 * n + k][...], b) / sz.inner + EPS)
            beta = alpha * alpha * line_of(heads_p[...], 8 * k + b) / sz.inner
            halves.append((alpha, beta))
        alpha, beta = (
            pick(
                c == 0,
                jnp.concatenate([halves[0][q], halves[1][q]], axis=1),
                jnp.concatenate([halves[1][q], halves[0][q]], axis=1),
            )
            for q in range(2)
        )
    else:
        stats = src[1][...]
        for d in range(1, n):
            stats = stats + src[1 + d][...]
        alpha = lax.rsqrt(stats[0:1, :] / sz.inner + EPS)
        beta = alpha * alpha * alpha * stats[1:2, :] / sz.inner

    sub = lax.broadcasted_iota(jnp.int32, rp.shape, 0)
    cols = jnp.transpose(jnp.where(sub == 12, alpha, jnp.where(sub == 13, beta, rp)))
    alpha, beta = cols[:, 12:13], cols[:, 13:14]

    gl = gl_r[...]
    ssd = ssd_r[...]
    sig = sigmoid(gl)
    swish = gl * sig
    slope = sig * (1.0 + gl * (1.0 - sig))
    gated = ssd * swish
    if layer == 0:
        mixed_grad = ms[...]
        mixed_o[...] = mixed_grad
    else:
        mixed_grad = src[0][...]
    scaled_grad = dot(mixed_grad, ov[...], NT)
    gain = pv[5:6, :ch]
    normal = gated * alpha
    small[4:5, :ch] += jnp.sum(scaled_grad * normal, axis=0, keepdims=True)
    scaled_o[...] = (normal * gain).astype(LOW)
    gated_grad = alpha * (scaled_grad * gain) - beta * gated
    ssd_grad = (gated_grad * swish).astype(LOW)
    gate_grad = (gated_grad * ssd * slope).astype(LOW)
    sgf = ssd_grad.astype(F32)

    before = lin_r[pl.ds(pl.multiple_of(jnp.maximum(b * BLOCK - 16, 0), 16), 16), :]
    ext[0:8, :] = pick(b > 0, before.astype(F32)[8:16, :], halo[...])
    ext[8 : 8 + BLOCK, :] = lin_r[aligned(b * BLOCK, BLOCK), :].astype(F32)
    taps = pv[1:5, : sz.lin]
    pre = conv_forward(sz, ext, taps)
    psig = sigmoid(pre)
    pact = pre * psig
    pslope = psig * (1.0 + pre * (1.0 - psig))
    act = pact.astype(LOW)
    values, bm, cm = act[:, :ch], act[:, ch : ch + st], act[:, ch + st :]
    vf = values.astype(F32)
    small[5:6, :ch] += jnp.sum(sgf * vf, axis=0, keepdims=True)

    mask = lower_mask()
    gram = dot(cm, bm, NT)
    gram_grad = jnp.zeros((BLOCK, BLOCK), F32)
    mixes, parts = [], []
    for i in range(sz.heads):
        decay = decay_of(sz, cols, rp, i, mask)
        mixes.append((gram * decay).astype(LOW))
        parts.append(per_head(ssd_grad, i, sz.head_width))
        gram_grad = gram_grad + dot(parts[-1], values, NT) * decay
    intra_grad = dot(jnp.concatenate(mixes, axis=0), jnp.concatenate(parts, axis=0), TN)

    ecum = spread(cols, sz.heads, sz.heads, sz.head_width)
    to_end = spread(cols, 2 * sz.heads, sz.heads, sz.head_width)
    inter_grad = (sgf * ecum).astype(LOW)
    low_state = state[...].astype(LOW)
    carried = (vf * to_end).astype(LOW)
    carried_grad = dot(bm, low_state, NT)
    gram_low = gram_grad.astype(LOW)
    b_grad = dot(gram_low, cm, TN) + dot(carried, low_state, NN)
    c_grad = dot(gram_low, bm, NN) + dot(inter_grad, inc_r[0], NN)
    value_grad = intra_grad + pv[6:7, :ch] * sgf + carried_grad * to_end
    entry = dot(inter_grad, cm, TN)
    for i in range(sz.heads):
        rows = slice(i * sz.head_width, (i + 1) * sz.head_width)
        total = cols[BLOCK - 1 : BLOCK, sz.heads + i : sz.heads + i + 1]
        state[rows, :] = total * state[rows, :] + entry[rows]

    pre_grad = jnp.concatenate([value_grad, b_grad, c_grad], axis=1) * pslope
    back[0:BLOCK, :] = pre_grad
    lin_grad = taps[0:1] * back[sz.taps - 1 : sz.taps - 1 + BLOCK, :]
    for j in range(1, sz.taps):
        at = sz.taps - 1 - j
        lin_grad = lin_grad + taps[j : j + 1] * back[at : at + BLOCK, :]
    for j in range(sz.taps):
        small[j : j + 1, :] += jnp.sum(pre_grad * ext[5 + j : 5 + j + BLOCK, :], axis=0, keepdims=True)
    back[BLOCK : BLOCK + 8, :] = back[0:8, :]
    cat = jnp.concatenate([gate_grad, lin_grad.astype(LOW)], axis=1)
    cat_o[...] = cat
    normed_grad = dot(cat, wv[...], NT)
    part[...] = normed_grad.astype(LOW)
    product = normed_grad * normed_r[...].astype(F32)
    wide[0:1, :] += jnp.sum(product, axis=0, keepdims=True)
    along = jnp.sum(product, axis=1, keepdims=True)
    along = jnp.transpose(jnp.broadcast_to(along, (BLOCK, 128)))
    put_scalars(b, c, along[0:1, :], kept, sent)
    put_parts(sz, b, c, h, part, keep, send)

    @pl.when(i_step == sz.blocks - 1)
    def _():
        close_parts(sz, keep, send, kept, sent)
        fin_o[...] = state[...]
        rim_o[...] = back[0:8, :]
        table = small[...]
        lines = [
            jnp.concatenate([table[j : j + 1, :], table[j + 1 : j + 2, :]], axis=1)
            for j in range(0, sz.taps + 2, 2)
        ]
        lines[-1] = jnp.concatenate([table[4:5, :ch], table[5:6, :ch]] * 2, axis=1)
        lines.append(wide[0:1, :] / pv[0:1, :])
        high, low = split_low(jnp.concatenate(lines, axis=0))
        rest = jnp.zeros((PAD - 8, sz.width), F32)
        small_o[...] = jnp.concatenate([high, low, rest], axis=0).astype(LOW)


def weights_kernel(sz, sc, normed, cat, mixed, scaled, small, *outs):
    outs, full = outs[:-1], outs[-1]
    wide = cat.shape[1]
    step = sz.chunk
    for q in range(sz.head_axis):
        at = slice(q * step, (q + 1) * step)
        full[at, :wide] = dot(normed[:, at], cat[...], TN).astype(LOW)
        full[at, wide:] = dot(mixed[:, at], scaled[...], TN).astype(LOW)
    rows = sz.width // len(outs)
    for r, out in enumerate(outs):
        to = lax.rem(sc[2] + r, len(outs))
        out[:rows, :] = full[aligned(to * rows, rows), :]
        out[rows:, :] = small[...]


def join_kernel(sz, sc, keep, recv, sc_o, own, *sends):
    rows = sz.rows
    for i in range(4):
        sc_o[i] = sc[i]
    extra = keep[0, rows:, :].astype(F32) + recv[0, rows:, :].astype(F32)
    high, low = split_low(extra[0:8, :] + extra[8:16, :])
    extra = jnp.concatenate([high, low], axis=0)
    for d, out in enumerate((own,) + sends):
        out[:rows, :] = (keep[d, :rows, :].astype(F32) + recv[d, :rows, :].astype(F32)).astype(out.dtype)
        out[rows:, :] = extra.astype(out.dtype)


def total_of(parts, rows):
    total = parts[0][rows, :].astype(F32)
    for p in parts[1:]:
        total = total + p[rows, :].astype(F32)
    return total


def output_kernel(sz, layer, sc, *refs):
    n = sz.head_axis
    parts, refs = refs[:n], refs[n:]
    resid, res_o, low_o, mixed_o, square_o = refs
    extra = total_of(parts, slice(sz.rows, sz.rows + PAD))
    square = extra[0:8, :HALF] + extra[8:16, :HALF]
    square_o[...] = square
    inv = lax.rsqrt(square / sz.inner + EPS)
    for b in range(sz.blocks):
        rows = slice(b * HALF, (b + 1) * HALF)
        col = column_of(inv[b : b + 1, :], HALF)[:, 0:1]
        mixed = total_of(parts, rows) * col
        res = resid[rows, :].astype(F32) + mixed
        res_o[rows, :] = res
        low_o[rows, :] = res.astype(LOW)
        mixed_o[rows, :] = mixed


def input_kernel(sz, layer, sc, *refs):
    n = sz.head_axis
    parts, refs = refs[:n], refs[n:]
    resid, outg, inv_r, gains = refs[0], refs[1], refs[2], refs[3:5]
    refs = refs[5:]
    if layer == 1:
        mixed, refs = refs[0], refs[1:]
    grad_o, low_o, sc_o = refs
    for i in range(4):
        sc_o[i] = sc[i]
    c, h = sc[0], sc[1]
    mine = aligned(h * sz.chunk, sz.chunk)
    gain = pick(c == layer, gains[0][0:1, mine], gains[1][0:1, mine])
    extra = total_of(parts, slice(sz.rows, sz.rows + PAD))
    along = extra[0:8, :HALF] + extra[8:16, :HALF]
    tops, lows = [], []
    for b in range(sz.blocks):
        rows = slice(b * HALF, (b + 1) * HALF)
        at = b * BLOCK
        inv_row = pick(c == 0, inv_r[:, at : at + HALF], inv_r[:, at + HALF : at + BLOCK])
        inv = column_of(inv_row, HALF)[:, 0:1]
        share = column_of(along[b : b + 1, :] / sz.width, HALF)[:, 0:1]
        total = total_of(parts, rows)
        base = resid[rows, :].astype(F32)
        grad = outg[rows, :].astype(F32) + inv * (total * gain - base * (inv * share))
        grad_o[rows, :] = grad
        low = grad.astype(LOW)
        low_o[rows, :] = low
        if layer == 1:
            dots = jnp.sum(low.astype(F32) * mixed[rows, :], axis=1, keepdims=True)
            row = jnp.transpose(jnp.broadcast_to(dots, (HALF, 128)))[0:1, :]
            high, rest = split_low(row)
            tops.append(high)
            lows.append(rest)
    if layer == 1:
        fill = [jnp.zeros((8 - sz.blocks, HALF), F32)] if sz.blocks < 8 else []
        extra = jnp.concatenate(tops + fill + lows + fill, axis=0)
        extra = jnp.concatenate([extra] * (sz.chunk // HALF), axis=1)
        low_o[sz.rows :, :] = extra.astype(LOW)
    else:
        low_o[sz.rows :, :] = jnp.zeros((PAD, sz.chunk), LOW)


def sum_kernel(sz, sc, *refs):
    count = (len(refs) - 2) // 2
    for out, parts in ((refs[-2], refs[:count]), (refs[-1], refs[count : 2 * count])):
        out[...] = total_of(parts, slice(None))


def final_kernel(sz, count, sc, *refs):
    same, other = refs[:count], refs[count : 2 * count]
    sum_a, sum_b = refs[2 * count : 2 * count + 2]
    gate_o, inner_o, out_o, conv_o, norm_o, skip_o, own_o = refs[2 * count + 2 : 2 * count + 9]
    sends, both, table = refs[2 * count + 9 : -2], refs[-2], refs[-1]
    c, h = sc[0], sc[1]
    ch, st = sz.channels, sz.states

    @pl.when(c == 0)
    def _():
        both[0] = total_of(same, slice(None))
        both[1] = total_of(other, slice(None))

    @pl.when(c != 0)
    def _():
        both[0] = sum_a[...]
        both[1] = sum_b[...]

    rows = both.shape[1] - PAD
    small = []
    lane = lax.broadcasted_iota(jnp.int32, skip_o.shape, 1)
    for i in range(2):
        to = aligned(pick(i == 0, c, 1 - c) * ch, ch)
        gate_o[:, to] = both[i, :rows, :ch]
        inner_o[:, to] = both[i, :rows, ch : 2 * ch]
        out_o[to, :] = jnp.transpose(both[i, :rows, 2 * ch + 2 * st :])
        lines = both[i, rows : rows + 4, :] + both[i, rows + 4 : rows + 8, :]
        small.append(lines)
        for j in range(sz.taps):
            at = (j % 2) * sz.lin
            conv_o[j : j + 1, to] = lines[j // 2 : j // 2 + 1, at : at + ch]
        norm_o[:, to] = lines[2:3, :ch]
        skips = lines[2:3, ch : 2 * ch]
        for q in range(sz.heads):
            part = jnp.sum(per_head(skips, q, sz.head_width), axis=1, keepdims=True)
            old = jnp.zeros(skip_o.shape, F32) if (i == 0 and q == 0) else skip_o[...]
            place = pick(i == 0, c, 1 - c) * sz.heads + q
            skip_o[...] = jnp.where(lane == place, part, old)
    common = small[0] + small[1]
    chunk = sz.chunk
    lines = [
        common[j // 2 : j // 2 + 1, (j % 2) * sz.lin + ch : (j % 2 + 1) * sz.lin]
        for j in range(sz.taps)
    ]
    lines += [common[3:4, q * chunk : (q + 1) * chunk] for q in range(sz.head_axis)]
    high, low = split_low(jnp.concatenate(lines, axis=0))
    table[...] = both[0, :rows, 2 * ch : 2 * ch + 2 * st] + both[1, :rows, 2 * ch : 2 * ch + 2 * st]
    part = rows // sz.head_axis
    for d, out in enumerate((own_o,) + tuple(sends)):
        out[:PAD, :] = jnp.concatenate([high, low], axis=0).astype(out.dtype)
        out[PAD:, :] = table[aligned((h ^ d) * part, part), :].astype(out.dtype)


def heads_kernel(sz, *refs):
    parts, shared_o, common_o = refs[: sz.head_axis], refs[-2], refs[-1]
    shared_o[...] = total_of(parts, slice(PAD, None))
    lines = total_of(parts, slice(0, PAD))
    common_o[...] = lines[0:8, :] + lines[8:16, :]


def slice_kernel(sz, slots, with_rates, sc, order, *refs):
    sources = 2 if with_rates else 1
    src, outs, sc_o, sems = refs[:sources], refs[sources:-2], refs[-2], refs[-1]
    copies = []
    for r in range(slots):
        which = order[lax.rem(sc[3] + r, slots)]
        rows = src[0].at[which, aligned(sc[0] * HALF, HALF), :]
        copies.append(pltpu.make_async_copy(rows, outs[r], sems.at[len(copies)]))
        if with_rates:
            rates = src[1].at[0, which]
            copies.append(pltpu.make_async_copy(rates, outs[slots + r], sems.at[len(copies)]))
    for copy in copies:
        copy.start()
    for i in range(4):
        sc_o[i] = sc[i]
    for copy in copies:
        copy.wait()


def pack_kernel(sz, sc, gate, inner, shared, out, in_gain, conv_i, conv_s, skip, norm, *refs):
    w_o, o_o, mine_o, send_o, sems = refs
    c, h = sc[0], sc[1]
    ch = sz.channels
    cols = aligned((1 - c) * ch, ch)
    rows = aligned((h * 2 + 1 - c) * ch, ch)
    copies = [
        pltpu.make_async_copy(gate.at[0, :, cols], w_o.at[:, :ch], sems.at[0]),
        pltpu.make_async_copy(inner.at[0, :, cols], w_o.at[:, ch : 2 * ch], sems.at[1]),
        pltpu.make_async_copy(shared.at[0], w_o.at[:, 2 * ch :], sems.at[2]),
        pltpu.make_async_copy(out.at[0, rows, :], o_o, sems.at[3]),
    ]
    for copy in copies:
        copy.start()
    for which, ref in ((c, mine_o), (1 - c, send_o)):
        at = aligned(which * ch, ch)
        ref[...] = jnp.zeros_like(ref)
        ref[0:1, :] = in_gain[...]
        ref[1 : 1 + sz.taps, :ch] = conv_i[0, :, at]
        ref[1 : 1 + sz.taps, ch : sz.lin] = conv_s[0]
        ref[5:6, :ch] = norm[:, at]
        low = spread(skip[...], 0, sz.heads, sz.head_width)
        high = spread(skip[...], sz.heads, sz.heads, sz.head_width)
        ref[6:7, :ch] = pick(which == 0, low, high)
    for copy in copies:
        copy.wait()


def rates_kernel(sz, slots, sc, *refs):
    pieces, mine_o, send_o = refs[:slots], refs[slots], refs[slots + 1]
    n = sz.heads
    for r in range(slots):
        rate = pieces[r][...]
        lane = lax.broadcasted_iota(jnp.int32, rate.shape, 1)
        cum = rate
        step = 1
        while step < BLOCK:
            cum = cum + jnp.where(lane >= step, pltpu.roll(cum, step, 1), 0.0)
            step *= 2
        end = cum[:, BLOCK - 1 :]
        lines = [cum, jnp.exp(cum), jnp.exp(end - cum) * -rate, jnp.log(-rate) - cum]
        low = jnp.concatenate([v[:n] for v in lines], axis=0)
        high = jnp.concatenate([v[n:] for v in lines], axis=0)
        at = aligned(lax.rem(sc[3] - r + slots, slots) * BLOCK, BLOCK)
        mine_o[:, at] = pick(sc[0] == 0, low, high)
        send_o[:, at] = pick(sc[0] == 0, high, low)


def home_kernel(slots, sc, *refs):
    pieces, out = refs[:slots], refs[slots]
    for r in range(slots):
        out[lax.rem(sc[3] - r + slots, slots)] = pieces[r][...].astype(F32)


def whole(shape):
    return pl.BlockSpec(shape, lambda *_: (0,) * len(shape))


def per_device(
    tokens,
    slot_order,
    log_decay,
    grad_out,
    in_gain,
    w_gate,
    w_inner,
    w_shared,
    conv_inner,
    conv_shared,
    d_skip,
    norm_gain,
    w_out,
):
    slots = tokens.shape[0]
    span = tokens.shape[1]
    width = tokens.shape[2]
    seq = lax.axis_size("seq")
    head_axis = lax.axis_size("head")
    cores = lax.axis_size("section")
    spans = seq // slots
    c = lax.axis_index("section")
    z = lax.axis_index("seq")
    h = lax.axis_index("head")
    k = lax.rem(z, slots)
    inner_dev = w_gate.shape[2]
    channels = inner_dev // cores
    shared = w_shared.shape[2]
    heads_dev = d_skip.shape[1]
    taps = conv_inner.shape[1]
    sz = Sizes(
        slots * span // BLOCK,
        width,
        channels,
        heads_dev // cores,
        shared // 2,
        taps,
        head_axis,
        inner_dev * head_axis,
    )
    first = c == 0
    swap = [(0, 1), (1, 0)]
    nb, tok, rows, chunk = sz.blocks, sz.tokens, sz.rows, sz.chunk

    def cross(x):
        return lax.ppermute(x, "section", swap)

    def turn(x, r):
        pairs = [(i, i // slots * slots + (i % slots + r) % slots) for i in range(seq)]
        return lax.ppermute(x, "seq", pairs) if r else x

    def over_heads(x, d):
        return lax.ppermute(x, "head", [(i, i ^ d) for i in range(head_axis)])

    def next_span(x, way):
        pairs = [(i, i + way * slots) for i in range(seq) if 0 <= i + way * slots < seq]
        return lax.ppermute(x, "seq", pairs)

    def shape(dims, dtype):
        return jax.ShapeDtypeStruct(dims, dtype)

    prefetch = functools.partial(pltpu.PrefetchScalarGridSpec, num_scalar_prefetch=1)
    options = pltpu.CompilerParams(vmem_limit_bytes=VMEM_BYTES)
    anywhere = pl.BlockSpec(memory_space=pl.ANY)
    smem = pl.BlockSpec(memory_space=pltpu.SMEM)
    vmem = pl.BlockSpec(memory_space=pltpu.VMEM)
    index_shape = shape((4,), jnp.int32)

    def cost(flops, moved):
        return pl.CostEstimate(flops=int(flops), bytes_accessed=int(moved), transcendentals=0)

    def take_rows(sc, source, rates):
        given = [source] if rates is None else [source, rates]
        outs = [shape((HALF, width), LOW)] * slots
        if rates is not None:
            outs = outs + [shape((heads_dev, span), F32)] * slots
        got = pl.pallas_call(
            functools.partial(slice_kernel, sz, slots, rates is not None),
            in_specs=[smem, smem] + [anywhere] * len(given),
            out_specs=[anywhere] * len(outs) + [smem],
            out_shape=outs + [index_shape],
            scratch_shapes=[pltpu.SemaphoreType.DMA((len(outs),))],
            compiler_params=options,
        )(sc, slot_order, *given)
        own = [turn(got[r], r) for r in range(slots)]
        return own, got[slots:-1], got[-1]

    sc = jnp.stack([c, h, z, k]).astype(jnp.int32)
    tok_own, rate_parts, sc = take_rows(sc, tokens, log_decay)
    tok_other = [cross(x) for x in tok_own]

    wide = 2 * channels + shared
    w_sent, o_sent, pv_mine, pv_sent = pl.pallas_call(
        functools.partial(pack_kernel, sz),
        in_specs=[smem] + [anywhere] * 4 + [vmem] * 5,
        out_specs=[anywhere, anywhere, vmem, vmem],
        out_shape=[
            shape((width, wide), LOW),
            shape((channels, width), LOW),
            shape((16, width), F32),
            shape((16, width), F32),
        ],
        scratch_shapes=[pltpu.SemaphoreType.DMA((4,))],
        compiler_params=options,
    )(sc, w_gate, w_inner, w_shared, w_out, in_gain, conv_inner, conv_shared, d_skip, norm_gain)
    raw = [w_gate, w_inner, w_shared, w_out]
    sent = [cross(w_sent), cross(o_sent)]
    gains = [pv_mine, cross(pv_sent)]

    tab_mine, tab_sent = pl.pallas_call(
        functools.partial(rates_kernel, sz, slots),
        in_specs=[smem] + [vmem] * slots,
        out_shape=[shape((16, tok), F32)] * 2,
        compiler_params=options,
    )(sc, *[turn(x, r) for r, x in enumerate(rate_parts)])
    tables = [tab_mine, cross(tab_sent)]

    def span_total(layer):
        table = pick(c == layer, tables[0], tables[1])[: sz.heads, BLOCK - 1 :: BLOCK]
        return jnp.repeat(jnp.exp(jnp.sum(table, axis=1)), sz.head_width)[:, None]

    parts_shape = shape((head_axis, rows + PAD, chunk), LOW)
    weight_specs = [anywhere] * 6
    weight_scratch = [pltpu.VMEM((width, wide), LOW), pltpu.VMEM((channels, width), LOW)]
    dense = 2 * tok * width * (wide + channels)

    def forward(layer, sc, sources):
        def at(b, _):
            return (b, 0)

        piece = pl.BlockSpec((HALF, chunk), at)
        ordered = [whole((HALF, width))] * (2 * slots)
        src_specs = ordered if layer == 0 else [piece] * (2 * head_axis) + ordered
        mixed_spec = [] if layer == 0 else [pl.BlockSpec((BLOCK, width), at)]
        mixed_shape = [] if layer == 0 else [shape((tok, width), LOW)]
        table = pl.BlockSpec((16, BLOCK), lambda b, _: (0, b))

        def call(halo, begin):
            return pl.pallas_call(
                functools.partial(forward_kernel, sz, layer, slots),
                grid_spec=prefetch(
                    grid=(nb,),
                    in_specs=src_specs
                    + [table, table, whole((16, width)), whole((16, width))]
                    + weight_specs
                    + [whole((8, sz.lin)), whole((channels, sz.states))],
                    out_specs=[
                        pl.BlockSpec((BLOCK, width), at),
                        pl.BlockSpec((BLOCK, channels), at),
                        pl.BlockSpec((BLOCK, sz.lin), at),
                        pl.BlockSpec((BLOCK, channels), at),
                        pl.BlockSpec((1, channels, sz.states), lambda b, _: (b, 0, 0)),
                        pl.BlockSpec((1, BLOCK), lambda b, _: (0, b)),
                        pl.BlockSpec((2, BLOCK), lambda b, _: (0, b)),
                        whole(parts_shape.shape),
                        whole(parts_shape.shape),
                        whole((channels, sz.states)),
                        smem,
                        piece,
                    ]
                    + mixed_spec,
                    scratch_shapes=[
                        pltpu.VMEM((BLOCK, width), LOW),
                        pltpu.VMEM((BLOCK, width), LOW),
                        *weight_scratch,
                        pltpu.VMEM((BLOCK + 8, sz.lin), F32),
                        pltpu.VMEM((channels, sz.states), F32),
                        pltpu.VMEM((PAD, HALF), F32),
                        pltpu.VMEM((PAD, HALF), F32),
                        pltpu.VMEM((BLOCK, width), LOW),
                        pltpu.SemaphoreType.DMA((4,)),
                    ],
                ),
                out_shape=[
                    shape((tok, width), LOW),
                    shape((tok, channels), F32),
                    shape((tok, sz.lin), LOW),
                    shape((tok, channels), F32),
                    shape((nb, channels, sz.states), LOW),
                    shape((1, tok), F32),
                    shape((2, tok), F32),
                    parts_shape,
                    parts_shape,
                    shape((channels, sz.states), F32),
                    index_shape,
                    shape((rows, chunk), LOW),
                ]
                + mixed_shape,
                compiler_params=options,
                cost_estimate=cost(6 * dense, 16e6),
            )(sc, *sources, *tables, *gains, *raw, *sent, halo, begin)

        halo = jnp.zeros((8, sz.lin), F32)
        begin = jnp.zeros((channels, sz.states), F32)
        if spans == 1:
            return call(halo, begin), halo
        halo = next_span(call(halo, begin)[2][tok - 8 :].astype(F32), 1)
        local = call(halo, begin)[9]
        for _ in range(spans - 1):
            begin = next_span(span_total(layer) * begin + local, 1)
        return call(halo, begin), halo

    def backward(layer, sc, sources, saved, halo):
        def at(i, _):
            return (nb - 1 - i, 0)

        if layer == 0:
            src_specs = [whole(s.shape) for s in sources]
        else:
            stat = pl.BlockSpec((2, BLOCK), lambda i, _: (0, nb - 1 - i))
            src_specs = [pl.BlockSpec((BLOCK, width), at)] + [stat] * head_axis
        normed, gl, lin, ssd, inc = saved
        mixed_spec = [pl.BlockSpec((BLOCK, width), at)] if layer == 0 else []
        mixed_shape = [shape((tok, width), LOW)] if layer == 0 else []
        table = pl.BlockSpec((16, BLOCK), lambda i, _: (0, nb - 1 - i))

        def call(halo_grad, begin):
            return pl.pallas_call(
                functools.partial(backward_kernel, sz, layer),
                grid_spec=prefetch(
                    grid=(nb,),
                    in_specs=src_specs
                    + [
                        pl.BlockSpec((BLOCK, width), at),
                        pl.BlockSpec((BLOCK, channels), at),
                        whole(lin.shape),
                        pl.BlockSpec((BLOCK, channels), at),
                        pl.BlockSpec((1, channels, sz.states), lambda i, _: (nb - 1 - i, 0, 0)),
                        table,
                        table,
                        whole((16, width)),
                        whole((16, width)),
                        *weight_specs,
                        whole((8, sz.lin)),
                        whole((8, sz.lin)),
                        whole((channels, sz.states)),
                    ],
                    out_specs=[
                        whole(parts_shape.shape),
                        whole(parts_shape.shape),
                        pl.BlockSpec((BLOCK, wide), at),
                        pl.BlockSpec((BLOCK, channels), at),
                        whole((PAD, width)),
                        whole((channels, sz.states)),
                        whole((8, sz.lin)),
                    ]
                    + mixed_spec,
                    scratch_shapes=[
                        pltpu.VMEM((BLOCK, width), LOW),
                        *weight_scratch,
                        pltpu.VMEM((BLOCK + 8, sz.lin), F32),
                        pltpu.VMEM((BLOCK + 8, sz.lin), F32),
                        pltpu.VMEM((channels, sz.states), F32),
                        pltpu.VMEM((PAD, HALF), F32),
                        pltpu.VMEM((PAD, HALF), F32),
                        pltpu.VMEM((BLOCK, width), LOW),
                        pltpu.VMEM((PAD, HALF), F32),
                        pltpu.VMEM((8, sz.lin), F32),
                        pltpu.VMEM((8, width), F32),
                        pltpu.SemaphoreType.DMA((4,)),
                    ],
                ),
                out_shape=[
                    parts_shape,
                    parts_shape,
                    shape((tok, wide), LOW),
                    shape((tok, channels), LOW),
                    shape((PAD, width), LOW),
                    shape((channels, sz.states), F32),
                    shape((8, sz.lin), F32),
                ]
                + mixed_shape,
                compiler_params=options,
                cost_estimate=cost(8 * dense, 16e6),
            )(
                sc, *sources, normed, gl, lin, ssd, inc, *tables, *gains, *raw, *sent,
                halo, halo_grad, begin,
            )

        halo_grad = jnp.zeros((8, sz.lin), F32)
        begin = jnp.zeros((channels, sz.states), F32)
        if spans == 1:
            return call(halo_grad, begin)
        local = call(halo_grad, begin)[5]
        for _ in range(spans - 1):
            begin = next_span(span_total(layer) * begin + local, -1)
        halo_grad = next_span(call(halo_grad, begin)[6], -1)
        return call(halo_grad, begin)

    def scatter(sc, keep, send):
        joined = pl.pallas_call(
            functools.partial(join_kernel, sz),
            in_specs=[smem, vmem, vmem],
            out_specs=[smem] + [vmem] * head_axis,
            out_shape=[index_shape, shape((rows + PAD, chunk), F32)]
            + [shape((rows + PAD, chunk), LOW)] * (head_axis - 1),
            compiler_params=options,
        )(sc, keep, cross(send))
        return [joined[1]] + [over_heads(joined[1 + d], d) for d in range(1, head_axis)], joined[0]

    def gather(low):
        own = [low] + [over_heads(low, d) for d in range(1, head_axis)]
        return own + [cross(x) for x in own]

    def section_output(layer, sc, parts, resid):
        return pl.pallas_call(
            functools.partial(output_kernel, sz, layer),
            in_specs=[smem] + [vmem] * (head_axis + 1),
            out_shape=[
                shape((rows, chunk), F32),
                shape((rows, chunk), LOW),
                shape((rows, chunk), F32),
                shape((8, HALF), F32),
            ],
            compiler_params=options,
        )(sc, *parts, resid)

    def section_input(layer, sc, parts, *others):
        return pl.pallas_call(
            functools.partial(input_kernel, sz, layer),
            in_specs=[smem] + [vmem] * (head_axis + len(others)),
            out_specs=[vmem, vmem, smem],
            out_shape=[
                shape((rows, chunk), F32),
                shape((rows + PAD, chunk), LOW),
                index_shape,
            ],
            compiler_params=options,
        )(sc, *parts, *others)

    part = width // seq

    def weight_pieces(layer, sc, normed, cat, mixed, scaled, small):
        columns = wide + channels
        chunks = pl.pallas_call(
            functools.partial(weights_kernel, sz),
            in_specs=[smem] + [vmem] * 5,
            out_shape=[shape((part + PAD, columns), LOW)] * seq,
            scratch_shapes=[pltpu.VMEM((width, columns), LOW)],
            compiler_params=options,
            cost_estimate=cost(4 * dense, 12e6),
        )(sc, normed, cat, mixed, scaled, small)
        same, other = [chunks[0]], []
        for r in range(seq):
            for source in range(cores):
                if source == layer and r == 0:
                    continue
                pairs = [(source * seq + i, layer * seq + (i + r) % seq) for i in range(seq)]
                got = lax.ppermute(chunks[r], ("section", "seq"), pairs)
                (same if source == layer else other).append(got)
        return same, other

    def to_home(one, two):
        one = one[:rows].reshape(nb, HALF, chunk)
        two = two[:rows].reshape(nb, HALF, chunk)
        mine = pick(first, one, two)
        got = cross(pick(first, two, one))
        full = jnp.concatenate([pick(first, mine, got), pick(first, got, mine)], axis=1)
        pieces = [
            turn(lax.dynamic_index_in_dim(full, lax.rem(k + r, slots), 0, False), r)
            for r in range(slots)
        ]
        return pl.pallas_call(
            functools.partial(home_kernel, slots),
            in_specs=[smem] + [vmem] * slots,
            out_shape=shape((slots, BLOCK, chunk), F32),
            compiler_params=options,
        )(sc, *pieces)[None]

    fw0, halo0 = forward(0, sc, tok_own + tok_other)
    base0 = fw0[11]
    out_own, unused, sc_late = take_rows(fw0[10], grad_out, None)
    out_other = [cross(x) for x in out_own]
    parts, sc_join = scatter(sc, fw0[7], fw0[8])
    res1, low1, mixed0, square0 = section_output(0, sc, parts, base0)
    pieces1 = gather(low1)
    square_other = cross(square0)

    fw1, halo1 = forward(1, sc, pieces1 + out_own + out_other)
    stat = fw1[6] + cross(fw1[6])
    stats = [stat] + [over_heads(stat, d) for d in range(1, head_axis)]
    parts_out, sc_out = scatter(sc, fw1[7], fw1[8])
    bw1 = backward(1, sc_out, [fw1[12]] + stats, fw1[:5], halo1)
    parts, sc_join = scatter(sc, bw1[0], bw1[1])
    same1, other1 = weight_pieces(1, sc_join, fw1[0], bw1[2], fw1[12], bw1[3], bw1[4])
    igrad1, glow1, sc_in = section_input(1, sc, parts, res1, fw1[11], fw1[5], *gains, mixed0)
    piecesg = gather(glow1)

    bw0 = backward(0, sc, piecesg + [square0, square_other], fw0[:5], halo0)
    parts, sc_join = scatter(sc, bw0[0], bw0[1])
    same0, other0 = weight_pieces(0, sc_join, fw0[0], bw0[2], bw0[7], bw0[3], bw0[4])
    igrad0, glow0, sc_end = section_input(0, sc, parts, base0, igrad1, fw0[5], *gains)

    unused, low2, unused_mixed, unused_square = section_output(1, sc_in, parts_out, res1)
    section_out = to_home(low1, low2)
    input_grad = to_home(glow0, glow1)

    piece_shape = shape((part + PAD, wide + channels), F32)
    sums1 = pl.pallas_call(
        functools.partial(sum_kernel, sz),
        in_specs=[smem] + [vmem] * (2 * seq),
        out_shape=[piece_shape] * 2,
        compiler_params=options,
    )(sc_in, *same1, *other1)
    share = part // head_axis + PAD
    final = pl.pallas_call(
        functools.partial(final_kernel, sz, seq),
        in_specs=[smem] + [vmem] * (2 * seq + 2),
        out_shape=[
            shape((part, inner_dev), F32),
            shape((part, inner_dev), F32),
            shape((inner_dev, part), F32),
            shape((taps, inner_dev), F32),
            shape((1, inner_dev), F32),
            shape((1, heads_dev), F32),
            shape((share, shared), F32),
        ]
        + [shape((share, shared), LOW)] * (head_axis - 1),
        scratch_shapes=[
            pltpu.VMEM((2, part + PAD, wide + channels), F32),
            pltpu.VMEM((part, shared), F32),
        ],
        compiler_params=options,
    )(sc, *same0, *other0, *sums1)
    shared_g, common = pl.pallas_call(
        functools.partial(heads_kernel, sz),
        in_specs=[vmem] * head_axis,
        out_shape=[shape((share - PAD, shared), F32), shape((8, shared), F32)],
        compiler_params=options,
    )(final[6], *[over_heads(final[6 + d], d) for d in range(1, head_axis)])
    place = z * head_axis + h
    conv_part = shared // (seq * head_axis)
    gain_part = width // (seq * head_axis)
    return (
        section_out,
        input_grad,
        lax.dynamic_slice_in_dim(common[taps:].reshape(-1), place * gain_part, gain_part, 0)[None],
        final[0][None],
        final[1][None],
        shared_g[None],
        final[3][None],
        lax.dynamic_slice_in_dim(common[:taps], place * conv_part, conv_part, 1)[None],
        final[5],
        final[4],
        final[2][None],
    )


def solution(mesh):
    placed = (
        P(None, "seq", None),
        P(),
        P("section", None, "head", "seq"),
        P(None, "seq", None),
        P("section", None),
        P("section", None, "head"),
        P("section", None, "head"),
        P("section", None, None),
        P("section", None, "head"),
        P("section", None, None),
        P("section", "head"),
        P("section", "head"),
        P("section", None, None),
    )
    return jax.shard_map(
        per_device,
        mesh=mesh,
        in_specs=placed,
        out_specs=(
            P("section", None, "seq", "head"),
            P("section", None, "seq", "head"),
            P("section", ("seq", "head")),
            P("section", "seq", "head"),
            P("section", "seq", "head"),
            P("section", ("seq", "head"), None),
            P("section", None, "head"),
            P("section", None, ("seq", "head")),
            P("section", "head"),
            P("section", "head"),
            P("section", "head", "seq"),
        ),
        check_vma=False,
    )
```

```python
import functools

import jax
import jax.numpy as jnp
from jax import lax
from jax.experimental import pallas as pl
from jax.experimental.pallas import tpu as pltpu
from jax.sharding import PartitionSpec as P

BLOCK = 256
HALF = BLOCK // 2
PAD = 16
EPS = 1e-05
F32 = jnp.float32
LOW = jnp.bfloat16
HIDDEN = -1e30
NN = ((1,), (0,))
NT = ((1,), (1,))
TN = ((0,), (0,))
VMEM_BYTES = 50 * 1024 * 1024


def dot(a, b, dims):
    return lax.dot_general(a, b, (dims, ((), ())), preferred_element_type=F32)


def aligned(start, size):
    return pl.ds(pl.multiple_of(start, size), size)


def spread(cols, first, count, width):
    rows = cols.shape[0]
    lane = lax.broadcasted_iota(jnp.int32, (rows, count * width), 1)
    out = jnp.broadcast_to(cols[:, first : first + 1], (rows, count * width))
    for h in range(1, count):
        out = jnp.where(lane >= h * width, cols[:, first + h : first + h + 1], out)
    return out


def per_head(array, h, width):
    lane = lax.broadcasted_iota(jnp.int32, array.shape, 1)
    inside = (lane >= h * width) & (lane < (h + 1) * width)
    return jnp.where(inside, array, jnp.zeros_like(array))


def split_low(value):
    high = value.astype(LOW).astype(F32)
    return high, value - high


def column_of(row, size):
    return jnp.transpose(jnp.broadcast_to(row, (128, size)))


def sigmoid(v):
    return 0.5 * jnp.tanh(0.5 * v) + 0.5


def pick(flag, a, b):
    return jnp.where(flag, a, b)


class Sizes:
    def __init__(self, blocks, width, channels, heads, states, taps, head_axis, inner):
        self.blocks = blocks
        self.width = width
        self.channels = channels
        self.heads = heads
        self.head_width = channels // heads
        self.states = states
        self.lin = channels + 2 * states
        self.taps = taps
        self.head_axis = head_axis
        self.chunk = width // head_axis
        self.rows = blocks * HALF
        self.tokens = blocks * BLOCK
        self.inner = inner


def weight_copies(sz, layer, c, h, raw, got, wv, ov, sems):
    gate, inner, shared, out = raw
    ch = sz.channels
    cols = aligned(c * ch, ch)
    rows = aligned((h * 2 + c) * ch, ch)
    own = [
        (gate.at[0, :, cols], wv.at[:, :ch]),
        (inner.at[0, :, cols], wv.at[:, ch : 2 * ch]),
        (shared.at[0], wv.at[:, 2 * ch :]),
        (out.at[0, rows, :], ov),
    ]
    sent = [(got[0], wv), (got[1], ov)]
    return [
        (c == layer, [pltpu.make_async_copy(p, q, sems.at[i]) for i, (p, q) in enumerate(own)]),
        (c != layer, [pltpu.make_async_copy(p, q, sems.at[i]) for i, (p, q) in enumerate(sent)]),
    ]


def run_copies(choices, start, wait):
    for flag, copies in choices:

        @pl.when(flag)
        def _(copies=copies):
            if start:
                for copy in copies:
                    copy.start()
            if wait:
                for copy in copies:
                    copy.wait()


def put_ordered(sz, dst, c, k, b, own, other):
    for r in range(len(own)):

        @pl.when(lax.rem(k - b + len(own), len(own)) == r)
        def _(r=r):
            put_pair(dst, c, own[r][:HALF, :], other[r][:HALF, :])


def put_pair(dst, c, own, other):
    dst[aligned(c * HALF, HALF), :] = own
    dst[aligned((1 - c) * HALF, HALF), :] = other


def put_pieces(sz, dst, c, h, own, other):
    for d in range(sz.head_axis):
        cols = aligned((h ^ d) * sz.chunk, sz.chunk)
        dst[aligned(c * HALF, HALF), cols] = own[d]
        dst[aligned((1 - c) * HALF, HALF), cols] = other[d]


def put_parts(sz, b, c, h, part, keep, send):
    for d in range(sz.head_axis):
        cols = aligned((h ^ d) * sz.chunk, sz.chunk)
        keep[d, aligned(b * HALF, HALF), :] = part[aligned(c * HALF, HALF), cols]
        send[d, aligned(b * HALF, HALF), :] = part[aligned((1 - c) * HALF, HALF), cols]


def put_scalars(b, c, row, kept, sent):
    for scratch, flag in ((kept, c == 0), (sent, c != 0)):
        high, low = split_low(pick(flag, row[:, :HALF], row[:, HALF:]))
        line = lax.broadcasted_iota(jnp.int32, scratch.shape, 0)
        lower = jnp.where(line == 8 + b, low, scratch[...])
        scratch[...] = jnp.where(line == b, high, lower)


def line_of(table, at):
    line = lax.broadcasted_iota(jnp.int32, table.shape, 0)
    return jnp.sum(jnp.where(line == at, table, 0.0), axis=0, keepdims=True)


def close_parts(sz, keep, send, kept, sent):
    for scratch, out in ((kept, keep), (sent, send)):
        extra = jnp.concatenate([scratch[...]] * (sz.chunk // HALF), axis=1).astype(LOW)
        for d in range(sz.head_axis):
            out[d, sz.rows :, :] = extra


def conv_forward(sz, ext, taps):
    pre = taps[0:1] * ext[5 : 5 + BLOCK, :]
    for j in range(1, sz.taps):
        pre = pre + taps[j : j + 1] * ext[5 + j : 5 + j + BLOCK, :]
    return pre


def decay_of(sz, cols, rp, h, mask):
    rows = cols[:, h : h + 1] + rp[12 + h : 13 + h, :]
    return jnp.exp(jnp.where(mask, rows, HIDDEN))


def lower_mask():
    t = lax.broadcasted_iota(jnp.int32, (BLOCK, BLOCK), 0)
    s = lax.broadcasted_iota(jnp.int32, (BLOCK, BLOCK), 1)
    return t >= s


def forward_kernel(sz, layer, slots, sc, *refs):
    n = sz.head_axis
    sources = 2 * slots if layer == 0 else 2 * n + 2 * slots
    src, refs = refs[:sources], refs[sources:]
    if layer == 1:
        table, refs = refs[0], refs[1:]
    gains, raw, got, halo, begin = refs[0:2], refs[2:6], refs[6:8], refs[8], refs[9]
    normed_o, gl_o, lin_o, ssd_o, inc_o, inv_o, part_o, keep, send, fin_o, sc_o, base_o = refs[10:22]
    refs = refs[22:]
    if layer == 1:
        mixed_o, refs = refs[0], refs[1:]
    else:
        tables_o, refs = refs[0:2], refs[2:]
    xs, ms, wv, ov, ext, state, kept, sent, part, sems = refs
    b = pl.program_id(0)
    c, h, k = sc[0], sc[1], sc[3]
    ch, st = sz.channels, sz.states
    copies = weight_copies(sz, layer, c, h, raw, got, wv, ov, sems)

    @pl.when(b == 0)
    def _():
        run_copies(copies, True, False)
        ext[0:8, :] = halo[...]
        state[...] = begin[...]
        kept[...] = jnp.zeros_like(kept)
        sent[...] = jnp.zeros_like(sent)
        for i in range(4):
            sc_o[i] = sc[i]

    mine = aligned(c * HALF, HALF)
    cols = aligned(h * sz.chunk, sz.chunk)
    if layer == 0:
        put_ordered(sz, xs, c, k, b, src[:slots], src[slots:])
        base_o[...] = xs[mine, cols]
        for r in range(slots):

            @pl.when(lax.rem(k - b + slots, slots) == r)
            def _(r=r):
                own = decay_table(rates_of(src[r]), c, sz.heads)
                other = decay_table(rates_of(src[slots + r]), c, sz.heads)
                tables_o[0][...] = pick(c == 0, own, other)
                tables_o[1][...] = pick(c == 0, other, own)

        rp = tables_o[0][...]
    else:
        put_pieces(sz, xs, c, h, [r[...] for r in src[:n]], [r[...] for r in src[n : 2 * n]])
        put_ordered(sz, ms, c, k, b, src[2 * n : 2 * n + slots], src[2 * n + slots :])
        base_o[...] = ms[mine, cols]
        mixed_o[...] = ms[...]
        rp = table[...]

    pv = pick(c == layer, gains[0][...], gains[1][...])
    x = xs[...].astype(F32)
    inv_in = lax.rsqrt(jnp.mean(x * x, axis=1, keepdims=True) + EPS)
    normed = (x * inv_in * pv[0:1, : sz.width]).astype(LOW)
    normed_o[...] = normed

    @pl.when(b == 0)
    def _():
        run_copies(copies, False, True)

    proj = dot(normed, wv[...], NN)
    gl = proj[:, :ch]
    gl_o[...] = gl
    lin = proj[:, ch:].astype(LOW)
    lin_o[...] = lin
    ext[8 : 8 + BLOCK, :] = lin.astype(F32)
    pre = conv_forward(sz, ext, pv[1:5, : sz.lin])
    ext[0:8, :] = ext[BLOCK : BLOCK + 8, :]
    act = (pre * sigmoid(pre)).astype(LOW)
    values, bm, cm = act[:, :ch], act[:, ch : ch + st], act[:, ch + st :]

    cols = jnp.transpose(rp)
    mask = lower_mask()
    gram = dot(cm, bm, NT)
    mixes, parts = [], []
    for i in range(sz.heads):
        mixes.append((gram * decay_of(sz, cols, rp, i, mask)).astype(LOW))
        parts.append(per_head(values, i, sz.head_width))
    intra = dot(jnp.concatenate(mixes, axis=1), jnp.concatenate(parts, axis=0), NN)

    low_state = state[...].astype(LOW)
    inc_o[0] = low_state
    ecum = spread(cols, sz.heads, sz.heads, sz.head_width)
    inter = dot(cm, low_state, NT) * ecum
    vf = values.astype(F32)
    carried = (vf * spread(cols, 2 * sz.heads, sz.heads, sz.head_width)).astype(LOW)
    local = dot(carried, bm, TN)
    for i in range(sz.heads):
        rows = slice(i * sz.head_width, (i + 1) * sz.head_width)
        total = cols[BLOCK - 1 : BLOCK, sz.heads + i : sz.heads + i + 1]
        state[rows, :] = total * state[rows, :] + local[rows]
    ssd = intra + inter + pv[6:7, :ch] * vf
    ssd_o[...] = ssd
    gated = ssd * (gl * sigmoid(gl))
    weighty = gated * pv[5:6, :ch]
    part[...] = dot(weighty.astype(LOW), ov[...], NN).astype(LOW)

    lane = lax.broadcasted_iota(jnp.int32, (BLOCK, 128), 1)
    square = jnp.sum(gated * gated, axis=1, keepdims=True)
    if layer == 0:
        project = jnp.zeros_like(square)
    else:
        scaled_grad = dot(ms[...], ov[...], NT)
        project = jnp.sum(scaled_grad * weighty, axis=1, keepdims=True)
    stats = jnp.where(lane == 0, square, jnp.where(lane == 1, project, inv_in))
    stats = jnp.transpose(stats)
    part_o[...] = stats[0:2, :]
    inv_o[...] = stats[2:3, :]
    put_scalars(b, c, stats[0:1, :], kept, sent)
    put_parts(sz, b, c, h, part, keep, send)

    @pl.when(b == sz.blocks - 1)
    def _():
        close_parts(sz, keep, send, kept, sent)
        fin_o[...] = state[...]


def backward_kernel(sz, layer, sc, *refs):
    n = sz.head_axis
    sources = 2 * n + 2 if layer == 0 else 1 + n
    src, refs = refs[:sources], refs[sources:]
    normed_r, gl_r, lin_r, ssd_r, inc_r = refs[:5]
    table, gains, raw, got = refs[5], refs[6:8], refs[8:12], refs[12:14]
    halo, halo_grad, begin = refs[14:17]
    keep, send, cat_o, scaled_o, small_o, common_o, fin_o, rim_o, sc_o = refs[17:26]
    refs = refs[26:]
    if layer == 0:
        mixed_o, refs = refs[0], refs[1:]
    ms, wv, ov, ext, back, state, kept, sent, part, heads_p, small, wide, sems = refs
    i_step = pl.program_id(0)
    b = sz.blocks - 1 - i_step
    c, h = sc[0], sc[1]
    ch, st = sz.channels, sz.states
    copies = weight_copies(sz, layer, c, h, raw, got, wv, ov, sems)
    pv = pick(c == layer, gains[0][...], gains[1][...])
    rp = table[...]

    @pl.when(i_step == 0)
    def _():
        run_copies(copies, True, True)
        back[BLOCK : BLOCK + 8, :] = halo_grad[...]
        state[...] = begin[...]
        kept[...] = jnp.zeros_like(kept)
        sent[...] = jnp.zeros_like(sent)
        small[...] = jnp.zeros_like(small)
        wide[...] = jnp.zeros_like(wide)
        for i in range(4):
            sc_o[i] = sc[i]
        if layer == 0:
            for i in range(2):
                extra = src[i * n][sz.rows :, :].astype(F32)
                for d in range(1, n):
                    extra = extra + src[i * n + d][sz.rows :, :].astype(F32)
                heads_p[8 * i : 8 * i + 8, :] = extra[0:8, :HALF] + extra[8:16, :HALF]

    if layer == 0:
        rows = aligned(b * HALF, HALF)
        put_pieces(
            sz, ms, c, h, [r[rows, :] for r in src[:n]], [r[rows, :] for r in src[n : 2 * n]]
        )
        halves = []
        for k in range(2):
            alpha = lax.rsqrt(line_of(src[2 * n + k][...], b) / sz.inner + EPS)
            beta = alpha * alpha * line_of(heads_p[...], 8 * k + b) / sz.inner
            halves.append((alpha, beta))
        alpha, beta = (
            pick(
                c == 0,
                jnp.concatenate([halves[0][q], halves[1][q]], axis=1),
                jnp.concatenate([halves[1][q], halves[0][q]], axis=1),
            )
            for q in range(2)
        )
    else:
        stats = src[1][...]
        for d in range(1, n):
            stats = stats + src[1 + d][...]
        alpha = lax.rsqrt(stats[0:1, :] / sz.inner + EPS)
        beta = alpha * alpha * alpha * stats[1:2, :] / sz.inner

    sub = lax.broadcasted_iota(jnp.int32, rp.shape, 0)
    cols = jnp.transpose(jnp.where(sub == 12, alpha, jnp.where(sub == 13, beta, rp)))
    alpha, beta = cols[:, 12:13], cols[:, 13:14]

    gl = gl_r[...]
    ssd = ssd_r[...]
    sig = sigmoid(gl)
    swish = gl * sig
    slope = sig * (1.0 + gl * (1.0 - sig))
    gated = ssd * swish
    if layer == 0:
        mixed_grad = ms[...]
        mixed_o[...] = mixed_grad
    else:
        mixed_grad = src[0][...]
    scaled_grad = dot(mixed_grad, ov[...], NT)
    gain = pv[5:6, :ch]
    normal = gated * alpha
    small[4:5, :ch] += jnp.sum(scaled_grad * normal, axis=0, keepdims=True)
    scaled_o[...] = (normal * gain).astype(LOW)
    gated_grad = alpha * (scaled_grad * gain) - beta * gated
    ssd_grad = (gated_grad * swish).astype(LOW)
    gate_grad = (gated_grad * ssd * slope).astype(LOW)
    sgf = ssd_grad.astype(F32)

    before = lin_r[pl.ds(pl.multiple_of(jnp.maximum(b * BLOCK - 16, 0), 16), 16), :]
    ext[0:8, :] = pick(b > 0, before.astype(F32)[8:16, :], halo[...])
    ext[8 : 8 + BLOCK, :] = lin_r[aligned(b * BLOCK, BLOCK), :].astype(F32)
    taps = pv[1:5, : sz.lin]
    pre = conv_forward(sz, ext, taps)
    psig = sigmoid(pre)
    pact = pre * psig
    pslope = psig * (1.0 + pre * (1.0 - psig))
    act = pact.astype(LOW)
    values, bm, cm = act[:, :ch], act[:, ch : ch + st], act[:, ch + st :]
    vf = values.astype(F32)
    small[5:6, :ch] += jnp.sum(sgf * vf, axis=0, keepdims=True)

    mask = lower_mask()
    gram = dot(cm, bm, NT)
    gram_grad = jnp.zeros((BLOCK, BLOCK), F32)
    mixes, parts = [], []
    for i in range(sz.heads):
        decay = decay_of(sz, cols, rp, i, mask)
        mixes.append((gram * decay).astype(LOW))
        parts.append(per_head(ssd_grad, i, sz.head_width))
        gram_grad = gram_grad + dot(parts[-1], values, NT) * decay
    intra_grad = dot(jnp.concatenate(mixes, axis=0), jnp.concatenate(parts, axis=0), TN)

    ecum = spread(cols, sz.heads, sz.heads, sz.head_width)
    to_end = spread(cols, 2 * sz.heads, sz.heads, sz.head_width)
    inter_grad = (sgf * ecum).astype(LOW)
    low_state = state[...].astype(LOW)
    carried = (vf * to_end).astype(LOW)
    carried_grad = dot(bm, low_state, NT)
    gram_low = gram_grad.astype(LOW)
    b_grad = dot(gram_low, cm, TN) + dot(carried, low_state, NN)
    c_grad = dot(gram_low, bm, NN) + dot(inter_grad, inc_r[0], NN)
    value_grad = intra_grad + pv[6:7, :ch] * sgf + carried_grad * to_end
    entry = dot(inter_grad, cm, TN)
    for i in range(sz.heads):
        rows = slice(i * sz.head_width, (i + 1) * sz.head_width)
        total = cols[BLOCK - 1 : BLOCK, sz.heads + i : sz.heads + i + 1]
        state[rows, :] = total * state[rows, :] + entry[rows]

    pre_grad = jnp.concatenate([value_grad, b_grad, c_grad], axis=1) * pslope
    back[0:BLOCK, :] = pre_grad
    lin_grad = taps[0:1] * back[sz.taps - 1 : sz.taps - 1 + BLOCK, :]
    for j in range(1, sz.taps):
        at = sz.taps - 1 - j
        lin_grad = lin_grad + taps[j : j + 1] * back[at : at + BLOCK, :]
    for j in range(sz.taps):
        small[j : j + 1, :] += jnp.sum(pre_grad * ext[5 + j : 5 + j + BLOCK, :], axis=0, keepdims=True)
    back[BLOCK : BLOCK + 8, :] = back[0:8, :]
    cat = jnp.concatenate([gate_grad, lin_grad.astype(LOW)], axis=1)
    cat_o[...] = cat
    normed_grad = dot(cat, wv[...], NT)
    part[...] = normed_grad.astype(LOW)
    product = normed_grad * normed_r[...].astype(F32)
    wide[0:1, :] += jnp.sum(product, axis=0, keepdims=True)
    along = jnp.sum(product, axis=1, keepdims=True)
    along = jnp.transpose(jnp.broadcast_to(along, (BLOCK, 128)))
    put_scalars(b, c, along[0:1, :], kept, sent)
    put_parts(sz, b, c, h, part, keep, send)

    @pl.when(i_step == sz.blocks - 1)
    def _():
        close_parts(sz, keep, send, kept, sent)
        fin_o[...] = state[...]
        rim_o[...] = back[0:8, :]
        sums = small[...]
        flat = [sums[j : j + 1, :ch] for j in range(sz.taps + 2)]
        flat = [jnp.concatenate(flat[j : j + 3], axis=1) for j in range(0, len(flat), 3)]
        flat = flat + [jnp.zeros_like(flat[0])] * (4 - len(flat))
        high, low = split_low(jnp.concatenate(flat, axis=0))
        rest = jnp.zeros((PAD - 8, high.shape[1]), F32)
        small_o[...] = jnp.concatenate([high, low, rest], axis=0).astype(LOW)
        gain_grad = wide[0:1, :] / pv[0:1, :]
        flat = [sums[j : j + 1, ch:] for j in range(sz.taps)]
        flat += [gain_grad[:, q * sz.chunk : (q + 1) * sz.chunk] for q in range(n)]
        high, low = split_low(jnp.concatenate(flat, axis=0))
        common_o[...] = jnp.concatenate([high, low], axis=0).astype(LOW)


def weights_kernel(sz, seq, behind, sc, normed, cat, mixed, scaled, small, common, *refs):
    sc_o, refs = refs[behind], refs[behind + 1 :]
    if behind:
        refs = refs[1:]
    for i in range(4):
        sc_o[i] = sc[i]
    outs, heads, full, wide = refs[:seq], refs[seq:-2], refs[-2], refs[-1]
    ch, st = sz.channels, sz.states
    step = sz.chunk
    for q in range(sz.head_axis):
        at = slice(q * step, (q + 1) * step)
        grads = dot(normed[:, at], cat[...], TN)
        full[at, : 2 * ch] = grads[:, : 2 * ch].astype(LOW)
        wide[at, :] = grads[:, 2 * ch :]
        full[at, 2 * ch :] = dot(mixed[:, at], scaled[...], TN).astype(LOW)
    rows = sz.width // seq
    part = rows // sz.head_axis
    for r, out in enumerate(outs):
        out[:rows, :] = full[aligned(lax.rem(sc[2] + r, seq) * rows, rows), :]
        out[rows:, :] = small[...]
    for d, out in enumerate(heads):
        lines = [
            wide[aligned(lax.rem(sc[2] + r, seq) * rows + (sc[1] ^ d) * part, part), :]
            for r in range(seq)
        ]
        out[PAD:, :] = jnp.concatenate(lines, axis=0).astype(LOW)
        out[:PAD, :] = common[...]


def resplit(extra, half):
    high, low = split_low(extra[:half, :] + extra[half : 2 * half, :])
    return jnp.concatenate([high, low], axis=0)


def heads_kernel(sz, sc, *refs):
    n = sz.head_axis
    zero, one, own_o, send_o = refs[:n], refs[n : 2 * n], refs[-2], refs[-1]
    first = sc[0] == 0
    zero, one = total_of(zero, slice(None)), total_of(one, slice(None))
    for out, flag in ((own_o, first), (send_o, jnp.logical_not(first))):
        rows = pick(flag, zero, one)
        rows = jnp.concatenate([resplit(rows[:PAD], PAD // 2), rows[PAD:]], axis=0)
        out[...] = rows.astype(out.dtype)


def spans_kernel(sz, own, got, *outs):
    rows = own[...] + got[...].astype(F32)
    extra = resplit(rows[:PAD], PAD // 2)
    part = outs[0].shape[0] - PAD
    for r, out in enumerate(outs):
        at = PAD + r * part
        out[...] = jnp.concatenate([extra, rows[at : at + part]], axis=0).astype(LOW)


def join_kernel(sz, sc, keep, recv, sc_o, own, *sends):
    rows = sz.rows
    for i in range(4):
        sc_o[i] = sc[i]
    extra = keep[0, rows:, :].astype(F32) + recv[0, rows:, :].astype(F32)
    high, low = split_low(extra[0:8, :] + extra[8:16, :])
    extra = jnp.concatenate([high, low], axis=0)
    for d, out in enumerate((own,) + sends):
        out[:rows, :] = (keep[d, :rows, :].astype(F32) + recv[d, :rows, :].astype(F32)).astype(out.dtype)
        out[rows:, :] = extra.astype(out.dtype)


def total_of(parts, rows):
    total = parts[0][rows, :].astype(F32)
    for p in parts[1:]:
        total = total + p[rows, :].astype(F32)
    return total


def output_kernel(sz, layer, sc, *refs):
    n = sz.head_axis
    parts, refs = refs[:n], refs[n:]
    resid, res_o, low_o, mixed_o, square_o = refs
    extra = total_of(parts, slice(sz.rows, sz.rows + PAD))
    square = extra[0:8, :HALF] + extra[8:16, :HALF]
    square_o[...] = square
    inv = lax.rsqrt(square / sz.inner + EPS)
    for b in range(sz.blocks):
        rows = slice(b * HALF, (b + 1) * HALF)
        col = column_of(inv[b : b + 1, :], HALF)[:, 0:1]
        mixed = total_of(parts, rows) * col
        res = resid[rows, :].astype(F32) + mixed
        res_o[rows, :] = res
        low_o[rows, :] = res.astype(LOW)
        mixed_o[rows, :] = mixed


def input_kernel(sz, layer, sc, *refs):
    n = sz.head_axis
    parts, refs = refs[:n], refs[n:]
    resid, outg, inv_r, gains = refs[0], refs[1], refs[2], refs[3:5]
    refs = refs[5:]
    if layer == 1:
        mixed, refs = refs[0], refs[1:]
    grad_o, low_o, sc_o = refs
    for i in range(4):
        sc_o[i] = sc[i]
    c, h = sc[0], sc[1]
    mine = aligned(h * sz.chunk, sz.chunk)
    gain = pick(c == layer, gains[0][0:1, mine], gains[1][0:1, mine])
    extra = total_of(parts, slice(sz.rows, sz.rows + PAD))
    along = extra[0:8, :HALF] + extra[8:16, :HALF]
    tops, lows = [], []
    for b in range(sz.blocks):
        rows = slice(b * HALF, (b + 1) * HALF)
        at = b * BLOCK
        inv_row = pick(c == 0, inv_r[:, at : at + HALF], inv_r[:, at + HALF : at + BLOCK])
        inv = column_of(inv_row, HALF)[:, 0:1]
        share = column_of(along[b : b + 1, :] / sz.width, HALF)[:, 0:1]
        total = total_of(parts, rows)
        base = resid[rows, :].astype(F32)
        grad = outg[rows, :].astype(F32) + inv * (total * gain - base * (inv * share))
        grad_o[rows, :] = grad
        low = grad.astype(LOW)
        low_o[rows, :] = low
        if layer == 1:
            dots = jnp.sum(low.astype(F32) * mixed[rows, :], axis=1, keepdims=True)
            row = jnp.transpose(jnp.broadcast_to(dots, (HALF, 128)))[0:1, :]
            high, rest = split_low(row)
            tops.append(high)
            lows.append(rest)
    if layer == 1:
        fill = [jnp.zeros((8 - sz.blocks, HALF), F32)] if sz.blocks < 8 else []
        extra = jnp.concatenate(tops + fill + lows + fill, axis=0)
        extra = jnp.concatenate([extra] * (sz.chunk // HALF), axis=1)
        low_o[sz.rows :, :] = extra.astype(LOW)
    else:
        low_o[sz.rows :, :] = jnp.zeros((PAD, sz.chunk), LOW)


def sum_kernel(sz, sc, *refs):
    parts, out = refs[:-1], refs[-1]
    rows = out.shape[0] - PAD
    out[:rows, :] = total_of(parts, slice(0, rows)).astype(LOW)
    extra = total_of(parts, slice(rows, rows + PAD))
    high, low = split_low(extra[0:4, :] + extra[4:8, :])
    extra = jnp.concatenate([high, low, jnp.zeros((PAD - 8, extra.shape[1]), F32)], axis=0)
    out[rows:, :] = extra.astype(LOW)


def final_kernel(sz, sc, zero, one, got, *refs):
    parts, refs = refs[:-8], refs[-8:]
    gate_o, inner_o, out_o, conv_o, norm_o, skip_o, shared_o, common_o = refs
    c = sc[0]
    ch = sz.channels
    rows = zero.shape[0] - PAD
    lane = lax.broadcasted_iota(jnp.int32, skip_o.shape, 1)
    skip = jnp.zeros(skip_o.shape, F32)
    for i in range(2):
        which = pick(i == 0, c, 1 - c)
        to = aligned(which * ch, ch)
        sums = (pick(c == 0, zero[...], one[...]) if i == 0 else got[...]).astype(F32)
        gate_o[:, to] = sums[:rows, :ch]
        inner_o[:, to] = sums[:rows, ch : 2 * ch]
        out_o[to, :] = jnp.transpose(sums[:rows, 2 * ch :])
        lines = sums[rows : rows + 4, :] + sums[rows + 4 : rows + 8, :]
        for j in range(sz.taps):
            conv_o[j : j + 1, to] = lines[j // 3 : j // 3 + 1, (j % 3) * ch : (j % 3 + 1) * ch]
        norm_o[:, to] = lines[1:2, ch : 2 * ch]
        skips = lines[1:2, 2 * ch :]
        for q in range(sz.heads):
            part = jnp.sum(per_head(skips, q, sz.head_width), axis=1, keepdims=True)
            skip = jnp.where(lane == which * sz.heads + q, part, skip)
    skip_o[...] = skip
    total = total_of(parts, slice(None))
    shared_o[...] = total[PAD:]
    common_o[...] = total[: PAD // 2] + total[PAD // 2 : PAD]


def slice_kernel(sz, slots, with_rates, sc, order, *refs):
    sources = 2 if with_rates else 1
    src, refs = refs[:sources], refs[sources:]
    outs, sc_o, refs = refs[:slots], refs[slots], refs[slots + 1 :]
    sems = refs[-1]
    copies = []
    for r in range(slots):
        which = order[lax.rem(sc[3] + r, slots)]
        rows = src[0].at[which, aligned(sc[0] * HALF, HALF), :]
        to = outs[r].at[:HALF] if with_rates else outs[r]
        copies.append(pltpu.make_async_copy(rows, to, sems.at[r]))
    for copy in copies:
        copy.start()
    for i in range(4):
        sc_o[i] = sc[i]
    if with_rates:
        thirds = refs[0]
        for r in range(slots):
            which = order[lax.rem(sc[3] + r, slots)]
            first, rest = split_low(src[1][0, which])
            second, rest = split_low(rest)
            lines = jnp.concatenate([first, second, rest, jnp.zeros_like(rest)], axis=1)
            lines = jnp.concatenate([lines, jnp.zeros_like(lines)], axis=0)
            thirds[r] = lines.astype(LOW)
        more = [
            pltpu.make_async_copy(thirds.at[r], outs[r].at[HALF:], sems.at[slots + r])
            for r in range(slots)
        ]
        for copy in more:
            copy.start()
        copies = copies + more
    for copy in copies:
        copy.wait()


def pass_kernel(sc, *refs):
    for i in range(4):
        refs[-2][i] = sc[i]


def rates_of(piece):
    lines = piece[HALF:, :].astype(F32)[:8, :]
    return (lines[:, :BLOCK] + lines[:, BLOCK : 2 * BLOCK]) + lines[:, 2 * BLOCK : 3 * BLOCK]


def pack_kernel(sz, sc, gate, inner, shared, out, in_gain, conv_i, conv_s, skip, norm, *refs):
    w_o, o_o, mine_o, send_o, sems = refs
    c, h = sc[0], sc[1]
    ch = sz.channels
    cols = aligned((1 - c) * ch, ch)
    rows = aligned((h * 2 + 1 - c) * ch, ch)
    copies = [
        pltpu.make_async_copy(gate.at[0, :, cols], w_o.at[:, :ch], sems.at[0]),
        pltpu.make_async_copy(inner.at[0, :, cols], w_o.at[:, ch : 2 * ch], sems.at[1]),
        pltpu.make_async_copy(shared.at[0], w_o.at[:, 2 * ch :], sems.at[2]),
        pltpu.make_async_copy(out.at[0, rows, :], o_o, sems.at[3]),
    ]
    for copy in copies:
        copy.start()
    for which, ref in ((c, mine_o), (1 - c, send_o)):
        at = aligned(which * ch, ch)
        ref[...] = jnp.zeros_like(ref)
        ref[0:1, :] = in_gain[...]
        ref[1 : 1 + sz.taps, :ch] = conv_i[0, :, at]
        ref[1 : 1 + sz.taps, ch : sz.lin] = conv_s[0]
        ref[5:6, :ch] = norm[:, at]
        low = spread(skip[...], 0, sz.heads, sz.head_width)
        high = spread(skip[...], sz.heads, sz.heads, sz.head_width)
        ref[6:7, :ch] = pick(which == 0, low, high)
    for copy in copies:
        copy.wait()


def decay_table(rate, c, n):
    lane = lax.broadcasted_iota(jnp.int32, rate.shape, 1)
    cum = rate
    step = 1
    while step < BLOCK:
        cum = cum + jnp.where(lane >= step, pltpu.roll(cum, step, 1), 0.0)
        step *= 2
    end = cum[:, BLOCK - 1 :]
    lines = [cum, jnp.exp(cum), jnp.exp(end - cum) * -rate, jnp.log(-rate) - cum]
    low = jnp.concatenate([v[:n] for v in lines], axis=0)
    high = jnp.concatenate([v[n:] for v in lines], axis=0)
    return pick(c == 0, low, high)


def leave_kernel(sz, slots, sc, zero_own, zero_other, one_own, one_other, *outs):
    c = sc[0]
    for r in range(slots):
        rows = aligned(lax.rem(sc[3] + r, slots) * HALF, HALF)
        own = pick(c == 0, zero_own[rows, :], one_own[rows, :])
        other = pick(c == 0, zero_other[rows, :], one_other[rows, :])
        put_pair(outs[r], c, own, other)


def home_kernel(slots, sc, *refs):
    early, late, out, grad = refs[:slots], refs[slots : 2 * slots], refs[-2], refs[-1]
    first = sc[0] == 0
    for r in range(slots):
        at = lax.rem(sc[3] - r + slots, slots)
        out[at] = pick(first, early[r][...], late[r][...]).astype(F32)
        grad[at] = pick(first, late[r][...], early[r][...]).astype(F32)


def whole(shape):
    return pl.BlockSpec(shape, lambda *_: (0,) * len(shape))


def per_device(
    tokens,
    slot_order,
    log_decay,
    grad_out,
    in_gain,
    w_gate,
    w_inner,
    w_shared,
    conv_inner,
    conv_shared,
    d_skip,
    norm_gain,
    w_out,
):
    slots = tokens.shape[0]
    span = tokens.shape[1]
    width = tokens.shape[2]
    seq = lax.axis_size("seq")
    head_axis = lax.axis_size("head")
    cores = lax.axis_size("section")
    spans = seq // slots
    c = lax.axis_index("section")
    z = lax.axis_index("seq")
    h = lax.axis_index("head")
    k = lax.rem(z, slots)
    inner_dev = w_gate.shape[2]
    channels = inner_dev // cores
    shared = w_shared.shape[2]
    heads_dev = d_skip.shape[1]
    taps = conv_inner.shape[1]
    sz = Sizes(
        slots * span // BLOCK,
        width,
        channels,
        heads_dev // cores,
        shared // 2,
        taps,
        head_axis,
        inner_dev * head_axis,
    )
    first = c == 0
    swap = [(0, 1), (1, 0)]
    nb, tok, rows, chunk = sz.blocks, sz.tokens, sz.rows, sz.chunk

    def cross(x):
        return lax.ppermute(x, "section", swap)

    def turn(x, r):
        pairs = [(i, i // slots * slots + (i % slots + r) % slots) for i in range(seq)]
        return lax.ppermute(x, "seq", pairs) if r else x

    def over_heads(x, d):
        return lax.ppermute(x, "head", [(i, i ^ d) for i in range(head_axis)])

    def next_span(x, way):
        pairs = [(i, i + way * slots) for i in range(seq) if 0 <= i + way * slots < seq]
        return lax.ppermute(x, "seq", pairs)

    def shape(dims, dtype):
        return jax.ShapeDtypeStruct(dims, dtype)

    prefetch = functools.partial(pltpu.PrefetchScalarGridSpec, num_scalar_prefetch=1)
    options = pltpu.CompilerParams(vmem_limit_bytes=VMEM_BYTES)
    anywhere = pl.BlockSpec(memory_space=pl.ANY)
    smem = pl.BlockSpec(memory_space=pltpu.SMEM)
    vmem = pl.BlockSpec(memory_space=pltpu.VMEM)
    index_shape = shape((4,), jnp.int32)

    def cost(flops, moved):
        return pl.CostEstimate(flops=int(flops), bytes_accessed=int(moved), transcendentals=0)

    def take_rows(sc, source, rates):
        given = [source] if rates is None else [source, rates]
        more = 0 if rates is None else PAD
        got = pl.pallas_call(
            functools.partial(slice_kernel, sz, slots, rates is not None),
            in_specs=[smem, smem, anywhere] + ([] if rates is None else [vmem]),
            out_specs=[anywhere] * slots + [smem],
            out_shape=[shape((HALF + more, width), LOW)] * slots + [index_shape],
            scratch_shapes=([pltpu.VMEM((slots, PAD, width), LOW)] if more else [])
            + [pltpu.SemaphoreType.DMA((2 * slots,))],
            compiler_params=options,
        )(sc, slot_order, *given)
        own = [turn(got[r], r) for r in range(slots)]
        return own + [cross(x) for x in own], got[slots]

    sc = jnp.stack([c, h, z, k]).astype(jnp.int32)
    tok_pieces, sc = take_rows(sc, tokens, log_decay)

    wide = 2 * channels + shared
    w_sent, o_sent, pv_mine, pv_sent = pl.pallas_call(
        functools.partial(pack_kernel, sz),
        in_specs=[smem] + [anywhere] * 4 + [vmem] * 5,
        out_specs=[anywhere, anywhere, vmem, vmem],
        out_shape=[
            shape((width, wide), LOW),
            shape((channels, width), LOW),
            shape((16, width), F32),
            shape((16, width), F32),
        ],
        scratch_shapes=[pltpu.SemaphoreType.DMA((4,))],
        compiler_params=options,
    )(sc, w_gate, w_inner, w_shared, w_out, in_gain, conv_inner, conv_shared, d_skip, norm_gain)
    raw = [w_gate, w_inner, w_shared, w_out]
    sent = [cross(w_sent), cross(o_sent)]
    gains = [pv_mine, cross(pv_sent)]

    def after(sc, *arrays):
        last = arrays[-1]
        return pl.pallas_call(
            pass_kernel,
            in_specs=[smem] + [anywhere] * len(arrays),
            out_specs=[smem, anywhere],
            out_shape=[index_shape, shape(last.shape, last.dtype)],
            input_output_aliases={len(arrays): 1},
            compiler_params=options,
        )(sc, *arrays)

    def span_total(table):
        ends = table[: sz.heads, BLOCK - 1 :: BLOCK]
        return jnp.repeat(jnp.exp(jnp.sum(ends, axis=1)), sz.head_width)[:, None]

    parts_shape = shape((head_axis, rows + PAD, chunk), LOW)
    weight_specs = [anywhere] * 6
    weight_scratch = [pltpu.VMEM((width, wide), LOW), pltpu.VMEM((channels, width), LOW)]
    dense = 2 * tok * width * (wide + channels)

    def forward(layer, sc, sources):
        def at(b, _):
            return (b, 0)

        piece = pl.BlockSpec((HALF, chunk), at)
        table = pl.BlockSpec((16, BLOCK), lambda b, _: (0, b))
        if layer == 0:
            src_specs = [whole((HALF + PAD, width))] * (2 * slots)
            more_specs = [table, table]
            more_shapes = [shape((16, tok), F32)] * 2
        else:
            src_specs = [piece] * (2 * head_axis) + [whole((HALF, width))] * (2 * slots) + [table]
            more_specs = [pl.BlockSpec((BLOCK, width), at)]
            more_shapes = [shape((tok, width), LOW)]

        def call(halo, begin):
            return pl.pallas_call(
                functools.partial(forward_kernel, sz, layer, slots),
                grid_spec=prefetch(
                    grid=(nb,),
                    in_specs=src_specs
                    + [whole((16, width)), whole((16, width))]
                    + weight_specs
                    + [whole((8, sz.lin)), whole((channels, sz.states))],
                    out_specs=[
                        pl.BlockSpec((BLOCK, width), at),
                        pl.BlockSpec((BLOCK, channels), at),
                        pl.BlockSpec((BLOCK, sz.lin), at),
                        pl.BlockSpec((BLOCK, channels), at),
                        pl.BlockSpec((1, channels, sz.states), lambda b, _: (b, 0, 0)),
                        pl.BlockSpec((1, BLOCK), lambda b, _: (0, b)),
                        pl.BlockSpec((2, BLOCK), lambda b, _: (0, b)),
                        whole(parts_shape.shape),
                        whole(parts_shape.shape),
                        whole((channels, sz.states)),
                        smem,
                        piece,
                    ]
                    + more_specs,
                    scratch_shapes=[
                        pltpu.VMEM((BLOCK, width), LOW),
                        pltpu.VMEM((BLOCK, width), LOW),
                        *weight_scratch,
                        pltpu.VMEM((BLOCK + 8, sz.lin), F32),
                        pltpu.VMEM((channels, sz.states), F32),
                        pltpu.VMEM((PAD, HALF), F32),
                        pltpu.VMEM((PAD, HALF), F32),
                        pltpu.VMEM((BLOCK, width), LOW),
                        pltpu.SemaphoreType.DMA((4,)),
                    ],
                ),
                out_shape=[
                    shape((tok, width), LOW),
                    shape((tok, channels), F32),
                    shape((tok, sz.lin), LOW),
                    shape((tok, channels), F32),
                    shape((nb, channels, sz.states), LOW),
                    shape((1, tok), F32),
                    shape((2, tok), F32),
                    parts_shape,
                    parts_shape,
                    shape((channels, sz.states), F32),
                    index_shape,
                    shape((rows, chunk), LOW),
                ]
                + more_shapes,
                compiler_params=options,
                cost_estimate=cost(6 * dense, 16e6),
            )(sc, *sources, *gains, *raw, *sent, halo, begin)

        halo = jnp.zeros((8, sz.lin), F32)
        begin = jnp.zeros((channels, sz.states), F32)
        if spans == 1:
            return call(halo, begin), halo
        trial = call(halo, begin)
        halo = next_span(trial[2][tok - 8 :].astype(F32), 1)
        local = call(halo, begin)[9]
        total = span_total(trial[12] if layer == 0 else sources[-1])
        for _ in range(spans - 1):
            begin = next_span(total * begin + local, 1)
        return call(halo, begin), halo

    def backward(layer, sc, sources, saved, decays, halo):
        def at(i, _):
            return (nb - 1 - i, 0)

        if layer == 0:
            src_specs = [whole(s.shape) for s in sources]
        else:
            stat = pl.BlockSpec((2, BLOCK), lambda i, _: (0, nb - 1 - i))
            src_specs = [pl.BlockSpec((BLOCK, width), at)] + [stat] * head_axis
        normed, gl, lin, ssd, inc = saved
        mixed_spec = [pl.BlockSpec((BLOCK, width), at)] if layer == 0 else []
        mixed_shape = [shape((tok, width), LOW)] if layer == 0 else []
        table = pl.BlockSpec((16, BLOCK), lambda i, _: (0, nb - 1 - i))

        def call(halo_grad, begin):
            return pl.pallas_call(
                functools.partial(backward_kernel, sz, layer),
                grid_spec=prefetch(
                    grid=(nb,),
                    in_specs=src_specs
                    + [
                        pl.BlockSpec((BLOCK, width), at),
                        pl.BlockSpec((BLOCK, channels), at),
                        whole(lin.shape),
                        pl.BlockSpec((BLOCK, channels), at),
                        pl.BlockSpec((1, channels, sz.states), lambda i, _: (nb - 1 - i, 0, 0)),
                        table,
                        whole((16, width)),
                        whole((16, width)),
                        *weight_specs,
                        whole((8, sz.lin)),
                        whole((8, sz.lin)),
                        whole((channels, sz.states)),
                    ],
                    out_specs=[
                        whole(parts_shape.shape),
                        whole(parts_shape.shape),
                        pl.BlockSpec((BLOCK, wide), at),
                        pl.BlockSpec((BLOCK, channels), at),
                        whole((PAD, 3 * channels)),
                        whole((PAD, chunk)),
                        whole((channels, sz.states)),
                        whole((8, sz.lin)),
                        smem,
                    ]
                    + mixed_spec,
                    scratch_shapes=[
                        pltpu.VMEM((BLOCK, width), LOW),
                        *weight_scratch,
                        pltpu.VMEM((BLOCK + 8, sz.lin), F32),
                        pltpu.VMEM((BLOCK + 8, sz.lin), F32),
                        pltpu.VMEM((channels, sz.states), F32),
                        pltpu.VMEM((PAD, HALF), F32),
                        pltpu.VMEM((PAD, HALF), F32),
                        pltpu.VMEM((BLOCK, width), LOW),
                        pltpu.VMEM((PAD, HALF), F32),
                        pltpu.VMEM((8, sz.lin), F32),
                        pltpu.VMEM((8, width), F32),
                        pltpu.SemaphoreType.DMA((4,)),
                    ],
                ),
                out_shape=[
                    parts_shape,
                    parts_shape,
                    shape((tok, wide), LOW),
                    shape((tok, channels), LOW),
                    shape((PAD, 3 * channels), LOW),
                    shape((PAD, chunk), LOW),
                    shape((channels, sz.states), F32),
                    shape((8, sz.lin), F32),
                    index_shape,
                ]
                + mixed_shape,
                compiler_params=options,
                cost_estimate=cost(8 * dense, 16e6),
            )(
                sc, *sources, normed, gl, lin, ssd, inc, decays, *gains, *raw, *sent,
                halo, halo_grad, begin,
            )

        halo_grad = jnp.zeros((8, sz.lin), F32)
        begin = jnp.zeros((channels, sz.states), F32)
        if spans == 1:
            return call(halo_grad, begin)
        local = call(halo_grad, begin)[6]
        for _ in range(spans - 1):
            begin = next_span(span_total(decays) * begin + local, -1)
        halo_grad = next_span(call(halo_grad, begin)[7], -1)
        return call(halo_grad, begin)

    def scatter(sc, keep, send):
        joined = pl.pallas_call(
            functools.partial(join_kernel, sz),
            in_specs=[smem, vmem, vmem],
            out_specs=[smem] + [vmem] * head_axis,
            out_shape=[index_shape, shape((rows + PAD, chunk), F32)]
            + [shape((rows + PAD, chunk), LOW)] * (head_axis - 1),
            compiler_params=options,
        )(sc, keep, cross(send))
        return [joined[1]] + [over_heads(joined[1 + d], d) for d in range(1, head_axis)], joined[0]

    def gather(low):
        own = [low] + [over_heads(low, d) for d in range(1, head_axis)]
        return own + [cross(x) for x in own]

    def section_output(layer, sc, parts, resid):
        return pl.pallas_call(
            functools.partial(output_kernel, sz, layer),
            in_specs=[smem] + [vmem] * (head_axis + 1),
            out_shape=[
                shape((rows, chunk), F32),
                shape((rows, chunk), LOW),
                shape((rows, chunk), F32),
                shape((8, HALF), F32),
            ],
            compiler_params=options,
        )(sc, *parts, resid)

    def section_input(layer, sc, parts, *others):
        return pl.pallas_call(
            functools.partial(input_kernel, sz, layer),
            in_specs=[smem] + [vmem] * (head_axis + len(others)),
            out_specs=[vmem, vmem, smem],
            out_shape=[
                shape((rows, chunk), F32),
                shape((rows + PAD, chunk), LOW),
                index_shape,
            ],
            compiler_params=options,
        )(sc, *parts, *others)

    part = width // seq

    columns = 3 * channels
    share = part // head_axis

    def weight_pieces(sc, normed, cat, mixed, scaled, small, common, *behind):
        count = len(behind)
        outs = pl.pallas_call(
            functools.partial(weights_kernel, sz, seq, count),
            in_specs=[smem] + [vmem] * 6 + [anywhere] * count,
            out_specs=[smem] + [anywhere] * (count > 0) + [vmem] * (seq + head_axis),
            out_shape=[index_shape]
            + [shape(x.shape, x.dtype) for x in behind[-1:]]
            + [shape((part + PAD, columns), LOW)] * seq
            + [shape((seq * share + PAD, shared), LOW)] * head_axis,
            scratch_shapes=[pltpu.VMEM((width, columns), LOW), pltpu.VMEM((width, shared), F32)],
            input_output_aliases={6 + count: 1} if count else {},
            compiler_params=options,
            cost_estimate=cost(4 * dense, 12e6),
        )(sc, normed, cat, mixed, scaled, small, common, *behind)
        chunks = outs[-seq - head_axis : -head_axis]
        pieces = [chunks[0]]
        for r in range(1, seq):
            pieces.append(lax.ppermute(chunks[r], "seq", [(i, (i + r) % seq) for i in range(seq)]))
        by_head = [over_heads(outs[d - head_axis], d) if d else outs[-head_axis] for d in range(head_axis)]
        return pieces, by_head, outs[0], outs[1]

    def leave(sc, *arrays):
        pieces = pl.pallas_call(
            functools.partial(leave_kernel, sz, slots),
            in_specs=[smem] + [vmem] * 4,
            out_shape=[shape((BLOCK, chunk), LOW)] * slots,
            compiler_params=options,
        )(sc, *arrays)
        return [turn(x, r) for r, x in enumerate(pieces)]

    fw0, halo0 = forward(0, sc, tok_pieces)
    base0, decays = fw0[11], fw0[12:14]
    parts, sc_join = scatter(sc, fw0[7], fw0[8])
    out_pieces, unused = take_rows(sc_join, grad_out, None)
    res1, low1, mixed0, square0 = section_output(0, sc, parts, base0)
    pieces1 = gather(low1)
    square_other = cross(square0)

    fw1, halo1 = forward(1, sc, pieces1 + out_pieces + [decays[1]])
    stat = fw1[6] + cross(fw1[6])
    stats = [stat] + [over_heads(stat, d) for d in range(1, head_axis)]
    parts_out, sc_out = scatter(sc, fw1[7], fw1[8])
    bw1 = backward(1, sc_out, [fw1[12]] + stats, fw1[:5], decays[1], halo1)
    sc_out, send = after(bw1[8], *parts_out[1:], bw1[1])
    parts, sc_join = scatter(sc_out, bw1[0], send)
    weights1, heads1, sc_weights, unused = weight_pieces(
        sc_join, fw1[0], bw1[2], fw1[12], *bw1[3:6]
    )
    igrad1, glow1, sc_in = section_input(
        1, sc_weights, parts, res1, fw1[11], fw1[5], *gains, mixed0
    )
    piecesg = gather(glow1)

    bw0 = backward(0, sc, piecesg + [square0, square_other], fw0[:5], decays[0], halo0)
    weights0, heads0, sc_weights, send = weight_pieces(
        bw0[8], fw0[0], bw0[2], bw0[9], *bw0[3:6], *weights1, bw0[1]
    )
    parts, sc_join = scatter(sc_weights, bw0[0], send)
    igrad0, glow0, sc_end = section_input(0, sc_join, parts, base0, igrad1, fw0[5], *gains)

    unused, low2, unused_mixed, unused_square = section_output(1, sc_in, parts_out, res1)
    early = leave(sc_in, low1, pieces1[head_axis], glow1, piecesg[head_axis])
    swapped = cross(pick(first, low2, glow0[:rows]))
    late = leave(sc_end, glow0, swapped, low2, swapped)
    section_out, input_grad = pl.pallas_call(
        functools.partial(home_kernel, slots),
        in_specs=[smem] + [vmem] * (2 * slots),
        out_shape=[shape((slots, BLOCK, chunk), F32)] * 2,
        compiler_params=options,
    )(sc, *early, *late)

    def summed(sc, pieces):
        return pl.pallas_call(
            functools.partial(sum_kernel, sz),
            in_specs=[smem] + [vmem] * seq,
            out_shape=shape((part + PAD, columns), LOW),
            compiler_params=options,
        )(sc, *pieces)

    sums1, sums0 = summed(sc_in, weights1), summed(sc_end, weights0)
    shared_shape = (seq * share + PAD, shared)
    shared_own, shared_sent = pl.pallas_call(
        functools.partial(heads_kernel, sz),
        in_specs=[smem] + [vmem] * (2 * head_axis),
        out_shape=[shape(shared_shape, F32), shape(shared_shape, LOW)],
        compiler_params=options,
    )(sc_end, *heads0, *heads1)
    spans_of = pl.pallas_call(
        functools.partial(spans_kernel, sz),
        in_specs=[vmem, vmem],
        out_shape=[shape((share + PAD, shared), LOW)] * seq,
        compiler_params=options,
    )(shared_own, cross(shared_sent))
    shared_parts = [spans_of[0]]
    for r in range(1, seq):
        pairs = [(i, (i + r) % seq) for i in range(seq)]
        shared_parts.append(lax.ppermute(spans_of[r], "seq", pairs))
    final = pl.pallas_call(
        functools.partial(final_kernel, sz),
        in_specs=[smem] + [vmem] * (3 + seq),
        out_shape=[
            shape((part, inner_dev), F32),
            shape((part, inner_dev), F32),
            shape((inner_dev, part), F32),
            shape((taps, inner_dev), F32),
            shape((1, inner_dev), F32),
            shape((1, heads_dev), F32),
            shape((share, shared), F32),
            shape((PAD // 2, shared), F32),
        ],
        compiler_params=options,
    )(sc, sums0, sums1, cross(pick(first, sums1, sums0)), *shared_parts)
    common = final[7]
    place = z * head_axis + h
    conv_part = shared // (seq * head_axis)
    gain_part = width // (seq * head_axis)
    return (
        section_out[None],
        input_grad[None],
        lax.dynamic_slice_in_dim(common[taps:].reshape(-1), place * gain_part, gain_part, 0)[None],
        final[0][None],
        final[1][None],
        final[6][None],
        final[3][None],
        lax.dynamic_slice_in_dim(common[:taps], place * conv_part, conv_part, 1)[None],
        final[5],
        final[4],
        final[2][None],
    )


def solution(mesh):
    placed = (
        P(None, "seq", None),
        P(),
        P("section", None, "head", "seq"),
        P(None, "seq", None),
        P("section", None),
        P("section", None, "head"),
        P("section", None, "head"),
        P("section", None, None),
        P("section", None, "head"),
        P("section", None, None),
        P("section", "head"),
        P("section", "head"),
        P("section", None, None),
    )
    return jax.shard_map(
        per_device,
        mesh=mesh,
        in_specs=placed,
        out_specs=(
            P("section", None, "seq", "head"),
            P("section", None, "seq", "head"),
            P("section", ("seq", "head")),
            P("section", "seq", "head"),
            P("section", "seq", "head"),
            P("section", ("seq", "head"), None),
            P("section", None, "head"),
            P("section", None, ("seq", "head")),
            P("section", "head"),
            P("section", "head"),
            P("section", "head", "seq"),
        ),
        check_vma=False,
    )
```

```python
import functools

import jax
import jax.numpy as jnp
from jax import lax
from jax.experimental import pallas as pl
from jax.experimental.pallas import tpu as pltpu
from jax.sharding import PartitionSpec as P

BLOCK = 256
HALF = BLOCK // 2
PAD = 16
EPS = 1e-05
F32 = jnp.float32
LOW = jnp.bfloat16
HIDDEN = -1e30
NN = ((1,), (0,))
NT = ((1,), (1,))
TN = ((0,), (0,))
VMEM_BYTES = 50 * 1024 * 1024


def dot(a, b, dims):
    return lax.dot_general(a, b, (dims, ((), ())), preferred_element_type=F32)


def aligned(start, size):
    return pl.ds(pl.multiple_of(start, size), size)


def spread(cols, first, count, width):
    rows = cols.shape[0]
    lane = lax.broadcasted_iota(jnp.int32, (rows, count * width), 1)
    out = jnp.broadcast_to(cols[:, first : first + 1], (rows, count * width))
    for h in range(1, count):
        out = jnp.where(lane >= h * width, cols[:, first + h : first + h + 1], out)
    return out


def per_head(array, h, width):
    lane = lax.broadcasted_iota(jnp.int32, array.shape, 1)
    inside = (lane >= h * width) & (lane < (h + 1) * width)
    return jnp.where(inside, array, jnp.zeros_like(array))


def split_low(value):
    high = value.astype(LOW).astype(F32)
    return high, value - high


def column_of(row, size):
    return jnp.transpose(jnp.broadcast_to(row, (128, size)))


def sigmoid(v):
    return 0.5 * jnp.tanh(0.5 * v) + 0.5


def pick(flag, a, b):
    return jnp.where(flag, a, b)


class Sizes:
    def __init__(self, blocks, width, channels, heads, states, taps, head_axis, inner):
        self.blocks = blocks
        self.width = width
        self.channels = channels
        self.heads = heads
        self.head_width = channels // heads
        self.states = states
        self.lin = channels + 2 * states
        self.taps = taps
        self.head_axis = head_axis
        self.chunk = width // head_axis
        self.rows = blocks * HALF
        self.tokens = blocks * BLOCK
        self.inner = inner


def weight_copies(sz, layer, c, h, raw, got, wv, ov, sems):
    gate, inner, shared, out = raw
    ch = sz.channels
    cols = aligned(c * ch, ch)
    rows = aligned((h * 2 + c) * ch, ch)
    own = [
        (gate.at[0, :, cols], wv.at[:, :ch]),
        (inner.at[0, :, cols], wv.at[:, ch : 2 * ch]),
        (shared.at[0], wv.at[:, 2 * ch :]),
        (out.at[0, rows, :], ov),
    ]
    sent = [(got[0], wv), (got[1], ov)]
    return [
        (c == layer, [pltpu.make_async_copy(p, q, sems.at[i]) for i, (p, q) in enumerate(own)]),
        (c != layer, [pltpu.make_async_copy(p, q, sems.at[i]) for i, (p, q) in enumerate(sent)]),
    ]


def run_copies(choices, start, wait):
    for flag, copies in choices:

        @pl.when(flag)
        def _(copies=copies):
            if start:
                for copy in copies:
                    copy.start()
            if wait:
                for copy in copies:
                    copy.wait()


def put_ordered(sz, dst, c, k, b, own, other):
    for r in range(len(own)):

        @pl.when(lax.rem(k - b + len(own), len(own)) == r)
        def _(r=r):
            put_pair(dst, c, own[r][:HALF, :], other[r][:HALF, :])


def put_pair(dst, c, own, other):
    dst[aligned(c * HALF, HALF), :] = own
    dst[aligned((1 - c) * HALF, HALF), :] = other


def put_pieces(sz, dst, c, h, own, other):
    for d in range(sz.head_axis):
        cols = aligned((h ^ d) * sz.chunk, sz.chunk)
        dst[aligned(c * HALF, HALF), cols] = own[d]
        dst[aligned((1 - c) * HALF, HALF), cols] = other[d]


def put_parts(sz, b, c, h, part, keep, send):
    for d in range(sz.head_axis):
        cols = aligned((h ^ d) * sz.chunk, sz.chunk)
        keep[d, aligned(b * HALF, HALF), :] = part[aligned(c * HALF, HALF), cols]
        send[d, aligned(b * HALF, HALF), :] = part[aligned((1 - c) * HALF, HALF), cols]


def put_scalars(b, c, row, kept, sent):
    for scratch, flag in ((kept, c == 0), (sent, c != 0)):
        high, low = split_low(pick(flag, row[:, :HALF], row[:, HALF:]))
        line = lax.broadcasted_iota(jnp.int32, scratch.shape, 0)
        lower = jnp.where(line == 8 + b, low, scratch[...])
        scratch[...] = jnp.where(line == b, high, lower)


def line_of(table, at):
    line = lax.broadcasted_iota(jnp.int32, table.shape, 0)
    return jnp.sum(jnp.where(line == at, table, 0.0), axis=0, keepdims=True)


def close_parts(sz, keep, send, kept, sent):
    for scratch, out in ((kept, keep), (sent, send)):
        extra = jnp.concatenate([scratch[...]] * (sz.chunk // HALF), axis=1).astype(LOW)
        for d in range(sz.head_axis):
            out[d, sz.rows :, :] = extra


def conv_forward(sz, ext, taps):
    pre = taps[0:1] * ext[5 : 5 + BLOCK, :]
    for j in range(1, sz.taps):
        pre = pre + taps[j : j + 1] * ext[5 + j : 5 + j + BLOCK, :]
    return pre


def decay_of(sz, cols, rp, h, mask):
    rows = cols[:, h : h + 1] + rp[12 + h : 13 + h, :]
    return jnp.exp(jnp.where(mask, rows, HIDDEN))


def lower_mask():
    t = lax.broadcasted_iota(jnp.int32, (BLOCK, BLOCK), 0)
    s = lax.broadcasted_iota(jnp.int32, (BLOCK, BLOCK), 1)
    return t >= s


def forward_kernel(sz, layer, slots, sc, *refs):
    n = sz.head_axis
    sources = 2 * slots if layer == 0 else 2 * n + 2 * slots
    src, refs = refs[:sources], refs[sources:]
    if layer == 1:
        table, refs = refs[0], refs[1:]
    gains, raw, got, halo, begin = refs[0:2], refs[2:6], refs[6:8], refs[8], refs[9]
    normed_o, gl_o, lin_o, ssd_o, inc_o, inv_o, part_o, keep, send, fin_o, sc_o, base_o = refs[10:22]
    refs = refs[22:]
    if layer == 1:
        mixed_o, refs = refs[0], refs[1:]
    else:
        tables_o, refs = refs[0:2], refs[2:]
    xs, ms, wv, ov, ext, state, kept, sent, part, sems = refs
    b = pl.program_id(0)
    c, h, k = sc[0], sc[1], sc[3]
    ch, st = sz.channels, sz.states
    copies = weight_copies(sz, layer, c, h, raw, got, wv, ov, sems)

    @pl.when(b == 0)
    def _():
        run_copies(copies, True, False)
        ext[0:8, :] = halo[...]
        state[...] = begin[...]
        kept[...] = jnp.zeros_like(kept)
        sent[...] = jnp.zeros_like(sent)
        for i in range(4):
            sc_o[i] = sc[i]

    mine = aligned(c * HALF, HALF)
    cols = aligned(h * sz.chunk, sz.chunk)
    if layer == 0:
        put_ordered(sz, xs, c, k, b, src[:slots], src[slots:])
        base_o[...] = xs[mine, cols]
        for r in range(slots):

            @pl.when(lax.rem(k - b + slots, slots) == r)
            def _(r=r):
                own = decay_table(rates_of(src[r]), c, sz.heads)
                other = decay_table(rates_of(src[slots + r]), c, sz.heads)
                tables_o[0][...] = pick(c == 0, own, other)
                tables_o[1][...] = pick(c == 0, other, own)

        rp = tables_o[0][...]
    else:
        put_pieces(sz, xs, c, h, [r[...] for r in src[:n]], [r[...] for r in src[n : 2 * n]])
        put_ordered(sz, ms, c, k, b, src[2 * n : 2 * n + slots], src[2 * n + slots :])
        base_o[...] = ms[mine, cols]
        mixed_o[...] = ms[...]
        rp = table[...]

    pv = pick(c == layer, gains[0][...], gains[1][...])
    x = xs[...].astype(F32)
    inv_in = lax.rsqrt(jnp.mean(x * x, axis=1, keepdims=True) + EPS)
    normed = (x * inv_in * pv[0:1, : sz.width]).astype(LOW)
    normed_o[...] = normed

    @pl.when(b == 0)
    def _():
        run_copies(copies, False, True)

    proj = dot(normed, wv[...], NN)
    gl = proj[:, :ch]
    gl_o[...] = gl
    lin = proj[:, ch:].astype(LOW)
    lin_o[...] = lin
    ext[8 : 8 + BLOCK, :] = lin.astype(F32)
    pre = conv_forward(sz, ext, pv[1:5, : sz.lin])
    ext[0:8, :] = ext[BLOCK : BLOCK + 8, :]
    act = (pre * sigmoid(pre)).astype(LOW)
    values, bm, cm = act[:, :ch], act[:, ch : ch + st], act[:, ch + st :]

    cols = jnp.transpose(rp)
    mask = lower_mask()
    gram = dot(cm, bm, NT)
    mixes, parts = [], []
    for i in range(sz.heads):
        mixes.append((gram * decay_of(sz, cols, rp, i, mask)).astype(LOW))
        parts.append(per_head(values, i, sz.head_width))
    intra = dot(jnp.concatenate(mixes, axis=1), jnp.concatenate(parts, axis=0), NN)

    low_state = state[...].astype(LOW)
    inc_o[0] = low_state
    ecum = spread(cols, sz.heads, sz.heads, sz.head_width)
    inter = dot(cm, low_state, NT) * ecum
    vf = values.astype(F32)
    carried = (vf * spread(cols, 2 * sz.heads, sz.heads, sz.head_width)).astype(LOW)
    local = dot(carried, bm, TN)
    for i in range(sz.heads):
        rows = slice(i * sz.head_width, (i + 1) * sz.head_width)
        total = cols[BLOCK - 1 : BLOCK, sz.heads + i : sz.heads + i + 1]
        state[rows, :] = total * state[rows, :] + local[rows]
    ssd = intra + inter + pv[6:7, :ch] * vf
    ssd_o[...] = ssd
    gated = ssd * (gl * sigmoid(gl))
    weighty = gated * pv[5:6, :ch]
    part[...] = dot(weighty.astype(LOW), ov[...], NN).astype(LOW)

    lane = lax.broadcasted_iota(jnp.int32, (BLOCK, 128), 1)
    square = jnp.sum(gated * gated, axis=1, keepdims=True)
    if layer == 0:
        project = jnp.zeros_like(square)
    else:
        scaled_grad = dot(ms[...], ov[...], NT)
        project = jnp.sum(scaled_grad * weighty, axis=1, keepdims=True)
    stats = jnp.where(lane == 0, square, jnp.where(lane == 1, project, inv_in))
    stats = jnp.transpose(stats)
    part_o[...] = stats[0:2, :]
    inv_o[...] = stats[2:3, :]
    put_scalars(b, c, stats[0:1, :], kept, sent)
    put_parts(sz, b, c, h, part, keep, send)

    @pl.when(b == sz.blocks - 1)
    def _():
        close_parts(sz, keep, send, kept, sent)
        fin_o[...] = state[...]


def backward_kernel(sz, layer, sc, *refs):
    n = sz.head_axis
    sources = 2 * n + 2 if layer == 0 else 1 + n
    src, refs = refs[:sources], refs[sources:]
    normed_r, gl_r, lin_r, ssd_r, inc_r = refs[:5]
    table, gains, raw, got = refs[5], refs[6:8], refs[8:12], refs[12:14]
    halo, halo_grad, begin = refs[14:17]
    keep, send, cat_o, scaled_o, small_o, common_o, fin_o, rim_o, sc_o = refs[17:26]
    refs = refs[26:]
    if layer == 0:
        mixed_o, refs = refs[0], refs[1:]
    ms, wv, ov, ext, back, state, kept, sent, part, heads_p, small, wide, sems = refs
    i_step = pl.program_id(0)
    b = sz.blocks - 1 - i_step
    c, h = sc[0], sc[1]
    ch, st = sz.channels, sz.states
    copies = weight_copies(sz, layer, c, h, raw, got, wv, ov, sems)
    pv = pick(c == layer, gains[0][...], gains[1][...])
    rp = table[...]

    @pl.when(i_step == 0)
    def _():
        run_copies(copies, True, True)
        back[BLOCK : BLOCK + 8, :] = halo_grad[...]
        state[...] = begin[...]
        kept[...] = jnp.zeros_like(kept)
        sent[...] = jnp.zeros_like(sent)
        small[...] = jnp.zeros_like(small)
        wide[...] = jnp.zeros_like(wide)
        for i in range(4):
            sc_o[i] = sc[i]
        if layer == 0:
            for i in range(2):
                extra = src[i * n][sz.rows :, :].astype(F32)
                for d in range(1, n):
                    extra = extra + src[i * n + d][sz.rows :, :].astype(F32)
                heads_p[8 * i : 8 * i + 8, :] = extra[0:8, :HALF] + extra[8:16, :HALF]

    if layer == 0:
        rows = aligned(b * HALF, HALF)
        put_pieces(
            sz, ms, c, h, [r[rows, :] for r in src[:n]], [r[rows, :] for r in src[n : 2 * n]]
        )
        halves = []
        for k in range(2):
            alpha = lax.rsqrt(line_of(src[2 * n + k][...], b) / sz.inner + EPS)
            beta = alpha * alpha * line_of(heads_p[...], 8 * k + b) / sz.inner
            halves.append((alpha, beta))
        alpha, beta = (
            pick(
                c == 0,
                jnp.concatenate([halves[0][q], halves[1][q]], axis=1),
                jnp.concatenate([halves[1][q], halves[0][q]], axis=1),
            )
            for q in range(2)
        )
    else:
        stats = src[1][...]
        for d in range(1, n):
            stats = stats + src[1 + d][...]
        alpha = lax.rsqrt(stats[0:1, :] / sz.inner + EPS)
        beta = alpha * alpha * alpha * stats[1:2, :] / sz.inner

    sub = lax.broadcasted_iota(jnp.int32, rp.shape, 0)
    cols = jnp.transpose(jnp.where(sub == 12, alpha, jnp.where(sub == 13, beta, rp)))
    alpha, beta = cols[:, 12:13], cols[:, 13:14]

    gl = gl_r[...]
    ssd = ssd_r[...]
    sig = sigmoid(gl)
    swish = gl * sig
    slope = sig * (1.0 + gl * (1.0 - sig))
    gated = ssd * swish
    if layer == 0:
        mixed_grad = ms[...]
        mixed_o[...] = mixed_grad
    else:
        mixed_grad = src[0][...]
    scaled_grad = dot(mixed_grad, ov[...], NT)
    gain = pv[5:6, :ch]
    normal = gated * alpha
    small[4:5, :ch] += jnp.sum(scaled_grad * normal, axis=0, keepdims=True)
    scaled_o[...] = (normal * gain).astype(LOW)
    gated_grad = alpha * (scaled_grad * gain) - beta * gated
    ssd_grad = (gated_grad * swish).astype(LOW)
    gate_grad = (gated_grad * ssd * slope).astype(LOW)
    sgf = ssd_grad.astype(F32)

    before = lin_r[pl.ds(pl.multiple_of(jnp.maximum(b * BLOCK - 16, 0), 16), 16), :]
    ext[0:8, :] = pick(b > 0, before.astype(F32)[8:16, :], halo[...])
    ext[8 : 8 + BLOCK, :] = lin_r[aligned(b * BLOCK, BLOCK), :].astype(F32)
    taps = pv[1:5, : sz.lin]
    pre = conv_forward(sz, ext, taps)
    psig = sigmoid(pre)
    pact = pre * psig
    pslope = psig * (1.0 + pre * (1.0 - psig))
    act = pact.astype(LOW)
    values, bm, cm = act[:, :ch], act[:, ch : ch + st], act[:, ch + st :]
    vf = values.astype(F32)
    small[5:6, :ch] += jnp.sum(sgf * vf, axis=0, keepdims=True)

    mask = lower_mask()
    gram = dot(cm, bm, NT)
    gram_grad = jnp.zeros((BLOCK, BLOCK), F32)
    mixes, parts = [], []
    for i in range(sz.heads):
        decay = decay_of(sz, cols, rp, i, mask)
        mixes.append((gram * decay).astype(LOW))
        parts.append(per_head(ssd_grad, i, sz.head_width))
        gram_grad = gram_grad + dot(parts[-1], values, NT) * decay
    intra_grad = dot(jnp.concatenate(mixes, axis=0), jnp.concatenate(parts, axis=0), TN)

    ecum = spread(cols, sz.heads, sz.heads, sz.head_width)
    to_end = spread(cols, 2 * sz.heads, sz.heads, sz.head_width)
    inter_grad = (sgf * ecum).astype(LOW)
    low_state = state[...].astype(LOW)
    carried = (vf * to_end).astype(LOW)
    carried_grad = dot(bm, low_state, NT)
    gram_low = gram_grad.astype(LOW)
    b_grad = dot(gram_low, cm, TN) + dot(carried, low_state, NN)
    c_grad = dot(gram_low, bm, NN) + dot(inter_grad, inc_r[0], NN)
    value_grad = intra_grad + pv[6:7, :ch] * sgf + carried_grad * to_end
    entry = dot(inter_grad, cm, TN)
    for i in range(sz.heads):
        rows = slice(i * sz.head_width, (i + 1) * sz.head_width)
        total = cols[BLOCK - 1 : BLOCK, sz.heads + i : sz.heads + i + 1]
        state[rows, :] = total * state[rows, :] + entry[rows]

    pre_grad = jnp.concatenate([value_grad, b_grad, c_grad], axis=1) * pslope
    back[0:BLOCK, :] = pre_grad
    lin_grad = taps[0:1] * back[sz.taps - 1 : sz.taps - 1 + BLOCK, :]
    for j in range(1, sz.taps):
        at = sz.taps - 1 - j
        lin_grad = lin_grad + taps[j : j + 1] * back[at : at + BLOCK, :]
    for j in range(sz.taps):
        small[j : j + 1, :] += jnp.sum(pre_grad * ext[5 + j : 5 + j + BLOCK, :], axis=0, keepdims=True)
    back[BLOCK : BLOCK + 8, :] = back[0:8, :]
    cat = jnp.concatenate([gate_grad, lin_grad.astype(LOW)], axis=1)
    cat_o[...] = cat
    normed_grad = dot(cat, wv[...], NT)
    part[...] = normed_grad.astype(LOW)
    product = normed_grad * normed_r[...].astype(F32)
    wide[0:1, :] += jnp.sum(product, axis=0, keepdims=True)
    along = jnp.sum(product, axis=1, keepdims=True)
    along = jnp.transpose(jnp.broadcast_to(along, (BLOCK, 128)))
    put_scalars(b, c, along[0:1, :], kept, sent)
    put_parts(sz, b, c, h, part, keep, send)

    @pl.when(i_step == sz.blocks - 1)
    def _():
        close_parts(sz, keep, send, kept, sent)
        fin_o[...] = state[...]
        rim_o[...] = back[0:8, :]
        sums = small[...]
        flat = [sums[j : j + 1, :ch] for j in range(sz.taps + 2)]
        flat = [jnp.concatenate(flat[j : j + 3], axis=1) for j in range(0, len(flat), 3)]
        flat = flat + [jnp.zeros_like(flat[0])] * (4 - len(flat))
        high, low = split_low(jnp.concatenate(flat, axis=0))
        rest = jnp.zeros((PAD - 8, high.shape[1]), F32)
        small_o[...] = jnp.concatenate([high, low, rest], axis=0).astype(LOW)
        gain_grad = wide[0:1, :] / pv[0:1, :]
        flat = [sums[j : j + 1, ch:] for j in range(sz.taps)]
        flat += [gain_grad[:, q * sz.chunk : (q + 1) * sz.chunk] for q in range(n)]
        high, low = split_low(jnp.concatenate(flat, axis=0))
        common_o[...] = jnp.concatenate([high, low], axis=0).astype(LOW)


def weights_kernel(sz, seq, in_one, sc, normed, cat, mixed, scaled, small, common, *refs):
    sc_o, outs, heads, full, wide = refs[0], refs[1:-3], refs[-3], refs[-2], refs[-1]
    for i in range(4):
        sc_o[i] = sc[i]
    ch, st = sz.channels, sz.states
    step = sz.chunk
    for q in range(sz.head_axis):
        at = slice(q * step, (q + 1) * step)
        grads = dot(normed[:, at], cat[...], TN)
        full[at, : 2 * ch] = grads[:, : 2 * ch].astype(LOW)
        wide[at, :] = grads[:, 2 * ch :]
        full[at, 2 * ch :] = dot(mixed[:, at], scaled[...], TN).astype(LOW)
    rows = sz.width // seq
    part = rows // sz.head_axis
    for r in range(seq):
        if in_one:
            at = r * (rows + PAD)
            outs[0][at : at + rows, :] = full[r * rows : (r + 1) * rows, :]
            outs[0][at + rows : at + rows + PAD, :] = small[...]
        else:
            outs[r][:rows, :] = full[aligned(lax.rem(sc[2] + r, seq) * rows, rows), :]
            outs[r][rows:, :] = small[...]
    extra = common[...].astype(F32)
    for i in range(seq * sz.head_axis):
        lines = jnp.concatenate([extra, wide[i * part : (i + 1) * part, :]], axis=0)
        heads[i * (part + PAD) : (i + 1) * (part + PAD), :] = lines.astype(LOW)


def join_kernel(sz, sc, keep, recv, sc_o, own, *sends):
    rows = sz.rows
    for i in range(4):
        sc_o[i] = sc[i]
    extra = keep[0, rows:, :].astype(F32) + recv[0, rows:, :].astype(F32)
    high, low = split_low(extra[0:8, :] + extra[8:16, :])
    extra = jnp.concatenate([high, low], axis=0)
    for d, out in enumerate((own,) + sends):
        out[:rows, :] = (keep[d, :rows, :].astype(F32) + recv[d, :rows, :].astype(F32)).astype(out.dtype)
        out[rows:, :] = extra.astype(out.dtype)


def total_of(parts, rows):
    total = parts[0][rows, :].astype(F32)
    for p in parts[1:]:
        total = total + p[rows, :].astype(F32)
    return total


def output_kernel(sz, layer, sc, *refs):
    n = sz.head_axis
    parts, refs = refs[:n], refs[n:]
    resid, res_o, low_o, mixed_o, square_o = refs
    extra = total_of(parts, slice(sz.rows, sz.rows + PAD))
    square = extra[0:8, :HALF] + extra[8:16, :HALF]
    square_o[...] = square
    inv = lax.rsqrt(square / sz.inner + EPS)
    for b in range(sz.blocks):
        rows = slice(b * HALF, (b + 1) * HALF)
        col = column_of(inv[b : b + 1, :], HALF)[:, 0:1]
        mixed = total_of(parts, rows) * col
        res = resid[rows, :].astype(F32) + mixed
        res_o[rows, :] = res
        low_o[rows, :] = res.astype(LOW)
        mixed_o[rows, :] = mixed


def input_kernel(sz, layer, sc, *refs):
    n = sz.head_axis
    parts, refs = refs[:n], refs[n:]
    resid, outg, inv_r, gains = refs[0], refs[1], refs[2], refs[3:5]
    refs = refs[5:]
    if layer == 1:
        mixed, refs = refs[0], refs[1:]
    grad_o, low_o, sc_o = refs
    for i in range(4):
        sc_o[i] = sc[i]
    c, h = sc[0], sc[1]
    mine = aligned(h * sz.chunk, sz.chunk)
    gain = pick(c == layer, gains[0][0:1, mine], gains[1][0:1, mine])
    extra = total_of(parts, slice(sz.rows, sz.rows + PAD))
    along = extra[0:8, :HALF] + extra[8:16, :HALF]
    tops, lows = [], []
    for b in range(sz.blocks):
        rows = slice(b * HALF, (b + 1) * HALF)
        at = b * BLOCK
        inv_row = pick(c == 0, inv_r[:, at : at + HALF], inv_r[:, at + HALF : at + BLOCK])
        inv = column_of(inv_row, HALF)[:, 0:1]
        share = column_of(along[b : b + 1, :] / sz.width, HALF)[:, 0:1]
        total = total_of(parts, rows)
        base = resid[rows, :].astype(F32)
        grad = outg[rows, :].astype(F32) + inv * (total * gain - base * (inv * share))
        grad_o[rows, :] = grad
        low = grad.astype(LOW)
        low_o[rows, :] = low
        if layer == 1:
            dots = jnp.sum(low.astype(F32) * mixed[rows, :], axis=1, keepdims=True)
            row = jnp.transpose(jnp.broadcast_to(dots, (HALF, 128)))[0:1, :]
            high, rest = split_low(row)
            tops.append(high)
            lows.append(rest)
    if layer == 1:
        fill = [jnp.zeros((8 - sz.blocks, HALF), F32)] if sz.blocks < 8 else []
        extra = jnp.concatenate(tops + fill + lows + fill, axis=0)
        extra = jnp.concatenate([extra] * (sz.chunk // HALF), axis=1)
        low_o[sz.rows :, :] = extra.astype(LOW)
    else:
        low_o[sz.rows :, :] = jnp.zeros((PAD, sz.chunk), LOW)


def sum_kernel(sz, sc, *refs):
    parts, out = refs[:-1], refs[-1]
    rows = out.shape[0] - PAD
    out[:rows, :] = total_of(parts, slice(0, rows)).astype(LOW)
    extra = total_of(parts, slice(rows, rows + PAD))
    high, low = split_low(extra[0:4, :] + extra[4:8, :])
    extra = jnp.concatenate([high, low, jnp.zeros((PAD - 8, extra.shape[1]), F32)], axis=0)
    out[rows:, :] = extra.astype(LOW)


def final_kernel(sz, sc, zero, one, got, shared_zero, shared_one, shared_got, *refs):
    gate_o, inner_o, out_o, conv_o, norm_o, skip_o, shared_o, common_o = refs
    c = sc[0]
    ch = sz.channels
    rows = zero.shape[0] - PAD
    lane = lax.broadcasted_iota(jnp.int32, skip_o.shape, 1)
    skip = jnp.zeros(skip_o.shape, F32)
    for i in range(2):
        which = pick(i == 0, c, 1 - c)
        to = aligned(which * ch, ch)
        sums = (pick(c == 0, zero[...], one[...]) if i == 0 else got[...]).astype(F32)
        gate_o[:, to] = sums[:rows, :ch]
        inner_o[:, to] = sums[:rows, ch : 2 * ch]
        out_o[to, :] = jnp.transpose(sums[:rows, 2 * ch :])
        lines = sums[rows : rows + 4, :] + sums[rows + 4 : rows + 8, :]
        for j in range(sz.taps):
            conv_o[j : j + 1, to] = lines[j // 3 : j // 3 + 1, (j % 3) * ch : (j % 3 + 1) * ch]
        norm_o[:, to] = lines[1:2, ch : 2 * ch]
        skips = lines[1:2, 2 * ch :]
        for q in range(sz.heads):
            part = jnp.sum(per_head(skips, q, sz.head_width), axis=1, keepdims=True)
            skip = jnp.where(lane == which * sz.heads + q, part, skip)
    skip_o[...] = skip
    total = pick(c == 0, shared_zero[...], shared_one[...]).astype(F32) + shared_got[...].astype(F32)
    shared_o[...] = total[PAD:]
    common_o[...] = total[: PAD // 2] + total[PAD // 2 : PAD]


def slice_kernel(sz, slots, with_rates, sc, order, *refs):
    sources = 2 if with_rates else 1
    src, refs = refs[:sources], refs[sources:]
    outs, sc_o, refs = refs[:slots], refs[slots], refs[slots + 1 :]
    sems = refs[-1]
    copies = []
    for r in range(slots):
        which = order[lax.rem(sc[3] + r, slots)]
        rows = src[0].at[which, aligned(sc[0] * HALF, HALF), :]
        to = outs[r].at[:HALF] if with_rates else outs[r]
        copies.append(pltpu.make_async_copy(rows, to, sems.at[r]))
    for copy in copies:
        copy.start()
    for i in range(4):
        sc_o[i] = sc[i]
    if with_rates:
        thirds = refs[0]
        for r in range(slots):
            which = order[lax.rem(sc[3] + r, slots)]
            first, rest = split_low(src[1][0, which])
            second, rest = split_low(rest)
            lines = jnp.concatenate([first, second, rest, jnp.zeros_like(rest)], axis=1)
            lines = jnp.concatenate([lines, jnp.zeros_like(lines)], axis=0)
            thirds[r] = lines.astype(LOW)
        more = [
            pltpu.make_async_copy(thirds.at[r], outs[r].at[HALF:], sems.at[slots + r])
            for r in range(slots)
        ]
        for copy in more:
            copy.start()
        copies = copies + more
    for copy in copies:
        copy.wait()


def pass_kernel(count, sc, *refs):
    for i in range(4):
        refs[-count - 1][i] = sc[i]


def rates_of(piece):
    lines = piece[HALF:, :].astype(F32)[:8, :]
    return (lines[:, :BLOCK] + lines[:, BLOCK : 2 * BLOCK]) + lines[:, 2 * BLOCK : 3 * BLOCK]


def pack_kernel(sz, sc, gate, inner, shared, out, in_gain, conv_i, conv_s, skip, norm, *refs):
    w_o, o_o, mine_o, send_o, sems = refs
    c, h = sc[0], sc[1]
    ch = sz.channels
    cols = aligned((1 - c) * ch, ch)
    rows = aligned((h * 2 + 1 - c) * ch, ch)
    copies = [
        pltpu.make_async_copy(gate.at[0, :, cols], w_o.at[:, :ch], sems.at[0]),
        pltpu.make_async_copy(inner.at[0, :, cols], w_o.at[:, ch : 2 * ch], sems.at[1]),
        pltpu.make_async_copy(shared.at[0], w_o.at[:, 2 * ch :], sems.at[2]),
        pltpu.make_async_copy(out.at[0, rows, :], o_o, sems.at[3]),
    ]
    for copy in copies:
        copy.start()
    for which, ref in ((c, mine_o), (1 - c, send_o)):
        at = aligned(which * ch, ch)
        ref[...] = jnp.zeros_like(ref)
        ref[0:1, :] = in_gain[...]
        ref[1 : 1 + sz.taps, :ch] = conv_i[0, :, at]
        ref[1 : 1 + sz.taps, ch : sz.lin] = conv_s[0]
        ref[5:6, :ch] = norm[:, at]
        low = spread(skip[...], 0, sz.heads, sz.head_width)
        high = spread(skip[...], sz.heads, sz.heads, sz.head_width)
        ref[6:7, :ch] = pick(which == 0, low, high)
    for copy in copies:
        copy.wait()


def decay_table(rate, c, n):
    lane = lax.broadcasted_iota(jnp.int32, rate.shape, 1)
    cum = rate
    step = 1
    while step < BLOCK:
        cum = cum + jnp.where(lane >= step, pltpu.roll(cum, step, 1), 0.0)
        step *= 2
    end = cum[:, BLOCK - 1 :]
    lines = [cum, jnp.exp(cum), jnp.exp(end - cum) * -rate, jnp.log(-rate) - cum]
    low = jnp.concatenate([v[:n] for v in lines], axis=0)
    high = jnp.concatenate([v[n:] for v in lines], axis=0)
    return pick(c == 0, low, high)


def leave_kernel(sz, slots, sc, zero_own, zero_other, one_own, one_other, *outs):
    c = sc[0]
    for i in range(4):
        outs[slots][i] = sc[i]
    for r in range(slots):
        rows = aligned(lax.rem(sc[3] + r, slots) * HALF, HALF)
        own = pick(c == 0, zero_own[rows, :], one_own[rows, :])
        other = pick(c == 0, zero_other[rows, :], one_other[rows, :])
        put_pair(outs[r], c, own, other)


def home_kernel(slots, sc, *refs):
    early, late, out, grad = refs[:slots], refs[slots : 2 * slots], refs[-2], refs[-1]
    first = sc[0] == 0
    for r in range(slots):
        at = lax.rem(sc[3] - r + slots, slots)
        out[at] = pick(first, early[r][...], late[r][...]).astype(F32)
        grad[at] = pick(first, late[r][...], early[r][...]).astype(F32)


def whole(shape):
    return pl.BlockSpec(shape, lambda *_: (0,) * len(shape))


def per_device(
    tokens,
    slot_order,
    log_decay,
    grad_out,
    in_gain,
    w_gate,
    w_inner,
    w_shared,
    conv_inner,
    conv_shared,
    d_skip,
    norm_gain,
    w_out,
):
    slots = tokens.shape[0]
    span = tokens.shape[1]
    width = tokens.shape[2]
    seq = lax.axis_size("seq")
    head_axis = lax.axis_size("head")
    cores = lax.axis_size("section")
    spans = seq // slots
    c = lax.axis_index("section")
    z = lax.axis_index("seq")
    h = lax.axis_index("head")
    k = lax.rem(z, slots)
    inner_dev = w_gate.shape[2]
    channels = inner_dev // cores
    shared = w_shared.shape[2]
    heads_dev = d_skip.shape[1]
    taps = conv_inner.shape[1]
    sz = Sizes(
        slots * span // BLOCK,
        width,
        channels,
        heads_dev // cores,
        shared // 2,
        taps,
        head_axis,
        inner_dev * head_axis,
    )
    first = c == 0
    swap = [(0, 1), (1, 0)]
    nb, tok, rows, chunk = sz.blocks, sz.tokens, sz.rows, sz.chunk

    def cross(x):
        return lax.ppermute(x, "section", swap)

    def turn(x, r):
        pairs = [(i, i // slots * slots + (i % slots + r) % slots) for i in range(seq)]
        return lax.ppermute(x, "seq", pairs) if r else x

    def over_heads(x, d):
        return lax.ppermute(x, "head", [(i, i ^ d) for i in range(head_axis)])

    def next_span(x, way):
        pairs = [(i, i + way * slots) for i in range(seq) if 0 <= i + way * slots < seq]
        return lax.ppermute(x, "seq", pairs)

    def shape(dims, dtype):
        return jax.ShapeDtypeStruct(dims, dtype)

    prefetch = functools.partial(pltpu.PrefetchScalarGridSpec, num_scalar_prefetch=1)
    options = pltpu.CompilerParams(vmem_limit_bytes=VMEM_BYTES)
    anywhere = pl.BlockSpec(memory_space=pl.ANY)
    smem = pl.BlockSpec(memory_space=pltpu.SMEM)
    vmem = pl.BlockSpec(memory_space=pltpu.VMEM)
    index_shape = shape((4,), jnp.int32)

    def cost(flops, moved):
        return pl.CostEstimate(flops=int(flops), bytes_accessed=int(moved), transcendentals=0)

    def take_rows(sc, source, rates):
        given = [source] if rates is None else [source, rates]
        more = 0 if rates is None else PAD
        got = pl.pallas_call(
            functools.partial(slice_kernel, sz, slots, rates is not None),
            in_specs=[smem, smem, anywhere] + ([] if rates is None else [vmem]),
            out_specs=[anywhere] * slots + [smem],
            out_shape=[shape((HALF + more, width), LOW)] * slots + [index_shape],
            scratch_shapes=([pltpu.VMEM((slots, PAD, width), LOW)] if more else [])
            + [pltpu.SemaphoreType.DMA((2 * slots,))],
            compiler_params=options,
        )(sc, slot_order, *given)
        return got[:slots], got[slots]

    def to_members(pieces):
        return [turn(x, r) for r, x in enumerate(pieces)]

    sc = jnp.stack([c, h, z, k]).astype(jnp.int32)
    tok_slices, sc = take_rows(sc, tokens, log_decay)
    tok_pieces = to_members(tok_slices)
    tok_others = [cross(x) for x in tok_pieces]

    wide = 2 * channels + shared
    w_sent, o_sent, pv_mine, pv_sent = pl.pallas_call(
        functools.partial(pack_kernel, sz),
        in_specs=[smem] + [anywhere] * 4 + [vmem] * 5,
        out_specs=[anywhere, anywhere, vmem, vmem],
        out_shape=[
            shape((width, wide), LOW),
            shape((channels, width), LOW),
            shape((16, width), F32),
            shape((16, width), F32),
        ],
        scratch_shapes=[pltpu.SemaphoreType.DMA((4,))],
        compiler_params=options,
    )(sc, w_gate, w_inner, w_shared, w_out, in_gain, conv_inner, conv_shared, d_skip, norm_gain)
    raw = [w_gate, w_inner, w_shared, w_out]
    sent = [cross(w_sent), cross(o_sent)]
    gains = [pv_mine, cross(pv_sent)]

    def after(sc, first, then):
        given = list(first) + list(then)
        count = len(then)
        outs = pl.pallas_call(
            functools.partial(pass_kernel, count),
            in_specs=[smem] + [anywhere] * len(given),
            out_specs=[smem] + [anywhere] * count,
            out_shape=[index_shape] + [shape(x.shape, x.dtype) for x in then],
            input_output_aliases={1 + len(first) + i: 1 + i for i in range(count)},
            compiler_params=options,
        )(sc, *given)
        return outs[0], outs[1:]

    def span_total(table):
        ends = table[: sz.heads, BLOCK - 1 :: BLOCK]
        return jnp.repeat(jnp.exp(jnp.sum(ends, axis=1)), sz.head_width)[:, None]

    parts_shape = shape((head_axis, rows + PAD, chunk), LOW)
    weight_specs = [anywhere] * 6
    weight_scratch = [pltpu.VMEM((width, wide), LOW), pltpu.VMEM((channels, width), LOW)]
    dense = 2 * tok * width * (wide + channels)

    def forward(layer, sc, sources):
        def at(b, _):
            return (b, 0)

        piece = pl.BlockSpec((HALF, chunk), at)
        table = pl.BlockSpec((16, BLOCK), lambda b, _: (0, b))
        if layer == 0:
            src_specs = [whole((HALF + PAD, width))] * (2 * slots)
            more_specs = [table, table]
            more_shapes = [shape((16, tok), F32)] * 2
        else:
            src_specs = [piece] * (2 * head_axis) + [whole((HALF, width))] * (2 * slots) + [table]
            more_specs = [pl.BlockSpec((BLOCK, width), at)]
            more_shapes = [shape((tok, width), LOW)]

        def call(halo, begin):
            return pl.pallas_call(
                functools.partial(forward_kernel, sz, layer, slots),
                grid_spec=prefetch(
                    grid=(nb,),
                    in_specs=src_specs
                    + [whole((16, width)), whole((16, width))]
                    + weight_specs
                    + [whole((8, sz.lin)), whole((channels, sz.states))],
                    out_specs=[
                        pl.BlockSpec((BLOCK, width), at),
                        pl.BlockSpec((BLOCK, channels), at),
                        pl.BlockSpec((BLOCK, sz.lin), at),
                        pl.BlockSpec((BLOCK, channels), at),
                        pl.BlockSpec((1, channels, sz.states), lambda b, _: (b, 0, 0)),
                        pl.BlockSpec((1, BLOCK), lambda b, _: (0, b)),
                        pl.BlockSpec((2, BLOCK), lambda b, _: (0, b)),
                        whole(parts_shape.shape),
                        whole(parts_shape.shape),
                        whole((channels, sz.states)),
                        smem,
                        piece,
                    ]
                    + more_specs,
                    scratch_shapes=[
                        pltpu.VMEM((BLOCK, width), LOW),
                        pltpu.VMEM((BLOCK, width), LOW),
                        *weight_scratch,
                        pltpu.VMEM((BLOCK + 8, sz.lin), F32),
                        pltpu.VMEM((channels, sz.states), F32),
                        pltpu.VMEM((PAD, HALF), F32),
                        pltpu.VMEM((PAD, HALF), F32),
                        pltpu.VMEM((BLOCK, width), LOW),
                        pltpu.SemaphoreType.DMA((4,)),
                    ],
                ),
                out_shape=[
                    shape((tok, width), LOW),
                    shape((tok, channels), F32),
                    shape((tok, sz.lin), LOW),
                    shape((tok, channels), F32),
                    shape((nb, channels, sz.states), LOW),
                    shape((1, tok), F32),
                    shape((2, tok), F32),
                    parts_shape,
                    parts_shape,
                    shape((channels, sz.states), F32),
                    index_shape,
                    shape((rows, chunk), LOW),
                ]
                + more_shapes,
                compiler_params=options,
                cost_estimate=cost(6 * dense, 16e6),
            )(sc, *sources, *gains, *raw, *sent, halo, begin)

        halo = jnp.zeros((8, sz.lin), F32)
        begin = jnp.zeros((channels, sz.states), F32)
        if spans == 1:
            return call(halo, begin), halo
        trial = call(halo, begin)
        halo = next_span(trial[2][tok - 8 :].astype(F32), 1)
        local = call(halo, begin)[9]
        total = span_total(trial[12] if layer == 0 else sources[-1])
        for _ in range(spans - 1):
            begin = next_span(total * begin + local, 1)
        return call(halo, begin), halo

    def backward(layer, sc, sources, saved, decays, halo):
        def at(i, _):
            return (nb - 1 - i, 0)

        if layer == 0:
            src_specs = [whole(s.shape) for s in sources]
        else:
            stat = pl.BlockSpec((2, BLOCK), lambda i, _: (0, nb - 1 - i))
            src_specs = [pl.BlockSpec((BLOCK, width), at)] + [stat] * head_axis
        normed, gl, lin, ssd, inc = saved
        mixed_spec = [pl.BlockSpec((BLOCK, width), at)] if layer == 0 else []
        mixed_shape = [shape((tok, width), LOW)] if layer == 0 else []
        table = pl.BlockSpec((16, BLOCK), lambda i, _: (0, nb - 1 - i))

        def call(halo_grad, begin):
            return pl.pallas_call(
                functools.partial(backward_kernel, sz, layer),
                grid_spec=prefetch(
                    grid=(nb,),
                    in_specs=src_specs
                    + [
                        pl.BlockSpec((BLOCK, width), at),
                        pl.BlockSpec((BLOCK, channels), at),
                        whole(lin.shape),
                        pl.BlockSpec((BLOCK, channels), at),
                        pl.BlockSpec((1, channels, sz.states), lambda i, _: (nb - 1 - i, 0, 0)),
                        table,
                        whole((16, width)),
                        whole((16, width)),
                        *weight_specs,
                        whole((8, sz.lin)),
                        whole((8, sz.lin)),
                        whole((channels, sz.states)),
                    ],
                    out_specs=[
                        whole(parts_shape.shape),
                        whole(parts_shape.shape),
                        pl.BlockSpec((BLOCK, wide), at),
                        pl.BlockSpec((BLOCK, channels), at),
                        whole((PAD, 3 * channels)),
                        whole((PAD, chunk)),
                        whole((channels, sz.states)),
                        whole((8, sz.lin)),
                        smem,
                    ]
                    + mixed_spec,
                    scratch_shapes=[
                        pltpu.VMEM((BLOCK, width), LOW),
                        *weight_scratch,
                        pltpu.VMEM((BLOCK + 8, sz.lin), F32),
                        pltpu.VMEM((BLOCK + 8, sz.lin), F32),
                        pltpu.VMEM((channels, sz.states), F32),
                        pltpu.VMEM((PAD, HALF), F32),
                        pltpu.VMEM((PAD, HALF), F32),
                        pltpu.VMEM((BLOCK, width), LOW),
                        pltpu.VMEM((PAD, HALF), F32),
                        pltpu.VMEM((8, sz.lin), F32),
                        pltpu.VMEM((8, width), F32),
                        pltpu.SemaphoreType.DMA((4,)),
                    ],
                ),
                out_shape=[
                    parts_shape,
                    parts_shape,
                    shape((tok, wide), LOW),
                    shape((tok, channels), LOW),
                    shape((PAD, 3 * channels), LOW),
                    shape((PAD, chunk), LOW),
                    shape((channels, sz.states), F32),
                    shape((8, sz.lin), F32),
                    index_shape,
                ]
                + mixed_shape,
                compiler_params=options,
                cost_estimate=cost(8 * dense, 16e6),
            )(
                sc, *sources, normed, gl, lin, ssd, inc, decays, *gains, *raw, *sent,
                halo, halo_grad, begin,
            )

        halo_grad = jnp.zeros((8, sz.lin), F32)
        begin = jnp.zeros((channels, sz.states), F32)
        if spans == 1:
            return call(halo_grad, begin)
        local = call(halo_grad, begin)[6]
        for _ in range(spans - 1):
            begin = next_span(span_total(decays) * begin + local, -1)
        halo_grad = next_span(call(halo_grad, begin)[7], -1)
        return call(halo_grad, begin)

    def scatter(sc, keep, send):
        joined = pl.pallas_call(
            functools.partial(join_kernel, sz),
            in_specs=[smem, vmem, vmem],
            out_specs=[smem] + [vmem] * head_axis,
            out_shape=[index_shape, shape((rows + PAD, chunk), F32)]
            + [shape((rows + PAD, chunk), LOW)] * (head_axis - 1),
            compiler_params=options,
        )(sc, keep, cross(send))
        return [joined[1]] + [over_heads(joined[1 + d], d) for d in range(1, head_axis)], joined[0]

    def gather(low):
        own = [low] + [over_heads(low, d) for d in range(1, head_axis)]
        return own + [cross(x) for x in own]

    def section_output(layer, sc, parts, resid):
        return pl.pallas_call(
            functools.partial(output_kernel, sz, layer),
            in_specs=[smem] + [vmem] * (head_axis + 1),
            out_shape=[
                shape((rows, chunk), F32),
                shape((rows, chunk), LOW),
                shape((rows, chunk), F32),
                shape((8, HALF), F32),
            ],
            compiler_params=options,
        )(sc, *parts, resid)

    def section_input(layer, sc, parts, *others):
        return pl.pallas_call(
            functools.partial(input_kernel, sz, layer),
            in_specs=[smem] + [vmem] * (head_axis + len(others)),
            out_specs=[vmem, vmem, smem],
            out_shape=[
                shape((rows, chunk), F32),
                shape((rows + PAD, chunk), LOW),
                index_shape,
            ],
            compiler_params=options,
        )(sc, *parts, *others)

    part = width // seq

    columns = 3 * channels
    share = part // head_axis

    def weight_grads(sc, in_one, normed, cat, mixed, scaled, small, common):
        if in_one:
            out_shapes = [shape((seq * (part + PAD), columns), LOW)]
        else:
            out_shapes = [shape((part + PAD, columns), LOW)] * seq
        outs = pl.pallas_call(
            functools.partial(weights_kernel, sz, seq, in_one),
            in_specs=[smem] + [vmem] * 6,
            out_specs=[smem] + [vmem] * (len(out_shapes) + 1),
            out_shape=[index_shape]
            + out_shapes
            + [shape((seq * head_axis * (share + PAD), shared), LOW)],
            scratch_shapes=[pltpu.VMEM((width, columns), LOW), pltpu.VMEM((width, shared), F32)],
            compiler_params=options,
            cost_estimate=cost(4 * dense, 12e6),
        )(sc, normed, cat, mixed, scaled, small, common)
        both = lax.psum_scatter(outs[-1], ("seq", "head"), scatter_dimension=0, tiled=True)
        if in_one:
            return lax.psum_scatter(outs[1], "seq", scatter_dimension=0, tiled=True), both, outs[0]
        pieces = [outs[1]]
        for r in range(1, seq):
            pairs = [(i, (i + r) % seq) for i in range(seq)]
            pieces.append(lax.ppermute(outs[1 + r], "seq", pairs))
        return pieces, both, outs[0]

    def leave(sc, *arrays):
        pieces = pl.pallas_call(
            functools.partial(leave_kernel, sz, slots),
            in_specs=[smem] + [vmem] * 4,
            out_specs=[vmem] * slots + [smem],
            out_shape=[shape((BLOCK, chunk), LOW)] * slots + [index_shape],
            compiler_params=options,
        )(sc, *arrays)
        return to_members(pieces[:slots]), pieces[slots]

    out_slices, unused = take_rows(sc, grad_out, None)
    unused, out_slices = after(sc, tok_pieces[1:], out_slices)
    out_pieces = to_members(out_slices)
    fw0, halo0 = forward(0, sc, tok_pieces + tok_others)
    base0, decays = fw0[11], fw0[12:14]
    unused, send = after(fw0[10], out_pieces[1:], fw0[8:9])
    out_others = [cross(x) for x in out_pieces]
    parts, sc_join = scatter(sc, fw0[7], *send)
    res1, low1, mixed0, square0 = section_output(0, sc, parts, base0)
    pieces1 = gather(low1)
    square_other = cross(square0)

    fw1, halo1 = forward(1, sc, pieces1 + out_pieces + out_others + [decays[1]])
    stat = fw1[6] + cross(fw1[6])
    stats = [stat] + [over_heads(stat, d) for d in range(1, head_axis)]
    parts_out, sc_out = scatter(sc, fw1[7], fw1[8])
    bw1 = backward(1, sc_out, [fw1[12]] + stats, fw1[:5], decays[1], halo1)
    sc_out, send = after(bw1[8], parts_out[1:], bw1[1:2])
    parts, sc_join = scatter(sc_out, bw1[0], *send)
    sums1, shared1, sc_weights = weight_grads(sc_join, True, fw1[0], bw1[2], fw1[12], *bw1[3:6])
    igrad1, glow1, sc_in = section_input(
        1, sc_weights, parts, res1, fw1[11], fw1[5], *gains, mixed0
    )
    piecesg = gather(glow1)

    early, unused = leave(sc_in, low1, pieces1[head_axis], glow1, piecesg[head_axis])
    bw0 = backward(0, sc, piecesg + [square0, square_other], fw0[:5], decays[0], halo0)
    sc_out, send = after(bw0[8], early[1:], bw0[1:2])
    parts, sc_join = scatter(sc_out, bw0[0], *send)
    weights0, shared0, sc_weights = weight_grads(
        sc_join, False, fw0[0], bw0[2], bw0[9], *bw0[3:6]
    )
    igrad0, glow0, sc_end = section_input(0, sc_weights, parts, base0, igrad1, fw0[5], *gains)

    unused, low2, unused_mixed, unused_square = section_output(1, sc_in, parts_out, res1)
    swapped = cross(pick(first, low2, glow0[:rows]))
    late, sc_end = leave(sc_end, glow0, swapped, low2, swapped)
    section_out, input_grad = pl.pallas_call(
        functools.partial(home_kernel, slots),
        in_specs=[smem] + [vmem] * (2 * slots),
        out_shape=[shape((slots, BLOCK, chunk), F32)] * 2,
        compiler_params=options,
    )(sc, *early, *late)

    sums0 = pl.pallas_call(
        functools.partial(sum_kernel, sz),
        in_specs=[smem] + [vmem] * seq,
        out_shape=shape((part + PAD, columns), LOW),
        compiler_params=options,
    )(sc_end, *weights0)
    final = pl.pallas_call(
        functools.partial(final_kernel, sz),
        in_specs=[smem] + [vmem] * 6,
        out_shape=[
            shape((part, inner_dev), F32),
            shape((part, inner_dev), F32),
            shape((inner_dev, part), F32),
            shape((taps, inner_dev), F32),
            shape((1, inner_dev), F32),
            shape((1, heads_dev), F32),
            shape((share, shared), F32),
            shape((PAD // 2, shared), F32),
        ],
        compiler_params=options,
    )(
        sc,
        *(sums0, sums1, cross(pick(first, sums1, sums0))),
        *(shared0, shared1, cross(pick(first, shared1, shared0))),
    )
    common = final[7]
    place = z * head_axis + h
    conv_part = shared // (seq * head_axis)
    gain_part = width // (seq * head_axis)
    return (
        section_out[None],
        input_grad[None],
        lax.dynamic_slice_in_dim(common[taps:].reshape(-1), place * gain_part, gain_part, 0)[None],
        final[0][None],
        final[1][None],
        final[6][None],
        final[3][None],
        lax.dynamic_slice_in_dim(common[:taps], place * conv_part, conv_part, 1)[None],
        final[5],
        final[4],
        final[2][None],
    )


def solution(mesh):
    placed = (
        P(None, "seq", None),
        P(),
        P("section", None, "head", "seq"),
        P(None, "seq", None),
        P("section", None),
        P("section", None, "head"),
        P("section", None, "head"),
        P("section", None, None),
        P("section", None, "head"),
        P("section", None, None),
        P("section", "head"),
        P("section", "head"),
        P("section", None, None),
    )
    return jax.shard_map(
        per_device,
        mesh=mesh,
        in_specs=placed,
        out_specs=(
            P("section", None, "seq", "head"),
            P("section", None, "seq", "head"),
            P("section", ("seq", "head")),
            P("section", "seq", "head"),
            P("section", "seq", "head"),
            P("section", ("seq", "head"), None),
            P("section", None, "head"),
            P("section", None, ("seq", "head")),
            P("section", "head"),
            P("section", "head"),
            P("section", "head", "seq"),
        ),
        check_vma=False,
    )
```

```python
import functools

import jax
import jax.numpy as jnp
from jax import lax
from jax.experimental import pallas as pl
from jax.experimental.pallas import tpu as pltpu
from jax.sharding import PartitionSpec as P

BLOCK = 256
HALF = BLOCK // 2
PAD = 16
EPS = 1e-05
F32 = jnp.float32
LOW = jnp.bfloat16
HIDDEN = -1e30
NN = ((1,), (0,))
NT = ((1,), (1,))
TN = ((0,), (0,))
VMEM_BYTES = 50 * 1024 * 1024


def dot(a, b, dims):
    return lax.dot_general(a, b, (dims, ((), ())), preferred_element_type=F32)


def aligned(start, size):
    return pl.ds(pl.multiple_of(start, size), size)


def spread(cols, first, count, width):
    rows = cols.shape[0]
    lane = lax.broadcasted_iota(jnp.int32, (rows, count * width), 1)
    out = jnp.broadcast_to(cols[:, first : first + 1], (rows, count * width))
    for h in range(1, count):
        out = jnp.where(lane >= h * width, cols[:, first + h : first + h + 1], out)
    return out


def per_head(array, h, width):
    lane = lax.broadcasted_iota(jnp.int32, array.shape, 1)
    inside = (lane >= h * width) & (lane < (h + 1) * width)
    return jnp.where(inside, array, jnp.zeros_like(array))


def split_low(value):
    high = value.astype(LOW).astype(F32)
    return high, value - high


def column_of(row, size):
    return jnp.transpose(jnp.broadcast_to(row, (128, size)))


def sigmoid(v):
    return 0.5 * jnp.tanh(0.5 * v) + 0.5


def pick(flag, a, b):
    return jnp.where(flag, a, b)


class Sizes:
    def __init__(self, blocks, width, channels, heads, states, taps, head_axis, inner):
        self.blocks = blocks
        self.width = width
        self.channels = channels
        self.heads = heads
        self.head_width = channels // heads
        self.states = states
        self.lin = channels + 2 * states
        self.taps = taps
        self.head_axis = head_axis
        self.chunk = width // head_axis
        self.rows = blocks * HALF
        self.tokens = blocks * BLOCK
        self.inner = inner


def weight_copies(sz, layer, c, h, raw, got, wv, ov, sems):
    gate, inner, shared, out = raw
    ch = sz.channels
    cols = aligned(c * ch, ch)
    rows = aligned((h * 2 + c) * ch, ch)
    own, sent = [], []
    if wv is not None:
        own += [
            (gate.at[0, :, cols], wv.at[:, :ch]),
            (inner.at[0, :, cols], wv.at[:, ch : 2 * ch]),
            (shared.at[0], wv.at[:, 2 * ch :]),
        ]
        sent += [(got[0], wv)]
    if ov is not None:
        own += [(out.at[0, rows, :], ov)]
        sent += [(got[1], ov)]
    return [
        (c == layer, [pltpu.make_async_copy(p, q, sems.at[i]) for i, (p, q) in enumerate(own)]),
        (c != layer, [pltpu.make_async_copy(p, q, sems.at[i]) for i, (p, q) in enumerate(sent)]),
    ]


def run_copies(choices, start, wait):
    for flag, copies in choices:

        @pl.when(flag)
        def _(copies=copies):
            if start:
                for copy in copies:
                    copy.start()
            if wait:
                for copy in copies:
                    copy.wait()


def put_ordered(sz, dst, c, k, b, own, other):
    for r in range(len(own)):

        @pl.when(lax.rem(k - b + len(own), len(own)) == r)
        def _(r=r):
            put_pair(dst, c, own[r][:HALF, :], other[r][:HALF, :])


def put_pair(dst, c, own, other):
    dst[aligned(c * HALF, HALF), :] = own
    dst[aligned((1 - c) * HALF, HALF), :] = other


def put_pieces(sz, dst, c, h, own, other):
    for d in range(sz.head_axis):
        cols = aligned((h ^ d) * sz.chunk, sz.chunk)
        dst[aligned(c * HALF, HALF), cols] = own[d]
        dst[aligned((1 - c) * HALF, HALF), cols] = other[d]


def put_parts(sz, b, c, h, part, keep, send):
    for d in range(sz.head_axis):
        cols = aligned((h ^ d) * sz.chunk, sz.chunk)
        keep[d, aligned(b * HALF, HALF), :] = part[aligned(c * HALF, HALF), cols]
        send[d, aligned(b * HALF, HALF), :] = part[aligned((1 - c) * HALF, HALF), cols]


def put_scalars(b, c, row, kept, sent):
    for scratch, flag in ((kept, c == 0), (sent, c != 0)):
        high, low = split_low(pick(flag, row[:, :HALF], row[:, HALF:]))
        line = lax.broadcasted_iota(jnp.int32, scratch.shape, 0)
        lower = jnp.where(line == 8 + b, low, scratch[...])
        scratch[...] = jnp.where(line == b, high, lower)


def line_of(table, at):
    line = lax.broadcasted_iota(jnp.int32, table.shape, 0)
    return jnp.sum(jnp.where(line == at, table, 0.0), axis=0, keepdims=True)


def close_parts(sz, keep, send, kept, sent):
    for scratch, out in ((kept, keep), (sent, send)):
        extra = jnp.concatenate([scratch[...]] * (sz.chunk // HALF), axis=1).astype(LOW)
        for d in range(sz.head_axis):
            out[d, sz.rows :, :] = extra


def conv_forward(sz, ext, taps):
    pre = taps[0:1] * ext[5 : 5 + BLOCK, :]
    for j in range(1, sz.taps):
        pre = pre + taps[j : j + 1] * ext[5 + j : 5 + j + BLOCK, :]
    return pre


def decay_of(sz, cols, rp, h, mask):
    rows = cols[:, h : h + 1] + rp[12 + h : 13 + h, :]
    return jnp.exp(jnp.where(mask, rows, HIDDEN))


def lower_mask():
    t = lax.broadcasted_iota(jnp.int32, (BLOCK, BLOCK), 0)
    s = lax.broadcasted_iota(jnp.int32, (BLOCK, BLOCK), 1)
    return t >= s


def forward_kernel(sz, layer, slots, sc, *refs):
    n = sz.head_axis
    sources = 2 * slots if layer == 0 else 2 * n + 2 * slots
    src, refs = refs[:sources], refs[sources:]
    if layer == 1:
        table, refs = refs[0], refs[1:]
    gains, raw, got, halo, begin = refs[0:2], refs[2:6], refs[6:8], refs[8], refs[9]
    normed_o, gl_o, lin_o, ssd_o, inc_o, inv_o, part_o, unit_o, fin_o, sc_o, base_o = refs[10:21]
    refs = refs[21:]
    if layer == 1:
        mixed_o, refs = refs[0], refs[1:]
    else:
        tables_o, refs = refs[0:2], refs[2:]
    xs, ms, wv, ov, ext, state, sems = refs
    b = pl.program_id(0)
    c, h, k = sc[0], sc[1], sc[3]
    ch, st = sz.channels, sz.states
    copies = weight_copies(sz, layer, c, h, raw, got, wv, ov if layer == 1 else None, sems)

    @pl.when(b == 0)
    def _():
        run_copies(copies, True, False)
        ext[0:8, :] = halo[...]
        state[...] = begin[...]
        for i in range(4):
            sc_o[i] = sc[i]

    mine = aligned(c * HALF, HALF)
    cols = aligned(h * sz.chunk, sz.chunk)
    if layer == 0:
        put_ordered(sz, xs, c, k, b, src[:slots], src[slots:])
        base_o[...] = xs[mine, cols]
        for r in range(slots):

            @pl.when(lax.rem(k - b + slots, slots) == r)
            def _(r=r):
                own = decay_table(rates_of(src[r]), c, sz.heads)
                other = decay_table(rates_of(src[slots + r]), c, sz.heads)
                tables_o[0][...] = pick(c == 0, own, other)
                tables_o[1][...] = pick(c == 0, other, own)

        rp = tables_o[0][...]
    else:
        put_pieces(sz, xs, c, h, [r[...] for r in src[:n]], [r[...] for r in src[n : 2 * n]])
        put_ordered(sz, ms, c, k, b, src[2 * n : 2 * n + slots], src[2 * n + slots :])
        base_o[...] = ms[mine, cols]
        mixed_o[...] = ms[...]
        rp = table[...]

    pv = pick(c == layer, gains[0][...], gains[1][...])
    x = xs[...].astype(F32)
    inv_in = lax.rsqrt(jnp.mean(x * x, axis=1, keepdims=True) + EPS)
    normed = (x * inv_in * pv[0:1, : sz.width]).astype(LOW)
    normed_o[...] = normed

    @pl.when(b == 0)
    def _():
        run_copies(copies, False, True)

    proj = dot(normed, wv[...], NN)
    gl = proj[:, :ch]
    gl_o[...] = gl
    lin = proj[:, ch:].astype(LOW)
    lin_o[...] = lin
    ext[8 : 8 + BLOCK, :] = lin.astype(F32)
    pre = conv_forward(sz, ext, pv[1:5, : sz.lin])
    ext[0:8, :] = ext[BLOCK : BLOCK + 8, :]
    act = (pre * sigmoid(pre)).astype(LOW)
    values, bm, cm = act[:, :ch], act[:, ch : ch + st], act[:, ch + st :]

    cols = jnp.transpose(rp)
    mask = lower_mask()
    gram = dot(cm, bm, NT)
    mixes, parts = [], []
    for i in range(sz.heads):
        mixes.append((gram * decay_of(sz, cols, rp, i, mask)).astype(LOW))
        parts.append(per_head(values, i, sz.head_width))
    intra = dot(jnp.concatenate(mixes, axis=1), jnp.concatenate(parts, axis=0), NN)

    low_state = state[...].astype(LOW)
    inc_o[0] = low_state
    ecum = spread(cols, sz.heads, sz.heads, sz.head_width)
    inter = dot(cm, low_state, NT) * ecum
    vf = values.astype(F32)
    carried = (vf * spread(cols, 2 * sz.heads, sz.heads, sz.head_width)).astype(LOW)
    local = dot(carried, bm, TN)
    for i in range(sz.heads):
        rows = slice(i * sz.head_width, (i + 1) * sz.head_width)
        total = cols[BLOCK - 1 : BLOCK, sz.heads + i : sz.heads + i + 1]
        state[rows, :] = total * state[rows, :] + local[rows]
    ssd = intra + inter + pv[6:7, :ch] * vf
    ssd_o[...] = ssd
    gated = ssd * (gl * sigmoid(gl))
    weighty = gated * pv[5:6, :ch]
    unit_o[...] = weighty.astype(LOW)

    lane = lax.broadcasted_iota(jnp.int32, (BLOCK, 128), 1)
    square = jnp.sum(gated * gated, axis=1, keepdims=True)
    if layer == 0:
        project = jnp.zeros_like(square)
    else:
        scaled_grad = dot(ms[...], ov[...], NT)
        project = jnp.sum(scaled_grad * weighty, axis=1, keepdims=True)
    stats = jnp.where(lane == 0, square, jnp.where(lane == 1, project, inv_in))
    stats = jnp.transpose(stats)
    part_o[...] = stats[0:2, :]
    inv_o[...] = stats[2:3, :]

    @pl.when(b == sz.blocks - 1)
    def _():
        fin_o[...] = state[...]


def project_kernel(sz, layer, back, deps, sc, rows_r, extra_r, *refs):
    raw, got, refs = refs[:4], refs[4:6], refs[6:]
    if back:
        gains, small_r, refs = refs[:2], refs[2], refs[3:]
    refs = refs[deps:]
    keep, send, sc_o, refs = refs[0], refs[1], refs[2], refs[3:]
    if back:
        common_o, wide, refs = refs[0], refs[1], refs[2:]
    weights, part, kept, sent, sems = refs
    b = pl.program_id(0)
    c, h = sc[0], sc[1]
    copies = weight_copies(
        sz, layer, c, h, raw, got, weights if back else None, None if back else weights, sems
    )

    @pl.when(b == 0)
    def _():
        run_copies(copies, True, True)
        kept[...] = jnp.zeros_like(kept)
        sent[...] = jnp.zeros_like(sent)
        for i in range(4):
            sc_o[i] = sc[i]
        if back:
            wide[...] = jnp.zeros_like(wide)

    if back:
        product = dot(rows_r[...], weights[...], NT)
        part[...] = product.astype(LOW)
        product = product * extra_r[...].astype(F32)
        wide[0:1, :] += jnp.sum(product, axis=0, keepdims=True)
        along = jnp.sum(product, axis=1, keepdims=True)
        row = jnp.transpose(jnp.broadcast_to(along, (BLOCK, 128)))[0:1, :]
    else:
        part[...] = dot(rows_r[...], weights[...], NN).astype(LOW)
        row = extra_r[0:1, :]
    put_scalars(b, c, row, kept, sent)
    put_parts(sz, b, c, h, part, keep, send)

    @pl.when(b == sz.blocks - 1)
    def _():
        close_parts(sz, keep, send, kept, sent)
        if back:
            gain = pick(c == layer, gains[0][0:1, :], gains[1][0:1, :])
            gain_grad = wide[0:1, :] / gain
            flat = [small_r[j : j + 1, sz.channels :] for j in range(sz.taps)]
            flat += [gain_grad[:, q * sz.chunk : (q + 1) * sz.chunk] for q in range(sz.head_axis)]
            high, low = split_low(jnp.concatenate(flat, axis=0))
            common_o[...] = jnp.concatenate([high, low], axis=0).astype(LOW)


def backward_kernel(sz, layer, deps, sc, *refs):
    n = sz.head_axis
    sources = 2 * n + 2 if layer == 0 else 1 + n
    src, refs = refs[:sources], refs[sources:]
    gl_r, lin_r, ssd_r, inc_r = refs[:4]
    table, gains, raw, got = refs[4], refs[5:7], refs[7:11], refs[11:13]
    halo, halo_grad, begin = refs[13:16]
    refs = refs[16 + deps :]
    cat_o, scaled_o, small_o, sums_o, fin_o, rim_o, sc_o = refs[:7]
    refs = refs[7:]
    if layer == 0:
        mixed_o, refs = refs[0], refs[1:]
    ms, ov, ext, back, state, heads_p, small, sems = refs
    i_step = pl.program_id(0)
    b = sz.blocks - 1 - i_step
    c, h = sc[0], sc[1]
    ch, st = sz.channels, sz.states
    copies = weight_copies(sz, layer, c, h, raw, got, None, ov, sems)
    pv = pick(c == layer, gains[0][...], gains[1][...])
    rp = table[...]

    @pl.when(i_step == 0)
    def _():
        run_copies(copies, True, True)
        back[BLOCK : BLOCK + 8, :] = halo_grad[...]
        state[...] = begin[...]
        small[...] = jnp.zeros_like(small)
        for i in range(4):
            sc_o[i] = sc[i]
        if layer == 0:
            for i in range(2):
                extra = src[i * n][sz.rows :, :].astype(F32)
                for d in range(1, n):
                    extra = extra + src[i * n + d][sz.rows :, :].astype(F32)
                heads_p[8 * i : 8 * i + 8, :] = extra[0:8, :HALF] + extra[8:16, :HALF]

    if layer == 0:
        rows = aligned(b * HALF, HALF)
        put_pieces(
            sz, ms, c, h, [r[rows, :] for r in src[:n]], [r[rows, :] for r in src[n : 2 * n]]
        )
        halves = []
        for k in range(2):
            alpha = lax.rsqrt(line_of(src[2 * n + k][...], b) / sz.inner + EPS)
            beta = alpha * alpha * line_of(heads_p[...], 8 * k + b) / sz.inner
            halves.append((alpha, beta))
        alpha, beta = (
            pick(
                c == 0,
                jnp.concatenate([halves[0][q], halves[1][q]], axis=1),
                jnp.concatenate([halves[1][q], halves[0][q]], axis=1),
            )
            for q in range(2)
        )
    else:
        stats = src[1][...]
        for d in range(1, n):
            stats = stats + src[1 + d][...]
        alpha = lax.rsqrt(stats[0:1, :] / sz.inner + EPS)
        beta = alpha * alpha * alpha * stats[1:2, :] / sz.inner

    sub = lax.broadcasted_iota(jnp.int32, rp.shape, 0)
    cols = jnp.transpose(jnp.where(sub == 12, alpha, jnp.where(sub == 13, beta, rp)))
    alpha, beta = cols[:, 12:13], cols[:, 13:14]

    gl = gl_r[...]
    ssd = ssd_r[...]
    sig = sigmoid(gl)
    swish = gl * sig
    slope = sig * (1.0 + gl * (1.0 - sig))
    gated = ssd * swish
    if layer == 0:
        mixed_grad = ms[...]
        mixed_o[...] = mixed_grad
    else:
        mixed_grad = src[0][...]
    scaled_grad = dot(mixed_grad, ov[...], NT)
    gain = pv[5:6, :ch]
    normal = gated * alpha
    small[4:5, :ch] += jnp.sum(scaled_grad * normal, axis=0, keepdims=True)
    scaled_o[...] = (normal * gain).astype(LOW)
    gated_grad = alpha * (scaled_grad * gain) - beta * gated
    ssd_grad = (gated_grad * swish).astype(LOW)
    gate_grad = (gated_grad * ssd * slope).astype(LOW)
    sgf = ssd_grad.astype(F32)

    before = lin_r[pl.ds(pl.multiple_of(jnp.maximum(b * BLOCK - 16, 0), 16), 16), :]
    ext[0:8, :] = pick(b > 0, before.astype(F32)[8:16, :], halo[...])
    ext[8 : 8 + BLOCK, :] = lin_r[aligned(b * BLOCK, BLOCK), :].astype(F32)
    taps = pv[1:5, : sz.lin]
    pre = conv_forward(sz, ext, taps)
    psig = sigmoid(pre)
    pact = pre * psig
    pslope = psig * (1.0 + pre * (1.0 - psig))
    act = pact.astype(LOW)
    values, bm, cm = act[:, :ch], act[:, ch : ch + st], act[:, ch + st :]
    vf = values.astype(F32)
    small[5:6, :ch] += jnp.sum(sgf * vf, axis=0, keepdims=True)

    mask = lower_mask()
    gram = dot(cm, bm, NT)
    gram_grad = jnp.zeros((BLOCK, BLOCK), F32)
    mixes, parts = [], []
    for i in range(sz.heads):
        decay = decay_of(sz, cols, rp, i, mask)
        mixes.append((gram * decay).astype(LOW))
        parts.append(per_head(ssd_grad, i, sz.head_width))
        gram_grad = gram_grad + dot(parts[-1], values, NT) * decay
    intra_grad = dot(jnp.concatenate(mixes, axis=0), jnp.concatenate(parts, axis=0), TN)

    ecum = spread(cols, sz.heads, sz.heads, sz.head_width)
    to_end = spread(cols, 2 * sz.heads, sz.heads, sz.head_width)
    inter_grad = (sgf * ecum).astype(LOW)
    low_state = state[...].astype(LOW)
    carried = (vf * to_end).astype(LOW)
    carried_grad = dot(bm, low_state, NT)
    gram_low = gram_grad.astype(LOW)
    b_grad = dot(gram_low, cm, TN) + dot(carried, low_state, NN)
    c_grad = dot(gram_low, bm, NN) + dot(inter_grad, inc_r[0], NN)
    value_grad = intra_grad + pv[6:7, :ch] * sgf + carried_grad * to_end
    entry = dot(inter_grad, cm, TN)
    for i in range(sz.heads):
        rows = slice(i * sz.head_width, (i + 1) * sz.head_width)
        total = cols[BLOCK - 1 : BLOCK, sz.heads + i : sz.heads + i + 1]
        state[rows, :] = total * state[rows, :] + entry[rows]

    pre_grad = jnp.concatenate([value_grad, b_grad, c_grad], axis=1) * pslope
    back[0:BLOCK, :] = pre_grad
    lin_grad = taps[0:1] * back[sz.taps - 1 : sz.taps - 1 + BLOCK, :]
    for j in range(1, sz.taps):
        at = sz.taps - 1 - j
        lin_grad = lin_grad + taps[j : j + 1] * back[at : at + BLOCK, :]
    for j in range(sz.taps):
        small[j : j + 1, :] += jnp.sum(pre_grad * ext[5 + j : 5 + j + BLOCK, :], axis=0, keepdims=True)
    back[BLOCK : BLOCK + 8, :] = back[0:8, :]
    cat_o[...] = jnp.concatenate([gate_grad, lin_grad.astype(LOW)], axis=1)

    @pl.when(i_step == sz.blocks - 1)
    def _():
        fin_o[...] = state[...]
        rim_o[...] = back[0:8, :]
        sums = small[...]
        flat = [sums[j : j + 1, :ch] for j in range(sz.taps + 2)]
        flat = [jnp.concatenate(flat[j : j + 3], axis=1) for j in range(0, len(flat), 3)]
        flat = flat + [jnp.zeros_like(flat[0])] * (4 - len(flat))
        high, low = split_low(jnp.concatenate(flat, axis=0))
        rest = jnp.zeros((PAD - 8, high.shape[1]), F32)
        small_o[...] = jnp.concatenate([high, low, rest], axis=0).astype(LOW)
        sums_o[...] = sums


def weights_kernel(sz, seq, sc, normed, cat, mixed, scaled, small, common, *refs):
    sc_o, outs, heads, full, wide = refs[0], refs[1 : seq + 1], refs[seq + 1 : -2], refs[-2], refs[-1]
    for i in range(4):
        sc_o[i] = sc[i]
    ch, st = sz.channels, sz.states
    step = sz.chunk
    for q in range(sz.head_axis):
        at = slice(q * step, (q + 1) * step)
        grads = dot(normed[:, at], cat[...], TN)
        full[at, : 2 * ch] = grads[:, : 2 * ch].astype(LOW)
        wide[at, :] = grads[:, 2 * ch :]
        full[at, 2 * ch :] = dot(mixed[:, at], scaled[...], TN).astype(LOW)
    rows = sz.width // seq
    part = rows // sz.head_axis
    for r, out in enumerate(outs):
        out[:rows, :] = full[aligned(lax.rem(sc[2] + r, seq) * rows, rows), :]
        out[rows:, :] = small[...]
    for d, out in enumerate(heads):
        lines = [
            wide[aligned(lax.rem(sc[2] + r, seq) * rows + (sc[1] ^ d) * part, part), :]
            for r in range(seq)
        ]
        out[:PAD, :] = common[...]
        out[PAD:, :] = jnp.concatenate(lines, axis=0).astype(LOW)


def resplit(extra):
    half = extra.shape[0] // 2
    high, low = split_low(extra[:half, :] + extra[half:, :])
    return jnp.concatenate([high, low], axis=0)


def join_kernel(sz, riders, sc, keep, recv, *refs):
    n = sz.head_axis
    more, refs = [refs[i * n : (i + 1) * n] for i in range(riders)], refs[riders * n :]
    sc_o, outs = refs[0], refs[1:]
    rows = sz.rows
    for i in range(4):
        sc_o[i] = sc[i]
    extra = resplit(keep[0, rows:, :].astype(F32) + recv[0, rows:, :].astype(F32))
    for d, out in enumerate(outs):
        out[:rows, :] = (keep[d, :rows, :].astype(F32) + recv[d, :rows, :].astype(F32)).astype(out.dtype)
        out[rows : rows + PAD, :] = extra.astype(out.dtype)
        at = rows + PAD
        for rider in more:
            size = rider[d].shape[0]
            out[at : at + size, :] = rider[d][...].astype(out.dtype)
            at += size


def total_of(parts, rows):
    total = parts[0][rows, :].astype(F32)
    for p in parts[1:]:
        total = total + p[rows, :].astype(F32)
    return total


def output_kernel(sz, layer, sc, *refs):
    n = sz.head_axis
    parts, refs = refs[:n], refs[n:]
    resid, res_o, low_o, mixed_o, square_o, sc_o = refs
    for i in range(4):
        sc_o[i] = sc[i]
    extra = total_of(parts, slice(sz.rows, sz.rows + PAD))
    square = extra[0:8, :HALF] + extra[8:16, :HALF]
    square_o[...] = square
    inv = lax.rsqrt(square / sz.inner + EPS)
    for b in range(sz.blocks):
        rows = slice(b * HALF, (b + 1) * HALF)
        col = column_of(inv[b : b + 1, :], HALF)[:, 0:1]
        mixed = total_of(parts, rows) * col
        res = resid[rows, :].astype(F32) + mixed
        res_o[rows, :] = res
        low_o[rows, :] = res.astype(LOW)
        mixed_o[rows, :] = mixed


def input_kernel(sz, layer, sc, *refs):
    n = sz.head_axis
    parts, refs = refs[:n], refs[n:]
    resid, outg, inv_r, gains = refs[0], refs[1], refs[2], refs[3:5]
    refs = refs[5:]
    if layer == 1:
        mixed, refs = refs[0], refs[1:]
        grad_o, low_o, sc_o = refs
    else:
        one_low = refs[0]
        low_o, swap_o, shared_o, sc_o = refs[-4:]
    for i in range(4):
        sc_o[i] = sc[i]
    c, h = sc[0], sc[1]
    first = c == 0
    mine = aligned(h * sz.chunk, sz.chunk)
    gain = pick(c == layer, gains[0][0:1, mine], gains[1][0:1, mine])
    extra = total_of(parts, slice(sz.rows, sz.rows + PAD))
    along = extra[0:8, :HALF] + extra[8:16, :HALF]
    tops, lows = [], []
    for b in range(sz.blocks):
        rows = slice(b * HALF, (b + 1) * HALF)
        at = b * BLOCK
        inv_row = pick(c == 0, inv_r[:, at : at + HALF], inv_r[:, at + HALF : at + BLOCK])
        inv = column_of(inv_row, HALF)[:, 0:1]
        share = column_of(along[b : b + 1, :] / sz.width, HALF)[:, 0:1]
        total = total_of(parts, rows)
        base = resid[rows, :].astype(F32)
        grad = outg[rows, :].astype(F32) + inv * (total * gain - base * (inv * share))
        low = grad.astype(LOW)
        low_o[rows, :] = low
        if layer == 0:
            swap_o[rows, :] = pick(first, one_low[rows, :], low)
        else:
            grad_o[rows, :] = grad
            dots = jnp.sum(low.astype(F32) * mixed[rows, :], axis=1, keepdims=True)
            row = jnp.transpose(jnp.broadcast_to(dots, (HALF, 128)))[0:1, :]
            high, rest = split_low(row)
            tops.append(high)
            lows.append(rest)
    if layer == 1:
        fill = [jnp.zeros((8 - sz.blocks, HALF), F32)] if sz.blocks < 8 else []
        extra = jnp.concatenate(tops + fill + lows + fill, axis=0)
        extra = jnp.concatenate([extra] * (sz.chunk // HALF), axis=1)
        low_o[sz.rows :, :] = extra.astype(LOW)
    else:
        size = shared_o.shape[0]
        at = sz.rows + PAD
        zero = total_of(parts, slice(at, at + size))
        one = total_of(parts, slice(at + size, at + 2 * size))
        zero, one = (jnp.concatenate([resplit(v[:PAD]), v[PAD:]], axis=0) for v in (zero, one))
        shared_o[...] = pick(first, zero, one)
        swap_o[sz.rows :, :] = pick(first, one, zero).astype(LOW)


def sum_kernel(sz, sc, *refs):
    parts, out = refs[:-1], refs[-1]
    rows = out.shape[0] - PAD
    out[:rows, :] = total_of(parts, slice(0, rows)).astype(LOW)
    extra = total_of(parts, slice(rows, rows + PAD))
    high, low = split_low(extra[0:4, :] + extra[4:8, :])
    extra = jnp.concatenate([high, low, jnp.zeros((PAD - 8, extra.shape[1]), F32)], axis=0)
    out[rows:, :] = extra.astype(LOW)


def final_kernel(sz, sc, zero, one, got, *refs):
    pieces, refs = refs[:-8], refs[-8:]
    gate_o, inner_o, out_o, conv_o, norm_o, skip_o, shared_o, common_o = refs
    c = sc[0]
    ch = sz.channels
    rows = zero.shape[0] - PAD
    lane = lax.broadcasted_iota(jnp.int32, skip_o.shape, 1)
    skip = jnp.zeros(skip_o.shape, F32)
    for i in range(2):
        which = pick(i == 0, c, 1 - c)
        to = aligned(which * ch, ch)
        sums = (pick(c == 0, zero[...], one[...]) if i == 0 else got[...]).astype(F32)
        gate_o[:, to] = sums[:rows, :ch]
        inner_o[:, to] = sums[:rows, ch : 2 * ch]
        out_o[to, :] = jnp.transpose(sums[:rows, 2 * ch :])
        lines = sums[rows : rows + 4, :] + sums[rows + 4 : rows + 8, :]
        for j in range(sz.taps):
            conv_o[j : j + 1, to] = lines[j // 3 : j // 3 + 1, (j % 3) * ch : (j % 3 + 1) * ch]
        norm_o[:, to] = lines[1:2, ch : 2 * ch]
        skips = lines[1:2, 2 * ch :]
        for q in range(sz.heads):
            part = jnp.sum(per_head(skips, q, sz.head_width), axis=1, keepdims=True)
            skip = jnp.where(lane == which * sz.heads + q, part, skip)
    skip_o[...] = skip
    total = total_of(pieces, slice(BLOCK, None))
    shared_o[...] = total[PAD:]
    common_o[...] = total[: PAD // 2] + total[PAD // 2 : PAD]


def slice_kernel(sz, slots, with_rates, deps, sc, order, *refs):
    sources = 2 if with_rates else 1
    src, refs = refs[:sources], refs[sources + deps :]
    outs, sc_o, refs = refs[:slots], refs[slots], refs[slots + 1 :]
    sems = refs[-1]
    copies = []
    for r in range(slots):
        which = order[lax.rem(sc[3] + r, slots)]
        rows = src[0].at[which, aligned(sc[0] * HALF, HALF), :]
        to = outs[r].at[:HALF] if with_rates else outs[r]
        copies.append(pltpu.make_async_copy(rows, to, sems.at[r]))
    for copy in copies:
        copy.start()
    for i in range(4):
        sc_o[i] = sc[i]
    if with_rates:
        thirds = refs[0]
        for r in range(slots):
            which = order[lax.rem(sc[3] + r, slots)]
            first, rest = split_low(src[1][0, which])
            second, rest = split_low(rest)
            lines = jnp.concatenate([first, second, rest, jnp.zeros_like(rest)], axis=1)
            lines = jnp.concatenate([lines, jnp.zeros_like(lines)], axis=0)
            thirds[r] = lines.astype(LOW)
        more = [
            pltpu.make_async_copy(thirds.at[r], outs[r].at[HALF:], sems.at[slots + r])
            for r in range(slots)
        ]
        for copy in more:
            copy.start()
        copies = copies + more
    for copy in copies:
        copy.wait()


def rates_of(piece):
    lines = piece[HALF:, :].astype(F32)[:8, :]
    return (lines[:, :BLOCK] + lines[:, BLOCK : 2 * BLOCK]) + lines[:, 2 * BLOCK : 3 * BLOCK]


def pack_kernel(sz, sc, gate, inner, shared, out, in_gain, conv_i, conv_s, skip, norm, *refs):
    w_o, o_o, mine_o, send_o, sems = refs
    c, h = sc[0], sc[1]
    ch = sz.channels
    cols = aligned((1 - c) * ch, ch)
    rows = aligned((h * 2 + 1 - c) * ch, ch)
    copies = [
        pltpu.make_async_copy(gate.at[0, :, cols], w_o.at[:, :ch], sems.at[0]),
        pltpu.make_async_copy(inner.at[0, :, cols], w_o.at[:, ch : 2 * ch], sems.at[1]),
        pltpu.make_async_copy(shared.at[0], w_o.at[:, 2 * ch :], sems.at[2]),
        pltpu.make_async_copy(out.at[0, rows, :], o_o, sems.at[3]),
    ]
    for copy in copies:
        copy.start()
    for which, ref in ((c, mine_o), (1 - c, send_o)):
        at = aligned(which * ch, ch)
        ref[...] = jnp.zeros_like(ref)
        ref[0:1, :] = in_gain[...]
        ref[1 : 1 + sz.taps, :ch] = conv_i[0, :, at]
        ref[1 : 1 + sz.taps, ch : sz.lin] = conv_s[0]
        ref[5:6, :ch] = norm[:, at]
        low = spread(skip[...], 0, sz.heads, sz.head_width)
        high = spread(skip[...], sz.heads, sz.heads, sz.head_width)
        ref[6:7, :ch] = pick(which == 0, low, high)
    for copy in copies:
        copy.wait()


def decay_table(rate, c, n):
    lane = lax.broadcasted_iota(jnp.int32, rate.shape, 1)
    cum = rate
    step = 1
    while step < BLOCK:
        cum = cum + jnp.where(lane >= step, pltpu.roll(cum, step, 1), 0.0)
        step *= 2
    end = cum[:, BLOCK - 1 :]
    lines = [cum, jnp.exp(cum), jnp.exp(end - cum) * -rate, jnp.log(-rate) - cum]
    low = jnp.concatenate([v[:n] for v in lines], axis=0)
    high = jnp.concatenate([v[n:] for v in lines], axis=0)
    return pick(c == 0, low, high)


def leave_kernel(sz, slots, riders, sc, zero_own, zero_other, one_own, one_other, *refs):
    c = sc[0]
    if riders:
        shared, refs = refs[0], refs[1:]
        total = shared[...] + one_other[sz.rows :, :].astype(F32)
        extra = resplit(total[:PAD])
        part = (total.shape[0] - PAD) // riders
    outs = refs[:slots]
    for i in range(4):
        refs[slots][i] = sc[i]
    for r in range(slots):
        rows = aligned(lax.rem(sc[3] + r, slots) * HALF, HALF)
        own = pick(c == 0, zero_own[rows, :], one_own[rows, :])
        other = pick(c == 0, zero_other[rows, :], one_other[rows, :])
        put_pair(outs[r], c, own, other)
        if riders:
            lines = [extra, total[PAD + r * part : PAD + (r + 1) * part]]
            outs[r][BLOCK:, :] = jnp.concatenate(lines, axis=0).astype(LOW)


def home_kernel(slots, sc, *refs):
    early, late, out, grad = refs[:slots], refs[slots : 2 * slots], refs[-3], refs[-2]
    for i in range(4):
        refs[-1][i] = sc[i]
    first = sc[0] == 0
    for r in range(slots):
        at = lax.rem(sc[3] - r + slots, slots)
        out[at] = pick(first, early[r][...], late[r][:BLOCK, :]).astype(F32)
        grad[at] = pick(first, late[r][:BLOCK, :], early[r][...]).astype(F32)


def whole(shape):
    return pl.BlockSpec(shape, lambda *_: (0,) * len(shape))


def per_device(
    tokens,
    slot_order,
    log_decay,
    grad_out,
    in_gain,
    w_gate,
    w_inner,
    w_shared,
    conv_inner,
    conv_shared,
    d_skip,
    norm_gain,
    w_out,
):
    slots = tokens.shape[0]
    span = tokens.shape[1]
    width = tokens.shape[2]
    seq = lax.axis_size("seq")
    head_axis = lax.axis_size("head")
    cores = lax.axis_size("section")
    spans = seq // slots
    c = lax.axis_index("section")
    z = lax.axis_index("seq")
    h = lax.axis_index("head")
    k = lax.rem(z, slots)
    inner_dev = w_gate.shape[2]
    channels = inner_dev // cores
    shared = w_shared.shape[2]
    heads_dev = d_skip.shape[1]
    taps = conv_inner.shape[1]
    sz = Sizes(
        slots * span // BLOCK,
        width,
        channels,
        heads_dev // cores,
        shared // 2,
        taps,
        head_axis,
        inner_dev * head_axis,
    )
    first = c == 0
    swap = [(0, 1), (1, 0)]
    nb, tok, rows, chunk = sz.blocks, sz.tokens, sz.rows, sz.chunk

    def cross(x):
        return lax.ppermute(x, "section", swap)

    def turn(x, r):
        pairs = [(i, i // slots * slots + (i % slots + r) % slots) for i in range(seq)]
        return lax.ppermute(x, "seq", pairs) if r else x

    def over_heads(x, d):
        return lax.ppermute(x, "head", [(i, i ^ d) for i in range(head_axis)])

    def next_span(x, way):
        pairs = [(i, i + way * slots) for i in range(seq) if 0 <= i + way * slots < seq]
        return lax.ppermute(x, "seq", pairs)

    def shape(dims, dtype):
        return jax.ShapeDtypeStruct(dims, dtype)

    prefetch = functools.partial(pltpu.PrefetchScalarGridSpec, num_scalar_prefetch=1)
    options = pltpu.CompilerParams(vmem_limit_bytes=VMEM_BYTES)
    anywhere = pl.BlockSpec(memory_space=pl.ANY)
    smem = pl.BlockSpec(memory_space=pltpu.SMEM)
    vmem = pl.BlockSpec(memory_space=pltpu.VMEM)
    index_shape = shape((4,), jnp.int32)

    def cost(flops, moved):
        return pl.CostEstimate(flops=int(flops), bytes_accessed=int(moved), transcendentals=0)

    def take_rows(sc, source, rates, deps=()):
        given = [source] if rates is None else [source, rates]
        more = 0 if rates is None else PAD
        got = pl.pallas_call(
            functools.partial(slice_kernel, sz, slots, rates is not None, len(deps)),
            in_specs=[smem, smem, anywhere]
            + ([] if rates is None else [vmem])
            + [anywhere] * len(deps),
            out_specs=[anywhere] * slots + [smem],
            out_shape=[shape((HALF + more, width), LOW)] * slots + [index_shape],
            scratch_shapes=([pltpu.VMEM((slots, PAD, width), LOW)] if more else [])
            + [pltpu.SemaphoreType.DMA((2 * slots,))],
            compiler_params=options,
        )(sc, slot_order, *given, *deps)
        return got[:slots], got[slots]

    def to_members(pieces):
        return [turn(x, r) for r, x in enumerate(pieces)]

    sc = jnp.stack([c, h, z, k]).astype(jnp.int32)
    tok_slices, sc = take_rows(sc, tokens, log_decay)
    tok_pieces = to_members(tok_slices)
    tok_others = [cross(x) for x in tok_pieces]

    wide = 2 * channels + shared
    w_sent, o_sent, pv_mine, pv_sent = pl.pallas_call(
        functools.partial(pack_kernel, sz),
        in_specs=[smem] + [anywhere] * 4 + [vmem] * 5,
        out_specs=[anywhere, anywhere, vmem, vmem],
        out_shape=[
            shape((width, wide), LOW),
            shape((channels, width), LOW),
            shape((16, width), F32),
            shape((16, width), F32),
        ],
        scratch_shapes=[pltpu.SemaphoreType.DMA((4,))],
        compiler_params=options,
    )(sc, w_gate, w_inner, w_shared, w_out, in_gain, conv_inner, conv_shared, d_skip, norm_gain)
    raw = [w_gate, w_inner, w_shared, w_out]
    sent = [cross(w_sent), cross(o_sent)]
    gains = [pv_mine, cross(pv_sent)]

    def span_total(table):
        ends = table[: sz.heads, BLOCK - 1 :: BLOCK]
        return jnp.repeat(jnp.exp(jnp.sum(ends, axis=1)), sz.head_width)[:, None]

    parts_shape = shape((head_axis, rows + PAD, chunk), LOW)
    weight_specs = [anywhere] * 6
    wide_weights = pltpu.VMEM((width, wide), LOW)
    out_weights = pltpu.VMEM((channels, width), LOW)
    copy_sems = pltpu.SemaphoreType.DMA((4,))
    dense = 2 * tok * width * (wide + channels)

    def forward(layer, sc, sources):
        def at(b, _):
            return (b, 0)

        piece = pl.BlockSpec((HALF, chunk), at)
        table = pl.BlockSpec((16, BLOCK), lambda b, _: (0, b))
        if layer == 0:
            src_specs = [whole((HALF + PAD, width))] * (2 * slots)
            more_specs = [table, table]
            more_shapes = [shape((16, tok), F32)] * 2
        else:
            src_specs = [piece] * (2 * head_axis) + [whole((HALF, width))] * (2 * slots) + [table]
            more_specs = [pl.BlockSpec((BLOCK, width), at)]
            more_shapes = [shape((tok, width), LOW)]

        def call(halo, begin):
            return pl.pallas_call(
                functools.partial(forward_kernel, sz, layer, slots),
                grid_spec=prefetch(
                    grid=(nb,),
                    in_specs=src_specs
                    + [whole((16, width)), whole((16, width))]
                    + weight_specs
                    + [whole((8, sz.lin)), whole((channels, sz.states))],
                    out_specs=[
                        pl.BlockSpec((BLOCK, width), at),
                        pl.BlockSpec((BLOCK, channels), at),
                        pl.BlockSpec((BLOCK, sz.lin), at),
                        pl.BlockSpec((BLOCK, channels), at),
                        pl.BlockSpec((1, channels, sz.states), lambda b, _: (b, 0, 0)),
                        pl.BlockSpec((1, BLOCK), lambda b, _: (0, b)),
                        pl.BlockSpec((2, BLOCK), lambda b, _: (0, b)),
                        pl.BlockSpec((BLOCK, channels), at),
                        whole((channels, sz.states)),
                        smem,
                        piece,
                    ]
                    + more_specs,
                    scratch_shapes=[
                        pltpu.VMEM((BLOCK, width), LOW),
                        pltpu.VMEM((BLOCK, width), LOW),
                        wide_weights,
                        out_weights,
                        pltpu.VMEM((BLOCK + 8, sz.lin), F32),
                        pltpu.VMEM((channels, sz.states), F32),
                        copy_sems,
                    ],
                ),
                out_shape=[
                    shape((tok, width), LOW),
                    shape((tok, channels), F32),
                    shape((tok, sz.lin), LOW),
                    shape((tok, channels), F32),
                    shape((nb, channels, sz.states), LOW),
                    shape((1, tok), F32),
                    shape((2, tok), F32),
                    shape((tok, channels), LOW),
                    shape((channels, sz.states), F32),
                    index_shape,
                    shape((rows, chunk), LOW),
                ]
                + more_shapes,
                compiler_params=options,
                cost_estimate=cost(6 * dense, 16e6),
            )(sc, *sources, *gains, *raw, *sent, halo, begin)

        halo = jnp.zeros((8, sz.lin), F32)
        begin = jnp.zeros((channels, sz.states), F32)
        if spans == 1:
            return call(halo, begin), halo
        trial = call(halo, begin)
        halo = next_span(trial[2][tok - 8 :].astype(F32), 1)
        local = call(halo, begin)[8]
        total = span_total(trial[11] if layer == 0 else sources[-1])
        for _ in range(spans - 1):
            begin = next_span(total * begin + local, 1)
        return call(halo, begin), halo

    def backward(layer, sc, sources, saved, decays, halo, deps):
        def at(i, _):
            return (nb - 1 - i, 0)

        if layer == 0:
            src_specs = [whole(s.shape) for s in sources]
        else:
            stat = pl.BlockSpec((2, BLOCK), lambda i, _: (0, nb - 1 - i))
            src_specs = [pl.BlockSpec((BLOCK, width), at)] + [stat] * head_axis
        gl, lin, ssd, inc = saved
        mixed_spec = [pl.BlockSpec((BLOCK, width), at)] if layer == 0 else []
        mixed_shape = [shape((tok, width), LOW)] if layer == 0 else []

        def call(halo_grad, begin):
            return pl.pallas_call(
                functools.partial(backward_kernel, sz, layer, len(deps)),
                grid_spec=prefetch(
                    grid=(nb,),
                    in_specs=src_specs
                    + [
                        pl.BlockSpec((BLOCK, channels), at),
                        whole(lin.shape),
                        pl.BlockSpec((BLOCK, channels), at),
                        pl.BlockSpec((1, channels, sz.states), lambda i, _: (nb - 1 - i, 0, 0)),
                        pl.BlockSpec((16, BLOCK), lambda i, _: (0, nb - 1 - i)),
                        whole((16, width)),
                        whole((16, width)),
                        *weight_specs,
                        whole((8, sz.lin)),
                        whole((8, sz.lin)),
                        whole((channels, sz.states)),
                    ]
                    + [anywhere] * len(deps),
                    out_specs=[
                        pl.BlockSpec((BLOCK, wide), at),
                        pl.BlockSpec((BLOCK, channels), at),
                        whole((PAD, 3 * channels)),
                        whole((8, sz.lin)),
                        whole((channels, sz.states)),
                        whole((8, sz.lin)),
                        smem,
                    ]
                    + mixed_spec,
                    scratch_shapes=[
                        pltpu.VMEM((BLOCK, width), LOW),
                        out_weights,
                        pltpu.VMEM((BLOCK + 8, sz.lin), F32),
                        pltpu.VMEM((BLOCK + 8, sz.lin), F32),
                        pltpu.VMEM((channels, sz.states), F32),
                        pltpu.VMEM((PAD, HALF), F32),
                        pltpu.VMEM((8, sz.lin), F32),
                        copy_sems,
                    ],
                ),
                out_shape=[
                    shape((tok, wide), LOW),
                    shape((tok, channels), LOW),
                    shape((PAD, 3 * channels), LOW),
                    shape((8, sz.lin), F32),
                    shape((channels, sz.states), F32),
                    shape((8, sz.lin), F32),
                    index_shape,
                ]
                + mixed_shape,
                compiler_params=options,
                cost_estimate=cost(8 * dense, 16e6),
            )(
                sc, *sources, gl, lin, ssd, inc, decays, *gains, *raw, *sent,
                halo, halo_grad, begin, *deps,
            )

        halo_grad = jnp.zeros((8, sz.lin), F32)
        begin = jnp.zeros((channels, sz.states), F32)
        if spans == 1:
            return call(halo_grad, begin)
        local = call(halo_grad, begin)[4]
        for _ in range(spans - 1):
            begin = next_span(span_total(decays) * begin + local, -1)
        halo_grad = next_span(call(halo_grad, begin)[5], -1)
        return call(halo_grad, begin)

    def project(layer, sc, given, extra, small, deps):
        back = small is not None
        row = pl.BlockSpec((2, BLOCK), lambda b, _: (0, b))
        block = pl.BlockSpec((BLOCK, width), lambda b, _: (b, 0))
        more = [*gains, small] if back else []
        return pl.pallas_call(
            functools.partial(project_kernel, sz, layer, back, len(deps)),
            grid_spec=prefetch(
                grid=(nb,),
                in_specs=[
                    pl.BlockSpec((BLOCK, given.shape[1]), lambda b, _: (b, 0)),
                    block if back else row,
                ]
                + weight_specs
                + [whole(x.shape) for x in more]
                + [anywhere] * len(deps),
                out_specs=[whole(parts_shape.shape), whole(parts_shape.shape), smem]
                + ([whole((PAD, chunk))] if back else []),
                scratch_shapes=([pltpu.VMEM((8, width), F32)] if back else [])
                + [
                    wide_weights if back else out_weights,
                    pltpu.VMEM((BLOCK, width), LOW),
                    pltpu.VMEM((PAD, HALF), F32),
                    pltpu.VMEM((PAD, HALF), F32),
                    copy_sems,
                ],
            ),
            out_shape=[parts_shape, parts_shape, index_shape]
            + ([shape((PAD, chunk), LOW)] if back else []),
            compiler_params=options,
            cost_estimate=cost(dense, 6e6),
        )(sc, given, extra, *raw, *sent, *more, *deps)

    def scatter(sc, keep, send, *riders):
        size = rows + PAD + sum(rider[0].shape[0] for rider in riders)
        flat = [x for rider in riders for x in rider]
        joined = pl.pallas_call(
            functools.partial(join_kernel, sz, len(riders)),
            in_specs=[smem] + [vmem] * (2 + len(flat)),
            out_specs=[smem] + [vmem] * head_axis,
            out_shape=[index_shape, shape((size, chunk), F32)]
            + [shape((size, chunk), LOW)] * (head_axis - 1),
            compiler_params=options,
        )(sc, keep, cross(send), *flat)
        return [joined[1]] + [over_heads(joined[1 + d], d) for d in range(1, head_axis)], joined[0]

    def gather(low):
        own = [low] + [over_heads(low, d) for d in range(1, head_axis)]
        return own + [cross(x) for x in own]

    def section_output(layer, sc, parts, resid):
        return pl.pallas_call(
            functools.partial(output_kernel, sz, layer),
            in_specs=[smem] + [vmem] * (head_axis + 1),
            out_specs=[vmem] * 4 + [smem],
            out_shape=[
                shape((rows, chunk), F32),
                shape((rows, chunk), LOW),
                shape((rows, chunk), F32),
                shape((8, HALF), F32),
                index_shape,
            ],
            compiler_params=options,
        )(sc, *parts, resid)

    part = width // seq
    columns = 3 * channels
    share = part // head_axis
    shared_size = seq * share + PAD

    def section_input(layer, sc, parts, *others, deps=()):
        if layer == 0:
            outs = [
                shape((rows + PAD, chunk), LOW),
                shape((rows + shared_size, chunk), LOW),
                shape((shared_size, chunk), F32),
            ]
        else:
            outs = [shape((rows, chunk), F32), shape((rows + PAD, chunk), LOW)]
        return pl.pallas_call(
            functools.partial(input_kernel, sz, layer),
            in_specs=[smem] + [vmem] * (head_axis + len(others)) + [anywhere] * len(deps),
            out_specs=[vmem] * len(outs) + [smem],
            out_shape=outs + [index_shape],
            compiler_params=options,
        )(sc, *parts, *others, *deps)

    def weight_grads(sc, normed, cat, mixed, scaled, small, common):
        outs = pl.pallas_call(
            functools.partial(weights_kernel, sz, seq),
            in_specs=[smem] + [vmem] * 6,
            out_specs=[smem] + [vmem] * (seq + head_axis),
            out_shape=[index_shape]
            + [shape((part + PAD, columns), LOW)] * seq
            + [shape((shared_size, shared), LOW)] * head_axis,
            scratch_shapes=[pltpu.VMEM((width, columns), LOW), pltpu.VMEM((width, shared), F32)],
            compiler_params=options,
            cost_estimate=cost(4 * dense, 12e6),
        )(sc, normed, cat, mixed, scaled, small, common)
        return over_seq(outs[1 : 1 + seq]), outs[1 + seq :], outs[0]

    def over_seq(chunks):
        pieces = [chunks[0]]
        for r in range(1, seq):
            pairs = [(i, (i + r) % seq) for i in range(seq)]
            pieces.append(lax.ppermute(chunks[r], "seq", pairs))
        return pieces

    def leave(sc, *arrays, riders=0):
        size = BLOCK + (share + PAD if riders else 0)
        pieces = pl.pallas_call(
            functools.partial(leave_kernel, sz, slots, riders),
            in_specs=[smem] + [vmem] * len(arrays),
            out_specs=[vmem] * slots + [smem],
            out_shape=[shape((size, chunk), LOW)] * slots + [index_shape],
            compiler_params=options,
        )(sc, *arrays)
        return to_members(pieces[:slots]), pieces[slots]

    out_slices, unused = take_rows(sc, grad_out, None, tok_pieces[1:])
    out_pieces = to_members(out_slices)
    fw0, halo0 = forward(0, sc, tok_pieces + tok_others)
    base0, decays = fw0[10], fw0[11:13]
    pr0 = project(0, fw0[9], fw0[7], fw0[6], None, [out_pieces[1], out_pieces[-1]])
    out_others = [cross(x) for x in out_pieces]
    parts, sc_join = scatter(sc, pr0[0], pr0[1])
    res1, low1, mixed0, square0, unused = section_output(0, sc, parts, base0)
    pieces1 = gather(low1)
    square_other = cross(square0)

    fw1, halo1 = forward(1, sc, pieces1 + out_pieces + out_others + [decays[1]])
    stat = fw1[6] + cross(fw1[6])
    stats = [stat] + [over_heads(stat, d) for d in range(1, head_axis)]
    pr1 = project(1, fw1[9], fw1[7], fw1[6], None, [])
    parts_out, sc_out = scatter(sc, pr1[0], pr1[1])
    bw1 = backward(1, sc_out, [fw1[11]] + stats, fw1[1:5], decays[1], halo1, [])
    pr1 = project(1, bw1[6], bw1[0], fw1[0], bw1[3], parts_out[1:])
    parts, sc_join = scatter(sc, pr1[0], pr1[1])
    weights1, heads1, sc_weights = weight_grads(
        sc_join, fw1[0], bw1[0], fw1[11], bw1[1], bw1[2], pr1[3]
    )
    igrad1, glow1, sc_in = section_input(
        1, sc_weights, parts, res1, fw1[10], fw1[5], *gains, mixed0
    )
    piecesg = gather(glow1)

    early, unused = leave(sc_in, low1, pieces1[head_axis], glow1, piecesg[head_axis])
    bw0 = backward(
        0, sc, piecesg + [square0, square_other], fw0[1:5], decays[0], halo0,
        [weights1[1], weights1[-1]],
    )
    pr0 = project(0, bw0[6], bw0[0], fw0[0], bw0[3], weights1[2:-1] + early[1:])
    weights0, heads0, sc_weights = weight_grads(
        pr0[2], fw0[0], bw0[0], bw0[7], bw0[1], bw0[2], pr0[3]
    )
    parts, sc_join = scatter(sc_weights, pr0[0], pr0[1], heads0, heads1)

    unused, low2, unused_mixed, unused_square, sc_out = section_output(1, sc_in, parts_out, res1)
    glow0, to_other, shared_own, sc_end = section_input(
        0, sc_out, parts, base0, igrad1, fw0[5], *gains, low2, deps=weights0[1:]
    )
    got = cross(to_other)
    if spans == 1:
        late, sc_end = leave(sc_end, glow0, got, low2, got, shared_own, riders=seq)
        shared_parts = late
    else:
        late, sc_end = leave(sc_end, glow0, got, low2, got)
        total = shared_own + got[rows:].astype(F32)
        extra = resplit(total[:PAD])
        fill = jnp.zeros((BLOCK, shared), F32)
        chunks = [
            jnp.concatenate([fill, extra, total[PAD + r * share : PAD + (r + 1) * share]])
            for r in range(seq)
        ]
        shared_parts = over_seq([x.astype(LOW) for x in chunks])
    section_out, input_grad, sc_end = pl.pallas_call(
        functools.partial(home_kernel, slots),
        in_specs=[smem] + [vmem] * (2 * slots),
        out_specs=[vmem, vmem, smem],
        out_shape=[shape((slots, BLOCK, chunk), F32)] * 2 + [index_shape],
        compiler_params=options,
    )(sc, *early, *late)

    def summed(sc, pieces):
        return pl.pallas_call(
            functools.partial(sum_kernel, sz),
            in_specs=[smem] + [vmem] * seq,
            out_shape=shape((part + PAD, columns), LOW),
            compiler_params=options,
        )(sc, *pieces)

    sums0, sums1 = summed(sc_end, weights0), summed(sc_in, weights1)
    final = pl.pallas_call(
        functools.partial(final_kernel, sz),
        in_specs=[smem] + [vmem] * (3 + seq),
        out_shape=[
            shape((part, inner_dev), F32),
            shape((part, inner_dev), F32),
            shape((inner_dev, part), F32),
            shape((taps, inner_dev), F32),
            shape((1, inner_dev), F32),
            shape((1, heads_dev), F32),
            shape((share, shared), F32),
            shape((PAD // 2, shared), F32),
        ],
        compiler_params=options,
    )(sc, sums0, sums1, cross(pick(first, sums1, sums0)), *shared_parts)
    common = final[7]
    place = z * head_axis + h
    conv_part = shared // (seq * head_axis)
    gain_part = width // (seq * head_axis)
    return (
        section_out[None],
        input_grad[None],
        lax.dynamic_slice_in_dim(common[taps:].reshape(-1), place * gain_part, gain_part, 0)[None],
        final[0][None],
        final[1][None],
        final[6][None],
        final[3][None],
        lax.dynamic_slice_in_dim(common[:taps], place * conv_part, conv_part, 1)[None],
        final[5],
        final[4],
        final[2][None],
    )


def solution(mesh):
    placed = (
        P(None, "seq", None),
        P(),
        P("section", None, "head", "seq"),
        P(None, "seq", None),
        P("section", None),
        P("section", None, "head"),
        P("section", None, "head"),
        P("section", None, None),
        P("section", None, "head"),
        P("section", None, None),
        P("section", "head"),
        P("section", "head"),
        P("section", None, None),
    )
    return jax.shard_map(
        per_device,
        mesh=mesh,
        in_specs=placed,
        out_specs=(
            P("section", None, "seq", "head"),
            P("section", None, "seq", "head"),
            P("section", ("seq", "head")),
            P("section", "seq", "head"),
            P("section", "seq", "head"),
            P("section", ("seq", "head"), None),
            P("section", None, "head"),
            P("section", None, ("seq", "head")),
            P("section", "head"),
            P("section", "head"),
            P("section", "head", "seq"),
        ),
        check_vma=False,
    )
```

```python
import functools

import jax
import jax.numpy as jnp
from jax import lax
from jax.experimental import pallas as pl
from jax.experimental.pallas import tpu as pltpu
from jax.sharding import PartitionSpec as P

BLOCK = 256
HALF = BLOCK // 2
PAD = 16
EPS = 1e-05
F32 = jnp.float32
LOW = jnp.bfloat16
HIDDEN = -1e30
NN = ((1,), (0,))
NT = ((1,), (1,))
TN = ((0,), (0,))
VMEM_BYTES = 50 * 1024 * 1024


def dot(a, b, dims):
    return lax.dot_general(a, b, (dims, ((), ())), preferred_element_type=F32)


def aligned(start, size):
    return pl.ds(pl.multiple_of(start, size), size)


def spread(cols, first, count, width):
    rows = cols.shape[0]
    lane = lax.broadcasted_iota(jnp.int32, (rows, count * width), 1)
    out = jnp.broadcast_to(cols[:, first : first + 1], (rows, count * width))
    for h in range(1, count):
        out = jnp.where(lane >= h * width, cols[:, first + h : first + h + 1], out)
    return out


def per_head(array, h, width):
    lane = lax.broadcasted_iota(jnp.int32, array.shape, 1)
    inside = (lane >= h * width) & (lane < (h + 1) * width)
    return jnp.where(inside, array, jnp.zeros_like(array))


def split_low(value):
    high = value.astype(LOW).astype(F32)
    return high, value - high


def column_of(row, size):
    return jnp.transpose(jnp.broadcast_to(row, (128, size)))


def sigmoid(v):
    return 0.5 * jnp.tanh(0.5 * v) + 0.5


def pick(flag, a, b):
    return jnp.where(flag, a, b)


class Sizes:
    def __init__(self, blocks, width, channels, heads, states, taps, head_axis, inner):
        self.blocks = blocks
        self.width = width
        self.channels = channels
        self.heads = heads
        self.head_width = channels // heads
        self.states = states
        self.lin = channels + 2 * states
        self.taps = taps
        self.head_axis = head_axis
        self.chunk = width // head_axis
        self.rows = blocks * HALF
        self.tokens = blocks * BLOCK
        self.inner = inner


def weight_copies(sz, layer, c, h, raw, got, wv, ov, sems):
    gate, inner, shared, out = raw
    ch = sz.channels
    cols = aligned(c * ch, ch)
    rows = aligned((h * 2 + c) * ch, ch)
    own, sent = [], []
    if wv is not None:
        own += [
            (gate.at[0, :, cols], wv.at[:, :ch]),
            (inner.at[0, :, cols], wv.at[:, ch : 2 * ch]),
            (shared.at[0], wv.at[:, 2 * ch :]),
        ]
        sent += [(got[0], wv)]
    if ov is not None:
        own += [(out.at[0, rows, :], ov)]
        sent += [(got[1], ov)]
    return [
        (c == layer, [pltpu.make_async_copy(p, q, sems.at[i]) for i, (p, q) in enumerate(own)]),
        (c != layer, [pltpu.make_async_copy(p, q, sems.at[i]) for i, (p, q) in enumerate(sent)]),
    ]


def run_copies(choices, start, wait):
    for flag, copies in choices:

        @pl.when(flag)
        def _(copies=copies):
            if start:
                for copy in copies:
                    copy.start()
            if wait:
                for copy in copies:
                    copy.wait()


def put_ordered(sz, dst, c, k, b, own, other):
    for r in range(len(own)):

        @pl.when(lax.rem(k - b + len(own), len(own)) == r)
        def _(r=r):
            put_pair(dst, c, own[r][:HALF, :], other[r][:HALF, :])


def put_pair(dst, c, own, other):
    dst[aligned(c * HALF, HALF), :] = own
    dst[aligned((1 - c) * HALF, HALF), :] = other


def put_pieces(sz, dst, c, h, own, other):
    for d in range(sz.head_axis):
        cols = aligned((h ^ d) * sz.chunk, sz.chunk)
        dst[aligned(c * HALF, HALF), cols] = own[d]
        dst[aligned((1 - c) * HALF, HALF), cols] = other[d]


def line_of(table, at):
    line = lax.broadcasted_iota(jnp.int32, table.shape, 0)
    return jnp.sum(jnp.where(line == at, table, 0.0), axis=0, keepdims=True)


def conv_forward(sz, ext, taps):
    pre = taps[0:1] * ext[5 : 5 + BLOCK, :]
    for j in range(1, sz.taps):
        pre = pre + taps[j : j + 1] * ext[5 + j : 5 + j + BLOCK, :]
    return pre


def decay_of(sz, cols, rp, h, mask):
    rows = cols[:, h : h + 1] + rp[12 + h : 13 + h, :]
    return jnp.exp(jnp.where(mask, rows, HIDDEN))


def lower_mask():
    t = lax.broadcasted_iota(jnp.int32, (BLOCK, BLOCK), 0)
    s = lax.broadcasted_iota(jnp.int32, (BLOCK, BLOCK), 1)
    return t >= s


def forward_kernel(sz, layer, slots, sc, *refs):
    n = sz.head_axis
    sources = 2 * slots if layer == 0 else 2 * n + 2 * slots
    src, refs = refs[:sources], refs[sources:]
    if layer == 1:
        table, refs = refs[0], refs[1:]
    gains, raw, got, halo, begin = refs[0:2], refs[2:6], refs[6:8], refs[8], refs[9]
    normed_o, gl_o, lin_o, ssd_o, inc_o, inv_o, part_o, unit_o, fin_o, sc_o, base_o = refs[10:21]
    refs = refs[21:]
    if layer == 1:
        mixed_o, refs = refs[0], refs[1:]
    else:
        tables_o, refs = refs[0:2], refs[2:]
    xs, ms, wv, ov, ext, state, sems = refs
    b = pl.program_id(0)
    c, h, k = sc[0], sc[1], sc[3]
    ch, st = sz.channels, sz.states
    copies = weight_copies(sz, layer, c, h, raw, got, wv, ov if layer == 1 else None, sems)

    @pl.when(b == 0)
    def _():
        run_copies(copies, True, False)
        ext[0:8, :] = halo[...]
        state[...] = begin[...]
        for i in range(4):
            sc_o[i] = sc[i]

    mine = aligned(c * HALF, HALF)
    cols = aligned(h * sz.chunk, sz.chunk)
    if layer == 0:
        put_ordered(sz, xs, c, k, b, src[:slots], src[slots:])
        base_o[...] = xs[mine, cols]
        for r in range(slots):

            @pl.when(lax.rem(k - b + slots, slots) == r)
            def _(r=r):
                own = decay_table(rates_of(src[r]), c, sz.heads)
                other = decay_table(rates_of(src[slots + r]), c, sz.heads)
                tables_o[0][...] = pick(c == 0, own, other)
                tables_o[1][...] = pick(c == 0, other, own)

        rp = tables_o[0][...]
    else:
        put_pieces(sz, xs, c, h, [r[...] for r in src[:n]], [r[...] for r in src[n : 2 * n]])
        put_ordered(sz, ms, c, k, b, src[2 * n : 2 * n + slots], src[2 * n + slots :])
        base_o[...] = ms[mine, cols]
        mixed_o[...] = ms[...]
        rp = table[...]

    pv = pick(c == layer, gains[0][...], gains[1][...])
    x = xs[...].astype(F32)
    inv_in = lax.rsqrt(jnp.mean(x * x, axis=1, keepdims=True) + EPS)
    normed = (x * inv_in * pv[0:1, : sz.width]).astype(LOW)
    normed_o[...] = normed

    @pl.when(b == 0)
    def _():
        run_copies(copies, False, True)

    proj = dot(normed, wv[...], NN)
    gl = proj[:, :ch]
    gl_o[...] = gl
    lin = proj[:, ch:].astype(LOW)
    lin_o[...] = lin
    ext[8 : 8 + BLOCK, :] = lin.astype(F32)
    pre = conv_forward(sz, ext, pv[1:5, : sz.lin])
    ext[0:8, :] = ext[BLOCK : BLOCK + 8, :]
    act = (pre * sigmoid(pre)).astype(LOW)
    values, bm, cm = act[:, :ch], act[:, ch : ch + st], act[:, ch + st :]

    cols = jnp.transpose(rp)
    mask = lower_mask()
    gram = dot(cm, bm, NT)
    mixes, parts = [], []
    for i in range(sz.heads):
        mixes.append((gram * decay_of(sz, cols, rp, i, mask)).astype(LOW))
        parts.append(per_head(values, i, sz.head_width))
    intra = dot(jnp.concatenate(mixes, axis=1), jnp.concatenate(parts, axis=0), NN)

    low_state = state[...].astype(LOW)
    inc_o[0] = low_state
    ecum = spread(cols, sz.heads, sz.heads, sz.head_width)
    inter = dot(cm, low_state, NT) * ecum
    vf = values.astype(F32)
    carried = (vf * spread(cols, 2 * sz.heads, sz.heads, sz.head_width)).astype(LOW)
    local = dot(carried, bm, TN)
    for i in range(sz.heads):
        rows = slice(i * sz.head_width, (i + 1) * sz.head_width)
        total = cols[BLOCK - 1 : BLOCK, sz.heads + i : sz.heads + i + 1]
        state[rows, :] = total * state[rows, :] + local[rows]
    ssd = intra + inter + pv[6:7, :ch] * vf
    ssd_o[...] = ssd
    gated = ssd * (gl * sigmoid(gl))
    weighty = gated * pv[5:6, :ch]
    unit_o[...] = weighty.astype(LOW)

    lane = lax.broadcasted_iota(jnp.int32, (BLOCK, 128), 1)
    square = jnp.sum(gated * gated, axis=1, keepdims=True)
    if layer == 0:
        project = jnp.zeros_like(square)
    else:
        scaled_grad = dot(ms[...], ov[...], NT)
        project = jnp.sum(scaled_grad * weighty, axis=1, keepdims=True)
    stats = jnp.where(lane == 0, square, jnp.where(lane == 1, project, inv_in))
    stats = jnp.transpose(stats)
    part_o[...] = stats[0:2, :]
    inv_o[...] = stats[2:3, :]

    @pl.when(b == sz.blocks - 1)
    def _():
        fin_o[...] = state[...]


def scalar_lines(sz, lines):
    fill = [jnp.zeros((8 - sz.blocks, HALF), F32)] if sz.blocks < 8 else []
    high, low = split_low(jnp.concatenate(lines + fill, axis=0))
    table = jnp.concatenate([high, low], axis=0).astype(LOW)
    return jnp.concatenate([table] * (sz.chunk // HALF), axis=1)


def own_rows(sz, ref, which):
    blocks = [ref[aligned(b * BLOCK + which * HALF, HALF), :] for b in range(sz.blocks)]
    return jnp.concatenate(blocks, axis=0)


def project_kernel(sz, layer, deps, sc, unit_r, stats_r, *refs):
    raw, got, refs = refs[:4], refs[4:6], refs[6 + deps :]
    keep, send, sc_o, weights, sems = refs
    c, h = sc[0], sc[1]
    copies = weight_copies(sz, layer, c, h, raw, got, None, weights, sems)
    run_copies(copies, True, False)
    for i in range(4):
        sc_o[i] = sc[i]
    sides = []
    for which, out in ((c, keep), (1 - c, send)):
        sides.append((out, own_rows(sz, unit_r, which)))
        lines = [
            stats_r[0:1, aligned(b * BLOCK + which * HALF, HALF)] for b in range(sz.blocks)
        ]
        table = scalar_lines(sz, lines)
        for d in range(sz.head_axis):
            out[d, sz.rows :, :] = table
    run_copies(copies, False, True)
    for out, rows in sides:
        for d in range(sz.head_axis):
            chunk = weights[:, aligned((h ^ d) * sz.chunk, sz.chunk)]
            out[d, : sz.rows, :] = dot(rows, chunk, NN).astype(LOW)


def lift_kernel(sz, layer, deps, sc, cat_r, normed_r, zero_gains, one_gains, small_r, *refs):
    raw, got, refs = refs[:4], refs[4:6], refs[6 + deps :]
    keep, send, sc_o, common_o, wide, weights, sems = refs
    c, h = sc[0], sc[1]
    copies = weight_copies(sz, layer, c, h, raw, got, weights, None, sems)
    run_copies(copies, True, False)
    for i in range(4):
        sc_o[i] = sc[i]
    wide[...] = jnp.zeros_like(wide)
    run_copies(copies, False, True)
    for which, out in ((c, keep), (1 - c, send)):
        rows = own_rows(sz, cat_r, which)
        along = jnp.zeros((sz.rows, 1), F32)
        for d in range(sz.head_axis):
            cols = aligned((h ^ d) * sz.chunk, sz.chunk)
            product = dot(rows, weights[cols, :], NT)
            out[d, : sz.rows, :] = product.astype(LOW)
            blocks = [
                normed_r[aligned(b * BLOCK + which * HALF, HALF), cols] for b in range(sz.blocks)
            ]
            product = product * jnp.concatenate(blocks, axis=0).astype(F32)
            wide[0:1, cols] += jnp.sum(product, axis=0, keepdims=True)
            along = along + jnp.sum(product, axis=1, keepdims=True)
        lines = [
            jnp.transpose(jnp.broadcast_to(along[b * HALF : (b + 1) * HALF], (HALF, 128)))[0:1, :]
            for b in range(sz.blocks)
        ]
        table = scalar_lines(sz, lines)
        for d in range(sz.head_axis):
            out[d, sz.rows :, :] = table
    gain_grad = wide[0:1, :] / pick(c == layer, zero_gains[0:1, :], one_gains[0:1, :])
    flat = [small_r[j : j + 1, sz.channels :] for j in range(sz.taps)]
    flat += [gain_grad[:, q * sz.chunk : (q + 1) * sz.chunk] for q in range(sz.head_axis)]
    high, low = split_low(jnp.concatenate(flat, axis=0))
    common_o[...] = jnp.concatenate([high, low], axis=0).astype(LOW)


def backward_kernel(sz, layer, deps, sc, *refs):
    n = sz.head_axis
    sources = 2 * n + 2 if layer == 0 else 1 + n
    src, refs = refs[:sources], refs[sources:]
    gl_r, lin_r, ssd_r, inc_r = refs[:4]
    table, gains, raw, got = refs[4], refs[5:7], refs[7:11], refs[11:13]
    halo, halo_grad, begin = refs[13:16]
    refs = refs[16 + deps :]
    cat_o, scaled_o, small_o, sums_o, fin_o, rim_o, sc_o = refs[:7]
    refs = refs[7:]
    if layer == 0:
        mixed_o, refs = refs[0], refs[1:]
    ms, ov, ext, back, state, heads_p, small, sems = refs
    i_step = pl.program_id(0)
    b = sz.blocks - 1 - i_step
    c, h = sc[0], sc[1]
    ch, st = sz.channels, sz.states
    copies = weight_copies(sz, layer, c, h, raw, got, None, ov, sems)
    pv = pick(c == layer, gains[0][...], gains[1][...])
    rp = table[...]

    @pl.when(i_step == 0)
    def _():
        run_copies(copies, True, True)
        back[BLOCK : BLOCK + 8, :] = halo_grad[...]
        state[...] = begin[...]
        small[...] = jnp.zeros_like(small)
        for i in range(4):
            sc_o[i] = sc[i]
        if layer == 0:
            for i in range(2):
                extra = src[i * n][sz.rows :, :].astype(F32)
                for d in range(1, n):
                    extra = extra + src[i * n + d][sz.rows :, :].astype(F32)
                heads_p[8 * i : 8 * i + 8, :] = extra[0:8, :HALF] + extra[8:16, :HALF]

    if layer == 0:
        rows = aligned(b * HALF, HALF)
        put_pieces(
            sz, ms, c, h, [r[rows, :] for r in src[:n]], [r[rows, :] for r in src[n : 2 * n]]
        )
        halves = []
        for k in range(2):
            alpha = lax.rsqrt(line_of(src[2 * n + k][...], b) / sz.inner + EPS)
            beta = alpha * alpha * line_of(heads_p[...], 8 * k + b) / sz.inner
            halves.append((alpha, beta))
        alpha, beta = (
            pick(
                c == 0,
                jnp.concatenate([halves[0][q], halves[1][q]], axis=1),
                jnp.concatenate([halves[1][q], halves[0][q]], axis=1),
            )
            for q in range(2)
        )
    else:
        stats = src[1][...]
        for d in range(1, n):
            stats = stats + src[1 + d][...]
        alpha = lax.rsqrt(stats[0:1, :] / sz.inner + EPS)
        beta = alpha * alpha * alpha * stats[1:2, :] / sz.inner

    sub = lax.broadcasted_iota(jnp.int32, rp.shape, 0)
    cols = jnp.transpose(jnp.where(sub == 12, alpha, jnp.where(sub == 13, beta, rp)))
    alpha, beta = cols[:, 12:13], cols[:, 13:14]

    gl = gl_r[...]
    ssd = ssd_r[...]
    sig = sigmoid(gl)
    swish = gl * sig
    slope = sig * (1.0 + gl * (1.0 - sig))
    gated = ssd * swish
    if layer == 0:
        mixed_grad = ms[...]
        mixed_o[...] = mixed_grad
    else:
        mixed_grad = src[0][...]
    scaled_grad = dot(mixed_grad, ov[...], NT)
    gain = pv[5:6, :ch]
    normal = gated * alpha
    small[4:5, :ch] += jnp.sum(scaled_grad * normal, axis=0, keepdims=True)
    scaled_o[...] = (normal * gain).astype(LOW)
    gated_grad = alpha * (scaled_grad * gain) - beta * gated
    ssd_grad = (gated_grad * swish).astype(LOW)
    gate_grad = (gated_grad * ssd * slope).astype(LOW)
    sgf = ssd_grad.astype(F32)

    before = lin_r[pl.ds(pl.multiple_of(jnp.maximum(b * BLOCK - 16, 0), 16), 16), :]
    ext[0:8, :] = pick(b > 0, before.astype(F32)[8:16, :], halo[...])
    ext[8 : 8 + BLOCK, :] = lin_r[aligned(b * BLOCK, BLOCK), :].astype(F32)
    taps = pv[1:5, : sz.lin]
    pre = conv_forward(sz, ext, taps)
    psig = sigmoid(pre)
    pact = pre * psig
    pslope = psig * (1.0 + pre * (1.0 - psig))
    act = pact.astype(LOW)
    values, bm, cm = act[:, :ch], act[:, ch : ch + st], act[:, ch + st :]
    vf = values.astype(F32)
    small[5:6, :ch] += jnp.sum(sgf * vf, axis=0, keepdims=True)

    mask = lower_mask()
    gram = dot(cm, bm, NT)
    gram_grad = jnp.zeros((BLOCK, BLOCK), F32)
    mixes, parts = [], []
    for i in range(sz.heads):
        decay = decay_of(sz, cols, rp, i, mask)
        mixes.append((gram * decay).astype(LOW))
        parts.append(per_head(ssd_grad, i, sz.head_width))
        gram_grad = gram_grad + dot(parts[-1], values, NT) * decay
    intra_grad = dot(jnp.concatenate(mixes, axis=0), jnp.concatenate(parts, axis=0), TN)

    ecum = spread(cols, sz.heads, sz.heads, sz.head_width)
    to_end = spread(cols, 2 * sz.heads, sz.heads, sz.head_width)
    inter_grad = (sgf * ecum).astype(LOW)
    low_state = state[...].astype(LOW)
    carried = (vf * to_end).astype(LOW)
    carried_grad = dot(bm, low_state, NT)
    gram_low = gram_grad.astype(LOW)
    b_grad = dot(gram_low, cm, TN) + dot(carried, low_state, NN)
    c_grad = dot(gram_low, bm, NN) + dot(inter_grad, inc_r[0], NN)
    value_grad = intra_grad + pv[6:7, :ch] * sgf + carried_grad * to_end
    entry = dot(inter_grad, cm, TN)
    for i in range(sz.heads):
        rows = slice(i * sz.head_width, (i + 1) * sz.head_width)
        total = cols[BLOCK - 1 : BLOCK, sz.heads + i : sz.heads + i + 1]
        state[rows, :] = total * state[rows, :] + entry[rows]

    pre_grad = jnp.concatenate([value_grad, b_grad, c_grad], axis=1) * pslope
    back[0:BLOCK, :] = pre_grad
    lin_grad = taps[0:1] * back[sz.taps - 1 : sz.taps - 1 + BLOCK, :]
    for j in range(1, sz.taps):
        at = sz.taps - 1 - j
        lin_grad = lin_grad + taps[j : j + 1] * back[at : at + BLOCK, :]
    for j in range(sz.taps):
        small[j : j + 1, :] += jnp.sum(pre_grad * ext[5 + j : 5 + j + BLOCK, :], axis=0, keepdims=True)
    back[BLOCK : BLOCK + 8, :] = back[0:8, :]
    cat_o[...] = jnp.concatenate([gate_grad, lin_grad.astype(LOW)], axis=1)

    @pl.when(i_step == sz.blocks - 1)
    def _():
        fin_o[...] = state[...]
        rim_o[...] = back[0:8, :]
        sums = small[...]
        flat = [sums[j : j + 1, :ch] for j in range(sz.taps + 2)]
        flat = [jnp.concatenate(flat[j : j + 3], axis=1) for j in range(0, len(flat), 3)]
        flat = flat + [jnp.zeros_like(flat[0])] * (4 - len(flat))
        high, low = split_low(jnp.concatenate(flat, axis=0))
        rest = jnp.zeros((PAD - 8, high.shape[1]), F32)
        small_o[...] = jnp.concatenate([high, low, rest], axis=0).astype(LOW)
        sums_o[...] = sums


def weights_kernel(sz, seq, sc, normed, cat, mixed, scaled, small, common, *refs):
    sc_o, outs, heads, full, wide = refs[0], refs[1 : seq + 1], refs[seq + 1 : -2], refs[-2], refs[-1]
    for i in range(4):
        sc_o[i] = sc[i]
    ch, st = sz.channels, sz.states
    step = sz.chunk
    for q in range(sz.head_axis):
        at = slice(q * step, (q + 1) * step)
        grads = dot(normed[:, at], cat[...], TN)
        full[at, : 2 * ch] = grads[:, : 2 * ch].astype(LOW)
        wide[at, :] = grads[:, 2 * ch :]
        full[at, 2 * ch :] = dot(mixed[:, at], scaled[...], TN).astype(LOW)
    rows = sz.width // seq
    part = rows // sz.head_axis
    for r, out in enumerate(outs):
        out[:rows, :] = full[aligned(lax.rem(sc[2] + r, seq) * rows, rows), :]
        out[rows:, :] = small[...]
    for d, out in enumerate(heads):
        lines = [
            wide[aligned(lax.rem(sc[2] + r, seq) * rows + (sc[1] ^ d) * part, part), :]
            for r in range(seq)
        ]
        out[:PAD, :] = common[...]
        out[PAD:, :] = jnp.concatenate(lines, axis=0).astype(LOW)


def resplit(extra):
    half = extra.shape[0] // 2
    high, low = split_low(extra[:half, :] + extra[half:, :])
    return jnp.concatenate([high, low], axis=0)


def join_kernel(sz, riders, sc, keep, recv, *refs):
    n = sz.head_axis
    more, refs = [refs[i * n : (i + 1) * n] for i in range(riders)], refs[riders * n :]
    sc_o, outs = refs[0], refs[1:]
    rows = sz.rows
    for i in range(4):
        sc_o[i] = sc[i]
    extra = resplit(keep[0, rows:, :].astype(F32) + recv[0, rows:, :].astype(F32))
    for d, out in enumerate(outs):
        out[:rows, :] = (keep[d, :rows, :].astype(F32) + recv[d, :rows, :].astype(F32)).astype(out.dtype)
        out[rows : rows + PAD, :] = extra.astype(out.dtype)
        at = rows + PAD
        for rider in more:
            size = rider[d].shape[0]
            out[at : at + size, :] = rider[d][...].astype(out.dtype)
            at += size


def total_of(parts, rows):
    total = parts[0][rows, :].astype(F32)
    for p in parts[1:]:
        total = total + p[rows, :].astype(F32)
    return total


def output_kernel(sz, layer, sc, *refs):
    n = sz.head_axis
    parts, refs = refs[:n], refs[n:]
    resid, res_o, low_o, mixed_o, square_o, sc_o = refs
    for i in range(4):
        sc_o[i] = sc[i]
    extra = total_of(parts, slice(sz.rows, sz.rows + PAD))
    square = extra[0:8, :HALF] + extra[8:16, :HALF]
    square_o[...] = square
    inv = lax.rsqrt(square / sz.inner + EPS)
    for b in range(sz.blocks):
        rows = slice(b * HALF, (b + 1) * HALF)
        col = column_of(inv[b : b + 1, :], HALF)[:, 0:1]
        mixed = total_of(parts, rows) * col
        res = resid[rows, :].astype(F32) + mixed
        res_o[rows, :] = res
        low_o[rows, :] = res.astype(LOW)
        mixed_o[rows, :] = mixed


def input_kernel(sz, layer, sc, *refs):
    n = sz.head_axis
    parts, refs = refs[:n], refs[n:]
    resid, outg, inv_r, gains = refs[0], refs[1], refs[2], refs[3:5]
    refs = refs[5:]
    if layer == 1:
        mixed = refs[0]
        grad_o, low_o, sc_o = refs[-3:]
    else:
        one_low = refs[0]
        low_o, swap_o, shared_o, sc_o = refs[-4:]
    for i in range(4):
        sc_o[i] = sc[i]
    c, h = sc[0], sc[1]
    first = c == 0
    mine = aligned(h * sz.chunk, sz.chunk)
    gain = pick(c == layer, gains[0][0:1, mine], gains[1][0:1, mine])
    extra = total_of(parts, slice(sz.rows, sz.rows + PAD))
    along = extra[0:8, :HALF] + extra[8:16, :HALF]
    tops, lows = [], []
    for b in range(sz.blocks):
        rows = slice(b * HALF, (b + 1) * HALF)
        at = b * BLOCK
        inv_row = pick(c == 0, inv_r[:, at : at + HALF], inv_r[:, at + HALF : at + BLOCK])
        inv = column_of(inv_row, HALF)[:, 0:1]
        share = column_of(along[b : b + 1, :] / sz.width, HALF)[:, 0:1]
        total = total_of(parts, rows)
        base = resid[rows, :].astype(F32)
        grad = outg[rows, :].astype(F32) + inv * (total * gain - base * (inv * share))
        low = grad.astype(LOW)
        low_o[rows, :] = low
        if layer == 0:
            swap_o[rows, :] = pick(first, one_low[rows, :], low)
        else:
            grad_o[rows, :] = grad
            dots = jnp.sum(low.astype(F32) * mixed[rows, :], axis=1, keepdims=True)
            row = jnp.transpose(jnp.broadcast_to(dots, (HALF, 128)))[0:1, :]
            high, rest = split_low(row)
            tops.append(high)
            lows.append(rest)
    if layer == 1:
        fill = [jnp.zeros((8 - sz.blocks, HALF), F32)] if sz.blocks < 8 else []
        extra = jnp.concatenate(tops + fill + lows + fill, axis=0)
        extra = jnp.concatenate([extra] * (sz.chunk // HALF), axis=1)
        low_o[sz.rows :, :] = extra.astype(LOW)
    else:
        size = shared_o.shape[0]
        at = sz.rows + PAD
        zero = total_of(parts, slice(at, at + size))
        one = total_of(parts, slice(at + size, at + 2 * size))
        zero, one = (jnp.concatenate([resplit(v[:PAD]), v[PAD:]], axis=0) for v in (zero, one))
        shared_o[...] = pick(first, zero, one)
        swap_o[sz.rows :, :] = pick(first, one, zero).astype(LOW)


def sum_kernel(sz, sc, *refs):
    parts, out = refs[:-1], refs[-1]
    rows = out.shape[0] - PAD
    out[:rows, :] = total_of(parts, slice(0, rows)).astype(LOW)
    extra = total_of(parts, slice(rows, rows + PAD))
    high, low = split_low(extra[0:4, :] + extra[4:8, :])
    extra = jnp.concatenate([high, low, jnp.zeros((PAD - 8, extra.shape[1]), F32)], axis=0)
    out[rows:, :] = extra.astype(LOW)


def final_kernel(sz, sc, zero, one, got, *refs):
    pieces, refs = refs[:-8], refs[-8:]
    gate_o, inner_o, out_o, conv_o, norm_o, skip_o, shared_o, common_o = refs
    c = sc[0]
    ch = sz.channels
    rows = zero.shape[0] - PAD
    lane = lax.broadcasted_iota(jnp.int32, skip_o.shape, 1)
    skip = jnp.zeros(skip_o.shape, F32)
    for i in range(2):
        which = pick(i == 0, c, 1 - c)
        to = aligned(which * ch, ch)
        sums = (pick(c == 0, zero[...], one[...]) if i == 0 else got[...]).astype(F32)
        gate_o[:, to] = sums[:rows, :ch]
        inner_o[:, to] = sums[:rows, ch : 2 * ch]
        out_o[to, :] = jnp.transpose(sums[:rows, 2 * ch :])
        lines = sums[rows : rows + 4, :] + sums[rows + 4 : rows + 8, :]
        for j in range(sz.taps):
            conv_o[j : j + 1, to] = lines[j // 3 : j // 3 + 1, (j % 3) * ch : (j % 3 + 1) * ch]
        norm_o[:, to] = lines[1:2, ch : 2 * ch]
        skips = lines[1:2, 2 * ch :]
        for q in range(sz.heads):
            part = jnp.sum(per_head(skips, q, sz.head_width), axis=1, keepdims=True)
            skip = jnp.where(lane == which * sz.heads + q, part, skip)
    skip_o[...] = skip
    total = total_of(pieces, slice(BLOCK, None))
    shared_o[...] = total[PAD:]
    common_o[...] = total[: PAD // 2] + total[PAD // 2 : PAD]


def slice_kernel(sz, slots, with_rates, deps, sc, order, *refs):
    sources = 2 if with_rates else 1
    src, refs = refs[:sources], refs[sources + deps :]
    outs, sc_o, refs = refs[:slots], refs[slots], refs[slots + 1 :]
    sems = refs[-1]
    copies = []
    for r in range(slots):
        which = order[lax.rem(sc[3] + r, slots)]
        rows = src[0].at[which, aligned(sc[0] * HALF, HALF), :]
        to = outs[r].at[:HALF] if with_rates else outs[r]
        copies.append(pltpu.make_async_copy(rows, to, sems.at[r]))
    for copy in copies:
        copy.start()
    for i in range(4):
        sc_o[i] = sc[i]
    if with_rates:
        thirds = refs[0]
        for r in range(slots):
            which = order[lax.rem(sc[3] + r, slots)]
            first, rest = split_low(src[1][0, which])
            second, rest = split_low(rest)
            lines = jnp.concatenate([first, second, rest, jnp.zeros_like(rest)], axis=1)
            lines = jnp.concatenate([lines, jnp.zeros_like(lines)], axis=0)
            thirds[r] = lines.astype(LOW)
        more = [
            pltpu.make_async_copy(thirds.at[r], outs[r].at[HALF:], sems.at[slots + r])
            for r in range(slots)
        ]
        for copy in more:
            copy.start()
        copies = copies + more
    for copy in copies:
        copy.wait()


def rates_of(piece):
    lines = piece[HALF:, :].astype(F32)[:8, :]
    return (lines[:, :BLOCK] + lines[:, BLOCK : 2 * BLOCK]) + lines[:, 2 * BLOCK : 3 * BLOCK]


def pack_kernel(sz, sc, gate, inner, shared, out, in_gain, conv_i, conv_s, skip, norm, *refs):
    w_o, o_o, mine_o, send_o, sems = refs
    c, h = sc[0], sc[1]
    ch = sz.channels
    cols = aligned((1 - c) * ch, ch)
    rows = aligned((h * 2 + 1 - c) * ch, ch)
    copies = [
        pltpu.make_async_copy(gate.at[0, :, cols], w_o.at[:, :ch], sems.at[0]),
        pltpu.make_async_copy(inner.at[0, :, cols], w_o.at[:, ch : 2 * ch], sems.at[1]),
        pltpu.make_async_copy(shared.at[0], w_o.at[:, 2 * ch :], sems.at[2]),
        pltpu.make_async_copy(out.at[0, rows, :], o_o, sems.at[3]),
    ]
    for copy in copies:
        copy.start()
    for which, ref in ((c, mine_o), (1 - c, send_o)):
        at = aligned(which * ch, ch)
        ref[...] = jnp.zeros_like(ref)
        ref[0:1, :] = in_gain[...]
        ref[1 : 1 + sz.taps, :ch] = conv_i[0, :, at]
        ref[1 : 1 + sz.taps, ch : sz.lin] = conv_s[0]
        ref[5:6, :ch] = norm[:, at]
        low = spread(skip[...], 0, sz.heads, sz.head_width)
        high = spread(skip[...], sz.heads, sz.heads, sz.head_width)
        ref[6:7, :ch] = pick(which == 0, low, high)
    for copy in copies:
        copy.wait()


def decay_table(rate, c, n):
    lane = lax.broadcasted_iota(jnp.int32, rate.shape, 1)
    cum = rate
    step = 1
    while step < BLOCK:
        cum = cum + jnp.where(lane >= step, pltpu.roll(cum, step, 1), 0.0)
        step *= 2
    end = cum[:, BLOCK - 1 :]
    lines = [cum, jnp.exp(cum), jnp.exp(end - cum) * -rate, jnp.log(-rate) - cum]
    low = jnp.concatenate([v[:n] for v in lines], axis=0)
    high = jnp.concatenate([v[n:] for v in lines], axis=0)
    return pick(c == 0, low, high)


def leave_kernel(sz, slots, riders, sc, zero_own, zero_other, one_own, one_other, *refs):
    c = sc[0]
    if riders:
        shared, refs = refs[0], refs[1:]
        total = shared[...] + one_other[sz.rows :, :].astype(F32)
        extra = resplit(total[:PAD])
        part = (total.shape[0] - PAD) // riders
    outs = refs[:slots]
    for i in range(4):
        refs[slots][i] = sc[i]
    for r in range(slots):
        rows = aligned(lax.rem(sc[3] + r, slots) * HALF, HALF)
        own = pick(c == 0, zero_own[rows, :], one_own[rows, :])
        other = pick(c == 0, zero_other[rows, :], one_other[rows, :])
        put_pair(outs[r], c, own, other)
        if riders:
            lines = [extra, total[PAD + r * part : PAD + (r + 1) * part]]
            outs[r][BLOCK:, :] = jnp.concatenate(lines, axis=0).astype(LOW)


def home_kernel(slots, sc, *refs):
    early, late, out, grad = refs[:slots], refs[slots : 2 * slots], refs[-3], refs[-2]
    for i in range(4):
        refs[-1][i] = sc[i]
    first = sc[0] == 0
    for r in range(slots):
        at = lax.rem(sc[3] - r + slots, slots)
        out[at] = pick(first, early[r][...], late[r][:BLOCK, :]).astype(F32)
        grad[at] = pick(first, late[r][:BLOCK, :], early[r][...]).astype(F32)


def whole(shape):
    return pl.BlockSpec(shape, lambda *_: (0,) * len(shape))


def per_device(
    tokens,
    slot_order,
    log_decay,
    grad_out,
    in_gain,
    w_gate,
    w_inner,
    w_shared,
    conv_inner,
    conv_shared,
    d_skip,
    norm_gain,
    w_out,
):
    slots = tokens.shape[0]
    span = tokens.shape[1]
    width = tokens.shape[2]
    seq = lax.axis_size("seq")
    head_axis = lax.axis_size("head")
    cores = lax.axis_size("section")
    spans = seq // slots
    c = lax.axis_index("section")
    z = lax.axis_index("seq")
    h = lax.axis_index("head")
    k = lax.rem(z, slots)
    inner_dev = w_gate.shape[2]
    channels = inner_dev // cores
    shared = w_shared.shape[2]
    heads_dev = d_skip.shape[1]
    taps = conv_inner.shape[1]
    sz = Sizes(
        slots * span // BLOCK,
        width,
        channels,
        heads_dev // cores,
        shared // 2,
        taps,
        head_axis,
        inner_dev * head_axis,
    )
    first = c == 0
    swap = [(0, 1), (1, 0)]
    nb, tok, rows, chunk = sz.blocks, sz.tokens, sz.rows, sz.chunk

    def cross(x):
        return lax.ppermute(x, "section", swap)

    def turn(x, r):
        pairs = [(i, i // slots * slots + (i % slots + r) % slots) for i in range(seq)]
        return lax.ppermute(x, "seq", pairs) if r else x

    def over_heads(x, d):
        return lax.ppermute(x, "head", [(i, i ^ d) for i in range(head_axis)])

    def next_span(x, way):
        pairs = [(i, i + way * slots) for i in range(seq) if 0 <= i + way * slots < seq]
        return lax.ppermute(x, "seq", pairs)

    def shape(dims, dtype):
        return jax.ShapeDtypeStruct(dims, dtype)

    prefetch = functools.partial(pltpu.PrefetchScalarGridSpec, num_scalar_prefetch=1)
    options = pltpu.CompilerParams(vmem_limit_bytes=VMEM_BYTES)
    anywhere = pl.BlockSpec(memory_space=pl.ANY)
    smem = pl.BlockSpec(memory_space=pltpu.SMEM)
    vmem = pl.BlockSpec(memory_space=pltpu.VMEM)
    index_shape = shape((4,), jnp.int32)

    def cost(flops, moved):
        return pl.CostEstimate(flops=int(flops), bytes_accessed=int(moved), transcendentals=0)

    def take_rows(sc, source, rates, deps=()):
        given = [source] if rates is None else [source, rates]
        more = 0 if rates is None else PAD
        got = pl.pallas_call(
            functools.partial(slice_kernel, sz, slots, rates is not None, len(deps)),
            in_specs=[smem, smem, anywhere]
            + ([] if rates is None else [vmem])
            + [anywhere] * len(deps),
            out_specs=[anywhere] * slots + [smem],
            out_shape=[shape((HALF + more, width), LOW)] * slots + [index_shape],
            scratch_shapes=([pltpu.VMEM((slots, PAD, width), LOW)] if more else [])
            + [pltpu.SemaphoreType.DMA((2 * slots,))],
            compiler_params=options,
        )(sc, slot_order, *given, *deps)
        return got[:slots], got[slots]

    def to_members(pieces):
        return [turn(x, r) for r, x in enumerate(pieces)]

    sc = jnp.stack([c, h, z, k]).astype(jnp.int32)
    tok_slices, sc = take_rows(sc, tokens, log_decay)
    tok_pieces = to_members(tok_slices)
    tok_others = [cross(x) for x in tok_pieces]

    wide = 2 * channels + shared
    w_sent, o_sent, pv_mine, pv_sent = pl.pallas_call(
        functools.partial(pack_kernel, sz),
        in_specs=[smem] + [anywhere] * 4 + [vmem] * 5,
        out_specs=[anywhere, anywhere, vmem, vmem],
        out_shape=[
            shape((width, wide), LOW),
            shape((channels, width), LOW),
            shape((16, width), F32),
            shape((16, width), F32),
        ],
        scratch_shapes=[pltpu.SemaphoreType.DMA((4,))],
        compiler_params=options,
    )(sc, w_gate, w_inner, w_shared, w_out, in_gain, conv_inner, conv_shared, d_skip, norm_gain)
    raw = [w_gate, w_inner, w_shared, w_out]
    sent = [cross(w_sent), cross(o_sent)]
    gains = [pv_mine, cross(pv_sent)]

    def span_total(table):
        ends = table[: sz.heads, BLOCK - 1 :: BLOCK]
        return jnp.repeat(jnp.exp(jnp.sum(ends, axis=1)), sz.head_width)[:, None]

    parts_shape = shape((head_axis, rows + PAD, chunk), LOW)
    weight_specs = [anywhere] * 6
    wide_weights = pltpu.VMEM((width, wide), LOW)
    out_weights = pltpu.VMEM((channels, width), LOW)
    copy_sems = pltpu.SemaphoreType.DMA((4,))
    dense = 2 * tok * width * (wide + channels)

    def forward(layer, sc, sources):
        def at(b, _):
            return (b, 0)

        piece = pl.BlockSpec((HALF, chunk), at)
        table = pl.BlockSpec((16, BLOCK), lambda b, _: (0, b))
        if layer == 0:
            src_specs = [whole((HALF + PAD, width))] * (2 * slots)
            more_specs = [table, table]
            more_shapes = [shape((16, tok), F32)] * 2
        else:
            src_specs = [piece] * (2 * head_axis) + [whole((HALF, width))] * (2 * slots) + [table]
            more_specs = [pl.BlockSpec((BLOCK, width), at)]
            more_shapes = [shape((tok, width), LOW)]

        def call(halo, begin):
            return pl.pallas_call(
                functools.partial(forward_kernel, sz, layer, slots),
                grid_spec=prefetch(
                    grid=(nb,),
                    in_specs=src_specs
                    + [whole((16, width)), whole((16, width))]
                    + weight_specs
                    + [whole((8, sz.lin)), whole((channels, sz.states))],
                    out_specs=[
                        pl.BlockSpec((BLOCK, width), at),
                        pl.BlockSpec((BLOCK, channels), at),
                        pl.BlockSpec((BLOCK, sz.lin), at),
                        pl.BlockSpec((BLOCK, channels), at),
                        pl.BlockSpec((1, channels, sz.states), lambda b, _: (b, 0, 0)),
                        pl.BlockSpec((1, BLOCK), lambda b, _: (0, b)),
                        pl.BlockSpec((2, BLOCK), lambda b, _: (0, b)),
                        pl.BlockSpec((BLOCK, channels), at),
                        whole((channels, sz.states)),
                        smem,
                        piece,
                    ]
                    + more_specs,
                    scratch_shapes=[
                        pltpu.VMEM((BLOCK, width), LOW),
                        pltpu.VMEM((BLOCK, width), LOW),
                        wide_weights,
                        out_weights,
                        pltpu.VMEM((BLOCK + 8, sz.lin), F32),
                        pltpu.VMEM((channels, sz.states), F32),
                        copy_sems,
                    ],
                ),
                out_shape=[
                    shape((tok, width), LOW),
                    shape((tok, channels), F32),
                    shape((tok, sz.lin), LOW),
                    shape((tok, channels), F32),
                    shape((nb, channels, sz.states), LOW),
                    shape((1, tok), F32),
                    shape((2, tok), F32),
                    shape((tok, channels), LOW),
                    shape((channels, sz.states), F32),
                    index_shape,
                    shape((rows, chunk), LOW),
                ]
                + more_shapes,
                compiler_params=options,
                cost_estimate=cost(6 * dense, 16e6),
            )(sc, *sources, *gains, *raw, *sent, halo, begin)

        halo = jnp.zeros((8, sz.lin), F32)
        begin = jnp.zeros((channels, sz.states), F32)
        if spans == 1:
            return call(halo, begin), halo
        trial = call(halo, begin)
        halo = next_span(trial[2][tok - 8 :].astype(F32), 1)
        local = call(halo, begin)[8]
        total = span_total(trial[11] if layer == 0 else sources[-1])
        for _ in range(spans - 1):
            begin = next_span(total * begin + local, 1)
        return call(halo, begin), halo

    def backward(layer, sc, sources, saved, decays, halo, deps):
        def at(i, _):
            return (nb - 1 - i, 0)

        if layer == 0:
            src_specs = [whole(s.shape) for s in sources]
        else:
            stat = pl.BlockSpec((2, BLOCK), lambda i, _: (0, nb - 1 - i))
            src_specs = [pl.BlockSpec((BLOCK, width), at)] + [stat] * head_axis
        gl, lin, ssd, inc = saved
        mixed_spec = [pl.BlockSpec((BLOCK, width), at)] if layer == 0 else []
        mixed_shape = [shape((tok, width), LOW)] if layer == 0 else []

        def call(halo_grad, begin):
            return pl.pallas_call(
                functools.partial(backward_kernel, sz, layer, len(deps)),
                grid_spec=prefetch(
                    grid=(nb,),
                    in_specs=src_specs
                    + [
                        pl.BlockSpec((BLOCK, channels), at),
                        whole(lin.shape),
                        pl.BlockSpec((BLOCK, channels), at),
                        pl.BlockSpec((1, channels, sz.states), lambda i, _: (nb - 1 - i, 0, 0)),
                        pl.BlockSpec((16, BLOCK), lambda i, _: (0, nb - 1 - i)),
                        whole((16, width)),
                        whole((16, width)),
                        *weight_specs,
                        whole((8, sz.lin)),
                        whole((8, sz.lin)),
                        whole((channels, sz.states)),
                    ]
                    + [anywhere] * len(deps),
                    out_specs=[
                        pl.BlockSpec((BLOCK, wide), at),
                        pl.BlockSpec((BLOCK, channels), at),
                        whole((PAD, 3 * channels)),
                        whole((8, sz.lin)),
                        whole((channels, sz.states)),
                        whole((8, sz.lin)),
                        smem,
                    ]
                    + mixed_spec,
                    scratch_shapes=[
                        pltpu.VMEM((BLOCK, width), LOW),
                        out_weights,
                        pltpu.VMEM((BLOCK + 8, sz.lin), F32),
                        pltpu.VMEM((BLOCK + 8, sz.lin), F32),
                        pltpu.VMEM((channels, sz.states), F32),
                        pltpu.VMEM((PAD, HALF), F32),
                        pltpu.VMEM((8, sz.lin), F32),
                        copy_sems,
                    ],
                ),
                out_shape=[
                    shape((tok, wide), LOW),
                    shape((tok, channels), LOW),
                    shape((PAD, 3 * channels), LOW),
                    shape((8, sz.lin), F32),
                    shape((channels, sz.states), F32),
                    shape((8, sz.lin), F32),
                    index_shape,
                ]
                + mixed_shape,
                compiler_params=options,
                cost_estimate=cost(8 * dense, 16e6),
            )(
                sc, *sources, gl, lin, ssd, inc, decays, *gains, *raw, *sent,
                halo, halo_grad, begin, *deps,
            )

        halo_grad = jnp.zeros((8, sz.lin), F32)
        begin = jnp.zeros((channels, sz.states), F32)
        if spans == 1:
            return call(halo_grad, begin)
        local = call(halo_grad, begin)[4]
        for _ in range(spans - 1):
            begin = next_span(span_total(decays) * begin + local, -1)
        halo_grad = next_span(call(halo_grad, begin)[5], -1)
        return call(halo_grad, begin)

    def project(layer, sc, unit, stats, deps):
        return pl.pallas_call(
            functools.partial(project_kernel, sz, layer, len(deps)),
            in_specs=[smem, vmem, vmem] + weight_specs + [anywhere] * len(deps),
            out_specs=[vmem, vmem, smem],
            out_shape=[parts_shape, parts_shape, index_shape],
            scratch_shapes=[out_weights, copy_sems],
            compiler_params=options,
            cost_estimate=cost(dense / 4, 4e6),
        )(sc, unit, stats, *raw, *sent, *deps)

    def lift(layer, sc, cat, normed, small, deps):
        return pl.pallas_call(
            functools.partial(lift_kernel, sz, layer, len(deps)),
            in_specs=[smem] + [vmem] * 5 + weight_specs + [anywhere] * len(deps),
            out_specs=[vmem, vmem, smem, vmem],
            out_shape=[parts_shape, parts_shape, index_shape, shape((PAD, chunk), LOW)],
            scratch_shapes=[pltpu.VMEM((8, width), F32), wide_weights, copy_sems],
            compiler_params=options,
            cost_estimate=cost(dense, 8e6),
        )(sc, cat, normed, *gains, small, *raw, *sent, *deps)

    def scatter(sc, keep, send, *riders):
        size = rows + PAD + sum(rider[0].shape[0] for rider in riders)
        flat = [x for rider in riders for x in rider]
        joined = pl.pallas_call(
            functools.partial(join_kernel, sz, len(riders)),
            in_specs=[smem] + [vmem] * (2 + len(flat)),
            out_specs=[smem] + [vmem] * head_axis,
            out_shape=[index_shape, shape((size, chunk), F32)]
            + [shape((size, chunk), LOW)] * (head_axis - 1),
            compiler_params=options,
        )(sc, keep, cross(send), *flat)
        return [joined[1]] + [over_heads(joined[1 + d], d) for d in range(1, head_axis)], joined[0]

    def gather(low):
        own = [low] + [over_heads(low, d) for d in range(1, head_axis)]
        return own + [cross(x) for x in own]

    def section_output(layer, sc, parts, resid):
        return pl.pallas_call(
            functools.partial(output_kernel, sz, layer),
            in_specs=[smem] + [vmem] * (head_axis + 1),
            out_specs=[vmem] * 4 + [smem],
            out_shape=[
                shape((rows, chunk), F32),
                shape((rows, chunk), LOW),
                shape((rows, chunk), F32),
                shape((8, HALF), F32),
                index_shape,
            ],
            compiler_params=options,
        )(sc, *parts, resid)

    part = width // seq
    columns = 3 * channels
    share = part // head_axis
    shared_size = seq * share + PAD

    def section_input(layer, sc, parts, *others, deps=()):
        if layer == 0:
            outs = [
                shape((rows + PAD, chunk), LOW),
                shape((rows + shared_size, chunk), LOW),
                shape((shared_size, chunk), F32),
            ]
        else:
            outs = [shape((rows, chunk), F32), shape((rows + PAD, chunk), LOW)]
        return pl.pallas_call(
            functools.partial(input_kernel, sz, layer),
            in_specs=[smem] + [vmem] * (head_axis + len(others)) + [anywhere] * len(deps),
            out_specs=[vmem] * len(outs) + [smem],
            out_shape=outs + [index_shape],
            compiler_params=options,
        )(sc, *parts, *others, *deps)

    def weight_grads(sc, normed, cat, mixed, scaled, small, common):
        outs = pl.pallas_call(
            functools.partial(weights_kernel, sz, seq),
            in_specs=[smem] + [vmem] * 6,
            out_specs=[smem] + [vmem] * (seq + head_axis),
            out_shape=[index_shape]
            + [shape((part + PAD, columns), LOW)] * seq
            + [shape((shared_size, shared), LOW)] * head_axis,
            scratch_shapes=[pltpu.VMEM((width, columns), LOW), pltpu.VMEM((width, shared), F32)],
            compiler_params=options,
            cost_estimate=cost(4 * dense, 12e6),
        )(sc, normed, cat, mixed, scaled, small, common)
        return over_seq(outs[1 : 1 + seq]), outs[1 + seq :], outs[0]

    def over_seq(chunks):
        pieces = [chunks[0]]
        for r in range(1, seq):
            pairs = [(i, (i + r) % seq) for i in range(seq)]
            pieces.append(lax.ppermute(chunks[r], "seq", pairs))
        return pieces

    def leave(sc, *arrays, riders=0):
        size = BLOCK + (share + PAD if riders else 0)
        pieces = pl.pallas_call(
            functools.partial(leave_kernel, sz, slots, riders),
            in_specs=[smem] + [vmem] * len(arrays),
            out_specs=[vmem] * slots + [smem],
            out_shape=[shape((size, chunk), LOW)] * slots + [index_shape],
            compiler_params=options,
        )(sc, *arrays)
        return to_members(pieces[:slots]), pieces[slots]

    out_slices, unused = take_rows(sc, grad_out, None, tok_pieces[1:])
    out_pieces = to_members(out_slices)
    fw0, halo0 = forward(0, sc, tok_pieces + tok_others)
    base0, decays = fw0[10], fw0[11:13]
    pr0 = project(0, fw0[9], fw0[7], fw0[6], [out_pieces[1], out_pieces[-1]])
    out_others = [cross(x) for x in out_pieces]
    parts, sc_join = scatter(sc, pr0[0], pr0[1])
    res1, low1, mixed0, square0, unused = section_output(0, sc, parts, base0)
    pieces1 = gather(low1)
    square_other = cross(square0)

    fw1, halo1 = forward(1, sc, pieces1 + out_pieces + out_others + [decays[1]])
    stat = fw1[6] + cross(fw1[6])
    stats = [stat] + [over_heads(stat, d) for d in range(1, head_axis)]
    pr1 = project(1, fw1[9], fw1[7], fw1[6], [])
    parts_out, sc_out = scatter(sc, pr1[0], pr1[1])
    bw1 = backward(1, sc_out, [fw1[11]] + stats, fw1[1:5], decays[1], halo1, [])
    lf1 = lift(1, bw1[6], bw1[0], fw1[0], bw1[3], parts_out[1:])
    weights1, heads1, sc_weights = weight_grads(
        lf1[2], fw1[0], bw1[0], fw1[11], bw1[1], bw1[2], lf1[3]
    )
    parts, sc_join = scatter(sc_weights, lf1[0], lf1[1])
    igrad1, glow1, sc_in = section_input(
        1, sc_join, parts, res1, fw1[10], fw1[5], *gains, mixed0, deps=weights1[1:2]
    )
    piecesg = gather(glow1)

    early, unused = leave(sc_in, low1, pieces1[head_axis], glow1, piecesg[head_axis])
    bw0 = backward(
        0, sc, piecesg + [square0, square_other], fw0[1:5], decays[0], halo0, weights1[-1:]
    )
    lf0 = lift(
        0, bw0[6], bw0[0], fw0[0], bw0[3], weights1[2:-1] + [early[1], early[-1]]
    )
    weights0, heads0, sc_weights = weight_grads(
        lf0[2], fw0[0], bw0[0], bw0[7], bw0[1], bw0[2], lf0[3]
    )
    parts, sc_join = scatter(sc_weights, lf0[0], lf0[1], heads0, heads1)

    unused, low2, unused_mixed, unused_square, sc_out = section_output(1, sc_in, parts_out, res1)
    glow0, to_other, shared_own, sc_end = section_input(
        0, sc_out, parts, base0, igrad1, fw0[5], *gains, low2,
        deps=weights0[1:-1] + early[2:-1],
    )
    got = cross(to_other)
    if spans == 1:
        late, sc_end = leave(sc_end, glow0, got, low2, got, shared_own, riders=seq)
        shared_parts = late
    else:
        late, sc_end = leave(sc_end, glow0, got, low2, got)
        total = shared_own + got[rows:].astype(F32)
        extra = resplit(total[:PAD])
        fill = jnp.zeros((BLOCK, shared), F32)
        chunks = [
            jnp.concatenate([fill, extra, total[PAD + r * share : PAD + (r + 1) * share]])
            for r in range(seq)
        ]
        shared_parts = over_seq([x.astype(LOW) for x in chunks])
    section_out, input_grad, sc_end = pl.pallas_call(
        functools.partial(home_kernel, slots),
        in_specs=[smem] + [vmem] * (2 * slots),
        out_specs=[vmem, vmem, smem],
        out_shape=[shape((slots, BLOCK, chunk), F32)] * 2 + [index_shape],
        compiler_params=options,
    )(sc, *early, *late)

    def summed(sc, pieces):
        return pl.pallas_call(
            functools.partial(sum_kernel, sz),
            in_specs=[smem] + [vmem] * seq,
            out_shape=shape((part + PAD, columns), LOW),
            compiler_params=options,
        )(sc, *pieces)

    sums0, sums1 = summed(sc_end, weights0), summed(sc_in, weights1)
    final = pl.pallas_call(
        functools.partial(final_kernel, sz),
        in_specs=[smem] + [vmem] * (3 + seq),
        out_shape=[
            shape((part, inner_dev), F32),
            shape((part, inner_dev), F32),
            shape((inner_dev, part), F32),
            shape((taps, inner_dev), F32),
            shape((1, inner_dev), F32),
            shape((1, heads_dev), F32),
            shape((share, shared), F32),
            shape((PAD // 2, shared), F32),
        ],
        compiler_params=options,
    )(sc, sums0, sums1, cross(pick(first, sums1, sums0)), *shared_parts)
    common = final[7]
    place = z * head_axis + h
    conv_part = shared // (seq * head_axis)
    gain_part = width // (seq * head_axis)
    return (
        section_out[None],
        input_grad[None],
        lax.dynamic_slice_in_dim(common[taps:].reshape(-1), place * gain_part, gain_part, 0)[None],
        final[0][None],
        final[1][None],
        final[6][None],
        final[3][None],
        lax.dynamic_slice_in_dim(common[:taps], place * conv_part, conv_part, 1)[None],
        final[5],
        final[4],
        final[2][None],
    )


def solution(mesh):
    placed = (
        P(None, "seq", None),
        P(),
        P("section", None, "head", "seq"),
        P(None, "seq", None),
        P("section", None),
        P("section", None, "head"),
        P("section", None, "head"),
        P("section", None, None),
        P("section", None, "head"),
        P("section", None, None),
        P("section", "head"),
        P("section", "head"),
        P("section", None, None),
    )
    return jax.shard_map(
        per_device,
        mesh=mesh,
        in_specs=placed,
        out_specs=(
            P("section", None, "seq", "head"),
            P("section", None, "seq", "head"),
            P("section", ("seq", "head")),
            P("section", "seq", "head"),
            P("section", "seq", "head"),
            P("section", ("seq", "head"), None),
            P("section", None, "head"),
            P("section", None, ("seq", "head")),
            P("section", "head"),
            P("section", "head"),
            P("section", "head", "seq"),
        ),
        check_vma=False,
    )
```

```python
import functools

import jax
import jax.numpy as jnp
from jax import lax
from jax.experimental import pallas as pl
from jax.experimental.pallas import tpu as pltpu
from jax.sharding import PartitionSpec as P

BLOCK = 256
HALF = BLOCK // 2
PAD = 16
EPS = 1e-05
F32 = jnp.float32
LOW = jnp.bfloat16
HIDDEN = -1e30
NN = ((1,), (0,))
NT = ((1,), (1,))
TN = ((0,), (0,))
VMEM_BYTES = 50 * 1024 * 1024


def dot(a, b, dims):
    return lax.dot_general(a, b, (dims, ((), ())), preferred_element_type=F32)


def aligned(start, size):
    return pl.ds(pl.multiple_of(start, size), size)


def spread(cols, first, count, width):
    rows = cols.shape[0]
    lane = lax.broadcasted_iota(jnp.int32, (rows, count * width), 1)
    out = jnp.broadcast_to(cols[:, first : first + 1], (rows, count * width))
    for h in range(1, count):
        out = jnp.where(lane >= h * width, cols[:, first + h : first + h + 1], out)
    return out


def per_head(array, h, width):
    lane = lax.broadcasted_iota(jnp.int32, array.shape, 1)
    inside = (lane >= h * width) & (lane < (h + 1) * width)
    return jnp.where(inside, array, jnp.zeros_like(array))


def split_low(value):
    high = value.astype(LOW).astype(F32)
    return high, value - high


def column_of(row, size):
    return jnp.transpose(jnp.broadcast_to(row, (128, size)))


def sigmoid(v):
    return 0.5 * jnp.tanh(0.5 * v) + 0.5


def pick(flag, a, b):
    return jnp.where(flag, a, b)


class Sizes:
    def __init__(self, blocks, width, channels, heads, states, taps, head_axis, inner):
        self.blocks = blocks
        self.width = width
        self.channels = channels
        self.heads = heads
        self.head_width = channels // heads
        self.states = states
        self.lin = channels + 2 * states
        self.taps = taps
        self.head_axis = head_axis
        self.chunk = width // head_axis
        self.rows = blocks * HALF
        self.tokens = blocks * BLOCK
        self.inner = inner


def weight_copies(sz, layer, c, h, raw, got, wv, ov, sems):
    gate, inner, shared, out = raw
    ch = sz.channels
    cols = aligned(c * ch, ch)
    rows = aligned((h * 2 + c) * ch, ch)
    own, sent = [], []
    if wv is not None:
        own += [
            (gate.at[0, :, cols], wv.at[:, :ch]),
            (inner.at[0, :, cols], wv.at[:, ch : 2 * ch]),
            (shared.at[0], wv.at[:, 2 * ch :]),
        ]
        sent += [(got[0], wv)]
    if ov is not None:
        own += [(out.at[0, rows, :], ov)]
        sent += [(got[1], ov)]
    return [
        (c == layer, [pltpu.make_async_copy(p, q, sems.at[i]) for i, (p, q) in enumerate(own)]),
        (c != layer, [pltpu.make_async_copy(p, q, sems.at[i]) for i, (p, q) in enumerate(sent)]),
    ]


def run_copies(choices, start, wait):
    for flag, copies in choices:

        @pl.when(flag)
        def _(copies=copies):
            if start:
                for copy in copies:
                    copy.start()
            if wait:
                for copy in copies:
                    copy.wait()


def put_ordered(sz, dst, c, k, b, own, other):
    for r in range(len(own)):

        @pl.when(lax.rem(k - b + len(own), len(own)) == r)
        def _(r=r):
            put_pair(dst, c, own[r][:HALF, :], other[r][:HALF, :])


def put_pair(dst, c, own, other):
    dst[aligned(c * HALF, HALF), :] = own
    dst[aligned((1 - c) * HALF, HALF), :] = other


def put_pieces(sz, dst, c, h, own, other):
    for d in range(sz.head_axis):
        cols = aligned((h ^ d) * sz.chunk, sz.chunk)
        dst[aligned(c * HALF, HALF), cols] = own[d]
        dst[aligned((1 - c) * HALF, HALF), cols] = other[d]


def line_of(table, at):
    line = lax.broadcasted_iota(jnp.int32, table.shape, 0)
    return jnp.sum(jnp.where(line == at, table, 0.0), axis=0, keepdims=True)


def conv_forward(sz, ext, taps):
    pre = taps[0:1] * ext[5 : 5 + BLOCK, :]
    for j in range(1, sz.taps):
        pre = pre + taps[j : j + 1] * ext[5 + j : 5 + j + BLOCK, :]
    return pre


def decay_of(sz, cols, rp, h, mask):
    rows = cols[:, h : h + 1] + rp[12 + h : 13 + h, :]
    return jnp.exp(jnp.where(mask, rows, HIDDEN))


def lower_mask():
    t = lax.broadcasted_iota(jnp.int32, (BLOCK, BLOCK), 0)
    s = lax.broadcasted_iota(jnp.int32, (BLOCK, BLOCK), 1)
    return t >= s


def forward_kernel(sz, layer, slots, sc, *refs):
    n = sz.head_axis
    sources = 2 * slots if layer == 0 else 2 * n + 2 * slots
    src, refs = refs[:sources], refs[sources:]
    if layer == 1:
        table, refs = refs[0], refs[1:]
    gains, raw, got, halo, begin = refs[0:2], refs[2:6], refs[6:8], refs[8], refs[9]
    normed_o, gl_o, lin_o, ssd_o, inc_o, inv_o, part_o, unit_o, fin_o, sc_o, base_o = refs[10:21]
    act_o, slope_o, decay_o, mix_o = refs[21:25]
    refs = refs[25:]
    if layer == 1:
        mixed_o, refs = refs[0], refs[1:]
    else:
        tables_o, refs = refs[0:2], refs[2:]
    xs, ms, wv, ov, ext, state, sems = refs
    b = pl.program_id(0)
    c, h, k = sc[0], sc[1], sc[3]
    ch, st = sz.channels, sz.states
    copies = weight_copies(sz, layer, c, h, raw, got, wv, ov if layer == 1 else None, sems)

    @pl.when(b == 0)
    def _():
        run_copies(copies, True, False)
        ext[0:8, :] = halo[...]
        state[...] = begin[...]
        for i in range(4):
            sc_o[i] = sc[i]

    mine = aligned(c * HALF, HALF)
    cols = aligned(h * sz.chunk, sz.chunk)
    if layer == 0:
        put_ordered(sz, xs, c, k, b, src[:slots], src[slots:])
        base_o[...] = xs[mine, cols]
        for r in range(slots):

            @pl.when(lax.rem(k - b + slots, slots) == r)
            def _(r=r):
                own = decay_table(rates_of(src[r]), c, sz.heads)
                other = decay_table(rates_of(src[slots + r]), c, sz.heads)
                tables_o[0][...] = pick(c == 0, own, other)
                tables_o[1][...] = pick(c == 0, other, own)

        rp = tables_o[0][...]
    else:
        put_pieces(sz, xs, c, h, [r[...] for r in src[:n]], [r[...] for r in src[n : 2 * n]])
        put_ordered(sz, ms, c, k, b, src[2 * n : 2 * n + slots], src[2 * n + slots :])
        base_o[...] = ms[mine, cols]
        mixed_o[...] = ms[...]
        rp = table[...]

    pv = pick(c == layer, gains[0][...], gains[1][...])
    x = xs[...].astype(F32)
    inv_in = lax.rsqrt(jnp.mean(x * x, axis=1, keepdims=True) + EPS)
    normed = (x * inv_in * pv[0:1, : sz.width]).astype(LOW)
    normed_o[...] = normed

    @pl.when(b == 0)
    def _():
        run_copies(copies, False, True)

    proj = dot(normed, wv[...], NN)
    gl = proj[:, :ch]
    gl_o[...] = gl
    lin = proj[:, ch:].astype(LOW)
    lin_o[...] = lin
    ext[8 : 8 + BLOCK, :] = lin.astype(F32)
    pre = conv_forward(sz, ext, pv[1:5, : sz.lin])
    ext[0:8, :] = ext[BLOCK : BLOCK + 8, :]
    sig = sigmoid(pre)
    act = (pre * sig).astype(LOW)
    act_o[...] = act
    slope_o[...] = (sig * (1.0 + pre * (1.0 - sig))).astype(LOW)
    values, bm, cm = act[:, :ch], act[:, ch : ch + st], act[:, ch + st :]

    cols = jnp.transpose(rp)
    mask = lower_mask()
    gram = dot(cm, bm, NT)
    mixes, parts = [], []
    for i in range(sz.heads):
        decay = decay_of(sz, cols, rp, i, mask)
        decay_o[i] = decay.astype(LOW)
        mixes.append((gram * decay).astype(LOW))
        mix_o[i] = mixes[-1]
        parts.append(per_head(values, i, sz.head_width))
    intra = dot(jnp.concatenate(mixes, axis=1), jnp.concatenate(parts, axis=0), NN)

    low_state = state[...].astype(LOW)
    inc_o[0] = low_state
    ecum = spread(cols, sz.heads, sz.heads, sz.head_width)
    inter = dot(cm, low_state, NT) * ecum
    vf = values.astype(F32)
    carried = (vf * spread(cols, 2 * sz.heads, sz.heads, sz.head_width)).astype(LOW)
    local = dot(carried, bm, TN)
    for i in range(sz.heads):
        rows = slice(i * sz.head_width, (i + 1) * sz.head_width)
        total = cols[BLOCK - 1 : BLOCK, sz.heads + i : sz.heads + i + 1]
        state[rows, :] = total * state[rows, :] + local[rows]
    ssd = intra + inter + pv[6:7, :ch] * vf
    ssd_o[...] = ssd
    gated = ssd * (gl * sigmoid(gl))
    weighty = gated * pv[5:6, :ch]
    unit_o[...] = weighty.astype(LOW)

    lane = lax.broadcasted_iota(jnp.int32, (BLOCK, 128), 1)
    square = jnp.sum(gated * gated, axis=1, keepdims=True)
    if layer == 0:
        project = jnp.zeros_like(square)
    else:
        scaled_grad = dot(ms[...], ov[...], NT)
        project = jnp.sum(scaled_grad * weighty, axis=1, keepdims=True)
    stats = jnp.where(lane == 0, square, jnp.where(lane == 1, project, inv_in))
    stats = jnp.transpose(stats)
    part_o[...] = stats[0:2, :]
    inv_o[...] = stats[2:3, :]

    @pl.when(b == sz.blocks - 1)
    def _():
        fin_o[...] = state[...]


def scalar_lines(sz, lines):
    fill = [jnp.zeros((8 - sz.blocks, HALF), F32)] if sz.blocks < 8 else []
    high, low = split_low(jnp.concatenate(lines + fill, axis=0))
    table = jnp.concatenate([high, low], axis=0).astype(LOW)
    return jnp.concatenate([table] * (sz.chunk // HALF), axis=1)


def own_rows(sz, ref, which):
    blocks = [ref[aligned(b * BLOCK + which * HALF, HALF), :] for b in range(sz.blocks)]
    return jnp.concatenate(blocks, axis=0)


def project_kernel(sz, layer, deps, sc, unit_r, stats_r, *refs):
    raw, got, refs = refs[:4], refs[4:6], refs[6 + deps :]
    keep, send, sc_o, weights, sems = refs
    c, h = sc[0], sc[1]
    copies = weight_copies(sz, layer, c, h, raw, got, None, weights, sems)
    run_copies(copies, True, False)
    for i in range(4):
        sc_o[i] = sc[i]
    sides = []
    for which, out in ((c, keep), (1 - c, send)):
        sides.append((out, own_rows(sz, unit_r, which)))
        lines = [
            stats_r[0:1, aligned(b * BLOCK + which * HALF, HALF)] for b in range(sz.blocks)
        ]
        table = scalar_lines(sz, lines)
        for d in range(sz.head_axis):
            out[d, sz.rows :, :] = table
    run_copies(copies, False, True)
    for out, rows in sides:
        for d in range(sz.head_axis):
            chunk = weights[:, aligned((h ^ d) * sz.chunk, sz.chunk)]
            out[d, : sz.rows, :] = dot(rows, chunk, NN).astype(LOW)


def lift_kernel(sz, layer, deps, sc, cat_r, normed_r, zero_gains, one_gains, small_r, *refs):
    raw, got, refs = refs[:4], refs[4:6], refs[6 + deps :]
    keep, send, sc_o, common_o, wide, weights, sems = refs
    c, h = sc[0], sc[1]
    copies = weight_copies(sz, layer, c, h, raw, got, weights, None, sems)
    run_copies(copies, True, False)
    for i in range(4):
        sc_o[i] = sc[i]
    wide[...] = jnp.zeros_like(wide)
    run_copies(copies, False, True)
    for which, out in ((c, keep), (1 - c, send)):
        rows = own_rows(sz, cat_r, which)
        along = jnp.zeros((sz.rows, 1), F32)
        for d in range(sz.head_axis):
            cols = aligned((h ^ d) * sz.chunk, sz.chunk)
            product = dot(rows, weights[cols, :], NT)
            out[d, : sz.rows, :] = product.astype(LOW)
            blocks = [
                normed_r[aligned(b * BLOCK + which * HALF, HALF), cols] for b in range(sz.blocks)
            ]
            product = product * jnp.concatenate(blocks, axis=0).astype(F32)
            wide[0:1, cols] += jnp.sum(product, axis=0, keepdims=True)
            along = along + jnp.sum(product, axis=1, keepdims=True)
        lines = [
            jnp.transpose(jnp.broadcast_to(along[b * HALF : (b + 1) * HALF], (HALF, 128)))[0:1, :]
            for b in range(sz.blocks)
        ]
        table = scalar_lines(sz, lines)
        for d in range(sz.head_axis):
            out[d, sz.rows :, :] = table
    gain_grad = wide[0:1, :] / pick(c == layer, zero_gains[0:1, :], one_gains[0:1, :])
    flat = [small_r[j : j + 1, sz.channels :] for j in range(sz.taps)]
    flat += [gain_grad[:, q * sz.chunk : (q + 1) * sz.chunk] for q in range(sz.head_axis)]
    high, low = split_low(jnp.concatenate(flat, axis=0))
    common_o[...] = jnp.concatenate([high, low], axis=0).astype(LOW)


def backward_kernel(sz, layer, deps, sc, *refs):
    n = sz.head_axis
    sources = 2 * n + 2 if layer == 0 else 1 + n
    src, refs = refs[:sources], refs[sources:]
    gl_r, lin_r, ssd_r, inc_r, act_r, slope_r, decay_r, mix_r = refs[:8]
    refs = refs[4:]
    table, gains, raw, got = refs[4], refs[5:7], refs[7:11], refs[11:13]
    halo, halo_grad, begin = refs[13:16]
    refs = refs[16 + deps :]
    cat_o, scaled_o, small_o, sums_o, fin_o, rim_o, sc_o = refs[:7]
    refs = refs[7:]
    if layer == 0:
        mixed_o, refs = refs[0], refs[1:]
    ms, ov, ext, back, state, heads_p, small, sems = refs
    i_step = pl.program_id(0)
    b = sz.blocks - 1 - i_step
    c, h = sc[0], sc[1]
    ch, st = sz.channels, sz.states
    copies = weight_copies(sz, layer, c, h, raw, got, None, ov, sems)
    pv = pick(c == layer, gains[0][...], gains[1][...])
    rp = table[...]

    @pl.when(i_step == 0)
    def _():
        run_copies(copies, True, True)
        back[BLOCK : BLOCK + 8, :] = halo_grad[...]
        state[...] = begin[...]
        small[...] = jnp.zeros_like(small)
        for i in range(4):
            sc_o[i] = sc[i]
        if layer == 0:
            for i in range(2):
                extra = src[i * n][sz.rows :, :].astype(F32)
                for d in range(1, n):
                    extra = extra + src[i * n + d][sz.rows :, :].astype(F32)
                heads_p[8 * i : 8 * i + 8, :] = extra[0:8, :HALF] + extra[8:16, :HALF]

    if layer == 0:
        rows = aligned(b * HALF, HALF)
        put_pieces(
            sz, ms, c, h, [r[rows, :] for r in src[:n]], [r[rows, :] for r in src[n : 2 * n]]
        )
        halves = []
        for k in range(2):
            alpha = lax.rsqrt(line_of(src[2 * n + k][...], b) / sz.inner + EPS)
            beta = alpha * alpha * line_of(heads_p[...], 8 * k + b) / sz.inner
            halves.append((alpha, beta))
        alpha, beta = (
            pick(
                c == 0,
                jnp.concatenate([halves[0][q], halves[1][q]], axis=1),
                jnp.concatenate([halves[1][q], halves[0][q]], axis=1),
            )
            for q in range(2)
        )
    else:
        stats = src[1][...]
        for d in range(1, n):
            stats = stats + src[1 + d][...]
        alpha = lax.rsqrt(stats[0:1, :] / sz.inner + EPS)
        beta = alpha * alpha * alpha * stats[1:2, :] / sz.inner

    sub = lax.broadcasted_iota(jnp.int32, rp.shape, 0)
    cols = jnp.transpose(jnp.where(sub == 12, alpha, jnp.where(sub == 13, beta, rp)))
    alpha, beta = cols[:, 12:13], cols[:, 13:14]

    gl = gl_r[...]
    ssd = ssd_r[...]
    sig = sigmoid(gl)
    swish = gl * sig
    slope = sig * (1.0 + gl * (1.0 - sig))
    gated = ssd * swish
    if layer == 0:
        mixed_grad = ms[...]
        mixed_o[...] = mixed_grad
    else:
        mixed_grad = src[0][...]
    scaled_grad = dot(mixed_grad, ov[...], NT)
    gain = pv[5:6, :ch]
    normal = gated * alpha
    small[4:5, :ch] += jnp.sum(scaled_grad * normal, axis=0, keepdims=True)
    scaled_o[...] = (normal * gain).astype(LOW)
    gated_grad = alpha * (scaled_grad * gain) - beta * gated
    ssd_grad = (gated_grad * swish).astype(LOW)
    gate_grad = (gated_grad * ssd * slope).astype(LOW)
    sgf = ssd_grad.astype(F32)

    before = lin_r[pl.ds(pl.multiple_of(jnp.maximum(b * BLOCK - 16, 0), 16), 16), :]
    ext[0:8, :] = pick(b > 0, before.astype(F32)[8:16, :], halo[...])
    ext[8 : 8 + BLOCK, :] = lin_r[aligned(b * BLOCK, BLOCK), :].astype(F32)
    taps = pv[1:5, : sz.lin]
    act = act_r[...]
    values, bm, cm = act[:, :ch], act[:, ch : ch + st], act[:, ch + st :]
    vf = values.astype(F32)
    small[5:6, :ch] += jnp.sum(sgf * vf, axis=0, keepdims=True)

    gram_grad = jnp.zeros((BLOCK, BLOCK), F32)
    mixes, parts = [], []
    for i in range(sz.heads):
        mixes.append(mix_r[i])
        parts.append(per_head(ssd_grad, i, sz.head_width))
        gram_grad = gram_grad + dot(parts[-1], values, NT) * decay_r[i].astype(F32)
    intra_grad = dot(jnp.concatenate(mixes, axis=0), jnp.concatenate(parts, axis=0), TN)

    ecum = spread(cols, sz.heads, sz.heads, sz.head_width)
    to_end = spread(cols, 2 * sz.heads, sz.heads, sz.head_width)
    inter_grad = (sgf * ecum).astype(LOW)
    low_state = state[...].astype(LOW)
    carried = (vf * to_end).astype(LOW)
    carried_grad = dot(bm, low_state, NT)
    gram_low = gram_grad.astype(LOW)
    b_grad = dot(gram_low, cm, TN) + dot(carried, low_state, NN)
    c_grad = dot(gram_low, bm, NN) + dot(inter_grad, inc_r[0], NN)
    value_grad = intra_grad + pv[6:7, :ch] * sgf + carried_grad * to_end
    entry = dot(inter_grad, cm, TN)
    for i in range(sz.heads):
        rows = slice(i * sz.head_width, (i + 1) * sz.head_width)
        total = cols[BLOCK - 1 : BLOCK, sz.heads + i : sz.heads + i + 1]
        state[rows, :] = total * state[rows, :] + entry[rows]

    pre_grad = jnp.concatenate([value_grad, b_grad, c_grad], axis=1) * slope_r[...].astype(F32)
    back[0:BLOCK, :] = pre_grad
    lin_grad = taps[0:1] * back[sz.taps - 1 : sz.taps - 1 + BLOCK, :]
    for j in range(1, sz.taps):
        at = sz.taps - 1 - j
        lin_grad = lin_grad + taps[j : j + 1] * back[at : at + BLOCK, :]
    for j in range(sz.taps):
        small[j : j + 1, :] += jnp.sum(pre_grad * ext[5 + j : 5 + j + BLOCK, :], axis=0, keepdims=True)
    back[BLOCK : BLOCK + 8, :] = back[0:8, :]
    cat_o[...] = jnp.concatenate([gate_grad, lin_grad.astype(LOW)], axis=1)

    @pl.when(i_step == sz.blocks - 1)
    def _():
        fin_o[...] = state[...]
        rim_o[...] = back[0:8, :]
        sums = small[...]
        flat = [sums[j : j + 1, :ch] for j in range(sz.taps + 2)]
        flat = [jnp.concatenate(flat[j : j + 3], axis=1) for j in range(0, len(flat), 3)]
        flat = flat + [jnp.zeros_like(flat[0])] * (4 - len(flat))
        high, low = split_low(jnp.concatenate(flat, axis=0))
        rest = jnp.zeros((PAD - 8, high.shape[1]), F32)
        small_o[...] = jnp.concatenate([high, low, rest], axis=0).astype(LOW)
        sums_o[...] = sums


def weights_kernel(sz, seq, sc, normed, cat, mixed, scaled, small, common, *refs):
    sc_o, outs, heads, full, wide = refs[0], refs[1 : seq + 1], refs[seq + 1 : -2], refs[-2], refs[-1]
    for i in range(4):
        sc_o[i] = sc[i]
    ch, st = sz.channels, sz.states
    step = sz.chunk
    for q in range(sz.head_axis):
        at = slice(q * step, (q + 1) * step)
        grads = dot(normed[:, at], cat[...], TN)
        full[at, : 2 * ch] = grads[:, : 2 * ch].astype(LOW)
        wide[at, :] = grads[:, 2 * ch :]
        full[at, 2 * ch :] = dot(mixed[:, at], scaled[...], TN).astype(LOW)
    rows = sz.width // seq
    part = rows // sz.head_axis
    for r, out in enumerate(outs):
        out[:rows, :] = full[aligned(lax.rem(sc[2] + r, seq) * rows, rows), :]
        out[rows:, :] = small[...]
    for d, out in enumerate(heads):
        lines = [
            wide[aligned(lax.rem(sc[2] + r, seq) * rows + (sc[1] ^ d) * part, part), :]
            for r in range(seq)
        ]
        out[:PAD, :] = common[...]
        out[PAD:, :] = jnp.concatenate(lines, axis=0).astype(LOW)


def resplit(extra):
    half = extra.shape[0] // 2
    high, low = split_low(extra[:half, :] + extra[half:, :])
    return jnp.concatenate([high, low], axis=0)


def join_kernel(sz, riders, sc, keep, recv, *refs):
    n = sz.head_axis
    more, refs = [refs[i * n : (i + 1) * n] for i in range(riders)], refs[riders * n :]
    sc_o, outs = refs[0], refs[1:]
    rows = sz.rows
    for i in range(4):
        sc_o[i] = sc[i]
    extra = resplit(keep[0, rows:, :].astype(F32) + recv[0, rows:, :].astype(F32))
    for d, out in enumerate(outs):
        out[:rows, :] = (keep[d, :rows, :].astype(F32) + recv[d, :rows, :].astype(F32)).astype(out.dtype)
        out[rows : rows + PAD, :] = extra.astype(out.dtype)
        at = rows + PAD
        for rider in more:
            size = rider[d].shape[0]
            out[at : at + size, :] = rider[d][...].astype(out.dtype)
            at += size


def total_of(parts, rows):
    total = parts[0][rows, :].astype(F32)
    for p in parts[1:]:
        total = total + p[rows, :].astype(F32)
    return total


def output_kernel(sz, layer, sc, *refs):
    n = sz.head_axis
    parts, refs = refs[:n], refs[n:]
    resid, res_o, low_o, mixed_o, square_o, sc_o = refs
    for i in range(4):
        sc_o[i] = sc[i]
    extra = total_of(parts, slice(sz.rows, sz.rows + PAD))
    square = extra[0:8, :HALF] + extra[8:16, :HALF]
    square_o[...] = square
    inv = lax.rsqrt(square / sz.inner + EPS)
    for b in range(sz.blocks):
        rows = slice(b * HALF, (b + 1) * HALF)
        col = column_of(inv[b : b + 1, :], HALF)[:, 0:1]
        mixed = total_of(parts, rows) * col
        res = resid[rows, :].astype(F32) + mixed
        res_o[rows, :] = res
        low_o[rows, :] = res.astype(LOW)
        mixed_o[rows, :] = mixed


def input_kernel(sz, layer, sc, *refs):
    n = sz.head_axis
    parts, refs = refs[:n], refs[n:]
    resid, outg, inv_r, gains = refs[0], refs[1], refs[2], refs[3:5]
    refs = refs[5:]
    if layer == 1:
        mixed = refs[0]
        grad_o, low_o, sc_o = refs[-3:]
    else:
        one_low = refs[0]
        low_o, swap_o, shared_o, sc_o = refs[-4:]
    for i in range(4):
        sc_o[i] = sc[i]
    c, h = sc[0], sc[1]
    first = c == 0
    mine = aligned(h * sz.chunk, sz.chunk)
    gain = pick(c == layer, gains[0][0:1, mine], gains[1][0:1, mine])
    extra = total_of(parts, slice(sz.rows, sz.rows + PAD))
    along = extra[0:8, :HALF] + extra[8:16, :HALF]
    tops, lows = [], []
    for b in range(sz.blocks):
        rows = slice(b * HALF, (b + 1) * HALF)
        at = b * BLOCK
        inv_row = pick(c == 0, inv_r[:, at : at + HALF], inv_r[:, at + HALF : at + BLOCK])
        inv = column_of(inv_row, HALF)[:, 0:1]
        share = column_of(along[b : b + 1, :] / sz.width, HALF)[:, 0:1]
        total = total_of(parts, rows)
        base = resid[rows, :].astype(F32)
        grad = outg[rows, :].astype(F32) + inv * (total * gain - base * (inv * share))
        low = grad.astype(LOW)
        low_o[rows, :] = low
        if layer == 0:
            swap_o[rows, :] = pick(first, one_low[rows, :], low)
        else:
            grad_o[rows, :] = grad
            dots = jnp.sum(low.astype(F32) * mixed[rows, :], axis=1, keepdims=True)
            row = jnp.transpose(jnp.broadcast_to(dots, (HALF, 128)))[0:1, :]
            high, rest = split_low(row)
            tops.append(high)
            lows.append(rest)
    if layer == 1:
        fill = [jnp.zeros((8 - sz.blocks, HALF), F32)] if sz.blocks < 8 else []
        extra = jnp.concatenate(tops + fill + lows + fill, axis=0)
        extra = jnp.concatenate([extra] * (sz.chunk // HALF), axis=1)
        low_o[sz.rows :, :] = extra.astype(LOW)
    else:
        size = shared_o.shape[0]
        at = sz.rows + PAD
        zero = total_of(parts, slice(at, at + size))
        one = total_of(parts, slice(at + size, at + 2 * size))
        zero, one = (jnp.concatenate([resplit(v[:PAD]), v[PAD:]], axis=0) for v in (zero, one))
        shared_o[...] = pick(first, zero, one)
        swap_o[sz.rows :, :] = pick(first, one, zero).astype(LOW)


def sum_kernel(sz, sc, *refs):
    parts, out = refs[:-1], refs[-1]
    rows = out.shape[0] - PAD
    out[:rows, :] = total_of(parts, slice(0, rows)).astype(LOW)
    extra = total_of(parts, slice(rows, rows + PAD))
    high, low = split_low(extra[0:4, :] + extra[4:8, :])
    extra = jnp.concatenate([high, low, jnp.zeros((PAD - 8, extra.shape[1]), F32)], axis=0)
    out[rows:, :] = extra.astype(LOW)


def final_kernel(sz, sc, zero, one, got, *refs):
    pieces, refs = refs[:-8], refs[-8:]
    gate_o, inner_o, out_o, conv_o, norm_o, skip_o, shared_o, common_o = refs
    c = sc[0]
    ch = sz.channels
    rows = zero.shape[0] - PAD
    lane = lax.broadcasted_iota(jnp.int32, skip_o.shape, 1)
    skip = jnp.zeros(skip_o.shape, F32)
    for i in range(2):
        which = pick(i == 0, c, 1 - c)
        to = aligned(which * ch, ch)
        sums = (pick(c == 0, zero[...], one[...]) if i == 0 else got[...]).astype(F32)
        gate_o[:, to] = sums[:rows, :ch]
        inner_o[:, to] = sums[:rows, ch : 2 * ch]
        out_o[to, :] = jnp.transpose(sums[:rows, 2 * ch :])
        lines = sums[rows : rows + 4, :] + sums[rows + 4 : rows + 8, :]
        for j in range(sz.taps):
            conv_o[j : j + 1, to] = lines[j // 3 : j // 3 + 1, (j % 3) * ch : (j % 3 + 1) * ch]
        norm_o[:, to] = lines[1:2, ch : 2 * ch]
        skips = lines[1:2, 2 * ch :]
        for q in range(sz.heads):
            part = jnp.sum(per_head(skips, q, sz.head_width), axis=1, keepdims=True)
            skip = jnp.where(lane == which * sz.heads + q, part, skip)
    skip_o[...] = skip
    total = total_of(pieces, slice(BLOCK, None))
    shared_o[...] = total[PAD:]
    common_o[...] = total[: PAD // 2] + total[PAD // 2 : PAD]


def slice_kernel(sz, slots, with_rates, deps, sc, order, *refs):
    sources = 2 if with_rates else 1
    src, refs = refs[:sources], refs[sources + deps :]
    outs, sc_o, refs = refs[:slots], refs[slots], refs[slots + 1 :]
    sems = refs[-1]
    copies = []
    for r in range(slots):
        which = order[lax.rem(sc[3] + r, slots)]
        rows = src[0].at[which, aligned(sc[0] * HALF, HALF), :]
        to = outs[r].at[:HALF] if with_rates else outs[r]
        copies.append(pltpu.make_async_copy(rows, to, sems.at[r]))
    for copy in copies:
        copy.start()
    for i in range(4):
        sc_o[i] = sc[i]
    if with_rates:
        thirds, rates = refs[0], refs[1]
        loads = [
            pltpu.make_async_copy(
                src[1].at[0, order[lax.rem(sc[3] + r, slots)]], rates.at[r], sems.at[2 * slots + r]
            )
            for r in range(slots)
        ]
        for copy in loads:
            copy.start()
        for copy in loads:
            copy.wait()
        for r in range(slots):
            first, rest = split_low(rates[r])
            second, rest = split_low(rest)
            lines = jnp.concatenate([first, second, rest, jnp.zeros_like(rest)], axis=1)
            lines = jnp.concatenate([lines, jnp.zeros_like(lines)], axis=0)
            thirds[r] = lines.astype(LOW)
        more = [
            pltpu.make_async_copy(thirds.at[r], outs[r].at[HALF:], sems.at[slots + r])
            for r in range(slots)
        ]
        for copy in more:
            copy.start()
        copies = copies + more
    for copy in copies:
        copy.wait()


def rates_of(piece):
    lines = piece[HALF:, :].astype(F32)[:8, :]
    return (lines[:, :BLOCK] + lines[:, BLOCK : 2 * BLOCK]) + lines[:, 2 * BLOCK : 3 * BLOCK]


def pack_kernel(sz, sc, gate, inner, shared, out, in_gain, conv_i, conv_s, skip, norm, *refs):
    w_o, o_o, mine_o, send_o, sems = refs
    c, h = sc[0], sc[1]
    ch = sz.channels
    cols = aligned((1 - c) * ch, ch)
    rows = aligned((h * 2 + 1 - c) * ch, ch)
    copies = [
        pltpu.make_async_copy(gate.at[0, :, cols], w_o.at[:, :ch], sems.at[0]),
        pltpu.make_async_copy(inner.at[0, :, cols], w_o.at[:, ch : 2 * ch], sems.at[1]),
        pltpu.make_async_copy(shared.at[0], w_o.at[:, 2 * ch :], sems.at[2]),
        pltpu.make_async_copy(out.at[0, rows, :], o_o, sems.at[3]),
    ]
    for copy in copies:
        copy.start()
    for which, ref in ((c, mine_o), (1 - c, send_o)):
        at = aligned(which * ch, ch)
        ref[...] = jnp.zeros_like(ref)
        ref[0:1, :] = in_gain[...]
        ref[1 : 1 + sz.taps, :ch] = conv_i[0, :, at]
        ref[1 : 1 + sz.taps, ch : sz.lin] = conv_s[0]
        ref[5:6, :ch] = norm[:, at]
        low = spread(skip[...], 0, sz.heads, sz.head_width)
        high = spread(skip[...], sz.heads, sz.heads, sz.head_width)
        ref[6:7, :ch] = pick(which == 0, low, high)
    for copy in copies:
        copy.wait()


def decay_table(rate, c, n):
    lane = lax.broadcasted_iota(jnp.int32, rate.shape, 1)
    cum = rate
    step = 1
    while step < BLOCK:
        cum = cum + jnp.where(lane >= step, pltpu.roll(cum, step, 1), 0.0)
        step *= 2
    end = cum[:, BLOCK - 1 :]
    lines = [cum, jnp.exp(cum), jnp.exp(end - cum) * -rate, jnp.log(-rate) - cum]
    low = jnp.concatenate([v[:n] for v in lines], axis=0)
    high = jnp.concatenate([v[n:] for v in lines], axis=0)
    return pick(c == 0, low, high)


def leave_kernel(sz, slots, riders, sc, zero_own, zero_other, one_own, one_other, *refs):
    c = sc[0]
    if riders:
        shared, refs = refs[0], refs[1:]
        total = shared[...] + one_other[sz.rows :, :].astype(F32)
        extra = resplit(total[:PAD])
        part = (total.shape[0] - PAD) // riders
    outs = refs[:slots]
    for i in range(4):
        refs[slots][i] = sc[i]
    for r in range(slots):
        rows = aligned(lax.rem(sc[3] + r, slots) * HALF, HALF)
        own = pick(c == 0, zero_own[rows, :], one_own[rows, :])
        other = pick(c == 0, zero_other[rows, :], one_other[rows, :])
        put_pair(outs[r], c, own, other)
        if riders:
            lines = [extra, total[PAD + r * part : PAD + (r + 1) * part]]
            outs[r][BLOCK:, :] = jnp.concatenate(lines, axis=0).astype(LOW)


def home_kernel(slots, sc, *refs):
    early, late, out, grad = refs[:slots], refs[slots : 2 * slots], refs[-3], refs[-2]
    for i in range(4):
        refs[-1][i] = sc[i]
    first = sc[0] == 0
    for r in range(slots):
        at = lax.rem(sc[3] - r + slots, slots)
        out[at] = pick(first, early[r][...], late[r][:BLOCK, :]).astype(F32)
        grad[at] = pick(first, late[r][:BLOCK, :], early[r][...]).astype(F32)


def whole(shape):
    return pl.BlockSpec(shape, lambda *_: (0,) * len(shape))


def per_device(
    tokens,
    slot_order,
    log_decay,
    grad_out,
    in_gain,
    w_gate,
    w_inner,
    w_shared,
    conv_inner,
    conv_shared,
    d_skip,
    norm_gain,
    w_out,
):
    slots = tokens.shape[0]
    span = tokens.shape[1]
    width = tokens.shape[2]
    seq = lax.axis_size("seq")
    head_axis = lax.axis_size("head")
    cores = lax.axis_size("section")
    spans = seq // slots
    c = lax.axis_index("section")
    z = lax.axis_index("seq")
    h = lax.axis_index("head")
    k = lax.rem(z, slots)
    inner_dev = w_gate.shape[2]
    channels = inner_dev // cores
    shared = w_shared.shape[2]
    heads_dev = d_skip.shape[1]
    taps = conv_inner.shape[1]
    sz = Sizes(
        slots * span // BLOCK,
        width,
        channels,
        heads_dev // cores,
        shared // 2,
        taps,
        head_axis,
        inner_dev * head_axis,
    )
    first = c == 0
    swap = [(0, 1), (1, 0)]
    nb, tok, rows, chunk = sz.blocks, sz.tokens, sz.rows, sz.chunk

    def cross(x):
        return lax.ppermute(x, "section", swap)

    def turn(x, r):
        pairs = [(i, i // slots * slots + (i % slots + r) % slots) for i in range(seq)]
        return lax.ppermute(x, "seq", pairs) if r else x

    def over_heads(x, d):
        return lax.ppermute(x, "head", [(i, i ^ d) for i in range(head_axis)])

    def next_span(x, way):
        pairs = [(i, i + way * slots) for i in range(seq) if 0 <= i + way * slots < seq]
        return lax.ppermute(x, "seq", pairs)

    def shape(dims, dtype):
        return jax.ShapeDtypeStruct(dims, dtype)

    prefetch = functools.partial(pltpu.PrefetchScalarGridSpec, num_scalar_prefetch=1)
    options = pltpu.CompilerParams(vmem_limit_bytes=VMEM_BYTES)
    anywhere = pl.BlockSpec(memory_space=pl.ANY)
    in_hbm = pl.BlockSpec(memory_space=pltpu.HBM)
    smem = pl.BlockSpec(memory_space=pltpu.SMEM)
    vmem = pl.BlockSpec(memory_space=pltpu.VMEM)
    index_shape = shape((4,), jnp.int32)

    def cost(flops, moved):
        return pl.CostEstimate(flops=int(flops), bytes_accessed=int(moved), transcendentals=0)

    def take_rows(sc, source, rates, deps=()):
        given = [source] if rates is None else [source, rates]
        more = 0 if rates is None else PAD
        got = pl.pallas_call(
            functools.partial(slice_kernel, sz, slots, rates is not None, len(deps)),
            in_specs=[smem, smem, in_hbm]
            + ([] if rates is None else [in_hbm])
            + [anywhere] * len(deps),
            out_specs=[anywhere] * slots + [smem],
            out_shape=[shape((HALF + more, width), LOW)] * slots + [index_shape],
            scratch_shapes=(
                [
                    pltpu.VMEM((slots, PAD, width), LOW),
                    pltpu.VMEM((slots, heads_dev, span), F32),
                ]
                if more
                else []
            )
            + [pltpu.SemaphoreType.DMA((3 * slots,))],
            compiler_params=options,
        )(sc, slot_order, *given, *deps)
        return got[:slots], got[slots]

    def to_members(pieces):
        return [turn(x, r) for r, x in enumerate(pieces)]

    sc = jnp.stack([c, h, z, k]).astype(jnp.int32)
    tok_slices, sc = take_rows(sc, tokens, log_decay)
    tok_pieces = to_members(tok_slices)
    tok_others = [cross(x) for x in tok_pieces]

    wide = 2 * channels + shared
    w_sent, o_sent, pv_mine, pv_sent = pl.pallas_call(
        functools.partial(pack_kernel, sz),
        in_specs=[smem] + [in_hbm] * 4 + [vmem] * 5,
        out_specs=[in_hbm, in_hbm, vmem, vmem],
        out_shape=[
            shape((width, wide), LOW),
            shape((channels, width), LOW),
            shape((16, width), F32),
            shape((16, width), F32),
        ],
        scratch_shapes=[pltpu.SemaphoreType.DMA((4,))],
        compiler_params=options,
    )(
        sc, w_gate, w_inner, w_shared, w_out,
        in_gain, conv_inner, conv_shared, d_skip, norm_gain,
    )
    raw = [w_gate, w_inner, w_shared, w_out]
    sent = [cross(w_sent), cross(o_sent)]
    gains = [pv_mine, cross(pv_sent)]

    def span_total(table):
        ends = table[: sz.heads, BLOCK - 1 :: BLOCK]
        return jnp.repeat(jnp.exp(jnp.sum(ends, axis=1)), sz.head_width)[:, None]

    parts_shape = shape((head_axis, rows + PAD, chunk), LOW)
    weight_specs = [anywhere] * 6
    wide_weights = pltpu.VMEM((width, wide), LOW)
    out_weights = pltpu.VMEM((channels, width), LOW)
    copy_sems = pltpu.SemaphoreType.DMA((4,))
    dense = 2 * tok * width * (wide + channels)

    def forward(layer, sc, sources):
        def at(b, _):
            return (b, 0)

        piece = pl.BlockSpec((HALF, chunk), at)
        table = pl.BlockSpec((16, BLOCK), lambda b, _: (0, b))
        square = pl.BlockSpec((sz.heads, BLOCK, BLOCK), lambda b, _: (b, 0, 0))
        if layer == 0:
            src_specs = [whole((HALF + PAD, width))] * (2 * slots)
            more_specs = [table, table]
            more_shapes = [shape((16, tok), F32)] * 2
        else:
            src_specs = [piece] * (2 * head_axis) + [whole((HALF, width))] * (2 * slots) + [table]
            more_specs = [pl.BlockSpec((BLOCK, width), at)]
            more_shapes = [shape((tok, width), LOW)]

        def call(halo, begin):
            return pl.pallas_call(
                functools.partial(forward_kernel, sz, layer, slots),
                grid_spec=prefetch(
                    grid=(nb,),
                    in_specs=src_specs
                    + [whole((16, width)), whole((16, width))]
                    + weight_specs
                    + [whole((8, sz.lin)), whole((channels, sz.states))],
                    out_specs=[
                        pl.BlockSpec((BLOCK, width), at),
                        pl.BlockSpec((BLOCK, channels), at),
                        pl.BlockSpec((BLOCK, sz.lin), at),
                        pl.BlockSpec((BLOCK, channels), at),
                        pl.BlockSpec((1, channels, sz.states), lambda b, _: (b, 0, 0)),
                        pl.BlockSpec((1, BLOCK), lambda b, _: (0, b)),
                        pl.BlockSpec((2, BLOCK), lambda b, _: (0, b)),
                        pl.BlockSpec((BLOCK, channels), at),
                        whole((channels, sz.states)),
                        smem,
                        piece,
                        pl.BlockSpec((BLOCK, sz.lin), at),
                        pl.BlockSpec((BLOCK, sz.lin), at),
                        square,
                        square,
                    ]
                    + more_specs,
                    scratch_shapes=[
                        pltpu.VMEM((BLOCK, width), LOW),
                        pltpu.VMEM((BLOCK, width), LOW),
                        wide_weights,
                        out_weights,
                        pltpu.VMEM((BLOCK + 8, sz.lin), F32),
                        pltpu.VMEM((channels, sz.states), F32),
                        copy_sems,
                    ],
                ),
                out_shape=[
                    shape((tok, width), LOW),
                    shape((tok, channels), F32),
                    shape((tok, sz.lin), LOW),
                    shape((tok, channels), F32),
                    shape((nb, channels, sz.states), LOW),
                    shape((1, tok), F32),
                    shape((2, tok), F32),
                    shape((tok, channels), LOW),
                    shape((channels, sz.states), F32),
                    index_shape,
                    shape((rows, chunk), LOW),
                    shape((tok, sz.lin), LOW),
                    shape((tok, sz.lin), LOW),
                    shape((nb * sz.heads, BLOCK, BLOCK), LOW),
                    shape((nb * sz.heads, BLOCK, BLOCK), LOW),
                ]
                + more_shapes,
                compiler_params=options,
                cost_estimate=cost(6 * dense, 16e6),
            )(sc, *sources, *gains, *raw, *sent, halo, begin)

        halo = jnp.zeros((8, sz.lin), F32)
        begin = jnp.zeros((channels, sz.states), F32)
        if spans == 1:
            return call(halo, begin), halo
        trial = call(halo, begin)
        halo = next_span(trial[2][tok - 8 :].astype(F32), 1)
        local = call(halo, begin)[8]
        total = span_total(trial[15] if layer == 0 else sources[-1])
        for _ in range(spans - 1):
            begin = next_span(total * begin + local, 1)
        return call(halo, begin), halo

    def backward(layer, sc, sources, saved, decays, halo, deps):
        def at(i, _):
            return (nb - 1 - i, 0)

        if layer == 0:
            src_specs = [whole(s.shape) for s in sources]
        else:
            stat = pl.BlockSpec((2, BLOCK), lambda i, _: (0, nb - 1 - i))
            src_specs = [pl.BlockSpec((BLOCK, width), at)] + [stat] * head_axis
        gl, lin, ssd, inc, *kept = saved
        square = pl.BlockSpec((sz.heads, BLOCK, BLOCK), lambda i, _: (nb - 1 - i, 0, 0))
        mixed_spec = [pl.BlockSpec((BLOCK, width), at)] if layer == 0 else []
        mixed_shape = [shape((tok, width), LOW)] if layer == 0 else []

        def call(halo_grad, begin):
            return pl.pallas_call(
                functools.partial(backward_kernel, sz, layer, len(deps)),
                grid_spec=prefetch(
                    grid=(nb,),
                    in_specs=src_specs
                    + [
                        pl.BlockSpec((BLOCK, channels), at),
                        whole(lin.shape),
                        pl.BlockSpec((BLOCK, channels), at),
                        pl.BlockSpec((1, channels, sz.states), lambda i, _: (nb - 1 - i, 0, 0)),
                        pl.BlockSpec((BLOCK, sz.lin), at),
                        pl.BlockSpec((BLOCK, sz.lin), at),
                        square,
                        square,
                        pl.BlockSpec((16, BLOCK), lambda i, _: (0, nb - 1 - i)),
                        whole((16, width)),
                        whole((16, width)),
                        *weight_specs,
                        whole((8, sz.lin)),
                        whole((8, sz.lin)),
                        whole((channels, sz.states)),
                    ]
                    + [anywhere] * len(deps),
                    out_specs=[
                        pl.BlockSpec((BLOCK, wide), at),
                        pl.BlockSpec((BLOCK, channels), at),
                        whole((PAD, 3 * channels)),
                        whole((8, sz.lin)),
                        whole((channels, sz.states)),
                        whole((8, sz.lin)),
                        smem,
                    ]
                    + mixed_spec,
                    scratch_shapes=[
                        pltpu.VMEM((BLOCK, width), LOW),
                        out_weights,
                        pltpu.VMEM((BLOCK + 8, sz.lin), F32),
                        pltpu.VMEM((BLOCK + 8, sz.lin), F32),
                        pltpu.VMEM((channels, sz.states), F32),
                        pltpu.VMEM((PAD, HALF), F32),
                        pltpu.VMEM((8, sz.lin), F32),
                        copy_sems,
                    ],
                ),
                out_shape=[
                    shape((tok, wide), LOW),
                    shape((tok, channels), LOW),
                    shape((PAD, 3 * channels), LOW),
                    shape((8, sz.lin), F32),
                    shape((channels, sz.states), F32),
                    shape((8, sz.lin), F32),
                    index_shape,
                ]
                + mixed_shape,
                compiler_params=options,
                cost_estimate=cost(8 * dense, 16e6),
            )(
                sc, *sources, gl, lin, ssd, inc, *kept, decays, *gains, *raw, *sent,
                halo, halo_grad, begin, *deps,
            )

        halo_grad = jnp.zeros((8, sz.lin), F32)
        begin = jnp.zeros((channels, sz.states), F32)
        if spans == 1:
            return call(halo_grad, begin)
        local = call(halo_grad, begin)[4]
        for _ in range(spans - 1):
            begin = next_span(span_total(decays) * begin + local, -1)
        halo_grad = next_span(call(halo_grad, begin)[5], -1)
        return call(halo_grad, begin)

    def project(layer, sc, unit, stats, deps):
        return pl.pallas_call(
            functools.partial(project_kernel, sz, layer, len(deps)),
            in_specs=[smem, vmem, vmem] + weight_specs + [anywhere] * len(deps),
            out_specs=[vmem, vmem, smem],
            out_shape=[parts_shape, parts_shape, index_shape],
            scratch_shapes=[out_weights, copy_sems],
            compiler_params=options,
            cost_estimate=cost(dense / 4, 4e6),
        )(sc, unit, stats, *raw, *sent, *deps)

    def lift(layer, sc, cat, normed, small, deps):
        return pl.pallas_call(
            functools.partial(lift_kernel, sz, layer, len(deps)),
            in_specs=[smem] + [vmem] * 5 + weight_specs + [anywhere] * len(deps),
            out_specs=[vmem, vmem, smem, vmem],
            out_shape=[parts_shape, parts_shape, index_shape, shape((PAD, chunk), LOW)],
            scratch_shapes=[pltpu.VMEM((8, width), F32), wide_weights, copy_sems],
            compiler_params=options,
            cost_estimate=cost(dense, 8e6),
        )(sc, cat, normed, *gains, small, *raw, *sent, *deps)

    def scatter(sc, keep, send, *riders):
        size = rows + PAD + sum(rider[0].shape[0] for rider in riders)
        flat = [x for rider in riders for x in rider]
        joined = pl.pallas_call(
            functools.partial(join_kernel, sz, len(riders)),
            in_specs=[smem] + [vmem] * (2 + len(flat)),
            out_specs=[smem] + [vmem] * head_axis,
            out_shape=[index_shape, shape((size, chunk), F32)]
            + [shape((size, chunk), LOW)] * (head_axis - 1),
            compiler_params=options,
        )(sc, keep, cross(send), *flat)
        far = {d: over_heads(joined[1 + d], d) for d in range(head_axis - 1, 0, -1)}
        return [joined[1]] + [far[d] for d in range(1, head_axis)], joined[0]

    def gather(low):
        far = {d: over_heads(low, d) for d in range(head_axis - 1, 0, -1)}
        own = [low] + [far[d] for d in range(1, head_axis)]
        return own + [cross(x) for x in own]

    def section_output(layer, sc, parts, resid):
        return pl.pallas_call(
            functools.partial(output_kernel, sz, layer),
            in_specs=[smem] + [vmem] * (head_axis + 1),
            out_specs=[vmem] * 4 + [smem],
            out_shape=[
                shape((rows, chunk), F32),
                shape((rows, chunk), LOW),
                shape((rows, chunk), F32),
                shape((8, HALF), F32),
                index_shape,
            ],
            compiler_params=options,
        )(sc, *parts, resid)

    part = width // seq
    columns = 3 * channels
    share = part // head_axis
    shared_size = seq * share + PAD

    def section_input(layer, sc, parts, *others, deps=()):
        if layer == 0:
            outs = [
                shape((rows + PAD, chunk), LOW),
                shape((rows + shared_size, chunk), LOW),
                shape((shared_size, chunk), F32),
            ]
        else:
            outs = [shape((rows, chunk), F32), shape((rows + PAD, chunk), LOW)]
        return pl.pallas_call(
            functools.partial(input_kernel, sz, layer),
            in_specs=[smem] + [vmem] * (head_axis + len(others)) + [anywhere] * len(deps),
            out_specs=[vmem] * len(outs) + [smem],
            out_shape=outs + [index_shape],
            compiler_params=options,
        )(sc, *parts, *others, *deps)

    def weight_grads(sc, normed, cat, mixed, scaled, small, common):
        outs = pl.pallas_call(
            functools.partial(weights_kernel, sz, seq),
            in_specs=[smem] + [vmem] * 6,
            out_specs=[smem] + [vmem] * (seq + head_axis),
            out_shape=[index_shape]
            + [shape((part + PAD, columns), LOW)] * seq
            + [shape((shared_size, shared), LOW)] * head_axis,
            scratch_shapes=[pltpu.VMEM((width, columns), LOW), pltpu.VMEM((width, shared), F32)],
            compiler_params=options,
            cost_estimate=cost(4 * dense, 12e6),
        )(sc, normed, cat, mixed, scaled, small, common)
        return over_seq(outs[1 : 1 + seq]), outs[1 + seq :], outs[0]

    def over_seq(chunks):
        pieces = [chunks[0]]
        for r in range(1, seq):
            pairs = [(i, (i + r) % seq) for i in range(seq)]
            pieces.append(lax.ppermute(chunks[r], "seq", pairs))
        return pieces

    def leave(sc, *arrays, riders=0):
        size = BLOCK + (share + PAD if riders else 0)
        pieces = pl.pallas_call(
            functools.partial(leave_kernel, sz, slots, riders),
            in_specs=[smem] + [vmem] * len(arrays),
            out_specs=[vmem] * slots + [smem],
            out_shape=[shape((size, chunk), LOW)] * slots + [index_shape],
            compiler_params=options,
        )(sc, *arrays)
        return to_members(pieces[:slots]), pieces[slots]

    out_slices, unused = take_rows(sc, grad_out, None, tok_pieces[1:])
    out_pieces = to_members(out_slices)
    fw0, halo0 = forward(0, sc, tok_pieces + tok_others)
    base0, decays = fw0[10], fw0[15:17]
    pr0 = project(0, fw0[9], fw0[7], fw0[6], [out_pieces[1], out_pieces[-1]])
    out_others = [cross(x) for x in out_pieces]
    parts, sc_join = scatter(sc, pr0[0], pr0[1])
    res1, low1, mixed0, square0, unused = section_output(0, sc, parts, base0)
    pieces1 = gather(low1)
    square_other = cross(square0)

    fw1, halo1 = forward(1, sc, pieces1 + out_pieces + out_others + [decays[1]])
    stat = fw1[6] + cross(fw1[6])
    stats = [stat] + [over_heads(stat, d) for d in range(1, head_axis)]
    bw1 = backward(
        1, sc, [fw1[15]] + stats, [*fw1[1:5], *fw1[11:15]], decays[1], halo1, []
    )
    lf1 = lift(1, bw1[6], bw1[0], fw1[0], bw1[3], [])
    weights1, heads1, sc_weights = weight_grads(
        lf1[2], fw1[0], bw1[0], fw1[15], bw1[1], bw1[2], lf1[3]
    )
    parts, sc_join = scatter(sc_weights, lf1[0], lf1[1])
    igrad1, glow1, sc_in = section_input(
        1, sc_join, parts, res1, fw1[10], fw1[5], *gains, mixed0,
        deps=[weights1[1], weights1[-1]],
    )
    piecesg = gather(glow1)
    pr1 = project(1, sc_in, fw1[7], fw1[6], [])
    parts_out, sc_out = scatter(sc_in, pr1[0], pr1[1])

    early, unused = leave(sc_in, low1, pieces1[head_axis], glow1, piecesg[head_axis])
    bw0 = backward(
        0, sc, piecesg + [square0, square_other], [*fw0[1:5], *fw0[11:15]], decays[0], halo0,
        weights1[2:-1],
    )
    lf0 = lift(
        0, bw0[6], bw0[0], fw0[0], bw0[3], [early[1], early[-1]] + parts_out[1:]
    )
    weights0, heads0, sc_weights = weight_grads(
        lf0[2], fw0[0], bw0[0], bw0[7], bw0[1], bw0[2], lf0[3]
    )
    parts, sc_join = scatter(sc_weights, lf0[0], lf0[1], heads0, heads1)

    unused, low2, unused_mixed, unused_square, sc_out = section_output(1, sc_in, parts_out, res1)
    glow0, to_other, shared_own, sc_end = section_input(
        0, sc_out, parts, base0, igrad1, fw0[5], *gains, low2,
        deps=weights0[1:-1] + early[2:-1],
    )
    got = cross(to_other)
    if spans == 1:
        late, sc_end = leave(sc_end, glow0, got, low2, got, shared_own, riders=seq)
        shared_parts = late
    else:
        late, sc_end = leave(sc_end, glow0, got, low2, got)
        total = shared_own + got[rows:].astype(F32)
        extra = resplit(total[:PAD])
        fill = jnp.zeros((BLOCK, shared), F32)
        chunks = [
            jnp.concatenate([fill, extra, total[PAD + r * share : PAD + (r + 1) * share]])
            for r in range(seq)
        ]
        shared_parts = over_seq([x.astype(LOW) for x in chunks])
    section_out, input_grad, sc_end = pl.pallas_call(
        functools.partial(home_kernel, slots),
        in_specs=[smem] + [vmem] * (2 * slots),
        out_specs=[vmem, vmem, smem],
        out_shape=[shape((slots, BLOCK, chunk), F32)] * 2 + [index_shape],
        compiler_params=options,
    )(sc, *early, *late)

    def summed(sc, pieces):
        return pl.pallas_call(
            functools.partial(sum_kernel, sz),
            in_specs=[smem] + [vmem] * seq,
            out_shape=shape((part + PAD, columns), LOW),
            compiler_params=options,
        )(sc, *pieces)

    sums0, sums1 = summed(sc_end, weights0), summed(sc_in, weights1)
    final = pl.pallas_call(
        functools.partial(final_kernel, sz),
        in_specs=[smem] + [vmem] * (3 + seq),
        out_shape=[
            shape((part, inner_dev), F32),
            shape((part, inner_dev), F32),
            shape((inner_dev, part), F32),
            shape((taps, inner_dev), F32),
            shape((1, inner_dev), F32),
            shape((1, heads_dev), F32),
            shape((share, shared), F32),
            shape((PAD // 2, shared), F32),
        ],
        compiler_params=options,
    )(sc, sums0, sums1, cross(pick(first, sums1, sums0)), *shared_parts)
    common = final[7]
    place = z * head_axis + h
    conv_part = shared // (seq * head_axis)
    gain_part = width // (seq * head_axis)
    return (
        section_out[None],
        input_grad[None],
        lax.dynamic_slice_in_dim(common[taps:].reshape(-1), place * gain_part, gain_part, 0)[None],
        final[0][None],
        final[1][None],
        final[6][None],
        final[3][None],
        lax.dynamic_slice_in_dim(common[:taps], place * conv_part, conv_part, 1)[None],
        final[5],
        final[4],
        final[2][None],
    )


def solution(mesh):
    placed = (
        P(None, "seq", None),
        P(),
        P("section", None, "head", "seq"),
        P(None, "seq", None),
        P("section", None),
        P("section", None, "head"),
        P("section", None, "head"),
        P("section", None, None),
        P("section", None, "head"),
        P("section", None, None),
        P("section", "head"),
        P("section", "head"),
        P("section", None, None),
    )
    return jax.shard_map(
        per_device,
        mesh=mesh,
        in_specs=placed,
        out_specs=(
            P("section", None, "seq", "head"),
            P("section", None, "seq", "head"),
            P("section", ("seq", "head")),
            P("section", "seq", "head"),
            P("section", "seq", "head"),
            P("section", ("seq", "head"), None),
            P("section", None, "head"),
            P("section", None, ("seq", "head")),
            P("section", "head"),
            P("section", "head"),
            P("section", "head", "seq"),
        ),
        check_vma=False,
    )
```

```python
import functools

import jax
import jax.numpy as jnp
from jax import lax
from jax.experimental import pallas as pl
from jax.experimental.pallas import tpu as pltpu
from jax.sharding import PartitionSpec as P

BLOCK = 256
HALF = BLOCK // 2
PAD = 16
EPS = 1e-05
F32 = jnp.float32
LOW = jnp.bfloat16
HIDDEN = -1e30
NN = ((1,), (0,))
NT = ((1,), (1,))
TN = ((0,), (0,))
VMEM_BYTES = 50 * 1024 * 1024
ALL_VMEM_BYTES = 63 * 1024 * 1024


def dot(a, b, dims):
    return lax.dot_general(a, b, (dims, ((), ())), preferred_element_type=F32)


def aligned(start, size):
    return pl.ds(pl.multiple_of(start, size), size)


def spread(cols, first, count, width):
    rows = cols.shape[0]
    lane = lax.broadcasted_iota(jnp.int32, (rows, count * width), 1)
    out = jnp.broadcast_to(cols[:, first : first + 1], (rows, count * width))
    for h in range(1, count):
        out = jnp.where(lane >= h * width, cols[:, first + h : first + h + 1], out)
    return out


def per_head(array, h, width):
    lane = lax.broadcasted_iota(jnp.int32, array.shape, 1)
    inside = (lane >= h * width) & (lane < (h + 1) * width)
    return jnp.where(inside, array, jnp.zeros_like(array))


def split_low(value):
    high = value.astype(LOW).astype(F32)
    return high, value - high


def column_of(row, size):
    return jnp.transpose(jnp.broadcast_to(row, (128, size)))


def sigmoid(v):
    return 0.5 * jnp.tanh(0.5 * v) + 0.5


def pick(flag, a, b):
    return jnp.where(flag, a, b)


class Sizes:
    def __init__(self, blocks, width, channels, heads, states, taps, head_axis, inner):
        self.blocks = blocks
        self.width = width
        self.channels = channels
        self.heads = heads
        self.head_width = channels // heads
        self.states = states
        self.lin = channels + 2 * states
        self.taps = taps
        self.head_axis = head_axis
        self.chunk = width // head_axis
        self.rows = blocks * HALF
        self.tokens = blocks * BLOCK
        self.inner = inner


def weight_copies(sz, layer, c, h, raw, got, wv, ov, sems):
    gate, inner, shared, out = raw
    ch = sz.channels
    cols = aligned(c * ch, ch)
    rows = aligned((h * 2 + c) * ch, ch)
    own, sent = [], []
    if wv is not None:
        own += [
            (gate.at[0, :, cols], wv.at[:, :ch]),
            (inner.at[0, :, cols], wv.at[:, ch : 2 * ch]),
            (shared.at[0], wv.at[:, 2 * ch :]),
        ]
        sent += [(got[0], wv)]
    if ov is not None:
        own += [(out.at[0, rows, :], ov)]
        sent += [(got[1], ov)]
    return [
        (c == layer, [pltpu.make_async_copy(p, q, sems.at[i]) for i, (p, q) in enumerate(own)]),
        (c != layer, [pltpu.make_async_copy(p, q, sems.at[i]) for i, (p, q) in enumerate(sent)]),
    ]


def run_copies(choices, start, wait):
    for flag, copies in choices:

        @pl.when(flag)
        def _(copies=copies):
            if start:
                for copy in copies:
                    copy.start()
            if wait:
                for copy in copies:
                    copy.wait()


def put_ordered(sz, dst, c, k, b, own, other):
    for r in range(len(own)):

        @pl.when(lax.rem(k - b + len(own), len(own)) == r)
        def _(r=r):
            put_pair(dst, c, own[r][:HALF, :], other[r][:HALF, :])


def put_pair(dst, c, own, other):
    dst[aligned(c * HALF, HALF), :] = own
    dst[aligned((1 - c) * HALF, HALF), :] = other


def far_first(count):
    return [0] + list(range(count - 1, 0, -1))


def put_pieces(sz, dst, c, h, own, other):
    own, other = (dict(zip(far_first(sz.head_axis), side)) for side in (own, other))
    for d in range(sz.head_axis):
        cols = aligned((h ^ d) * sz.chunk, sz.chunk)
        dst[aligned(c * HALF, HALF), cols] = own[d]
        dst[aligned((1 - c) * HALF, HALF), cols] = other[d]


def line_of(table, at):
    line = lax.broadcasted_iota(jnp.int32, table.shape, 0)
    return jnp.sum(jnp.where(line == at, table, 0.0), axis=0, keepdims=True)


def conv_forward(sz, ext, taps):
    pre = taps[0:1] * ext[5 : 5 + BLOCK, :]
    for j in range(1, sz.taps):
        pre = pre + taps[j : j + 1] * ext[5 + j : 5 + j + BLOCK, :]
    return pre


def decay_of(sz, cols, rp, h, mask):
    rows = cols[:, h : h + 1] + rp[12 + h : 13 + h, :]
    return jnp.exp(jnp.where(mask, rows, HIDDEN))


def lower_mask():
    t = lax.broadcasted_iota(jnp.int32, (BLOCK, BLOCK), 0)
    s = lax.broadcasted_iota(jnp.int32, (BLOCK, BLOCK), 1)
    return t >= s


def forward_kernel(sz, layer, slots, sc, *refs):
    n = sz.head_axis
    sources = 2 * slots if layer == 0 else 2 * n + 2 * slots
    src, refs = refs[:sources], refs[sources:]
    if layer == 1:
        table, refs = refs[0], refs[1:]
    gains, raw, got, halo, begin = refs[0:2], refs[2:6], refs[6:8], refs[8], refs[9]
    if layer == 1:
        ov, refs = refs[10], refs[1:]
    normed_o, gl_o, lin_o, ssd_o, inc_o, inv_o, part_o, unit_o, fin_o, sc_o, base_o = refs[10:21]
    refs = refs[21:]
    if layer == 1:
        mixed_o, refs = refs[0], refs[1:]
    else:
        tables_o, refs = refs[0:2], refs[2:]
    xs, ms, wv, ext, state, sems = refs
    b = pl.program_id(0)
    c, h, k = sc[0], sc[1], sc[3]
    ch, st = sz.channels, sz.states
    copies = weight_copies(sz, layer, c, h, raw, got, wv, None, sems)

    @pl.when(b == 0)
    def _():
        run_copies(copies, True, False)
        ext[0:8, :] = halo[...]
        state[...] = begin[...]
        for i in range(4):
            sc_o[i] = sc[i]

    mine = aligned(c * HALF, HALF)
    cols = aligned(h * sz.chunk, sz.chunk)
    if layer == 0:
        put_ordered(sz, xs, c, k, b, src[:slots], src[slots:])
        base_o[...] = xs[mine, cols]
        for r in range(slots):

            @pl.when(lax.rem(k - b + slots, slots) == r)
            def _(r=r):
                own = decay_table(rates_of(src[r]), c, sz.heads)
                other = decay_table(rates_of(src[slots + r]), c, sz.heads)
                tables_o[0][...] = pick(c == 0, own, other)
                tables_o[1][...] = pick(c == 0, other, own)

        rp = tables_o[0][...]
    else:
        put_pieces(sz, xs, c, h, [r[...] for r in src[:n]], [r[...] for r in src[n : 2 * n]])
        put_ordered(sz, ms, c, k, b, src[2 * n : 2 * n + slots], src[2 * n + slots :])
        base_o[...] = ms[mine, cols]
        mixed_o[...] = ms[...]
        rp = table[...]

    pv = pick(c == layer, gains[0][...], gains[1][...])
    x = xs[...].astype(F32)
    inv_in = lax.rsqrt(jnp.mean(x * x, axis=1, keepdims=True) + EPS)
    normed = (x * inv_in * pv[0:1, : sz.width]).astype(LOW)
    normed_o[...] = normed

    @pl.when(b == 0)
    def _():
        run_copies(copies, False, True)

    proj = dot(normed, wv[...], NN)
    gl = proj[:, :ch]
    gl_o[...] = gl
    lin = proj[:, ch:].astype(LOW)
    lin_o[...] = lin
    ext[8 : 8 + BLOCK, :] = lin.astype(F32)
    pre = conv_forward(sz, ext, pv[1:5, : sz.lin])
    ext[0:8, :] = ext[BLOCK : BLOCK + 8, :]
    act = (pre * sigmoid(pre)).astype(LOW)
    values, bm, cm = act[:, :ch], act[:, ch : ch + st], act[:, ch + st :]

    cols = jnp.transpose(rp)
    mask = lower_mask()
    gram = dot(cm, bm, NT)
    mixes, parts = [], []
    for i in range(sz.heads):
        mixes.append((gram * decay_of(sz, cols, rp, i, mask)).astype(LOW))
        parts.append(per_head(values, i, sz.head_width))
    intra = dot(jnp.concatenate(mixes, axis=1), jnp.concatenate(parts, axis=0), NN)

    low_state = state[...].astype(LOW)
    inc_o[0] = low_state
    ecum = spread(cols, sz.heads, sz.heads, sz.head_width)
    inter = dot(cm, low_state, NT) * ecum
    vf = values.astype(F32)
    carried = (vf * spread(cols, 2 * sz.heads, sz.heads, sz.head_width)).astype(LOW)
    local = dot(carried, bm, TN)
    for i in range(sz.heads):
        rows = slice(i * sz.head_width, (i + 1) * sz.head_width)
        total = cols[BLOCK - 1 : BLOCK, sz.heads + i : sz.heads + i + 1]
        state[rows, :] = total * state[rows, :] + local[rows]
    ssd = intra + inter + pv[6:7, :ch] * vf
    ssd_o[...] = ssd
    gated = ssd * (gl * sigmoid(gl))
    weighty = gated * pv[5:6, :ch]
    unit_o[...] = weighty.astype(LOW)

    lane = lax.broadcasted_iota(jnp.int32, (BLOCK, 128), 1)
    square = jnp.sum(gated * gated, axis=1, keepdims=True)
    if layer == 0:
        project = jnp.zeros_like(square)
    else:
        scaled_grad = dot(ms[...], ov[...], NN)
        project = jnp.sum(scaled_grad * weighty, axis=1, keepdims=True)
    stats = jnp.where(lane == 0, square, jnp.where(lane == 1, project, inv_in))
    stats = jnp.transpose(stats)
    part_o[...] = stats[0:2, :]
    inv_o[...] = stats[2:3, :]

    @pl.when(b == sz.blocks - 1)
    def _():
        fin_o[...] = state[...]


def scalar_lines(sz, lines):
    fill = [jnp.zeros((8 - sz.blocks, HALF), F32)] if sz.blocks < 8 else []
    high, low = split_low(jnp.concatenate(lines + fill, axis=0))
    table = jnp.concatenate([high, low], axis=0).astype(LOW)
    return jnp.concatenate([table] * (sz.chunk // HALF), axis=1)


def own_rows(sz, ref, which):
    blocks = [ref[aligned(b * BLOCK + which * HALF, HALF), :] for b in range(sz.blocks)]
    return jnp.concatenate(blocks, axis=0)


def project_kernel(sz, layer, deps, sc, unit_r, stats_r, *refs):
    raw, got, refs = refs[:4], refs[4:6], refs[6 + deps :]
    keep, send, sc_o, weights, sems = refs
    c, h = sc[0], sc[1]
    copies = weight_copies(sz, layer, c, h, raw, got, None, weights, sems)
    run_copies(copies, True, False)
    for i in range(4):
        sc_o[i] = sc[i]
    sides = []
    for which, out in ((c, keep), (1 - c, send)):
        sides.append((out, own_rows(sz, unit_r, which)))
        lines = [
            stats_r[0:1, aligned(b * BLOCK + which * HALF, HALF)] for b in range(sz.blocks)
        ]
        table = scalar_lines(sz, lines)
        for d in range(sz.head_axis):
            out[d, sz.rows :, :] = table
    run_copies(copies, False, True)
    for out, rows in sides:
        for d in range(sz.head_axis):
            chunk = weights[:, aligned((h ^ d) * sz.chunk, sz.chunk)]
            out[d, : sz.rows, :] = dot(rows, chunk, NN).astype(LOW)


def turn_kernel(sz, sc, *refs):
    raw, got = refs[:4], refs[4:6]
    wide_o, out_o, wv, ov, sems = refs[6:8], refs[8:10], refs[10], refs[11], refs[12]
    for layer in range(2):
        copies = weight_copies(sz, layer, sc[0], sc[1], raw, got, wv, ov, sems)
        run_copies(copies, True, True)
        wide_o[layer][...] = jnp.transpose(wv[...])
        out_o[layer][...] = jnp.transpose(ov[...])


def lift_kernel(sz, layer, deps, sc, cat_r, normed_r, zero_gains, one_gains, small_r, *refs):
    weights, refs = refs[0], refs[1 + deps :]
    keep, send, sc_o, common_o, wide = refs
    c, h = sc[0], sc[1]
    for i in range(4):
        sc_o[i] = sc[i]
    wide[...] = jnp.zeros_like(wide)
    for which, out in ((c, keep), (1 - c, send)):
        rows = own_rows(sz, cat_r, which)
        along = jnp.zeros((sz.rows, 1), F32)
        for d in range(sz.head_axis):
            cols = aligned((h ^ d) * sz.chunk, sz.chunk)
            product = dot(rows, weights[:, cols], NN)
            out[d, : sz.rows, :] = product.astype(LOW)
            blocks = [
                normed_r[aligned(b * BLOCK + which * HALF, HALF), cols] for b in range(sz.blocks)
            ]
            product = product * jnp.concatenate(blocks, axis=0).astype(F32)
            wide[0:1, cols] += jnp.sum(product, axis=0, keepdims=True)
            along = along + jnp.sum(product, axis=1, keepdims=True)
        lines = [
            jnp.transpose(jnp.broadcast_to(along[b * HALF : (b + 1) * HALF], (HALF, 128)))[0:1, :]
            for b in range(sz.blocks)
        ]
        table = scalar_lines(sz, lines)
        for d in range(sz.head_axis):
            out[d, sz.rows :, :] = table
    gain_grad = wide[0:1, :] / pick(c == layer, zero_gains[0:1, :], one_gains[0:1, :])
    flat = [small_r[j : j + 1, sz.channels :] for j in range(sz.taps)]
    flat += [gain_grad[:, q * sz.chunk : (q + 1) * sz.chunk] for q in range(sz.head_axis)]
    high, low = split_low(jnp.concatenate(flat, axis=0))
    common_o[...] = jnp.concatenate([high, low], axis=0).astype(LOW)


def backward_kernel(sz, layer, deps, sc, *refs):
    n = sz.head_axis
    sources = 2 * n + 2 if layer == 0 else 1 + n
    src, refs = refs[:sources], refs[sources:]
    gl_r, lin_r, ssd_r, inc_r = refs[:4]
    table, gains, ov = refs[4], refs[5:7], refs[7]
    halo, halo_grad, begin = refs[8:11]
    refs = refs[11 + deps :]
    cat_o, scaled_o, small_o, sums_o, fin_o, rim_o, sc_o = refs[:7]
    refs = refs[7:]
    if layer == 0:
        mixed_o, refs = refs[0], refs[1:]
    ms, ext, back, state, heads_p, small = refs
    i_step = pl.program_id(0)
    b = sz.blocks - 1 - i_step
    c, h = sc[0], sc[1]
    ch, st = sz.channels, sz.states
    pv = pick(c == layer, gains[0][...], gains[1][...])
    rp = table[...]

    @pl.when(i_step == 0)
    def _():
        back[BLOCK : BLOCK + 8, :] = halo_grad[...]
        state[...] = begin[...]
        small[...] = jnp.zeros_like(small)
        for i in range(4):
            sc_o[i] = sc[i]
        if layer == 0:
            for i in range(2):
                extra = src[i * n][sz.rows :, :].astype(F32)
                for d in range(1, n):
                    extra = extra + src[i * n + d][sz.rows :, :].astype(F32)
                heads_p[8 * i : 8 * i + 8, :] = extra[0:8, :HALF] + extra[8:16, :HALF]

    if layer == 0:
        rows = aligned(b * HALF, HALF)
        put_pieces(
            sz, ms, c, h, [r[rows, :] for r in src[:n]], [r[rows, :] for r in src[n : 2 * n]]
        )
        halves = []
        for k in range(2):
            alpha = lax.rsqrt(line_of(src[2 * n + k][...], b) / sz.inner + EPS)
            beta = alpha * alpha * line_of(heads_p[...], 8 * k + b) / sz.inner
            halves.append((alpha, beta))
        alpha, beta = (
            pick(
                c == 0,
                jnp.concatenate([halves[0][q], halves[1][q]], axis=1),
                jnp.concatenate([halves[1][q], halves[0][q]], axis=1),
            )
            for q in range(2)
        )
    else:
        stats = src[1][...]
        for d in range(1, n):
            stats = stats + src[1 + d][...]
        alpha = lax.rsqrt(stats[0:1, :] / sz.inner + EPS)
        beta = alpha * alpha * alpha * stats[1:2, :] / sz.inner

    sub = lax.broadcasted_iota(jnp.int32, rp.shape, 0)
    cols = jnp.transpose(jnp.where(sub == 12, alpha, jnp.where(sub == 13, beta, rp)))
    alpha, beta = cols[:, 12:13], cols[:, 13:14]

    gl = gl_r[...]
    ssd = ssd_r[...]
    sig = sigmoid(gl)
    swish = gl * sig
    slope = sig * (1.0 + gl * (1.0 - sig))
    gated = ssd * swish
    if layer == 0:
        mixed_grad = ms[...]
        mixed_o[...] = mixed_grad
    else:
        mixed_grad = src[0][...]
    scaled_grad = dot(mixed_grad, ov[...], NN)
    gain = pv[5:6, :ch]
    normal = gated * alpha
    small[4:5, :ch] += jnp.sum(scaled_grad * normal, axis=0, keepdims=True)
    scaled_o[...] = (normal * gain).astype(LOW)
    gated_grad = alpha * (scaled_grad * gain) - beta * gated
    ssd_grad = (gated_grad * swish).astype(LOW)
    gate_grad = (gated_grad * ssd * slope).astype(LOW)
    sgf = ssd_grad.astype(F32)

    before = lin_r[pl.ds(pl.multiple_of(jnp.maximum(b * BLOCK - 16, 0), 16), 16), :]
    ext[0:8, :] = pick(b > 0, before.astype(F32)[8:16, :], halo[...])
    ext[8 : 8 + BLOCK, :] = lin_r[aligned(b * BLOCK, BLOCK), :].astype(F32)
    taps = pv[1:5, : sz.lin]
    pre = conv_forward(sz, ext, taps)
    psig = sigmoid(pre)
    pact = pre * psig
    pslope = psig * (1.0 + pre * (1.0 - psig))
    act = pact.astype(LOW)
    values, bm, cm = act[:, :ch], act[:, ch : ch + st], act[:, ch + st :]
    vf = values.astype(F32)
    small[5:6, :ch] += jnp.sum(sgf * vf, axis=0, keepdims=True)

    mask = lower_mask()
    gram = dot(cm, bm, NT)
    gram_grad = jnp.zeros((BLOCK, BLOCK), F32)
    mixes, parts = [], []
    for i in range(sz.heads):
        decay = decay_of(sz, cols, rp, i, mask)
        mixes.append((gram * decay).astype(LOW))
        parts.append(per_head(ssd_grad, i, sz.head_width))
        gram_grad = gram_grad + dot(parts[-1], values, NT) * decay
    intra_grad = dot(jnp.concatenate(mixes, axis=0), jnp.concatenate(parts, axis=0), TN)

    ecum = spread(cols, sz.heads, sz.heads, sz.head_width)
    to_end = spread(cols, 2 * sz.heads, sz.heads, sz.head_width)
    inter_grad = (sgf * ecum).astype(LOW)
    low_state = state[...].astype(LOW)
    carried = (vf * to_end).astype(LOW)
    carried_grad = dot(bm, low_state, NT)
    gram_low = gram_grad.astype(LOW)
    b_grad = dot(gram_low, cm, TN) + dot(carried, low_state, NN)
    c_grad = dot(gram_low, bm, NN) + dot(inter_grad, inc_r[0], NN)
    value_grad = intra_grad + pv[6:7, :ch] * sgf + carried_grad * to_end
    entry = dot(inter_grad, cm, TN)
    for i in range(sz.heads):
        rows = slice(i * sz.head_width, (i + 1) * sz.head_width)
        total = cols[BLOCK - 1 : BLOCK, sz.heads + i : sz.heads + i + 1]
        state[rows, :] = total * state[rows, :] + entry[rows]

    pre_grad = jnp.concatenate([value_grad, b_grad, c_grad], axis=1) * pslope
    back[0:BLOCK, :] = pre_grad
    lin_grad = taps[0:1] * back[sz.taps - 1 : sz.taps - 1 + BLOCK, :]
    for j in range(1, sz.taps):
        at = sz.taps - 1 - j
        lin_grad = lin_grad + taps[j : j + 1] * back[at : at + BLOCK, :]
    for j in range(sz.taps):
        small[j : j + 1, :] += jnp.sum(pre_grad * ext[5 + j : 5 + j + BLOCK, :], axis=0, keepdims=True)
    back[BLOCK : BLOCK + 8, :] = back[0:8, :]
    cat_o[...] = jnp.concatenate([gate_grad, lin_grad.astype(LOW)], axis=1)

    @pl.when(i_step == sz.blocks - 1)
    def _():
        fin_o[...] = state[...]
        rim_o[...] = back[0:8, :]
        sums = small[...]
        flat = [sums[j : j + 1, :ch] for j in range(sz.taps + 2)]
        flat = [jnp.concatenate(flat[j : j + 3], axis=1) for j in range(0, len(flat), 3)]
        flat = flat + [jnp.zeros_like(flat[0])] * (4 - len(flat))
        high, low = split_low(jnp.concatenate(flat, axis=0))
        rest = jnp.zeros((PAD - 8, high.shape[1]), F32)
        small_o[...] = jnp.concatenate([high, low, rest], axis=0).astype(LOW)
        sums_o[...] = sums


def weights_kernel(sz, seq, sc, normed, cat, mixed, scaled, small, common, *refs):
    sc_o, outs, heads, full, wide = refs[0], refs[1 : seq + 1], refs[seq + 1 : -2], refs[-2], refs[-1]
    for i in range(4):
        sc_o[i] = sc[i]
    ch, st = sz.channels, sz.states
    step = sz.chunk
    for q in range(sz.head_axis):
        at = slice(q * step, (q + 1) * step)
        grads = dot(normed[:, at], cat[...], TN)
        full[at, : 2 * ch] = grads[:, : 2 * ch].astype(LOW)
        wide[at, :] = grads[:, 2 * ch :]
        full[at, 2 * ch :] = dot(mixed[:, at], scaled[...], TN).astype(LOW)
    rows = sz.width // seq
    part = rows // sz.head_axis
    for r, out in enumerate(outs):
        out[:rows, :] = full[aligned(lax.rem(sc[2] + r, seq) * rows, rows), :]
        out[rows:, :] = small[...]
    for d, out in enumerate(heads):
        lines = [
            wide[aligned(lax.rem(sc[2] + r, seq) * rows + (sc[1] ^ d) * part, part), :]
            for r in range(seq)
        ]
        out[:PAD, :] = common[...]
        out[PAD:, :] = jnp.concatenate(lines, axis=0).astype(LOW)


def resplit(extra):
    half = extra.shape[0] // 2
    high, low = split_low(extra[:half, :] + extra[half:, :])
    return jnp.concatenate([high, low], axis=0)


def join_kernel(sz, riders, sc, keep, recv, *refs):
    n = sz.head_axis
    more, refs = [refs[i * n : (i + 1) * n] for i in range(riders)], refs[riders * n :]
    sc_o, outs = refs[0], refs[1:]
    rows = sz.rows
    for i in range(4):
        sc_o[i] = sc[i]
    extra = resplit(keep[0, rows:, :].astype(F32) + recv[0, rows:, :].astype(F32))
    for d, out in enumerate(outs):
        out[:rows, :] = (keep[d, :rows, :].astype(F32) + recv[d, :rows, :].astype(F32)).astype(out.dtype)
        out[rows : rows + PAD, :] = extra.astype(out.dtype)
        at = rows + PAD
        for rider in more:
            size = rider[d].shape[0]
            out[at : at + size, :] = rider[d][...].astype(out.dtype)
            at += size


def total_of(parts, rows):
    total = parts[0][rows, :].astype(F32)
    for p in parts[1:]:
        total = total + p[rows, :].astype(F32)
    return total


def output_kernel(sz, layer, sc, *refs):
    n = sz.head_axis
    parts, refs = refs[:n], refs[n:]
    resid = refs[0]
    res_o, low_o, mixed_o, square_o, sc_o = refs[-5:]
    for i in range(4):
        sc_o[i] = sc[i]
    extra = total_of(parts, slice(sz.rows, sz.rows + PAD))
    square = extra[0:8, :HALF] + extra[8:16, :HALF]
    square_o[...] = square
    inv = lax.rsqrt(square / sz.inner + EPS)
    for b in range(sz.blocks):
        rows = slice(b * HALF, (b + 1) * HALF)
        col = column_of(inv[b : b + 1, :], HALF)[:, 0:1]
        mixed = total_of(parts, rows) * col
        res = resid[rows, :].astype(F32) + mixed
        res_o[rows, :] = res
        low_o[rows, :] = res.astype(LOW)
        mixed_o[rows, :] = mixed


def input_kernel(sz, layer, sc, *refs):
    n = sz.head_axis
    parts, refs = refs[:n], refs[n:]
    resid, outg, inv_r, gains = refs[0], refs[1], refs[2], refs[3:5]
    refs = refs[5:]
    if layer == 1:
        mixed = refs[0]
        grad_o, low_o, sc_o = refs[-3:]
    else:
        one_low = refs[0]
        low_o, swap_o, shared_o, sc_o = refs[-4:]
    for i in range(4):
        sc_o[i] = sc[i]
    c, h = sc[0], sc[1]
    first = c == 0
    mine = aligned(h * sz.chunk, sz.chunk)
    gain = pick(c == layer, gains[0][0:1, mine], gains[1][0:1, mine])
    extra = total_of(parts, slice(sz.rows, sz.rows + PAD))
    along = extra[0:8, :HALF] + extra[8:16, :HALF]
    tops, lows = [], []
    for b in range(sz.blocks):
        rows = slice(b * HALF, (b + 1) * HALF)
        at = b * BLOCK
        inv_row = pick(c == 0, inv_r[:, at : at + HALF], inv_r[:, at + HALF : at + BLOCK])
        inv = column_of(inv_row, HALF)[:, 0:1]
        share = column_of(along[b : b + 1, :] / sz.width, HALF)[:, 0:1]
        total = total_of(parts, rows)
        base = resid[rows, :].astype(F32)
        grad = outg[rows, :].astype(F32) + inv * (total * gain - base * (inv * share))
        low = grad.astype(LOW)
        low_o[rows, :] = low
        if layer == 0:
            swap_o[rows, :] = pick(first, one_low[rows, :], low)
        else:
            grad_o[rows, :] = grad
            dots = jnp.sum(low.astype(F32) * mixed[rows, :], axis=1, keepdims=True)
            row = jnp.transpose(jnp.broadcast_to(dots, (HALF, 128)))[0:1, :]
            high, rest = split_low(row)
            tops.append(high)
            lows.append(rest)
    if layer == 1:
        fill = [jnp.zeros((8 - sz.blocks, HALF), F32)] if sz.blocks < 8 else []
        extra = jnp.concatenate(tops + fill + lows + fill, axis=0)
        extra = jnp.concatenate([extra] * (sz.chunk // HALF), axis=1)
        low_o[sz.rows :, :] = extra.astype(LOW)
    else:
        size = shared_o.shape[0]
        at = sz.rows + PAD
        zero = total_of(parts, slice(at, at + size))
        one = total_of(parts, slice(at + size, at + 2 * size))
        zero, one = (jnp.concatenate([resplit(v[:PAD]), v[PAD:]], axis=0) for v in (zero, one))
        shared_o[...] = pick(first, zero, one)
        swap_o[sz.rows :, :] = pick(first, one, zero).astype(LOW)


def sum_kernel(sz, last, sc, *refs):
    if last:
        parts, done, outs = refs[:-3], refs[-3], refs[-2:]
    else:
        parts, outs = refs[:-1], refs[-1:]
    rows = outs[0].shape[0] - PAD
    extra = total_of(parts, slice(rows, rows + PAD))
    high, low = split_low(extra[0:4, :] + extra[4:8, :])
    extra = jnp.concatenate([high, low, jnp.zeros((PAD - 8, extra.shape[1]), F32)], axis=0)
    sums = jnp.concatenate([total_of(parts, slice(0, rows)), extra], axis=0).astype(LOW)
    if last:
        outs[0][...] = pick(sc[0] == 0, sums, done[...])
        outs[1][...] = pick(sc[0] == 0, done[...], sums)
    else:
        outs[0][...] = sums


def final_kernel(sz, seq, sc, own, got, *refs):
    pieces, refs = refs[:-9], refs[-9:]
    gate_o, inner_o, out_o, conv_o, norm_o, skip_o, shared_o, taps_o, gain_o = refs
    c = sc[0]
    ch = sz.channels
    rows = own.shape[0] - PAD
    lane = lax.broadcasted_iota(jnp.int32, skip_o.shape, 1)
    skip = jnp.zeros(skip_o.shape, F32)
    for i in range(2):
        which = pick(i == 0, c, 1 - c)
        to = aligned(which * ch, ch)
        sums = (own if i == 0 else got)[...].astype(F32)
        gate_o[:, to] = sums[:rows, :ch]
        inner_o[:, to] = sums[:rows, ch : 2 * ch]
        out_o[to, :] = jnp.transpose(sums[:rows, 2 * ch :])
        lines = sums[rows : rows + 4, :] + sums[rows + 4 : rows + 8, :]
        for j in range(sz.taps):
            conv_o[j : j + 1, to] = lines[j // 3 : j // 3 + 1, (j % 3) * ch : (j % 3 + 1) * ch]
        norm_o[:, to] = lines[1:2, ch : 2 * ch]
        skips = lines[1:2, 2 * ch :]
        for q in range(sz.heads):
            part = jnp.sum(per_head(skips, q, sz.head_width), axis=1, keepdims=True)
            skip = jnp.where(lane == which * sz.heads + q, part, skip)
    skip_o[...] = skip
    total = total_of(pieces, slice(BLOCK, None))
    shared_o[...] = total[PAD:]
    common = total[: PAD // 2] + total[PAD // 2 : PAD]
    place = sc[2] * sz.head_axis + sc[1]
    span = common.shape[1]
    size = span // (seq * sz.head_axis)
    turned = pltpu.roll(common, lax.rem(span - place * size, span), 1)
    taps_o[...] = turned[: sz.taps, :size]
    size = sz.width // (seq * sz.head_axis)
    at = place * size
    line = jnp.broadcast_to(line_of(common, sz.taps + at // span), common.shape)
    turned = pltpu.roll(line, lax.rem(span - lax.rem(at, span), span), 1)
    gain_o[...] = turned[:1, :size]


def slice_kernel(sz, slots, with_rates, deps, sc, order, *refs):
    sources = 2 if with_rates else 1
    src, refs = refs[:sources], refs[sources + deps :]
    outs, sc_o, refs = refs[:slots], refs[slots], refs[slots + 1 :]
    sems = refs[-1]
    copies = []
    for r in range(slots):
        which = order[lax.rem(sc[3] + r, slots)]
        rows = src[0].at[which, aligned(sc[0] * HALF, HALF), :]
        to = outs[r].at[:HALF] if with_rates else outs[r]
        copies.append(pltpu.make_async_copy(rows, to, sems.at[r]))
    for copy in copies:
        copy.start()
    for i in range(4):
        sc_o[i] = sc[i]
    if with_rates:
        thirds = refs[0]
        for r in range(slots):
            which = order[lax.rem(sc[3] + r, slots)]
            first, rest = split_low(src[1][0, which])
            second, rest = split_low(rest)
            lines = jnp.concatenate([first, second, rest, jnp.zeros_like(rest)], axis=1)
            lines = jnp.concatenate([lines, jnp.zeros_like(lines)], axis=0)
            thirds[r] = lines.astype(LOW)
        more = [
            pltpu.make_async_copy(thirds.at[r], outs[r].at[HALF:], sems.at[slots + r])
            for r in range(slots)
        ]
        for copy in more:
            copy.start()
        copies = copies + more
    for copy in copies:
        copy.wait()


def rates_of(piece):
    lines = piece[HALF:, :].astype(F32)[:8, :]
    return (lines[:, :BLOCK] + lines[:, BLOCK : 2 * BLOCK]) + lines[:, 2 * BLOCK : 3 * BLOCK]


def pack_kernel(sz, sc, gate, inner, shared, out, in_gain, conv_i, conv_s, skip, norm, *refs):
    w_o, o_o, mine_o, send_o, sems = refs
    c, h = sc[0], sc[1]
    ch = sz.channels
    cols = aligned((1 - c) * ch, ch)
    rows = aligned((h * 2 + 1 - c) * ch, ch)
    copies = [
        pltpu.make_async_copy(gate.at[0, :, cols], w_o.at[:, :ch], sems.at[0]),
        pltpu.make_async_copy(inner.at[0, :, cols], w_o.at[:, ch : 2 * ch], sems.at[1]),
        pltpu.make_async_copy(shared.at[0], w_o.at[:, 2 * ch :], sems.at[2]),
        pltpu.make_async_copy(out.at[0, rows, :], o_o, sems.at[3]),
    ]
    for copy in copies:
        copy.start()
    for which, ref in ((c, mine_o), (1 - c, send_o)):
        at = aligned(which * ch, ch)
        ref[...] = jnp.zeros_like(ref)
        ref[0:1, :] = in_gain[...]
        ref[1 : 1 + sz.taps, :ch] = conv_i[0, :, at]
        ref[1 : 1 + sz.taps, ch : sz.lin] = conv_s[0]
        ref[5:6, :ch] = norm[:, at]
        low = spread(skip[...], 0, sz.heads, sz.head_width)
        high = spread(skip[...], sz.heads, sz.heads, sz.head_width)
        ref[6:7, :ch] = pick(which == 0, low, high)
    for copy in copies:
        copy.wait()


def decay_table(rate, c, n):
    lane = lax.broadcasted_iota(jnp.int32, rate.shape, 1)
    cum = rate
    step = 1
    while step < BLOCK:
        cum = cum + jnp.where(lane >= step, pltpu.roll(cum, step, 1), 0.0)
        step *= 2
    end = cum[:, BLOCK - 1 :]
    lines = [cum, jnp.exp(cum), jnp.exp(end - cum) * -rate, jnp.log(-rate) - cum]
    low = jnp.concatenate([v[:n] for v in lines], axis=0)
    high = jnp.concatenate([v[n:] for v in lines], axis=0)
    return pick(c == 0, low, high)


def leave_kernel(sz, slots, riders, sc, zero_own, zero_other, one_own, one_other, *refs):
    c = sc[0]
    if riders:
        shared, refs = refs[0], refs[1:]
        total = shared[...] + one_other[sz.rows :, :].astype(F32)
        extra = resplit(total[:PAD])
        part = (total.shape[0] - PAD) // riders
    outs = refs[:slots]
    for i in range(4):
        refs[slots][i] = sc[i]
    for r in range(slots):
        rows = aligned(lax.rem(sc[3] + r, slots) * HALF, HALF)
        own = pick(c == 0, zero_own[rows, :], one_own[rows, :])
        other = pick(c == 0, zero_other[rows, :], one_other[rows, :])
        put_pair(outs[r], c, own, other)
        if riders:
            lines = [extra, total[PAD + r * part : PAD + (r + 1) * part]]
            outs[r][BLOCK:, :] = jnp.concatenate(lines, axis=0).astype(LOW)


def home_kernel(slots, sc, *refs):
    early, late, out, grad = refs[:slots], refs[slots : 2 * slots], refs[-3], refs[-2]
    for i in range(4):
        refs[-1][i] = sc[i]
    first = sc[0] == 0
    for r in range(slots):
        at = lax.rem(sc[3] - r + slots, slots)
        out[at] = pick(first, early[r][...], late[r][:BLOCK, :]).astype(F32)
        grad[at] = pick(first, late[r][:BLOCK, :], early[r][...]).astype(F32)


def whole(shape):
    return pl.BlockSpec(shape, lambda *_: (0,) * len(shape))


def per_device(
    tokens,
    slot_order,
    log_decay,
    grad_out,
    in_gain,
    w_gate,
    w_inner,
    w_shared,
    conv_inner,
    conv_shared,
    d_skip,
    norm_gain,
    w_out,
):
    slots = tokens.shape[0]
    span = tokens.shape[1]
    width = tokens.shape[2]
    seq = lax.axis_size("seq")
    head_axis = lax.axis_size("head")
    cores = lax.axis_size("section")
    spans = seq // slots
    c = lax.axis_index("section")
    z = lax.axis_index("seq")
    h = lax.axis_index("head")
    k = lax.rem(z, slots)
    inner_dev = w_gate.shape[2]
    channels = inner_dev // cores
    shared = w_shared.shape[2]
    heads_dev = d_skip.shape[1]
    taps = conv_inner.shape[1]
    sz = Sizes(
        slots * span // BLOCK,
        width,
        channels,
        heads_dev // cores,
        shared // 2,
        taps,
        head_axis,
        inner_dev * head_axis,
    )
    first = c == 0
    swap = [(0, 1), (1, 0)]
    nb, tok, rows, chunk = sz.blocks, sz.tokens, sz.rows, sz.chunk

    def cross(x):
        return lax.ppermute(x, "section", swap)

    def turn(x, r):
        pairs = [(i, i // slots * slots + (i % slots + r) % slots) for i in range(seq)]
        return lax.ppermute(x, "seq", pairs) if r else x

    def over_heads(x, d):
        return x if d == 0 else lax.ppermute(x, "head", [(i, i ^ d) for i in range(head_axis)])

    def next_span(x, way):
        pairs = [(i, i + way * slots) for i in range(seq) if 0 <= i + way * slots < seq]
        return lax.ppermute(x, "seq", pairs)

    def shape(dims, dtype):
        return jax.ShapeDtypeStruct(dims, dtype)

    prefetch = functools.partial(pltpu.PrefetchScalarGridSpec, num_scalar_prefetch=1)
    options = pltpu.CompilerParams(vmem_limit_bytes=VMEM_BYTES)
    from_hbm = pltpu.CompilerParams(vmem_limit_bytes=ALL_VMEM_BYTES)
    anywhere = pl.BlockSpec(memory_space=pl.ANY)
    smem = pl.BlockSpec(memory_space=pltpu.SMEM)
    vmem = pl.BlockSpec(memory_space=pltpu.VMEM)
    index_shape = shape((4,), jnp.int32)

    def cost(flops, moved):
        return pl.CostEstimate(flops=int(flops), bytes_accessed=int(moved), transcendentals=0)

    def take_rows(sc, source, rates, deps=()):
        given = [source] if rates is None else [source, rates]
        more = 0 if rates is None else PAD
        got = pl.pallas_call(
            functools.partial(slice_kernel, sz, slots, rates is not None, len(deps)),
            in_specs=[smem, smem, anywhere]
            + ([] if rates is None else [vmem])
            + [anywhere] * len(deps),
            out_specs=[anywhere] * slots + [smem],
            out_shape=[shape((HALF + more, width), LOW)] * slots + [index_shape],
            scratch_shapes=([pltpu.VMEM((slots, PAD, width), LOW)] if more else [])
            + [pltpu.SemaphoreType.DMA((2 * slots,))],
            compiler_params=options if deps else from_hbm,
        )(sc, slot_order, *given, *deps)
        return got[:slots], got[slots]

    def to_members(pieces):
        return [turn(x, r) for r, x in enumerate(pieces)]

    sc = jnp.stack([c, h, z, k]).astype(jnp.int32)
    tok_slices, sc = take_rows(sc, tokens, log_decay)
    tok_pieces = to_members(tok_slices)
    tok_others = [cross(x) for x in tok_pieces]

    wide = 2 * channels + shared
    w_sent, o_sent, pv_mine, pv_sent = pl.pallas_call(
        functools.partial(pack_kernel, sz),
        in_specs=[smem] + [anywhere] * 4 + [vmem] * 5,
        out_specs=[anywhere, anywhere, vmem, vmem],
        out_shape=[
            shape((width, wide), LOW),
            shape((channels, width), LOW),
            shape((16, width), F32),
            shape((16, width), F32),
        ],
        scratch_shapes=[pltpu.SemaphoreType.DMA((4,))],
        compiler_params=from_hbm,
    )(sc, w_gate, w_inner, w_shared, w_out, in_gain, conv_inner, conv_shared, d_skip, norm_gain)
    raw = [w_gate, w_inner, w_shared, w_out]
    sent = [cross(w_sent), cross(o_sent)]
    gains = [pv_mine, cross(pv_sent)]

    def span_total(table):
        ends = table[: sz.heads, BLOCK - 1 :: BLOCK]
        return jnp.repeat(jnp.exp(jnp.sum(ends, axis=1)), sz.head_width)[:, None]

    parts_shape = shape((head_axis, rows + PAD, chunk), LOW)
    weight_specs = [anywhere] * 6
    wide_weights = pltpu.VMEM((width, wide), LOW)
    out_weights = pltpu.VMEM((channels, width), LOW)
    copy_sems = pltpu.SemaphoreType.DMA((4,))
    dense = 2 * tok * width * (wide + channels)

    def forward(layer, sc, sources):
        def at(b, _):
            return (b, 0)

        piece = pl.BlockSpec((HALF, chunk), at)
        table = pl.BlockSpec((16, BLOCK), lambda b, _: (0, b))
        if layer == 0:
            src_specs = [whole((HALF + PAD, width))] * (2 * slots)
            more_specs = [table, table]
            more_shapes = [shape((16, tok), F32)] * 2
        else:
            src_specs = [piece] * (2 * head_axis) + [whole((HALF, width))] * (2 * slots) + [table]
            more_specs = [pl.BlockSpec((BLOCK, width), at)]
            more_shapes = [shape((tok, width), LOW)]

        last = [] if layer == 0 else [turned[3]]

        def call(halo, begin):
            return pl.pallas_call(
                functools.partial(forward_kernel, sz, layer, slots),
                grid_spec=prefetch(
                    grid=(nb,),
                    in_specs=src_specs
                    + [whole((16, width)), whole((16, width))]
                    + weight_specs
                    + [whole((8, sz.lin)), whole((channels, sz.states))]
                    + [whole(x.shape) for x in last],
                    out_specs=[
                        pl.BlockSpec((BLOCK, width), at),
                        pl.BlockSpec((BLOCK, channels), at),
                        pl.BlockSpec((BLOCK, sz.lin), at),
                        pl.BlockSpec((BLOCK, channels), at),
                        pl.BlockSpec((1, channels, sz.states), lambda b, _: (b, 0, 0)),
                        pl.BlockSpec((1, BLOCK), lambda b, _: (0, b)),
                        pl.BlockSpec((2, BLOCK), lambda b, _: (0, b)),
                        pl.BlockSpec((BLOCK, channels), at),
                        whole((channels, sz.states)),
                        smem,
                        piece,
                    ]
                    + more_specs,
                    scratch_shapes=[
                        pltpu.VMEM((BLOCK, width), LOW),
                        pltpu.VMEM((BLOCK, width), LOW),
                        wide_weights,
                        pltpu.VMEM((BLOCK + 8, sz.lin), F32),
                        pltpu.VMEM((channels, sz.states), F32),
                        copy_sems,
                    ],
                ),
                out_shape=[
                    shape((tok, width), LOW),
                    shape((tok, channels), F32),
                    shape((tok, sz.lin), LOW),
                    shape((tok, channels), F32),
                    shape((nb, channels, sz.states), LOW),
                    shape((1, tok), F32),
                    shape((2, tok), F32),
                    shape((tok, channels), LOW),
                    shape((channels, sz.states), F32),
                    index_shape,
                    shape((rows, chunk), LOW),
                ]
                + more_shapes,
                compiler_params=options,
                cost_estimate=cost(6 * dense, 16e6),
            )(sc, *sources, *gains, *raw, *sent, halo, begin, *last)

        halo = jnp.zeros((8, sz.lin), F32)
        begin = jnp.zeros((channels, sz.states), F32)
        if spans == 1:
            return call(halo, begin), halo
        trial = call(halo, begin)
        halo = next_span(trial[2][tok - 8 :].astype(F32), 1)
        local = call(halo, begin)[8]
        total = span_total(trial[11] if layer == 0 else sources[-1])
        for _ in range(spans - 1):
            begin = next_span(total * begin + local, 1)
        return call(halo, begin), halo

    def backward(layer, sc, sources, saved, decays, halo, deps):
        def at(i, _):
            return (nb - 1 - i, 0)

        if layer == 0:
            src_specs = [whole(s.shape) for s in sources]
        else:
            stat = pl.BlockSpec((2, BLOCK), lambda i, _: (0, nb - 1 - i))
            src_specs = [pl.BlockSpec((BLOCK, width), at)] + [stat] * head_axis
        gl, lin, ssd, inc = saved
        mixed_spec = [pl.BlockSpec((BLOCK, width), at)] if layer == 0 else []
        mixed_shape = [shape((tok, width), LOW)] if layer == 0 else []

        def call(halo_grad, begin):
            return pl.pallas_call(
                functools.partial(backward_kernel, sz, layer, len(deps)),
                grid_spec=prefetch(
                    grid=(nb,),
                    in_specs=src_specs
                    + [
                        pl.BlockSpec((BLOCK, channels), at),
                        whole(lin.shape),
                        pl.BlockSpec((BLOCK, channels), at),
                        pl.BlockSpec((1, channels, sz.states), lambda i, _: (nb - 1 - i, 0, 0)),
                        pl.BlockSpec((16, BLOCK), lambda i, _: (0, nb - 1 - i)),
                        whole((16, width)),
                        whole((16, width)),
                        whole((width, channels)),
                        whole((8, sz.lin)),
                        whole((8, sz.lin)),
                        whole((channels, sz.states)),
                    ]
                    + [anywhere] * len(deps),
                    out_specs=[
                        pl.BlockSpec((BLOCK, wide), at),
                        pl.BlockSpec((BLOCK, channels), at),
                        whole((PAD, 3 * channels)),
                        whole((8, sz.lin)),
                        whole((channels, sz.states)),
                        whole((8, sz.lin)),
                        smem,
                    ]
                    + mixed_spec,
                    scratch_shapes=[
                        pltpu.VMEM((BLOCK, width), LOW),
                        pltpu.VMEM((BLOCK + 8, sz.lin), F32),
                        pltpu.VMEM((BLOCK + 8, sz.lin), F32),
                        pltpu.VMEM((channels, sz.states), F32),
                        pltpu.VMEM((PAD, HALF), F32),
                        pltpu.VMEM((8, sz.lin), F32),
                    ],
                ),
                out_shape=[
                    shape((tok, wide), LOW),
                    shape((tok, channels), LOW),
                    shape((PAD, 3 * channels), LOW),
                    shape((8, sz.lin), F32),
                    shape((channels, sz.states), F32),
                    shape((8, sz.lin), F32),
                    index_shape,
                ]
                + mixed_shape,
                compiler_params=options,
                cost_estimate=cost(8 * dense, 16e6),
            )(
                sc, *sources, gl, lin, ssd, inc, decays, *gains, turned[2 + layer],
                halo, halo_grad, begin, *deps,
            )

        halo_grad = jnp.zeros((8, sz.lin), F32)
        begin = jnp.zeros((channels, sz.states), F32)
        if spans == 1:
            return call(halo_grad, begin)
        local = call(halo_grad, begin)[4]
        for _ in range(spans - 1):
            begin = next_span(span_total(decays) * begin + local, -1)
        halo_grad = next_span(call(halo_grad, begin)[5], -1)
        return call(halo_grad, begin)

    def project(layer, sc, unit, stats, deps):
        return pl.pallas_call(
            functools.partial(project_kernel, sz, layer, len(deps)),
            in_specs=[smem, vmem, vmem] + weight_specs + [anywhere] * len(deps),
            out_specs=[vmem, vmem, smem],
            out_shape=[parts_shape, parts_shape, index_shape],
            scratch_shapes=[out_weights, copy_sems],
            compiler_params=options,
            cost_estimate=cost(dense / 4, 4e6),
        )(sc, unit, stats, *raw, *sent, *deps)

    def lift(layer, sc, cat, normed, small, deps):
        return pl.pallas_call(
            functools.partial(lift_kernel, sz, layer, len(deps)),
            in_specs=[smem] + [vmem] * 6 + [anywhere] * len(deps),
            out_specs=[vmem, vmem, smem, vmem],
            out_shape=[parts_shape, parts_shape, index_shape, shape((PAD, chunk), LOW)],
            scratch_shapes=[pltpu.VMEM((8, width), F32)],
            compiler_params=options,
            cost_estimate=cost(dense, 8e6),
        )(sc, cat, normed, *gains, small, turned[layer], *deps)

    def scatter(sc, keep, send, *riders):
        size = rows + PAD + sum(rider[0].shape[0] for rider in riders)
        flat = [x for rider in riders for x in rider]
        joined = pl.pallas_call(
            functools.partial(join_kernel, sz, len(riders)),
            in_specs=[smem] + [vmem] * (2 + len(flat)),
            out_specs=[smem] + [vmem] * head_axis,
            out_shape=[index_shape, shape((size, chunk), F32)]
            + [shape((size, chunk), LOW)] * (head_axis - 1),
            compiler_params=options,
        )(sc, keep, cross(send), *flat)
        return [over_heads(joined[1 + d], d) for d in far_first(head_axis)], joined[0]

    def gather(low):
        own = [over_heads(low, d) for d in far_first(head_axis)]
        return own + [cross(x) for x in own]

    turned = pl.pallas_call(
        functools.partial(turn_kernel, sz),
        in_specs=[smem] + weight_specs,
        out_specs=[vmem] * 4,
        out_shape=[shape((wide, width), LOW)] * 2 + [shape((width, channels), LOW)] * 2,
        scratch_shapes=[wide_weights, out_weights, copy_sems],
        compiler_params=options,
        cost_estimate=cost(1e9, 8e6),
    )

    def section_output(layer, sc, parts, resid, deps=()):
        return pl.pallas_call(
            functools.partial(output_kernel, sz, layer),
            in_specs=[smem] + [vmem] * (head_axis + 1) + [anywhere] * len(deps),
            out_specs=[vmem] * 4 + [smem],
            out_shape=[
                shape((rows, chunk), F32),
                shape((rows, chunk), LOW),
                shape((rows, chunk), F32),
                shape((8, HALF), F32),
                index_shape,
            ],
            compiler_params=options,
        )(sc, *parts, resid, *deps)

    part = width // seq
    columns = 3 * channels
    share = part // head_axis
    shared_size = seq * share + PAD

    def section_input(layer, sc, parts, *others, deps=()):
        if layer == 0:
            outs = [
                shape((rows + PAD, chunk), LOW),
                shape((rows + shared_size, chunk), LOW),
                shape((shared_size, chunk), F32),
            ]
        else:
            outs = [shape((rows, chunk), F32), shape((rows + PAD, chunk), LOW)]
        return pl.pallas_call(
            functools.partial(input_kernel, sz, layer),
            in_specs=[smem] + [vmem] * (head_axis + len(others)) + [anywhere] * len(deps),
            out_specs=[vmem] * len(outs) + [smem],
            out_shape=outs + [index_shape],
            compiler_params=options,
        )(sc, *parts, *others, *deps)

    def weight_grads(sc, normed, cat, mixed, scaled, small, common):
        outs = pl.pallas_call(
            functools.partial(weights_kernel, sz, seq),
            in_specs=[smem] + [vmem] * 6,
            out_specs=[smem] + [vmem] * (seq + head_axis),
            out_shape=[index_shape]
            + [shape((part + PAD, columns), LOW)] * seq
            + [shape((shared_size, shared), LOW)] * head_axis,
            scratch_shapes=[pltpu.VMEM((width, columns), LOW), pltpu.VMEM((width, shared), F32)],
            compiler_params=options,
            cost_estimate=cost(4 * dense, 12e6),
        )(sc, normed, cat, mixed, scaled, small, common)
        return over_seq(outs[1 : 1 + seq]), outs[1 + seq :], outs[0]

    def over_seq(chunks):
        pieces = [chunks[0]]
        for r in range(1, seq):
            pairs = [(i, (i + r) % seq) for i in range(seq)]
            pieces.append(lax.ppermute(chunks[r], "seq", pairs))
        return pieces

    def leave(sc, *arrays, riders=0):
        size = BLOCK + (share + PAD if riders else 0)
        pieces = pl.pallas_call(
            functools.partial(leave_kernel, sz, slots, riders),
            in_specs=[smem] + [vmem] * len(arrays),
            out_specs=[vmem] * slots + [smem],
            out_shape=[shape((size, chunk), LOW)] * slots + [index_shape],
            compiler_params=options,
        )(sc, *arrays)
        return to_members(pieces[:slots]), pieces[slots]

    out_slices, unused = take_rows(sc, grad_out, None, tok_pieces[1:])
    out_pieces = to_members(out_slices)
    fw0, halo0 = forward(0, sc, tok_pieces + tok_others)
    base0, decays = fw0[10], fw0[11:13]
    pr0 = project(0, fw0[9], fw0[7], fw0[6], [out_pieces[1], out_pieces[-1]])
    out_others = [cross(x) for x in out_pieces]
    parts, sc_join = scatter(sc, pr0[0], pr0[1])
    turned = turned(sc_join, *raw, *sent)
    res1, low1, mixed0, square0, unused = section_output(0, sc, parts, base0, turned)
    pieces1 = gather(low1)
    square_other = cross(square0)

    fw1, halo1 = forward(1, sc, pieces1 + out_pieces + out_others + [decays[1]])
    stat = fw1[6] + cross(fw1[6])
    stats = [stat] + [over_heads(stat, d) for d in range(1, head_axis)]
    pr1 = project(1, fw1[9], fw1[7], fw1[6], [])
    parts_out, sc_out = scatter(sc, pr1[0], pr1[1])
    bw1 = backward(1, sc_out, [fw1[11]] + stats, fw1[1:5], decays[1], halo1, [])
    lf1 = lift(1, bw1[6], bw1[0], fw1[0], bw1[3], parts_out[1:])
    weights1, heads1, sc_weights = weight_grads(
        lf1[2], fw1[0], bw1[0], fw1[11], bw1[1], bw1[2], lf1[3]
    )
    parts, sc_join = scatter(sc_weights, lf1[0], lf1[1])
    igrad1, glow1, sc_in = section_input(
        1, sc_join, parts, res1, fw1[10], fw1[5], *gains, mixed0,
        deps=[weights1[1], weights1[-1]],
    )
    piecesg = gather(glow1)

    early, unused = leave(sc_in, low1, pieces1[head_axis], glow1, piecesg[head_axis])
    bw0 = backward(
        0, sc, piecesg + [square0, square_other], fw0[1:5], decays[0], halo0, weights1[2:-1]
    )
    lf0 = lift(0, bw0[6], bw0[0], fw0[0], bw0[3], [early[1], early[-1]])
    weights0, heads0, sc_weights = weight_grads(
        lf0[2], fw0[0], bw0[0], bw0[7], bw0[1], bw0[2], lf0[3]
    )
    parts, sc_join = scatter(sc_weights, lf0[0], lf0[1], heads0, heads1)

    unused, low2, unused_mixed, unused_square, sc_out = section_output(1, sc_in, parts_out, res1)
    glow0, to_other, shared_own, sc_end = section_input(
        0, sc_out, parts, base0, igrad1, fw0[5], *gains, low2,
        deps=weights0[1:-1] + early[2:-1],
    )
    got = cross(to_other)
    if spans == 1:
        late, sc_end = leave(sc_end, glow0, got, low2, got, shared_own, riders=seq)
        shared_parts = late
    else:
        late, sc_end = leave(sc_end, glow0, got, low2, got)
        total = shared_own + got[rows:].astype(F32)
        extra = resplit(total[:PAD])
        fill = jnp.zeros((BLOCK, shared), F32)
        chunks = [
            jnp.concatenate([fill, extra, total[PAD + r * share : PAD + (r + 1) * share]])
            for r in range(seq)
        ]
        shared_parts = over_seq([x.astype(LOW) for x in chunks])
    section_out, input_grad, sc_end = pl.pallas_call(
        functools.partial(home_kernel, slots),
        in_specs=[smem] + [vmem] * (2 * slots),
        out_specs=[vmem, vmem, smem],
        out_shape=[shape((slots, BLOCK, chunk), F32)] * 2 + [index_shape],
        compiler_params=options,
    )(sc, *early, *late)

    def summed(sc, pieces, *done):
        return pl.pallas_call(
            functools.partial(sum_kernel, sz, bool(done)),
            in_specs=[smem] + [vmem] * (seq + len(done)),
            out_shape=[shape((part + PAD, columns), LOW)] * (1 + len(done)),
            compiler_params=options,
        )(sc, *pieces, *done)

    own_sums, other_sums = summed(sc_end, weights0, *summed(sc_in, weights1))
    final = pl.pallas_call(
        functools.partial(final_kernel, sz, seq),
        in_specs=[smem] + [vmem] * (2 + seq),
        out_shape=[
            shape((part, inner_dev), F32),
            shape((part, inner_dev), F32),
            shape((inner_dev, part), F32),
            shape((taps, inner_dev), F32),
            shape((1, inner_dev), F32),
            shape((1, heads_dev), F32),
            shape((share, shared), F32),
            shape((taps, shared // (seq * head_axis)), F32),
            shape((1, width // (seq * head_axis)), F32),
        ],
        compiler_params=options,
    )(sc, own_sums, cross(other_sums), *shared_parts)
    return (
        section_out[None],
        input_grad[None],
        final[8],
        final[0][None],
        final[1][None],
        final[6][None],
        final[3][None],
        final[7][None],
        final[5],
        final[4],
        final[2][None],
    )


def solution(mesh):
    placed = (
        P(None, "seq", None),
        P(),
        P("section", None, "head", "seq"),
        P(None, "seq", None),
        P("section", None),
        P("section", None, "head"),
        P("section", None, "head"),
        P("section", None, None),
        P("section", None, "head"),
        P("section", None, None),
        P("section", "head"),
        P("section", "head"),
        P("section", None, None),
    )
    return jax.shard_map(
        per_device,
        mesh=mesh,
        in_specs=placed,
        out_specs=(
            P("section", None, "seq", "head"),
            P("section", None, "seq", "head"),
            P("section", ("seq", "head")),
            P("section", "seq", "head"),
            P("section", "seq", "head"),
            P("section", ("seq", "head"), None),
            P("section", None, "head"),
            P("section", None, ("seq", "head")),
            P("section", "head"),
            P("section", "head"),
            P("section", "head", "seq"),
        ),
        check_vma=False,
    )
```

```python
import functools

import jax
import jax.numpy as jnp
from jax import lax
from jax.experimental import pallas as pl
from jax.experimental.pallas import tpu as pltpu
from jax.sharding import PartitionSpec as P

BLOCK = 256
HALF = BLOCK // 2
PAD = 16
EPS = 1e-05
F32 = jnp.float32
LOW = jnp.bfloat16
HIDDEN = -1e30
NN = ((1,), (0,))
NT = ((1,), (1,))
TN = ((0,), (0,))
VMEM_BYTES = 50 * 1024 * 1024
ALL_VMEM_BYTES = 63 * 1024 * 1024


def dot(a, b, dims):
    return lax.dot_general(a, b, (dims, ((), ())), preferred_element_type=F32)


def aligned(start, size):
    return pl.ds(pl.multiple_of(start, size), size)


def spread(cols, first, count, width):
    rows = cols.shape[0]
    lane = lax.broadcasted_iota(jnp.int32, (rows, count * width), 1)
    out = jnp.broadcast_to(cols[:, first : first + 1], (rows, count * width))
    for h in range(1, count):
        out = jnp.where(lane >= h * width, cols[:, first + h : first + h + 1], out)
    return out


def per_head(array, h, width):
    lane = lax.broadcasted_iota(jnp.int32, array.shape, 1)
    inside = (lane >= h * width) & (lane < (h + 1) * width)
    return jnp.where(inside, array, jnp.zeros_like(array))


def split_low(value):
    high = value.astype(LOW).astype(F32)
    return high, value - high


def column_of(row, size):
    return jnp.transpose(jnp.broadcast_to(row, (128, size)))


def sigmoid(v):
    return 0.5 * jnp.tanh(0.5 * v) + 0.5


def pick(flag, a, b):
    return jnp.where(flag, a, b)


class Sizes:
    def __init__(self, blocks, width, channels, heads, states, taps, head_axis, inner):
        self.blocks = blocks
        self.width = width
        self.channels = channels
        self.heads = heads
        self.head_width = channels // heads
        self.states = states
        self.lin = channels + 2 * states
        self.taps = taps
        self.head_axis = head_axis
        self.chunk = width // head_axis
        self.rows = blocks * HALF
        self.tokens = blocks * BLOCK
        self.inner = inner


def weight_copies(sz, layer, c, h, raw, got, wv, ov, sems):
    gate, inner, shared, out = raw
    ch = sz.channels
    cols = aligned(c * ch, ch)
    rows = aligned((h * 2 + c) * ch, ch)
    own, sent = [], []
    if wv is not None:
        own += [
            (gate.at[0, :, cols], wv.at[:, :ch]),
            (inner.at[0, :, cols], wv.at[:, ch : 2 * ch]),
            (shared.at[0], wv.at[:, 2 * ch :]),
        ]
        sent += [(got[0], wv)]
    if ov is not None:
        own += [(out.at[0, rows, :], ov)]
        sent += [(got[1], ov)]
    return [
        (c == layer, [pltpu.make_async_copy(p, q, sems.at[i]) for i, (p, q) in enumerate(own)]),
        (c != layer, [pltpu.make_async_copy(p, q, sems.at[i]) for i, (p, q) in enumerate(sent)]),
    ]


def run_copies(choices, start, wait):
    for flag, copies in choices:

        @pl.when(flag)
        def _(copies=copies):
            if start:
                for copy in copies:
                    copy.start()
            if wait:
                for copy in copies:
                    copy.wait()


def put_ordered(sz, dst, c, k, b, own, other):
    for r in range(len(own)):

        @pl.when(lax.rem(k - b + len(own), len(own)) == r)
        def _(r=r):
            put_pair(dst, c, own[r][:HALF, :], other[r][:HALF, :])


def put_pair(dst, c, own, other):
    dst[aligned(c * HALF, HALF), :] = own
    dst[aligned((1 - c) * HALF, HALF), :] = other


def far_first(count):
    return [0] + list(range(count - 1, 0, -1))


def put_pieces(sz, dst, c, h, own, other):
    own, other = (dict(zip(far_first(sz.head_axis), side)) for side in (own, other))
    for d in range(sz.head_axis):
        cols = aligned((h ^ d) * sz.chunk, sz.chunk)
        dst[aligned(c * HALF, HALF), cols] = own[d]
        dst[aligned((1 - c) * HALF, HALF), cols] = other[d]


def line_of(table, at):
    line = lax.broadcasted_iota(jnp.int32, table.shape, 0)
    return jnp.sum(jnp.where(line == at, table, 0.0), axis=0, keepdims=True)


def conv_forward(sz, ext, taps):
    pre = taps[0:1] * ext[5 : 5 + BLOCK, :]
    for j in range(1, sz.taps):
        pre = pre + taps[j : j + 1] * ext[5 + j : 5 + j + BLOCK, :]
    return pre


def decay_of(sz, cols, rp, h, mask):
    rows = cols[:, h : h + 1] + rp[12 + h : 13 + h, :]
    return jnp.exp(jnp.where(mask, rows, HIDDEN))


def lower_mask():
    t = lax.broadcasted_iota(jnp.int32, (BLOCK, BLOCK), 0)
    s = lax.broadcasted_iota(jnp.int32, (BLOCK, BLOCK), 1)
    return t >= s


def forward_kernel(sz, layer, slots, sc, *refs):
    n = sz.head_axis
    sources = 2 * slots if layer == 0 else 2 * n + 2 * slots
    src, refs = refs[:sources], refs[sources:]
    if layer == 1:
        table, refs = refs[0], refs[1:]
    gains, raw, got, halo, begin = refs[0:2], refs[2:6], refs[6:8], refs[8], refs[9]
    if layer == 1:
        ov, refs = refs[10], refs[1:]
    normed_o, gl_o, lin_o, ssd_o, inc_o, inv_o, part_o, unit_o, fin_o, sc_o, base_o = refs[10:21]
    refs = refs[21:]
    if layer == 1:
        mixed_o, refs = refs[0], refs[1:]
    else:
        tables_o, refs = refs[0:2], refs[2:]
    xs, ms, wv, ext, state, sems = refs
    b = pl.program_id(0)
    c, h, k = sc[0], sc[1], sc[3]
    ch, st = sz.channels, sz.states
    copies = weight_copies(sz, layer, c, h, raw, got, wv, None, sems)

    @pl.when(b == 0)
    def _():
        run_copies(copies, True, False)
        ext[0:8, :] = halo[...]
        state[...] = begin[...]
        for i in range(4):
            sc_o[i] = sc[i]

    mine = aligned(c * HALF, HALF)
    cols = aligned(h * sz.chunk, sz.chunk)
    if layer == 0:
        put_ordered(sz, xs, c, k, b, src[:slots], src[slots:])
        base_o[...] = xs[mine, cols]
        for r in range(slots):

            @pl.when(lax.rem(k - b + slots, slots) == r)
            def _(r=r):
                own = decay_table(rates_of(src[r]), c, sz.heads)
                other = decay_table(rates_of(src[slots + r]), c, sz.heads)
                tables_o[0][...] = pick(c == 0, own, other)
                tables_o[1][...] = pick(c == 0, other, own)

        rp = tables_o[0][...]
    else:
        put_pieces(sz, xs, c, h, [r[...] for r in src[:n]], [r[...] for r in src[n : 2 * n]])
        put_ordered(sz, ms, c, k, b, src[2 * n : 2 * n + slots], src[2 * n + slots :])
        base_o[...] = ms[mine, cols]
        mixed_o[...] = ms[...]
        rp = table[...]

    pv = pick(c == layer, gains[0][...], gains[1][...])
    x = xs[...].astype(F32)
    inv_in = lax.rsqrt(jnp.mean(x * x, axis=1, keepdims=True) + EPS)
    normed = (x * inv_in * pv[0:1, : sz.width]).astype(LOW)
    normed_o[...] = normed

    @pl.when(b == 0)
    def _():
        run_copies(copies, False, True)

    proj = dot(normed, wv[...], NN)
    gl = proj[:, :ch]
    gl_o[...] = gl
    lin = proj[:, ch:].astype(LOW)
    lin_o[...] = lin
    ext[8 : 8 + BLOCK, :] = lin.astype(F32)
    pre = conv_forward(sz, ext, pv[1:5, : sz.lin])
    ext[0:8, :] = ext[BLOCK : BLOCK + 8, :]
    act = (pre * sigmoid(pre)).astype(LOW)
    values, bm, cm = act[:, :ch], act[:, ch : ch + st], act[:, ch + st :]

    cols = jnp.transpose(rp)
    mask = lower_mask()
    gram = dot(cm, bm, NT)
    mixes, parts = [], []
    for i in range(sz.heads):
        mixes.append((gram * decay_of(sz, cols, rp, i, mask)).astype(LOW))
        parts.append(per_head(values, i, sz.head_width))
    intra = dot(jnp.concatenate(mixes, axis=1), jnp.concatenate(parts, axis=0), NN)

    low_state = state[...].astype(LOW)
    inc_o[0] = low_state
    ecum = spread(cols, sz.heads, sz.heads, sz.head_width)
    inter = dot(cm, low_state, NT) * ecum
    vf = values.astype(F32)
    carried = (vf * spread(cols, 2 * sz.heads, sz.heads, sz.head_width)).astype(LOW)
    local = dot(carried, bm, TN)
    for i in range(sz.heads):
        rows = slice(i * sz.head_width, (i + 1) * sz.head_width)
        total = cols[BLOCK - 1 : BLOCK, sz.heads + i : sz.heads + i + 1]
        state[rows, :] = total * state[rows, :] + local[rows]
    ssd = intra + inter + pv[6:7, :ch] * vf
    ssd_o[...] = ssd
    gated = ssd * (gl * sigmoid(gl))
    weighty = gated * pv[5:6, :ch]
    unit_o[...] = weighty.astype(LOW)

    lane = lax.broadcasted_iota(jnp.int32, (BLOCK, 128), 1)
    square = jnp.sum(gated * gated, axis=1, keepdims=True)
    if layer == 0:
        project = jnp.zeros_like(square)
    else:
        scaled_grad = dot(ms[...], ov[...], NN)
        project = jnp.sum(scaled_grad * weighty, axis=1, keepdims=True)
    stats = jnp.where(lane == 0, square, jnp.where(lane == 1, project, inv_in))
    stats = jnp.transpose(stats)
    part_o[...] = stats[0:2, :]
    inv_o[...] = stats[2:3, :]

    @pl.when(b == sz.blocks - 1)
    def _():
        fin_o[...] = state[...]


def scalar_lines(sz, lines):
    fill = [jnp.zeros((8 - sz.blocks, HALF), F32)] if sz.blocks < 8 else []
    high, low = split_low(jnp.concatenate(lines + fill, axis=0))
    table = jnp.concatenate([high, low], axis=0).astype(LOW)
    return jnp.concatenate([table] * (sz.chunk // HALF), axis=1)


def own_rows(sz, ref, which):
    blocks = [ref[aligned(b * BLOCK + which * HALF, HALF), :] for b in range(sz.blocks)]
    return jnp.concatenate(blocks, axis=0)


def project_kernel(sz, layer, deps, sc, unit_r, stats_r, *refs):
    raw, got, refs = refs[:4], refs[4:6], refs[6 + deps :]
    keep, send, sc_o, weights, sems = refs
    c, h = sc[0], sc[1]
    copies = weight_copies(sz, layer, c, h, raw, got, None, weights, sems)
    run_copies(copies, True, False)
    for i in range(4):
        sc_o[i] = sc[i]
    sides = []
    for which, out in ((c, keep), (1 - c, send)):
        sides.append((out, own_rows(sz, unit_r, which)))
        lines = [
            stats_r[0:1, aligned(b * BLOCK + which * HALF, HALF)] for b in range(sz.blocks)
        ]
        table = scalar_lines(sz, lines)
        for d in range(sz.head_axis):
            out[d, sz.rows :, :] = table
    run_copies(copies, False, True)
    for out, rows in sides:
        for d in range(sz.head_axis):
            chunk = weights[:, aligned((h ^ d) * sz.chunk, sz.chunk)]
            out[d, : sz.rows, :] = dot(rows, chunk, NN).astype(LOW)


def turn_kernel(sz, sc, *refs):
    raw, got = refs[:4], refs[4:6]
    wide_o, out_o, wv, ov, sems = refs[6:8], refs[8:10], refs[10], refs[11], refs[12]
    for layer in range(2):
        copies = weight_copies(sz, layer, sc[0], sc[1], raw, got, wv, ov, sems)
        run_copies(copies, True, True)
        wide_o[layer][...] = jnp.transpose(wv[...])
        out_o[layer][...] = jnp.transpose(ov[...])


def lift_kernel(sz, layer, deps, sc, cat_r, normed_r, zero_gains, one_gains, small_r, *refs):
    weights, refs = refs[0], refs[1 + deps :]
    keep, send, sc_o, common_o, wide = refs
    c, h = sc[0], sc[1]
    for i in range(4):
        sc_o[i] = sc[i]
    wide[...] = jnp.zeros_like(wide)
    for which, out in ((c, keep), (1 - c, send)):
        rows = own_rows(sz, cat_r, which)
        along = jnp.zeros((sz.rows, 1), F32)
        for d in range(sz.head_axis):
            cols = aligned((h ^ d) * sz.chunk, sz.chunk)
            product = dot(rows, weights[:, cols], NN)
            out[d, : sz.rows, :] = product.astype(LOW)
            blocks = [
                normed_r[aligned(b * BLOCK + which * HALF, HALF), cols] for b in range(sz.blocks)
            ]
            product = product * jnp.concatenate(blocks, axis=0).astype(F32)
            wide[0:1, cols] += jnp.sum(product, axis=0, keepdims=True)
            along = along + jnp.sum(product, axis=1, keepdims=True)
        lines = [
            jnp.transpose(jnp.broadcast_to(along[b * HALF : (b + 1) * HALF], (HALF, 128)))[0:1, :]
            for b in range(sz.blocks)
        ]
        table = scalar_lines(sz, lines)
        for d in range(sz.head_axis):
            out[d, sz.rows :, :] = table
    gain_grad = wide[0:1, :] / pick(c == layer, zero_gains[0:1, :], one_gains[0:1, :])
    flat = [small_r[j : j + 1, sz.channels :] for j in range(sz.taps)]
    flat += [gain_grad[:, q * sz.chunk : (q + 1) * sz.chunk] for q in range(sz.head_axis)]
    high, low = split_low(jnp.concatenate(flat, axis=0))
    common_o[...] = jnp.concatenate([high, low], axis=0).astype(LOW)


def backward_kernel(sz, layer, deps, sc, *refs):
    n = sz.head_axis
    sources = 2 * n + 2 if layer == 0 else 1 + n
    src, refs = refs[:sources], refs[sources:]
    gl_r, lin_r, ssd_r, inc_r = refs[:4]
    table, gains, ov = refs[4], refs[5:7], refs[7]
    halo, halo_grad, begin = refs[8:11]
    refs = refs[11 + deps :]
    cat_o, scaled_o, small_o, sums_o, fin_o, rim_o, sc_o = refs[:7]
    refs = refs[7:]
    if layer == 0:
        mixed_o, refs = refs[0], refs[1:]
    ms, ext, back, state, heads_p, small = refs
    i_step = pl.program_id(0)
    b = sz.blocks - 1 - i_step
    c, h = sc[0], sc[1]
    ch, st = sz.channels, sz.states
    pv = pick(c == layer, gains[0][...], gains[1][...])
    rp = table[...]

    @pl.when(i_step == 0)
    def _():
        back[BLOCK : BLOCK + 8, :] = halo_grad[...]
        state[...] = begin[...]
        small[...] = jnp.zeros_like(small)
        for i in range(4):
            sc_o[i] = sc[i]
        if layer == 0:
            for i in range(2):
                extra = src[i * n][sz.rows :, :].astype(F32)
                for d in range(1, n):
                    extra = extra + src[i * n + d][sz.rows :, :].astype(F32)
                heads_p[8 * i : 8 * i + 8, :] = extra[0:8, :HALF] + extra[8:16, :HALF]

    if layer == 0:
        rows = aligned(b * HALF, HALF)
        put_pieces(
            sz, ms, c, h, [r[rows, :] for r in src[:n]], [r[rows, :] for r in src[n : 2 * n]]
        )
        halves = []
        for k in range(2):
            alpha = lax.rsqrt(line_of(src[2 * n + k][...], b) / sz.inner + EPS)
            beta = alpha * alpha * line_of(heads_p[...], 8 * k + b) / sz.inner
            halves.append((alpha, beta))
        alpha, beta = (
            pick(
                c == 0,
                jnp.concatenate([halves[0][q], halves[1][q]], axis=1),
                jnp.concatenate([halves[1][q], halves[0][q]], axis=1),
            )
            for q in range(2)
        )
    else:
        stats = src[1][...]
        for d in range(1, n):
            stats = stats + src[1 + d][...]
        alpha = lax.rsqrt(stats[0:1, :] / sz.inner + EPS)
        beta = alpha * alpha * alpha * stats[1:2, :] / sz.inner

    sub = lax.broadcasted_iota(jnp.int32, rp.shape, 0)
    cols = jnp.transpose(jnp.where(sub == 12, alpha, jnp.where(sub == 13, beta, rp)))
    alpha, beta = cols[:, 12:13], cols[:, 13:14]

    gl = gl_r[...]
    ssd = ssd_r[...]
    sig = sigmoid(gl)
    swish = gl * sig
    slope = sig * (1.0 + gl * (1.0 - sig))
    gated = ssd * swish
    if layer == 0:
        mixed_grad = ms[...]
        mixed_o[...] = mixed_grad
    else:
        mixed_grad = src[0][...]
    scaled_grad = dot(mixed_grad, ov[...], NN)
    gain = pv[5:6, :ch]
    normal = gated * alpha
    small[4:5, :ch] += jnp.sum(scaled_grad * normal, axis=0, keepdims=True)
    scaled_o[...] = (normal * gain).astype(LOW)
    gated_grad = alpha * (scaled_grad * gain) - beta * gated
    ssd_grad = (gated_grad * swish).astype(LOW)
    gate_grad = (gated_grad * ssd * slope).astype(LOW)
    sgf = ssd_grad.astype(F32)

    before = lin_r[pl.ds(pl.multiple_of(jnp.maximum(b * BLOCK - 16, 0), 16), 16), :]
    ext[0:8, :] = pick(b > 0, before.astype(F32)[8:16, :], halo[...])
    ext[8 : 8 + BLOCK, :] = lin_r[aligned(b * BLOCK, BLOCK), :].astype(F32)
    taps = pv[1:5, : sz.lin]
    pre = conv_forward(sz, ext, taps)
    psig = sigmoid(pre)
    pact = pre * psig
    pslope = psig * (1.0 + pre * (1.0 - psig))
    act = pact.astype(LOW)
    values, bm, cm = act[:, :ch], act[:, ch : ch + st], act[:, ch + st :]
    vf = values.astype(F32)
    small[5:6, :ch] += jnp.sum(sgf * vf, axis=0, keepdims=True)

    mask = lower_mask()
    gram = dot(cm, bm, NT)
    gram_grad = jnp.zeros((BLOCK, BLOCK), F32)
    mixes, parts = [], []
    for i in range(sz.heads):
        decay = decay_of(sz, cols, rp, i, mask)
        mixes.append((gram * decay).astype(LOW))
        parts.append(per_head(ssd_grad, i, sz.head_width))
        gram_grad = gram_grad + dot(parts[-1], values, NT) * decay
    intra_grad = dot(jnp.concatenate(mixes, axis=0), jnp.concatenate(parts, axis=0), TN)

    ecum = spread(cols, sz.heads, sz.heads, sz.head_width)
    to_end = spread(cols, 2 * sz.heads, sz.heads, sz.head_width)
    inter_grad = (sgf * ecum).astype(LOW)
    low_state = state[...].astype(LOW)
    carried = (vf * to_end).astype(LOW)
    carried_grad = dot(bm, low_state, NT)
    gram_low = gram_grad.astype(LOW)
    b_grad = dot(gram_low, cm, TN) + dot(carried, low_state, NN)
    c_grad = dot(gram_low, bm, NN) + dot(inter_grad, inc_r[0], NN)
    value_grad = intra_grad + pv[6:7, :ch] * sgf + carried_grad * to_end
    entry = dot(inter_grad, cm, TN)
    for i in range(sz.heads):
        rows = slice(i * sz.head_width, (i + 1) * sz.head_width)
        total = cols[BLOCK - 1 : BLOCK, sz.heads + i : sz.heads + i + 1]
        state[rows, :] = total * state[rows, :] + entry[rows]

    pre_grad = jnp.concatenate([value_grad, b_grad, c_grad], axis=1) * pslope
    back[0:BLOCK, :] = pre_grad
    lin_grad = taps[0:1] * back[sz.taps - 1 : sz.taps - 1 + BLOCK, :]
    for j in range(1, sz.taps):
        at = sz.taps - 1 - j
        lin_grad = lin_grad + taps[j : j + 1] * back[at : at + BLOCK, :]
    for j in range(sz.taps):
        small[j : j + 1, :] += jnp.sum(pre_grad * ext[5 + j : 5 + j + BLOCK, :], axis=0, keepdims=True)
    back[BLOCK : BLOCK + 8, :] = back[0:8, :]
    cat_o[...] = jnp.concatenate([gate_grad, lin_grad.astype(LOW)], axis=1)

    @pl.when(i_step == sz.blocks - 1)
    def _():
        fin_o[...] = state[...]
        rim_o[...] = back[0:8, :]
        sums = small[...]
        flat = [sums[j : j + 1, :ch] for j in range(sz.taps + 2)]
        flat = [jnp.concatenate(flat[j : j + 3], axis=1) for j in range(0, len(flat), 3)]
        flat = flat + [jnp.zeros_like(flat[0])] * (4 - len(flat))
        high, low = split_low(jnp.concatenate(flat, axis=0))
        rest = jnp.zeros((PAD - 8, high.shape[1]), F32)
        small_o[...] = jnp.concatenate([high, low, rest], axis=0).astype(LOW)
        sums_o[...] = sums


def weights_kernel(sz, seq, sc, normed, cat, mixed, scaled, small, common, *refs):
    sc_o, outs, heads, full, wide = refs[0], refs[1 : seq + 1], refs[seq + 1 : -2], refs[-2], refs[-1]
    for i in range(4):
        sc_o[i] = sc[i]
    ch, st = sz.channels, sz.states
    step = sz.chunk
    for q in range(sz.head_axis):
        at = slice(q * step, (q + 1) * step)
        grads = dot(normed[:, at], cat[...], TN)
        full[at, : 2 * ch] = grads[:, : 2 * ch].astype(LOW)
        wide[at, :] = grads[:, 2 * ch :]
        full[at, 2 * ch :] = dot(mixed[:, at], scaled[...], TN).astype(LOW)
    rows = sz.width // seq
    part = rows // sz.head_axis
    for r, out in enumerate(outs):
        out[:rows, :] = full[aligned(lax.rem(sc[2] + r, seq) * rows, rows), :]
        out[rows:, :] = small[...]
    for d, out in enumerate(heads):
        lines = [
            wide[aligned(lax.rem(sc[2] + r, seq) * rows + (sc[1] ^ d) * part, part), :]
            for r in range(seq)
        ]
        out[:PAD, :] = common[...]
        out[PAD:, :] = jnp.concatenate(lines, axis=0).astype(LOW)


def resplit(extra):
    half = extra.shape[0] // 2
    high, low = split_low(extra[:half, :] + extra[half:, :])
    return jnp.concatenate([high, low], axis=0)


def join_kernel(sz, riders, sc, keep, recv, *refs):
    n = sz.head_axis
    more, refs = [refs[i * n : (i + 1) * n] for i in range(riders)], refs[riders * n :]
    sc_o, outs = refs[0], refs[1:]
    rows = sz.rows
    for i in range(4):
        sc_o[i] = sc[i]
    extra = resplit(keep[0, rows:, :].astype(F32) + recv[0, rows:, :].astype(F32))
    for d, out in enumerate(outs):
        out[:rows, :] = (keep[d, :rows, :].astype(F32) + recv[d, :rows, :].astype(F32)).astype(out.dtype)
        out[rows : rows + PAD, :] = extra.astype(out.dtype)
        at = rows + PAD
        for rider in more:
            size = rider[d].shape[0]
            out[at : at + size, :] = rider[d][...].astype(out.dtype)
            at += size


def total_of(parts, rows):
    total = parts[0][rows, :].astype(F32)
    for p in parts[1:]:
        total = total + p[rows, :].astype(F32)
    return total


def output_kernel(sz, layer, sc, *refs):
    n = sz.head_axis
    parts, refs = refs[:n], refs[n:]
    resid = refs[0]
    res_o, low_o, mixed_o, square_o, sc_o = refs[-5:]
    for i in range(4):
        sc_o[i] = sc[i]
    extra = total_of(parts, slice(sz.rows, sz.rows + PAD))
    square = extra[0:8, :HALF] + extra[8:16, :HALF]
    square_o[...] = square
    inv = lax.rsqrt(square / sz.inner + EPS)
    for b in range(sz.blocks):
        rows = slice(b * HALF, (b + 1) * HALF)
        col = column_of(inv[b : b + 1, :], HALF)[:, 0:1]
        mixed = total_of(parts, rows) * col
        res = resid[rows, :].astype(F32) + mixed
        res_o[rows, :] = res
        low_o[rows, :] = res.astype(LOW)
        mixed_o[rows, :] = mixed


def input_kernel(sz, layer, sc, *refs):
    n = sz.head_axis
    parts, refs = refs[:n], refs[n:]
    resid, outg, inv_r, gains = refs[0], refs[1], refs[2], refs[3:5]
    refs = refs[5:]
    if layer == 1:
        mixed = refs[0]
        grad_o, low_o, sc_o = refs[-3:]
    else:
        one_low = refs[0]
        low_o, swap_o, shared_o, sc_o = refs[-4:]
    for i in range(4):
        sc_o[i] = sc[i]
    c, h = sc[0], sc[1]
    first = c == 0
    mine = aligned(h * sz.chunk, sz.chunk)
    gain = pick(c == layer, gains[0][0:1, mine], gains[1][0:1, mine])
    extra = total_of(parts, slice(sz.rows, sz.rows + PAD))
    along = extra[0:8, :HALF] + extra[8:16, :HALF]
    tops, lows = [], []
    for b in range(sz.blocks):
        rows = slice(b * HALF, (b + 1) * HALF)
        at = b * BLOCK
        inv_row = pick(c == 0, inv_r[:, at : at + HALF], inv_r[:, at + HALF : at + BLOCK])
        inv = column_of(inv_row, HALF)[:, 0:1]
        share = column_of(along[b : b + 1, :] / sz.width, HALF)[:, 0:1]
        total = total_of(parts, rows)
        base = resid[rows, :].astype(F32)
        grad = outg[rows, :].astype(F32) + inv * (total * gain - base * (inv * share))
        low = grad.astype(LOW)
        low_o[rows, :] = low
        if layer == 0:
            swap_o[rows, :] = pick(first, one_low[rows, :], low)
        else:
            grad_o[rows, :] = grad
            dots = jnp.sum(low.astype(F32) * mixed[rows, :], axis=1, keepdims=True)
            row = jnp.transpose(jnp.broadcast_to(dots, (HALF, 128)))[0:1, :]
            high, rest = split_low(row)
            tops.append(high)
            lows.append(rest)
    if layer == 1:
        fill = [jnp.zeros((8 - sz.blocks, HALF), F32)] if sz.blocks < 8 else []
        extra = jnp.concatenate(tops + fill + lows + fill, axis=0)
        extra = jnp.concatenate([extra] * (sz.chunk // HALF), axis=1)
        low_o[sz.rows :, :] = extra.astype(LOW)
    else:
        size = shared_o.shape[0]
        at = sz.rows + PAD
        zero = total_of(parts, slice(at, at + size))
        one = total_of(parts, slice(at + size, at + 2 * size))
        zero, one = (jnp.concatenate([resplit(v[:PAD]), v[PAD:]], axis=0) for v in (zero, one))
        shared_o[...] = pick(first, zero, one)
        swap_o[sz.rows :, :] = pick(first, one, zero).astype(LOW)


def sum_kernel(sz, last, sc, *refs):
    if last:
        parts, done, outs = refs[:-3], refs[-3], refs[-2:]
    else:
        parts, outs = refs[:-1], refs[-1:]
    rows = outs[0].shape[0] - PAD
    extra = total_of(parts, slice(rows, rows + PAD))
    high, low = split_low(extra[0:4, :] + extra[4:8, :])
    extra = jnp.concatenate([high, low, jnp.zeros((PAD - 8, extra.shape[1]), F32)], axis=0)
    sums = jnp.concatenate([total_of(parts, slice(0, rows)), extra], axis=0).astype(LOW)
    if last:
        outs[0][...] = pick(sc[0] == 0, sums, done[...])
        outs[1][...] = pick(sc[0] == 0, done[...], sums)
    else:
        outs[0][...] = sums


def final_kernel(sz, seq, sc, own, got, *refs):
    pieces, refs = refs[:-9], refs[-9:]
    gate_o, inner_o, out_o, conv_o, norm_o, skip_o, shared_o, taps_o, gain_o = refs
    c = sc[0]
    ch = sz.channels
    rows = own.shape[0] - PAD
    lane = lax.broadcasted_iota(jnp.int32, skip_o.shape, 1)
    skip = jnp.zeros(skip_o.shape, F32)
    for i in range(2):
        which = pick(i == 0, c, 1 - c)
        to = aligned(which * ch, ch)
        sums = (own if i == 0 else got)[...].astype(F32)
        gate_o[:, to] = sums[:rows, :ch]
        inner_o[:, to] = sums[:rows, ch : 2 * ch]
        out_o[to, :] = jnp.transpose(sums[:rows, 2 * ch :])
        lines = sums[rows : rows + 4, :] + sums[rows + 4 : rows + 8, :]
        for j in range(sz.taps):
            conv_o[j : j + 1, to] = lines[j // 3 : j // 3 + 1, (j % 3) * ch : (j % 3 + 1) * ch]
        norm_o[:, to] = lines[1:2, ch : 2 * ch]
        skips = lines[1:2, 2 * ch :]
        for q in range(sz.heads):
            part = jnp.sum(per_head(skips, q, sz.head_width), axis=1, keepdims=True)
            skip = jnp.where(lane == which * sz.heads + q, part, skip)
    skip_o[...] = skip
    total = total_of(pieces, slice(BLOCK, None))
    shared_o[...] = total[PAD:]
    common = total[: PAD // 2] + total[PAD // 2 : PAD]
    place = sc[2] * sz.head_axis + sc[1]
    span = common.shape[1]
    size = span // (seq * sz.head_axis)
    turned = pltpu.roll(common, lax.rem(span - place * size, span), 1)
    taps_o[...] = turned[: sz.taps, :size]
    size = sz.width // (seq * sz.head_axis)
    at = place * size
    line = jnp.broadcast_to(line_of(common, sz.taps + at // span), common.shape)
    turned = pltpu.roll(line, lax.rem(span - lax.rem(at, span), span), 1)
    gain_o[...] = turned[:1, :size]


def slice_kernel(sz, slots, sc, order, tokens, rates, *refs):
    outs, sc_o, sems = refs[:slots], refs[slots], refs[slots + 1]
    copies = []
    for r in range(slots):
        rows = tokens.at[order[lax.rem(sc[3] + r, slots)], aligned(sc[0] * HALF, HALF), :]
        copies.append(pltpu.make_async_copy(rows, outs[r].at[:HALF], sems.at[r]))
    for copy in copies:
        copy.start()
    for i in range(4):
        sc_o[i] = sc[i]
    for r in range(slots):
        first, rest = split_low(rates[0, order[lax.rem(sc[3] + r, slots)]])
        second, rest = split_low(rest)
        lines = jnp.concatenate([first, second, rest, jnp.zeros_like(rest)], axis=1)
        lines = jnp.concatenate([lines, jnp.zeros_like(lines)], axis=0)
        outs[r][HALF:, :] = lines.astype(LOW)
    for copy in copies:
        copy.wait()


def rates_of(piece):
    lines = piece[HALF:, :].astype(F32)[:8, :]
    return (lines[:, :BLOCK] + lines[:, BLOCK : 2 * BLOCK]) + lines[:, 2 * BLOCK : 3 * BLOCK]


def pack_kernel(sz, sc, order, grads, gate, inner, shared, out, in_gain, conv_i, conv_s, skip, norm, *refs):
    w_o, o_o, mine_o, send_o, sems = *refs[:4], refs[-1]
    c, h = sc[0], sc[1]
    ch = sz.channels
    outs = refs[4:-1]
    slices = []
    for r, to in enumerate(outs):
        rows = grads.at[order[lax.rem(sc[3] + r, len(outs))], aligned(c * HALF, HALF), :]
        slices.append(pltpu.make_async_copy(rows, to, sems.at[4 + r]))
    cols = aligned((1 - c) * ch, ch)
    rows = aligned((h * 2 + 1 - c) * ch, ch)
    copies = [
        pltpu.make_async_copy(gate.at[0, :, cols], w_o.at[:, :ch], sems.at[0]),
        pltpu.make_async_copy(inner.at[0, :, cols], w_o.at[:, ch : 2 * ch], sems.at[1]),
        pltpu.make_async_copy(shared.at[0], w_o.at[:, 2 * ch :], sems.at[2]),
        pltpu.make_async_copy(out.at[0, rows, :], o_o, sems.at[3]),
        *slices,
    ]
    for copy in copies:
        copy.start()
    for which, ref in ((c, mine_o), (1 - c, send_o)):
        at = aligned(which * ch, ch)
        ref[...] = jnp.zeros_like(ref)
        ref[0:1, :] = in_gain[...]
        ref[1 : 1 + sz.taps, :ch] = conv_i[0, :, at]
        ref[1 : 1 + sz.taps, ch : sz.lin] = conv_s[0]
        ref[5:6, :ch] = norm[:, at]
        low = spread(skip[...], 0, sz.heads, sz.head_width)
        high = spread(skip[...], sz.heads, sz.heads, sz.head_width)
        ref[6:7, :ch] = pick(which == 0, low, high)
    for copy in copies:
        copy.wait()


def decay_table(rate, c, n):
    lane = lax.broadcasted_iota(jnp.int32, rate.shape, 1)
    cum = rate
    step = 1
    while step < BLOCK:
        cum = cum + jnp.where(lane >= step, pltpu.roll(cum, step, 1), 0.0)
        step *= 2
    end = cum[:, BLOCK - 1 :]
    lines = [cum, jnp.exp(cum), jnp.exp(end - cum) * -rate, jnp.log(-rate) - cum]
    low = jnp.concatenate([v[:n] for v in lines], axis=0)
    high = jnp.concatenate([v[n:] for v in lines], axis=0)
    return pick(c == 0, low, high)


def leave_kernel(sz, slots, riders, sc, zero_own, zero_other, one_own, one_other, *refs):
    c = sc[0]
    if riders:
        shared, refs = refs[0], refs[1:]
        total = shared[...] + one_other[sz.rows :, :].astype(F32)
        extra = resplit(total[:PAD])
        part = (total.shape[0] - PAD) // riders
    outs = refs[:slots]
    for i in range(4):
        refs[slots][i] = sc[i]
    for r in range(slots):
        rows = aligned(lax.rem(sc[3] + r, slots) * HALF, HALF)
        own = pick(c == 0, zero_own[rows, :], one_own[rows, :])
        other = pick(c == 0, zero_other[rows, :], one_other[rows, :])
        put_pair(outs[r], c, own, other)
        if riders:
            lines = [extra, total[PAD + r * part : PAD + (r + 1) * part]]
            outs[r][BLOCK:, :] = jnp.concatenate(lines, axis=0).astype(LOW)


def home_kernel(slots, sc, *refs):
    early, late, out, grad = refs[:slots], refs[slots : 2 * slots], refs[-3], refs[-2]
    for i in range(4):
        refs[-1][i] = sc[i]
    first = sc[0] == 0
    for r in range(slots):
        at = lax.rem(sc[3] - r + slots, slots)
        out[at] = pick(first, early[r][...], late[r][:BLOCK, :]).astype(F32)
        grad[at] = pick(first, late[r][:BLOCK, :], early[r][...]).astype(F32)


def whole(shape):
    return pl.BlockSpec(shape, lambda *_: (0,) * len(shape))


def per_device(
    tokens,
    slot_order,
    log_decay,
    grad_out,
    in_gain,
    w_gate,
    w_inner,
    w_shared,
    conv_inner,
    conv_shared,
    d_skip,
    norm_gain,
    w_out,
):
    slots = tokens.shape[0]
    span = tokens.shape[1]
    width = tokens.shape[2]
    seq = lax.axis_size("seq")
    head_axis = lax.axis_size("head")
    cores = lax.axis_size("section")
    spans = seq // slots
    c = lax.axis_index("section")
    z = lax.axis_index("seq")
    h = lax.axis_index("head")
    k = lax.rem(z, slots)
    inner_dev = w_gate.shape[2]
    channels = inner_dev // cores
    shared = w_shared.shape[2]
    heads_dev = d_skip.shape[1]
    taps = conv_inner.shape[1]
    sz = Sizes(
        slots * span // BLOCK,
        width,
        channels,
        heads_dev // cores,
        shared // 2,
        taps,
        head_axis,
        inner_dev * head_axis,
    )
    first = c == 0
    swap = [(0, 1), (1, 0)]
    nb, tok, rows, chunk = sz.blocks, sz.tokens, sz.rows, sz.chunk

    def cross(x):
        return lax.ppermute(x, "section", swap)

    def turn(x, r):
        pairs = [(i, i // slots * slots + (i % slots + r) % slots) for i in range(seq)]
        return lax.ppermute(x, "seq", pairs) if r else x

    def over_heads(x, d):
        return x if d == 0 else lax.ppermute(x, "head", [(i, i ^ d) for i in range(head_axis)])

    def next_span(x, way):
        pairs = [(i, i + way * slots) for i in range(seq) if 0 <= i + way * slots < seq]
        return lax.ppermute(x, "seq", pairs)

    def shape(dims, dtype):
        return jax.ShapeDtypeStruct(dims, dtype)

    prefetch = functools.partial(pltpu.PrefetchScalarGridSpec, num_scalar_prefetch=1)
    options = pltpu.CompilerParams(vmem_limit_bytes=VMEM_BYTES)
    from_hbm = pltpu.CompilerParams(vmem_limit_bytes=ALL_VMEM_BYTES)
    anywhere = pl.BlockSpec(memory_space=pl.ANY)
    smem = pl.BlockSpec(memory_space=pltpu.SMEM)
    vmem = pl.BlockSpec(memory_space=pltpu.VMEM)
    index_shape = shape((4,), jnp.int32)

    def cost(flops, moved):
        return pl.CostEstimate(flops=int(flops), bytes_accessed=int(moved), transcendentals=0)

    def to_members(pieces):
        return [turn(x, r) for r, x in enumerate(pieces)]

    sc = jnp.stack([c, h, z, k]).astype(jnp.int32)
    *tok_slices, sc = pl.pallas_call(
        functools.partial(slice_kernel, sz, slots),
        in_specs=[smem, smem, anywhere, vmem],
        out_specs=[vmem] * slots + [smem],
        out_shape=[shape((HALF + PAD, width), LOW)] * slots + [index_shape],
        scratch_shapes=[pltpu.SemaphoreType.DMA((slots,))],
        compiler_params=from_hbm,
    )(sc, slot_order, tokens, log_decay)
    tok_pieces = to_members(tok_slices)
    tok_others = [cross(x) for x in tok_pieces]

    wide = 2 * channels + shared
    w_sent, o_sent, pv_mine, pv_sent, *out_slices = pl.pallas_call(
        functools.partial(pack_kernel, sz),
        in_specs=[smem, smem] + [anywhere] * 5 + [vmem] * 5,
        out_specs=[vmem] * (4 + slots),
        out_shape=[
            shape((width, wide), LOW),
            shape((channels, width), LOW),
            shape((16, width), F32),
            shape((16, width), F32),
        ]
        + [shape((HALF, width), LOW)] * slots,
        scratch_shapes=[pltpu.SemaphoreType.DMA((4 + slots,))],
        compiler_params=from_hbm,
    )(
        sc, slot_order, grad_out, w_gate, w_inner, w_shared, w_out,
        in_gain, conv_inner, conv_shared, d_skip, norm_gain,
    )
    raw = [w_gate, w_inner, w_shared, w_out]
    sent = [cross(w_sent), cross(o_sent)]
    gains = [pv_mine, cross(pv_sent)]

    def span_total(table):
        ends = table[: sz.heads, BLOCK - 1 :: BLOCK]
        return jnp.repeat(jnp.exp(jnp.sum(ends, axis=1)), sz.head_width)[:, None]

    parts_shape = shape((head_axis, rows + PAD, chunk), LOW)
    weight_specs = [anywhere] * 6
    wide_weights = pltpu.VMEM((width, wide), LOW)
    out_weights = pltpu.VMEM((channels, width), LOW)
    copy_sems = pltpu.SemaphoreType.DMA((4,))
    dense = 2 * tok * width * (wide + channels)

    def forward(layer, sc, sources):
        def at(b, _):
            return (b, 0)

        piece = pl.BlockSpec((HALF, chunk), at)
        table = pl.BlockSpec((16, BLOCK), lambda b, _: (0, b))
        if layer == 0:
            src_specs = [whole((HALF + PAD, width))] * (2 * slots)
            more_specs = [table, table]
            more_shapes = [shape((16, tok), F32)] * 2
        else:
            src_specs = [piece] * (2 * head_axis) + [whole((HALF, width))] * (2 * slots) + [table]
            more_specs = [pl.BlockSpec((BLOCK, width), at)]
            more_shapes = [shape((tok, width), LOW)]

        last = [] if layer == 0 else [turned[3]]

        def call(halo, begin):
            return pl.pallas_call(
                functools.partial(forward_kernel, sz, layer, slots),
                grid_spec=prefetch(
                    grid=(nb,),
                    in_specs=src_specs
                    + [whole((16, width)), whole((16, width))]
                    + weight_specs
                    + [whole((8, sz.lin)), whole((channels, sz.states))]
                    + [whole(x.shape) for x in last],
                    out_specs=[
                        pl.BlockSpec((BLOCK, width), at),
                        pl.BlockSpec((BLOCK, channels), at),
                        pl.BlockSpec((BLOCK, sz.lin), at),
                        pl.BlockSpec((BLOCK, channels), at),
                        pl.BlockSpec((1, channels, sz.states), lambda b, _: (b, 0, 0)),
                        pl.BlockSpec((1, BLOCK), lambda b, _: (0, b)),
                        pl.BlockSpec((2, BLOCK), lambda b, _: (0, b)),
                        pl.BlockSpec((BLOCK, channels), at),
                        whole((channels, sz.states)),
                        smem,
                        piece,
                    ]
                    + more_specs,
                    scratch_shapes=[
                        pltpu.VMEM((BLOCK, width), LOW),
                        pltpu.VMEM((BLOCK, width), LOW),
                        wide_weights,
                        pltpu.VMEM((BLOCK + 8, sz.lin), F32),
                        pltpu.VMEM((channels, sz.states), F32),
                        copy_sems,
                    ],
                ),
                out_shape=[
                    shape((tok, width), LOW),
                    shape((tok, channels), F32),
                    shape((tok, sz.lin), LOW),
                    shape((tok, channels), F32),
                    shape((nb, channels, sz.states), LOW),
                    shape((1, tok), F32),
                    shape((2, tok), F32),
                    shape((tok, channels), LOW),
                    shape((channels, sz.states), F32),
                    index_shape,
                    shape((rows, chunk), LOW),
                ]
                + more_shapes,
                compiler_params=options,
                cost_estimate=cost(6 * dense, 16e6),
            )(sc, *sources, *gains, *raw, *sent, halo, begin, *last)

        halo = jnp.zeros((8, sz.lin), F32)
        begin = jnp.zeros((channels, sz.states), F32)
        if spans == 1:
            return call(halo, begin), halo
        trial = call(halo, begin)
        halo = next_span(trial[2][tok - 8 :].astype(F32), 1)
        local = call(halo, begin)[8]
        total = span_total(trial[11] if layer == 0 else sources[-1])
        for _ in range(spans - 1):
            begin = next_span(total * begin + local, 1)
        return call(halo, begin), halo

    def backward(layer, sc, sources, saved, decays, halo, deps):
        def at(i, _):
            return (nb - 1 - i, 0)

        if layer == 0:
            src_specs = [whole(s.shape) for s in sources]
        else:
            stat = pl.BlockSpec((2, BLOCK), lambda i, _: (0, nb - 1 - i))
            src_specs = [pl.BlockSpec((BLOCK, width), at)] + [stat] * head_axis
        gl, lin, ssd, inc = saved
        mixed_spec = [pl.BlockSpec((BLOCK, width), at)] if layer == 0 else []
        mixed_shape = [shape((tok, width), LOW)] if layer == 0 else []

        def call(halo_grad, begin):
            return pl.pallas_call(
                functools.partial(backward_kernel, sz, layer, len(deps)),
                grid_spec=prefetch(
                    grid=(nb,),
                    in_specs=src_specs
                    + [
                        pl.BlockSpec((BLOCK, channels), at),
                        whole(lin.shape),
                        pl.BlockSpec((BLOCK, channels), at),
                        pl.BlockSpec((1, channels, sz.states), lambda i, _: (nb - 1 - i, 0, 0)),
                        pl.BlockSpec((16, BLOCK), lambda i, _: (0, nb - 1 - i)),
                        whole((16, width)),
                        whole((16, width)),
                        whole((width, channels)),
                        whole((8, sz.lin)),
                        whole((8, sz.lin)),
                        whole((channels, sz.states)),
                    ]
                    + [anywhere] * len(deps),
                    out_specs=[
                        pl.BlockSpec((BLOCK, wide), at),
                        pl.BlockSpec((BLOCK, channels), at),
                        whole((PAD, 3 * channels)),
                        whole((8, sz.lin)),
                        whole((channels, sz.states)),
                        whole((8, sz.lin)),
                        smem,
                    ]
                    + mixed_spec,
                    scratch_shapes=[
                        pltpu.VMEM((BLOCK, width), LOW),
                        pltpu.VMEM((BLOCK + 8, sz.lin), F32),
                        pltpu.VMEM((BLOCK + 8, sz.lin), F32),
                        pltpu.VMEM((channels, sz.states), F32),
                        pltpu.VMEM((PAD, HALF), F32),
                        pltpu.VMEM((8, sz.lin), F32),
                    ],
                ),
                out_shape=[
                    shape((tok, wide), LOW),
                    shape((tok, channels), LOW),
                    shape((PAD, 3 * channels), LOW),
                    shape((8, sz.lin), F32),
                    shape((channels, sz.states), F32),
                    shape((8, sz.lin), F32),
                    index_shape,
                ]
                + mixed_shape,
                compiler_params=options,
                cost_estimate=cost(8 * dense, 16e6),
            )(
                sc, *sources, gl, lin, ssd, inc, decays, *gains, turned[2 + layer],
                halo, halo_grad, begin, *deps,
            )

        halo_grad = jnp.zeros((8, sz.lin), F32)
        begin = jnp.zeros((channels, sz.states), F32)
        if spans == 1:
            return call(halo_grad, begin)
        local = call(halo_grad, begin)[4]
        for _ in range(spans - 1):
            begin = next_span(span_total(decays) * begin + local, -1)
        halo_grad = next_span(call(halo_grad, begin)[5], -1)
        return call(halo_grad, begin)

    def project(layer, sc, unit, stats, deps):
        return pl.pallas_call(
            functools.partial(project_kernel, sz, layer, len(deps)),
            in_specs=[smem, vmem, vmem] + weight_specs + [anywhere] * len(deps),
            out_specs=[vmem, vmem, smem],
            out_shape=[parts_shape, parts_shape, index_shape],
            scratch_shapes=[out_weights, copy_sems],
            compiler_params=options,
            cost_estimate=cost(dense / 4, 4e6),
        )(sc, unit, stats, *raw, *sent, *deps)

    def lift(layer, sc, cat, normed, small, deps):
        return pl.pallas_call(
            functools.partial(lift_kernel, sz, layer, len(deps)),
            in_specs=[smem] + [vmem] * 6 + [anywhere] * len(deps),
            out_specs=[vmem, vmem, smem, vmem],
            out_shape=[parts_shape, parts_shape, index_shape, shape((PAD, chunk), LOW)],
            scratch_shapes=[pltpu.VMEM((8, width), F32)],
            compiler_params=options,
            cost_estimate=cost(dense, 8e6),
        )(sc, cat, normed, *gains, small, turned[layer], *deps)

    def scatter(sc, keep, send, *riders):
        size = rows + PAD + sum(rider[0].shape[0] for rider in riders)
        flat = [x for rider in riders for x in rider]
        joined = pl.pallas_call(
            functools.partial(join_kernel, sz, len(riders)),
            in_specs=[smem] + [vmem] * (2 + len(flat)),
            out_specs=[smem] + [vmem] * head_axis,
            out_shape=[index_shape, shape((size, chunk), F32)]
            + [shape((size, chunk), LOW)] * (head_axis - 1),
            compiler_params=options,
        )(sc, keep, cross(send), *flat)
        return [over_heads(joined[1 + d], d) for d in far_first(head_axis)], joined[0]

    def gather(low):
        own = [over_heads(low, d) for d in far_first(head_axis)]
        return own + [cross(x) for x in own]

    turned = pl.pallas_call(
        functools.partial(turn_kernel, sz),
        in_specs=[smem] + weight_specs,
        out_specs=[vmem] * 4,
        out_shape=[shape((wide, width), LOW)] * 2 + [shape((width, channels), LOW)] * 2,
        scratch_shapes=[wide_weights, out_weights, copy_sems],
        compiler_params=options,
        cost_estimate=cost(1e9, 8e6),
    )

    def section_output(layer, sc, parts, resid, deps=()):
        return pl.pallas_call(
            functools.partial(output_kernel, sz, layer),
            in_specs=[smem] + [vmem] * (head_axis + 1) + [anywhere] * len(deps),
            out_specs=[vmem] * 4 + [smem],
            out_shape=[
                shape((rows, chunk), F32),
                shape((rows, chunk), LOW),
                shape((rows, chunk), F32),
                shape((8, HALF), F32),
                index_shape,
            ],
            compiler_params=options,
        )(sc, *parts, resid, *deps)

    part = width // seq
    columns = 3 * channels
    share = part // head_axis
    shared_size = seq * share + PAD

    def section_input(layer, sc, parts, *others, deps=()):
        if layer == 0:
            outs = [
                shape((rows + PAD, chunk), LOW),
                shape((rows + shared_size, chunk), LOW),
                shape((shared_size, chunk), F32),
            ]
        else:
            outs = [shape((rows, chunk), F32), shape((rows + PAD, chunk), LOW)]
        return pl.pallas_call(
            functools.partial(input_kernel, sz, layer),
            in_specs=[smem] + [vmem] * (head_axis + len(others)) + [anywhere] * len(deps),
            out_specs=[vmem] * len(outs) + [smem],
            out_shape=outs + [index_shape],
            compiler_params=options,
        )(sc, *parts, *others, *deps)

    def weight_grads(sc, normed, cat, mixed, scaled, small, common):
        outs = pl.pallas_call(
            functools.partial(weights_kernel, sz, seq),
            in_specs=[smem] + [vmem] * 6,
            out_specs=[smem] + [vmem] * (seq + head_axis),
            out_shape=[index_shape]
            + [shape((part + PAD, columns), LOW)] * seq
            + [shape((shared_size, shared), LOW)] * head_axis,
            scratch_shapes=[pltpu.VMEM((width, columns), LOW), pltpu.VMEM((width, shared), F32)],
            compiler_params=options,
            cost_estimate=cost(4 * dense, 12e6),
        )(sc, normed, cat, mixed, scaled, small, common)
        return over_seq(outs[1 : 1 + seq]), outs[1 + seq :], outs[0]

    def over_seq(chunks):
        pieces = [chunks[0]]
        for r in range(1, seq):
            pairs = [(i, (i + r) % seq) for i in range(seq)]
            pieces.append(lax.ppermute(chunks[r], "seq", pairs))
        return pieces

    def leave(sc, *arrays, riders=0):
        size = BLOCK + (share + PAD if riders else 0)
        pieces = pl.pallas_call(
            functools.partial(leave_kernel, sz, slots, riders),
            in_specs=[smem] + [vmem] * len(arrays),
            out_specs=[vmem] * slots + [smem],
            out_shape=[shape((size, chunk), LOW)] * slots + [index_shape],
            compiler_params=options,
        )(sc, *arrays)
        return to_members(pieces[:slots]), pieces[slots]

    out_pieces = to_members(out_slices)
    fw0, halo0 = forward(0, sc, tok_pieces + tok_others)
    base0, decays = fw0[10], fw0[11:13]
    pr0 = project(0, fw0[9], fw0[7], fw0[6], [out_pieces[1], out_pieces[-1]])
    out_others = [cross(x) for x in out_pieces]
    parts, sc_join = scatter(sc, pr0[0], pr0[1])
    turned = turned(sc_join, *raw, *sent)
    res1, low1, mixed0, square0, unused = section_output(0, sc, parts, base0, turned)
    pieces1 = gather(low1)
    square_other = cross(square0)

    fw1, halo1 = forward(1, sc, pieces1 + out_pieces + out_others + [decays[1]])
    stat = fw1[6] + cross(fw1[6])
    stats = [stat] + [over_heads(stat, d) for d in range(1, head_axis)]
    pr1 = project(1, fw1[9], fw1[7], fw1[6], [])
    parts_out, sc_out = scatter(sc, pr1[0], pr1[1])
    bw1 = backward(1, sc_out, [fw1[11]] + stats, fw1[1:5], decays[1], halo1, [])
    lf1 = lift(1, bw1[6], bw1[0], fw1[0], bw1[3], parts_out[1:])
    weights1, heads1, sc_weights = weight_grads(
        lf1[2], fw1[0], bw1[0], fw1[11], bw1[1], bw1[2], lf1[3]
    )
    parts, sc_join = scatter(sc_weights, lf1[0], lf1[1])
    igrad1, glow1, sc_in = section_input(
        1, sc_join, parts, res1, fw1[10], fw1[5], *gains, mixed0,
        deps=[weights1[1], weights1[-1]],
    )
    piecesg = gather(glow1)

    early, unused = leave(sc_in, low1, pieces1[head_axis], glow1, piecesg[head_axis])
    bw0 = backward(
        0, sc, piecesg + [square0, square_other], fw0[1:5], decays[0], halo0, weights1[2:-1]
    )
    lf0 = lift(0, bw0[6], bw0[0], fw0[0], bw0[3], [early[1], early[-1]])
    weights0, heads0, sc_weights = weight_grads(
        lf0[2], fw0[0], bw0[0], bw0[7], bw0[1], bw0[2], lf0[3]
    )
    parts, sc_join = scatter(sc_weights, lf0[0], lf0[1], heads0, heads1)

    unused, low2, unused_mixed, unused_square, sc_out = section_output(1, sc_in, parts_out, res1)
    glow0, to_other, shared_own, sc_end = section_input(
        0, sc_out, parts, base0, igrad1, fw0[5], *gains, low2,
        deps=weights0[1:-1] + early[2:-1],
    )
    got = cross(to_other)
    if spans == 1:
        late, sc_end = leave(sc_end, glow0, got, low2, got, shared_own, riders=seq)
        shared_parts = late
    else:
        late, sc_end = leave(sc_end, glow0, got, low2, got)
        total = shared_own + got[rows:].astype(F32)
        extra = resplit(total[:PAD])
        fill = jnp.zeros((BLOCK, shared), F32)
        chunks = [
            jnp.concatenate([fill, extra, total[PAD + r * share : PAD + (r + 1) * share]])
            for r in range(seq)
        ]
        shared_parts = over_seq([x.astype(LOW) for x in chunks])
    section_out, input_grad, sc_end = pl.pallas_call(
        functools.partial(home_kernel, slots),
        in_specs=[smem] + [vmem] * (2 * slots),
        out_specs=[vmem, vmem, smem],
        out_shape=[shape((slots, BLOCK, chunk), F32)] * 2 + [index_shape],
        compiler_params=options,
    )(sc, *early, *late)

    def summed(sc, pieces, *done):
        return pl.pallas_call(
            functools.partial(sum_kernel, sz, bool(done)),
            in_specs=[smem] + [vmem] * (seq + len(done)),
            out_shape=[shape((part + PAD, columns), LOW)] * (1 + len(done)),
            compiler_params=options,
        )(sc, *pieces, *done)

    own_sums, other_sums = summed(sc_end, weights0, *summed(sc_in, weights1))
    final = pl.pallas_call(
        functools.partial(final_kernel, sz, seq),
        in_specs=[smem] + [vmem] * (2 + seq),
        out_shape=[
            shape((part, inner_dev), F32),
            shape((part, inner_dev), F32),
            shape((inner_dev, part), F32),
            shape((taps, inner_dev), F32),
            shape((1, inner_dev), F32),
            shape((1, heads_dev), F32),
            shape((share, shared), F32),
            shape((taps, shared // (seq * head_axis)), F32),
            shape((1, width // (seq * head_axis)), F32),
        ],
        compiler_params=options,
    )(sc, own_sums, cross(other_sums), *shared_parts)
    return (
        section_out[None],
        input_grad[None],
        final[8],
        final[0][None],
        final[1][None],
        final[6][None],
        final[3][None],
        final[7][None],
        final[5],
        final[4],
        final[2][None],
    )


def solution(mesh):
    placed = (
        P(None, "seq", None),
        P(),
        P("section", None, "head", "seq"),
        P(None, "seq", None),
        P("section", None),
        P("section", None, "head"),
        P("section", None, "head"),
        P("section", None, None),
        P("section", None, "head"),
        P("section", None, None),
        P("section", "head"),
        P("section", "head"),
        P("section", None, None),
    )
    return jax.shard_map(
        per_device,
        mesh=mesh,
        in_specs=placed,
        out_specs=(
            P("section", None, "seq", "head"),
            P("section", None, "seq", "head"),
            P("section", ("seq", "head")),
            P("section", "seq", "head"),
            P("section", "seq", "head"),
            P("section", ("seq", "head"), None),
            P("section", None, "head"),
            P("section", None, ("seq", "head")),
            P("section", "head"),
            P("section", "head"),
            P("section", "head", "seq"),
        ),
        check_vma=False,
    )
```

```python
import functools

import jax
import jax.numpy as jnp
from jax import lax
from jax.experimental import pallas as pl
from jax.experimental.pallas import tpu as pltpu
from jax.sharding import PartitionSpec as P

BLOCK = 256
HALF = BLOCK // 2
PAD = 16
EPS = 1e-05
F32 = jnp.float32
LOW = jnp.bfloat16
HIDDEN = -1e30
NN = ((1,), (0,))
NT = ((1,), (1,))
TN = ((0,), (0,))
VMEM_BYTES = 50 * 1024 * 1024
ALL_VMEM_BYTES = 63 * 1024 * 1024


def dot(a, b, dims):
    return lax.dot_general(a, b, (dims, ((), ())), preferred_element_type=F32)


def aligned(start, size):
    return pl.ds(pl.multiple_of(start, size), size)


def spread(cols, first, count, width):
    rows = cols.shape[0]
    lane = lax.broadcasted_iota(jnp.int32, (rows, count * width), 1)
    out = jnp.broadcast_to(cols[:, first : first + 1], (rows, count * width))
    for h in range(1, count):
        out = jnp.where(lane >= h * width, cols[:, first + h : first + h + 1], out)
    return out


def per_head(array, h, width):
    lane = lax.broadcasted_iota(jnp.int32, array.shape, 1)
    inside = (lane >= h * width) & (lane < (h + 1) * width)
    return jnp.where(inside, array, jnp.zeros_like(array))


def split_low(value):
    high = value.astype(LOW).astype(F32)
    return high, value - high


def column_of(row, size):
    return jnp.transpose(jnp.broadcast_to(row, (128, size)))


def sigmoid(v):
    return 0.5 * jnp.tanh(0.5 * v) + 0.5


def pick(flag, a, b):
    return jnp.where(flag, a, b)


class Sizes:
    def __init__(self, blocks, width, channels, heads, states, taps, head_axis, inner):
        self.blocks = blocks
        self.width = width
        self.channels = channels
        self.heads = heads
        self.head_width = channels // heads
        self.states = states
        self.lin = channels + 2 * states
        self.taps = taps
        self.head_axis = head_axis
        self.chunk = width // head_axis
        self.rows = blocks * HALF
        self.tokens = blocks * BLOCK
        self.inner = inner


def weight_copies(sz, layer, c, h, raw, got, wv, ov, sems):
    gate, inner, shared, out = raw
    ch = sz.channels
    cols = aligned(c * ch, ch)
    rows = aligned((h * 2 + c) * ch, ch)
    own, sent = [], []
    if wv is not None:
        own += [
            (gate.at[0, :, cols], wv.at[:, :ch]),
            (inner.at[0, :, cols], wv.at[:, ch : 2 * ch]),
            (shared.at[0], wv.at[:, 2 * ch :]),
        ]
        sent += [(got[0], wv)]
    if ov is not None:
        own += [(out.at[0, rows, :], ov)]
        sent += [(got[1], ov)]
    return [
        (c == layer, [pltpu.make_async_copy(p, q, sems.at[i]) for i, (p, q) in enumerate(own)]),
        (c != layer, [pltpu.make_async_copy(p, q, sems.at[i]) for i, (p, q) in enumerate(sent)]),
    ]


def run_copies(choices, start, wait):
    for flag, copies in choices:

        @pl.when(flag)
        def _(copies=copies):
            if start:
                for copy in copies:
                    copy.start()
            if wait:
                for copy in copies:
                    copy.wait()


def put_ordered(sz, dst, c, k, b, own, other):
    for r in range(len(own)):

        @pl.when(lax.rem(k - b + len(own), len(own)) == r)
        def _(r=r):
            put_pair(dst, c, own[r][:HALF, :], other[r][:HALF, :])


def put_pair(dst, c, own, other):
    dst[aligned(c * HALF, HALF), :] = own
    dst[aligned((1 - c) * HALF, HALF), :] = other


def far_first(count):
    return [0] + list(range(count - 1, 0, -1))


def put_pieces(sz, dst, c, h, own, other):
    own, other = (dict(zip(far_first(sz.head_axis), side)) for side in (own, other))
    for d in range(sz.head_axis):
        cols = aligned((h ^ d) * sz.chunk, sz.chunk)
        dst[aligned(c * HALF, HALF), cols] = own[d]
        dst[aligned((1 - c) * HALF, HALF), cols] = other[d]


def line_of(table, at):
    line = lax.broadcasted_iota(jnp.int32, table.shape, 0)
    return jnp.sum(jnp.where(line == at, table, 0.0), axis=0, keepdims=True)


def conv_forward(sz, ext, taps):
    pre = taps[0:1] * ext[5 : 5 + BLOCK, :]
    for j in range(1, sz.taps):
        pre = pre + taps[j : j + 1] * ext[5 + j : 5 + j + BLOCK, :]
    return pre


def decay_of(sz, cols, rp, h, mask):
    rows = cols[:, h : h + 1] + rp[12 + h : 13 + h, :]
    return jnp.exp(jnp.where(mask, rows, HIDDEN))


def lower_mask():
    t = lax.broadcasted_iota(jnp.int32, (BLOCK, BLOCK), 0)
    s = lax.broadcasted_iota(jnp.int32, (BLOCK, BLOCK), 1)
    return t >= s


def forward_kernel(sz, layer, slots, sc, *refs):
    n = sz.head_axis
    sources = 2 if layer == 0 else 2 * n + 2 * slots
    src, refs = refs[:sources], refs[sources:]
    if layer == 1:
        table, refs = refs[0], refs[1:]
    gains, raw, got, halo, begin = refs[0:2], refs[2:6], refs[6:8], refs[8], refs[9]
    if layer == 1:
        ov, refs = refs[10], refs[1:]
    normed_o, gl_o, lin_o, ssd_o, inc_o, inv_o, part_o, unit_o, fin_o, sc_o, base_o = refs[10:21]
    refs = refs[21:]
    if layer == 1:
        mixed_o, refs = refs[0], refs[1:]
    else:
        tables_o, refs = refs[0:2], refs[2:]
    xs, ms, wv, ext, state, sems = refs
    b = pl.program_id(0)
    c, h, k = sc[0], sc[1], sc[3]
    ch, st = sz.channels, sz.states
    copies = weight_copies(sz, layer, c, h, raw, got, wv, None, sems)

    @pl.when(b == 0)
    def _():
        run_copies(copies, True, False)
        ext[0:8, :] = halo[...]
        state[...] = begin[...]
        for i in range(4):
            sc_o[i] = sc[i]

    mine = aligned(c * HALF, HALF)
    cols = aligned(h * sz.chunk, sz.chunk)
    if layer == 0:
        own, other = src[0][0], src[1][0]
        put_pair(xs, c, own[:HALF], other[:HALF])
        base_o[...] = xs[mine, cols]
        own = decay_table(rates_of(own), c, sz.heads)
        other = decay_table(rates_of(other), c, sz.heads)
        tables_o[0][...] = pick(c == 0, own, other)
        tables_o[1][...] = pick(c == 0, other, own)
        rp = tables_o[0][...]
    else:
        put_pieces(sz, xs, c, h, [r[...] for r in src[:n]], [r[...] for r in src[n : 2 * n]])
        put_ordered(sz, ms, c, k, b, src[2 * n : 2 * n + slots], src[2 * n + slots :])
        base_o[...] = ms[mine, cols]
        mixed_o[...] = ms[...]
        rp = table[...]

    pv = pick(c == layer, gains[0][...], gains[1][...])
    x = xs[...].astype(F32)
    inv_in = lax.rsqrt(jnp.mean(x * x, axis=1, keepdims=True) + EPS)
    normed = (x * inv_in * pv[0:1, : sz.width]).astype(LOW)
    normed_o[...] = normed

    @pl.when(b == 0)
    def _():
        run_copies(copies, False, True)

    proj = dot(normed, wv[...], NN)
    gl = proj[:, :ch]
    gl_o[...] = gl
    lin = proj[:, ch:].astype(LOW)
    lin_o[...] = lin
    ext[8 : 8 + BLOCK, :] = lin.astype(F32)
    pre = conv_forward(sz, ext, pv[1:5, : sz.lin])
    ext[0:8, :] = ext[BLOCK : BLOCK + 8, :]
    act = (pre * sigmoid(pre)).astype(LOW)
    values, bm, cm = act[:, :ch], act[:, ch : ch + st], act[:, ch + st :]

    cols = jnp.transpose(rp)
    mask = lower_mask()
    gram = dot(cm, bm, NT)
    mixes, parts = [], []
    for i in range(sz.heads):
        mixes.append((gram * decay_of(sz, cols, rp, i, mask)).astype(LOW))
        parts.append(per_head(values, i, sz.head_width))
    intra = dot(jnp.concatenate(mixes, axis=1), jnp.concatenate(parts, axis=0), NN)

    low_state = state[...].astype(LOW)
    inc_o[0] = low_state
    ecum = spread(cols, sz.heads, sz.heads, sz.head_width)
    inter = dot(cm, low_state, NT) * ecum
    vf = values.astype(F32)
    carried = (vf * spread(cols, 2 * sz.heads, sz.heads, sz.head_width)).astype(LOW)
    local = dot(carried, bm, TN)
    for i in range(sz.heads):
        rows = slice(i * sz.head_width, (i + 1) * sz.head_width)
        total = cols[BLOCK - 1 : BLOCK, sz.heads + i : sz.heads + i + 1]
        state[rows, :] = total * state[rows, :] + local[rows]
    ssd = intra + inter + pv[6:7, :ch] * vf
    ssd_o[...] = ssd
    gated = ssd * (gl * sigmoid(gl))
    weighty = gated * pv[5:6, :ch]
    unit_o[...] = weighty.astype(LOW)

    lane = lax.broadcasted_iota(jnp.int32, (BLOCK, 128), 1)
    square = jnp.sum(gated * gated, axis=1, keepdims=True)
    if layer == 0:
        project = jnp.zeros_like(square)
    else:
        scaled_grad = dot(ms[...], ov[...], NN)
        project = jnp.sum(scaled_grad * weighty, axis=1, keepdims=True)
    stats = jnp.where(lane == 0, square, jnp.where(lane == 1, project, inv_in))
    stats = jnp.transpose(stats)
    part_o[...] = stats[0:2, :]
    inv_o[...] = stats[2:3, :]

    @pl.when(b == sz.blocks - 1)
    def _():
        fin_o[...] = state[...]


def scalar_lines(sz, lines):
    fill = [jnp.zeros((8 - sz.blocks, HALF), F32)] if sz.blocks < 8 else []
    high, low = split_low(jnp.concatenate(lines + fill, axis=0))
    table = jnp.concatenate([high, low], axis=0).astype(LOW)
    return jnp.concatenate([table] * (sz.chunk // HALF), axis=1)


def own_rows(sz, ref, which):
    blocks = [ref[aligned(b * BLOCK + which * HALF, HALF), :] for b in range(sz.blocks)]
    return jnp.concatenate(blocks, axis=0)


def project_kernel(sz, layer, deps, sc, unit_r, stats_r, *refs):
    raw, got, refs = refs[:4], refs[4:6], refs[6 + deps :]
    keep, send, sc_o, weights, sems = refs
    c, h = sc[0], sc[1]
    copies = weight_copies(sz, layer, c, h, raw, got, None, weights, sems)
    run_copies(copies, True, False)
    for i in range(4):
        sc_o[i] = sc[i]
    sides = []
    for which, out in ((c, keep), (1 - c, send)):
        sides.append((out, own_rows(sz, unit_r, which)))
        lines = [
            stats_r[0:1, aligned(b * BLOCK + which * HALF, HALF)] for b in range(sz.blocks)
        ]
        table = scalar_lines(sz, lines)
        for d in range(sz.head_axis):
            out[d, sz.rows :, :] = table
    run_copies(copies, False, True)
    for out, rows in sides:
        for d in range(sz.head_axis):
            chunk = weights[:, aligned((h ^ d) * sz.chunk, sz.chunk)]
            out[d, : sz.rows, :] = dot(rows, chunk, NN).astype(LOW)


def turn_kernel(sz, sc, *refs):
    raw, got = refs[:4], refs[4:6]
    wide_o, out_o, wv, ov, sems = refs[6:8], refs[8:10], refs[10], refs[11], refs[12]
    for layer in range(2):
        copies = weight_copies(sz, layer, sc[0], sc[1], raw, got, wv, ov, sems)
        run_copies(copies, True, True)
        wide_o[layer][...] = jnp.transpose(wv[...])
        out_o[layer][...] = jnp.transpose(ov[...])


def lift_kernel(sz, layer, deps, sc, cat_r, normed_r, zero_gains, one_gains, small_r, *refs):
    weights, refs = refs[0], refs[1 + deps :]
    keep, send, sc_o, common_o, wide = refs
    c, h = sc[0], sc[1]
    for i in range(4):
        sc_o[i] = sc[i]
    wide[...] = jnp.zeros_like(wide)
    for which, out in ((c, keep), (1 - c, send)):
        rows = own_rows(sz, cat_r, which)
        along = jnp.zeros((sz.rows, 1), F32)
        for d in range(sz.head_axis):
            cols = aligned((h ^ d) * sz.chunk, sz.chunk)
            product = dot(rows, weights[:, cols], NN)
            out[d, : sz.rows, :] = product.astype(LOW)
            blocks = [
                normed_r[aligned(b * BLOCK + which * HALF, HALF), cols] for b in range(sz.blocks)
            ]
            product = product * jnp.concatenate(blocks, axis=0).astype(F32)
            wide[0:1, cols] += jnp.sum(product, axis=0, keepdims=True)
            along = along + jnp.sum(product, axis=1, keepdims=True)
        lines = [
            jnp.transpose(jnp.broadcast_to(along[b * HALF : (b + 1) * HALF], (HALF, 128)))[0:1, :]
            for b in range(sz.blocks)
        ]
        table = scalar_lines(sz, lines)
        for d in range(sz.head_axis):
            out[d, sz.rows :, :] = table
    gain_grad = wide[0:1, :] / pick(c == layer, zero_gains[0:1, :], one_gains[0:1, :])
    flat = [small_r[j : j + 1, sz.channels :] for j in range(sz.taps)]
    flat += [gain_grad[:, q * sz.chunk : (q + 1) * sz.chunk] for q in range(sz.head_axis)]
    high, low = split_low(jnp.concatenate(flat, axis=0))
    common_o[...] = jnp.concatenate([high, low], axis=0).astype(LOW)


def backward_kernel(sz, layer, deps, sc, *refs):
    n = sz.head_axis
    sources = 2 * n + 2 if layer == 0 else 1 + n
    src, refs = refs[:sources], refs[sources:]
    gl_r, lin_r, ssd_r, inc_r = refs[:4]
    table, gains, ov = refs[4], refs[5:7], refs[7]
    halo, halo_grad, begin = refs[8:11]
    refs = refs[11 + deps :]
    cat_o, scaled_o, small_o, sums_o, fin_o, rim_o, sc_o = refs[:7]
    refs = refs[7:]
    if layer == 0:
        mixed_o, refs = refs[0], refs[1:]
    ms, ext, back, state, heads_p, small = refs
    i_step = pl.program_id(0)
    b = sz.blocks - 1 - i_step
    c, h = sc[0], sc[1]
    ch, st = sz.channels, sz.states
    pv = pick(c == layer, gains[0][...], gains[1][...])
    rp = table[...]

    @pl.when(i_step == 0)
    def _():
        back[BLOCK : BLOCK + 8, :] = halo_grad[...]
        state[...] = begin[...]
        small[...] = jnp.zeros_like(small)
        for i in range(4):
            sc_o[i] = sc[i]
        if layer == 0:
            for i in range(2):
                extra = src[i * n][sz.rows :, :].astype(F32)
                for d in range(1, n):
                    extra = extra + src[i * n + d][sz.rows :, :].astype(F32)
                heads_p[8 * i : 8 * i + 8, :] = extra[0:8, :HALF] + extra[8:16, :HALF]

    if layer == 0:
        rows = aligned(b * HALF, HALF)
        put_pieces(
            sz, ms, c, h, [r[rows, :] for r in src[:n]], [r[rows, :] for r in src[n : 2 * n]]
        )
        halves = []
        for k in range(2):
            alpha = lax.rsqrt(line_of(src[2 * n + k][...], b) / sz.inner + EPS)
            beta = alpha * alpha * line_of(heads_p[...], 8 * k + b) / sz.inner
            halves.append((alpha, beta))
        alpha, beta = (
            pick(
                c == 0,
                jnp.concatenate([halves[0][q], halves[1][q]], axis=1),
                jnp.concatenate([halves[1][q], halves[0][q]], axis=1),
            )
            for q in range(2)
        )
    else:
        stats = src[1][...]
        for d in range(1, n):
            stats = stats + src[1 + d][...]
        alpha = lax.rsqrt(stats[0:1, :] / sz.inner + EPS)
        beta = alpha * alpha * alpha * stats[1:2, :] / sz.inner

    sub = lax.broadcasted_iota(jnp.int32, rp.shape, 0)
    cols = jnp.transpose(jnp.where(sub == 12, alpha, jnp.where(sub == 13, beta, rp)))
    alpha, beta = cols[:, 12:13], cols[:, 13:14]

    gl = gl_r[...]
    ssd = ssd_r[...]
    sig = sigmoid(gl)
    swish = gl * sig
    slope = sig * (1.0 + gl * (1.0 - sig))
    gated = ssd * swish
    if layer == 0:
        mixed_grad = ms[...]
        mixed_o[...] = mixed_grad
    else:
        mixed_grad = src[0][...]
    scaled_grad = dot(mixed_grad, ov[...], NN)
    gain = pv[5:6, :ch]
    normal = gated * alpha
    small[4:5, :ch] += jnp.sum(scaled_grad * normal, axis=0, keepdims=True)
    scaled_o[...] = (normal * gain).astype(LOW)
    gated_grad = alpha * (scaled_grad * gain) - beta * gated
    ssd_grad = (gated_grad * swish).astype(LOW)
    gate_grad = (gated_grad * ssd * slope).astype(LOW)
    sgf = ssd_grad.astype(F32)

    before = lin_r[pl.ds(pl.multiple_of(jnp.maximum(b * BLOCK - 16, 0), 16), 16), :]
    ext[0:8, :] = pick(b > 0, before.astype(F32)[8:16, :], halo[...])
    ext[8 : 8 + BLOCK, :] = lin_r[aligned(b * BLOCK, BLOCK), :].astype(F32)
    taps = pv[1:5, : sz.lin]
    pre = conv_forward(sz, ext, taps)
    psig = sigmoid(pre)
    pact = pre * psig
    pslope = psig * (1.0 + pre * (1.0 - psig))
    act = pact.astype(LOW)
    values, bm, cm = act[:, :ch], act[:, ch : ch + st], act[:, ch + st :]
    vf = values.astype(F32)
    small[5:6, :ch] += jnp.sum(sgf * vf, axis=0, keepdims=True)

    mask = lower_mask()
    gram = dot(cm, bm, NT)
    gram_grad = jnp.zeros((BLOCK, BLOCK), F32)
    mixes, parts = [], []
    for i in range(sz.heads):
        decay = decay_of(sz, cols, rp, i, mask)
        mixes.append((gram * decay).astype(LOW))
        parts.append(per_head(ssd_grad, i, sz.head_width))
        gram_grad = gram_grad + dot(parts[-1], values, NT) * decay
    intra_grad = dot(jnp.concatenate(mixes, axis=0), jnp.concatenate(parts, axis=0), TN)

    ecum = spread(cols, sz.heads, sz.heads, sz.head_width)
    to_end = spread(cols, 2 * sz.heads, sz.heads, sz.head_width)
    inter_grad = (sgf * ecum).astype(LOW)
    low_state = state[...].astype(LOW)
    carried = (vf * to_end).astype(LOW)
    carried_grad = dot(bm, low_state, NT)
    gram_low = gram_grad.astype(LOW)
    b_grad = dot(gram_low, cm, TN) + dot(carried, low_state, NN)
    c_grad = dot(gram_low, bm, NN) + dot(inter_grad, inc_r[0], NN)
    value_grad = intra_grad + pv[6:7, :ch] * sgf + carried_grad * to_end
    entry = dot(inter_grad, cm, TN)
    for i in range(sz.heads):
        rows = slice(i * sz.head_width, (i + 1) * sz.head_width)
        total = cols[BLOCK - 1 : BLOCK, sz.heads + i : sz.heads + i + 1]
        state[rows, :] = total * state[rows, :] + entry[rows]

    pre_grad = jnp.concatenate([value_grad, b_grad, c_grad], axis=1) * pslope
    back[0:BLOCK, :] = pre_grad
    lin_grad = taps[0:1] * back[sz.taps - 1 : sz.taps - 1 + BLOCK, :]
    for j in range(1, sz.taps):
        at = sz.taps - 1 - j
        lin_grad = lin_grad + taps[j : j + 1] * back[at : at + BLOCK, :]
    for j in range(sz.taps):
        small[j : j + 1, :] += jnp.sum(pre_grad * ext[5 + j : 5 + j + BLOCK, :], axis=0, keepdims=True)
    back[BLOCK : BLOCK + 8, :] = back[0:8, :]
    cat_o[...] = jnp.concatenate([gate_grad, lin_grad.astype(LOW)], axis=1)

    @pl.when(i_step == sz.blocks - 1)
    def _():
        fin_o[...] = state[...]
        rim_o[...] = back[0:8, :]
        sums = small[...]
        flat = [sums[j : j + 1, :ch] for j in range(sz.taps + 2)]
        flat = [jnp.concatenate(flat[j : j + 3], axis=1) for j in range(0, len(flat), 3)]
        flat = flat + [jnp.zeros_like(flat[0])] * (4 - len(flat))
        high, low = split_low(jnp.concatenate(flat, axis=0))
        rest = jnp.zeros((PAD - 8, high.shape[1]), F32)
        small_o[...] = jnp.concatenate([high, low, rest], axis=0).astype(LOW)
        sums_o[...] = sums


def weights_kernel(sz, seq, sc, normed, cat, mixed, scaled, small, common, *refs):
    sc_o, outs, heads, full, wide = refs[0], refs[1 : seq + 1], refs[seq + 1 : -2], refs[-2], refs[-1]
    for i in range(4):
        sc_o[i] = sc[i]
    ch, st = sz.channels, sz.states
    step = sz.chunk
    for q in range(sz.head_axis):
        at = slice(q * step, (q + 1) * step)
        grads = dot(normed[:, at], cat[...], TN)
        full[at, : 2 * ch] = grads[:, : 2 * ch].astype(LOW)
        wide[at, :] = grads[:, 2 * ch :]
        full[at, 2 * ch :] = dot(mixed[:, at], scaled[...], TN).astype(LOW)
    rows = sz.width // seq
    part = rows // sz.head_axis
    for r, out in enumerate(outs):
        out[:rows, :] = full[aligned(lax.rem(sc[2] + r, seq) * rows, rows), :]
        out[rows:, :] = small[...]
    for d, out in enumerate(heads):
        lines = [
            wide[aligned(lax.rem(sc[2] + r, seq) * rows + (sc[1] ^ d) * part, part), :]
            for r in range(seq)
        ]
        out[:PAD, :] = common[...]
        out[PAD:, :] = jnp.concatenate(lines, axis=0).astype(LOW)


def resplit(extra):
    half = extra.shape[0] // 2
    high, low = split_low(extra[:half, :] + extra[half:, :])
    return jnp.concatenate([high, low], axis=0)


def join_kernel(sz, riders, sc, keep, recv, *refs):
    n = sz.head_axis
    more, refs = [refs[i * n : (i + 1) * n] for i in range(riders)], refs[riders * n :]
    sc_o, outs = refs[0], refs[1:]
    rows = sz.rows
    for i in range(4):
        sc_o[i] = sc[i]
    extra = resplit(keep[0, rows:, :].astype(F32) + recv[0, rows:, :].astype(F32))
    for d, out in enumerate(outs):
        out[:rows, :] = (keep[d, :rows, :].astype(F32) + recv[d, :rows, :].astype(F32)).astype(out.dtype)
        out[rows : rows + PAD, :] = extra.astype(out.dtype)
        at = rows + PAD
        for rider in more:
            size = rider[d].shape[0]
            out[at : at + size, :] = rider[d][...].astype(out.dtype)
            at += size


def total_of(parts, rows):
    total = parts[0][rows, :].astype(F32)
    for p in parts[1:]:
        total = total + p[rows, :].astype(F32)
    return total


def output_kernel(sz, layer, sc, *refs):
    n = sz.head_axis
    parts, refs = refs[:n], refs[n:]
    resid = refs[0]
    res_o, low_o, mixed_o, square_o, sc_o = refs[-5:]
    for i in range(4):
        sc_o[i] = sc[i]
    extra = total_of(parts, slice(sz.rows, sz.rows + PAD))
    square = extra[0:8, :HALF] + extra[8:16, :HALF]
    square_o[...] = square
    inv = lax.rsqrt(square / sz.inner + EPS)
    for b in range(sz.blocks):
        rows = slice(b * HALF, (b + 1) * HALF)
        col = column_of(inv[b : b + 1, :], HALF)[:, 0:1]
        mixed = total_of(parts, rows) * col
        res = resid[rows, :].astype(F32) + mixed
        res_o[rows, :] = res
        low_o[rows, :] = res.astype(LOW)
        mixed_o[rows, :] = mixed


def input_kernel(sz, layer, sc, *refs):
    n = sz.head_axis
    parts, refs = refs[:n], refs[n:]
    resid, outg, inv_r, gains = refs[0], refs[1], refs[2], refs[3:5]
    refs = refs[5:]
    if layer == 1:
        mixed = refs[0]
        grad_o, low_o, sc_o = refs[-3:]
    else:
        one_low = refs[0]
        low_o, swap_o, shared_o, sc_o = refs[-4:]
    for i in range(4):
        sc_o[i] = sc[i]
    c, h = sc[0], sc[1]
    first = c == 0
    mine = aligned(h * sz.chunk, sz.chunk)
    gain = pick(c == layer, gains[0][0:1, mine], gains[1][0:1, mine])
    extra = total_of(parts, slice(sz.rows, sz.rows + PAD))
    along = extra[0:8, :HALF] + extra[8:16, :HALF]
    tops, lows = [], []
    for b in range(sz.blocks):
        rows = slice(b * HALF, (b + 1) * HALF)
        at = b * BLOCK
        inv_row = pick(c == 0, inv_r[:, at : at + HALF], inv_r[:, at + HALF : at + BLOCK])
        inv = column_of(inv_row, HALF)[:, 0:1]
        share = column_of(along[b : b + 1, :] / sz.width, HALF)[:, 0:1]
        total = total_of(parts, rows)
        base = resid[rows, :].astype(F32)
        grad = outg[rows, :].astype(F32) + inv * (total * gain - base * (inv * share))
        low = grad.astype(LOW)
        low_o[rows, :] = low
        if layer == 0:
            swap_o[rows, :] = pick(first, one_low[rows, :], low)
        else:
            grad_o[rows, :] = grad
            dots = jnp.sum(low.astype(F32) * mixed[rows, :], axis=1, keepdims=True)
            row = jnp.transpose(jnp.broadcast_to(dots, (HALF, 128)))[0:1, :]
            high, rest = split_low(row)
            tops.append(high)
            lows.append(rest)
    if layer == 1:
        fill = [jnp.zeros((8 - sz.blocks, HALF), F32)] if sz.blocks < 8 else []
        extra = jnp.concatenate(tops + fill + lows + fill, axis=0)
        extra = jnp.concatenate([extra] * (sz.chunk // HALF), axis=1)
        low_o[sz.rows :, :] = extra.astype(LOW)
    else:
        size = shared_o.shape[0]
        at = sz.rows + PAD
        zero = total_of(parts, slice(at, at + size))
        one = total_of(parts, slice(at + size, at + 2 * size))
        zero, one = (jnp.concatenate([resplit(v[:PAD]), v[PAD:]], axis=0) for v in (zero, one))
        shared_o[...] = pick(first, zero, one)
        swap_o[sz.rows :, :] = pick(first, one, zero).astype(LOW)


def sum_kernel(sz, last, sc, *refs):
    if last:
        parts, done, outs = refs[:-3], refs[-3], refs[-2:]
    else:
        parts, outs = refs[:-1], refs[-1:]
    rows = outs[0].shape[0] - PAD
    extra = total_of(parts, slice(rows, rows + PAD))
    high, low = split_low(extra[0:4, :] + extra[4:8, :])
    extra = jnp.concatenate([high, low, jnp.zeros((PAD - 8, extra.shape[1]), F32)], axis=0)
    sums = jnp.concatenate([total_of(parts, slice(0, rows)), extra], axis=0).astype(LOW)
    if last:
        outs[0][...] = pick(sc[0] == 0, sums, done[...])
        outs[1][...] = pick(sc[0] == 0, done[...], sums)
    else:
        outs[0][...] = sums


def final_kernel(sz, seq, sc, own, got, *refs):
    pieces, refs = refs[:-9], refs[-9:]
    gate_o, inner_o, out_o, conv_o, norm_o, skip_o, shared_o, taps_o, gain_o = refs
    c = sc[0]
    ch = sz.channels
    rows = own.shape[0] - PAD
    lane = lax.broadcasted_iota(jnp.int32, skip_o.shape, 1)
    skip = jnp.zeros(skip_o.shape, F32)
    for i in range(2):
        which = pick(i == 0, c, 1 - c)
        to = aligned(which * ch, ch)
        sums = (own if i == 0 else got)[...].astype(F32)
        gate_o[:, to] = sums[:rows, :ch]
        inner_o[:, to] = sums[:rows, ch : 2 * ch]
        out_o[to, :] = jnp.transpose(sums[:rows, 2 * ch :])
        lines = sums[rows : rows + 4, :] + sums[rows + 4 : rows + 8, :]
        for j in range(sz.taps):
            conv_o[j : j + 1, to] = lines[j // 3 : j // 3 + 1, (j % 3) * ch : (j % 3 + 1) * ch]
        norm_o[:, to] = lines[1:2, ch : 2 * ch]
        skips = lines[1:2, 2 * ch :]
        for q in range(sz.heads):
            part = jnp.sum(per_head(skips, q, sz.head_width), axis=1, keepdims=True)
            skip = jnp.where(lane == which * sz.heads + q, part, skip)
    skip_o[...] = skip
    total = pieces[0][0, BLOCK:, :].astype(F32)
    for r in range(1, seq):
        total = total + pieces[0][r, BLOCK:, :].astype(F32)
    shared_o[...] = total[PAD:]
    common = total[: PAD // 2] + total[PAD // 2 : PAD]
    place = sc[2] * sz.head_axis + sc[1]
    span = common.shape[1]
    size = span // (seq * sz.head_axis)
    turned = pltpu.roll(common, lax.rem(span - place * size, span), 1)
    taps_o[...] = turned[: sz.taps, :size]
    size = sz.width // (seq * sz.head_axis)
    at = place * size
    line = jnp.broadcast_to(line_of(common, sz.taps + at // span), common.shape)
    turned = pltpu.roll(line, lax.rem(span - lax.rem(at, span), span), 1)
    gain_o[...] = turned[:1, :size]


def slice_kernel(sz, slots, sc, order, tokens, rates, out, sc_o, sems):
    copies = []
    for j in range(slots):
        rows = tokens.at[order[j], aligned(sc[0] * HALF, HALF), :]
        copies.append(pltpu.make_async_copy(rows, out.at[j, :HALF, :], sems.at[j]))
    for copy in copies:
        copy.start()
    for i in range(4):
        sc_o[i] = sc[i]
    for j in range(slots):
        first, rest = split_low(rates[0, order[j]])
        second, rest = split_low(rest)
        lines = jnp.concatenate([first, second, rest, jnp.zeros_like(rest)], axis=1)
        lines = jnp.concatenate([lines, jnp.zeros_like(lines)], axis=0)
        out[j, HALF:, :] = lines.astype(LOW)
    for copy in copies:
        copy.wait()


def rates_of(piece):
    lines = piece[HALF:, :].astype(F32)[:8, :]
    return (lines[:, :BLOCK] + lines[:, BLOCK : 2 * BLOCK]) + lines[:, 2 * BLOCK : 3 * BLOCK]


def pack_kernel(sz, sc, order, grads, gate, inner, shared, out, in_gain, conv_i, conv_s, skip, norm, *refs):
    w_o, o_o, mine_o, send_o, sems = *refs[:4], refs[-1]
    c, h = sc[0], sc[1]
    ch = sz.channels
    outs = refs[4:-1]
    slices = []
    for r, to in enumerate(outs):
        rows = grads.at[order[lax.rem(sc[3] + r, len(outs))], aligned(c * HALF, HALF), :]
        slices.append(pltpu.make_async_copy(rows, to, sems.at[4 + r]))
    cols = aligned((1 - c) * ch, ch)
    rows = aligned((h * 2 + 1 - c) * ch, ch)
    copies = [
        pltpu.make_async_copy(gate.at[0, :, cols], w_o.at[:, :ch], sems.at[0]),
        pltpu.make_async_copy(inner.at[0, :, cols], w_o.at[:, ch : 2 * ch], sems.at[1]),
        pltpu.make_async_copy(shared.at[0], w_o.at[:, 2 * ch :], sems.at[2]),
        pltpu.make_async_copy(out.at[0, rows, :], o_o, sems.at[3]),
        *slices,
    ]
    for copy in copies:
        copy.start()
    for which, ref in ((c, mine_o), (1 - c, send_o)):
        at = aligned(which * ch, ch)
        ref[...] = jnp.zeros_like(ref)
        ref[0:1, :] = in_gain[...]
        ref[1 : 1 + sz.taps, :ch] = conv_i[0, :, at]
        ref[1 : 1 + sz.taps, ch : sz.lin] = conv_s[0]
        ref[5:6, :ch] = norm[:, at]
        low = spread(skip[...], 0, sz.heads, sz.head_width)
        high = spread(skip[...], sz.heads, sz.heads, sz.head_width)
        ref[6:7, :ch] = pick(which == 0, low, high)
    for copy in copies:
        copy.wait()


def decay_table(rate, c, n):
    lane = lax.broadcasted_iota(jnp.int32, rate.shape, 1)
    cum = rate
    step = 1
    while step < BLOCK:
        cum = cum + jnp.where(lane >= step, pltpu.roll(cum, step, 1), 0.0)
        step *= 2
    end = cum[:, BLOCK - 1 :]
    lines = [cum, jnp.exp(cum), jnp.exp(end - cum) * -rate, jnp.log(-rate) - cum]
    low = jnp.concatenate([v[:n] for v in lines], axis=0)
    high = jnp.concatenate([v[n:] for v in lines], axis=0)
    return pick(c == 0, low, high)


def leave_kernel(sz, slots, riders, sc, zero_own, zero_other, one_own, one_other, *refs):
    c = sc[0]
    if riders:
        shared, refs = refs[0], refs[1:]
        total = shared[...] + one_other[sz.rows :, :].astype(F32)
        extra = resplit(total[:PAD])
        part = (total.shape[0] - PAD) // riders
    for i in range(4):
        refs[-1][i] = sc[i]
    for r in range(slots):
        stacked = len(refs) == 2
        out = refs[0].at[r] if stacked else refs[r]
        at = r if stacked else lax.rem(sc[3] + r, slots)
        rows = aligned(at * HALF, HALF)
        own = pick(c == 0, zero_own[rows, :], one_own[rows, :])
        other = pick(c == 0, zero_other[rows, :], one_other[rows, :])
        put_pair(out, c, own, other)
        if riders:
            at = PAD + lax.rem(r - sc[2] + riders, riders) * part
            lines = [extra, shared[pl.ds(at, part), :] + one_other[pl.ds(sz.rows + at, part), :].astype(F32)]
            out[BLOCK:, :] = jnp.concatenate(lines, axis=0).astype(LOW)


def home_kernel(slots, sc, *refs):
    early, late, out, grad = refs[:slots], refs[slots], refs[-3], refs[-2]
    for i in range(4):
        refs[-1][i] = sc[i]
    first = sc[0] == 0
    for r in range(slots):
        at = lax.rem(sc[3] - r + slots, slots)
        piece = late[at, :BLOCK, :]
        out[at] = pick(first, early[r][...], piece).astype(F32)
        grad[at] = pick(first, piece, early[r][...]).astype(F32)


def whole(shape):
    return pl.BlockSpec(shape, lambda *_: (0,) * len(shape))


def per_device(
    tokens,
    slot_order,
    log_decay,
    grad_out,
    in_gain,
    w_gate,
    w_inner,
    w_shared,
    conv_inner,
    conv_shared,
    d_skip,
    norm_gain,
    w_out,
):
    slots = tokens.shape[0]
    span = tokens.shape[1]
    width = tokens.shape[2]
    seq = lax.axis_size("seq")
    head_axis = lax.axis_size("head")
    cores = lax.axis_size("section")
    spans = seq // slots
    c = lax.axis_index("section")
    z = lax.axis_index("seq")
    h = lax.axis_index("head")
    k = lax.rem(z, slots)
    inner_dev = w_gate.shape[2]
    channels = inner_dev // cores
    shared = w_shared.shape[2]
    heads_dev = d_skip.shape[1]
    taps = conv_inner.shape[1]
    sz = Sizes(
        slots * span // BLOCK,
        width,
        channels,
        heads_dev // cores,
        shared // 2,
        taps,
        head_axis,
        inner_dev * head_axis,
    )
    first = c == 0
    swap = [(0, 1), (1, 0)]
    nb, tok, rows, chunk = sz.blocks, sz.tokens, sz.rows, sz.chunk

    def cross(x):
        return lax.ppermute(x, "section", swap)

    def turn(x, r):
        pairs = [(i, i // slots * slots + (i % slots + r) % slots) for i in range(seq)]
        return lax.ppermute(x, "seq", pairs) if r else x

    def over_heads(x, d):
        return x if d == 0 else lax.ppermute(x, "head", [(i, i ^ d) for i in range(head_axis)])

    def next_span(x, way):
        pairs = [(i, i + way * slots) for i in range(seq) if 0 <= i + way * slots < seq]
        return lax.ppermute(x, "seq", pairs)

    def shape(dims, dtype):
        return jax.ShapeDtypeStruct(dims, dtype)

    prefetch = functools.partial(pltpu.PrefetchScalarGridSpec, num_scalar_prefetch=1)
    options = pltpu.CompilerParams(vmem_limit_bytes=VMEM_BYTES)
    from_hbm = pltpu.CompilerParams(vmem_limit_bytes=ALL_VMEM_BYTES)
    anywhere = pl.BlockSpec(memory_space=pl.ANY)
    smem = pl.BlockSpec(memory_space=pltpu.SMEM)
    vmem = pl.BlockSpec(memory_space=pltpu.VMEM)
    index_shape = shape((4,), jnp.int32)

    def cost(flops, moved):
        return pl.CostEstimate(flops=int(flops), bytes_accessed=int(moved), transcendentals=0)

    def to_members(pieces):
        return [turn(x, r) for r, x in enumerate(pieces)]

    sc = jnp.stack([c, h, z, k]).astype(jnp.int32)
    def exchange(stacked):
        if spans == 1:
            return lax.all_to_all(stacked, "seq", 0, 0, tiled=True)
        out = stacked
        for r in range(slots):
            item = lax.dynamic_index_in_dim(stacked, lax.rem(k + r, slots), 0, False)
            place = lax.rem(k + slots - r, slots)
            out = lax.dynamic_update_index_in_dim(out, turn(item, r), place, 0)
        return out

    tok_slices, sc = pl.pallas_call(
        functools.partial(slice_kernel, sz, slots),
        in_specs=[smem, smem, anywhere, vmem],
        out_specs=[vmem, smem],
        out_shape=[shape((slots, HALF + PAD, width), LOW), index_shape],
        scratch_shapes=[pltpu.SemaphoreType.DMA((slots,))],
        compiler_params=from_hbm,
    )(sc, slot_order, tokens, log_decay)
    tok_own = exchange(tok_slices)
    tok_pieces = [tok_own, cross(tok_own)]

    wide = 2 * channels + shared
    w_sent, o_sent, pv_mine, pv_sent, *out_slices = pl.pallas_call(
        functools.partial(pack_kernel, sz),
        in_specs=[smem, smem] + [anywhere] * 5 + [vmem] * 5,
        out_specs=[vmem] * (4 + slots),
        out_shape=[
            shape((width, wide), LOW),
            shape((channels, width), LOW),
            shape((16, width), F32),
            shape((16, width), F32),
        ]
        + [shape((HALF, width), LOW)] * slots,
        scratch_shapes=[pltpu.SemaphoreType.DMA((4 + slots,))],
        compiler_params=from_hbm,
    )(
        sc, slot_order, grad_out, w_gate, w_inner, w_shared, w_out,
        in_gain, conv_inner, conv_shared, d_skip, norm_gain,
    )
    raw = [w_gate, w_inner, w_shared, w_out]
    sent = [cross(w_sent), cross(o_sent)]
    gains = [pv_mine, cross(pv_sent)]

    def span_total(table):
        ends = table[: sz.heads, BLOCK - 1 :: BLOCK]
        return jnp.repeat(jnp.exp(jnp.sum(ends, axis=1)), sz.head_width)[:, None]

    parts_shape = shape((head_axis, rows + PAD, chunk), LOW)
    weight_specs = [anywhere] * 6
    wide_weights = pltpu.VMEM((width, wide), LOW)
    out_weights = pltpu.VMEM((channels, width), LOW)
    copy_sems = pltpu.SemaphoreType.DMA((4,))
    dense = 2 * tok * width * (wide + channels)

    def forward(layer, sc, sources):
        def at(b, _):
            return (b, 0)

        piece = pl.BlockSpec((HALF, chunk), at)
        table = pl.BlockSpec((16, BLOCK), lambda b, _: (0, b))
        if layer == 0:
            src_specs = [pl.BlockSpec((1, HALF + PAD, width), lambda b, _: (b, 0, 0))] * 2
            more_specs = [table, table]
            more_shapes = [shape((16, tok), F32)] * 2
        else:
            src_specs = [piece] * (2 * head_axis) + [whole((HALF, width))] * (2 * slots) + [table]
            more_specs = [pl.BlockSpec((BLOCK, width), at)]
            more_shapes = [shape((tok, width), LOW)]

        last = [] if layer == 0 else [turned[3]]

        def call(halo, begin):
            return pl.pallas_call(
                functools.partial(forward_kernel, sz, layer, slots),
                grid_spec=prefetch(
                    grid=(nb,),
                    in_specs=src_specs
                    + [whole((16, width)), whole((16, width))]
                    + weight_specs
                    + [whole((8, sz.lin)), whole((channels, sz.states))]
                    + [whole(x.shape) for x in last],
                    out_specs=[
                        pl.BlockSpec((BLOCK, width), at),
                        pl.BlockSpec((BLOCK, channels), at),
                        pl.BlockSpec((BLOCK, sz.lin), at),
                        pl.BlockSpec((BLOCK, channels), at),
                        pl.BlockSpec((1, channels, sz.states), lambda b, _: (b, 0, 0)),
                        pl.BlockSpec((1, BLOCK), lambda b, _: (0, b)),
                        pl.BlockSpec((2, BLOCK), lambda b, _: (0, b)),
                        pl.BlockSpec((BLOCK, channels), at),
                        whole((channels, sz.states)),
                        smem,
                        piece,
                    ]
                    + more_specs,
                    scratch_shapes=[
                        pltpu.VMEM((BLOCK, width), LOW),
                        pltpu.VMEM((BLOCK, width), LOW),
                        wide_weights,
                        pltpu.VMEM((BLOCK + 8, sz.lin), F32),
                        pltpu.VMEM((channels, sz.states), F32),
                        copy_sems,
                    ],
                ),
                out_shape=[
                    shape((tok, width), LOW),
                    shape((tok, channels), F32),
                    shape((tok, sz.lin), LOW),
                    shape((tok, channels), F32),
                    shape((nb, channels, sz.states), LOW),
                    shape((1, tok), F32),
                    shape((2, tok), F32),
                    shape((tok, channels), LOW),
                    shape((channels, sz.states), F32),
                    index_shape,
                    shape((rows, chunk), LOW),
                ]
                + more_shapes,
                compiler_params=options,
                cost_estimate=cost(6 * dense, 16e6),
            )(sc, *sources, *gains, *raw, *sent, halo, begin, *last)

        halo = jnp.zeros((8, sz.lin), F32)
        begin = jnp.zeros((channels, sz.states), F32)
        if spans == 1:
            return call(halo, begin), halo
        trial = call(halo, begin)
        halo = next_span(trial[2][tok - 8 :].astype(F32), 1)
        local = call(halo, begin)[8]
        total = span_total(trial[11] if layer == 0 else sources[-1])
        for _ in range(spans - 1):
            begin = next_span(total * begin + local, 1)
        return call(halo, begin), halo

    def backward(layer, sc, sources, saved, decays, halo, deps):
        def at(i, _):
            return (nb - 1 - i, 0)

        if layer == 0:
            src_specs = [whole(s.shape) for s in sources]
        else:
            stat = pl.BlockSpec((2, BLOCK), lambda i, _: (0, nb - 1 - i))
            src_specs = [pl.BlockSpec((BLOCK, width), at)] + [stat] * head_axis
        gl, lin, ssd, inc = saved
        mixed_spec = [pl.BlockSpec((BLOCK, width), at)] if layer == 0 else []
        mixed_shape = [shape((tok, width), LOW)] if layer == 0 else []

        def call(halo_grad, begin):
            return pl.pallas_call(
                functools.partial(backward_kernel, sz, layer, len(deps)),
                grid_spec=prefetch(
                    grid=(nb,),
                    in_specs=src_specs
                    + [
                        pl.BlockSpec((BLOCK, channels), at),
                        whole(lin.shape),
                        pl.BlockSpec((BLOCK, channels), at),
                        pl.BlockSpec((1, channels, sz.states), lambda i, _: (nb - 1 - i, 0, 0)),
                        pl.BlockSpec((16, BLOCK), lambda i, _: (0, nb - 1 - i)),
                        whole((16, width)),
                        whole((16, width)),
                        whole((width, channels)),
                        whole((8, sz.lin)),
                        whole((8, sz.lin)),
                        whole((channels, sz.states)),
                    ]
                    + [anywhere] * len(deps),
                    out_specs=[
                        pl.BlockSpec((BLOCK, wide), at),
                        pl.BlockSpec((BLOCK, channels), at),
                        whole((PAD, 3 * channels)),
                        whole((8, sz.lin)),
                        whole((channels, sz.states)),
                        whole((8, sz.lin)),
                        smem,
                    ]
                    + mixed_spec,
                    scratch_shapes=[
                        pltpu.VMEM((BLOCK, width), LOW),
                        pltpu.VMEM((BLOCK + 8, sz.lin), F32),
                        pltpu.VMEM((BLOCK + 8, sz.lin), F32),
                        pltpu.VMEM((channels, sz.states), F32),
                        pltpu.VMEM((PAD, HALF), F32),
                        pltpu.VMEM((8, sz.lin), F32),
                    ],
                ),
                out_shape=[
                    shape((tok, wide), LOW),
                    shape((tok, channels), LOW),
                    shape((PAD, 3 * channels), LOW),
                    shape((8, sz.lin), F32),
                    shape((channels, sz.states), F32),
                    shape((8, sz.lin), F32),
                    index_shape,
                ]
                + mixed_shape,
                compiler_params=options,
                cost_estimate=cost(8 * dense, 16e6),
            )(
                sc, *sources, gl, lin, ssd, inc, decays, *gains, turned[2 + layer],
                halo, halo_grad, begin, *deps,
            )

        halo_grad = jnp.zeros((8, sz.lin), F32)
        begin = jnp.zeros((channels, sz.states), F32)
        if spans == 1:
            return call(halo_grad, begin)
        local = call(halo_grad, begin)[4]
        for _ in range(spans - 1):
            begin = next_span(span_total(decays) * begin + local, -1)
        halo_grad = next_span(call(halo_grad, begin)[5], -1)
        return call(halo_grad, begin)

    def project(layer, sc, unit, stats, deps):
        return pl.pallas_call(
            functools.partial(project_kernel, sz, layer, len(deps)),
            in_specs=[smem, vmem, vmem] + weight_specs + [anywhere] * len(deps),
            out_specs=[vmem, vmem, smem],
            out_shape=[parts_shape, parts_shape, index_shape],
            scratch_shapes=[out_weights, copy_sems],
            compiler_params=options,
            cost_estimate=cost(dense / 4, 4e6),
        )(sc, unit, stats, *raw, *sent, *deps)

    def lift(layer, sc, cat, normed, small, deps):
        return pl.pallas_call(
            functools.partial(lift_kernel, sz, layer, len(deps)),
            in_specs=[smem] + [vmem] * 6 + [anywhere] * len(deps),
            out_specs=[vmem, vmem, smem, vmem],
            out_shape=[parts_shape, parts_shape, index_shape, shape((PAD, chunk), LOW)],
            scratch_shapes=[pltpu.VMEM((8, width), F32)],
            compiler_params=options,
            cost_estimate=cost(dense, 8e6),
        )(sc, cat, normed, *gains, small, turned[layer], *deps)

    def scatter(sc, keep, send, *riders):
        size = rows + PAD + sum(rider[0].shape[0] for rider in riders)
        flat = [x for rider in riders for x in rider]
        joined = pl.pallas_call(
            functools.partial(join_kernel, sz, len(riders)),
            in_specs=[smem] + [vmem] * (2 + len(flat)),
            out_specs=[smem] + [vmem] * head_axis,
            out_shape=[index_shape, shape((size, chunk), F32)]
            + [shape((size, chunk), LOW)] * (head_axis - 1),
            compiler_params=options,
        )(sc, keep, cross(send), *flat)
        return [over_heads(joined[1 + d], d) for d in far_first(head_axis)], joined[0]

    def gather(low):
        own = [over_heads(low, d) for d in far_first(head_axis)]
        return own + [cross(x) for x in own]

    turned = pl.pallas_call(
        functools.partial(turn_kernel, sz),
        in_specs=[smem] + weight_specs,
        out_specs=[vmem] * 4,
        out_shape=[shape((wide, width), LOW)] * 2 + [shape((width, channels), LOW)] * 2,
        scratch_shapes=[wide_weights, out_weights, copy_sems],
        compiler_params=options,
        cost_estimate=cost(1e9, 8e6),
    )

    def section_output(layer, sc, parts, resid, deps=()):
        return pl.pallas_call(
            functools.partial(output_kernel, sz, layer),
            in_specs=[smem] + [vmem] * (head_axis + 1) + [anywhere] * len(deps),
            out_specs=[vmem] * 4 + [smem],
            out_shape=[
                shape((rows, chunk), F32),
                shape((rows, chunk), LOW),
                shape((rows, chunk), F32),
                shape((8, HALF), F32),
                index_shape,
            ],
            compiler_params=options,
        )(sc, *parts, resid, *deps)

    part = width // seq
    columns = 3 * channels
    share = part // head_axis
    shared_size = seq * share + PAD

    def section_input(layer, sc, parts, *others, deps=()):
        if layer == 0:
            outs = [
                shape((rows + PAD, chunk), LOW),
                shape((rows + shared_size, chunk), LOW),
                shape((shared_size, chunk), F32),
            ]
        else:
            outs = [shape((rows, chunk), F32), shape((rows + PAD, chunk), LOW)]
        return pl.pallas_call(
            functools.partial(input_kernel, sz, layer),
            in_specs=[smem] + [vmem] * (head_axis + len(others)) + [anywhere] * len(deps),
            out_specs=[vmem] * len(outs) + [smem],
            out_shape=outs + [index_shape],
            compiler_params=options,
        )(sc, *parts, *others, *deps)

    def weight_grads(sc, normed, cat, mixed, scaled, small, common):
        outs = pl.pallas_call(
            functools.partial(weights_kernel, sz, seq),
            in_specs=[smem] + [vmem] * 6,
            out_specs=[smem] + [vmem] * (seq + head_axis),
            out_shape=[index_shape]
            + [shape((part + PAD, columns), LOW)] * seq
            + [shape((shared_size, shared), LOW)] * head_axis,
            scratch_shapes=[pltpu.VMEM((width, columns), LOW), pltpu.VMEM((width, shared), F32)],
            compiler_params=options,
            cost_estimate=cost(4 * dense, 12e6),
        )(sc, normed, cat, mixed, scaled, small, common)
        return over_seq(outs[1 : 1 + seq]), outs[1 + seq :], outs[0]

    def over_seq(chunks):
        pieces = [chunks[0]]
        for r in range(1, seq):
            pairs = [(i, (i + r) % seq) for i in range(seq)]
            pieces.append(lax.ppermute(chunks[r], "seq", pairs))
        return pieces

    def leave(sc, *arrays, riders=0, stacked=False):
        size = BLOCK + (share + PAD if riders else 0)
        if stacked:
            outs = [shape((slots, size, chunk), LOW)]
        else:
            outs = [shape((size, chunk), LOW)] * slots
        *pieces, sc = pl.pallas_call(
            functools.partial(leave_kernel, sz, slots, riders),
            in_specs=[smem] + [vmem] * len(arrays),
            out_specs=[vmem] * len(outs) + [smem],
            out_shape=outs + [index_shape],
            compiler_params=options,
        )(sc, *arrays)
        return exchange(pieces[0]) if stacked else to_members(pieces), sc

    out_pieces = to_members(out_slices)
    fw0, halo0 = forward(0, sc, tok_pieces)
    base0, decays = fw0[10], fw0[11:13]
    pr0 = project(0, fw0[9], fw0[7], fw0[6], [out_pieces[1], out_pieces[-1]])
    out_others = [cross(x) for x in out_pieces]
    parts, sc_join = scatter(sc, pr0[0], pr0[1])
    turned = turned(sc_join, *raw, *sent)
    res1, low1, mixed0, square0, unused = section_output(0, sc, parts, base0, turned)
    pieces1 = gather(low1)
    square_other = cross(square0)

    fw1, halo1 = forward(1, sc, pieces1 + out_pieces + out_others + [decays[1]])
    stat = fw1[6] + cross(fw1[6])
    stats = [stat] + [over_heads(stat, d) for d in range(1, head_axis)]
    pr1 = project(1, fw1[9], fw1[7], fw1[6], [])
    parts_out, sc_out = scatter(sc, pr1[0], pr1[1])
    bw1 = backward(1, sc_out, [fw1[11]] + stats, fw1[1:5], decays[1], halo1, [])
    lf1 = lift(1, bw1[6], bw1[0], fw1[0], bw1[3], parts_out[1:])
    weights1, heads1, sc_weights = weight_grads(
        lf1[2], fw1[0], bw1[0], fw1[11], bw1[1], bw1[2], lf1[3]
    )
    parts, sc_join = scatter(sc_weights, lf1[0], lf1[1])
    igrad1, glow1, sc_in = section_input(
        1, sc_join, parts, res1, fw1[10], fw1[5], *gains, mixed0,
        deps=[weights1[1], weights1[-1]],
    )
    piecesg = gather(glow1)

    early, unused = leave(sc_in, low1, pieces1[head_axis], glow1, piecesg[head_axis])
    bw0 = backward(
        0, sc, piecesg + [square0, square_other], fw0[1:5], decays[0], halo0, weights1[2:-1]
    )
    lf0 = lift(0, bw0[6], bw0[0], fw0[0], bw0[3], [early[1], early[-1]])
    weights0, heads0, sc_weights = weight_grads(
        lf0[2], fw0[0], bw0[0], bw0[7], bw0[1], bw0[2], lf0[3]
    )
    parts, sc_join = scatter(sc_weights, lf0[0], lf0[1], heads0, heads1)

    unused, low2, unused_mixed, unused_square, sc_out = section_output(1, sc_in, parts_out, res1)
    glow0, to_other, shared_own, sc_end = section_input(
        0, sc_out, parts, base0, igrad1, fw0[5], *gains, low2,
        deps=weights0[1:-1] + early[2:-1],
    )
    got = cross(to_other)
    if spans == 1:
        late, sc_end = leave(sc_end, glow0, got, low2, got, shared_own, riders=seq, stacked=True)
        shared_parts = [late]
    else:
        late, sc_end = leave(sc_end, glow0, got, low2, got, stacked=True)
        total = shared_own + got[rows:].astype(F32)
        extra = resplit(total[:PAD])
        fill = jnp.zeros((BLOCK, shared), F32)
        chunks = [
            jnp.concatenate([fill, extra, total[PAD + r * share : PAD + (r + 1) * share]])
            for r in range(seq)
        ]
        shared_parts = [jnp.stack(over_seq([x.astype(LOW) for x in chunks]))]
    section_out, input_grad, sc_end = pl.pallas_call(
        functools.partial(home_kernel, slots),
        in_specs=[smem] + [vmem] * (slots + 1),
        out_specs=[vmem, vmem, smem],
        out_shape=[shape((slots, BLOCK, chunk), F32)] * 2 + [index_shape],
        compiler_params=options,
    )(sc, *early, late)

    def summed(sc, pieces, *done):
        return pl.pallas_call(
            functools.partial(sum_kernel, sz, bool(done)),
            in_specs=[smem] + [vmem] * (seq + len(done)),
            out_shape=[shape((part + PAD, columns), LOW)] * (1 + len(done)),
            compiler_params=options,
        )(sc, *pieces, *done)

    own_sums, other_sums = summed(sc_end, weights0, *summed(sc_in, weights1))
    final = pl.pallas_call(
        functools.partial(final_kernel, sz, seq),
        in_specs=[smem] + [vmem] * 3,
        out_shape=[
            shape((part, inner_dev), F32),
            shape((part, inner_dev), F32),
            shape((inner_dev, part), F32),
            shape((taps, inner_dev), F32),
            shape((1, inner_dev), F32),
            shape((1, heads_dev), F32),
            shape((share, shared), F32),
            shape((taps, shared // (seq * head_axis)), F32),
            shape((1, width // (seq * head_axis)), F32),
        ],
        compiler_params=options,
    )(sc, own_sums, cross(other_sums), *shared_parts)
    return (
        section_out[None],
        input_grad[None],
        final[8],
        final[0][None],
        final[1][None],
        final[6][None],
        final[3][None],
        final[7][None],
        final[5],
        final[4],
        final[2][None],
    )


def solution(mesh):
    placed = (
        P(None, "seq", None),
        P(),
        P("section", None, "head", "seq"),
        P(None, "seq", None),
        P("section", None),
        P("section", None, "head"),
        P("section", None, "head"),
        P("section", None, None),
        P("section", None, "head"),
        P("section", None, None),
        P("section", "head"),
        P("section", "head"),
        P("section", None, None),
    )
    return jax.shard_map(
        per_device,
        mesh=mesh,
        in_specs=placed,
        out_specs=(
            P("section", None, "seq", "head"),
            P("section", None, "seq", "head"),
            P("section", ("seq", "head")),
            P("section", "seq", "head"),
            P("section", "seq", "head"),
            P("section", ("seq", "head"), None),
            P("section", None, "head"),
            P("section", None, ("seq", "head")),
            P("section", "head"),
            P("section", "head"),
            P("section", "head", "seq"),
        ),
        check_vma=False,
    )
```

```python
import functools

import jax
import jax.numpy as jnp
from jax import lax
from jax.experimental import pallas as pl
from jax.experimental.pallas import tpu as pltpu
from jax.sharding import PartitionSpec as P

BLOCK = 256
HALF = BLOCK // 2
PAD = 16
EPS = 1e-05
F32 = jnp.float32
LOW = jnp.bfloat16
HIDDEN = -1e30
NN = ((1,), (0,))
NT = ((1,), (1,))
TN = ((0,), (0,))
VMEM_BYTES = 50 * 1024 * 1024
ALL_VMEM_BYTES = 63 * 1024 * 1024


def dot(a, b, dims):
    return lax.dot_general(a, b, (dims, ((), ())), preferred_element_type=F32)


def aligned(start, size):
    return pl.ds(pl.multiple_of(start, size), size)


def spread(cols, first, count, width):
    rows = cols.shape[0]
    lane = lax.broadcasted_iota(jnp.int32, (rows, count * width), 1)
    out = jnp.broadcast_to(cols[:, first : first + 1], (rows, count * width))
    for h in range(1, count):
        out = jnp.where(lane >= h * width, cols[:, first + h : first + h + 1], out)
    return out


def per_head(array, h, width):
    lane = lax.broadcasted_iota(jnp.int32, array.shape, 1)
    inside = (lane >= h * width) & (lane < (h + 1) * width)
    return jnp.where(inside, array, jnp.zeros_like(array))


def split_low(value):
    high = value.astype(LOW).astype(F32)
    return high, value - high


def column_of(row, size):
    return jnp.transpose(jnp.broadcast_to(row, (128, size)))


def sigmoid(v):
    return 0.5 * jnp.tanh(0.5 * v) + 0.5


def pick(flag, a, b):
    return jnp.where(flag, a, b)


class Sizes:
    def __init__(self, blocks, width, channels, heads, states, taps, head_axis, inner):
        self.blocks = blocks
        self.width = width
        self.channels = channels
        self.heads = heads
        self.head_width = channels // heads
        self.states = states
        self.lin = channels + 2 * states
        self.taps = taps
        self.head_axis = head_axis
        self.chunk = width // head_axis
        self.rows = blocks * HALF
        self.tokens = blocks * BLOCK
        self.inner = inner


def weight_copies(sz, layer, c, h, raw, got, wv, ov, sems):
    gate, inner, shared, out = raw
    ch = sz.channels
    cols = aligned(c * ch, ch)
    rows = aligned((h * 2 + c) * ch, ch)
    own, sent = [], []
    if wv is not None:
        own += [
            (gate.at[0, :, cols], wv.at[:, :ch]),
            (inner.at[0, :, cols], wv.at[:, ch : 2 * ch]),
            (shared.at[0], wv.at[:, 2 * ch :]),
        ]
        sent += [(got[0], wv)]
    if ov is not None:
        own += [(out.at[0, rows, :], ov)]
        sent += [(got[1], ov)]
    return [
        (c == layer, [pltpu.make_async_copy(p, q, sems.at[i]) for i, (p, q) in enumerate(own)]),
        (c != layer, [pltpu.make_async_copy(p, q, sems.at[i]) for i, (p, q) in enumerate(sent)]),
    ]


def run_copies(choices, start, wait):
    for flag, copies in choices:

        @pl.when(flag)
        def _(copies=copies):
            if start:
                for copy in copies:
                    copy.start()
            if wait:
                for copy in copies:
                    copy.wait()


def put_ordered(sz, dst, c, k, b, own, other):
    for r in range(len(own)):

        @pl.when(lax.rem(k - b + len(own), len(own)) == r)
        def _(r=r):
            put_pair(dst, c, own[r][:HALF, :], other[r][:HALF, :])


def put_pair(dst, c, own, other):
    dst[aligned(c * HALF, HALF), :] = own
    dst[aligned((1 - c) * HALF, HALF), :] = other


def far_first(count):
    return [0] + list(range(count - 1, 0, -1))


def put_pieces(sz, dst, c, h, own, other):
    own, other = (dict(zip(far_first(sz.head_axis), side)) for side in (own, other))
    for d in range(sz.head_axis):
        cols = aligned((h ^ d) * sz.chunk, sz.chunk)
        dst[aligned(c * HALF, HALF), cols] = own[d]
        dst[aligned((1 - c) * HALF, HALF), cols] = other[d]


def line_of(table, at):
    line = lax.broadcasted_iota(jnp.int32, table.shape, 0)
    return jnp.sum(jnp.where(line == at, table, 0.0), axis=0, keepdims=True)


def conv_forward(sz, ext, taps):
    pre = taps[0:1] * ext[5 : 5 + BLOCK, :]
    for j in range(1, sz.taps):
        pre = pre + taps[j : j + 1] * ext[5 + j : 5 + j + BLOCK, :]
    return pre


def decay_of(sz, cols, rp, h, mask):
    rows = cols[:, h : h + 1] + rp[12 + h : 13 + h, :]
    return jnp.exp(jnp.where(mask, rows, HIDDEN))


def lower_mask():
    t = lax.broadcasted_iota(jnp.int32, (BLOCK, BLOCK), 0)
    s = lax.broadcasted_iota(jnp.int32, (BLOCK, BLOCK), 1)
    return t >= s


def forward_kernel(sz, layer, slots, sc, *refs):
    n = sz.head_axis
    sources = 2 * slots if layer == 0 else 2 * n + 2 * slots
    src, refs = refs[:sources], refs[sources:]
    if layer == 1:
        table, refs = refs[0], refs[1:]
    gains, raw, got, halo, begin = refs[0:2], refs[2:6], refs[6:8], refs[8], refs[9]
    if layer == 1:
        ov, refs = refs[10], refs[1:]
    normed_o, gl_o, lin_o, ssd_o, inc_o, inv_o, part_o, unit_o, fin_o, sc_o, base_o = refs[10:21]
    refs = refs[21:]
    if layer == 1:
        mixed_o, refs = refs[0], refs[1:]
    else:
        tables_o, refs = refs[0:2], refs[2:]
    xs, ms, wv, ext, state, sems = refs
    b = pl.program_id(0)
    c, h, k = sc[0], sc[1], sc[3]
    ch, st = sz.channels, sz.states
    copies = weight_copies(sz, layer, c, h, raw, got, wv, None, sems)

    @pl.when(b == 0)
    def _():
        run_copies(copies, True, False)
        ext[0:8, :] = halo[...]
        state[...] = begin[...]
        for i in range(4):
            sc_o[i] = sc[i]

    mine = aligned(c * HALF, HALF)
    cols = aligned(h * sz.chunk, sz.chunk)
    if layer == 0:
        put_ordered(sz, xs, c, k, b, src[:slots], src[slots:])
        base_o[...] = xs[mine, cols]
        for r in range(slots):

            @pl.when(lax.rem(k - b + slots, slots) == r)
            def _(r=r):
                own = decay_table(rates_of(src[r]), c, sz.heads)
                other = decay_table(rates_of(src[slots + r]), c, sz.heads)
                tables_o[0][...] = pick(c == 0, own, other)
                tables_o[1][...] = pick(c == 0, other, own)

        rp = tables_o[0][...]
    else:
        put_pieces(sz, xs, c, h, [r[...] for r in src[:n]], [r[...] for r in src[n : 2 * n]])
        put_ordered(sz, ms, c, k, b, src[2 * n : 2 * n + slots], src[2 * n + slots :])
        base_o[...] = ms[mine, cols]
        mixed_o[...] = ms[...]
        rp = table[...]

    pv = pick(c == layer, gains[0][...], gains[1][...])
    x = xs[...].astype(F32)
    inv_in = lax.rsqrt(jnp.mean(x * x, axis=1, keepdims=True) + EPS)
    normed = (x * inv_in * pv[0:1, : sz.width]).astype(LOW)
    normed_o[...] = normed

    @pl.when(b == 0)
    def _():
        run_copies(copies, False, True)

    proj = dot(normed, wv[...], NN)
    gl = proj[:, :ch]
    gl_o[...] = gl
    lin = proj[:, ch:].astype(LOW)
    lin_o[...] = lin
    ext[8 : 8 + BLOCK, :] = lin.astype(F32)
    pre = conv_forward(sz, ext, pv[1:5, : sz.lin])
    ext[0:8, :] = ext[BLOCK : BLOCK + 8, :]
    act = (pre * sigmoid(pre)).astype(LOW)
    values, bm, cm = act[:, :ch], act[:, ch : ch + st], act[:, ch + st :]

    cols = jnp.transpose(rp)
    mask = lower_mask()
    gram = dot(cm, bm, NT)
    mixes, parts = [], []
    for i in range(sz.heads):
        mixes.append((gram * decay_of(sz, cols, rp, i, mask)).astype(LOW))
        parts.append(per_head(values, i, sz.head_width))
    intra = dot(jnp.concatenate(mixes, axis=1), jnp.concatenate(parts, axis=0), NN)

    low_state = state[...].astype(LOW)
    inc_o[0] = low_state
    ecum = spread(cols, sz.heads, sz.heads, sz.head_width)
    inter = dot(cm, low_state, NT) * ecum
    vf = values.astype(F32)
    carried = (vf * spread(cols, 2 * sz.heads, sz.heads, sz.head_width)).astype(LOW)
    local = dot(carried, bm, TN)
    for i in range(sz.heads):
        rows = slice(i * sz.head_width, (i + 1) * sz.head_width)
        total = cols[BLOCK - 1 : BLOCK, sz.heads + i : sz.heads + i + 1]
        state[rows, :] = total * state[rows, :] + local[rows]
    ssd = intra + inter + pv[6:7, :ch] * vf
    ssd_o[...] = ssd
    gated = ssd * (gl * sigmoid(gl))
    weighty = gated * pv[5:6, :ch]
    unit_o[...] = weighty.astype(LOW)

    lane = lax.broadcasted_iota(jnp.int32, (BLOCK, 128), 1)
    square = jnp.sum(gated * gated, axis=1, keepdims=True)
    if layer == 0:
        project = jnp.zeros_like(square)
    else:
        scaled_grad = dot(ms[...], ov[...], NN)
        project = jnp.sum(scaled_grad * weighty, axis=1, keepdims=True)
    stats = jnp.where(lane == 0, square, jnp.where(lane == 1, project, inv_in))
    stats = jnp.transpose(stats)
    part_o[...] = stats[0:2, :]
    inv_o[...] = stats[2:3, :]

    @pl.when(b == sz.blocks - 1)
    def _():
        fin_o[...] = state[...]


def scalar_lines(sz, lines):
    fill = [jnp.zeros((8 - sz.blocks, HALF), F32)] if sz.blocks < 8 else []
    high, low = split_low(jnp.concatenate(lines + fill, axis=0))
    table = jnp.concatenate([high, low], axis=0).astype(LOW)
    return jnp.concatenate([table] * (sz.chunk // HALF), axis=1)


def own_rows(sz, ref, which):
    blocks = [ref[aligned(b * BLOCK + which * HALF, HALF), :] for b in range(sz.blocks)]
    return jnp.concatenate(blocks, axis=0)


def project_kernel(sz, layer, deps, sc, unit_r, stats_r, *refs):
    raw, got, refs = refs[:4], refs[4:6], refs[6 + deps :]
    keep, send, sc_o, weights, sems = refs
    c, h = sc[0], sc[1]
    copies = weight_copies(sz, layer, c, h, raw, got, None, weights, sems)
    run_copies(copies, True, False)
    for i in range(4):
        sc_o[i] = sc[i]
    sides = []
    for which, out in ((c, keep), (1 - c, send)):
        sides.append((out, own_rows(sz, unit_r, which)))
        lines = [
            stats_r[0:1, aligned(b * BLOCK + which * HALF, HALF)] for b in range(sz.blocks)
        ]
        table = scalar_lines(sz, lines)
        for d in range(sz.head_axis):
            out[d, sz.rows :, :] = table
    run_copies(copies, False, True)
    for out, rows in sides:
        for d in range(sz.head_axis):
            chunk = weights[:, aligned((h ^ d) * sz.chunk, sz.chunk)]
            out[d, : sz.rows, :] = dot(rows, chunk, NN).astype(LOW)


def turn_kernel(sz, sc, *refs):
    raw, got = refs[:4], refs[4:6]
    wide_o, out_o, wv, ov, sems = refs[6:8], refs[8:10], refs[10], refs[11], refs[12]
    for layer in range(2):
        copies = weight_copies(sz, layer, sc[0], sc[1], raw, got, wv, ov, sems)
        run_copies(copies, True, True)
        wide_o[layer][...] = jnp.transpose(wv[...])
        out_o[layer][...] = jnp.transpose(ov[...])


def out_at(out, d):
    return out[d] if isinstance(out, tuple) else out.at[d]


def lift_kernel(sz, layer, deps, sc, cat_r, normed_r, zero_gains, one_gains, small_r, *refs):
    weights, refs = refs[0], refs[1 + deps :]
    keep, send, sc_o, common_o, wide = refs[0], refs[1:-3], *refs[-3:]
    c, h = sc[0], sc[1]
    for i in range(4):
        sc_o[i] = sc[i]
    wide[...] = jnp.zeros_like(wide)
    for which, out in ((c, keep), (1 - c, send)):
        rows = own_rows(sz, cat_r, which)
        along = jnp.zeros((sz.rows, 1), F32)
        for d in range(sz.head_axis):
            cols = aligned((h ^ d) * sz.chunk, sz.chunk)
            product = dot(rows, weights[:, cols], NN)
            out_at(out, d)[: sz.rows, :] = product.astype(LOW)
            blocks = [
                normed_r[aligned(b * BLOCK + which * HALF, HALF), cols] for b in range(sz.blocks)
            ]
            product = product * jnp.concatenate(blocks, axis=0).astype(F32)
            wide[0:1, cols] += jnp.sum(product, axis=0, keepdims=True)
            along = along + jnp.sum(product, axis=1, keepdims=True)
        lines = [
            jnp.transpose(jnp.broadcast_to(along[b * HALF : (b + 1) * HALF], (HALF, 128)))[0:1, :]
            for b in range(sz.blocks)
        ]
        table = scalar_lines(sz, lines)
        for d in range(sz.head_axis):
            out_at(out, d)[sz.rows :, :] = table
    gain_grad = wide[0:1, :] / pick(c == layer, zero_gains[0:1, :], one_gains[0:1, :])
    flat = [small_r[j : j + 1, sz.channels :] for j in range(sz.taps)]
    flat += [gain_grad[:, q * sz.chunk : (q + 1) * sz.chunk] for q in range(sz.head_axis)]
    high, low = split_low(jnp.concatenate(flat, axis=0))
    common_o[...] = jnp.concatenate([high, low], axis=0).astype(LOW)


def backward_kernel(sz, layer, deps, sc, *refs):
    n = sz.head_axis
    sources = 2 * n + 2 if layer == 0 else 1 + n
    src, refs = refs[:sources], refs[sources:]
    gl_r, lin_r, ssd_r, inc_r = refs[:4]
    table, gains, ov = refs[4], refs[5:7], refs[7]
    halo, halo_grad, begin = refs[8:11]
    refs = refs[11 + deps :]
    cat_o, scaled_o, small_o, sums_o, fin_o, rim_o, sc_o = refs[:7]
    refs = refs[7:]
    if layer == 0:
        mixed_o, refs = refs[0], refs[1:]
    ms, ext, back, state, heads_p, small = refs
    i_step = pl.program_id(0)
    b = sz.blocks - 1 - i_step
    c, h = sc[0], sc[1]
    ch, st = sz.channels, sz.states
    pv = pick(c == layer, gains[0][...], gains[1][...])
    rp = table[...]

    @pl.when(i_step == 0)
    def _():
        back[BLOCK : BLOCK + 8, :] = halo_grad[...]
        state[...] = begin[...]
        small[...] = jnp.zeros_like(small)
        for i in range(4):
            sc_o[i] = sc[i]
        if layer == 0:
            for i in range(2):
                extra = src[i * n][sz.rows :, :].astype(F32)
                for d in range(1, n):
                    extra = extra + src[i * n + d][sz.rows :, :].astype(F32)
                heads_p[8 * i : 8 * i + 8, :] = extra[0:8, :HALF] + extra[8:16, :HALF]

    if layer == 0:
        rows = aligned(b * HALF, HALF)
        put_pieces(
            sz, ms, c, h, [r[rows, :] for r in src[:n]], [r[rows, :] for r in src[n : 2 * n]]
        )
        halves = []
        for k in range(2):
            alpha = lax.rsqrt(line_of(src[2 * n + k][...], b) / sz.inner + EPS)
            beta = alpha * alpha * line_of(heads_p[...], 8 * k + b) / sz.inner
            halves.append((alpha, beta))
        alpha, beta = (
            pick(
                c == 0,
                jnp.concatenate([halves[0][q], halves[1][q]], axis=1),
                jnp.concatenate([halves[1][q], halves[0][q]], axis=1),
            )
            for q in range(2)
        )
    else:
        stats = src[1][...]
        for d in range(1, n):
            stats = stats + src[1 + d][...]
        alpha = lax.rsqrt(stats[0:1, :] / sz.inner + EPS)
        beta = alpha * alpha * alpha * stats[1:2, :] / sz.inner

    sub = lax.broadcasted_iota(jnp.int32, rp.shape, 0)
    cols = jnp.transpose(jnp.where(sub == 12, alpha, jnp.where(sub == 13, beta, rp)))
    alpha, beta = cols[:, 12:13], cols[:, 13:14]

    gl = gl_r[...]
    ssd = ssd_r[...]
    sig = sigmoid(gl)
    swish = gl * sig
    slope = sig * (1.0 + gl * (1.0 - sig))
    gated = ssd * swish
    if layer == 0:
        mixed_grad = ms[...]
        mixed_o[...] = mixed_grad
    else:
        mixed_grad = src[0][...]
    scaled_grad = dot(mixed_grad, ov[...], NN)
    gain = pv[5:6, :ch]
    normal = gated * alpha
    small[4:5, :ch] += jnp.sum(scaled_grad * normal, axis=0, keepdims=True)
    scaled_o[...] = (normal * gain).astype(LOW)
    gated_grad = alpha * (scaled_grad * gain) - beta * gated
    ssd_grad = (gated_grad * swish).astype(LOW)
    gate_grad = (gated_grad * ssd * slope).astype(LOW)
    sgf = ssd_grad.astype(F32)

    before = lin_r[pl.ds(pl.multiple_of(jnp.maximum(b * BLOCK - 16, 0), 16), 16), :]
    ext[0:8, :] = pick(b > 0, before.astype(F32)[8:16, :], halo[...])
    ext[8 : 8 + BLOCK, :] = lin_r[aligned(b * BLOCK, BLOCK), :].astype(F32)
    taps = pv[1:5, : sz.lin]
    pre = conv_forward(sz, ext, taps)
    psig = sigmoid(pre)
    pact = pre * psig
    pslope = psig * (1.0 + pre * (1.0 - psig))
    act = pact.astype(LOW)
    values, bm, cm = act[:, :ch], act[:, ch : ch + st], act[:, ch + st :]
    vf = values.astype(F32)
    small[5:6, :ch] += jnp.sum(sgf * vf, axis=0, keepdims=True)

    mask = lower_mask()
    gram = dot(cm, bm, NT)
    gram_grad = jnp.zeros((BLOCK, BLOCK), F32)
    mixes, parts = [], []
    for i in range(sz.heads):
        decay = decay_of(sz, cols, rp, i, mask)
        mixes.append((gram * decay).astype(LOW))
        parts.append(per_head(ssd_grad, i, sz.head_width))
        gram_grad = gram_grad + dot(parts[-1], values, NT) * decay
    intra_grad = dot(jnp.concatenate(mixes, axis=0), jnp.concatenate(parts, axis=0), TN)

    ecum = spread(cols, sz.heads, sz.heads, sz.head_width)
    to_end = spread(cols, 2 * sz.heads, sz.heads, sz.head_width)
    inter_grad = (sgf * ecum).astype(LOW)
    low_state = state[...].astype(LOW)
    carried = (vf * to_end).astype(LOW)
    carried_grad = dot(bm, low_state, NT)
    gram_low = gram_grad.astype(LOW)
    b_grad = dot(gram_low, cm, TN) + dot(carried, low_state, NN)
    c_grad = dot(gram_low, bm, NN) + dot(inter_grad, inc_r[0], NN)
    value_grad = intra_grad + pv[6:7, :ch] * sgf + carried_grad * to_end
    entry = dot(inter_grad, cm, TN)
    for i in range(sz.heads):
        rows = slice(i * sz.head_width, (i + 1) * sz.head_width)
        total = cols[BLOCK - 1 : BLOCK, sz.heads + i : sz.heads + i + 1]
        state[rows, :] = total * state[rows, :] + entry[rows]

    pre_grad = jnp.concatenate([value_grad, b_grad, c_grad], axis=1) * pslope
    back[0:BLOCK, :] = pre_grad
    lin_grad = taps[0:1] * back[sz.taps - 1 : sz.taps - 1 + BLOCK, :]
    for j in range(1, sz.taps):
        at = sz.taps - 1 - j
        lin_grad = lin_grad + taps[j : j + 1] * back[at : at + BLOCK, :]
    for j in range(sz.taps):
        small[j : j + 1, :] += jnp.sum(pre_grad * ext[5 + j : 5 + j + BLOCK, :], axis=0, keepdims=True)
    back[BLOCK : BLOCK + 8, :] = back[0:8, :]
    cat_o[...] = jnp.concatenate([gate_grad, lin_grad.astype(LOW)], axis=1)

    @pl.when(i_step == sz.blocks - 1)
    def _():
        fin_o[...] = state[...]
        rim_o[...] = back[0:8, :]
        sums = small[...]
        flat = [sums[j : j + 1, :ch] for j in range(sz.taps + 2)]
        flat = [jnp.concatenate(flat[j : j + 3], axis=1) for j in range(0, len(flat), 3)]
        flat = flat + [jnp.zeros_like(flat[0])] * (4 - len(flat))
        high, low = split_low(jnp.concatenate(flat, axis=0))
        rest = jnp.zeros((PAD - 8, high.shape[1]), F32)
        small_o[...] = jnp.concatenate([high, low, rest], axis=0).astype(LOW)
        sums_o[...] = sums


def weights_kernel(sz, seq, deps, halved, sc, normed, cat, mixed, scaled, small, *refs):
    refs = refs[deps:]
    count = seq + halved
    sc_o, outs, heads, full, wide = refs[0], refs[1 : count + 1], refs[count + 1 : -2], refs[-2], refs[-1]
    for i in range(4):
        sc_o[i] = sc[i]
    ch, st = sz.channels, sz.states
    step = sz.chunk
    for q in range(sz.head_axis):
        at = slice(q * step, (q + 1) * step)
        grads = dot(normed[:, at], cat[...], TN)
        full[at, : 2 * ch] = grads[:, : 2 * ch].astype(LOW)
        wide[at, :] = grads[:, 2 * ch :]
        full[at, 2 * ch :] = dot(mixed[:, at], scaled[...], TN).astype(LOW)
    rows = sz.width // seq
    part = rows // sz.head_axis
    for i, out in enumerate(outs):
        r = i - (halved and i > seq // 2)
        at = lax.rem(sc[2] + r, seq) * rows
        if halved and i == seq // 2:
            out[...] = full[aligned(at, rows // 2), :]
            continue
        if halved and i == seq // 2 + 1:
            out[: rows // 2, :] = full[aligned(at + rows // 2, rows // 2), :]
        else:
            out[:rows, :] = full[aligned(at, rows), :]
        out[out.shape[0] - PAD :, :] = small[...]
    for d, out in enumerate(heads):
        lines = [
            wide[aligned(lax.rem(sc[2] + r, seq) * rows + (sc[1] ^ d) * part, part), :]
            for r in range(seq)
        ]
        out[...] = jnp.concatenate(lines, axis=0).astype(LOW)


def resplit(extra):
    half = extra.shape[0] // 2
    high, low = split_low(extra[:half, :] + extra[half:, :])
    return jnp.concatenate([high, low], axis=0)


def join_kernel(sz, parts, riders, deps, sc, keep, *refs):
    n = sz.head_axis
    recv, refs = refs[0] if parts == 1 else refs[:parts], refs[parts:]
    more = [(refs[i * (n + 1)], refs[i * (n + 1) + 1 : (i + 1) * (n + 1)]) for i in range(riders)]
    refs = refs[riders * (n + 1) + deps :]
    sc_o, outs = refs[0], refs[1:]
    rows = sz.rows
    for i in range(4):
        sc_o[i] = sc[i]
    extra = resplit(keep[0, rows:, :].astype(F32) + out_at(recv, 0)[rows:, :].astype(F32))
    for d, out in enumerate(outs):
        both = keep[d, :rows, :].astype(F32) + out_at(recv, d)[:rows, :].astype(F32)
        out[:rows, :] = both.astype(out.dtype)
        out[rows : rows + PAD, :] = extra.astype(out.dtype)
        at = rows + PAD
        for common, rider in more:
            size = rider[d].shape[0]
            out[at : at + PAD, :] = common[...].astype(out.dtype)
            out[at + PAD : at + PAD + size, :] = rider[d][...].astype(out.dtype)
            at += PAD + size


def total_of(parts, rows):
    total = parts[0][rows, :].astype(F32)
    for p in parts[1:]:
        total = total + p[rows, :].astype(F32)
    return total


def output_kernel(sz, layer, sc, *refs):
    n = sz.head_axis
    parts, refs = refs[:n], refs[n:]
    resid = refs[0]
    res_o, low_o, mixed_o, square_o, sc_o = refs[-5:]
    for i in range(4):
        sc_o[i] = sc[i]
    extra = total_of(parts, slice(sz.rows, sz.rows + PAD))
    square = extra[0:8, :HALF] + extra[8:16, :HALF]
    square_o[...] = square
    inv = lax.rsqrt(square / sz.inner + EPS)
    for b in range(sz.blocks):
        rows = slice(b * HALF, (b + 1) * HALF)
        col = column_of(inv[b : b + 1, :], HALF)[:, 0:1]
        mixed = total_of(parts, rows) * col
        res = resid[rows, :].astype(F32) + mixed
        res_o[rows, :] = res
        low_o[rows, :] = res.astype(LOW)
        mixed_o[rows, :] = mixed


def input_kernel(sz, layer, sc, *refs):
    n = sz.head_axis
    parts, refs = refs[:n], refs[n:]
    resid, outg, inv_r, gains = refs[0], refs[1], refs[2], refs[3:5]
    refs = refs[5:]
    if layer == 1:
        mixed = refs[0]
        grad_o, low_o, sc_o = refs[-3:]
    else:
        one_low = refs[0]
        low_o, swap_o, shared_o, sc_o = refs[-4:]
    for i in range(4):
        sc_o[i] = sc[i]
    c, h = sc[0], sc[1]
    first = c == 0
    mine = aligned(h * sz.chunk, sz.chunk)
    gain = pick(c == layer, gains[0][0:1, mine], gains[1][0:1, mine])
    extra = total_of(parts, slice(sz.rows, sz.rows + PAD))
    along = extra[0:8, :HALF] + extra[8:16, :HALF]
    tops, lows = [], []
    for b in range(sz.blocks):
        rows = slice(b * HALF, (b + 1) * HALF)
        at = b * BLOCK
        inv_row = pick(c == 0, inv_r[:, at : at + HALF], inv_r[:, at + HALF : at + BLOCK])
        inv = column_of(inv_row, HALF)[:, 0:1]
        share = column_of(along[b : b + 1, :] / sz.width, HALF)[:, 0:1]
        total = total_of(parts, rows)
        base = resid[rows, :].astype(F32)
        grad = outg[rows, :].astype(F32) + inv * (total * gain - base * (inv * share))
        low = grad.astype(LOW)
        low_o[rows, :] = low
        if layer == 0:
            swap_o[rows, :] = pick(first, one_low[rows, :], low)
        else:
            grad_o[rows, :] = grad
            dots = jnp.sum(low.astype(F32) * mixed[rows, :], axis=1, keepdims=True)
            row = jnp.transpose(jnp.broadcast_to(dots, (HALF, 128)))[0:1, :]
            high, rest = split_low(row)
            tops.append(high)
            lows.append(rest)
    if layer == 1:
        fill = [jnp.zeros((8 - sz.blocks, HALF), F32)] if sz.blocks < 8 else []
        extra = jnp.concatenate(tops + fill + lows + fill, axis=0)
        extra = jnp.concatenate([extra] * (sz.chunk // HALF), axis=1)
        low_o[sz.rows :, :] = extra.astype(LOW)
    else:
        size = shared_o.shape[0]
        at = sz.rows + PAD
        zero = total_of(parts, slice(at, at + size))
        one = total_of(parts, slice(at + size, at + 2 * size))
        zero, one = (jnp.concatenate([resplit(v[:PAD]), v[PAD:]], axis=0) for v in (zero, one))
        shared_o[...] = pick(first, zero, one)
        swap_o[sz.rows :, :] = pick(first, one, zero).astype(LOW)


def sum_kernel(sz, last, sc, *refs):
    if last:
        parts, done, outs = refs[:-3], refs[-3], refs[-2:]
    else:
        parts, outs = refs[:-1], refs[-1:]
    rows = outs[0].shape[0] - PAD
    values = [p[...].astype(F32) for p in parts if p.shape == outs[0].shape]
    halves = [p[...].astype(F32) for p in parts if p.shape != outs[0].shape]
    total = values[0]
    for value in values[1:] + ([jnp.concatenate(halves, axis=0)] if halves else []):
        total = total + value
    extra = total[rows:]
    high, low = split_low(extra[0:4, :] + extra[4:8, :])
    extra = jnp.concatenate([high, low, jnp.zeros((PAD - 8, extra.shape[1]), F32)], axis=0)
    sums = jnp.concatenate([total[:rows], extra], axis=0).astype(LOW)
    if last:
        outs[0][...] = pick(sc[0] == 0, sums, done[...])
        outs[1][...] = pick(sc[0] == 0, done[...], sums)
    else:
        outs[0][...] = sums


def final_kernel(sz, seq, sc, own, got, *refs):
    pieces, refs = refs[:-9], refs[-9:]
    gate_o, inner_o, out_o, conv_o, norm_o, skip_o, shared_o, taps_o, gain_o = refs
    c = sc[0]
    ch = sz.channels
    rows = own.shape[0] - PAD
    lane = lax.broadcasted_iota(jnp.int32, skip_o.shape, 1)
    skip = jnp.zeros(skip_o.shape, F32)
    for i in range(2):
        which = pick(i == 0, c, 1 - c)
        to = aligned(which * ch, ch)
        sums = (own if i == 0 else got)[...].astype(F32)
        gate_o[:, to] = sums[:rows, :ch]
        inner_o[:, to] = sums[:rows, ch : 2 * ch]
        out_o[to, :] = jnp.transpose(sums[:rows, 2 * ch :])
        lines = sums[rows : rows + 4, :] + sums[rows + 4 : rows + 8, :]
        for j in range(sz.taps):
            conv_o[j : j + 1, to] = lines[j // 3 : j // 3 + 1, (j % 3) * ch : (j % 3 + 1) * ch]
        norm_o[:, to] = lines[1:2, ch : 2 * ch]
        skips = lines[1:2, 2 * ch :]
        for q in range(sz.heads):
            part = jnp.sum(per_head(skips, q, sz.head_width), axis=1, keepdims=True)
            skip = jnp.where(lane == which * sz.heads + q, part, skip)
    skip_o[...] = skip
    total = total_of(pieces, slice(BLOCK, None))
    shared_o[...] = total[PAD:]
    common = total[: PAD // 2] + total[PAD // 2 : PAD]
    place = sc[2] * sz.head_axis + sc[1]
    span = common.shape[1]
    size = span // (seq * sz.head_axis)
    turned = pltpu.roll(common, lax.rem(span - place * size, span), 1)
    taps_o[...] = turned[: sz.taps, :size]
    size = sz.width // (seq * sz.head_axis)
    at = place * size
    line = jnp.broadcast_to(line_of(common, sz.taps + at // span), common.shape)
    turned = pltpu.roll(line, lax.rem(span - lax.rem(at, span), span), 1)
    gain_o[...] = turned[:1, :size]


def slice_kernel(sz, slots, sc, order, tokens, rates, *refs):
    outs, sc_o, sems = refs[:slots], refs[slots], refs[slots + 1]
    copies = []
    for r in range(slots):
        rows = tokens.at[order[lax.rem(sc[3] + r, slots)], aligned(sc[0] * HALF, HALF), :]
        copies.append(pltpu.make_async_copy(rows, outs[r].at[:HALF], sems.at[r]))
    for copy in copies:
        copy.start()
    for i in range(4):
        sc_o[i] = sc[i]
    for r in range(slots):
        first, rest = split_low(rates[0, order[lax.rem(sc[3] + r, slots)]])
        second, rest = split_low(rest)
        lines = jnp.concatenate([first, second, rest, jnp.zeros_like(rest)], axis=1)
        lines = jnp.concatenate([lines, jnp.zeros_like(lines)], axis=0)
        outs[r][HALF:, :] = lines.astype(LOW)
    for copy in copies:
        copy.wait()


def rates_of(piece):
    lines = piece[HALF:, :].astype(F32)[:8, :]
    return (lines[:, :BLOCK] + lines[:, BLOCK : 2 * BLOCK]) + lines[:, 2 * BLOCK : 3 * BLOCK]


def pack_kernel(sz, sc, order, grads, gate, inner, shared, out, in_gain, conv_i, conv_s, skip, norm, *refs):
    w_o, o_o, mine_o, send_o, sems = *refs[:4], refs[-1]
    c, h = sc[0], sc[1]
    ch = sz.channels
    outs = refs[4:-1]
    slices = []
    for r, to in enumerate(outs):
        rows = grads.at[order[lax.rem(sc[3] + r, len(outs))], aligned(c * HALF, HALF), :]
        slices.append(pltpu.make_async_copy(rows, to, sems.at[4 + r]))
    cols = aligned((1 - c) * ch, ch)
    rows = aligned((h * 2 + 1 - c) * ch, ch)
    copies = [
        pltpu.make_async_copy(gate.at[0, :, cols], w_o.at[:, :ch], sems.at[0]),
        pltpu.make_async_copy(inner.at[0, :, cols], w_o.at[:, ch : 2 * ch], sems.at[1]),
        pltpu.make_async_copy(shared.at[0], w_o.at[:, 2 * ch :], sems.at[2]),
        pltpu.make_async_copy(out.at[0, rows, :], o_o, sems.at[3]),
        *slices,
    ]
    for copy in copies:
        copy.start()
    for which, ref in ((c, mine_o), (1 - c, send_o)):
        at = aligned(which * ch, ch)
        ref[...] = jnp.zeros_like(ref)
        ref[0:1, :] = in_gain[...]
        ref[1 : 1 + sz.taps, :ch] = conv_i[0, :, at]
        ref[1 : 1 + sz.taps, ch : sz.lin] = conv_s[0]
        ref[5:6, :ch] = norm[:, at]
        low = spread(skip[...], 0, sz.heads, sz.head_width)
        high = spread(skip[...], sz.heads, sz.heads, sz.head_width)
        ref[6:7, :ch] = pick(which == 0, low, high)
    for copy in copies:
        copy.wait()


def decay_table(rate, c, n):
    lane = lax.broadcasted_iota(jnp.int32, rate.shape, 1)
    cum = rate
    step = 1
    while step < BLOCK:
        cum = cum + jnp.where(lane >= step, pltpu.roll(cum, step, 1), 0.0)
        step *= 2
    end = cum[:, BLOCK - 1 :]
    lines = [cum, jnp.exp(cum), jnp.exp(end - cum) * -rate, jnp.log(-rate) - cum]
    low = jnp.concatenate([v[:n] for v in lines], axis=0)
    high = jnp.concatenate([v[n:] for v in lines], axis=0)
    return pick(c == 0, low, high)


def leave_kernel(sz, slots, riders, sc, zero_own, zero_other, one_own, one_other, *refs):
    c = sc[0]
    if riders:
        shared, refs = refs[0], refs[1:]
        total = shared[...] + one_other[sz.rows :, :].astype(F32)
        extra = resplit(total[:PAD])
        part = (total.shape[0] - PAD) // riders
    outs = refs[:slots]
    for i in range(4):
        refs[slots][i] = sc[i]
    for r in range(slots):
        rows = aligned(lax.rem(sc[3] + r, slots) * HALF, HALF)
        own = pick(c == 0, zero_own[rows, :], one_own[rows, :])
        other = pick(c == 0, zero_other[rows, :], one_other[rows, :])
        put_pair(outs[r], c, own, other)
        if riders:
            lines = [extra, total[PAD + r * part : PAD + (r + 1) * part]]
            outs[r][BLOCK:, :] = jnp.concatenate(lines, axis=0).astype(LOW)


def home_kernel(slots, sc, *refs):
    early, late, out, grad = refs[:slots], refs[slots : 2 * slots], refs[-3], refs[-2]
    for i in range(4):
        refs[-1][i] = sc[i]
    first = sc[0] == 0
    for r in range(slots):
        at = lax.rem(sc[3] - r + slots, slots)
        out[at] = pick(first, early[r][...], late[r][:BLOCK, :]).astype(F32)
        grad[at] = pick(first, late[r][:BLOCK, :], early[r][...]).astype(F32)


def whole(shape):
    return pl.BlockSpec(shape, lambda *_: (0,) * len(shape))


def per_device(
    tokens,
    slot_order,
    log_decay,
    grad_out,
    in_gain,
    w_gate,
    w_inner,
    w_shared,
    conv_inner,
    conv_shared,
    d_skip,
    norm_gain,
    w_out,
):
    slots = tokens.shape[0]
    span = tokens.shape[1]
    width = tokens.shape[2]
    seq = lax.axis_size("seq")
    head_axis = lax.axis_size("head")
    cores = lax.axis_size("section")
    spans = seq // slots
    c = lax.axis_index("section")
    z = lax.axis_index("seq")
    h = lax.axis_index("head")
    k = lax.rem(z, slots)
    inner_dev = w_gate.shape[2]
    channels = inner_dev // cores
    shared = w_shared.shape[2]
    heads_dev = d_skip.shape[1]
    taps = conv_inner.shape[1]
    sz = Sizes(
        slots * span // BLOCK,
        width,
        channels,
        heads_dev // cores,
        shared // 2,
        taps,
        head_axis,
        inner_dev * head_axis,
    )
    first = c == 0
    swap = [(0, 1), (1, 0)]
    nb, tok, rows, chunk = sz.blocks, sz.tokens, sz.rows, sz.chunk

    def cross(x):
        return lax.ppermute(x, "section", swap)

    def turn(x, r):
        pairs = [(i, i // slots * slots + (i % slots + r) % slots) for i in range(seq)]
        return lax.ppermute(x, "seq", pairs) if r else x

    def over_heads(x, d):
        return x if d == 0 else lax.ppermute(x, "head", [(i, i ^ d) for i in range(head_axis)])

    def next_span(x, way):
        pairs = [(i, i + way * slots) for i in range(seq) if 0 <= i + way * slots < seq]
        return lax.ppermute(x, "seq", pairs)

    def shape(dims, dtype):
        return jax.ShapeDtypeStruct(dims, dtype)

    prefetch = functools.partial(pltpu.PrefetchScalarGridSpec, num_scalar_prefetch=1)
    options = pltpu.CompilerParams(vmem_limit_bytes=VMEM_BYTES)
    from_hbm = pltpu.CompilerParams(vmem_limit_bytes=ALL_VMEM_BYTES)
    anywhere = pl.BlockSpec(memory_space=pl.ANY)
    smem = pl.BlockSpec(memory_space=pltpu.SMEM)
    vmem = pl.BlockSpec(memory_space=pltpu.VMEM)
    index_shape = shape((4,), jnp.int32)

    def cost(flops, moved):
        return pl.CostEstimate(flops=int(flops), bytes_accessed=int(moved), transcendentals=0)

    def to_members(pieces):
        return [turn(x, r) for r, x in enumerate(pieces)]

    sc = jnp.stack([c, h, z, k]).astype(jnp.int32)
    *tok_slices, sc = pl.pallas_call(
        functools.partial(slice_kernel, sz, slots),
        in_specs=[smem, smem, anywhere, vmem],
        out_specs=[vmem] * slots + [smem],
        out_shape=[shape((HALF + PAD, width), LOW)] * slots + [index_shape],
        scratch_shapes=[pltpu.SemaphoreType.DMA((slots,))],
        compiler_params=from_hbm,
    )(sc, slot_order, tokens, log_decay)
    tok_pieces = to_members(tok_slices)
    tok_others = [cross(x) for x in tok_pieces]

    wide = 2 * channels + shared
    w_sent, o_sent, pv_mine, pv_sent, *out_slices = pl.pallas_call(
        functools.partial(pack_kernel, sz),
        in_specs=[smem, smem] + [anywhere] * 5 + [vmem] * 5,
        out_specs=[vmem] * (4 + slots),
        out_shape=[
            shape((width, wide), LOW),
            shape((channels, width), LOW),
            shape((16, width), F32),
            shape((16, width), F32),
        ]
        + [shape((HALF, width), LOW)] * slots,
        scratch_shapes=[pltpu.SemaphoreType.DMA((4 + slots,))],
        compiler_params=from_hbm,
    )(
        sc, slot_order, grad_out, w_gate, w_inner, w_shared, w_out,
        in_gain, conv_inner, conv_shared, d_skip, norm_gain,
    )
    raw = [w_gate, w_inner, w_shared, w_out]
    sent = [cross(w_sent), cross(o_sent)]
    gains = [pv_mine, cross(pv_sent)]

    def span_total(table):
        ends = table[: sz.heads, BLOCK - 1 :: BLOCK]
        return jnp.repeat(jnp.exp(jnp.sum(ends, axis=1)), sz.head_width)[:, None]

    parts_shape = shape((head_axis, rows + PAD, chunk), LOW)
    weight_specs = [anywhere] * 6
    wide_weights = pltpu.VMEM((width, wide), LOW)
    out_weights = pltpu.VMEM((channels, width), LOW)
    copy_sems = pltpu.SemaphoreType.DMA((4,))
    dense = 2 * tok * width * (wide + channels)

    def forward(layer, sc, sources):
        def at(b, _):
            return (b, 0)

        piece = pl.BlockSpec((HALF, chunk), at)
        table = pl.BlockSpec((16, BLOCK), lambda b, _: (0, b))
        if layer == 0:
            src_specs = [whole((HALF + PAD, width))] * (2 * slots)
            more_specs = [table, table]
            more_shapes = [shape((16, tok), F32)] * 2
        else:
            src_specs = [piece] * (2 * head_axis) + [whole((HALF, width))] * (2 * slots) + [table]
            more_specs = [pl.BlockSpec((BLOCK, width), at)]
            more_shapes = [shape((tok, width), LOW)]

        last = [] if layer == 0 else [turned[3]]

        def call(halo, begin):
            return pl.pallas_call(
                functools.partial(forward_kernel, sz, layer, slots),
                grid_spec=prefetch(
                    grid=(nb,),
                    in_specs=src_specs
                    + [whole((16, width)), whole((16, width))]
                    + weight_specs
                    + [whole((8, sz.lin)), whole((channels, sz.states))]
                    + [whole(x.shape) for x in last],
                    out_specs=[
                        pl.BlockSpec((BLOCK, width), at),
                        pl.BlockSpec((BLOCK, channels), at),
                        pl.BlockSpec((BLOCK, sz.lin), at),
                        pl.BlockSpec((BLOCK, channels), at),
                        pl.BlockSpec((1, channels, sz.states), lambda b, _: (b, 0, 0)),
                        pl.BlockSpec((1, BLOCK), lambda b, _: (0, b)),
                        pl.BlockSpec((2, BLOCK), lambda b, _: (0, b)),
                        pl.BlockSpec((BLOCK, channels), at),
                        whole((channels, sz.states)),
                        smem,
                        piece,
                    ]
                    + more_specs,
                    scratch_shapes=[
                        pltpu.VMEM((BLOCK, width), LOW),
                        pltpu.VMEM((BLOCK, width), LOW),
                        wide_weights,
                        pltpu.VMEM((BLOCK + 8, sz.lin), F32),
                        pltpu.VMEM((channels, sz.states), F32),
                        copy_sems,
                    ],
                ),
                out_shape=[
                    shape((tok, width), LOW),
                    shape((tok, channels), F32),
                    shape((tok, sz.lin), LOW),
                    shape((tok, channels), F32),
                    shape((nb, channels, sz.states), LOW),
                    shape((1, tok), F32),
                    shape((2, tok), F32),
                    shape((tok, channels), LOW),
                    shape((channels, sz.states), F32),
                    index_shape,
                    shape((rows, chunk), LOW),
                ]
                + more_shapes,
                compiler_params=options,
                cost_estimate=cost(6 * dense, 16e6),
            )(sc, *sources, *gains, *raw, *sent, halo, begin, *last)

        halo = jnp.zeros((8, sz.lin), F32)
        begin = jnp.zeros((channels, sz.states), F32)
        if spans == 1:
            return call(halo, begin), halo
        trial = call(halo, begin)
        halo = next_span(trial[2][tok - 8 :].astype(F32), 1)
        local = call(halo, begin)[8]
        total = span_total(trial[11] if layer == 0 else sources[-1])
        for _ in range(spans - 1):
            begin = next_span(total * begin + local, 1)
        return call(halo, begin), halo

    def backward(layer, sc, sources, saved, decays, halo, deps):
        def at(i, _):
            return (nb - 1 - i, 0)

        if layer == 0:
            src_specs = [whole(s.shape) for s in sources]
        else:
            stat = pl.BlockSpec((2, BLOCK), lambda i, _: (0, nb - 1 - i))
            src_specs = [pl.BlockSpec((BLOCK, width), at)] + [stat] * head_axis
        gl, lin, ssd, inc = saved
        mixed_spec = [pl.BlockSpec((BLOCK, width), at)] if layer == 0 else []
        mixed_shape = [shape((tok, width), LOW)] if layer == 0 else []

        def call(halo_grad, begin):
            return pl.pallas_call(
                functools.partial(backward_kernel, sz, layer, len(deps)),
                grid_spec=prefetch(
                    grid=(nb,),
                    in_specs=src_specs
                    + [
                        pl.BlockSpec((BLOCK, channels), at),
                        whole(lin.shape),
                        pl.BlockSpec((BLOCK, channels), at),
                        pl.BlockSpec((1, channels, sz.states), lambda i, _: (nb - 1 - i, 0, 0)),
                        pl.BlockSpec((16, BLOCK), lambda i, _: (0, nb - 1 - i)),
                        whole((16, width)),
                        whole((16, width)),
                        whole((width, channels)),
                        whole((8, sz.lin)),
                        whole((8, sz.lin)),
                        whole((channels, sz.states)),
                    ]
                    + [anywhere] * len(deps),
                    out_specs=[
                        pl.BlockSpec((BLOCK, wide), at),
                        pl.BlockSpec((BLOCK, channels), at),
                        whole((PAD, 3 * channels)),
                        whole((8, sz.lin)),
                        whole((channels, sz.states)),
                        whole((8, sz.lin)),
                        smem,
                    ]
                    + mixed_spec,
                    scratch_shapes=[
                        pltpu.VMEM((BLOCK, width), LOW),
                        pltpu.VMEM((BLOCK + 8, sz.lin), F32),
                        pltpu.VMEM((BLOCK + 8, sz.lin), F32),
                        pltpu.VMEM((channels, sz.states), F32),
                        pltpu.VMEM((PAD, HALF), F32),
                        pltpu.VMEM((8, sz.lin), F32),
                    ],
                ),
                out_shape=[
                    shape((tok, wide), LOW),
                    shape((tok, channels), LOW),
                    shape((PAD, 3 * channels), LOW),
                    shape((8, sz.lin), F32),
                    shape((channels, sz.states), F32),
                    shape((8, sz.lin), F32),
                    index_shape,
                ]
                + mixed_shape,
                compiler_params=options,
                cost_estimate=cost(8 * dense, 16e6),
            )(
                sc, *sources, gl, lin, ssd, inc, decays, *gains, turned[2 + layer],
                halo, halo_grad, begin, *deps,
            )

        halo_grad = jnp.zeros((8, sz.lin), F32)
        begin = jnp.zeros((channels, sz.states), F32)
        if spans == 1:
            return call(halo_grad, begin)
        local = call(halo_grad, begin)[4]
        for _ in range(spans - 1):
            begin = next_span(span_total(decays) * begin + local, -1)
        halo_grad = next_span(call(halo_grad, begin)[5], -1)
        return call(halo_grad, begin)

    def project(layer, sc, unit, stats, deps):
        return pl.pallas_call(
            functools.partial(project_kernel, sz, layer, len(deps)),
            in_specs=[smem, vmem, vmem] + weight_specs + [anywhere] * len(deps),
            out_specs=[vmem, vmem, smem],
            out_shape=[parts_shape, parts_shape, index_shape],
            scratch_shapes=[out_weights, copy_sems],
            compiler_params=options,
            cost_estimate=cost(dense / 4, 4e6),
        )(sc, unit, stats, *raw, *sent, *deps)

    def lift(layer, sc, cat, normed, small, deps):
        outs = pl.pallas_call(
            functools.partial(lift_kernel, sz, layer, len(deps)),
            in_specs=[smem] + [vmem] * 6 + [anywhere] * len(deps),
            out_specs=[vmem] * (1 + head_axis) + [smem, vmem],
            out_shape=[parts_shape]
            + [shape(parts_shape.shape[1:], LOW)] * head_axis
            + [index_shape, shape((PAD, chunk), LOW)],
            scratch_shapes=[pltpu.VMEM((8, width), F32)],
            compiler_params=options,
            cost_estimate=cost(dense, 8e6),
        )(sc, cat, normed, *gains, small, turned[layer], *deps)
        return outs[0], list(outs[1:-2]), outs[-2], outs[-1]

    def scatter(sc, keep, send, riders=(), deps=()):
        size = rows + PAD + sum(PAD + rider[1].shape[0] for rider in riders)
        flat = [x for rider in riders for x in rider]
        got = [cross(x) for x in (send if isinstance(send, list) else [send])]
        joined = pl.pallas_call(
            functools.partial(join_kernel, sz, len(got), len(riders), len(deps)),
            in_specs=[smem] + [vmem] * (1 + len(got) + len(flat)) + [anywhere] * len(deps),
            out_specs=[smem] + [vmem] * head_axis,
            out_shape=[index_shape, shape((size, chunk), F32)]
            + [shape((size, chunk), LOW)] * (head_axis - 1),
            compiler_params=options,
        )(sc, keep, *got, *flat, *deps)
        return [over_heads(joined[1 + d], d) for d in far_first(head_axis)], joined[0]

    def gather(low):
        own = [over_heads(low, d) for d in far_first(head_axis)]
        return own + [cross(x) for x in own]

    turned = pl.pallas_call(
        functools.partial(turn_kernel, sz),
        in_specs=[smem] + weight_specs,
        out_specs=[vmem] * 4,
        out_shape=[shape((wide, width), LOW)] * 2 + [shape((width, channels), LOW)] * 2,
        scratch_shapes=[wide_weights, out_weights, copy_sems],
        compiler_params=options,
        cost_estimate=cost(1e9, 8e6),
    )

    def section_output(layer, sc, parts, resid, deps=()):
        return pl.pallas_call(
            functools.partial(output_kernel, sz, layer),
            in_specs=[smem] + [vmem] * (head_axis + 1) + [anywhere] * len(deps),
            out_specs=[vmem] * 4 + [smem],
            out_shape=[
                shape((rows, chunk), F32),
                shape((rows, chunk), LOW),
                shape((rows, chunk), F32),
                shape((8, HALF), F32),
                index_shape,
            ],
            compiler_params=options,
        )(sc, *parts, resid, *deps)

    part = width // seq
    columns = 3 * channels
    share = part // head_axis
    shared_size = seq * share + PAD

    def section_input(layer, sc, parts, *others, deps=()):
        if layer == 0:
            outs = [
                shape((rows + PAD, chunk), LOW),
                shape((rows + shared_size, chunk), LOW),
                shape((shared_size, chunk), F32),
            ]
        else:
            outs = [shape((rows, chunk), F32), shape((rows + PAD, chunk), LOW)]
        return pl.pallas_call(
            functools.partial(input_kernel, sz, layer),
            in_specs=[smem] + [vmem] * (head_axis + len(others)) + [anywhere] * len(deps),
            out_specs=[vmem] * len(outs) + [smem],
            out_shape=outs + [index_shape],
            compiler_params=options,
        )(sc, *parts, *others, *deps)

    def weight_grads(sc, normed, cat, mixed, scaled, small, deps=(), halved=False):
        sizes = [part + PAD] * seq
        if halved:
            sizes[seq // 2 : seq // 2 + 1] = [part // 2, part // 2 + PAD]
        count = len(sizes)
        outs = pl.pallas_call(
            functools.partial(weights_kernel, sz, seq, len(deps), halved),
            in_specs=[smem] + [vmem] * 5 + [anywhere] * len(deps),
            out_specs=[smem] + [vmem] * (count + head_axis),
            out_shape=[index_shape]
            + [shape((size, columns), LOW) for size in sizes]
            + [shape((seq * share, shared), LOW)] * head_axis,
            scratch_shapes=[pltpu.VMEM((width, columns), LOW), pltpu.VMEM((width, shared), F32)],
            compiler_params=options,
            cost_estimate=cost(4 * dense, 12e6),
        )(sc, normed, cat, mixed, scaled, small, *deps)
        pieces = outs[1 : 1 + count]
        if halved:
            low, high = pieces[seq // 2], pieces[seq // 2 + 1]
            pieces = over_seq([*pieces[: seq // 2], low, *pieces[seq // 2 + 2 :]])
            pieces.insert(seq // 2 + 1, shifted(high, seq // 2))
        else:
            pieces = over_seq(pieces)
        return pieces, outs[1 + count :], outs[0]

    def shifted(x, r):
        return lax.ppermute(x, "seq", [(i, (i + r) % seq) for i in range(seq)]) if r else x

    def over_seq(chunks):
        return [shifted(x, r) for r, x in enumerate(chunks)]

    def leave(sc, *arrays, riders=0):
        size = BLOCK + (share + PAD if riders else 0)
        pieces = pl.pallas_call(
            functools.partial(leave_kernel, sz, slots, riders),
            in_specs=[smem] + [vmem] * len(arrays),
            out_specs=[vmem] * slots + [smem],
            out_shape=[shape((size, chunk), LOW)] * slots + [index_shape],
            compiler_params=options,
        )(sc, *arrays)
        return to_members(pieces[:slots]), pieces[slots]

    out_pieces = to_members(out_slices)
    fw0, halo0 = forward(0, sc, tok_pieces + tok_others)
    base0, decays = fw0[10], fw0[11:13]
    pr0 = project(0, fw0[9], fw0[7], fw0[6], [out_pieces[1], out_pieces[-1]])
    out_others = [cross(x) for x in out_pieces]
    parts, sc_join = scatter(sc, pr0[0], pr0[1])
    turned = turned(sc_join, *raw, *sent)
    res1, low1, mixed0, square0, unused = section_output(0, sc, parts, base0, turned)
    pieces1 = gather(low1)
    square_other = cross(square0)

    fw1, halo1 = forward(1, sc, pieces1 + out_pieces + out_others + [decays[1]])
    stat = fw1[6] + cross(fw1[6])
    stats = [stat] + [over_heads(stat, d) for d in range(1, head_axis)]
    pr1 = project(1, fw1[9], fw1[7], fw1[6], [])
    parts_out, sc_out = scatter(sc, pr1[0], pr1[1])
    bw1 = backward(1, sc_out, [fw1[11]] + stats, fw1[1:5], decays[1], halo1, [])
    lf1 = lift(1, bw1[6], bw1[0], fw1[0], bw1[3], parts_out[1:])
    weights1, heads1, sc_weights = weight_grads(
        lf1[2], fw1[0], bw1[0], fw1[11], bw1[1], bw1[2], halved=True
    )
    parts, sc_join = scatter(sc_weights, lf1[0], lf1[1])
    igrad1, glow1, sc_in = section_input(
        1, sc_join, parts, res1, fw1[10], fw1[5], *gains, mixed0,
        deps=[weights1[1], weights1[-1]],
    )
    piecesg = gather(glow1)

    early, unused = leave(sc_in, low1, pieces1[head_axis], glow1, piecesg[head_axis])
    bw0 = backward(
        0, sc, piecesg + [square0, square_other], fw0[1:5], decays[0], halo0,
        weights1[2 : seq // 2 + 1],
    )
    weights0, heads0, sc_weights = weight_grads(
        bw0[6], fw0[0], bw0[0], bw0[7], bw0[1], bw0[2], deps=early[1:] + weights1[seq // 2 + 1 : -1],
    )
    lf0 = lift(0, sc_weights, bw0[0], fw0[0], bw0[3], [])
    riders = [[lf0[3], *heads0], [lf1[3], *heads1]]
    parts, sc_join = scatter(lf0[2], lf0[0], lf0[1], riders, weights0[1:2])

    unused, low2, unused_mixed, unused_square, sc_out = section_output(1, sc_in, parts_out, res1)
    glow0, to_other, shared_own, sc_end = section_input(
        0, sc_out, parts, base0, igrad1, fw0[5], *gains, low2,
        deps=weights0[2:],
    )
    got = cross(to_other)
    if spans == 1:
        late, sc_end = leave(sc_end, glow0, got, low2, got, shared_own, riders=seq)
        shared_parts = late
    else:
        late, sc_end = leave(sc_end, glow0, got, low2, got)
        total = shared_own + got[rows:].astype(F32)
        extra = resplit(total[:PAD])
        fill = jnp.zeros((BLOCK, shared), F32)
        chunks = [
            jnp.concatenate([fill, extra, total[PAD + r * share : PAD + (r + 1) * share]])
            for r in range(seq)
        ]
        shared_parts = over_seq([x.astype(LOW) for x in chunks])
    section_out, input_grad, unused = pl.pallas_call(
        functools.partial(home_kernel, slots),
        in_specs=[smem] + [vmem] * (2 * slots),
        out_specs=[vmem, vmem, smem],
        out_shape=[shape((slots, BLOCK, chunk), F32)] * 2 + [index_shape],
        compiler_params=options,
    )(sc, *early, *late)

    def summed(sc, pieces, *done):
        return pl.pallas_call(
            functools.partial(sum_kernel, sz, bool(done)),
            in_specs=[smem] + [vmem] * (len(pieces) + len(done)),
            out_shape=[shape((part + PAD, columns), LOW)] * (1 + len(done)),
            compiler_params=options,
        )(sc, *pieces, *done)

    own_sums, other_sums = summed(sc_end, weights0, *summed(sc_in, weights1))
    final = pl.pallas_call(
        functools.partial(final_kernel, sz, seq),
        in_specs=[smem] + [vmem] * (2 + seq),
        out_shape=[
            shape((part, inner_dev), F32),
            shape((part, inner_dev), F32),
            shape((inner_dev, part), F32),
            shape((taps, inner_dev), F32),
            shape((1, inner_dev), F32),
            shape((1, heads_dev), F32),
            shape((share, shared), F32),
            shape((taps, shared // (seq * head_axis)), F32),
            shape((1, width // (seq * head_axis)), F32),
        ],
        compiler_params=options,
    )(sc, own_sums, cross(other_sums), *shared_parts)
    return (
        section_out[None],
        input_grad[None],
        final[8],
        final[0][None],
        final[1][None],
        final[6][None],
        final[3][None],
        final[7][None],
        final[5],
        final[4],
        final[2][None],
    )


def solution(mesh):
    placed = (
        P(None, "seq", None),
        P(),
        P("section", None, "head", "seq"),
        P(None, "seq", None),
        P("section", None),
        P("section", None, "head"),
        P("section", None, "head"),
        P("section", None, None),
        P("section", None, "head"),
        P("section", None, None),
        P("section", "head"),
        P("section", "head"),
        P("section", None, None),
    )
    return jax.shard_map(
        per_device,
        mesh=mesh,
        in_specs=placed,
        out_specs=(
            P("section", None, "seq", "head"),
            P("section", None, "seq", "head"),
            P("section", ("seq", "head")),
            P("section", "seq", "head"),
            P("section", "seq", "head"),
            P("section", ("seq", "head"), None),
            P("section", None, "head"),
            P("section", None, ("seq", "head")),
            P("section", "head"),
            P("section", "head"),
            P("section", "head", "seq"),
        ),
        check_vma=False,
    )
```

```python
import functools

import jax
import jax.numpy as jnp
from jax import lax
from jax.experimental import pallas as pl
from jax.experimental.pallas import tpu as pltpu
from jax.sharding import PartitionSpec as P

BLOCK = 256
HALF = BLOCK // 2
PAD = 16
EPS = 1e-05
F32 = jnp.float32
LOW = jnp.bfloat16
HIDDEN = -1e30
NN = ((1,), (0,))
NT = ((1,), (1,))
TN = ((0,), (0,))
VMEM_BYTES = 50 * 1024 * 1024
ALL_VMEM_BYTES = 63 * 1024 * 1024


def dot(a, b, dims):
    return lax.dot_general(a, b, (dims, ((), ())), preferred_element_type=F32)


def aligned(start, size):
    return pl.ds(pl.multiple_of(start, size), size)


def spread(cols, first, count, width):
    rows = cols.shape[0]
    lane = lax.broadcasted_iota(jnp.int32, (rows, count * width), 1)
    out = jnp.broadcast_to(cols[:, first : first + 1], (rows, count * width))
    for h in range(1, count):
        out = jnp.where(lane >= h * width, cols[:, first + h : first + h + 1], out)
    return out


def per_head(array, h, width):
    lane = lax.broadcasted_iota(jnp.int32, array.shape, 1)
    inside = (lane >= h * width) & (lane < (h + 1) * width)
    return jnp.where(inside, array, jnp.zeros_like(array))


def split_low(value):
    high = value.astype(LOW).astype(F32)
    return high, value - high


def column_of(row, size):
    return jnp.transpose(jnp.broadcast_to(row, (128, size)))


def sigmoid(v):
    return 0.5 * jnp.tanh(0.5 * v) + 0.5


def pick(flag, a, b):
    return jnp.where(flag, a, b)


class Sizes:
    def __init__(self, blocks, width, channels, heads, states, taps, head_axis, inner):
        self.blocks = blocks
        self.width = width
        self.channels = channels
        self.heads = heads
        self.head_width = channels // heads
        self.states = states
        self.lin = channels + 2 * states
        self.taps = taps
        self.head_axis = head_axis
        self.chunk = width // head_axis
        self.rows = blocks * HALF
        self.tokens = blocks * BLOCK
        self.inner = inner


def weight_copies(sz, layer, c, h, raw, got, wv, ov, sems):
    gate, inner, shared, out = raw
    ch = sz.channels
    cols = aligned(c * ch, ch)
    rows = aligned((h * 2 + c) * ch, ch)
    own, sent = [], []
    if wv is not None:
        own += [
            (gate.at[0, :, cols], wv.at[:, :ch]),
            (inner.at[0, :, cols], wv.at[:, ch : 2 * ch]),
            (shared.at[0], wv.at[:, 2 * ch :]),
        ]
        sent += [(got[0], wv)]
    if ov is not None:
        own += [(out.at[0, rows, :], ov)]
        sent += [(got[1], ov)]
    return [
        (c == layer, [pltpu.make_async_copy(p, q, sems.at[i]) for i, (p, q) in enumerate(own)]),
        (c != layer, [pltpu.make_async_copy(p, q, sems.at[i]) for i, (p, q) in enumerate(sent)]),
    ]


def run_copies(choices, start, wait):
    for flag, copies in choices:

        @pl.when(flag)
        def _(copies=copies):
            if start:
                for copy in copies:
                    copy.start()
            if wait:
                for copy in copies:
                    copy.wait()


def put_ordered(sz, dst, c, k, b, own, other):
    for r in range(len(own)):

        @pl.when(lax.rem(k - b + len(own), len(own)) == r)
        def _(r=r):
            put_pair(dst, c, own[r][:HALF, :], other[r][:HALF, :])


def put_pair(dst, c, own, other):
    dst[aligned(c * HALF, HALF), :] = own
    dst[aligned((1 - c) * HALF, HALF), :] = other


def far_first(count):
    return [0] + list(range(count - 1, 0, -1))


def put_pieces(sz, dst, c, h, own, other):
    own, other = (dict(zip(far_first(sz.head_axis), side)) for side in (own, other))
    for d in range(sz.head_axis):
        cols = aligned((h ^ d) * sz.chunk, sz.chunk)
        dst[aligned(c * HALF, HALF), cols] = own[d]
        dst[aligned((1 - c) * HALF, HALF), cols] = other[d]


def line_of(table, at):
    line = lax.broadcasted_iota(jnp.int32, table.shape, 0)
    return jnp.sum(jnp.where(line == at, table, 0.0), axis=0, keepdims=True)


def conv_forward(sz, ext, taps):
    pre = taps[0:1] * ext[5 : 5 + BLOCK, :]
    for j in range(1, sz.taps):
        pre = pre + taps[j : j + 1] * ext[5 + j : 5 + j + BLOCK, :]
    return pre


def decay_of(sz, cols, rp, h, mask):
    rows = cols[:, h : h + 1] + rp[12 + h : 13 + h, :]
    return jnp.exp(jnp.where(mask, rows, HIDDEN))


def lower_mask():
    t = lax.broadcasted_iota(jnp.int32, (BLOCK, BLOCK), 0)
    s = lax.broadcasted_iota(jnp.int32, (BLOCK, BLOCK), 1)
    return t >= s


def forward_kernel(sz, layer, slots, sc, *refs):
    n = sz.head_axis
    sources = 2 * slots if layer == 0 else 2 * n + 2 * slots
    src, refs = refs[:sources], refs[sources:]
    if layer == 1:
        table, refs = refs[0], refs[1:]
    gains, raw, got, halo, begin = refs[0:2], refs[2:6], refs[6:8], refs[8], refs[9]
    if layer == 1:
        ov, refs = refs[10], refs[1:]
    normed_o, gl_o, lin_o, ssd_o, inc_o, inv_o, part_o, unit_o, fin_o, sc_o, base_o = refs[10:21]
    refs = refs[21:]
    if layer == 1:
        mixed_o, refs = refs[0], refs[1:]
    else:
        tables_o, refs = refs[0:2], refs[2:]
    xs, ms, wv, ext, state, sems = refs
    b = pl.program_id(0)
    c, h, k = sc[0], sc[1], sc[3]
    ch, st = sz.channels, sz.states
    copies = weight_copies(sz, layer, c, h, raw, got, wv, None, sems)

    @pl.when(b == 0)
    def _():
        run_copies(copies, True, False)
        ext[0:8, :] = halo[...]
        state[...] = begin[...]
        for i in range(4):
            sc_o[i] = sc[i]

    mine = aligned(c * HALF, HALF)
    cols = aligned(h * sz.chunk, sz.chunk)
    if layer == 0:
        put_ordered(sz, xs, c, k, b, src[:slots], src[slots:])
        base_o[...] = xs[mine, cols]
        for r in range(slots):

            @pl.when(lax.rem(k - b + slots, slots) == r)
            def _(r=r):
                own = decay_table(rates_of(src[r]), c, sz.heads)
                other = decay_table(rates_of(src[slots + r]), c, sz.heads)
                tables_o[0][...] = pick(c == 0, own, other)
                tables_o[1][...] = pick(c == 0, other, own)

        rp = tables_o[0][...]
    else:
        put_pieces(sz, xs, c, h, [r[...] for r in src[:n]], [r[...] for r in src[n : 2 * n]])
        put_ordered(sz, ms, c, k, b, src[2 * n : 2 * n + slots], src[2 * n + slots :])
        base_o[...] = ms[mine, cols]
        mixed_o[...] = ms[...]
        rp = table[...]

    pv = pick(c == layer, gains[0][...], gains[1][...])
    x = xs[...].astype(F32)
    inv_in = lax.rsqrt(jnp.mean(x * x, axis=1, keepdims=True) + EPS)
    normed = (x * inv_in * pv[0:1, : sz.width]).astype(LOW)
    normed_o[...] = normed

    @pl.when(b == 0)
    def _():
        run_copies(copies, False, True)

    proj = dot(normed, wv[...], NN)
    gl = proj[:, :ch]
    gl_o[...] = gl
    lin = proj[:, ch:].astype(LOW)
    lin_o[...] = lin
    ext[8 : 8 + BLOCK, :] = lin.astype(F32)
    pre = conv_forward(sz, ext, pv[1:5, : sz.lin])
    ext[0:8, :] = ext[BLOCK : BLOCK + 8, :]
    act = (pre * sigmoid(pre)).astype(LOW)
    values, bm, cm = act[:, :ch], act[:, ch : ch + st], act[:, ch + st :]

    cols = jnp.transpose(rp)
    mask = lower_mask()
    gram = dot(cm, bm, NT)
    mixes, parts = [], []
    for i in range(sz.heads):
        mixes.append((gram * decay_of(sz, cols, rp, i, mask)).astype(LOW))
        parts.append(per_head(values, i, sz.head_width))
    intra = dot(jnp.concatenate(mixes, axis=1), jnp.concatenate(parts, axis=0), NN)

    low_state = state[...].astype(LOW)
    inc_o[0] = low_state
    ecum = spread(cols, sz.heads, sz.heads, sz.head_width)
    inter = dot(cm, low_state, NT) * ecum
    vf = values.astype(F32)
    carried = (vf * spread(cols, 2 * sz.heads, sz.heads, sz.head_width)).astype(LOW)
    local = dot(carried, bm, TN)
    for i in range(sz.heads):
        rows = slice(i * sz.head_width, (i + 1) * sz.head_width)
        total = cols[BLOCK - 1 : BLOCK, sz.heads + i : sz.heads + i + 1]
        state[rows, :] = total * state[rows, :] + local[rows]
    ssd = intra + inter + pv[6:7, :ch] * vf
    ssd_o[...] = ssd
    gated = ssd * (gl * sigmoid(gl))
    weighty = gated * pv[5:6, :ch]
    unit_o[...] = weighty.astype(LOW)

    lane = lax.broadcasted_iota(jnp.int32, (BLOCK, 128), 1)
    square = jnp.sum(gated * gated, axis=1, keepdims=True)
    if layer == 0:
        project = jnp.zeros_like(square)
    else:
        scaled_grad = dot(ms[...], ov[...], NN)
        project = jnp.sum(scaled_grad * weighty, axis=1, keepdims=True)
    stats = jnp.where(lane == 0, square, jnp.where(lane == 1, project, inv_in))
    stats = jnp.transpose(stats)
    part_o[...] = stats[0:2, :]
    inv_o[...] = stats[2:3, :]

    @pl.when(b == sz.blocks - 1)
    def _():
        fin_o[...] = state[...]


def scalar_lines(sz, lines):
    fill = [jnp.zeros((8 - sz.blocks, HALF), F32)] if sz.blocks < 8 else []
    high, low = split_low(jnp.concatenate(lines + fill, axis=0))
    table = jnp.concatenate([high, low], axis=0).astype(LOW)
    return jnp.concatenate([table] * (sz.chunk // HALF), axis=1)


def own_rows(sz, ref, which):
    blocks = [ref[aligned(b * BLOCK + which * HALF, HALF), :] for b in range(sz.blocks)]
    return jnp.concatenate(blocks, axis=0)


def project_kernel(sz, layer, deps, sc, unit_r, stats_r, *refs):
    raw, got, refs = refs[:4], refs[4:6], refs[6 + deps :]
    keep, send, sc_o, weights, sems = refs
    c, h = sc[0], sc[1]
    copies = weight_copies(sz, layer, c, h, raw, got, None, weights, sems)
    run_copies(copies, True, False)
    for i in range(4):
        sc_o[i] = sc[i]
    sides = []
    for which, out in ((c, keep), (1 - c, send)):
        sides.append((out, own_rows(sz, unit_r, which)))
        lines = [
            stats_r[0:1, aligned(b * BLOCK + which * HALF, HALF)] for b in range(sz.blocks)
        ]
        table = scalar_lines(sz, lines)
        for d in range(sz.head_axis):
            out[d, sz.rows :, :] = table
    run_copies(copies, False, True)
    for out, rows in sides:
        for d in range(sz.head_axis):
            chunk = weights[:, aligned((h ^ d) * sz.chunk, sz.chunk)]
            out[d, : sz.rows, :] = dot(rows, chunk, NN).astype(LOW)


def turn_kernel(sz, sc, *refs):
    raw, got = refs[:4], refs[4:6]
    wide_o, out_o, wv, ov, sems = refs[6:8], refs[8:10], refs[10], refs[11], refs[12]
    for layer in range(2):
        copies = weight_copies(sz, layer, sc[0], sc[1], raw, got, wv, ov, sems)
        run_copies(copies, True, True)
        wide_o[layer][...] = jnp.transpose(wv[...])
        out_o[layer][...] = jnp.transpose(ov[...])


def out_at(out, d):
    return out[d] if isinstance(out, tuple) else out.at[d]


def lift_kernel(sz, layer, deps, sc, cat_r, normed_r, zero_gains, one_gains, small_r, *refs):
    weights, refs = refs[0], refs[1 + deps :]
    keep, send, sc_o, common_o, wide = refs[0], refs[1:-3], *refs[-3:]
    c, h = sc[0], sc[1]
    for i in range(4):
        sc_o[i] = sc[i]
    wide[...] = jnp.zeros_like(wide)
    for which, out in ((c, keep), (1 - c, send)):
        rows = own_rows(sz, cat_r, which)
        along = jnp.zeros((sz.rows, 1), F32)
        for d in range(sz.head_axis):
            cols = aligned((h ^ d) * sz.chunk, sz.chunk)
            product = dot(rows, weights[:, cols], NN)
            out_at(out, d)[: sz.rows, :] = product.astype(LOW)
            blocks = [
                normed_r[aligned(b * BLOCK + which * HALF, HALF), cols] for b in range(sz.blocks)
            ]
            product = product * jnp.concatenate(blocks, axis=0).astype(F32)
            wide[0:1, cols] += jnp.sum(product, axis=0, keepdims=True)
            along = along + jnp.sum(product, axis=1, keepdims=True)
        lines = [
            jnp.transpose(jnp.broadcast_to(along[b * HALF : (b + 1) * HALF], (HALF, 128)))[0:1, :]
            for b in range(sz.blocks)
        ]
        table = scalar_lines(sz, lines)
        for d in range(sz.head_axis):
            out_at(out, d)[sz.rows :, :] = table
    gain_grad = wide[0:1, :] / pick(c == layer, zero_gains[0:1, :], one_gains[0:1, :])
    flat = [small_r[j : j + 1, sz.channels :] for j in range(sz.taps)]
    flat += [gain_grad[:, q * sz.chunk : (q + 1) * sz.chunk] for q in range(sz.head_axis)]
    high, low = split_low(jnp.concatenate(flat, axis=0))
    common_o[...] = jnp.concatenate([high, low], axis=0).astype(LOW)


def backward_kernel(sz, layer, deps, sc, *refs):
    n = sz.head_axis
    sources = 2 * n + 2 if layer == 0 else 1 + n
    src, refs = refs[:sources], refs[sources:]
    gl_r, lin_r, ssd_r, inc_r = refs[:4]
    table, gains, ov = refs[4], refs[5:7], refs[7]
    halo, halo_grad, begin = refs[8:11]
    refs = refs[11 + deps :]
    cat_o, scaled_o, small_o, sums_o, fin_o, rim_o, sc_o = refs[:7]
    refs = refs[7:]
    if layer == 0:
        mixed_o, refs = refs[0], refs[1:]
    ms, ext, back, state, heads_p, small = refs
    i_step = pl.program_id(0)
    b = sz.blocks - 1 - i_step
    c, h = sc[0], sc[1]
    ch, st = sz.channels, sz.states
    pv = pick(c == layer, gains[0][...], gains[1][...])
    rp = table[...]

    @pl.when(i_step == 0)
    def _():
        back[BLOCK : BLOCK + 8, :] = halo_grad[...]
        state[...] = begin[...]
        small[...] = jnp.zeros_like(small)
        for i in range(4):
            sc_o[i] = sc[i]
        if layer == 0:
            for i in range(2):
                extra = src[i * n][sz.rows :, :].astype(F32)
                for d in range(1, n):
                    extra = extra + src[i * n + d][sz.rows :, :].astype(F32)
                heads_p[8 * i : 8 * i + 8, :] = extra[0:8, :HALF] + extra[8:16, :HALF]

    if layer == 0:
        rows = aligned(b * HALF, HALF)
        put_pieces(
            sz, ms, c, h, [r[rows, :] for r in src[:n]], [r[rows, :] for r in src[n : 2 * n]]
        )
        halves = []
        for k in range(2):
            alpha = lax.rsqrt(line_of(src[2 * n + k][...], b) / sz.inner + EPS)
            beta = alpha * alpha * line_of(heads_p[...], 8 * k + b) / sz.inner
            halves.append((alpha, beta))
        alpha, beta = (
            pick(
                c == 0,
                jnp.concatenate([halves[0][q], halves[1][q]], axis=1),
                jnp.concatenate([halves[1][q], halves[0][q]], axis=1),
            )
            for q in range(2)
        )
    else:
        stats = src[1][...]
        for d in range(1, n):
            stats = stats + src[1 + d][...]
        alpha = lax.rsqrt(stats[0:1, :] / sz.inner + EPS)
        beta = alpha * alpha * alpha * stats[1:2, :] / sz.inner

    sub = lax.broadcasted_iota(jnp.int32, rp.shape, 0)
    cols = jnp.transpose(jnp.where(sub == 12, alpha, jnp.where(sub == 13, beta, rp)))
    alpha, beta = cols[:, 12:13], cols[:, 13:14]

    gl = gl_r[...]
    ssd = ssd_r[...]
    sig = sigmoid(gl)
    swish = gl * sig
    slope = sig * (1.0 + gl * (1.0 - sig))
    gated = ssd * swish
    if layer == 0:
        mixed_grad = ms[...]
        mixed_o[...] = mixed_grad
    else:
        mixed_grad = src[0][...]
    scaled_grad = dot(mixed_grad, ov[...], NN)
    gain = pv[5:6, :ch]
    normal = gated * alpha
    small[4:5, :ch] += jnp.sum(scaled_grad * normal, axis=0, keepdims=True)
    scaled_o[...] = (normal * gain).astype(LOW)
    gated_grad = alpha * (scaled_grad * gain) - beta * gated
    ssd_grad = (gated_grad * swish).astype(LOW)
    gate_grad = (gated_grad * ssd * slope).astype(LOW)
    sgf = ssd_grad.astype(F32)

    before = lin_r[pl.ds(pl.multiple_of(jnp.maximum(b * BLOCK - 16, 0), 16), 16), :]
    ext[0:8, :] = pick(b > 0, before.astype(F32)[8:16, :], halo[...])
    ext[8 : 8 + BLOCK, :] = lin_r[aligned(b * BLOCK, BLOCK), :].astype(F32)
    taps = pv[1:5, : sz.lin]
    pre = conv_forward(sz, ext, taps)
    psig = sigmoid(pre)
    pact = pre * psig
    pslope = psig * (1.0 + pre * (1.0 - psig))
    act = pact.astype(LOW)
    values, bm, cm = act[:, :ch], act[:, ch : ch + st], act[:, ch + st :]
    vf = values.astype(F32)
    small[5:6, :ch] += jnp.sum(sgf * vf, axis=0, keepdims=True)

    mask = lower_mask()
    gram = dot(cm, bm, NT)
    gram_grad = jnp.zeros((BLOCK, BLOCK), F32)
    mixes, parts = [], []
    for i in range(sz.heads):
        decay = decay_of(sz, cols, rp, i, mask)
        mixes.append((gram * decay).astype(LOW))
        parts.append(per_head(ssd_grad, i, sz.head_width))
        gram_grad = gram_grad + dot(parts[-1], values, NT) * decay
    intra_grad = dot(jnp.concatenate(mixes, axis=0), jnp.concatenate(parts, axis=0), TN)

    ecum = spread(cols, sz.heads, sz.heads, sz.head_width)
    to_end = spread(cols, 2 * sz.heads, sz.heads, sz.head_width)
    inter_grad = (sgf * ecum).astype(LOW)
    low_state = state[...].astype(LOW)
    carried = (vf * to_end).astype(LOW)
    carried_grad = dot(bm, low_state, NT)
    gram_low = gram_grad.astype(LOW)
    b_grad = dot(gram_low, cm, TN) + dot(carried, low_state, NN)
    c_grad = dot(gram_low, bm, NN) + dot(inter_grad, inc_r[0], NN)
    value_grad = intra_grad + pv[6:7, :ch] * sgf + carried_grad * to_end
    entry = dot(inter_grad, cm, TN)
    for i in range(sz.heads):
        rows = slice(i * sz.head_width, (i + 1) * sz.head_width)
        total = cols[BLOCK - 1 : BLOCK, sz.heads + i : sz.heads + i + 1]
        state[rows, :] = total * state[rows, :] + entry[rows]

    pre_grad = jnp.concatenate([value_grad, b_grad, c_grad], axis=1) * pslope
    back[0:BLOCK, :] = pre_grad
    lin_grad = taps[0:1] * back[sz.taps - 1 : sz.taps - 1 + BLOCK, :]
    for j in range(1, sz.taps):
        at = sz.taps - 1 - j
        lin_grad = lin_grad + taps[j : j + 1] * back[at : at + BLOCK, :]
    for j in range(sz.taps):
        small[j : j + 1, :] += jnp.sum(pre_grad * ext[5 + j : 5 + j + BLOCK, :], axis=0, keepdims=True)
    back[BLOCK : BLOCK + 8, :] = back[0:8, :]
    cat_o[...] = jnp.concatenate([gate_grad, lin_grad.astype(LOW)], axis=1)

    @pl.when(i_step == sz.blocks - 1)
    def _():
        fin_o[...] = state[...]
        rim_o[...] = back[0:8, :]
        sums = small[...]
        flat = [sums[j : j + 1, :ch] for j in range(sz.taps + 2)]
        flat = [jnp.concatenate(flat[j : j + 3], axis=1) for j in range(0, len(flat), 3)]
        flat = flat + [jnp.zeros_like(flat[0])] * (4 - len(flat))
        high, low = split_low(jnp.concatenate(flat, axis=0))
        rest = jnp.zeros((PAD - 8, high.shape[1]), F32)
        small_o[...] = jnp.concatenate([high, low, rest], axis=0).astype(LOW)
        sums_o[...] = sums


def weights_kernel(sz, seq, deps, with_common, sc, normed, cat, mixed, scaled, small, *refs):
    if with_common:
        common, refs = refs[0], refs[1:]
    refs = refs[deps:]
    sc_o, outs, heads, full, wide = refs[0], refs[1 : seq + 1], refs[seq + 1 : -2], refs[-2], refs[-1]
    for i in range(4):
        sc_o[i] = sc[i]
    ch, st = sz.channels, sz.states
    step = sz.chunk
    for q in range(sz.head_axis):
        at = slice(q * step, (q + 1) * step)
        grads = dot(normed[:, at], cat[...], TN)
        full[at, : 2 * ch] = grads[:, : 2 * ch].astype(LOW)
        wide[at, :] = grads[:, 2 * ch :]
        full[at, 2 * ch :] = dot(mixed[:, at], scaled[...], TN).astype(LOW)
    rows = sz.width // seq
    part = rows // sz.head_axis
    for r, out in enumerate(outs):
        out[:rows, :] = full[aligned(lax.rem(sc[2] + r, seq) * rows, rows), :]
        out[rows:, :] = small[...]
    for d, out in enumerate(heads):
        lines = [
            wide[aligned(lax.rem(sc[2] + r, seq) * rows + (sc[1] ^ d) * part, part), :]
            for r in range(seq)
        ]
        if with_common:
            lines = [common[...].astype(F32)] + lines
        out[...] = jnp.concatenate(lines, axis=0).astype(LOW)


def resplit(extra):
    half = extra.shape[0] // 2
    high, low = split_low(extra[:half, :] + extra[half:, :])
    return jnp.concatenate([high, low], axis=0)


def join_kernel(sz, parts, riders, deps, sc, keep, *refs):
    n = sz.head_axis
    recv, refs = refs[0] if parts == 1 else refs[:parts], refs[parts:]
    more = [(refs[i * (n + 1)], refs[i * (n + 1) + 1 : (i + 1) * (n + 1)]) for i in range(riders)]
    refs = refs[riders * (n + 1) + deps :]
    sc_o, outs = refs[0], refs[1:]
    rows = sz.rows
    for i in range(4):
        sc_o[i] = sc[i]
    extra = resplit(keep[0, rows:, :].astype(F32) + out_at(recv, 0)[rows:, :].astype(F32))
    for d, out in enumerate(outs):
        both = keep[d, :rows, :].astype(F32) + out_at(recv, d)[:rows, :].astype(F32)
        out[:rows, :] = both.astype(out.dtype)
        out[rows : rows + PAD, :] = extra.astype(out.dtype)
        at = rows + PAD
        for common, rider in more:
            size = rider[d].shape[0]
            out[at : at + PAD, :] = common[...].astype(out.dtype)
            out[at + PAD : at + PAD + size, :] = rider[d][...].astype(out.dtype)
            at += PAD + size


def total_of(parts, rows):
    total = parts[0][rows, :].astype(F32)
    for p in parts[1:]:
        total = total + p[rows, :].astype(F32)
    return total


def output_kernel(sz, layer, sc, *refs):
    n = sz.head_axis
    parts, refs = refs[:n], refs[n:]
    resid = refs[0]
    res_o, low_o, mixed_o, square_o, sc_o = refs[-5:]
    for i in range(4):
        sc_o[i] = sc[i]
    extra = total_of(parts, slice(sz.rows, sz.rows + PAD))
    square = extra[0:8, :HALF] + extra[8:16, :HALF]
    square_o[...] = square
    inv = lax.rsqrt(square / sz.inner + EPS)
    for b in range(sz.blocks):
        rows = slice(b * HALF, (b + 1) * HALF)
        col = column_of(inv[b : b + 1, :], HALF)[:, 0:1]
        mixed = total_of(parts, rows) * col
        res = resid[rows, :].astype(F32) + mixed
        res_o[rows, :] = res
        low_o[rows, :] = res.astype(LOW)
        mixed_o[rows, :] = mixed


def input_kernel(sz, layer, sc, *refs):
    n = sz.head_axis
    parts, refs = refs[:n], refs[n:]
    resid, outg, inv_r, gains = refs[0], refs[1], refs[2], refs[3:5]
    refs = refs[5:]
    if layer == 1:
        mixed = refs[0]
        grad_o, low_o, sc_o = refs[-3:]
    else:
        one_low, one_heads = refs[0], refs[1 : 1 + n]
        low_o, swap_o, shared_o, sc_o = refs[-4:]
    for i in range(4):
        sc_o[i] = sc[i]
    c, h = sc[0], sc[1]
    first = c == 0
    mine = aligned(h * sz.chunk, sz.chunk)
    gain = pick(c == layer, gains[0][0:1, mine], gains[1][0:1, mine])
    extra = total_of(parts, slice(sz.rows, sz.rows + PAD))
    along = extra[0:8, :HALF] + extra[8:16, :HALF]
    tops, lows = [], []
    for b in range(sz.blocks):
        rows = slice(b * HALF, (b + 1) * HALF)
        at = b * BLOCK
        inv_row = pick(c == 0, inv_r[:, at : at + HALF], inv_r[:, at + HALF : at + BLOCK])
        inv = column_of(inv_row, HALF)[:, 0:1]
        share = column_of(along[b : b + 1, :] / sz.width, HALF)[:, 0:1]
        total = total_of(parts, rows)
        base = resid[rows, :].astype(F32)
        grad = outg[rows, :].astype(F32) + inv * (total * gain - base * (inv * share))
        low = grad.astype(LOW)
        low_o[rows, :] = low
        if layer == 0:
            swap_o[rows, :] = pick(first, one_low[rows, :], low)
        else:
            grad_o[rows, :] = grad
            dots = jnp.sum(low.astype(F32) * mixed[rows, :], axis=1, keepdims=True)
            row = jnp.transpose(jnp.broadcast_to(dots, (HALF, 128)))[0:1, :]
            high, rest = split_low(row)
            tops.append(high)
            lows.append(rest)
    if layer == 1:
        fill = [jnp.zeros((8 - sz.blocks, HALF), F32)] if sz.blocks < 8 else []
        extra = jnp.concatenate(tops + fill + lows + fill, axis=0)
        extra = jnp.concatenate([extra] * (sz.chunk // HALF), axis=1)
        low_o[sz.rows :, :] = extra.astype(LOW)
    else:
        size = shared_o.shape[0]
        at = sz.rows + PAD
        zero = total_of(parts, slice(at, at + size))
        one = total_of(one_heads, slice(None))
        zero, one = (jnp.concatenate([resplit(v[:PAD]), v[PAD:]], axis=0) for v in (zero, one))
        shared_o[...] = pick(first, zero, one)
        swap_o[sz.rows :, :] = pick(first, one, zero).astype(LOW)


def sum_kernel(sz, last, sc, *refs):
    if last:
        parts, done, outs = refs[:-3], refs[-3], refs[-2:]
    else:
        parts, outs = refs[:-1], refs[-1:]
    rows = outs[0].shape[0] - PAD
    total = total_of(parts, slice(None))
    extra = total[rows:]
    high, low = split_low(extra[0:4, :] + extra[4:8, :])
    extra = jnp.concatenate([high, low, jnp.zeros((PAD - 8, extra.shape[1]), F32)], axis=0)
    sums = jnp.concatenate([total[:rows], extra], axis=0).astype(LOW)
    if last:
        outs[0][...] = pick(sc[0] == 0, sums, done[...])
        outs[1][...] = pick(sc[0] == 0, done[...], sums)
    else:
        outs[0][...] = sums


def final_kernel(sz, seq, sc, own, got, *refs):
    pieces, refs = refs[:-9], refs[-9:]
    gate_o, inner_o, out_o, conv_o, norm_o, skip_o, shared_o, taps_o, gain_o = refs
    c = sc[0]
    ch = sz.channels
    rows = own.shape[0] - PAD
    lane = lax.broadcasted_iota(jnp.int32, skip_o.shape, 1)
    skip = jnp.zeros(skip_o.shape, F32)
    for i in range(2):
        which = pick(i == 0, c, 1 - c)
        to = aligned(which * ch, ch)
        sums = (own if i == 0 else got)[...].astype(F32)
        gate_o[:, to] = sums[:rows, :ch]
        inner_o[:, to] = sums[:rows, ch : 2 * ch]
        out_o[to, :] = jnp.transpose(sums[:rows, 2 * ch :])
        lines = sums[rows : rows + 4, :] + sums[rows + 4 : rows + 8, :]
        for j in range(sz.taps):
            conv_o[j : j + 1, to] = lines[j // 3 : j // 3 + 1, (j % 3) * ch : (j % 3 + 1) * ch]
        norm_o[:, to] = lines[1:2, ch : 2 * ch]
        skips = lines[1:2, 2 * ch :]
        for q in range(sz.heads):
            part = jnp.sum(per_head(skips, q, sz.head_width), axis=1, keepdims=True)
            skip = jnp.where(lane == which * sz.heads + q, part, skip)
    skip_o[...] = skip
    total = total_of(pieces, slice(BLOCK, None))
    shared_o[...] = total[PAD:]
    common = total[: PAD // 2] + total[PAD // 2 : PAD]
    place = sc[2] * sz.head_axis + sc[1]
    span = common.shape[1]
    size = span // (seq * sz.head_axis)
    turned = pltpu.roll(common, lax.rem(span - place * size, span), 1)
    taps_o[...] = turned[: sz.taps, :size]
    size = sz.width // (seq * sz.head_axis)
    at = place * size
    line = jnp.broadcast_to(line_of(common, sz.taps + at // span), common.shape)
    turned = pltpu.roll(line, lax.rem(span - lax.rem(at, span), span), 1)
    gain_o[...] = turned[:1, :size]


def slice_kernel(sz, slots, sc, order, tokens, rates, *refs):
    outs, sc_o, sems = refs[:slots], refs[slots], refs[slots + 1]
    copies = []
    for r in range(slots):
        rows = tokens.at[order[lax.rem(sc[3] + r, slots)], aligned(sc[0] * HALF, HALF), :]
        copies.append(pltpu.make_async_copy(rows, outs[r].at[:HALF], sems.at[r]))
    for copy in copies:
        copy.start()
    for i in range(4):
        sc_o[i] = sc[i]
    for r in range(slots):
        first, rest = split_low(rates[0, order[lax.rem(sc[3] + r, slots)]])
        second, rest = split_low(rest)
        lines = jnp.concatenate([first, second, rest, jnp.zeros_like(rest)], axis=1)
        lines = jnp.concatenate([lines, jnp.zeros_like(lines)], axis=0)
        outs[r][HALF:, :] = lines.astype(LOW)
    for copy in copies:
        copy.wait()


def rates_of(piece):
    lines = piece[HALF:, :].astype(F32)[:8, :]
    return (lines[:, :BLOCK] + lines[:, BLOCK : 2 * BLOCK]) + lines[:, 2 * BLOCK : 3 * BLOCK]


def pack_kernel(sz, sc, order, grads, gate, inner, shared, out, in_gain, conv_i, conv_s, skip, norm, *refs):
    w_o, o_o, mine_o, send_o, sems = *refs[:4], refs[-1]
    c, h = sc[0], sc[1]
    ch = sz.channels
    outs = refs[4:-1]
    slices = []
    for r, to in enumerate(outs):
        rows = grads.at[order[lax.rem(sc[3] + r, len(outs))], aligned(c * HALF, HALF), :]
        slices.append(pltpu.make_async_copy(rows, to, sems.at[4 + r]))
    cols = aligned((1 - c) * ch, ch)
    rows = aligned((h * 2 + 1 - c) * ch, ch)
    copies = [
        pltpu.make_async_copy(gate.at[0, :, cols], w_o.at[:, :ch], sems.at[0]),
        pltpu.make_async_copy(inner.at[0, :, cols], w_o.at[:, ch : 2 * ch], sems.at[1]),
        pltpu.make_async_copy(shared.at[0], w_o.at[:, 2 * ch :], sems.at[2]),
        pltpu.make_async_copy(out.at[0, rows, :], o_o, sems.at[3]),
        *slices,
    ]
    for copy in copies:
        copy.start()
    for which, ref in ((c, mine_o), (1 - c, send_o)):
        at = aligned(which * ch, ch)
        ref[...] = jnp.zeros_like(ref)
        ref[0:1, :] = in_gain[...]
        ref[1 : 1 + sz.taps, :ch] = conv_i[0, :, at]
        ref[1 : 1 + sz.taps, ch : sz.lin] = conv_s[0]
        ref[5:6, :ch] = norm[:, at]
        low = spread(skip[...], 0, sz.heads, sz.head_width)
        high = spread(skip[...], sz.heads, sz.heads, sz.head_width)
        ref[6:7, :ch] = pick(which == 0, low, high)
    for copy in copies:
        copy.wait()


def decay_table(rate, c, n):
    lane = lax.broadcasted_iota(jnp.int32, rate.shape, 1)
    cum = rate
    step = 1
    while step < BLOCK:
        cum = cum + jnp.where(lane >= step, pltpu.roll(cum, step, 1), 0.0)
        step *= 2
    end = cum[:, BLOCK - 1 :]
    lines = [cum, jnp.exp(cum), jnp.exp(end - cum) * -rate, jnp.log(-rate) - cum]
    low = jnp.concatenate([v[:n] for v in lines], axis=0)
    high = jnp.concatenate([v[n:] for v in lines], axis=0)
    return pick(c == 0, low, high)


def leave_kernel(sz, slots, riders, sc, zero_own, zero_other, one_own, one_other, *refs):
    c = sc[0]
    if riders:
        shared, refs = refs[0], refs[1:]
        total = shared[...] + one_other[sz.rows :, :].astype(F32)
        extra = resplit(total[:PAD])
        part = (total.shape[0] - PAD) // riders
    outs = refs[:slots]
    for i in range(4):
        refs[slots][i] = sc[i]
    for r in range(slots):
        rows = aligned(lax.rem(sc[3] + r, slots) * HALF, HALF)
        own = pick(c == 0, zero_own[rows, :], one_own[rows, :])
        other = pick(c == 0, zero_other[rows, :], one_other[rows, :])
        put_pair(outs[r], c, own, other)
        if riders:
            lines = [extra, total[PAD + r * part : PAD + (r + 1) * part]]
            outs[r][BLOCK:, :] = jnp.concatenate(lines, axis=0).astype(LOW)


def home_kernel(slots, sc, *refs):
    early, late, out, grad = refs[:slots], refs[slots : 2 * slots], refs[-3], refs[-2]
    for i in range(4):
        refs[-1][i] = sc[i]
    first = sc[0] == 0
    for r in range(slots):
        at = lax.rem(sc[3] - r + slots, slots)
        out[at] = pick(first, early[r][...], late[r][:BLOCK, :]).astype(F32)
        grad[at] = pick(first, late[r][:BLOCK, :], early[r][...]).astype(F32)


def whole(shape):
    return pl.BlockSpec(shape, lambda *_: (0,) * len(shape))


def per_device(
    tokens,
    slot_order,
    log_decay,
    grad_out,
    in_gain,
    w_gate,
    w_inner,
    w_shared,
    conv_inner,
    conv_shared,
    d_skip,
    norm_gain,
    w_out,
):
    slots = tokens.shape[0]
    span = tokens.shape[1]
    width = tokens.shape[2]
    seq = lax.axis_size("seq")
    head_axis = lax.axis_size("head")
    cores = lax.axis_size("section")
    spans = seq // slots
    c = lax.axis_index("section")
    z = lax.axis_index("seq")
    h = lax.axis_index("head")
    k = lax.rem(z, slots)
    inner_dev = w_gate.shape[2]
    channels = inner_dev // cores
    shared = w_shared.shape[2]
    heads_dev = d_skip.shape[1]
    taps = conv_inner.shape[1]
    sz = Sizes(
        slots * span // BLOCK,
        width,
        channels,
        heads_dev // cores,
        shared // 2,
        taps,
        head_axis,
        inner_dev * head_axis,
    )
    first = c == 0
    swap = [(0, 1), (1, 0)]
    nb, tok, rows, chunk = sz.blocks, sz.tokens, sz.rows, sz.chunk

    def cross(x):
        return lax.ppermute(x, "section", swap)

    def turn(x, r):
        pairs = [(i, i // slots * slots + (i % slots + r) % slots) for i in range(seq)]
        return lax.ppermute(x, "seq", pairs) if r else x

    def over_heads(x, d):
        return x if d == 0 else lax.ppermute(x, "head", [(i, i ^ d) for i in range(head_axis)])

    def next_span(x, way):
        pairs = [(i, i + way * slots) for i in range(seq) if 0 <= i + way * slots < seq]
        return lax.ppermute(x, "seq", pairs)

    def shape(dims, dtype):
        return jax.ShapeDtypeStruct(dims, dtype)

    prefetch = functools.partial(pltpu.PrefetchScalarGridSpec, num_scalar_prefetch=1)
    options = pltpu.CompilerParams(vmem_limit_bytes=VMEM_BYTES)
    from_hbm = pltpu.CompilerParams(vmem_limit_bytes=ALL_VMEM_BYTES)
    anywhere = pl.BlockSpec(memory_space=pl.ANY)
    smem = pl.BlockSpec(memory_space=pltpu.SMEM)
    vmem = pl.BlockSpec(memory_space=pltpu.VMEM)
    index_shape = shape((4,), jnp.int32)

    def cost(flops, moved):
        return pl.CostEstimate(flops=int(flops), bytes_accessed=int(moved), transcendentals=0)

    def to_members(pieces):
        return [turn(x, r) for r, x in enumerate(pieces)]

    sc = jnp.stack([c, h, z, k]).astype(jnp.int32)
    *tok_slices, sc = pl.pallas_call(
        functools.partial(slice_kernel, sz, slots),
        in_specs=[smem, smem, anywhere, vmem],
        out_specs=[vmem] * slots + [smem],
        out_shape=[shape((HALF + PAD, width), LOW)] * slots + [index_shape],
        scratch_shapes=[pltpu.SemaphoreType.DMA((slots,))],
        compiler_params=from_hbm,
    )(sc, slot_order, tokens, log_decay)
    tok_pieces = to_members(tok_slices)
    tok_others = [cross(x) for x in tok_pieces]

    wide = 2 * channels + shared
    w_sent, o_sent, pv_mine, pv_sent, *out_slices = pl.pallas_call(
        functools.partial(pack_kernel, sz),
        in_specs=[smem, smem] + [anywhere] * 5 + [vmem] * 5,
        out_specs=[vmem] * (4 + slots),
        out_shape=[
            shape((width, wide), LOW),
            shape((channels, width), LOW),
            shape((16, width), F32),
            shape((16, width), F32),
        ]
        + [shape((HALF, width), LOW)] * slots,
        scratch_shapes=[pltpu.SemaphoreType.DMA((4 + slots,))],
        compiler_params=from_hbm,
    )(
        sc, slot_order, grad_out, w_gate, w_inner, w_shared, w_out,
        in_gain, conv_inner, conv_shared, d_skip, norm_gain,
    )
    raw = [w_gate, w_inner, w_shared, w_out]
    sent = [cross(w_sent), cross(o_sent)]
    gains = [pv_mine, cross(pv_sent)]

    def span_total(table):
        ends = table[: sz.heads, BLOCK - 1 :: BLOCK]
        return jnp.repeat(jnp.exp(jnp.sum(ends, axis=1)), sz.head_width)[:, None]

    parts_shape = shape((head_axis, rows + PAD, chunk), LOW)
    weight_specs = [anywhere] * 6
    wide_weights = pltpu.VMEM((width, wide), LOW)
    out_weights = pltpu.VMEM((channels, width), LOW)
    copy_sems = pltpu.SemaphoreType.DMA((4,))
    dense = 2 * tok * width * (wide + channels)

    def forward(layer, sc, sources):
        def at(b, _):
            return (b, 0)

        piece = pl.BlockSpec((HALF, chunk), at)
        table = pl.BlockSpec((16, BLOCK), lambda b, _: (0, b))
        if layer == 0:
            src_specs = [whole((HALF + PAD, width))] * (2 * slots)
            more_specs = [table, table]
            more_shapes = [shape((16, tok), F32)] * 2
        else:
            src_specs = [piece] * (2 * head_axis) + [whole((HALF, width))] * (2 * slots) + [table]
            more_specs = [pl.BlockSpec((BLOCK, width), at)]
            more_shapes = [shape((tok, width), LOW)]

        last = [] if layer == 0 else [turned[3]]

        def call(halo, begin):
            return pl.pallas_call(
                functools.partial(forward_kernel, sz, layer, slots),
                grid_spec=prefetch(
                    grid=(nb,),
                    in_specs=src_specs
                    + [whole((16, width)), whole((16, width))]
                    + weight_specs
                    + [whole((8, sz.lin)), whole((channels, sz.states))]
                    + [whole(x.shape) for x in last],
                    out_specs=[
                        pl.BlockSpec((BLOCK, width), at),
                        pl.BlockSpec((BLOCK, channels), at),
                        pl.BlockSpec((BLOCK, sz.lin), at),
                        pl.BlockSpec((BLOCK, channels), at),
                        pl.BlockSpec((1, channels, sz.states), lambda b, _: (b, 0, 0)),
                        pl.BlockSpec((1, BLOCK), lambda b, _: (0, b)),
                        pl.BlockSpec((2, BLOCK), lambda b, _: (0, b)),
                        pl.BlockSpec((BLOCK, channels), at),
                        whole((channels, sz.states)),
                        smem,
                        piece,
                    ]
                    + more_specs,
                    scratch_shapes=[
                        pltpu.VMEM((BLOCK, width), LOW),
                        pltpu.VMEM((BLOCK, width), LOW),
                        wide_weights,
                        pltpu.VMEM((BLOCK + 8, sz.lin), F32),
                        pltpu.VMEM((channels, sz.states), F32),
                        copy_sems,
                    ],
                ),
                out_shape=[
                    shape((tok, width), LOW),
                    shape((tok, channels), F32),
                    shape((tok, sz.lin), LOW),
                    shape((tok, channels), F32),
                    shape((nb, channels, sz.states), LOW),
                    shape((1, tok), F32),
                    shape((2, tok), F32),
                    shape((tok, channels), LOW),
                    shape((channels, sz.states), F32),
                    index_shape,
                    shape((rows, chunk), LOW),
                ]
                + more_shapes,
                compiler_params=options,
                cost_estimate=cost(6 * dense, 16e6),
            )(sc, *sources, *gains, *raw, *sent, halo, begin, *last)

        halo = jnp.zeros((8, sz.lin), F32)
        begin = jnp.zeros((channels, sz.states), F32)
        if spans == 1:
            return call(halo, begin), halo
        trial = call(halo, begin)
        halo = next_span(trial[2][tok - 8 :].astype(F32), 1)
        local = call(halo, begin)[8]
        total = span_total(trial[11] if layer == 0 else sources[-1])
        for _ in range(spans - 1):
            begin = next_span(total * begin + local, 1)
        return call(halo, begin), halo

    def backward(layer, sc, sources, saved, decays, halo, deps):
        def at(i, _):
            return (nb - 1 - i, 0)

        if layer == 0:
            src_specs = [whole(s.shape) for s in sources]
        else:
            stat = pl.BlockSpec((2, BLOCK), lambda i, _: (0, nb - 1 - i))
            src_specs = [pl.BlockSpec((BLOCK, width), at)] + [stat] * head_axis
        gl, lin, ssd, inc = saved
        mixed_spec = [pl.BlockSpec((BLOCK, width), at)] if layer == 0 else []
        mixed_shape = [shape((tok, width), LOW)] if layer == 0 else []

        def call(halo_grad, begin):
            return pl.pallas_call(
                functools.partial(backward_kernel, sz, layer, len(deps)),
                grid_spec=prefetch(
                    grid=(nb,),
                    in_specs=src_specs
                    + [
                        pl.BlockSpec((BLOCK, channels), at),
                        whole(lin.shape),
                        pl.BlockSpec((BLOCK, channels), at),
                        pl.BlockSpec((1, channels, sz.states), lambda i, _: (nb - 1 - i, 0, 0)),
                        pl.BlockSpec((16, BLOCK), lambda i, _: (0, nb - 1 - i)),
                        whole((16, width)),
                        whole((16, width)),
                        whole((width, channels)),
                        whole((8, sz.lin)),
                        whole((8, sz.lin)),
                        whole((channels, sz.states)),
                    ]
                    + [anywhere] * len(deps),
                    out_specs=[
                        pl.BlockSpec((BLOCK, wide), at),
                        pl.BlockSpec((BLOCK, channels), at),
                        whole((PAD, 3 * channels)),
                        whole((8, sz.lin)),
                        whole((channels, sz.states)),
                        whole((8, sz.lin)),
                        smem,
                    ]
                    + mixed_spec,
                    scratch_shapes=[
                        pltpu.VMEM((BLOCK, width), LOW),
                        pltpu.VMEM((BLOCK + 8, sz.lin), F32),
                        pltpu.VMEM((BLOCK + 8, sz.lin), F32),
                        pltpu.VMEM((channels, sz.states), F32),
                        pltpu.VMEM((PAD, HALF), F32),
                        pltpu.VMEM((8, sz.lin), F32),
                    ],
                ),
                out_shape=[
                    shape((tok, wide), LOW),
                    shape((tok, channels), LOW),
                    shape((PAD, 3 * channels), LOW),
                    shape((8, sz.lin), F32),
                    shape((channels, sz.states), F32),
                    shape((8, sz.lin), F32),
                    index_shape,
                ]
                + mixed_shape,
                compiler_params=options,
                cost_estimate=cost(8 * dense, 16e6),
            )(
                sc, *sources, gl, lin, ssd, inc, decays, *gains, turned[2 + layer],
                halo, halo_grad, begin, *deps,
            )

        halo_grad = jnp.zeros((8, sz.lin), F32)
        begin = jnp.zeros((channels, sz.states), F32)
        if spans == 1:
            return call(halo_grad, begin)
        local = call(halo_grad, begin)[4]
        for _ in range(spans - 1):
            begin = next_span(span_total(decays) * begin + local, -1)
        halo_grad = next_span(call(halo_grad, begin)[5], -1)
        return call(halo_grad, begin)

    def project(layer, sc, unit, stats, deps):
        return pl.pallas_call(
            functools.partial(project_kernel, sz, layer, len(deps)),
            in_specs=[smem, vmem, vmem] + weight_specs + [anywhere] * len(deps),
            out_specs=[vmem, vmem, smem],
            out_shape=[parts_shape, parts_shape, index_shape],
            scratch_shapes=[out_weights, copy_sems],
            compiler_params=options,
            cost_estimate=cost(dense / 4, 4e6),
        )(sc, unit, stats, *raw, *sent, *deps)

    def lift(layer, sc, cat, normed, small, deps):
        outs = pl.pallas_call(
            functools.partial(lift_kernel, sz, layer, len(deps)),
            in_specs=[smem] + [vmem] * 6 + [anywhere] * len(deps),
            out_specs=[vmem] * (1 + head_axis) + [smem, vmem],
            out_shape=[parts_shape]
            + [shape(parts_shape.shape[1:], LOW)] * head_axis
            + [index_shape, shape((PAD, chunk), LOW)],
            scratch_shapes=[pltpu.VMEM((8, width), F32)],
            compiler_params=options,
            cost_estimate=cost(dense, 8e6),
        )(sc, cat, normed, *gains, small, turned[layer], *deps)
        return outs[0], list(outs[1:-2]), outs[-2], outs[-1]

    def scatter(sc, keep, send, riders=(), deps=()):
        size = rows + PAD + sum(PAD + rider[1].shape[0] for rider in riders)
        flat = [x for rider in riders for x in rider]
        got = [cross(x) for x in (send if isinstance(send, list) else [send])]
        joined = pl.pallas_call(
            functools.partial(join_kernel, sz, len(got), len(riders), len(deps)),
            in_specs=[smem] + [vmem] * (1 + len(got) + len(flat)) + [anywhere] * len(deps),
            out_specs=[smem] + [vmem] * head_axis,
            out_shape=[index_shape, shape((size, chunk), F32)]
            + [shape((size, chunk), LOW)] * (head_axis - 1),
            compiler_params=options,
        )(sc, keep, *got, *flat, *deps)
        return [over_heads(joined[1 + d], d) for d in far_first(head_axis)], joined[0]

    def gather(low):
        own = [over_heads(low, d) for d in far_first(head_axis)]
        return own + [cross(x) for x in own]

    turned = pl.pallas_call(
        functools.partial(turn_kernel, sz),
        in_specs=[smem] + weight_specs,
        out_specs=[vmem] * 4,
        out_shape=[shape((wide, width), LOW)] * 2 + [shape((width, channels), LOW)] * 2,
        scratch_shapes=[wide_weights, out_weights, copy_sems],
        compiler_params=options,
        cost_estimate=cost(1e9, 8e6),
    )

    def section_output(layer, sc, parts, resid, deps=()):
        return pl.pallas_call(
            functools.partial(output_kernel, sz, layer),
            in_specs=[smem] + [vmem] * (head_axis + 1) + [anywhere] * len(deps),
            out_specs=[vmem] * 4 + [smem],
            out_shape=[
                shape((rows, chunk), F32),
                shape((rows, chunk), LOW),
                shape((rows, chunk), F32),
                shape((8, HALF), F32),
                index_shape,
            ],
            compiler_params=options,
        )(sc, *parts, resid, *deps)

    part = width // seq
    columns = 3 * channels
    share = part // head_axis
    shared_size = seq * share + PAD

    def section_input(layer, sc, parts, *others, deps=()):
        if layer == 0:
            outs = [
                shape((rows + PAD, chunk), LOW),
                shape((rows + shared_size, chunk), LOW),
                shape((shared_size, chunk), F32),
            ]
        else:
            outs = [shape((rows, chunk), F32), shape((rows + PAD, chunk), LOW)]
        return pl.pallas_call(
            functools.partial(input_kernel, sz, layer),
            in_specs=[smem] + [vmem] * (head_axis + len(others)) + [anywhere] * len(deps),
            out_specs=[vmem] * len(outs) + [smem],
            out_shape=outs + [index_shape],
            compiler_params=options,
        )(sc, *parts, *others, *deps)

    def weight_grads(sc, normed, cat, mixed, scaled, small, deps=(), common=None):
        more = [] if common is None else [common]
        size = seq * share + PAD * len(more)
        outs = pl.pallas_call(
            functools.partial(weights_kernel, sz, seq, len(deps), bool(more)),
            in_specs=[smem] + [vmem] * (5 + len(more)) + [anywhere] * len(deps),
            out_specs=[smem] + [vmem] * (seq + head_axis),
            out_shape=[index_shape]
            + [shape((part + PAD, columns), LOW)] * seq
            + [shape((size, shared), LOW)] * head_axis,
            scratch_shapes=[pltpu.VMEM((width, columns), LOW), pltpu.VMEM((width, shared), F32)],
            compiler_params=options,
            cost_estimate=cost(4 * dense, 12e6),
        )(sc, normed, cat, mixed, scaled, small, *more, *deps)
        return over_seq(outs[1 : 1 + seq]), outs[1 + seq :], outs[0]

    def shifted(x, r):
        return lax.ppermute(x, "seq", [(i, (i + r) % seq) for i in range(seq)]) if r else x

    def over_seq(chunks):
        return [shifted(x, r) for r, x in enumerate(chunks)]

    def leave(sc, *arrays, riders=0):
        size = BLOCK + (share + PAD if riders else 0)
        pieces = pl.pallas_call(
            functools.partial(leave_kernel, sz, slots, riders),
            in_specs=[smem] + [vmem] * len(arrays),
            out_specs=[vmem] * slots + [smem],
            out_shape=[shape((size, chunk), LOW)] * slots + [index_shape],
            compiler_params=options,
        )(sc, *arrays)
        return to_members(pieces[:slots]), pieces[slots]

    out_pieces = to_members(out_slices)
    fw0, halo0 = forward(0, sc, tok_pieces + tok_others)
    base0, decays = fw0[10], fw0[11:13]
    pr0 = project(0, fw0[9], fw0[7], fw0[6], [out_pieces[1], out_pieces[-1]])
    out_others = [cross(x) for x in out_pieces]
    parts, sc_join = scatter(sc, pr0[0], pr0[1])
    turned = turned(sc_join, *raw, *sent)
    res1, low1, mixed0, square0, unused = section_output(0, sc, parts, base0, turned)
    pieces1 = gather(low1)
    square_other = cross(square0)

    fw1, halo1 = forward(1, sc, pieces1 + out_pieces + out_others + [decays[1]])
    stat = fw1[6] + cross(fw1[6])
    stats = [stat] + [over_heads(stat, d) for d in range(1, head_axis)]
    pr1 = project(1, fw1[9], fw1[7], fw1[6], [])
    parts_out, sc_out = scatter(sc, pr1[0], pr1[1])
    bw1 = backward(1, sc_out, [fw1[11]] + stats, fw1[1:5], decays[1], halo1, [])
    lf1 = lift(1, bw1[6], bw1[0], fw1[0], bw1[3], parts_out[1:])
    weights1, heads1, sc_weights = weight_grads(
        lf1[2], fw1[0], bw1[0], fw1[11], bw1[1], bw1[2], common=lf1[3]
    )
    parts, sc_join = scatter(sc_weights, lf1[0], lf1[1])
    igrad1, glow1, sc_in = section_input(
        1, sc_join, parts, res1, fw1[10], fw1[5], *gains, mixed0,
        deps=[weights1[1], weights1[-1]],
    )
    piecesg = gather(glow1)

    heads1 = [over_heads(heads1[d], d) for d in far_first(head_axis)]

    early, unused = leave(sc_in, low1, pieces1[head_axis], glow1, piecesg[head_axis])
    bw0 = backward(
        0, sc, piecesg + [square0, square_other], fw0[1:5], decays[0], halo0,
        weights1[2:-1],
    )
    weights0, heads0, sc_weights = weight_grads(
        bw0[6], fw0[0], bw0[0], bw0[7], bw0[1], bw0[2], deps=early[1:],
    )
    lf0 = lift(0, sc_weights, bw0[0], fw0[0], bw0[3], heads1[1:])
    parts, sc_join = scatter(lf0[2], lf0[0], lf0[1], [[lf0[3], *heads0]], weights0[1:2])

    unused, low2, unused_mixed, unused_square, sc_out = section_output(1, sc_in, parts_out, res1)
    glow0, to_other, shared_own, sc_end = section_input(
        0, sc_out, parts, base0, igrad1, fw0[5], *gains, low2, *heads1,
        deps=weights0[2:],
    )
    got = cross(to_other)
    if spans == 1:
        late, sc_end = leave(sc_end, glow0, got, low2, got, shared_own, riders=seq)
        shared_parts = late
    else:
        late, sc_end = leave(sc_end, glow0, got, low2, got)
        total = shared_own + got[rows:].astype(F32)
        extra = resplit(total[:PAD])
        fill = jnp.zeros((BLOCK, shared), F32)
        chunks = [
            jnp.concatenate([fill, extra, total[PAD + r * share : PAD + (r + 1) * share]])
            for r in range(seq)
        ]
        shared_parts = over_seq([x.astype(LOW) for x in chunks])
    section_out, input_grad, unused = pl.pallas_call(
        functools.partial(home_kernel, slots),
        in_specs=[smem] + [vmem] * (2 * slots),
        out_specs=[vmem, vmem, smem],
        out_shape=[shape((slots, BLOCK, chunk), F32)] * 2 + [index_shape],
        compiler_params=options,
    )(sc, *early, *late)

    def summed(sc, pieces, *done):
        return pl.pallas_call(
            functools.partial(sum_kernel, sz, bool(done)),
            in_specs=[smem] + [vmem] * (len(pieces) + len(done)),
            out_shape=[shape((part + PAD, columns), LOW)] * (1 + len(done)),
            compiler_params=options,
        )(sc, *pieces, *done)

    own_sums, other_sums = summed(sc_end, weights0, *summed(sc_in, weights1))
    final = pl.pallas_call(
        functools.partial(final_kernel, sz, seq),
        in_specs=[smem] + [vmem] * (2 + seq),
        out_shape=[
            shape((part, inner_dev), F32),
            shape((part, inner_dev), F32),
            shape((inner_dev, part), F32),
            shape((taps, inner_dev), F32),
            shape((1, inner_dev), F32),
            shape((1, heads_dev), F32),
            shape((share, shared), F32),
            shape((taps, shared // (seq * head_axis)), F32),
            shape((1, width // (seq * head_axis)), F32),
        ],
        compiler_params=options,
    )(sc, own_sums, cross(other_sums), *shared_parts)
    return (
        section_out[None],
        input_grad[None],
        final[8],
        final[0][None],
        final[1][None],
        final[6][None],
        final[3][None],
        final[7][None],
        final[5],
        final[4],
        final[2][None],
    )


def solution(mesh):
    placed = (
        P(None, "seq", None),
        P(),
        P("section", None, "head", "seq"),
        P(None, "seq", None),
        P("section", None),
        P("section", None, "head"),
        P("section", None, "head"),
        P("section", None, None),
        P("section", None, "head"),
        P("section", None, None),
        P("section", "head"),
        P("section", "head"),
        P("section", None, None),
    )
    return jax.shard_map(
        per_device,
        mesh=mesh,
        in_specs=placed,
        out_specs=(
            P("section", None, "seq", "head"),
            P("section", None, "seq", "head"),
            P("section", ("seq", "head")),
            P("section", "seq", "head"),
            P("section", "seq", "head"),
            P("section", ("seq", "head"), None),
            P("section", None, "head"),
            P("section", None, ("seq", "head")),
            P("section", "head"),
            P("section", "head"),
            P("section", "head", "seq"),
        ),
        check_vma=False,
    )
```

```python
import functools

import jax
import jax.numpy as jnp
from jax import lax
from jax.experimental import pallas as pl
from jax.experimental.pallas import tpu as pltpu
from jax.sharding import PartitionSpec as P

BLOCK = 256
HALF = BLOCK // 2
PAD = 16
EPS = 1e-05
F32 = jnp.float32
LOW = jnp.bfloat16
HIDDEN = -1e30
NN = ((1,), (0,))
NT = ((1,), (1,))
TN = ((0,), (0,))
VMEM_BYTES = 50 * 1024 * 1024
ALL_VMEM_BYTES = 63 * 1024 * 1024


def dot(a, b, dims):
    return lax.dot_general(a, b, (dims, ((), ())), preferred_element_type=F32)


def aligned(start, size):
    return pl.ds(pl.multiple_of(start, size), size)


def spread(cols, first, count, width):
    rows = cols.shape[0]
    lane = lax.broadcasted_iota(jnp.int32, (rows, count * width), 1)
    out = jnp.broadcast_to(cols[:, first : first + 1], (rows, count * width))
    for h in range(1, count):
        out = jnp.where(lane >= h * width, cols[:, first + h : first + h + 1], out)
    return out


def per_head(array, h, width):
    lane = lax.broadcasted_iota(jnp.int32, array.shape, 1)
    inside = (lane >= h * width) & (lane < (h + 1) * width)
    return jnp.where(inside, array, jnp.zeros_like(array))


def split_low(value):
    high = value.astype(LOW).astype(F32)
    return high, value - high


def column_of(row, size):
    return jnp.transpose(jnp.broadcast_to(row, (128, size)))


def sigmoid(v):
    return 0.5 * jnp.tanh(0.5 * v) + 0.5


def pick(flag, a, b):
    return jnp.where(flag, a, b)


class Sizes:
    def __init__(self, blocks, width, channels, heads, states, taps, head_axis, inner):
        self.blocks = blocks
        self.width = width
        self.channels = channels
        self.heads = heads
        self.head_width = channels // heads
        self.states = states
        self.lin = channels + 2 * states
        self.taps = taps
        self.head_axis = head_axis
        self.chunk = width // head_axis
        self.rows = blocks * HALF
        self.tokens = blocks * BLOCK
        self.inner = inner


def weight_copies(sz, layer, c, h, raw, got, wv, ov, sems):
    gate, inner, shared, out = raw
    ch = sz.channels
    cols = aligned(c * ch, ch)
    rows = aligned((h * 2 + c) * ch, ch)
    own, sent = [], []
    if wv is not None:
        own += [
            (gate.at[0, :, cols], wv.at[:, :ch]),
            (inner.at[0, :, cols], wv.at[:, ch : 2 * ch]),
            (shared.at[0], wv.at[:, 2 * ch :]),
        ]
        sent += [
            (got[0], wv.at[:, :ch]),
            (got[1], wv.at[:, ch : 2 * ch]),
            (got[2], wv.at[:, 2 * ch :]),
        ]
    if ov is not None:
        own += [(out.at[0, rows, :], ov)]
        sent += [(got[3], ov)]
    return [
        (c == layer, [pltpu.make_async_copy(p, q, sems.at[i]) for i, (p, q) in enumerate(own)]),
        (c != layer, [pltpu.make_async_copy(p, q, sems.at[i]) for i, (p, q) in enumerate(sent)]),
    ]


def run_copies(choices, start, wait):
    for flag, copies in choices:

        @pl.when(flag)
        def _(copies=copies):
            if start:
                for copy in copies:
                    copy.start()
            if wait:
                for copy in copies:
                    copy.wait()


def put_ordered(sz, dst, c, k, b, own, other):
    for r in range(len(own)):

        @pl.when(lax.rem(k - b + len(own), len(own)) == r)
        def _(r=r):
            put_pair(dst, c, own[r][:HALF, :], other[r][:HALF, :])


def put_pair(dst, c, own, other):
    dst[aligned(c * HALF, HALF), :] = own
    dst[aligned((1 - c) * HALF, HALF), :] = other


def far_first(count):
    return [0] + list(range(count - 1, 0, -1))


def put_pieces(sz, dst, c, h, own, other):
    own, other = (dict(zip(far_first(sz.head_axis), side)) for side in (own, other))
    for d in range(sz.head_axis):
        cols = aligned((h ^ d) * sz.chunk, sz.chunk)
        dst[aligned(c * HALF, HALF), cols] = own[d]
        dst[aligned((1 - c) * HALF, HALF), cols] = other[d]


def line_of(table, at):
    line = lax.broadcasted_iota(jnp.int32, table.shape, 0)
    return jnp.sum(jnp.where(line == at, table, 0.0), axis=0, keepdims=True)


def conv_forward(sz, ext, taps):
    pre = taps[0:1] * ext[5 : 5 + BLOCK, :]
    for j in range(1, sz.taps):
        pre = pre + taps[j : j + 1] * ext[5 + j : 5 + j + BLOCK, :]
    return pre


def decay_of(sz, cols, rp, h, mask):
    rows = cols[:, h : h + 1] + rp[12 + h : 13 + h, :]
    return jnp.exp(jnp.where(mask, rows, HIDDEN))


def lower_mask():
    t = lax.broadcasted_iota(jnp.int32, (BLOCK, BLOCK), 0)
    s = lax.broadcasted_iota(jnp.int32, (BLOCK, BLOCK), 1)
    return t >= s


def forward_kernel(sz, layer, slots, sc, *refs):
    n = sz.head_axis
    sources = 2 * slots if layer == 0 else 2 * n + 2 * slots
    src, refs = refs[:sources], refs[sources:]
    if layer == 1:
        table, refs = refs[0], refs[1:]
    gains, raw, got, halo, begin = refs[0:2], refs[2:6], refs[6:10], refs[10], refs[11]
    refs = refs[12:]
    if layer == 1:
        ov, refs = refs[0], refs[1:]
    normed_o, gl_o, lin_o, ssd_o, inc_o, inv_o, part_o, unit_o, fin_o, sc_o, base_o = refs[:11]
    refs = refs[11:]
    if layer == 1:
        mixed_o, refs = refs[0], refs[1:]
    else:
        tables_o, refs = refs[0:2], refs[2:]
    xs, ms, wv, ext, state, sems = refs
    b = pl.program_id(0)
    c, h, k = sc[0], sc[1], sc[3]
    ch, st = sz.channels, sz.states
    copies = weight_copies(sz, layer, c, h, raw, got, wv, None, sems)

    @pl.when(b == 0)
    def _():
        run_copies(copies, True, False)
        ext[0:8, :] = halo[...]
        state[...] = begin[...]
        for i in range(4):
            sc_o[i] = sc[i]

    mine = aligned(c * HALF, HALF)
    cols = aligned(h * sz.chunk, sz.chunk)
    if layer == 0:
        put_ordered(sz, xs, c, k, b, src[:slots], src[slots:])
        base_o[...] = xs[mine, cols]
        for r in range(slots):

            @pl.when(lax.rem(k - b + slots, slots) == r)
            def _(r=r):
                own = decay_table(rates_of(src[r]), c, sz.heads)
                other = decay_table(rates_of(src[slots + r]), c, sz.heads)
                tables_o[0][...] = pick(c == 0, own, other)
                tables_o[1][...] = pick(c == 0, other, own)

        rp = tables_o[0][...]
    else:
        put_pieces(sz, xs, c, h, [r[...] for r in src[:n]], [r[...] for r in src[n : 2 * n]])
        put_ordered(sz, ms, c, k, b, src[2 * n : 2 * n + slots], src[2 * n + slots :])
        base_o[...] = ms[mine, cols]
        mixed_o[...] = ms[...]
        rp = table[...]

    pv = pick(c == layer, gains[0][...], gains[1][...])
    x = xs[...].astype(F32)
    inv_in = lax.rsqrt(jnp.mean(x * x, axis=1, keepdims=True) + EPS)
    normed = (x * inv_in * pv[0:1, : sz.width]).astype(LOW)
    normed_o[...] = normed

    @pl.when(b == 0)
    def _():
        run_copies(copies, False, True)

    proj = dot(normed, wv[...], NN)
    gl = proj[:, :ch]
    gl_o[...] = gl
    lin = proj[:, ch:].astype(LOW)
    lin_o[...] = lin
    ext[8 : 8 + BLOCK, :] = lin.astype(F32)
    pre = conv_forward(sz, ext, pv[1:5, : sz.lin])
    ext[0:8, :] = ext[BLOCK : BLOCK + 8, :]
    act = (pre * sigmoid(pre)).astype(LOW)
    values, bm, cm = act[:, :ch], act[:, ch : ch + st], act[:, ch + st :]

    cols = jnp.transpose(rp)
    mask = lower_mask()
    gram = dot(cm, bm, NT)
    mixes, parts = [], []
    for i in range(sz.heads):
        mixes.append((gram * decay_of(sz, cols, rp, i, mask)).astype(LOW))
        parts.append(per_head(values, i, sz.head_width))
    intra = dot(jnp.concatenate(mixes, axis=1), jnp.concatenate(parts, axis=0), NN)

    low_state = state[...].astype(LOW)
    inc_o[0] = low_state
    ecum = spread(cols, sz.heads, sz.heads, sz.head_width)
    inter = dot(cm, low_state, NT) * ecum
    vf = values.astype(F32)
    carried = (vf * spread(cols, 2 * sz.heads, sz.heads, sz.head_width)).astype(LOW)
    local = dot(carried, bm, TN)
    for i in range(sz.heads):
        rows = slice(i * sz.head_width, (i + 1) * sz.head_width)
        total = cols[BLOCK - 1 : BLOCK, sz.heads + i : sz.heads + i + 1]
        state[rows, :] = total * state[rows, :] + local[rows]
    ssd = intra + inter + pv[6:7, :ch] * vf
    ssd_o[...] = ssd
    gated = ssd * (gl * sigmoid(gl))
    weighty = gated * pv[5:6, :ch]
    unit_o[...] = weighty.astype(LOW)

    lane = lax.broadcasted_iota(jnp.int32, (BLOCK, 128), 1)
    square = jnp.sum(gated * gated, axis=1, keepdims=True)
    if layer == 0:
        project = jnp.zeros_like(square)
    else:
        scaled_grad = dot(ms[...], ov[...], NN)
        project = jnp.sum(scaled_grad * weighty, axis=1, keepdims=True)
    stats = jnp.where(lane == 0, square, jnp.where(lane == 1, project, inv_in))
    stats = jnp.transpose(stats)
    part_o[...] = stats[0:2, :]
    inv_o[...] = stats[2:3, :]

    @pl.when(b == sz.blocks - 1)
    def _():
        fin_o[...] = state[...]


def scalar_lines(sz, lines):
    fill = [jnp.zeros((8 - sz.blocks, HALF), F32)] if sz.blocks < 8 else []
    high, low = split_low(jnp.concatenate(lines + fill, axis=0))
    table = jnp.concatenate([high, low], axis=0).astype(LOW)
    return jnp.concatenate([table] * (sz.chunk // HALF), axis=1)


def own_rows(sz, ref, which):
    blocks = [ref[aligned(b * BLOCK + which * HALF, HALF), :] for b in range(sz.blocks)]
    return jnp.concatenate(blocks, axis=0)


def project_kernel(sz, layer, deps, sc, unit_r, stats_r, *refs):
    raw, got, refs = refs[:4], refs[4:8], refs[8 + deps :]
    keep, send, sc_o, weights, sems = refs
    c, h = sc[0], sc[1]
    copies = weight_copies(sz, layer, c, h, raw, got, None, weights, sems)
    run_copies(copies, True, False)
    for i in range(4):
        sc_o[i] = sc[i]
    sides = []
    for which, out in ((c, keep), (1 - c, send)):
        sides.append((out, own_rows(sz, unit_r, which)))
        lines = [
            stats_r[0:1, aligned(b * BLOCK + which * HALF, HALF)] for b in range(sz.blocks)
        ]
        table = scalar_lines(sz, lines)
        for d in range(sz.head_axis):
            out[d, sz.rows :, :] = table
    run_copies(copies, False, True)
    for out, rows in sides:
        for d in range(sz.head_axis):
            chunk = weights[:, aligned((h ^ d) * sz.chunk, sz.chunk)]
            out[d, : sz.rows, :] = dot(rows, chunk, NN).astype(LOW)


def turn_kernel(sz, sc, *refs):
    raw, got, refs = refs[:4], refs[4:8], refs[8:]
    wide_o, out_o, wv, ov, sems = refs[:2], refs[2:4], refs[4], refs[5], refs[6]
    for layer in range(2):
        copies = weight_copies(sz, layer, sc[0], sc[1], raw, got, wv, ov, sems)
        run_copies(copies, True, True)
        wide_o[layer][...] = jnp.transpose(wv[...])
        out_o[layer][...] = jnp.transpose(ov[...])


def out_at(out, d):
    return out[d] if isinstance(out, tuple) else out.at[d]


def lift_kernel(sz, layer, deps, sc, cat_r, normed_r, zero_gains, one_gains, small_r, *refs):
    weights, refs = refs[0], refs[1 + deps :]
    keep, send, sc_o, common_o, wide = refs[0], refs[1:-3], *refs[-3:]
    c, h = sc[0], sc[1]
    for i in range(4):
        sc_o[i] = sc[i]
    wide[...] = jnp.zeros_like(wide)
    for which, out in ((c, keep), (1 - c, send)):
        rows = own_rows(sz, cat_r, which)
        along = jnp.zeros((sz.rows, 1), F32)
        for d in range(sz.head_axis):
            cols = aligned((h ^ d) * sz.chunk, sz.chunk)
            product = dot(rows, weights[:, cols], NN)
            out_at(out, d)[: sz.rows, :] = product.astype(LOW)
            blocks = [
                normed_r[aligned(b * BLOCK + which * HALF, HALF), cols] for b in range(sz.blocks)
            ]
            product = product * jnp.concatenate(blocks, axis=0).astype(F32)
            wide[0:1, cols] += jnp.sum(product, axis=0, keepdims=True)
            along = along + jnp.sum(product, axis=1, keepdims=True)
        lines = [
            jnp.transpose(jnp.broadcast_to(along[b * HALF : (b + 1) * HALF], (HALF, 128)))[0:1, :]
            for b in range(sz.blocks)
        ]
        table = scalar_lines(sz, lines)
        for d in range(sz.head_axis):
            out_at(out, d)[sz.rows :, :] = table
    gain_grad = wide[0:1, :] / pick(c == layer, zero_gains[0:1, :], one_gains[0:1, :])
    flat = [small_r[j : j + 1, sz.channels :] for j in range(sz.taps)]
    flat += [gain_grad[:, q * sz.chunk : (q + 1) * sz.chunk] for q in range(sz.head_axis)]
    high, low = split_low(jnp.concatenate(flat, axis=0))
    common_o[...] = jnp.concatenate([high, low], axis=0).astype(LOW)


def backward_kernel(sz, layer, deps, sc, *refs):
    n = sz.head_axis
    sources = 2 * n + 2 if layer == 0 else 1 + n
    src, refs = refs[:sources], refs[sources:]
    gl_r, lin_r, ssd_r, inc_r = refs[:4]
    table, gains, ov = refs[4], refs[5:7], refs[7]
    halo, halo_grad, begin = refs[8:11]
    refs = refs[11 + deps :]
    cat_o, scaled_o, small_o, sums_o, fin_o, rim_o, sc_o = refs[:7]
    refs = refs[7:]
    if layer == 0:
        mixed_o, refs = refs[0], refs[1:]
    ms, ext, back, state, heads_p, small = refs
    i_step = pl.program_id(0)
    b = sz.blocks - 1 - i_step
    c, h = sc[0], sc[1]
    ch, st = sz.channels, sz.states
    pv = pick(c == layer, gains[0][...], gains[1][...])
    rp = table[...]

    @pl.when(i_step == 0)
    def _():
        back[BLOCK : BLOCK + 8, :] = halo_grad[...]
        state[...] = begin[...]
        small[...] = jnp.zeros_like(small)
        for i in range(4):
            sc_o[i] = sc[i]
        if layer == 0:
            for i in range(2):
                extra = src[i * n][sz.rows :, :].astype(F32)
                for d in range(1, n):
                    extra = extra + src[i * n + d][sz.rows :, :].astype(F32)
                heads_p[8 * i : 8 * i + 8, :] = extra[0:8, :HALF] + extra[8:16, :HALF]

    if layer == 0:
        rows = aligned(b * HALF, HALF)
        put_pieces(
            sz, ms, c, h, [r[rows, :] for r in src[:n]], [r[rows, :] for r in src[n : 2 * n]]
        )
        halves = []
        for k in range(2):
            alpha = lax.rsqrt(line_of(src[2 * n + k][...], b) / sz.inner + EPS)
            beta = alpha * alpha * line_of(heads_p[...], 8 * k + b) / sz.inner
            halves.append((alpha, beta))
        alpha, beta = (
            pick(
                c == 0,
                jnp.concatenate([halves[0][q], halves[1][q]], axis=1),
                jnp.concatenate([halves[1][q], halves[0][q]], axis=1),
            )
            for q in range(2)
        )
    else:
        stats = src[1][...]
        for d in range(1, n):
            stats = stats + src[1 + d][...]
        alpha = lax.rsqrt(stats[0:1, :] / sz.inner + EPS)
        beta = alpha * alpha * alpha * stats[1:2, :] / sz.inner

    sub = lax.broadcasted_iota(jnp.int32, rp.shape, 0)
    cols = jnp.transpose(jnp.where(sub == 12, alpha, jnp.where(sub == 13, beta, rp)))
    alpha, beta = cols[:, 12:13], cols[:, 13:14]

    gl = gl_r[...]
    ssd = ssd_r[...]
    sig = sigmoid(gl)
    swish = gl * sig
    slope = sig * (1.0 + gl * (1.0 - sig))
    gated = ssd * swish
    if layer == 0:
        mixed_grad = ms[...]
        mixed_o[...] = mixed_grad
    else:
        mixed_grad = src[0][...]
    scaled_grad = dot(mixed_grad, ov[...], NN)
    gain = pv[5:6, :ch]
    normal = gated * alpha
    small[4:5, :ch] += jnp.sum(scaled_grad * normal, axis=0, keepdims=True)
    scaled_o[...] = (normal * gain).astype(LOW)
    gated_grad = alpha * (scaled_grad * gain) - beta * gated
    ssd_grad = (gated_grad * swish).astype(LOW)
    gate_grad = (gated_grad * ssd * slope).astype(LOW)
    sgf = ssd_grad.astype(F32)

    before = lin_r[pl.ds(pl.multiple_of(jnp.maximum(b * BLOCK - 16, 0), 16), 16), :]
    ext[0:8, :] = pick(b > 0, before.astype(F32)[8:16, :], halo[...])
    ext[8 : 8 + BLOCK, :] = lin_r[aligned(b * BLOCK, BLOCK), :].astype(F32)
    taps = pv[1:5, : sz.lin]
    pre = conv_forward(sz, ext, taps)
    psig = sigmoid(pre)
    pact = pre * psig
    pslope = psig * (1.0 + pre * (1.0 - psig))
    act = pact.astype(LOW)
    values, bm, cm = act[:, :ch], act[:, ch : ch + st], act[:, ch + st :]
    vf = values.astype(F32)
    small[5:6, :ch] += jnp.sum(sgf * vf, axis=0, keepdims=True)

    mask = lower_mask()
    gram = dot(cm, bm, NT)
    gram_grad = jnp.zeros((BLOCK, BLOCK), F32)
    mixes, parts = [], []
    for i in range(sz.heads):
        decay = decay_of(sz, cols, rp, i, mask)
        mixes.append((gram * decay).astype(LOW))
        parts.append(per_head(ssd_grad, i, sz.head_width))
        gram_grad = gram_grad + dot(parts[-1], values, NT) * decay
    intra_grad = dot(jnp.concatenate(mixes, axis=0), jnp.concatenate(parts, axis=0), TN)

    ecum = spread(cols, sz.heads, sz.heads, sz.head_width)
    to_end = spread(cols, 2 * sz.heads, sz.heads, sz.head_width)
    inter_grad = (sgf * ecum).astype(LOW)
    low_state = state[...].astype(LOW)
    carried = (vf * to_end).astype(LOW)
    carried_grad = dot(bm, low_state, NT)
    gram_low = gram_grad.astype(LOW)
    b_grad = dot(gram_low, cm, TN) + dot(carried, low_state, NN)
    c_grad = dot(gram_low, bm, NN) + dot(inter_grad, inc_r[0], NN)
    value_grad = intra_grad + pv[6:7, :ch] * sgf + carried_grad * to_end
    entry = dot(inter_grad, cm, TN)
    for i in range(sz.heads):
        rows = slice(i * sz.head_width, (i + 1) * sz.head_width)
        total = cols[BLOCK - 1 : BLOCK, sz.heads + i : sz.heads + i + 1]
        state[rows, :] = total * state[rows, :] + entry[rows]

    pre_grad = jnp.concatenate([value_grad, b_grad, c_grad], axis=1) * pslope
    back[0:BLOCK, :] = pre_grad
    lin_grad = taps[0:1] * back[sz.taps - 1 : sz.taps - 1 + BLOCK, :]
    for j in range(1, sz.taps):
        at = sz.taps - 1 - j
        lin_grad = lin_grad + taps[j : j + 1] * back[at : at + BLOCK, :]
    for j in range(sz.taps):
        small[j : j + 1, :] += jnp.sum(pre_grad * ext[5 + j : 5 + j + BLOCK, :], axis=0, keepdims=True)
    back[BLOCK : BLOCK + 8, :] = back[0:8, :]
    cat_o[...] = jnp.concatenate([gate_grad, lin_grad.astype(LOW)], axis=1)

    @pl.when(i_step == sz.blocks - 1)
    def _():
        fin_o[...] = state[...]
        rim_o[...] = back[0:8, :]
        sums = small[...]
        flat = [sums[j : j + 1, :ch] for j in range(sz.taps + 2)]
        flat = [jnp.concatenate(flat[j : j + 3], axis=1) for j in range(0, len(flat), 3)]
        flat = flat + [jnp.zeros_like(flat[0])] * (4 - len(flat))
        high, low = split_low(jnp.concatenate(flat, axis=0))
        rest = jnp.zeros((PAD - 8, high.shape[1]), F32)
        small_o[...] = jnp.concatenate([high, low, rest], axis=0).astype(LOW)
        sums_o[...] = sums


def weights_kernel(sz, seq, deps, with_common, sc, normed, cat, mixed, scaled, small, *refs):
    if with_common:
        common, refs = refs[0], refs[1:]
    refs = refs[deps:]
    sc_o, outs, heads, full, wide = refs[0], refs[1 : seq + 1], refs[seq + 1 : -2], refs[-2], refs[-1]
    for i in range(4):
        sc_o[i] = sc[i]
    ch, st = sz.channels, sz.states
    step = sz.chunk
    for q in range(sz.head_axis):
        at = slice(q * step, (q + 1) * step)
        grads = dot(normed[:, at], cat[...], TN)
        full[at, : 2 * ch] = grads[:, : 2 * ch].astype(LOW)
        wide[at, :] = grads[:, 2 * ch :]
        full[at, 2 * ch :] = dot(mixed[:, at], scaled[...], TN).astype(LOW)
    rows = sz.width // seq
    part = rows // sz.head_axis
    for r, out in enumerate(outs):
        out[:rows, :] = full[aligned(lax.rem(sc[2] + r, seq) * rows, rows), :]
        out[rows:, :] = small[...]
    for d, out in enumerate(heads):
        lines = [
            wide[aligned(lax.rem(sc[2] + r, seq) * rows + (sc[1] ^ d) * part, part), :]
            for r in range(seq)
        ]
        if with_common:
            lines = [common[...].astype(F32)] + lines
        out[...] = jnp.concatenate(lines, axis=0).astype(LOW)


def resplit(extra):
    half = extra.shape[0] // 2
    high, low = split_low(extra[:half, :] + extra[half:, :])
    return jnp.concatenate([high, low], axis=0)


def join_kernel(sz, parts, riders, deps, sc, keep, *refs):
    n = sz.head_axis
    recv, refs = refs[0] if parts == 1 else refs[:parts], refs[parts:]
    more = [(refs[i * (n + 1)], refs[i * (n + 1) + 1 : (i + 1) * (n + 1)]) for i in range(riders)]
    refs = refs[riders * (n + 1) + deps :]
    sc_o, outs = refs[0], refs[1:]
    rows = sz.rows
    for i in range(4):
        sc_o[i] = sc[i]
    extra = resplit(keep[0, rows:, :].astype(F32) + out_at(recv, 0)[rows:, :].astype(F32))
    for d, out in enumerate(outs):
        both = keep[d, :rows, :].astype(F32) + out_at(recv, d)[:rows, :].astype(F32)
        out[:rows, :] = both.astype(out.dtype)
        out[rows : rows + PAD, :] = extra.astype(out.dtype)
        at = rows + PAD
        for common, rider in more:
            size = rider[d].shape[0]
            out[at : at + PAD, :] = common[...].astype(out.dtype)
            out[at + PAD : at + PAD + size, :] = rider[d][...].astype(out.dtype)
            at += PAD + size


def total_of(parts, rows):
    total = parts[0][rows, :].astype(F32)
    for p in parts[1:]:
        total = total + p[rows, :].astype(F32)
    return total


def output_kernel(sz, layer, sc, *refs):
    n = sz.head_axis
    parts, refs = refs[:n], refs[n:]
    resid = refs[0]
    res_o, low_o, mixed_o, square_o, sc_o = refs[-5:]
    for i in range(4):
        sc_o[i] = sc[i]
    extra = total_of(parts, slice(sz.rows, sz.rows + PAD))
    square = extra[0:8, :HALF] + extra[8:16, :HALF]
    square_o[...] = square
    inv = lax.rsqrt(square / sz.inner + EPS)
    for b in range(sz.blocks):
        rows = slice(b * HALF, (b + 1) * HALF)
        col = column_of(inv[b : b + 1, :], HALF)[:, 0:1]
        mixed = total_of(parts, rows) * col
        res = resid[rows, :].astype(F32) + mixed
        res_o[rows, :] = res
        low_o[rows, :] = res.astype(LOW)
        mixed_o[rows, :] = mixed


def input_kernel(sz, layer, sc, *refs):
    n = sz.head_axis
    parts, refs = refs[:n], refs[n:]
    resid, outg, inv_r, gains = refs[0], refs[1], refs[2], refs[3:5]
    refs = refs[5:]
    if layer == 1:
        mixed = refs[0]
        grad_o, low_o, sc_o = refs[-3:]
    else:
        one_low, one_heads = refs[0], refs[1 : 1 + n]
        low_o, swap_o, shared_o, sc_o = refs[-4:]
    for i in range(4):
        sc_o[i] = sc[i]
    c, h = sc[0], sc[1]
    first = c == 0
    mine = aligned(h * sz.chunk, sz.chunk)
    gain = pick(c == layer, gains[0][0:1, mine], gains[1][0:1, mine])
    extra = total_of(parts, slice(sz.rows, sz.rows + PAD))
    along = extra[0:8, :HALF] + extra[8:16, :HALF]
    tops, lows = [], []
    for b in range(sz.blocks):
        rows = slice(b * HALF, (b + 1) * HALF)
        at = b * BLOCK
        inv_row = pick(c == 0, inv_r[:, at : at + HALF], inv_r[:, at + HALF : at + BLOCK])
        inv = column_of(inv_row, HALF)[:, 0:1]
        share = column_of(along[b : b + 1, :] / sz.width, HALF)[:, 0:1]
        total = total_of(parts, rows)
        base = resid[rows, :].astype(F32)
        grad = outg[rows, :].astype(F32) + inv * (total * gain - base * (inv * share))
        low = grad.astype(LOW)
        low_o[rows, :] = low
        if layer == 0:
            swap_o[rows, :] = pick(first, one_low[rows, :], low)
        else:
            grad_o[rows, :] = grad
            dots = jnp.sum(low.astype(F32) * mixed[rows, :], axis=1, keepdims=True)
            row = jnp.transpose(jnp.broadcast_to(dots, (HALF, 128)))[0:1, :]
            high, rest = split_low(row)
            tops.append(high)
            lows.append(rest)
    if layer == 1:
        fill = [jnp.zeros((8 - sz.blocks, HALF), F32)] if sz.blocks < 8 else []
        extra = jnp.concatenate(tops + fill + lows + fill, axis=0)
        extra = jnp.concatenate([extra] * (sz.chunk // HALF), axis=1)
        low_o[sz.rows :, :] = extra.astype(LOW)
    else:
        size = shared_o.shape[0]
        at = sz.rows + PAD
        zero = total_of(parts, slice(at, at + size))
        one = total_of(one_heads, slice(None))
        zero, one = (jnp.concatenate([resplit(v[:PAD]), v[PAD:]], axis=0) for v in (zero, one))
        shared_o[...] = pick(first, zero, one)
        swap_o[sz.rows :, :] = pick(first, one, zero).astype(LOW)


def sum_kernel(sz, last, sc, *refs):
    if last:
        parts, done, outs = refs[:-3], refs[-3], refs[-2:]
    else:
        parts, outs = refs[:-1], refs[-1:]
    rows = outs[0].shape[0] - PAD
    total = total_of(parts, slice(None))
    extra = total[rows:]
    high, low = split_low(extra[0:4, :] + extra[4:8, :])
    extra = jnp.concatenate([high, low, jnp.zeros((PAD - 8, extra.shape[1]), F32)], axis=0)
    sums = jnp.concatenate([total[:rows], extra], axis=0).astype(LOW)
    if last:
        outs[0][...] = pick(sc[0] == 0, sums, done[...])
        outs[1][...] = pick(sc[0] == 0, done[...], sums)
    else:
        outs[0][...] = sums


def final_kernel(sz, seq, sc, own, got, *refs):
    pieces, refs = refs[:-9], refs[-9:]
    gate_o, inner_o, out_o, conv_o, norm_o, skip_o, shared_o, taps_o, gain_o = refs
    c = sc[0]
    ch = sz.channels
    rows = own.shape[0] - PAD
    lane = lax.broadcasted_iota(jnp.int32, skip_o.shape, 1)
    skip = jnp.zeros(skip_o.shape, F32)
    for i in range(2):
        which = pick(i == 0, c, 1 - c)
        to = aligned(which * ch, ch)
        sums = (own if i == 0 else got)[...].astype(F32)
        gate_o[:, to] = sums[:rows, :ch]
        inner_o[:, to] = sums[:rows, ch : 2 * ch]
        out_o[to, :] = jnp.transpose(sums[:rows, 2 * ch :])
        lines = sums[rows : rows + 4, :] + sums[rows + 4 : rows + 8, :]
        for j in range(sz.taps):
            conv_o[j : j + 1, to] = lines[j // 3 : j // 3 + 1, (j % 3) * ch : (j % 3 + 1) * ch]
        norm_o[:, to] = lines[1:2, ch : 2 * ch]
        skips = lines[1:2, 2 * ch :]
        for q in range(sz.heads):
            part = jnp.sum(per_head(skips, q, sz.head_width), axis=1, keepdims=True)
            skip = jnp.where(lane == which * sz.heads + q, part, skip)
    skip_o[...] = skip
    total = total_of(pieces, slice(BLOCK, None))
    shared_o[...] = total[PAD:]
    common = total[: PAD // 2] + total[PAD // 2 : PAD]
    place = sc[2] * sz.head_axis + sc[1]
    span = common.shape[1]
    size = span // (seq * sz.head_axis)
    turned = pltpu.roll(common, lax.rem(span - place * size, span), 1)
    taps_o[...] = turned[: sz.taps, :size]
    size = sz.width // (seq * sz.head_axis)
    at = place * size
    line = jnp.broadcast_to(line_of(common, sz.taps + at // span), common.shape)
    turned = pltpu.roll(line, lax.rem(span - lax.rem(at, span), span), 1)
    gain_o[...] = turned[:1, :size]


def slice_kernel(sz, slots, sc, order, tokens, rates, *refs):
    outs, sc_o, sems = refs[:slots], refs[slots], refs[slots + 1]
    copies = []
    for r in range(slots):
        rows = tokens.at[order[lax.rem(sc[3] + r, slots)], aligned(sc[0] * HALF, HALF), :]
        copies.append(pltpu.make_async_copy(rows, outs[r].at[:HALF], sems.at[r]))
    for copy in copies:
        copy.start()
    for i in range(4):
        sc_o[i] = sc[i]
    for r in range(slots):
        first, rest = split_low(rates[0, order[lax.rem(sc[3] + r, slots)]])
        second, rest = split_low(rest)
        lines = jnp.concatenate([first, second, rest, jnp.zeros_like(rest)], axis=1)
        lines = jnp.concatenate([lines, jnp.zeros_like(lines)], axis=0)
        outs[r][HALF:, :] = lines.astype(LOW)
    for copy in copies:
        copy.wait()


def rates_of(piece):
    lines = piece[HALF:, :].astype(F32)[:8, :]
    return (lines[:, :BLOCK] + lines[:, BLOCK : 2 * BLOCK]) + lines[:, 2 * BLOCK : 3 * BLOCK]


def pack_kernel(sz, sc, order, grads, gate, inner, out, in_gain, conv_i, conv_s, skip, norm, *refs):
    gate_o, inner_o, o_o, mine_o, send_o, sems = *refs[:5], refs[-1]
    c, h = sc[0], sc[1]
    ch = sz.channels
    outs = refs[5:-1]
    slices = []
    for r, to in enumerate(outs):
        rows = grads.at[order[lax.rem(sc[3] + r, len(outs))], aligned(c * HALF, HALF), :]
        slices.append(pltpu.make_async_copy(rows, to, sems.at[3 + r]))
    cols = aligned((1 - c) * ch, ch)
    rows = aligned((h * 2 + 1 - c) * ch, ch)
    copies = [
        pltpu.make_async_copy(gate.at[0, :, cols], gate_o, sems.at[0]),
        pltpu.make_async_copy(inner.at[0, :, cols], inner_o, sems.at[1]),
        pltpu.make_async_copy(out.at[0, rows, :], o_o, sems.at[2]),
        *slices,
    ]
    for copy in copies:
        copy.start()
    for which, ref in ((c, mine_o), (1 - c, send_o)):
        at = aligned(which * ch, ch)
        ref[...] = jnp.zeros_like(ref)
        ref[0:1, :] = in_gain[...]
        ref[1 : 1 + sz.taps, :ch] = conv_i[0, :, at]
        ref[1 : 1 + sz.taps, ch : sz.lin] = conv_s[0]
        ref[5:6, :ch] = norm[:, at]
        low = spread(skip[...], 0, sz.heads, sz.head_width)
        high = spread(skip[...], sz.heads, sz.heads, sz.head_width)
        ref[6:7, :ch] = pick(which == 0, low, high)
    for copy in copies:
        copy.wait()


def decay_table(rate, c, n):
    lane = lax.broadcasted_iota(jnp.int32, rate.shape, 1)
    cum = rate
    step = 1
    while step < BLOCK:
        cum = cum + jnp.where(lane >= step, pltpu.roll(cum, step, 1), 0.0)
        step *= 2
    end = cum[:, BLOCK - 1 :]
    lines = [cum, jnp.exp(cum), jnp.exp(end - cum) * -rate, jnp.log(-rate) - cum]
    low = jnp.concatenate([v[:n] for v in lines], axis=0)
    high = jnp.concatenate([v[n:] for v in lines], axis=0)
    return pick(c == 0, low, high)


def leave_kernel(sz, slots, riders, sc, zero_own, zero_other, one_own, one_other, *refs):
    c = sc[0]
    if riders:
        shared, refs = refs[0], refs[1:]
        total = shared[...] + one_other[sz.rows :, :].astype(F32)
        extra = resplit(total[:PAD])
        part = (total.shape[0] - PAD) // riders
    outs = refs[:slots]
    for i in range(4):
        refs[slots][i] = sc[i]
    for r in range(slots):
        rows = aligned(lax.rem(sc[3] + r, slots) * HALF, HALF)
        own = pick(c == 0, zero_own[rows, :], one_own[rows, :])
        other = pick(c == 0, zero_other[rows, :], one_other[rows, :])
        put_pair(outs[r], c, own, other)
        if riders:
            lines = [extra, total[PAD + r * part : PAD + (r + 1) * part]]
            outs[r][BLOCK:, :] = jnp.concatenate(lines, axis=0).astype(LOW)


def home_kernel(slots, sc, *refs):
    early, late, out, grad = refs[:slots], refs[slots : 2 * slots], refs[-3], refs[-2]
    for i in range(4):
        refs[-1][i] = sc[i]
    first = sc[0] == 0
    for r in range(slots):
        at = lax.rem(sc[3] - r + slots, slots)
        out[at] = pick(first, early[r][...], late[r][:BLOCK, :]).astype(F32)
        grad[at] = pick(first, late[r][:BLOCK, :], early[r][...]).astype(F32)


def whole(shape):
    return pl.BlockSpec(shape, lambda *_: (0,) * len(shape))


def per_device(
    tokens,
    slot_order,
    log_decay,
    grad_out,
    in_gain,
    w_gate,
    w_inner,
    w_shared,
    conv_inner,
    conv_shared,
    d_skip,
    norm_gain,
    w_out,
):
    slots = tokens.shape[0]
    span = tokens.shape[1]
    width = tokens.shape[2]
    seq = lax.axis_size("seq")
    head_axis = lax.axis_size("head")
    cores = lax.axis_size("section")
    spans = seq // slots
    c = lax.axis_index("section")
    z = lax.axis_index("seq")
    h = lax.axis_index("head")
    k = lax.rem(z, slots)
    inner_dev = w_gate.shape[2]
    channels = inner_dev // cores
    shared = w_shared.shape[2]
    heads_dev = d_skip.shape[1]
    taps = conv_inner.shape[1]
    sz = Sizes(
        slots * span // BLOCK,
        width,
        channels,
        heads_dev // cores,
        shared // 2,
        taps,
        head_axis,
        inner_dev * head_axis,
    )
    first = c == 0
    swap = [(0, 1), (1, 0)]
    nb, tok, rows, chunk = sz.blocks, sz.tokens, sz.rows, sz.chunk

    def cross(x):
        return lax.ppermute(x, "section", swap)

    def turn(x, r):
        pairs = [(i, i // slots * slots + (i % slots + r) % slots) for i in range(seq)]
        return lax.ppermute(x, "seq", pairs) if r else x

    def over_heads(x, d):
        return x if d == 0 else lax.ppermute(x, "head", [(i, i ^ d) for i in range(head_axis)])

    def next_span(x, way):
        pairs = [(i, i + way * slots) for i in range(seq) if 0 <= i + way * slots < seq]
        return lax.ppermute(x, "seq", pairs)

    def shape(dims, dtype):
        return jax.ShapeDtypeStruct(dims, dtype)

    prefetch = functools.partial(pltpu.PrefetchScalarGridSpec, num_scalar_prefetch=1)
    options = pltpu.CompilerParams(vmem_limit_bytes=VMEM_BYTES)
    from_hbm = pltpu.CompilerParams(vmem_limit_bytes=ALL_VMEM_BYTES)
    anywhere = pl.BlockSpec(memory_space=pl.ANY)
    smem = pl.BlockSpec(memory_space=pltpu.SMEM)
    vmem = pl.BlockSpec(memory_space=pltpu.VMEM)
    index_shape = shape((4,), jnp.int32)

    def cost(flops, moved):
        return pl.CostEstimate(flops=int(flops), bytes_accessed=int(moved), transcendentals=0)

    def to_members(pieces):
        return [turn(x, r) for r, x in enumerate(pieces)]

    sc = jnp.stack([c, h, z, k]).astype(jnp.int32)
    *tok_slices, sc = pl.pallas_call(
        functools.partial(slice_kernel, sz, slots),
        in_specs=[smem, smem, anywhere, vmem],
        out_specs=[vmem] * slots + [smem],
        out_shape=[shape((HALF + PAD, width), LOW)] * slots + [index_shape],
        scratch_shapes=[pltpu.SemaphoreType.DMA((slots,))],
        compiler_params=from_hbm,
    )(sc, slot_order, tokens, log_decay)
    tok_pieces = to_members(tok_slices)
    tok_others = [cross(x) for x in tok_pieces]

    wide = 2 * channels + shared
    gate_sent, inner_sent, o_sent, pv_mine, pv_sent, *out_slices = pl.pallas_call(
        functools.partial(pack_kernel, sz),
        in_specs=[smem, smem] + [anywhere] * 4 + [vmem] * 5,
        out_specs=[vmem] * (5 + slots),
        out_shape=[
            shape((width, channels), LOW),
            shape((width, channels), LOW),
            shape((channels, width), LOW),
            shape((16, width), F32),
            shape((16, width), F32),
        ]
        + [shape((HALF, width), LOW)] * slots,
        scratch_shapes=[pltpu.SemaphoreType.DMA((3 + slots,))],
        compiler_params=from_hbm,
    )(
        sc, slot_order, grad_out, w_gate, w_inner, w_out,
        in_gain, conv_inner, conv_shared, d_skip, norm_gain,
    )
    raw = [w_gate, w_inner, w_shared, w_out]
    sent = [cross(x) for x in (gate_sent, inner_sent, w_shared[0], o_sent)]
    gains = [pv_mine, cross(pv_sent)]

    def span_total(table):
        ends = table[: sz.heads, BLOCK - 1 :: BLOCK]
        return jnp.repeat(jnp.exp(jnp.sum(ends, axis=1)), sz.head_width)[:, None]

    parts_shape = shape((head_axis, rows + PAD, chunk), LOW)
    weight_specs = [anywhere] * 8
    wide_weights = pltpu.VMEM((width, wide), LOW)
    out_weights = pltpu.VMEM((channels, width), LOW)
    copy_sems = pltpu.SemaphoreType.DMA((4,))
    dense = 2 * tok * width * (wide + channels)

    def forward(layer, sc, sources):
        def at(b, _):
            return (b, 0)

        piece = pl.BlockSpec((HALF, chunk), at)
        table = pl.BlockSpec((16, BLOCK), lambda b, _: (0, b))
        if layer == 0:
            src_specs = [whole((HALF + PAD, width))] * (2 * slots)
            more_specs = [table, table]
            more_shapes = [shape((16, tok), F32)] * 2
        else:
            src_specs = [piece] * (2 * head_axis) + [whole((HALF, width))] * (2 * slots) + [table]
            more_specs = [pl.BlockSpec((BLOCK, width), at)]
            more_shapes = [shape((tok, width), LOW)]

        last = [] if layer == 0 else [turned[3]]

        def call(halo, begin):
            return pl.pallas_call(
                functools.partial(forward_kernel, sz, layer, slots),
                grid_spec=prefetch(
                    grid=(nb,),
                    in_specs=src_specs
                    + [whole((16, width)), whole((16, width))]
                    + weight_specs
                    + [whole((8, sz.lin)), whole((channels, sz.states))]
                    + [whole(x.shape) for x in last],
                    out_specs=[
                        pl.BlockSpec((BLOCK, width), at),
                        pl.BlockSpec((BLOCK, channels), at),
                        pl.BlockSpec((BLOCK, sz.lin), at),
                        pl.BlockSpec((BLOCK, channels), at),
                        pl.BlockSpec((1, channels, sz.states), lambda b, _: (b, 0, 0)),
                        pl.BlockSpec((1, BLOCK), lambda b, _: (0, b)),
                        pl.BlockSpec((2, BLOCK), lambda b, _: (0, b)),
                        pl.BlockSpec((BLOCK, channels), at),
                        whole((channels, sz.states)),
                        smem,
                        piece,
                    ]
                    + more_specs,
                    scratch_shapes=[
                        pltpu.VMEM((BLOCK, width), LOW),
                        pltpu.VMEM((BLOCK, width), LOW),
                        wide_weights,
                        pltpu.VMEM((BLOCK + 8, sz.lin), F32),
                        pltpu.VMEM((channels, sz.states), F32),
                        copy_sems,
                    ],
                ),
                out_shape=[
                    shape((tok, width), LOW),
                    shape((tok, channels), F32),
                    shape((tok, sz.lin), LOW),
                    shape((tok, channels), F32),
                    shape((nb, channels, sz.states), LOW),
                    shape((1, tok), F32),
                    shape((2, tok), F32),
                    shape((tok, channels), LOW),
                    shape((channels, sz.states), F32),
                    index_shape,
                    shape((rows, chunk), LOW),
                ]
                + more_shapes,
                compiler_params=options,
                cost_estimate=cost(6 * dense, 16e6),
            )(sc, *sources, *gains, *raw, *sent, halo, begin, *last)

        halo = jnp.zeros((8, sz.lin), F32)
        begin = jnp.zeros((channels, sz.states), F32)
        if spans == 1:
            return call(halo, begin), halo
        trial = call(halo, begin)
        halo = next_span(trial[2][tok - 8 :].astype(F32), 1)
        local = call(halo, begin)[8]
        total = span_total(trial[11] if layer == 0 else sources[-1])
        for _ in range(spans - 1):
            begin = next_span(total * begin + local, 1)
        return call(halo, begin), halo

    def backward(layer, sc, sources, saved, decays, halo, deps):
        def at(i, _):
            return (nb - 1 - i, 0)

        if layer == 0:
            src_specs = [whole(s.shape) for s in sources]
        else:
            stat = pl.BlockSpec((2, BLOCK), lambda i, _: (0, nb - 1 - i))
            src_specs = [pl.BlockSpec((BLOCK, width), at)] + [stat] * head_axis
        gl, lin, ssd, inc = saved
        mixed_spec = [pl.BlockSpec((BLOCK, width), at)] if layer == 0 else []
        mixed_shape = [shape((tok, width), LOW)] if layer == 0 else []

        def call(halo_grad, begin):
            return pl.pallas_call(
                functools.partial(backward_kernel, sz, layer, len(deps)),
                grid_spec=prefetch(
                    grid=(nb,),
                    in_specs=src_specs
                    + [
                        pl.BlockSpec((BLOCK, channels), at),
                        whole(lin.shape),
                        pl.BlockSpec((BLOCK, channels), at),
                        pl.BlockSpec((1, channels, sz.states), lambda i, _: (nb - 1 - i, 0, 0)),
                        pl.BlockSpec((16, BLOCK), lambda i, _: (0, nb - 1 - i)),
                        whole((16, width)),
                        whole((16, width)),
                        whole((width, channels)),
                        whole((8, sz.lin)),
                        whole((8, sz.lin)),
                        whole((channels, sz.states)),
                    ]
                    + [anywhere] * len(deps),
                    out_specs=[
                        pl.BlockSpec((BLOCK, wide), at),
                        pl.BlockSpec((BLOCK, channels), at),
                        whole((PAD, 3 * channels)),
                        whole((8, sz.lin)),
                        whole((channels, sz.states)),
                        whole((8, sz.lin)),
                        smem,
                    ]
                    + mixed_spec,
                    scratch_shapes=[
                        pltpu.VMEM((BLOCK, width), LOW),
                        pltpu.VMEM((BLOCK + 8, sz.lin), F32),
                        pltpu.VMEM((BLOCK + 8, sz.lin), F32),
                        pltpu.VMEM((channels, sz.states), F32),
                        pltpu.VMEM((PAD, HALF), F32),
                        pltpu.VMEM((8, sz.lin), F32),
                    ],
                ),
                out_shape=[
                    shape((tok, wide), LOW),
                    shape((tok, channels), LOW),
                    shape((PAD, 3 * channels), LOW),
                    shape((8, sz.lin), F32),
                    shape((channels, sz.states), F32),
                    shape((8, sz.lin), F32),
                    index_shape,
                ]
                + mixed_shape,
                compiler_params=options,
                cost_estimate=cost(8 * dense, 16e6),
            )(
                sc, *sources, gl, lin, ssd, inc, decays, *gains, turned[2 + layer],
                halo, halo_grad, begin, *deps,
            )

        halo_grad = jnp.zeros((8, sz.lin), F32)
        begin = jnp.zeros((channels, sz.states), F32)
        if spans == 1:
            return call(halo_grad, begin)
        local = call(halo_grad, begin)[4]
        for _ in range(spans - 1):
            begin = next_span(span_total(decays) * begin + local, -1)
        halo_grad = next_span(call(halo_grad, begin)[5], -1)
        return call(halo_grad, begin)

    def project(layer, sc, unit, stats, deps):
        return pl.pallas_call(
            functools.partial(project_kernel, sz, layer, len(deps)),
            in_specs=[smem, vmem, vmem] + weight_specs + [anywhere] * len(deps),
            out_specs=[vmem, vmem, smem],
            out_shape=[parts_shape, parts_shape, index_shape],
            scratch_shapes=[out_weights, copy_sems],
            compiler_params=options,
            cost_estimate=cost(dense / 4, 4e6),
        )(sc, unit, stats, *raw, *sent, *deps)

    def lift(layer, sc, cat, normed, small, deps):
        outs = pl.pallas_call(
            functools.partial(lift_kernel, sz, layer, len(deps)),
            in_specs=[smem] + [vmem] * 6 + [anywhere] * len(deps),
            out_specs=[vmem] * (1 + head_axis) + [smem, vmem],
            out_shape=[parts_shape]
            + [shape(parts_shape.shape[1:], LOW)] * head_axis
            + [index_shape, shape((PAD, chunk), LOW)],
            scratch_shapes=[pltpu.VMEM((8, width), F32)],
            compiler_params=options,
            cost_estimate=cost(dense, 8e6),
        )(sc, cat, normed, *gains, small, turned[layer], *deps)
        return outs[0], list(outs[1:-2]), outs[-2], outs[-1]

    def scatter(sc, keep, send, riders=(), deps=()):
        size = rows + PAD + sum(PAD + rider[1].shape[0] for rider in riders)
        flat = [x for rider in riders for x in rider]
        got = [cross(x) for x in (send if isinstance(send, list) else [send])]
        joined = pl.pallas_call(
            functools.partial(join_kernel, sz, len(got), len(riders), len(deps)),
            in_specs=[smem] + [vmem] * (1 + len(got) + len(flat)) + [anywhere] * len(deps),
            out_specs=[smem] + [vmem] * head_axis,
            out_shape=[index_shape, shape((size, chunk), F32)]
            + [shape((size, chunk), LOW)] * (head_axis - 1),
            compiler_params=options,
        )(sc, keep, *got, *flat, *deps)
        return [over_heads(joined[1 + d], d) for d in far_first(head_axis)], joined[0]

    def gather(low):
        own = [over_heads(low, d) for d in far_first(head_axis)]
        return own + [cross(x) for x in own]

    turned = pl.pallas_call(
        functools.partial(turn_kernel, sz),
        in_specs=[smem] + weight_specs,
        out_specs=[vmem] * 4,
        out_shape=[shape((wide, width), LOW)] * 2 + [shape((width, channels), LOW)] * 2,
        scratch_shapes=[wide_weights, out_weights, copy_sems],
        compiler_params=options,
        cost_estimate=cost(1e9, 8e6),
    )

    def section_output(layer, sc, parts, resid, deps=()):
        return pl.pallas_call(
            functools.partial(output_kernel, sz, layer),
            in_specs=[smem] + [vmem] * (head_axis + 1) + [anywhere] * len(deps),
            out_specs=[vmem] * 4 + [smem],
            out_shape=[
                shape((rows, chunk), F32),
                shape((rows, chunk), LOW),
                shape((rows, chunk), F32),
                shape((8, HALF), F32),
                index_shape,
            ],
            compiler_params=options,
        )(sc, *parts, resid, *deps)

    part = width // seq
    columns = 3 * channels
    share = part // head_axis
    shared_size = seq * share + PAD

    def section_input(layer, sc, parts, *others, deps=()):
        if layer == 0:
            outs = [
                shape((rows + PAD, chunk), LOW),
                shape((rows + shared_size, chunk), LOW),
                shape((shared_size, chunk), F32),
            ]
        else:
            outs = [shape((rows, chunk), F32), shape((rows + PAD, chunk), LOW)]
        return pl.pallas_call(
            functools.partial(input_kernel, sz, layer),
            in_specs=[smem] + [vmem] * (head_axis + len(others)) + [anywhere] * len(deps),
            out_specs=[vmem] * len(outs) + [smem],
            out_shape=outs + [index_shape],
            compiler_params=options,
        )(sc, *parts, *others, *deps)

    def weight_grads(sc, normed, cat, mixed, scaled, small, deps=(), common=None):
        more = [] if common is None else [common]
        size = seq * share + PAD * len(more)
        outs = pl.pallas_call(
            functools.partial(weights_kernel, sz, seq, len(deps), bool(more)),
            in_specs=[smem] + [vmem] * (5 + len(more)) + [anywhere] * len(deps),
            out_specs=[smem] + [vmem] * (seq + head_axis),
            out_shape=[index_shape]
            + [shape((part + PAD, columns), LOW)] * seq
            + [shape((size, shared), LOW)] * head_axis,
            scratch_shapes=[pltpu.VMEM((width, columns), LOW), pltpu.VMEM((width, shared), F32)],
            compiler_params=options,
            cost_estimate=cost(4 * dense, 12e6),
        )(sc, normed, cat, mixed, scaled, small, *more, *deps)
        return over_seq(outs[1 : 1 + seq]), outs[1 + seq :], outs[0]

    def shifted(x, r):
        return lax.ppermute(x, "seq", [(i, (i + r) % seq) for i in range(seq)]) if r else x

    def over_seq(chunks):
        return [shifted(x, r) for r, x in enumerate(chunks)]

    def leave(sc, *arrays, riders=0):
        size = BLOCK + (share + PAD if riders else 0)
        pieces = pl.pallas_call(
            functools.partial(leave_kernel, sz, slots, riders),
            in_specs=[smem] + [vmem] * len(arrays),
            out_specs=[vmem] * slots + [smem],
            out_shape=[shape((size, chunk), LOW)] * slots + [index_shape],
            compiler_params=options,
        )(sc, *arrays)
        return to_members(pieces[:slots]), pieces[slots]

    out_pieces = to_members(out_slices)
    fw0, halo0 = forward(0, sc, tok_pieces + tok_others)
    base0, decays = fw0[10], fw0[11:13]
    pr0 = project(0, fw0[9], fw0[7], fw0[6], [out_pieces[1], out_pieces[-1]])
    out_others = [cross(x) for x in out_pieces]
    parts, sc_join = scatter(sc, pr0[0], pr0[1])
    turned = turned(sc_join, *raw, *sent)
    res1, low1, mixed0, square0, unused = section_output(0, sc, parts, base0, turned)
    pieces1 = gather(low1)
    square_other = cross(square0)

    fw1, halo1 = forward(1, sc, pieces1 + out_pieces + out_others + [decays[1]])
    stat = fw1[6] + cross(fw1[6])
    stats = [stat] + [over_heads(stat, d) for d in range(1, head_axis)]
    pr1 = project(1, fw1[9], fw1[7], fw1[6], [])
    parts_out, sc_out = scatter(sc, pr1[0], pr1[1])
    bw1 = backward(1, sc_out, [fw1[11]] + stats, fw1[1:5], decays[1], halo1, [])
    lf1 = lift(1, bw1[6], bw1[0], fw1[0], bw1[3], parts_out[1:])
    weights1, heads1, sc_weights = weight_grads(
        lf1[2], fw1[0], bw1[0], fw1[11], bw1[1], bw1[2], common=lf1[3]
    )
    parts, sc_join = scatter(sc_weights, lf1[0], lf1[1])
    igrad1, glow1, sc_in = section_input(
        1, sc_join, parts, res1, fw1[10], fw1[5], *gains, mixed0,
        deps=[weights1[1], weights1[-1]],
    )
    piecesg = gather(glow1)

    heads1 = [over_heads(heads1[d], d) for d in far_first(head_axis)]

    early, unused = leave(sc_in, low1, pieces1[head_axis], glow1, piecesg[head_axis])
    bw0 = backward(
        0, sc, piecesg + [square0, square_other], fw0[1:5], decays[0], halo0,
        weights1[2:-1],
    )
    weights0, heads0, sc_weights = weight_grads(
        bw0[6], fw0[0], bw0[0], bw0[7], bw0[1], bw0[2], deps=early[1:],
    )
    lf0 = lift(0, sc_weights, bw0[0], fw0[0], bw0[3], heads1[1:])
    parts, sc_join = scatter(lf0[2], lf0[0], lf0[1], [[lf0[3], *heads0]], weights0[1:2])

    unused, low2, unused_mixed, unused_square, sc_out = section_output(1, sc_in, parts_out, res1)
    glow0, to_other, shared_own, sc_end = section_input(
        0, sc_out, parts, base0, igrad1, fw0[5], *gains, low2, *heads1,
        deps=weights0[2:],
    )
    got = cross(to_other)
    if spans == 1:
        late, sc_end = leave(sc_end, glow0, got, low2, got, shared_own, riders=seq)
        shared_parts = late
    else:
        late, sc_end = leave(sc_end, glow0, got, low2, got)
        total = shared_own + got[rows:].astype(F32)
        extra = resplit(total[:PAD])
        fill = jnp.zeros((BLOCK, shared), F32)
        chunks = [
            jnp.concatenate([fill, extra, total[PAD + r * share : PAD + (r + 1) * share]])
            for r in range(seq)
        ]
        shared_parts = over_seq([x.astype(LOW) for x in chunks])
    section_out, input_grad, unused = pl.pallas_call(
        functools.partial(home_kernel, slots),
        in_specs=[smem] + [vmem] * (2 * slots),
        out_specs=[vmem, vmem, smem],
        out_shape=[shape((slots, BLOCK, chunk), F32)] * 2 + [index_shape],
        compiler_params=options,
    )(sc, *early, *late)

    def summed(sc, pieces, *done):
        return pl.pallas_call(
            functools.partial(sum_kernel, sz, bool(done)),
            in_specs=[smem] + [vmem] * (len(pieces) + len(done)),
            out_shape=[shape((part + PAD, columns), LOW)] * (1 + len(done)),
            compiler_params=options,
        )(sc, *pieces, *done)

    own_sums, other_sums = summed(sc_end, weights0, *summed(sc_in, weights1))
    final = pl.pallas_call(
        functools.partial(final_kernel, sz, seq),
        in_specs=[smem] + [vmem] * (2 + seq),
        out_shape=[
            shape((part, inner_dev), F32),
            shape((part, inner_dev), F32),
            shape((inner_dev, part), F32),
            shape((taps, inner_dev), F32),
            shape((1, inner_dev), F32),
            shape((1, heads_dev), F32),
            shape((share, shared), F32),
            shape((taps, shared // (seq * head_axis)), F32),
            shape((1, width // (seq * head_axis)), F32),
        ],
        compiler_params=options,
    )(sc, own_sums, cross(other_sums), *shared_parts)
    return (
        section_out[None],
        input_grad[None],
        final[8],
        final[0][None],
        final[1][None],
        final[6][None],
        final[3][None],
        final[7][None],
        final[5],
        final[4],
        final[2][None],
    )


def solution(mesh):
    placed = (
        P(None, "seq", None),
        P(),
        P("section", None, "head", "seq"),
        P(None, "seq", None),
        P("section", None),
        P("section", None, "head"),
        P("section", None, "head"),
        P("section", None, None),
        P("section", None, "head"),
        P("section", None, None),
        P("section", "head"),
        P("section", "head"),
        P("section", None, None),
    )
    return jax.shard_map(
        per_device,
        mesh=mesh,
        in_specs=placed,
        out_specs=(
            P("section", None, "seq", "head"),
            P("section", None, "seq", "head"),
            P("section", ("seq", "head")),
            P("section", "seq", "head"),
            P("section", "seq", "head"),
            P("section", ("seq", "head"), None),
            P("section", None, "head"),
            P("section", None, ("seq", "head")),
            P("section", "head"),
            P("section", "head"),
            P("section", "head", "seq"),
        ),
        check_vma=False,
    )
```

```python
import functools

import jax
import jax.numpy as jnp
from jax import lax
from jax.experimental import pallas as pl
from jax.experimental.pallas import tpu as pltpu
from jax.sharding import PartitionSpec as P

BLOCK = 256
HALF = BLOCK // 2
PAD = 16
EPS = 1e-05
F32 = jnp.float32
LOW = jnp.bfloat16
HIDDEN = -1e30
NN = ((1,), (0,))
NT = ((1,), (1,))
TN = ((0,), (0,))
VMEM_BYTES = 50 * 1024 * 1024
ALL_VMEM_BYTES = 63 * 1024 * 1024


def dot(a, b, dims):
    return lax.dot_general(a, b, (dims, ((), ())), preferred_element_type=F32)


def aligned(start, size):
    return pl.ds(pl.multiple_of(start, size), size)


def spread(cols, first, count, width):
    rows = cols.shape[0]
    lane = lax.broadcasted_iota(jnp.int32, (rows, count * width), 1)
    out = jnp.broadcast_to(cols[:, first : first + 1], (rows, count * width))
    for h in range(1, count):
        out = jnp.where(lane >= h * width, cols[:, first + h : first + h + 1], out)
    return out


def per_head(array, h, width):
    lane = lax.broadcasted_iota(jnp.int32, array.shape, 1)
    inside = (lane >= h * width) & (lane < (h + 1) * width)
    return jnp.where(inside, array, jnp.zeros_like(array))


def split_low(value):
    high = value.astype(LOW).astype(F32)
    return high, value - high


def column_of(row, size):
    return jnp.transpose(jnp.broadcast_to(row, (128, size)))


def sigmoid(v):
    return 0.5 * jnp.tanh(0.5 * v) + 0.5


def pick(flag, a, b):
    return jnp.where(flag, a, b)


class Sizes:
    def __init__(self, blocks, width, channels, heads, states, taps, head_axis, inner):
        self.blocks = blocks
        self.width = width
        self.channels = channels
        self.heads = heads
        self.head_width = channels // heads
        self.states = states
        self.lin = channels + 2 * states
        self.taps = taps
        self.head_axis = head_axis
        self.chunk = width // head_axis
        self.rows = blocks * HALF
        self.tokens = blocks * BLOCK
        self.inner = inner


def weight_copies(sz, layer, c, h, given, dst, sems):
    ch = sz.channels
    cols = aligned(c * ch, ch)
    places = [dst.at[:, :ch], dst.at[:, ch : 2 * ch], dst.at[:, 2 * ch :]]
    own = [given[0].at[0, :, cols], given[1].at[0, :, cols], given[2].at[0]]
    return copies_for(layer, c, own, given[3:], places, sems)


def out_copies(sz, layer, c, h, given, dst, sems):
    rows = aligned((h * 2 + c) * sz.channels, sz.channels)
    return copies_for(layer, c, [given[0].at[0, rows, :]], given[1:], [dst], sems)


def copies_for(layer, c, own, sent, places, sems):
    both = []
    for flag, sources in ((c == layer, own), (c != layer, sent)):
        copies = [
            pltpu.make_async_copy(p, q, sems.at[i]) for i, (p, q) in enumerate(zip(sources, places))
        ]
        both.append((flag, copies))
    return both


def run_copies(choices, start, wait):
    for flag, copies in choices:

        @pl.when(flag)
        def _(copies=copies):
            if start:
                for copy in copies:
                    copy.start()
            if wait:
                for copy in copies:
                    copy.wait()


def put_ordered(sz, dst, c, k, b, own, other):
    for r in range(len(own)):

        @pl.when(lax.rem(k - b + len(own), len(own)) == r)
        def _(r=r):
            put_pair(dst, c, own[r][:HALF, :], other[r][:HALF, :])


def put_pair(dst, c, own, other):
    dst[aligned(c * HALF, HALF), :] = own
    dst[aligned((1 - c) * HALF, HALF), :] = other


def far_first(count):
    return [0] + list(range(count - 1, 0, -1))


def put_pieces(sz, dst, c, h, own, other):
    own, other = (dict(zip(far_first(sz.head_axis), side)) for side in (own, other))
    for d in range(sz.head_axis):
        cols = aligned((h ^ d) * sz.chunk, sz.chunk)
        dst[aligned(c * HALF, HALF), cols] = own[d]
        dst[aligned((1 - c) * HALF, HALF), cols] = other[d]


def line_of(table, at):
    line = lax.broadcasted_iota(jnp.int32, table.shape, 0)
    return jnp.sum(jnp.where(line == at, table, 0.0), axis=0, keepdims=True)


def conv_forward(sz, ext, taps):
    pre = taps[0:1] * ext[5 : 5 + BLOCK, :]
    for j in range(1, sz.taps):
        pre = pre + taps[j : j + 1] * ext[5 + j : 5 + j + BLOCK, :]
    return pre


def decay_of(sz, cols, rp, h, mask):
    rows = cols[:, h : h + 1] + rp[12 + h : 13 + h, :]
    return jnp.exp(jnp.where(mask, rows, HIDDEN))


def lower_mask():
    t = lax.broadcasted_iota(jnp.int32, (BLOCK, BLOCK), 0)
    s = lax.broadcasted_iota(jnp.int32, (BLOCK, BLOCK), 1)
    return t >= s


def forward_kernel(sz, layer, slots, sc, *refs):
    n = sz.head_axis
    sources = 2 * slots if layer == 0 else 2 * n + 2 * slots
    src, refs = refs[:sources], refs[sources:]
    if layer == 1:
        table, refs = refs[0], refs[1:]
    gains, given, halo, begin = refs[0:2], refs[2:8], refs[8], refs[9]
    refs = refs[10:]
    if layer == 1:
        ov, refs = refs[0], refs[1:]
    normed_o, gl_o, lin_o, ssd_o, inc_o, inv_o, part_o, unit_o, fin_o, sc_o, base_o = refs[:11]
    refs = refs[11:]
    if layer == 1:
        mixed_o, refs = refs[0], refs[1:]
    else:
        tables_o, refs = refs[0:2], refs[2:]
    xs, ms, wv, ext, state, sems = refs
    b = pl.program_id(0)
    c, h, k = sc[0], sc[1], sc[3]
    ch, st = sz.channels, sz.states
    copies = weight_copies(sz, layer, c, h, given, wv, sems)

    @pl.when(b == 0)
    def _():
        run_copies(copies, True, False)
        ext[0:8, :] = halo[...]
        state[...] = begin[...]
        for i in range(4):
            sc_o[i] = sc[i]

    mine = aligned(c * HALF, HALF)
    cols = aligned(h * sz.chunk, sz.chunk)
    if layer == 0:
        put_ordered(sz, xs, c, k, b, src[:slots], src[slots:])
        base_o[...] = xs[mine, cols]
        for r in range(slots):

            @pl.when(lax.rem(k - b + slots, slots) == r)
            def _(r=r):
                own = decay_table(rates_of(src[r]), c, sz.heads)
                other = decay_table(rates_of(src[slots + r]), c, sz.heads)
                tables_o[0][...] = pick(c == 0, own, other)
                tables_o[1][...] = pick(c == 0, other, own)

        rp = tables_o[0][...]
    else:
        put_pieces(sz, xs, c, h, [r[...] for r in src[:n]], [r[...] for r in src[n : 2 * n]])
        put_ordered(sz, ms, c, k, b, src[2 * n : 2 * n + slots], src[2 * n + slots :])
        base_o[...] = ms[mine, cols]
        mixed_o[...] = ms[...]
        rp = table[...]

    pv = pick(c == layer, gains[0][...], gains[1][...])
    x = xs[...].astype(F32)
    inv_in = lax.rsqrt(jnp.mean(x * x, axis=1, keepdims=True) + EPS)
    normed = (x * inv_in * pv[0:1, : sz.width]).astype(LOW)
    normed_o[...] = normed

    @pl.when(b == 0)
    def _():
        run_copies(copies, False, True)

    proj = dot(normed, wv[...], NN)
    gl = proj[:, :ch]
    gl_o[...] = gl
    lin = proj[:, ch:].astype(LOW)
    lin_o[...] = lin
    ext[8 : 8 + BLOCK, :] = lin.astype(F32)
    pre = conv_forward(sz, ext, pv[1:5, : sz.lin])
    ext[0:8, :] = ext[BLOCK : BLOCK + 8, :]
    act = (pre * sigmoid(pre)).astype(LOW)
    values, bm, cm = act[:, :ch], act[:, ch : ch + st], act[:, ch + st :]

    cols = jnp.transpose(rp)
    mask = lower_mask()
    gram = dot(cm, bm, NT)
    mixes, parts = [], []
    for i in range(sz.heads):
        mixes.append((gram * decay_of(sz, cols, rp, i, mask)).astype(LOW))
        parts.append(per_head(values, i, sz.head_width))
    intra = dot(jnp.concatenate(mixes, axis=1), jnp.concatenate(parts, axis=0), NN)

    low_state = state[...].astype(LOW)
    inc_o[0] = low_state
    ecum = spread(cols, sz.heads, sz.heads, sz.head_width)
    inter = dot(cm, low_state, NT) * ecum
    vf = values.astype(F32)
    carried = (vf * spread(cols, 2 * sz.heads, sz.heads, sz.head_width)).astype(LOW)
    local = dot(carried, bm, TN)
    for i in range(sz.heads):
        rows = slice(i * sz.head_width, (i + 1) * sz.head_width)
        total = cols[BLOCK - 1 : BLOCK, sz.heads + i : sz.heads + i + 1]
        state[rows, :] = total * state[rows, :] + local[rows]
    ssd = intra + inter + pv[6:7, :ch] * vf
    ssd_o[...] = ssd
    gated = ssd * (gl * sigmoid(gl))
    weighty = gated * pv[5:6, :ch]
    unit_o[...] = weighty.astype(LOW)

    lane = lax.broadcasted_iota(jnp.int32, (BLOCK, 128), 1)
    square = jnp.sum(gated * gated, axis=1, keepdims=True)
    if layer == 0:
        project = jnp.zeros_like(square)
    else:
        scaled_grad = dot(ms[...], ov[...], NN)
        project = jnp.sum(scaled_grad * weighty, axis=1, keepdims=True)
    stats = jnp.where(lane == 0, square, jnp.where(lane == 1, project, inv_in))
    stats = jnp.transpose(stats)
    part_o[...] = stats[0:2, :]
    inv_o[...] = stats[2:3, :]

    @pl.when(b == sz.blocks - 1)
    def _():
        fin_o[...] = state[...]


def scalar_lines(sz, lines):
    fill = [jnp.zeros((8 - sz.blocks, HALF), F32)] if sz.blocks < 8 else []
    high, low = split_low(jnp.concatenate(lines + fill, axis=0))
    table = jnp.concatenate([high, low], axis=0).astype(LOW)
    return jnp.concatenate([table] * (sz.chunk // HALF), axis=1)


def own_rows(sz, ref, which):
    blocks = [ref[aligned(b * BLOCK + which * HALF, HALF), :] for b in range(sz.blocks)]
    return jnp.concatenate(blocks, axis=0)


def project_kernel(sz, layer, deps, sc, unit_r, stats_r, *refs):
    given, refs = refs[:2], refs[2 + deps :]
    keep, send, sc_o, weights, sems = refs
    c, h = sc[0], sc[1]
    copies = out_copies(sz, layer, c, h, given, weights, sems)
    run_copies(copies, True, False)
    for i in range(4):
        sc_o[i] = sc[i]
    sides = []
    for which, out in ((c, keep), (1 - c, send)):
        sides.append((out, own_rows(sz, unit_r, which)))
        lines = [
            stats_r[0:1, aligned(b * BLOCK + which * HALF, HALF)] for b in range(sz.blocks)
        ]
        table = scalar_lines(sz, lines)
        for d in range(sz.head_axis):
            out[d, sz.rows :, :] = table
    run_copies(copies, False, True)
    for out, rows in sides:
        for d in range(sz.head_axis):
            chunk = weights[:, aligned((h ^ d) * sz.chunk, sz.chunk)]
            out[d, : sz.rows, :] = dot(rows, chunk, NN).astype(LOW)


def turn_kernel(sz, sc, *refs):
    given, given_out, refs = refs[:6], refs[6:8], refs[8:]
    wide_o, out_o, wv, ov, sems = refs[:2], refs[2:4], refs[4], refs[5], refs[6]
    for layer in range(2):
        copies = weight_copies(sz, layer, sc[0], sc[1], given, wv, sems)
        run_copies(copies, True, True)
        copies = out_copies(sz, layer, sc[0], sc[1], given_out, ov, sems)
        run_copies(copies, True, True)
        wide_o[layer][...] = jnp.transpose(wv[...])
        out_o[layer][...] = jnp.transpose(ov[...])


def out_at(out, d):
    return out[d] if isinstance(out, tuple) else out.at[d]


def lift_kernel(sz, layer, deps, sc, cat_r, normed_r, zero_gains, one_gains, small_r, *refs):
    weights, refs = refs[0], refs[1 + deps :]
    keep, send, sc_o, common_o, wide = refs[0], refs[1:-3], *refs[-3:]
    c, h = sc[0], sc[1]
    for i in range(4):
        sc_o[i] = sc[i]
    wide[...] = jnp.zeros_like(wide)
    for which, out in ((c, keep), (1 - c, send)):
        rows = own_rows(sz, cat_r, which)
        along = jnp.zeros((sz.rows, 1), F32)
        for d in range(sz.head_axis):
            cols = aligned((h ^ d) * sz.chunk, sz.chunk)
            product = dot(rows, weights[:, cols], NN)
            out_at(out, d)[: sz.rows, :] = product.astype(LOW)
            blocks = [
                normed_r[aligned(b * BLOCK + which * HALF, HALF), cols] for b in range(sz.blocks)
            ]
            product = product * jnp.concatenate(blocks, axis=0).astype(F32)
            wide[0:1, cols] += jnp.sum(product, axis=0, keepdims=True)
            along = along + jnp.sum(product, axis=1, keepdims=True)
        lines = [
            jnp.transpose(jnp.broadcast_to(along[b * HALF : (b + 1) * HALF], (HALF, 128)))[0:1, :]
            for b in range(sz.blocks)
        ]
        table = scalar_lines(sz, lines)
        for d in range(sz.head_axis):
            out_at(out, d)[sz.rows :, :] = table
    gain_grad = wide[0:1, :] / pick(c == layer, zero_gains[0:1, :], one_gains[0:1, :])
    flat = [small_r[j : j + 1, sz.channels :] for j in range(sz.taps)]
    flat += [gain_grad[:, q * sz.chunk : (q + 1) * sz.chunk] for q in range(sz.head_axis)]
    high, low = split_low(jnp.concatenate(flat, axis=0))
    common_o[...] = jnp.concatenate([high, low], axis=0).astype(LOW)


def backward_kernel(sz, layer, deps, sc, *refs):
    n = sz.head_axis
    sources = 2 * n + 2 if layer == 0 else 1 + n
    src, refs = refs[:sources], refs[sources:]
    gl_r, lin_r, ssd_r, inc_r = refs[:4]
    table, gains, ov = refs[4], refs[5:7], refs[7]
    halo, halo_grad, begin = refs[8:11]
    refs = refs[11 + deps :]
    cat_o, scaled_o, small_o, sums_o, fin_o, rim_o, sc_o = refs[:7]
    refs = refs[7:]
    if layer == 0:
        mixed_o, refs = refs[0], refs[1:]
    ms, ext, back, state, heads_p, small = refs
    i_step = pl.program_id(0)
    b = sz.blocks - 1 - i_step
    c, h = sc[0], sc[1]
    ch, st = sz.channels, sz.states
    pv = pick(c == layer, gains[0][...], gains[1][...])
    rp = table[...]

    @pl.when(i_step == 0)
    def _():
        back[BLOCK : BLOCK + 8, :] = halo_grad[...]
        state[...] = begin[...]
        small[...] = jnp.zeros_like(small)
        for i in range(4):
            sc_o[i] = sc[i]
        if layer == 0:
            for i in range(2):
                extra = src[i * n][sz.rows :, :].astype(F32)
                for d in range(1, n):
                    extra = extra + src[i * n + d][sz.rows :, :].astype(F32)
                heads_p[8 * i : 8 * i + 8, :] = extra[0:8, :HALF] + extra[8:16, :HALF]

    if layer == 0:
        rows = aligned(b * HALF, HALF)
        put_pieces(
            sz, ms, c, h, [r[rows, :] for r in src[:n]], [r[rows, :] for r in src[n : 2 * n]]
        )
        halves = []
        for k in range(2):
            alpha = lax.rsqrt(line_of(src[2 * n + k][...], b) / sz.inner + EPS)
            beta = alpha * alpha * line_of(heads_p[...], 8 * k + b) / sz.inner
            halves.append((alpha, beta))
        alpha, beta = (
            pick(
                c == 0,
                jnp.concatenate([halves[0][q], halves[1][q]], axis=1),
                jnp.concatenate([halves[1][q], halves[0][q]], axis=1),
            )
            for q in range(2)
        )
    else:
        stats = src[1][...]
        for d in range(1, n):
            stats = stats + src[1 + d][...]
        alpha = lax.rsqrt(stats[0:1, :] / sz.inner + EPS)
        beta = alpha * alpha * alpha * stats[1:2, :] / sz.inner

    sub = lax.broadcasted_iota(jnp.int32, rp.shape, 0)
    cols = jnp.transpose(jnp.where(sub == 12, alpha, jnp.where(sub == 13, beta, rp)))
    alpha, beta = cols[:, 12:13], cols[:, 13:14]

    gl = gl_r[...]
    ssd = ssd_r[...]
    sig = sigmoid(gl)
    swish = gl * sig
    slope = sig * (1.0 + gl * (1.0 - sig))
    gated = ssd * swish
    if layer == 0:
        mixed_grad = ms[...]
        mixed_o[...] = mixed_grad
    else:
        mixed_grad = src[0][...]
    scaled_grad = dot(mixed_grad, ov[...], NN)
    gain = pv[5:6, :ch]
    normal = gated * alpha
    small[4:5, :ch] += jnp.sum(scaled_grad * normal, axis=0, keepdims=True)
    scaled_o[...] = (normal * gain).astype(LOW)
    gated_grad = alpha * (scaled_grad * gain) - beta * gated
    ssd_grad = (gated_grad * swish).astype(LOW)
    gate_grad = (gated_grad * ssd * slope).astype(LOW)
    sgf = ssd_grad.astype(F32)

    before = lin_r[pl.ds(pl.multiple_of(jnp.maximum(b * BLOCK - 16, 0), 16), 16), :]
    ext[0:8, :] = pick(b > 0, before.astype(F32)[8:16, :], halo[...])
    ext[8 : 8 + BLOCK, :] = lin_r[aligned(b * BLOCK, BLOCK), :].astype(F32)
    taps = pv[1:5, : sz.lin]
    pre = conv_forward(sz, ext, taps)
    psig = sigmoid(pre)
    pact = pre * psig
    pslope = psig * (1.0 + pre * (1.0 - psig))
    act = pact.astype(LOW)
    values, bm, cm = act[:, :ch], act[:, ch : ch + st], act[:, ch + st :]
    vf = values.astype(F32)
    small[5:6, :ch] += jnp.sum(sgf * vf, axis=0, keepdims=True)

    mask = lower_mask()
    gram = dot(cm, bm, NT)
    gram_grad = jnp.zeros((BLOCK, BLOCK), F32)
    mixes, parts = [], []
    for i in range(sz.heads):
        decay = decay_of(sz, cols, rp, i, mask)
        mixes.append((gram * decay).astype(LOW))
        parts.append(per_head(ssd_grad, i, sz.head_width))
        gram_grad = gram_grad + dot(parts[-1], values, NT) * decay
    intra_grad = dot(jnp.concatenate(mixes, axis=0), jnp.concatenate(parts, axis=0), TN)

    ecum = spread(cols, sz.heads, sz.heads, sz.head_width)
    to_end = spread(cols, 2 * sz.heads, sz.heads, sz.head_width)
    inter_grad = (sgf * ecum).astype(LOW)
    low_state = state[...].astype(LOW)
    carried = (vf * to_end).astype(LOW)
    carried_grad = dot(bm, low_state, NT)
    gram_low = gram_grad.astype(LOW)
    b_grad = dot(gram_low, cm, TN) + dot(carried, low_state, NN)
    c_grad = dot(gram_low, bm, NN) + dot(inter_grad, inc_r[0], NN)
    value_grad = intra_grad + pv[6:7, :ch] * sgf + carried_grad * to_end
    entry = dot(inter_grad, cm, TN)
    for i in range(sz.heads):
        rows = slice(i * sz.head_width, (i + 1) * sz.head_width)
        total = cols[BLOCK - 1 : BLOCK, sz.heads + i : sz.heads + i + 1]
        state[rows, :] = total * state[rows, :] + entry[rows]

    pre_grad = jnp.concatenate([value_grad, b_grad, c_grad], axis=1) * pslope
    back[0:BLOCK, :] = pre_grad
    lin_grad = taps[0:1] * back[sz.taps - 1 : sz.taps - 1 + BLOCK, :]
    for j in range(1, sz.taps):
        at = sz.taps - 1 - j
        lin_grad = lin_grad + taps[j : j + 1] * back[at : at + BLOCK, :]
    for j in range(sz.taps):
        small[j : j + 1, :] += jnp.sum(pre_grad * ext[5 + j : 5 + j + BLOCK, :], axis=0, keepdims=True)
    back[BLOCK : BLOCK + 8, :] = back[0:8, :]
    cat_o[...] = jnp.concatenate([gate_grad, lin_grad.astype(LOW)], axis=1)

    @pl.when(i_step == sz.blocks - 1)
    def _():
        fin_o[...] = state[...]
        rim_o[...] = back[0:8, :]
        sums = small[...]
        flat = [sums[j : j + 1, :ch] for j in range(sz.taps + 2)]
        flat = [jnp.concatenate(flat[j : j + 3], axis=1) for j in range(0, len(flat), 3)]
        flat = flat + [jnp.zeros_like(flat[0])] * (4 - len(flat))
        high, low = split_low(jnp.concatenate(flat, axis=0))
        rest = jnp.zeros((PAD - 8, high.shape[1]), F32)
        small_o[...] = jnp.concatenate([high, low, rest], axis=0).astype(LOW)
        sums_o[...] = sums


def weights_kernel(sz, seq, deps, with_common, sc, normed, cat, mixed, scaled, small, *refs):
    if with_common:
        common, refs = refs[0], refs[1:]
    refs = refs[deps:]
    sc_o, outs, heads, full, wide = refs[0], refs[1 : seq + 1], refs[seq + 1 : -2], refs[-2], refs[-1]
    for i in range(4):
        sc_o[i] = sc[i]
    ch, st = sz.channels, sz.states
    step = sz.chunk
    for q in range(sz.head_axis):
        at = slice(q * step, (q + 1) * step)
        grads = dot(normed[:, at], cat[...], TN)
        full[at, : 2 * ch] = grads[:, : 2 * ch].astype(LOW)
        wide[at, :] = grads[:, 2 * ch :]
        full[at, 2 * ch :] = dot(mixed[:, at], scaled[...], TN).astype(LOW)
    rows = sz.width // seq
    part = rows // sz.head_axis
    for r, out in enumerate(outs):
        out[:rows, :] = full[aligned(lax.rem(sc[2] + r, seq) * rows, rows), :]
        out[rows:, :] = small[...]
    for d, out in enumerate(heads):
        lines = [
            wide[aligned(lax.rem(sc[2] + r, seq) * rows + (sc[1] ^ d) * part, part), :]
            for r in range(seq)
        ]
        if with_common:
            lines = [common[...].astype(F32)] + lines
        out[...] = jnp.concatenate(lines, axis=0).astype(LOW)


def resplit(extra):
    half = extra.shape[0] // 2
    high, low = split_low(extra[:half, :] + extra[half:, :])
    return jnp.concatenate([high, low], axis=0)


def join_kernel(sz, parts, riders, deps, sc, keep, *refs):
    n = sz.head_axis
    recv, refs = refs[0] if parts == 1 else refs[:parts], refs[parts:]
    more = [(refs[i * (n + 1)], refs[i * (n + 1) + 1 : (i + 1) * (n + 1)]) for i in range(riders)]
    refs = refs[riders * (n + 1) + deps :]
    sc_o, outs = refs[0], refs[1:]
    rows = sz.rows
    for i in range(4):
        sc_o[i] = sc[i]
    extra = resplit(keep[0, rows:, :].astype(F32) + out_at(recv, 0)[rows:, :].astype(F32))
    for d, out in enumerate(outs):
        both = keep[d, :rows, :].astype(F32) + out_at(recv, d)[:rows, :].astype(F32)
        out[:rows, :] = both.astype(out.dtype)
        out[rows : rows + PAD, :] = extra.astype(out.dtype)
        at = rows + PAD
        for common, rider in more:
            size = rider[d].shape[0]
            out[at : at + PAD, :] = common[...].astype(out.dtype)
            out[at + PAD : at + PAD + size, :] = rider[d][...].astype(out.dtype)
            at += PAD + size


def total_of(parts, rows):
    total = parts[0][rows, :].astype(F32)
    for p in parts[1:]:
        total = total + p[rows, :].astype(F32)
    return total


def output_kernel(sz, layer, sc, *refs):
    n = sz.head_axis
    parts, refs = refs[:n], refs[n:]
    resid = refs[0]
    res_o, low_o, mixed_o, square_o, sc_o = refs[-5:]
    for i in range(4):
        sc_o[i] = sc[i]
    extra = total_of(parts, slice(sz.rows, sz.rows + PAD))
    square = extra[0:8, :HALF] + extra[8:16, :HALF]
    square_o[...] = square
    inv = lax.rsqrt(square / sz.inner + EPS)
    for b in range(sz.blocks):
        rows = slice(b * HALF, (b + 1) * HALF)
        col = column_of(inv[b : b + 1, :], HALF)[:, 0:1]
        mixed = total_of(parts, rows) * col
        res = resid[rows, :].astype(F32) + mixed
        res_o[rows, :] = res
        low_o[rows, :] = res.astype(LOW)
        mixed_o[rows, :] = mixed


def input_kernel(sz, layer, sc, *refs):
    n = sz.head_axis
    parts, refs = refs[:n], refs[n:]
    resid, outg, inv_r, gains = refs[0], refs[1], refs[2], refs[3:5]
    refs = refs[5:]
    if layer == 1:
        mixed = refs[0]
        grad_o, low_o, sc_o = refs[-3:]
    else:
        one_low, one_heads = refs[0], refs[1 : 1 + n]
        low_o, swap_o, shared_o, sc_o = refs[-4:]
    for i in range(4):
        sc_o[i] = sc[i]
    c, h = sc[0], sc[1]
    first = c == 0
    mine = aligned(h * sz.chunk, sz.chunk)
    gain = pick(c == layer, gains[0][0:1, mine], gains[1][0:1, mine])
    extra = total_of(parts, slice(sz.rows, sz.rows + PAD))
    along = extra[0:8, :HALF] + extra[8:16, :HALF]
    tops, lows = [], []
    for b in range(sz.blocks):
        rows = slice(b * HALF, (b + 1) * HALF)
        at = b * BLOCK
        inv_row = pick(c == 0, inv_r[:, at : at + HALF], inv_r[:, at + HALF : at + BLOCK])
        inv = column_of(inv_row, HALF)[:, 0:1]
        share = column_of(along[b : b + 1, :] / sz.width, HALF)[:, 0:1]
        total = total_of(parts, rows)
        base = resid[rows, :].astype(F32)
        grad = outg[rows, :].astype(F32) + inv * (total * gain - base * (inv * share))
        low = grad.astype(LOW)
        low_o[rows, :] = low
        if layer == 0:
            swap_o[rows, :] = pick(first, one_low[rows, :], low)
        else:
            grad_o[rows, :] = grad
            dots = jnp.sum(low.astype(F32) * mixed[rows, :], axis=1, keepdims=True)
            row = jnp.transpose(jnp.broadcast_to(dots, (HALF, 128)))[0:1, :]
            high, rest = split_low(row)
            tops.append(high)
            lows.append(rest)
    if layer == 1:
        fill = [jnp.zeros((8 - sz.blocks, HALF), F32)] if sz.blocks < 8 else []
        extra = jnp.concatenate(tops + fill + lows + fill, axis=0)
        extra = jnp.concatenate([extra] * (sz.chunk // HALF), axis=1)
        low_o[sz.rows :, :] = extra.astype(LOW)
    else:
        size = shared_o.shape[0]
        at = sz.rows + PAD
        zero = total_of(parts, slice(at, at + size))
        one = total_of(one_heads, slice(None))
        zero, one = (jnp.concatenate([resplit(v[:PAD]), v[PAD:]], axis=0) for v in (zero, one))
        shared_o[...] = pick(first, zero, one)
        swap_o[sz.rows :, :] = pick(first, one, zero).astype(LOW)


def sum_kernel(sz, last, sc, *refs):
    if last:
        parts, done, outs = refs[:-3], refs[-3], refs[-2:]
    else:
        parts, outs = refs[:-1], refs[-1:]
    rows = outs[0].shape[0] - PAD
    total = total_of(parts, slice(None))
    extra = total[rows:]
    high, low = split_low(extra[0:4, :] + extra[4:8, :])
    extra = jnp.concatenate([high, low, jnp.zeros((PAD - 8, extra.shape[1]), F32)], axis=0)
    sums = jnp.concatenate([total[:rows], extra], axis=0).astype(LOW)
    if last:
        outs[0][...] = pick(sc[0] == 0, sums, done[...])
        outs[1][...] = pick(sc[0] == 0, done[...], sums)
    else:
        outs[0][...] = sums


def final_kernel(sz, sc, own, got, *refs):
    gate_o, inner_o, out_o, conv_o, norm_o, skip_o = refs
    c = sc[0]
    ch = sz.channels
    rows = own.shape[0] - PAD
    lane = lax.broadcasted_iota(jnp.int32, skip_o.shape, 1)
    skip = jnp.zeros(skip_o.shape, F32)
    for i in range(2):
        which = pick(i == 0, c, 1 - c)
        to = aligned(which * ch, ch)
        sums = (own if i == 0 else got)[...].astype(F32)
        gate_o[:, to] = sums[:rows, :ch]
        inner_o[:, to] = sums[:rows, ch : 2 * ch]
        out_o[to, :] = jnp.transpose(sums[:rows, 2 * ch :])
        lines = sums[rows : rows + 4, :] + sums[rows + 4 : rows + 8, :]
        for j in range(sz.taps):
            conv_o[j : j + 1, to] = lines[j // 3 : j // 3 + 1, (j % 3) * ch : (j % 3 + 1) * ch]
        norm_o[:, to] = lines[1:2, ch : 2 * ch]
        skips = lines[1:2, 2 * ch :]
        for q in range(sz.heads):
            part = jnp.sum(per_head(skips, q, sz.head_width), axis=1, keepdims=True)
            skip = jnp.where(lane == which * sz.heads + q, part, skip)
    skip_o[...] = skip
def shared_kernel(sz, seq, sc, *refs):
    pieces, shared_o, taps_o, gain_o = refs[:-3], *refs[-3:]
    total = total_of(pieces, slice(BLOCK, None))
    shared_o[...] = total[PAD:]
    common = total[: PAD // 2] + total[PAD // 2 : PAD]
    place = sc[2] * sz.head_axis + sc[1]
    span = common.shape[1]
    size = span // (seq * sz.head_axis)
    turned = pltpu.roll(common, lax.rem(span - place * size, span), 1)
    taps_o[...] = turned[: sz.taps, :size]
    size = sz.width // (seq * sz.head_axis)
    at = place * size
    line = jnp.broadcast_to(line_of(common, sz.taps + at // span), common.shape)
    turned = pltpu.roll(line, lax.rem(span - lax.rem(at, span), span), 1)
    gain_o[...] = turned[:1, :size]


def slice_kernel(sz, slots, sc, order, tokens, rates, *refs):
    outs, sc_o, sems = refs[:slots], refs[slots], refs[slots + 1]
    copies = []
    for r in range(slots):
        rows = tokens.at[order[lax.rem(sc[3] + r, slots)], aligned(sc[0] * HALF, HALF), :]
        copies.append(pltpu.make_async_copy(rows, outs[r].at[:HALF], sems.at[r]))
    for copy in copies:
        copy.start()
    for i in range(4):
        sc_o[i] = sc[i]
    for r in range(slots):
        first, rest = split_low(rates[0, order[lax.rem(sc[3] + r, slots)]])
        second, rest = split_low(rest)
        lines = jnp.concatenate([first, second, rest, jnp.zeros_like(rest)], axis=1)
        lines = jnp.concatenate([lines, jnp.zeros_like(lines)], axis=0)
        outs[r][HALF:, :] = lines.astype(LOW)
    for copy in copies:
        copy.wait()


def rates_of(piece):
    lines = piece[HALF:, :].astype(F32)[:8, :]
    return (lines[:, :BLOCK] + lines[:, BLOCK : 2 * BLOCK]) + lines[:, 2 * BLOCK : 3 * BLOCK]


def pack_kernel(sz, sc, order, grads, gate, inner, out, in_gain, conv_i, conv_s, skip, norm, *refs):
    gate_o, inner_o, o_o, mine_o, send_o, sems = *refs[:5], refs[-1]
    c, h = sc[0], sc[1]
    ch = sz.channels
    outs = refs[5:-1]
    slices = []
    for r, to in enumerate(outs):
        rows = grads.at[order[lax.rem(sc[3] + r, len(outs))], aligned(c * HALF, HALF), :]
        slices.append(pltpu.make_async_copy(rows, to, sems.at[3 + r]))
    cols = aligned((1 - c) * ch, ch)
    rows = aligned((h * 2 + 1 - c) * ch, ch)
    copies = [
        pltpu.make_async_copy(gate.at[0, :, cols], gate_o, sems.at[0]),
        pltpu.make_async_copy(inner.at[0, :, cols], inner_o, sems.at[1]),
        pltpu.make_async_copy(out.at[0, rows, :], o_o, sems.at[2]),
        *slices,
    ]
    for copy in copies:
        copy.start()
    for which, ref in ((c, mine_o), (1 - c, send_o)):
        at = aligned(which * ch, ch)
        ref[...] = jnp.zeros_like(ref)
        ref[0:1, :] = in_gain[...]
        ref[1 : 1 + sz.taps, :ch] = conv_i[0, :, at]
        ref[1 : 1 + sz.taps, ch : sz.lin] = conv_s[0]
        ref[5:6, :ch] = norm[:, at]
        low = spread(skip[...], 0, sz.heads, sz.head_width)
        high = spread(skip[...], sz.heads, sz.heads, sz.head_width)
        ref[6:7, :ch] = pick(which == 0, low, high)
    for copy in copies:
        copy.wait()


def decay_table(rate, c, n):
    lane = lax.broadcasted_iota(jnp.int32, rate.shape, 1)
    cum = rate
    step = 1
    while step < BLOCK:
        cum = cum + jnp.where(lane >= step, pltpu.roll(cum, step, 1), 0.0)
        step *= 2
    end = cum[:, BLOCK - 1 :]
    lines = [cum, jnp.exp(cum), jnp.exp(end - cum) * -rate, jnp.log(-rate) - cum]
    low = jnp.concatenate([v[:n] for v in lines], axis=0)
    high = jnp.concatenate([v[n:] for v in lines], axis=0)
    return pick(c == 0, low, high)


def leave_kernel(sz, slots, riders, sc, zero_own, zero_other, one_own, one_other, *refs):
    c = sc[0]
    if riders:
        shared, refs = refs[0], refs[1:]
        total = shared[...] + one_other[sz.rows :, :].astype(F32)
        extra = resplit(total[:PAD])
        part = (total.shape[0] - PAD) // riders
    outs = refs[:slots]
    for i in range(4):
        refs[slots][i] = sc[i]
    for r in range(slots):
        rows = aligned(lax.rem(sc[3] + r, slots) * HALF, HALF)
        own = pick(c == 0, zero_own[rows, :], one_own[rows, :])
        other = pick(c == 0, zero_other[rows, :], one_other[rows, :])
        put_pair(outs[r], c, own, other)
        if riders:
            lines = [extra, total[PAD + r * part : PAD + (r + 1) * part]]
            outs[r][BLOCK:, :] = jnp.concatenate(lines, axis=0).astype(LOW)


def home_kernel(slots, sc, *refs):
    early, late, out, grad = refs[:slots], refs[slots : 2 * slots], refs[-3], refs[-2]
    for i in range(4):
        refs[-1][i] = sc[i]
    first = sc[0] == 0
    for r in range(slots):
        at = lax.rem(sc[3] - r + slots, slots)
        out[at] = pick(first, early[r][...], late[r][:BLOCK, :]).astype(F32)
        grad[at] = pick(first, late[r][:BLOCK, :], early[r][...]).astype(F32)


def whole(shape):
    return pl.BlockSpec(shape, lambda *_: (0,) * len(shape))


def per_device(
    tokens,
    slot_order,
    log_decay,
    grad_out,
    in_gain,
    w_gate,
    w_inner,
    w_shared,
    conv_inner,
    conv_shared,
    d_skip,
    norm_gain,
    w_out,
):
    slots = tokens.shape[0]
    span = tokens.shape[1]
    width = tokens.shape[2]
    seq = lax.axis_size("seq")
    head_axis = lax.axis_size("head")
    cores = lax.axis_size("section")
    spans = seq // slots
    c = lax.axis_index("section")
    z = lax.axis_index("seq")
    h = lax.axis_index("head")
    k = lax.rem(z, slots)
    inner_dev = w_gate.shape[2]
    channels = inner_dev // cores
    shared = w_shared.shape[2]
    heads_dev = d_skip.shape[1]
    taps = conv_inner.shape[1]
    sz = Sizes(
        slots * span // BLOCK,
        width,
        channels,
        heads_dev // cores,
        shared // 2,
        taps,
        head_axis,
        inner_dev * head_axis,
    )
    first = c == 0
    swap = [(0, 1), (1, 0)]
    nb, tok, rows, chunk = sz.blocks, sz.tokens, sz.rows, sz.chunk

    def cross(x):
        return lax.ppermute(x, "section", swap)

    def turn(x, r):
        pairs = [(i, i // slots * slots + (i % slots + r) % slots) for i in range(seq)]
        return lax.ppermute(x, "seq", pairs) if r else x

    def over_heads(x, d):
        return x if d == 0 else lax.ppermute(x, "head", [(i, i ^ d) for i in range(head_axis)])

    def next_span(x, way):
        pairs = [(i, i + way * slots) for i in range(seq) if 0 <= i + way * slots < seq]
        return lax.ppermute(x, "seq", pairs)

    def shape(dims, dtype):
        return jax.ShapeDtypeStruct(dims, dtype)

    prefetch = functools.partial(pltpu.PrefetchScalarGridSpec, num_scalar_prefetch=1)
    options = pltpu.CompilerParams(vmem_limit_bytes=VMEM_BYTES)
    from_hbm = pltpu.CompilerParams(vmem_limit_bytes=ALL_VMEM_BYTES)
    anywhere = pl.BlockSpec(memory_space=pl.ANY)
    smem = pl.BlockSpec(memory_space=pltpu.SMEM)
    vmem = pl.BlockSpec(memory_space=pltpu.VMEM)
    index_shape = shape((4,), jnp.int32)

    def cost(flops, moved):
        return pl.CostEstimate(flops=int(flops), bytes_accessed=int(moved), transcendentals=0)

    def to_members(pieces):
        return [turn(x, r) for r, x in enumerate(pieces)]

    sc = jnp.stack([c, h, z, k]).astype(jnp.int32)
    *tok_slices, sc = pl.pallas_call(
        functools.partial(slice_kernel, sz, slots),
        in_specs=[smem, smem, anywhere, vmem],
        out_specs=[vmem] * slots + [smem],
        out_shape=[shape((HALF + PAD, width), LOW)] * slots + [index_shape],
        scratch_shapes=[pltpu.SemaphoreType.DMA((slots,))],
        compiler_params=from_hbm,
    )(sc, slot_order, tokens, log_decay)
    tok_pieces = to_members(tok_slices)
    tok_others = [cross(x) for x in tok_pieces]

    wide = 2 * channels + shared
    gate_sent, inner_sent, o_sent, pv_mine, pv_sent, *out_slices = pl.pallas_call(
        functools.partial(pack_kernel, sz),
        in_specs=[smem, smem] + [anywhere] * 4 + [vmem] * 5,
        out_specs=[vmem] * (5 + slots),
        out_shape=[
            shape((width, channels), LOW),
            shape((width, channels), LOW),
            shape((channels, width), LOW),
            shape((16, width), F32),
            shape((16, width), F32),
        ]
        + [shape((HALF, width), LOW)] * slots,
        scratch_shapes=[pltpu.SemaphoreType.DMA((3 + slots,))],
        compiler_params=from_hbm,
    )(
        sc, slot_order, grad_out, w_gate, w_inner, w_out,
        in_gain, conv_inner, conv_shared, d_skip, norm_gain,
    )
    sent = [cross(x) for x in (gate_sent, inner_sent, w_shared[0], o_sent)]
    gains = [pv_mine, cross(pv_sent)]

    def span_total(table):
        ends = table[: sz.heads, BLOCK - 1 :: BLOCK]
        return jnp.repeat(jnp.exp(jnp.sum(ends, axis=1)), sz.head_width)[:, None]

    parts_shape = shape((head_axis, rows + PAD, chunk), LOW)
    in_weights = [w_gate, w_inner, w_shared, *sent[:3]]
    last_weights = [w_out, sent[3]]
    wide_weights = pltpu.VMEM((width, wide), LOW)
    out_weights = pltpu.VMEM((channels, width), LOW)
    copy_sems = pltpu.SemaphoreType.DMA((4,))
    dense = 2 * tok * width * (wide + channels)

    def forward(layer, sc, sources):
        def at(b, _):
            return (b, 0)

        piece = pl.BlockSpec((HALF, chunk), at)
        table = pl.BlockSpec((16, BLOCK), lambda b, _: (0, b))
        if layer == 0:
            src_specs = [whole((HALF + PAD, width))] * (2 * slots)
            more_specs = [table, table]
            more_shapes = [shape((16, tok), F32)] * 2
        else:
            src_specs = [piece] * (2 * head_axis) + [whole((HALF, width))] * (2 * slots) + [table]
            more_specs = [pl.BlockSpec((BLOCK, width), at)]
            more_shapes = [shape((tok, width), LOW)]

        last = [] if layer == 0 else [turned[3]]

        def call(halo, begin):
            return pl.pallas_call(
                functools.partial(forward_kernel, sz, layer, slots),
                grid_spec=prefetch(
                    grid=(nb,),
                    in_specs=src_specs
                    + [whole((16, width)), whole((16, width))]
                    + [anywhere] * len(in_weights)
                    + [whole((8, sz.lin)), whole((channels, sz.states))]
                    + [whole(x.shape) for x in last],
                    out_specs=[
                        pl.BlockSpec((BLOCK, width), at),
                        pl.BlockSpec((BLOCK, channels), at),
                        pl.BlockSpec((BLOCK, sz.lin), at),
                        pl.BlockSpec((BLOCK, channels), at),
                        pl.BlockSpec((1, channels, sz.states), lambda b, _: (b, 0, 0)),
                        pl.BlockSpec((1, BLOCK), lambda b, _: (0, b)),
                        pl.BlockSpec((2, BLOCK), lambda b, _: (0, b)),
                        pl.BlockSpec((BLOCK, channels), at),
                        whole((channels, sz.states)),
                        smem,
                        piece,
                    ]
                    + more_specs,
                    scratch_shapes=[
                        pltpu.VMEM((BLOCK, width), LOW),
                        pltpu.VMEM((BLOCK, width), LOW),
                        wide_weights,
                        pltpu.VMEM((BLOCK + 8, sz.lin), F32),
                        pltpu.VMEM((channels, sz.states), F32),
                        copy_sems,
                    ],
                ),
                out_shape=[
                    shape((tok, width), LOW),
                    shape((tok, channels), F32),
                    shape((tok, sz.lin), LOW),
                    shape((tok, channels), F32),
                    shape((nb, channels, sz.states), LOW),
                    shape((1, tok), F32),
                    shape((2, tok), F32),
                    shape((tok, channels), LOW),
                    shape((channels, sz.states), F32),
                    index_shape,
                    shape((rows, chunk), LOW),
                ]
                + more_shapes,
                compiler_params=options,
                cost_estimate=cost(6 * dense, 16e6),
            )(sc, *sources, *gains, *in_weights, halo, begin, *last)

        halo = jnp.zeros((8, sz.lin), F32)
        begin = jnp.zeros((channels, sz.states), F32)
        if spans == 1:
            return call(halo, begin), halo
        trial = call(halo, begin)
        halo = next_span(trial[2][tok - 8 :].astype(F32), 1)
        local = call(halo, begin)[8]
        total = span_total(trial[11] if layer == 0 else sources[-1])
        for _ in range(spans - 1):
            begin = next_span(total * begin + local, 1)
        return call(halo, begin), halo

    def backward(layer, sc, sources, saved, decays, halo, deps):
        def at(i, _):
            return (nb - 1 - i, 0)

        if layer == 0:
            src_specs = [whole(s.shape) for s in sources]
        else:
            stat = pl.BlockSpec((2, BLOCK), lambda i, _: (0, nb - 1 - i))
            src_specs = [pl.BlockSpec((BLOCK, width), at)] + [stat] * head_axis
        gl, lin, ssd, inc = saved
        mixed_spec = [pl.BlockSpec((BLOCK, width), at)] if layer == 0 else []
        mixed_shape = [shape((tok, width), LOW)] if layer == 0 else []

        def call(halo_grad, begin):
            return pl.pallas_call(
                functools.partial(backward_kernel, sz, layer, len(deps)),
                grid_spec=prefetch(
                    grid=(nb,),
                    in_specs=src_specs
                    + [
                        pl.BlockSpec((BLOCK, channels), at),
                        whole(lin.shape),
                        pl.BlockSpec((BLOCK, channels), at),
                        pl.BlockSpec((1, channels, sz.states), lambda i, _: (nb - 1 - i, 0, 0)),
                        pl.BlockSpec((16, BLOCK), lambda i, _: (0, nb - 1 - i)),
                        whole((16, width)),
                        whole((16, width)),
                        whole((width, channels)),
                        whole((8, sz.lin)),
                        whole((8, sz.lin)),
                        whole((channels, sz.states)),
                    ]
                    + [anywhere] * len(deps),
                    out_specs=[
                        pl.BlockSpec((BLOCK, wide), at),
                        pl.BlockSpec((BLOCK, channels), at),
                        whole((PAD, 3 * channels)),
                        whole((8, sz.lin)),
                        whole((channels, sz.states)),
                        whole((8, sz.lin)),
                        smem,
                    ]
                    + mixed_spec,
                    scratch_shapes=[
                        pltpu.VMEM((BLOCK, width), LOW),
                        pltpu.VMEM((BLOCK + 8, sz.lin), F32),
                        pltpu.VMEM((BLOCK + 8, sz.lin), F32),
                        pltpu.VMEM((channels, sz.states), F32),
                        pltpu.VMEM((PAD, HALF), F32),
                        pltpu.VMEM((8, sz.lin), F32),
                    ],
                ),
                out_shape=[
                    shape((tok, wide), LOW),
                    shape((tok, channels), LOW),
                    shape((PAD, 3 * channels), LOW),
                    shape((8, sz.lin), F32),
                    shape((channels, sz.states), F32),
                    shape((8, sz.lin), F32),
                    index_shape,
                ]
                + mixed_shape,
                compiler_params=options,
                cost_estimate=cost(8 * dense, 16e6),
            )(
                sc, *sources, gl, lin, ssd, inc, decays, *gains, turned[2 + layer],
                halo, halo_grad, begin, *deps,
            )

        halo_grad = jnp.zeros((8, sz.lin), F32)
        begin = jnp.zeros((channels, sz.states), F32)
        if spans == 1:
            return call(halo_grad, begin)
        local = call(halo_grad, begin)[4]
        for _ in range(spans - 1):
            begin = next_span(span_total(decays) * begin + local, -1)
        halo_grad = next_span(call(halo_grad, begin)[5], -1)
        return call(halo_grad, begin)

    def project(layer, sc, unit, stats, deps):
        return pl.pallas_call(
            functools.partial(project_kernel, sz, layer, len(deps)),
            in_specs=[smem, vmem, vmem] + [anywhere] * (2 + len(deps)),
            out_specs=[vmem, vmem, smem],
            out_shape=[parts_shape, parts_shape, index_shape],
            scratch_shapes=[out_weights, copy_sems],
            compiler_params=options,
            cost_estimate=cost(dense / 4, 4e6),
        )(sc, unit, stats, *last_weights, *deps)

    def lift(layer, sc, cat, normed, small, deps):
        outs = pl.pallas_call(
            functools.partial(lift_kernel, sz, layer, len(deps)),
            in_specs=[smem] + [vmem] * 6 + [anywhere] * len(deps),
            out_specs=[vmem] * (1 + head_axis) + [smem, vmem],
            out_shape=[parts_shape]
            + [shape(parts_shape.shape[1:], LOW)] * head_axis
            + [index_shape, shape((PAD, chunk), LOW)],
            scratch_shapes=[pltpu.VMEM((8, width), F32)],
            compiler_params=options,
            cost_estimate=cost(dense, 8e6),
        )(sc, cat, normed, *gains, small, turned[layer], *deps)
        return outs[0], list(outs[1:-2]), outs[-2], outs[-1]

    def scatter(sc, keep, send, riders=(), deps=()):
        size = rows + PAD + sum(PAD + rider[1].shape[0] for rider in riders)
        flat = [x for rider in riders for x in rider]
        got = [cross(x) for x in (send if isinstance(send, list) else [send])]
        joined = pl.pallas_call(
            functools.partial(join_kernel, sz, len(got), len(riders), len(deps)),
            in_specs=[smem] + [vmem] * (1 + len(got) + len(flat)) + [anywhere] * len(deps),
            out_specs=[smem] + [vmem] * head_axis,
            out_shape=[index_shape, shape((size, chunk), F32)]
            + [shape((size, chunk), LOW)] * (head_axis - 1),
            compiler_params=options,
        )(sc, keep, *got, *flat, *deps)
        return [over_heads(joined[1 + d], d) for d in far_first(head_axis)], joined[0]

    def gather(low):
        own = [over_heads(low, d) for d in far_first(head_axis)]
        return own + [cross(x) for x in own]

    turned = pl.pallas_call(
        functools.partial(turn_kernel, sz),
        in_specs=[smem] + [anywhere] * 8,
        out_specs=[vmem] * 4,
        out_shape=[shape((wide, width), LOW)] * 2 + [shape((width, channels), LOW)] * 2,
        scratch_shapes=[wide_weights, out_weights, copy_sems],
        compiler_params=options,
        cost_estimate=cost(1e9, 8e6),
    )

    def section_output(layer, sc, parts, resid, deps=()):
        return pl.pallas_call(
            functools.partial(output_kernel, sz, layer),
            in_specs=[smem] + [vmem] * (head_axis + 1) + [anywhere] * len(deps),
            out_specs=[vmem] * 4 + [smem],
            out_shape=[
                shape((rows, chunk), F32),
                shape((rows, chunk), LOW),
                shape((rows, chunk), F32),
                shape((8, HALF), F32),
                index_shape,
            ],
            compiler_params=options,
        )(sc, *parts, resid, *deps)

    part = width // seq
    columns = 3 * channels
    share = part // head_axis
    shared_size = seq * share + PAD

    def section_input(layer, sc, parts, *others, deps=()):
        if layer == 0:
            outs = [
                shape((rows + PAD, chunk), LOW),
                shape((rows + shared_size, chunk), LOW),
                shape((shared_size, chunk), F32),
            ]
        else:
            outs = [shape((rows, chunk), F32), shape((rows + PAD, chunk), LOW)]
        return pl.pallas_call(
            functools.partial(input_kernel, sz, layer),
            in_specs=[smem] + [vmem] * (head_axis + len(others)) + [anywhere] * len(deps),
            out_specs=[vmem] * len(outs) + [smem],
            out_shape=outs + [index_shape],
            compiler_params=options,
        )(sc, *parts, *others, *deps)

    def weight_grads(sc, normed, cat, mixed, scaled, small, deps=(), common=None):
        more = [] if common is None else [common]
        size = seq * share + PAD * len(more)
        outs = pl.pallas_call(
            functools.partial(weights_kernel, sz, seq, len(deps), bool(more)),
            in_specs=[smem] + [vmem] * (5 + len(more)) + [anywhere] * len(deps),
            out_specs=[smem] + [vmem] * (seq + head_axis),
            out_shape=[index_shape]
            + [shape((part + PAD, columns), LOW)] * seq
            + [shape((size, shared), LOW)] * head_axis,
            scratch_shapes=[pltpu.VMEM((width, columns), LOW), pltpu.VMEM((width, shared), F32)],
            compiler_params=options,
            cost_estimate=cost(4 * dense, 12e6),
        )(sc, normed, cat, mixed, scaled, small, *more, *deps)
        return over_seq(outs[1 : 1 + seq]), outs[1 + seq :], outs[0]

    def shifted(x, r):
        return lax.ppermute(x, "seq", [(i, (i + r) % seq) for i in range(seq)]) if r else x

    def over_seq(chunks):
        return [shifted(x, r) for r, x in enumerate(chunks)]

    def leave(sc, *arrays, riders=0):
        size = BLOCK + (share + PAD if riders else 0)
        pieces = pl.pallas_call(
            functools.partial(leave_kernel, sz, slots, riders),
            in_specs=[smem] + [vmem] * len(arrays),
            out_specs=[vmem] * slots + [smem],
            out_shape=[shape((size, chunk), LOW)] * slots + [index_shape],
            compiler_params=options,
        )(sc, *arrays)
        return to_members(pieces[:slots]), pieces[slots]

    out_pieces = to_members(out_slices)
    fw0, halo0 = forward(0, sc, tok_pieces + tok_others)
    base0, decays = fw0[10], fw0[11:13]
    pr0 = project(0, fw0[9], fw0[7], fw0[6], [out_pieces[1], out_pieces[-1]])
    out_others = [cross(x) for x in out_pieces]
    parts, sc_join = scatter(sc, pr0[0], pr0[1])
    turned = turned(sc_join, *in_weights, *last_weights)
    res1, low1, mixed0, square0, unused = section_output(0, sc, parts, base0, turned)
    pieces1 = gather(low1)
    square_other = cross(square0)

    fw1, halo1 = forward(1, sc, pieces1 + out_pieces + out_others + [decays[1]])
    stat = fw1[6] + cross(fw1[6])
    stats = [stat] + [over_heads(stat, d) for d in range(1, head_axis)]
    pr1 = project(1, fw1[9], fw1[7], fw1[6], [])
    parts_out, sc_out = scatter(sc, pr1[0], pr1[1])
    bw1 = backward(1, sc_out, [fw1[11]] + stats, fw1[1:5], decays[1], halo1, [])
    lf1 = lift(1, bw1[6], bw1[0], fw1[0], bw1[3], parts_out[1:])
    weights1, heads1, sc_weights = weight_grads(
        lf1[2], fw1[0], bw1[0], fw1[11], bw1[1], bw1[2], common=lf1[3]
    )
    parts, sc_join = scatter(sc_weights, lf1[0], lf1[1])
    igrad1, glow1, sc_in = section_input(
        1, sc_join, parts, res1, fw1[10], fw1[5], *gains, mixed0,
        deps=weights1[2:-1],
    )
    piecesg = gather(glow1)

    heads1 = [over_heads(heads1[d], d) for d in far_first(head_axis)]

    early, unused = leave(sc_in, low1, pieces1[head_axis], glow1, piecesg[head_axis])
    bw0 = backward(
        0, sc, piecesg + [square0, square_other], fw0[1:5], decays[0], halo0,
        weights1[1:2],
    )
    weights0, heads0, sc_weights = weight_grads(
        bw0[6], fw0[0], bw0[0], bw0[7], bw0[1], bw0[2], deps=early[1:] + weights1[-1:],
    )
    lf0 = lift(0, sc_weights, bw0[0], fw0[0], bw0[3], heads1[1:])
    parts, sc_join = scatter(lf0[2], lf0[0], lf0[1], [[lf0[3], *heads0]], weights0[1:2])

    unused, low2, unused_mixed, unused_square, sc_out = section_output(1, sc_in, parts_out, res1)
    glow0, to_other, shared_own, sc_end = section_input(
        0, sc_out, parts, base0, igrad1, fw0[5], *gains, low2, *heads1,
        deps=weights0[2:],
    )
    got = cross(to_other)
    if spans == 1:
        late, sc_end = leave(sc_end, glow0, got, low2, got, shared_own, riders=seq)
        shared_parts = late
    else:
        late, sc_end = leave(sc_end, glow0, got, low2, got)
        total = shared_own + got[rows:].astype(F32)
        extra = resplit(total[:PAD])
        fill = jnp.zeros((BLOCK, shared), F32)
        chunks = [
            jnp.concatenate([fill, extra, total[PAD + r * share : PAD + (r + 1) * share]])
            for r in range(seq)
        ]
        shared_parts = over_seq([x.astype(LOW) for x in chunks])
    def summed(sc, pieces, *done):
        return pl.pallas_call(
            functools.partial(sum_kernel, sz, bool(done)),
            in_specs=[smem] + [vmem] * (len(pieces) + len(done)),
            out_shape=[shape((part + PAD, columns), LOW)] * (1 + len(done)),
            compiler_params=options,
        )(sc, *pieces, *done)

    own_sums, other_sums = summed(sc_end, weights0, *summed(sc_in, weights1))
    final = pl.pallas_call(
        functools.partial(final_kernel, sz),
        in_specs=[smem] + [vmem] * 2,
        out_shape=[
            shape((part, inner_dev), F32),
            shape((part, inner_dev), F32),
            shape((inner_dev, part), F32),
            shape((taps, inner_dev), F32),
            shape((1, inner_dev), F32),
            shape((1, heads_dev), F32),
        ],
        compiler_params=options,
    )(sc, own_sums, cross(other_sums))
    section_out, input_grad, unused = pl.pallas_call(
        functools.partial(home_kernel, slots),
        in_specs=[smem] + [vmem] * (2 * slots) + [anywhere],
        out_specs=[vmem, vmem, smem],
        out_shape=[shape((slots, BLOCK, chunk), F32)] * 2 + [index_shape],
        compiler_params=options,
    )(sc, *early, *late, final[4])

    shared_sum, tap_grads, gain_grads = pl.pallas_call(
        functools.partial(shared_kernel, sz, seq),
        in_specs=[smem] + [vmem] * seq,
        out_shape=[
            shape((share, shared), F32),
            shape((taps, shared // (seq * head_axis)), F32),
            shape((1, width // (seq * head_axis)), F32),
        ],
        compiler_params=options,
    )(sc, *shared_parts)
    return (
        section_out[None],
        input_grad[None],
        gain_grads,
        final[0][None],
        final[1][None],
        shared_sum[None],
        final[3][None],
        tap_grads[None],
        final[5],
        final[4],
        final[2][None],
    )


def solution(mesh):
    placed = (
        P(None, "seq", None),
        P(),
        P("section", None, "head", "seq"),
        P(None, "seq", None),
        P("section", None),
        P("section", None, "head"),
        P("section", None, "head"),
        P("section", None, None),
        P("section", None, "head"),
        P("section", None, None),
        P("section", "head"),
        P("section", "head"),
        P("section", None, None),
    )
    return jax.shard_map(
        per_device,
        mesh=mesh,
        in_specs=placed,
        out_specs=(
            P("section", None, "seq", "head"),
            P("section", None, "seq", "head"),
            P("section", ("seq", "head")),
            P("section", "seq", "head"),
            P("section", "seq", "head"),
            P("section", ("seq", "head"), None),
            P("section", None, "head"),
            P("section", None, ("seq", "head")),
            P("section", "head"),
            P("section", "head"),
            P("section", "head", "seq"),
        ),
        check_vma=False,
    )
```

```python
import functools

import jax
import jax.numpy as jnp
from jax import lax
from jax.experimental import pallas as pl
from jax.experimental.pallas import tpu as pltpu
from jax.sharding import PartitionSpec as P

BLOCK = 256
HALF = BLOCK // 2
PAD = 16
EPS = 1e-05
F32 = jnp.float32
LOW = jnp.bfloat16
HIDDEN = -1e30
NN = ((1,), (0,))
NT = ((1,), (1,))
TN = ((0,), (0,))
VMEM_BYTES = 50 * 1024 * 1024
ALL_VMEM_BYTES = 63 * 1024 * 1024


def dot(a, b, dims):
    return lax.dot_general(a, b, (dims, ((), ())), preferred_element_type=F32)


def aligned(start, size):
    return pl.ds(pl.multiple_of(start, size), size)


def spread(cols, first, count, width):
    rows = cols.shape[0]
    lane = lax.broadcasted_iota(jnp.int32, (rows, count * width), 1)
    out = jnp.broadcast_to(cols[:, first : first + 1], (rows, count * width))
    for h in range(1, count):
        out = jnp.where(lane >= h * width, cols[:, first + h : first + h + 1], out)
    return out


def per_head(array, h, width):
    lane = lax.broadcasted_iota(jnp.int32, array.shape, 1)
    inside = (lane >= h * width) & (lane < (h + 1) * width)
    return jnp.where(inside, array, jnp.zeros_like(array))


def split_low(value):
    high = value.astype(LOW).astype(F32)
    return high, value - high


def column_of(row, size):
    return jnp.transpose(jnp.broadcast_to(row, (128, size)))


def sigmoid(v):
    return 0.5 * jnp.tanh(0.5 * v) + 0.5


def pick(flag, a, b):
    return jnp.where(flag, a, b)


class Sizes:
    def __init__(self, blocks, width, channels, heads, states, taps, head_axis, inner):
        self.blocks = blocks
        self.width = width
        self.channels = channels
        self.heads = heads
        self.head_width = channels // heads
        self.states = states
        self.lin = channels + 2 * states
        self.taps = taps
        self.head_axis = head_axis
        self.chunk = width // head_axis
        self.rows = blocks * HALF
        self.tokens = blocks * BLOCK
        self.inner = inner


def weight_copies(sz, layer, c, h, given, dst, sems):
    ch = sz.channels
    cols = aligned(c * ch, ch)
    places = [dst.at[:, :ch], dst.at[:, ch : 2 * ch], dst.at[:, 2 * ch :]]
    own = [given[0].at[0, :, cols], given[1].at[0, :, cols], given[2].at[0]]
    return copies_for(layer, c, own, given[3:], places, sems)


def out_copies(sz, layer, c, h, given, dst, sems):
    rows = aligned((h * 2 + c) * sz.channels, sz.channels)
    return copies_for(layer, c, [given[0].at[0, rows, :]], given[1:], [dst], sems)


def copies_for(layer, c, own, sent, places, sems):
    both = []
    for flag, sources in ((c == layer, own), (c != layer, sent)):
        copies = [
            pltpu.make_async_copy(p, q, sems.at[i]) for i, (p, q) in enumerate(zip(sources, places))
        ]
        both.append((flag, copies))
    return both


def run_copies(choices, start, wait):
    for flag, copies in choices:

        @pl.when(flag)
        def _(copies=copies):
            if start:
                for copy in copies:
                    copy.start()
            if wait:
                for copy in copies:
                    copy.wait()


def put_ordered(sz, dst, c, k, b, own, other):
    for r in range(len(own)):

        @pl.when(lax.rem(k - b + len(own), len(own)) == r)
        def _(r=r):
            put_pair(dst, c, own[r][:HALF, :], other[r][:HALF, :])


def put_pair(dst, c, own, other):
    dst[aligned(c * HALF, HALF), :] = own
    dst[aligned((1 - c) * HALF, HALF), :] = other


def far_first(count):
    return [0] + list(range(count - 1, 0, -1))


def put_pieces(sz, dst, c, h, own, other):
    own, other = (dict(zip(far_first(sz.head_axis), side)) for side in (own, other))
    for d in range(sz.head_axis):
        cols = aligned((h ^ d) * sz.chunk, sz.chunk)
        dst[aligned(c * HALF, HALF), cols] = own[d]
        dst[aligned((1 - c) * HALF, HALF), cols] = other[d]


def line_of(table, at):
    line = lax.broadcasted_iota(jnp.int32, table.shape, 0)
    return jnp.sum(jnp.where(line == at, table, 0.0), axis=0, keepdims=True)


def conv_forward(sz, ext, taps):
    pre = taps[0:1] * ext[5 : 5 + BLOCK, :]
    for j in range(1, sz.taps):
        pre = pre + taps[j : j + 1] * ext[5 + j : 5 + j + BLOCK, :]
    return pre


def decay_of(sz, cols, rp, h, mask):
    rows = cols[:, h : h + 1] + rp[12 + h : 13 + h, :]
    return jnp.exp(jnp.where(mask, rows, HIDDEN))


def lower_mask():
    t = lax.broadcasted_iota(jnp.int32, (BLOCK, BLOCK), 0)
    s = lax.broadcasted_iota(jnp.int32, (BLOCK, BLOCK), 1)
    return t >= s


def forward_kernel(sz, layer, slots, sc, *refs):
    n = sz.head_axis
    sources = 2 * slots if layer == 0 else 2 * n + 2 * slots
    src, refs = refs[:sources], refs[sources:]
    if layer == 1:
        table, refs = refs[0], refs[1:]
    gains, given, halo, begin = refs[0:2], refs[2:8], refs[8], refs[9]
    refs = refs[10:]
    if layer == 1:
        ov, refs = refs[0], refs[1:]
    normed_o, gl_o, lin_o, ssd_o, inc_o, inv_o, part_o, unit_o, fin_o, sc_o, base_o = refs[:11]
    refs = refs[11:]
    if layer == 1:
        mixed_o, refs = refs[0], refs[1:]
    else:
        tables_o, refs = refs[0:2], refs[2:]
    xs, ms, wv, ext, state, sems = refs
    b = pl.program_id(0)
    c, h, k = sc[0], sc[1], sc[3]
    ch, st = sz.channels, sz.states
    copies = weight_copies(sz, layer, c, h, given, wv, sems)

    @pl.when(b == 0)
    def _():
        run_copies(copies, True, False)
        ext[0:8, :] = halo[...]
        state[...] = begin[...]
        for i in range(4):
            sc_o[i] = sc[i]

    mine = aligned(c * HALF, HALF)
    cols = aligned(h * sz.chunk, sz.chunk)
    if layer == 0:
        put_ordered(sz, xs, c, k, b, src[:slots], src[slots:])
        base_o[...] = xs[mine, cols]
        for r in range(slots):

            @pl.when(lax.rem(k - b + slots, slots) == r)
            def _(r=r):
                own = decay_table(rates_of(src[r]), c, sz.heads)
                other = decay_table(rates_of(src[slots + r]), c, sz.heads)
                tables_o[0][...] = pick(c == 0, own, other)
                tables_o[1][...] = pick(c == 0, other, own)

        rp = tables_o[0][...]
    else:
        put_pieces(sz, xs, c, h, [r[...] for r in src[:n]], [r[...] for r in src[n : 2 * n]])
        put_ordered(sz, ms, c, k, b, src[2 * n : 2 * n + slots], src[2 * n + slots :])
        base_o[...] = ms[mine, cols]
        mixed_o[...] = ms[...]
        rp = table[...]

    pv = pick(c == layer, gains[0][...], gains[1][...])
    x = xs[...].astype(F32)
    inv_in = lax.rsqrt(jnp.mean(x * x, axis=1, keepdims=True) + EPS)
    normed = (x * inv_in * pv[0:1, : sz.width]).astype(LOW)
    normed_o[...] = normed

    @pl.when(b == 0)
    def _():
        run_copies(copies, False, True)

    proj = dot(normed, wv[...], NN)
    gl = proj[:, :ch]
    gl_o[...] = gl
    lin = proj[:, ch:].astype(LOW)
    lin_o[...] = lin
    ext[8 : 8 + BLOCK, :] = lin.astype(F32)
    pre = conv_forward(sz, ext, pv[1:5, : sz.lin])
    ext[0:8, :] = ext[BLOCK : BLOCK + 8, :]
    act = (pre * sigmoid(pre)).astype(LOW)
    values, bm, cm = act[:, :ch], act[:, ch : ch + st], act[:, ch + st :]

    cols = jnp.transpose(rp)
    mask = lower_mask()
    gram = dot(cm, bm, NT)
    mixes, parts = [], []
    for i in range(sz.heads):
        mixes.append((gram * decay_of(sz, cols, rp, i, mask)).astype(LOW))
        parts.append(per_head(values, i, sz.head_width))
    intra = dot(jnp.concatenate(mixes, axis=1), jnp.concatenate(parts, axis=0), NN)

    low_state = state[...].astype(LOW)
    inc_o[0] = low_state
    ecum = spread(cols, sz.heads, sz.heads, sz.head_width)
    inter = dot(cm, low_state, NT) * ecum
    vf = values.astype(F32)
    carried = (vf * spread(cols, 2 * sz.heads, sz.heads, sz.head_width)).astype(LOW)
    local = dot(carried, bm, TN)
    for i in range(sz.heads):
        rows = slice(i * sz.head_width, (i + 1) * sz.head_width)
        total = cols[BLOCK - 1 : BLOCK, sz.heads + i : sz.heads + i + 1]
        state[rows, :] = total * state[rows, :] + local[rows]
    ssd = intra + inter + pv[6:7, :ch] * vf
    ssd_o[...] = ssd
    gated = ssd * (gl * sigmoid(gl))
    weighty = gated * pv[5:6, :ch]
    unit_o[...] = weighty.astype(LOW)

    lane = lax.broadcasted_iota(jnp.int32, (BLOCK, 128), 1)
    square = jnp.sum(gated * gated, axis=1, keepdims=True)
    if layer == 0:
        project = jnp.zeros_like(square)
    else:
        scaled_grad = dot(ms[...], ov[...], NN)
        project = jnp.sum(scaled_grad * weighty, axis=1, keepdims=True)
    stats = jnp.where(lane == 0, square, jnp.where(lane == 1, project, inv_in))
    stats = jnp.transpose(stats)
    part_o[...] = stats[0:2, :]
    inv_o[...] = stats[2:3, :]

    @pl.when(b == sz.blocks - 1)
    def _():
        fin_o[...] = state[...]


def scalar_lines(sz, lines):
    fill = [jnp.zeros((8 - sz.blocks, HALF), F32)] if sz.blocks < 8 else []
    high, low = split_low(jnp.concatenate(lines + fill, axis=0))
    table = jnp.concatenate([high, low], axis=0).astype(LOW)
    return jnp.concatenate([table] * (sz.chunk // HALF), axis=1)


def own_rows(sz, ref, which):
    blocks = [ref[aligned(b * BLOCK + which * HALF, HALF), :] for b in range(sz.blocks)]
    return jnp.concatenate(blocks, axis=0)


def project_kernel(sz, layer, deps, sc, unit_r, stats_r, *refs):
    given, refs = refs[:2], refs[2 + deps :]
    keep, send, sc_o, weights, sems = refs
    c, h = sc[0], sc[1]
    copies = out_copies(sz, layer, c, h, given, weights, sems)
    run_copies(copies, True, False)
    for i in range(4):
        sc_o[i] = sc[i]
    sides = []
    for which, out in ((c, keep), (1 - c, send)):
        sides.append((out, own_rows(sz, unit_r, which)))
        lines = [
            stats_r[0:1, aligned(b * BLOCK + which * HALF, HALF)] for b in range(sz.blocks)
        ]
        table = scalar_lines(sz, lines)
        for d in range(sz.head_axis):
            out[d, sz.rows :, :] = table
    run_copies(copies, False, True)
    for out, rows in sides:
        for d in range(sz.head_axis):
            chunk = weights[:, aligned((h ^ d) * sz.chunk, sz.chunk)]
            out[d, : sz.rows, :] = dot(rows, chunk, NN).astype(LOW)


def turn_kernel(sz, sc, *refs):
    given, given_out, refs = refs[:6], refs[6:8], refs[8:]
    wide_o, out_o, wv, ov, sems = refs[:2], refs[2:4], refs[4], refs[5], refs[6]
    for layer in range(2):
        copies = weight_copies(sz, layer, sc[0], sc[1], given, wv, sems)
        run_copies(copies, True, True)
        copies = out_copies(sz, layer, sc[0], sc[1], given_out, ov, sems)
        run_copies(copies, True, True)
        wide_o[layer][...] = jnp.transpose(wv[...])
        out_o[layer][...] = jnp.transpose(ov[...])


def out_at(out, d):
    return out[d] if isinstance(out, tuple) else out.at[d]


def lift_kernel(sz, layer, deps, sc, cat_r, normed_r, zero_gains, one_gains, small_r, *refs):
    weights, refs = refs[0], refs[1 + deps :]
    keep, send, sc_o, common_o, wide = refs[0], refs[1:-3], *refs[-3:]
    c, h = sc[0], sc[1]
    for i in range(4):
        sc_o[i] = sc[i]
    wide[...] = jnp.zeros_like(wide)
    for which, out in ((c, keep), (1 - c, send)):
        rows = own_rows(sz, cat_r, which)
        along = jnp.zeros((sz.rows, 1), F32)
        for d in range(sz.head_axis):
            cols = aligned((h ^ d) * sz.chunk, sz.chunk)
            product = dot(rows, weights[:, cols], NN)
            out_at(out, d)[: sz.rows, :] = product.astype(LOW)
            blocks = [
                normed_r[aligned(b * BLOCK + which * HALF, HALF), cols] for b in range(sz.blocks)
            ]
            product = product * jnp.concatenate(blocks, axis=0).astype(F32)
            wide[0:1, cols] += jnp.sum(product, axis=0, keepdims=True)
            along = along + jnp.sum(product, axis=1, keepdims=True)
        lines = [
            jnp.transpose(jnp.broadcast_to(along[b * HALF : (b + 1) * HALF], (HALF, 128)))[0:1, :]
            for b in range(sz.blocks)
        ]
        table = scalar_lines(sz, lines)
        for d in range(sz.head_axis):
            out_at(out, d)[sz.rows :, :] = table
    gain_grad = wide[0:1, :] / pick(c == layer, zero_gains[0:1, :], one_gains[0:1, :])
    flat = [small_r[j : j + 1, sz.channels :] for j in range(sz.taps)]
    flat += [gain_grad[:, q * sz.chunk : (q + 1) * sz.chunk] for q in range(sz.head_axis)]
    high, low = split_low(jnp.concatenate(flat, axis=0))
    common_o[...] = jnp.concatenate([high, low], axis=0).astype(LOW)


def backward_kernel(sz, layer, deps, sc, *refs):
    n = sz.head_axis
    sources = 2 * n + 2 if layer == 0 else 1 + n
    src, refs = refs[:sources], refs[sources:]
    gl_r, lin_r, ssd_r, inc_r = refs[:4]
    table, gains, ov = refs[4], refs[5:7], refs[7]
    halo, halo_grad, begin = refs[8:11]
    refs = refs[11 + deps :]
    cat_o, scaled_o, small_o, sums_o, fin_o, rim_o, sc_o = refs[:7]
    refs = refs[7:]
    if layer == 0:
        mixed_o, refs = refs[0], refs[1:]
    ms, ext, back, state, heads_p, small = refs
    i_step = pl.program_id(0)
    b = sz.blocks - 1 - i_step
    c, h = sc[0], sc[1]
    ch, st = sz.channels, sz.states
    pv = pick(c == layer, gains[0][...], gains[1][...])
    rp = table[...]

    @pl.when(i_step == 0)
    def _():
        back[BLOCK : BLOCK + 8, :] = halo_grad[...]
        state[...] = begin[...]
        small[...] = jnp.zeros_like(small)
        for i in range(4):
            sc_o[i] = sc[i]
        if layer == 0:
            for i in range(2):
                extra = src[i * n][sz.rows :, :].astype(F32)
                for d in range(1, n):
                    extra = extra + src[i * n + d][sz.rows :, :].astype(F32)
                heads_p[8 * i : 8 * i + 8, :] = extra[0:8, :HALF] + extra[8:16, :HALF]

    if layer == 0:
        rows = aligned(b * HALF, HALF)
        put_pieces(
            sz, ms, c, h, [r[rows, :] for r in src[:n]], [r[rows, :] for r in src[n : 2 * n]]
        )
        halves = []
        for k in range(2):
            alpha = lax.rsqrt(line_of(src[2 * n + k][...], b) / sz.inner + EPS)
            beta = alpha * alpha * line_of(heads_p[...], 8 * k + b) / sz.inner
            halves.append((alpha, beta))
        alpha, beta = (
            pick(
                c == 0,
                jnp.concatenate([halves[0][q], halves[1][q]], axis=1),
                jnp.concatenate([halves[1][q], halves[0][q]], axis=1),
            )
            for q in range(2)
        )
    else:
        stats = src[1][...]
        for d in range(1, n):
            stats = stats + src[1 + d][...]
        alpha = lax.rsqrt(stats[0:1, :] / sz.inner + EPS)
        beta = alpha * alpha * alpha * stats[1:2, :] / sz.inner

    sub = lax.broadcasted_iota(jnp.int32, rp.shape, 0)
    cols = jnp.transpose(jnp.where(sub == 12, alpha, jnp.where(sub == 13, beta, rp)))
    alpha, beta = cols[:, 12:13], cols[:, 13:14]

    gl = gl_r[...]
    ssd = ssd_r[...]
    sig = sigmoid(gl)
    swish = gl * sig
    slope = sig * (1.0 + gl * (1.0 - sig))
    gated = ssd * swish
    if layer == 0:
        mixed_grad = ms[...]
        mixed_o[...] = mixed_grad
    else:
        mixed_grad = src[0][...]
    scaled_grad = dot(mixed_grad, ov[...], NN)
    gain = pv[5:6, :ch]
    normal = gated * alpha
    small[4:5, :ch] += jnp.sum(scaled_grad * normal, axis=0, keepdims=True)
    scaled_o[...] = (normal * gain).astype(LOW)
    gated_grad = alpha * (scaled_grad * gain) - beta * gated
    ssd_grad = (gated_grad * swish).astype(LOW)
    gate_grad = (gated_grad * ssd * slope).astype(LOW)
    sgf = ssd_grad.astype(F32)

    before = lin_r[pl.ds(pl.multiple_of(jnp.maximum(b * BLOCK - 16, 0), 16), 16), :]
    ext[0:8, :] = pick(b > 0, before.astype(F32)[8:16, :], halo[...])
    ext[8 : 8 + BLOCK, :] = lin_r[aligned(b * BLOCK, BLOCK), :].astype(F32)
    taps = pv[1:5, : sz.lin]
    pre = conv_forward(sz, ext, taps)
    psig = sigmoid(pre)
    pact = pre * psig
    pslope = psig * (1.0 + pre * (1.0 - psig))
    act = pact.astype(LOW)
    values, bm, cm = act[:, :ch], act[:, ch : ch + st], act[:, ch + st :]
    vf = values.astype(F32)
    small[5:6, :ch] += jnp.sum(sgf * vf, axis=0, keepdims=True)

    mask = lower_mask()
    gram = dot(cm, bm, NT)
    gram_grad = jnp.zeros((BLOCK, BLOCK), F32)
    mixes, parts = [], []
    for i in range(sz.heads):
        decay = decay_of(sz, cols, rp, i, mask)
        mixes.append((gram * decay).astype(LOW))
        parts.append(per_head(ssd_grad, i, sz.head_width))
        gram_grad = gram_grad + dot(parts[-1], values, NT) * decay
    intra_grad = dot(jnp.concatenate(mixes, axis=0), jnp.concatenate(parts, axis=0), TN)

    ecum = spread(cols, sz.heads, sz.heads, sz.head_width)
    to_end = spread(cols, 2 * sz.heads, sz.heads, sz.head_width)
    inter_grad = (sgf * ecum).astype(LOW)
    low_state = state[...].astype(LOW)
    carried = (vf * to_end).astype(LOW)
    carried_grad = dot(bm, low_state, NT)
    gram_low = gram_grad.astype(LOW)
    b_grad = dot(gram_low, cm, TN) + dot(carried, low_state, NN)
    c_grad = dot(gram_low, bm, NN) + dot(inter_grad, inc_r[0], NN)
    value_grad = intra_grad + pv[6:7, :ch] * sgf + carried_grad * to_end
    entry = dot(inter_grad, cm, TN)
    for i in range(sz.heads):
        rows = slice(i * sz.head_width, (i + 1) * sz.head_width)
        total = cols[BLOCK - 1 : BLOCK, sz.heads + i : sz.heads + i + 1]
        state[rows, :] = total * state[rows, :] + entry[rows]

    pre_grad = jnp.concatenate([value_grad, b_grad, c_grad], axis=1) * pslope
    back[0:BLOCK, :] = pre_grad
    lin_grad = taps[0:1] * back[sz.taps - 1 : sz.taps - 1 + BLOCK, :]
    for j in range(1, sz.taps):
        at = sz.taps - 1 - j
        lin_grad = lin_grad + taps[j : j + 1] * back[at : at + BLOCK, :]
    for j in range(sz.taps):
        small[j : j + 1, :] += jnp.sum(pre_grad * ext[5 + j : 5 + j + BLOCK, :], axis=0, keepdims=True)
    back[BLOCK : BLOCK + 8, :] = back[0:8, :]
    cat_o[...] = jnp.concatenate([gate_grad, lin_grad.astype(LOW)], axis=1)

    @pl.when(i_step == sz.blocks - 1)
    def _():
        fin_o[...] = state[...]
        rim_o[...] = back[0:8, :]
        sums = small[...]
        flat = [sums[j : j + 1, :ch] for j in range(sz.taps + 2)]
        flat = [jnp.concatenate(flat[j : j + 3], axis=1) for j in range(0, len(flat), 3)]
        flat = flat + [jnp.zeros_like(flat[0])] * (4 - len(flat))
        high, low = split_low(jnp.concatenate(flat, axis=0))
        rest = jnp.zeros((PAD - 8, high.shape[1]), F32)
        small_o[...] = jnp.concatenate([high, low, rest], axis=0).astype(LOW)
        sums_o[...] = sums


def weights_kernel(sz, seq, deps, with_common, sc, normed, cat, mixed, scaled, small, *refs):
    if with_common:
        common, refs = refs[0], refs[1:]
    refs = refs[deps:]
    sc_o, outs, heads, full, wide = refs[0], refs[1 : seq + 1], refs[seq + 1 : -2], refs[-2], refs[-1]
    for i in range(4):
        sc_o[i] = sc[i]
    ch, st = sz.channels, sz.states
    step = sz.chunk
    for q in range(sz.head_axis):
        at = slice(q * step, (q + 1) * step)
        grads = dot(normed[:, at], cat[...], TN)
        full[at, : 2 * ch] = grads[:, : 2 * ch].astype(LOW)
        wide[at, :] = grads[:, 2 * ch :]
        full[at, 2 * ch :] = dot(mixed[:, at], scaled[...], TN).astype(LOW)
    rows = sz.width // seq
    part = rows // sz.head_axis
    for r, out in enumerate(outs):
        out[:rows, :] = full[aligned(lax.rem(sc[2] + r, seq) * rows, rows), :]
        out[rows:, :] = small[...]
    for d, out in enumerate(heads):
        lines = [
            wide[aligned(lax.rem(sc[2] + r, seq) * rows + (sc[1] ^ d) * part, part), :]
            for r in range(seq)
        ]
        if with_common:
            lines = [common[...].astype(F32)] + lines
        out[...] = jnp.concatenate(lines, axis=0).astype(LOW)


def resplit(extra):
    half = extra.shape[0] // 2
    high, low = split_low(extra[:half, :] + extra[half:, :])
    return jnp.concatenate([high, low], axis=0)


def join_kernel(sz, parts, riders, deps, sc, keep, *refs):
    n = sz.head_axis
    recv, refs = refs[0] if parts == 1 else refs[:parts], refs[parts:]
    more = [(refs[i * (n + 1)], refs[i * (n + 1) + 1 : (i + 1) * (n + 1)]) for i in range(riders)]
    refs = refs[riders * (n + 1) + deps :]
    sc_o, outs = refs[0], refs[1:]
    rows = sz.rows
    for i in range(4):
        sc_o[i] = sc[i]
    extra = resplit(keep[0, rows:, :].astype(F32) + out_at(recv, 0)[rows:, :].astype(F32))
    for d, out in enumerate(outs):
        both = keep[d, :rows, :].astype(F32) + out_at(recv, d)[:rows, :].astype(F32)
        out[:rows, :] = both.astype(out.dtype)
        out[rows : rows + PAD, :] = extra.astype(out.dtype)
        at = rows + PAD
        for common, rider in more:
            size = rider[d].shape[0]
            out[at : at + PAD, :] = common[...].astype(out.dtype)
            out[at + PAD : at + PAD + size, :] = rider[d][...].astype(out.dtype)
            at += PAD + size


def total_of(parts, rows):
    total = parts[0][rows, :].astype(F32)
    for p in parts[1:]:
        total = total + p[rows, :].astype(F32)
    return total


def output_kernel(sz, layer, sc, *refs):
    n = sz.head_axis
    parts, refs = refs[:n], refs[n:]
    resid = refs[0]
    res_o, low_o, mixed_o, square_o, sc_o = refs[-5:]
    for i in range(4):
        sc_o[i] = sc[i]
    extra = total_of(parts, slice(sz.rows, sz.rows + PAD))
    square = extra[0:8, :HALF] + extra[8:16, :HALF]
    square_o[...] = square
    inv = lax.rsqrt(square / sz.inner + EPS)
    for b in range(sz.blocks):
        rows = slice(b * HALF, (b + 1) * HALF)
        col = column_of(inv[b : b + 1, :], HALF)[:, 0:1]
        mixed = total_of(parts, rows) * col
        res = resid[rows, :].astype(F32) + mixed
        res_o[rows, :] = res
        low_o[rows, :] = res.astype(LOW)
        mixed_o[rows, :] = mixed


def input_kernel(sz, layer, sc, *refs):
    n = sz.head_axis
    parts, refs = refs[:n], refs[n:]
    resid, outg, inv_r, gains = refs[0], refs[1], refs[2], refs[3:5]
    refs = refs[5:]
    if layer == 1:
        mixed = refs[0]
        grad_o, low_o, sc_o = refs[-3:]
    else:
        one_low, one_heads = refs[0], refs[1 : 1 + n]
        low_o, swap_o, shared_o, sc_o = refs[-4:]
    for i in range(4):
        sc_o[i] = sc[i]
    c, h = sc[0], sc[1]
    first = c == 0
    mine = aligned(h * sz.chunk, sz.chunk)
    gain = pick(c == layer, gains[0][0:1, mine], gains[1][0:1, mine])
    extra = total_of(parts, slice(sz.rows, sz.rows + PAD))
    along = extra[0:8, :HALF] + extra[8:16, :HALF]
    tops, lows = [], []
    for b in range(sz.blocks):
        rows = slice(b * HALF, (b + 1) * HALF)
        at = b * BLOCK
        inv_row = pick(c == 0, inv_r[:, at : at + HALF], inv_r[:, at + HALF : at + BLOCK])
        inv = column_of(inv_row, HALF)[:, 0:1]
        share = column_of(along[b : b + 1, :] / sz.width, HALF)[:, 0:1]
        total = total_of(parts, rows)
        base = resid[rows, :].astype(F32)
        grad = outg[rows, :].astype(F32) + inv * (total * gain - base * (inv * share))
        low = grad.astype(LOW)
        low_o[rows, :] = low
        if layer == 0:
            swap_o[rows, :] = pick(first, one_low[rows, :], low)
        else:
            grad_o[rows, :] = grad
            dots = jnp.sum(low.astype(F32) * mixed[rows, :], axis=1, keepdims=True)
            row = jnp.transpose(jnp.broadcast_to(dots, (HALF, 128)))[0:1, :]
            high, rest = split_low(row)
            tops.append(high)
            lows.append(rest)
    if layer == 1:
        fill = [jnp.zeros((8 - sz.blocks, HALF), F32)] if sz.blocks < 8 else []
        extra = jnp.concatenate(tops + fill + lows + fill, axis=0)
        extra = jnp.concatenate([extra] * (sz.chunk // HALF), axis=1)
        low_o[sz.rows :, :] = extra.astype(LOW)
    else:
        size = shared_o.shape[0]
        at = sz.rows + PAD
        zero = total_of(parts, slice(at, at + size))
        one = total_of(one_heads, slice(None))
        zero, one = (jnp.concatenate([resplit(v[:PAD]), v[PAD:]], axis=0) for v in (zero, one))
        shared_o[...] = pick(first, zero, one)
        swap_o[sz.rows :, :] = pick(first, one, zero).astype(LOW)


def sum_kernel(sz, last, deps, sc, *refs):
    refs = refs[deps:]
    if last:
        parts, done, outs = refs[:-3], refs[-3], refs[-2:]
    else:
        parts, outs = refs[:-1], refs[-1:]
    rows = outs[0].shape[0] - PAD
    total = total_of(parts, slice(None))
    extra = total[rows:]
    high, low = split_low(extra[0:4, :] + extra[4:8, :])
    extra = jnp.concatenate([high, low, jnp.zeros((PAD - 8, extra.shape[1]), F32)], axis=0)
    sums = jnp.concatenate([total[:rows], extra], axis=0).astype(LOW)
    if last:
        outs[0][...] = pick(sc[0] == 0, sums, done[...])
        outs[1][...] = pick(sc[0] == 0, done[...], sums)
    else:
        outs[0][...] = sums


def final_kernel(sz, seq, sc, own, got, *refs):
    pieces, refs = refs[:-9], refs[-9:]
    gate_o, inner_o, out_o, conv_o, norm_o, skip_o, shared_o, taps_o, gain_o = refs
    c = sc[0]
    ch = sz.channels
    rows = own.shape[0] - PAD
    lane = lax.broadcasted_iota(jnp.int32, skip_o.shape, 1)
    skip = jnp.zeros(skip_o.shape, F32)
    for i in range(2):
        which = pick(i == 0, c, 1 - c)
        to = aligned(which * ch, ch)
        sums = (own if i == 0 else got)[...].astype(F32)
        gate_o[:, to] = sums[:rows, :ch]
        inner_o[:, to] = sums[:rows, ch : 2 * ch]
        out_o[to, :] = jnp.transpose(sums[:rows, 2 * ch :])
        lines = sums[rows : rows + 4, :] + sums[rows + 4 : rows + 8, :]
        for j in range(sz.taps):
            conv_o[j : j + 1, to] = lines[j // 3 : j // 3 + 1, (j % 3) * ch : (j % 3 + 1) * ch]
        norm_o[:, to] = lines[1:2, ch : 2 * ch]
        skips = lines[1:2, 2 * ch :]
        for q in range(sz.heads):
            part = jnp.sum(per_head(skips, q, sz.head_width), axis=1, keepdims=True)
            skip = jnp.where(lane == which * sz.heads + q, part, skip)
    skip_o[...] = skip
    total = total_of(pieces, slice(BLOCK, None))
    shared_o[...] = total[PAD:]
    common = total[: PAD // 2] + total[PAD // 2 : PAD]
    place = sc[2] * sz.head_axis + sc[1]
    span = common.shape[1]
    size = span // (seq * sz.head_axis)
    turned = pltpu.roll(common, lax.rem(span - place * size, span), 1)
    taps_o[...] = turned[: sz.taps, :size]
    size = sz.width // (seq * sz.head_axis)
    at = place * size
    line = jnp.broadcast_to(line_of(common, sz.taps + at // span), common.shape)
    turned = pltpu.roll(line, lax.rem(span - lax.rem(at, span), span), 1)
    gain_o[...] = turned[:1, :size]


def slice_kernel(sz, slots, sc, order, tokens, rates, *refs):
    outs, sc_o, sems = refs[:slots], refs[slots], refs[slots + 1]
    copies = []
    for r in range(slots):
        rows = tokens.at[order[lax.rem(sc[3] + r, slots)], aligned(sc[0] * HALF, HALF), :]
        copies.append(pltpu.make_async_copy(rows, outs[r].at[:HALF], sems.at[r]))
    for copy in copies:
        copy.start()
    for i in range(4):
        sc_o[i] = sc[i]
    for r in range(slots):
        first, rest = split_low(rates[0, order[lax.rem(sc[3] + r, slots)]])
        second, rest = split_low(rest)
        lines = jnp.concatenate([first, second, rest, jnp.zeros_like(rest)], axis=1)
        lines = jnp.concatenate([lines, jnp.zeros_like(lines)], axis=0)
        outs[r][HALF:, :] = lines.astype(LOW)
    for copy in copies:
        copy.wait()


def rates_of(piece):
    lines = piece[HALF:, :].astype(F32)[:8, :]
    return (lines[:, :BLOCK] + lines[:, BLOCK : 2 * BLOCK]) + lines[:, 2 * BLOCK : 3 * BLOCK]


def pack_kernel(sz, sc, order, grads, gate, inner, out, in_gain, conv_i, conv_s, skip, norm, *refs):
    gate_o, inner_o, o_o, mine_o, send_o, sems = *refs[:5], refs[-1]
    c, h = sc[0], sc[1]
    ch = sz.channels
    outs = refs[5:-1]
    slices = []
    for r, to in enumerate(outs):
        rows = grads.at[order[lax.rem(sc[3] + r, len(outs))], aligned(c * HALF, HALF), :]
        slices.append(pltpu.make_async_copy(rows, to, sems.at[3 + r]))
    cols = aligned((1 - c) * ch, ch)
    rows = aligned((h * 2 + 1 - c) * ch, ch)
    copies = [
        pltpu.make_async_copy(gate.at[0, :, cols], gate_o, sems.at[0]),
        pltpu.make_async_copy(inner.at[0, :, cols], inner_o, sems.at[1]),
        pltpu.make_async_copy(out.at[0, rows, :], o_o, sems.at[2]),
        *slices,
    ]
    for copy in copies:
        copy.start()
    for which, ref in ((c, mine_o), (1 - c, send_o)):
        at = aligned(which * ch, ch)
        ref[...] = jnp.zeros_like(ref)
        ref[0:1, :] = in_gain[...]
        ref[1 : 1 + sz.taps, :ch] = conv_i[0, :, at]
        ref[1 : 1 + sz.taps, ch : sz.lin] = conv_s[0]
        ref[5:6, :ch] = norm[:, at]
        low = spread(skip[...], 0, sz.heads, sz.head_width)
        high = spread(skip[...], sz.heads, sz.heads, sz.head_width)
        ref[6:7, :ch] = pick(which == 0, low, high)
    for copy in copies:
        copy.wait()


def decay_table(rate, c, n):
    lane = lax.broadcasted_iota(jnp.int32, rate.shape, 1)
    cum = rate
    step = 1
    while step < BLOCK:
        cum = cum + jnp.where(lane >= step, pltpu.roll(cum, step, 1), 0.0)
        step *= 2
    end = cum[:, BLOCK - 1 :]
    lines = [cum, jnp.exp(cum), jnp.exp(end - cum) * -rate, jnp.log(-rate) - cum]
    low = jnp.concatenate([v[:n] for v in lines], axis=0)
    high = jnp.concatenate([v[n:] for v in lines], axis=0)
    return pick(c == 0, low, high)


def leave_kernel(sz, slots, riders, sc, zero_own, zero_other, one_own, one_other, *refs):
    c = sc[0]
    if riders:
        shared, refs = refs[0], refs[1:]
        total = shared[...] + one_other[sz.rows :, :].astype(F32)
        extra = resplit(total[:PAD])
        part = (total.shape[0] - PAD) // riders
    outs = refs[:slots]
    for i in range(4):
        refs[slots][i] = sc[i]
    for r in range(slots):
        rows = aligned(lax.rem(sc[3] + r, slots) * HALF, HALF)
        own = pick(c == 0, zero_own[rows, :], one_own[rows, :])
        other = pick(c == 0, zero_other[rows, :], one_other[rows, :])
        put_pair(outs[r], c, own, other)
        if riders:
            lines = [extra, total[PAD + r * part : PAD + (r + 1) * part]]
            outs[r][BLOCK:, :] = jnp.concatenate(lines, axis=0).astype(LOW)


def home_kernel(slots, sc, *refs):
    early, late, out, grad = refs[:slots], refs[slots : 2 * slots], refs[-3], refs[-2]
    for i in range(4):
        refs[-1][i] = sc[i]
    first = sc[0] == 0
    for r in range(slots):
        at = lax.rem(sc[3] - r + slots, slots)
        out[at] = pick(first, early[r][...], late[r][:BLOCK, :]).astype(F32)
        grad[at] = pick(first, late[r][:BLOCK, :], early[r][...]).astype(F32)


def whole(shape):
    return pl.BlockSpec(shape, lambda *_: (0,) * len(shape))


def per_device(
    tokens,
    slot_order,
    log_decay,
    grad_out,
    in_gain,
    w_gate,
    w_inner,
    w_shared,
    conv_inner,
    conv_shared,
    d_skip,
    norm_gain,
    w_out,
):
    slots = tokens.shape[0]
    span = tokens.shape[1]
    width = tokens.shape[2]
    seq = lax.axis_size("seq")
    head_axis = lax.axis_size("head")
    cores = lax.axis_size("section")
    spans = seq // slots
    c = lax.axis_index("section")
    z = lax.axis_index("seq")
    h = lax.axis_index("head")
    k = lax.rem(z, slots)
    inner_dev = w_gate.shape[2]
    channels = inner_dev // cores
    shared = w_shared.shape[2]
    heads_dev = d_skip.shape[1]
    taps = conv_inner.shape[1]
    sz = Sizes(
        slots * span // BLOCK,
        width,
        channels,
        heads_dev // cores,
        shared // 2,
        taps,
        head_axis,
        inner_dev * head_axis,
    )
    first = c == 0
    swap = [(0, 1), (1, 0)]
    nb, tok, rows, chunk = sz.blocks, sz.tokens, sz.rows, sz.chunk

    def cross(x):
        return lax.ppermute(x, "section", swap)

    def turn(x, r):
        pairs = [(i, i // slots * slots + (i % slots + r) % slots) for i in range(seq)]
        return lax.ppermute(x, "seq", pairs) if r else x

    def over_heads(x, d):
        return x if d == 0 else lax.ppermute(x, "head", [(i, i ^ d) for i in range(head_axis)])

    def next_span(x, way):
        pairs = [(i, i + way * slots) for i in range(seq) if 0 <= i + way * slots < seq]
        return lax.ppermute(x, "seq", pairs)

    def shape(dims, dtype):
        return jax.ShapeDtypeStruct(dims, dtype)

    prefetch = functools.partial(pltpu.PrefetchScalarGridSpec, num_scalar_prefetch=1)
    options = pltpu.CompilerParams(vmem_limit_bytes=VMEM_BYTES)
    from_hbm = pltpu.CompilerParams(vmem_limit_bytes=ALL_VMEM_BYTES)
    anywhere = pl.BlockSpec(memory_space=pl.ANY)
    smem = pl.BlockSpec(memory_space=pltpu.SMEM)
    vmem = pl.BlockSpec(memory_space=pltpu.VMEM)
    index_shape = shape((4,), jnp.int32)

    def cost(flops, moved):
        return pl.CostEstimate(flops=int(flops), bytes_accessed=int(moved), transcendentals=0)

    def to_members(pieces):
        return [turn(x, r) for r, x in enumerate(pieces)]

    sc = jnp.stack([c, h, z, k]).astype(jnp.int32)
    *tok_slices, sc = pl.pallas_call(
        functools.partial(slice_kernel, sz, slots),
        in_specs=[smem, smem, anywhere, vmem],
        out_specs=[vmem] * slots + [smem],
        out_shape=[shape((HALF + PAD, width), LOW)] * slots + [index_shape],
        scratch_shapes=[pltpu.SemaphoreType.DMA((slots,))],
        compiler_params=from_hbm,
    )(sc, slot_order, tokens, log_decay)
    tok_pieces = to_members(tok_slices)
    tok_others = [cross(x) for x in tok_pieces]

    wide = 2 * channels + shared
    gate_sent, inner_sent, o_sent, pv_mine, pv_sent, *out_slices = pl.pallas_call(
        functools.partial(pack_kernel, sz),
        in_specs=[smem, smem] + [anywhere] * 4 + [vmem] * 5,
        out_specs=[vmem] * (5 + slots),
        out_shape=[
            shape((width, channels), LOW),
            shape((width, channels), LOW),
            shape((channels, width), LOW),
            shape((16, width), F32),
            shape((16, width), F32),
        ]
        + [shape((HALF, width), LOW)] * slots,
        scratch_shapes=[pltpu.SemaphoreType.DMA((3 + slots,))],
        compiler_params=from_hbm,
    )(
        sc, slot_order, grad_out, w_gate, w_inner, w_out,
        in_gain, conv_inner, conv_shared, d_skip, norm_gain,
    )
    sent = [cross(x) for x in (gate_sent, inner_sent, w_shared[0], o_sent)]
    gains = [pv_mine, cross(pv_sent)]

    def span_total(table):
        ends = table[: sz.heads, BLOCK - 1 :: BLOCK]
        return jnp.repeat(jnp.exp(jnp.sum(ends, axis=1)), sz.head_width)[:, None]

    parts_shape = shape((head_axis, rows + PAD, chunk), LOW)
    in_weights = [w_gate, w_inner, w_shared, *sent[:3]]
    last_weights = [w_out, sent[3]]
    wide_weights = pltpu.VMEM((width, wide), LOW)
    out_weights = pltpu.VMEM((channels, width), LOW)
    copy_sems = pltpu.SemaphoreType.DMA((4,))
    dense = 2 * tok * width * (wide + channels)

    def forward(layer, sc, sources):
        def at(b, _):
            return (b, 0)

        piece = pl.BlockSpec((HALF, chunk), at)
        table = pl.BlockSpec((16, BLOCK), lambda b, _: (0, b))
        if layer == 0:
            src_specs = [whole((HALF + PAD, width))] * (2 * slots)
            more_specs = [table, table]
            more_shapes = [shape((16, tok), F32)] * 2
        else:
            src_specs = [piece] * (2 * head_axis) + [whole((HALF, width))] * (2 * slots) + [table]
            more_specs = [pl.BlockSpec((BLOCK, width), at)]
            more_shapes = [shape((tok, width), LOW)]

        last = [] if layer == 0 else [turned[3]]

        def call(halo, begin):
            return pl.pallas_call(
                functools.partial(forward_kernel, sz, layer, slots),
                grid_spec=prefetch(
                    grid=(nb,),
                    in_specs=src_specs
                    + [whole((16, width)), whole((16, width))]
                    + [anywhere] * len(in_weights)
                    + [whole((8, sz.lin)), whole((channels, sz.states))]
                    + [whole(x.shape) for x in last],
                    out_specs=[
                        pl.BlockSpec((BLOCK, width), at),
                        pl.BlockSpec((BLOCK, channels), at),
                        pl.BlockSpec((BLOCK, sz.lin), at),
                        pl.BlockSpec((BLOCK, channels), at),
                        pl.BlockSpec((1, channels, sz.states), lambda b, _: (b, 0, 0)),
                        pl.BlockSpec((1, BLOCK), lambda b, _: (0, b)),
                        pl.BlockSpec((2, BLOCK), lambda b, _: (0, b)),
                        pl.BlockSpec((BLOCK, channels), at),
                        whole((channels, sz.states)),
                        smem,
                        piece,
                    ]
                    + more_specs,
                    scratch_shapes=[
                        pltpu.VMEM((BLOCK, width), LOW),
                        pltpu.VMEM((BLOCK, width), LOW),
                        wide_weights,
                        pltpu.VMEM((BLOCK + 8, sz.lin), F32),
                        pltpu.VMEM((channels, sz.states), F32),
                        copy_sems,
                    ],
                ),
                out_shape=[
                    shape((tok, width), LOW),
                    shape((tok, channels), F32),
                    shape((tok, sz.lin), LOW),
                    shape((tok, channels), F32),
                    shape((nb, channels, sz.states), LOW),
                    shape((1, tok), F32),
                    shape((2, tok), F32),
                    shape((tok, channels), LOW),
                    shape((channels, sz.states), F32),
                    index_shape,
                    shape((rows, chunk), LOW),
                ]
                + more_shapes,
                compiler_params=options,
                cost_estimate=cost(6 * dense, 16e6),
            )(sc, *sources, *gains, *in_weights, halo, begin, *last)

        halo = jnp.zeros((8, sz.lin), F32)
        begin = jnp.zeros((channels, sz.states), F32)
        if spans == 1:
            return call(halo, begin), halo
        trial = call(halo, begin)
        halo = next_span(trial[2][tok - 8 :].astype(F32), 1)
        local = call(halo, begin)[8]
        total = span_total(trial[11] if layer == 0 else sources[-1])
        for _ in range(spans - 1):
            begin = next_span(total * begin + local, 1)
        return call(halo, begin), halo

    def backward(layer, sc, sources, saved, decays, halo, deps):
        def at(i, _):
            return (nb - 1 - i, 0)

        if layer == 0:
            src_specs = [whole(s.shape) for s in sources]
        else:
            stat = pl.BlockSpec((2, BLOCK), lambda i, _: (0, nb - 1 - i))
            src_specs = [pl.BlockSpec((BLOCK, width), at)] + [stat] * head_axis
        gl, lin, ssd, inc = saved
        mixed_spec = [pl.BlockSpec((BLOCK, width), at)] if layer == 0 else []
        mixed_shape = [shape((tok, width), LOW)] if layer == 0 else []

        def call(halo_grad, begin):
            return pl.pallas_call(
                functools.partial(backward_kernel, sz, layer, len(deps)),
                grid_spec=prefetch(
                    grid=(nb,),
                    in_specs=src_specs
                    + [
                        pl.BlockSpec((BLOCK, channels), at),
                        whole(lin.shape),
                        pl.BlockSpec((BLOCK, channels), at),
                        pl.BlockSpec((1, channels, sz.states), lambda i, _: (nb - 1 - i, 0, 0)),
                        pl.BlockSpec((16, BLOCK), lambda i, _: (0, nb - 1 - i)),
                        whole((16, width)),
                        whole((16, width)),
                        whole((width, channels)),
                        whole((8, sz.lin)),
                        whole((8, sz.lin)),
                        whole((channels, sz.states)),
                    ]
                    + [anywhere] * len(deps),
                    out_specs=[
                        pl.BlockSpec((BLOCK, wide), at),
                        pl.BlockSpec((BLOCK, channels), at),
                        whole((PAD, 3 * channels)),
                        whole((8, sz.lin)),
                        whole((channels, sz.states)),
                        whole((8, sz.lin)),
                        smem,
                    ]
                    + mixed_spec,
                    scratch_shapes=[
                        pltpu.VMEM((BLOCK, width), LOW),
                        pltpu.VMEM((BLOCK + 8, sz.lin), F32),
                        pltpu.VMEM((BLOCK + 8, sz.lin), F32),
                        pltpu.VMEM((channels, sz.states), F32),
                        pltpu.VMEM((PAD, HALF), F32),
                        pltpu.VMEM((8, sz.lin), F32),
                    ],
                ),
                out_shape=[
                    shape((tok, wide), LOW),
                    shape((tok, channels), LOW),
                    shape((PAD, 3 * channels), LOW),
                    shape((8, sz.lin), F32),
                    shape((channels, sz.states), F32),
                    shape((8, sz.lin), F32),
                    index_shape,
                ]
                + mixed_shape,
                compiler_params=options,
                cost_estimate=cost(8 * dense, 16e6),
            )(
                sc, *sources, gl, lin, ssd, inc, decays, *gains, turned[2 + layer],
                halo, halo_grad, begin, *deps,
            )

        halo_grad = jnp.zeros((8, sz.lin), F32)
        begin = jnp.zeros((channels, sz.states), F32)
        if spans == 1:
            return call(halo_grad, begin)
        local = call(halo_grad, begin)[4]
        for _ in range(spans - 1):
            begin = next_span(span_total(decays) * begin + local, -1)
        halo_grad = next_span(call(halo_grad, begin)[5], -1)
        return call(halo_grad, begin)

    def project(layer, sc, unit, stats, deps):
        return pl.pallas_call(
            functools.partial(project_kernel, sz, layer, len(deps)),
            in_specs=[smem, vmem, vmem] + [anywhere] * (2 + len(deps)),
            out_specs=[vmem, vmem, smem],
            out_shape=[parts_shape, parts_shape, index_shape],
            scratch_shapes=[out_weights, copy_sems],
            compiler_params=options,
            cost_estimate=cost(dense / 4, 4e6),
        )(sc, unit, stats, *last_weights, *deps)

    def lift(layer, sc, cat, normed, small, deps):
        outs = pl.pallas_call(
            functools.partial(lift_kernel, sz, layer, len(deps)),
            in_specs=[smem] + [vmem] * 6 + [anywhere] * len(deps),
            out_specs=[vmem] * (1 + head_axis) + [smem, vmem],
            out_shape=[parts_shape]
            + [shape(parts_shape.shape[1:], LOW)] * head_axis
            + [index_shape, shape((PAD, chunk), LOW)],
            scratch_shapes=[pltpu.VMEM((8, width), F32)],
            compiler_params=options,
            cost_estimate=cost(dense, 8e6),
        )(sc, cat, normed, *gains, small, turned[layer], *deps)
        return outs[0], list(outs[1:-2]), outs[-2], outs[-1]

    def scatter(sc, keep, send, riders=(), deps=()):
        size = rows + PAD + sum(PAD + rider[1].shape[0] for rider in riders)
        flat = [x for rider in riders for x in rider]
        got = [cross(x) for x in (send if isinstance(send, list) else [send])]
        joined = pl.pallas_call(
            functools.partial(join_kernel, sz, len(got), len(riders), len(deps)),
            in_specs=[smem] + [vmem] * (1 + len(got) + len(flat)) + [anywhere] * len(deps),
            out_specs=[smem] + [vmem] * head_axis,
            out_shape=[index_shape, shape((size, chunk), F32)]
            + [shape((size, chunk), LOW)] * (head_axis - 1),
            compiler_params=options,
        )(sc, keep, *got, *flat, *deps)
        return [over_heads(joined[1 + d], d) for d in far_first(head_axis)], joined[0]

    def gather(low):
        own = [over_heads(low, d) for d in far_first(head_axis)]
        return own + [cross(x) for x in own]

    turned = pl.pallas_call(
        functools.partial(turn_kernel, sz),
        in_specs=[smem] + [anywhere] * 8,
        out_specs=[vmem] * 4,
        out_shape=[shape((wide, width), LOW)] * 2 + [shape((width, channels), LOW)] * 2,
        scratch_shapes=[wide_weights, out_weights, copy_sems],
        compiler_params=options,
        cost_estimate=cost(1e9, 8e6),
    )

    def section_output(layer, sc, parts, resid, deps=()):
        return pl.pallas_call(
            functools.partial(output_kernel, sz, layer),
            in_specs=[smem] + [vmem] * (head_axis + 1) + [anywhere] * len(deps),
            out_specs=[vmem] * 4 + [smem],
            out_shape=[
                shape((rows, chunk), F32),
                shape((rows, chunk), LOW),
                shape((rows, chunk), F32),
                shape((8, HALF), F32),
                index_shape,
            ],
            compiler_params=options,
        )(sc, *parts, resid, *deps)

    part = width // seq
    columns = 3 * channels
    share = part // head_axis
    shared_size = seq * share + PAD

    def section_input(layer, sc, parts, *others, deps=()):
        if layer == 0:
            outs = [
                shape((rows + PAD, chunk), LOW),
                shape((rows + shared_size, chunk), LOW),
                shape((shared_size, chunk), F32),
            ]
        else:
            outs = [shape((rows, chunk), F32), shape((rows + PAD, chunk), LOW)]
        return pl.pallas_call(
            functools.partial(input_kernel, sz, layer),
            in_specs=[smem] + [vmem] * (head_axis + len(others)) + [anywhere] * len(deps),
            out_specs=[vmem] * len(outs) + [smem],
            out_shape=outs + [index_shape],
            compiler_params=options,
        )(sc, *parts, *others, *deps)

    def weight_grads(sc, normed, cat, mixed, scaled, small, deps=(), common=None):
        more = [] if common is None else [common]
        size = seq * share + PAD * len(more)
        outs = pl.pallas_call(
            functools.partial(weights_kernel, sz, seq, len(deps), bool(more)),
            in_specs=[smem] + [vmem] * (5 + len(more)) + [anywhere] * len(deps),
            out_specs=[smem] + [vmem] * (seq + head_axis),
            out_shape=[index_shape]
            + [shape((part + PAD, columns), LOW)] * seq
            + [shape((size, shared), LOW)] * head_axis,
            scratch_shapes=[pltpu.VMEM((width, columns), LOW), pltpu.VMEM((width, shared), F32)],
            compiler_params=options,
            cost_estimate=cost(4 * dense, 12e6),
        )(sc, normed, cat, mixed, scaled, small, *more, *deps)
        return over_seq(outs[1 : 1 + seq]), outs[1 + seq :], outs[0]

    def shifted(x, r):
        return lax.ppermute(x, "seq", [(i, (i + r) % seq) for i in range(seq)]) if r else x

    def over_seq(chunks):
        return [shifted(x, r) for r, x in enumerate(chunks)]

    def leave(sc, *arrays, riders=0):
        size = BLOCK + (share + PAD if riders else 0)
        pieces = pl.pallas_call(
            functools.partial(leave_kernel, sz, slots, riders),
            in_specs=[smem] + [vmem] * len(arrays),
            out_specs=[vmem] * slots + [smem],
            out_shape=[shape((size, chunk), LOW)] * slots + [index_shape],
            compiler_params=options,
        )(sc, *arrays)
        return to_members(pieces[:slots]), pieces[slots]

    out_pieces = to_members(out_slices)
    fw0, halo0 = forward(0, sc, tok_pieces + tok_others)
    base0, decays = fw0[10], fw0[11:13]
    pr0 = project(0, fw0[9], fw0[7], fw0[6], [out_pieces[1], out_pieces[-1]])
    out_others = [cross(x) for x in out_pieces]
    parts, sc_join = scatter(sc, pr0[0], pr0[1])
    turned = turned(sc_join, *in_weights, *last_weights)
    res1, low1, mixed0, square0, unused = section_output(0, sc, parts, base0, turned)
    pieces1 = gather(low1)
    square_other = cross(square0)

    fw1, halo1 = forward(1, sc, pieces1 + out_pieces + out_others + [decays[1]])
    stat = fw1[6] + cross(fw1[6])
    stats = [stat] + [over_heads(stat, d) for d in range(1, head_axis)]
    pr1 = project(1, fw1[9], fw1[7], fw1[6], [])
    parts_out, sc_out = scatter(sc, pr1[0], pr1[1])
    bw1 = backward(1, sc_out, [fw1[11]] + stats, fw1[1:5], decays[1], halo1, [])
    lf1 = lift(1, bw1[6], bw1[0], fw1[0], bw1[3], parts_out[1:])
    weights1, heads1, sc_weights = weight_grads(
        lf1[2], fw1[0], bw1[0], fw1[11], bw1[1], bw1[2], common=lf1[3]
    )
    parts, sc_join = scatter(sc_weights, lf1[0], lf1[1])
    igrad1, glow1, sc_in = section_input(
        1, sc_join, parts, res1, fw1[10], fw1[5], *gains, mixed0,
        deps=weights1[2:-1],
    )
    piecesg = gather(glow1)

    heads1 = [over_heads(heads1[d], d) for d in far_first(head_axis)]

    early, unused = leave(sc_in, low1, pieces1[head_axis], glow1, piecesg[head_axis])
    bw0 = backward(
        0, sc, piecesg + [square0, square_other], fw0[1:5], decays[0], halo0,
        weights1[1:2],
    )
    weights0, heads0, sc_weights = weight_grads(
        bw0[6], fw0[0], bw0[0], bw0[7], bw0[1], bw0[2], deps=early[1:] + weights1[-1:],
    )
    lf0 = lift(0, sc_weights, bw0[0], fw0[0], bw0[3], heads1[1:])
    parts, sc_join = scatter(lf0[2], lf0[0], lf0[1], [[lf0[3], *heads0]], weights0[1:2])

    def summed(sc, pieces, *done, deps=()):
        return pl.pallas_call(
            functools.partial(sum_kernel, sz, bool(done), len(deps)),
            in_specs=[smem] + [anywhere] * len(deps) + [vmem] * (len(pieces) + len(done)),
            out_shape=[shape((part + PAD, columns), LOW)] * (1 + len(done)),
            compiler_params=options,
        )(sc, *deps, *pieces, *done)

    sums1 = summed(sc_in, weights1)
    unused, low2, unused_mixed, unused_square, sc_out = section_output(1, sc_in, parts_out, res1)
    glow0, to_other, shared_own, sc_end = section_input(
        0, sc_out, parts, base0, igrad1, fw0[5], *gains, low2, *heads1,
        deps=[*weights0[2:], *sums1],
    )
    got = cross(to_other)
    if spans == 1:
        late, sc_end = leave(sc_end, glow0, got, low2, got, shared_own, riders=seq)
        shared_parts = late
    else:
        late, sc_end = leave(sc_end, glow0, got, low2, got)
        total = shared_own + got[rows:].astype(F32)
        extra = resplit(total[:PAD])
        fill = jnp.zeros((BLOCK, shared), F32)
        chunks = [
            jnp.concatenate([fill, extra, total[PAD + r * share : PAD + (r + 1) * share]])
            for r in range(seq)
        ]
        shared_parts = over_seq([x.astype(LOW) for x in chunks])
    own_sums, other_sums = summed(sc_end, weights0, *sums1)
    final = pl.pallas_call(
        functools.partial(final_kernel, sz, seq),
        in_specs=[smem] + [vmem] * (2 + seq),
        out_shape=[
            shape((part, inner_dev), F32),
            shape((part, inner_dev), F32),
            shape((inner_dev, part), F32),
            shape((taps, inner_dev), F32),
            shape((1, inner_dev), F32),
            shape((1, heads_dev), F32),
            shape((share, shared), F32),
            shape((taps, shared // (seq * head_axis)), F32),
            shape((1, width // (seq * head_axis)), F32),
        ],
        compiler_params=options,
    )(sc, own_sums, cross(other_sums), *shared_parts)
    section_out, input_grad, unused = pl.pallas_call(
        functools.partial(home_kernel, slots),
        in_specs=[smem] + [vmem] * (2 * slots),
        out_specs=[vmem, vmem, smem],
        out_shape=[shape((slots, BLOCK, chunk), F32)] * 2 + [index_shape],
        compiler_params=options,
    )(sc, *early, *late)

    return (
        section_out[None],
        input_grad[None],
        final[8],
        final[0][None],
        final[1][None],
        final[6][None],
        final[3][None],
        final[7][None],
        final[5],
        final[4],
        final[2][None],
    )


def solution(mesh):
    placed = (
        P(None, "seq", None),
        P(),
        P("section", None, "head", "seq"),
        P(None, "seq", None),
        P("section", None),
        P("section", None, "head"),
        P("section", None, "head"),
        P("section", None, None),
        P("section", None, "head"),
        P("section", None, None),
        P("section", "head"),
        P("section", "head"),
        P("section", None, None),
    )
    return jax.shard_map(
        per_device,
        mesh=mesh,
        in_specs=placed,
        out_specs=(
            P("section", None, "seq", "head"),
            P("section", None, "seq", "head"),
            P("section", ("seq", "head")),
            P("section", "seq", "head"),
            P("section", "seq", "head"),
            P("section", ("seq", "head"), None),
            P("section", None, "head"),
            P("section", None, ("seq", "head")),
            P("section", "head"),
            P("section", "head"),
            P("section", "head", "seq"),
        ),
        check_vma=False,
    )
```

```python
import functools

import jax
import jax.numpy as jnp
from jax import lax
from jax.experimental import pallas as pl
from jax.experimental.pallas import tpu as pltpu
from jax.sharding import PartitionSpec as P

BLOCK = 256
HALF = BLOCK // 2
PAD = 16
EPS = 1e-05
F32 = jnp.float32
LOW = jnp.bfloat16
HIDDEN = -1e30
NN = ((1,), (0,))
NT = ((1,), (1,))
TN = ((0,), (0,))
VMEM_BYTES = 28 * 1024 * 1024
ALL_VMEM_BYTES = 63 * 1024 * 1024


def dot(a, b, dims):
    return lax.dot_general(a, b, (dims, ((), ())), preferred_element_type=F32)


def aligned(start, size):
    return pl.ds(pl.multiple_of(start, size), size)


def spread(cols, first, count, width):
    rows = cols.shape[0]
    lane = lax.broadcasted_iota(jnp.int32, (rows, count * width), 1)
    out = jnp.broadcast_to(cols[:, first : first + 1], (rows, count * width))
    for h in range(1, count):
        out = jnp.where(lane >= h * width, cols[:, first + h : first + h + 1], out)
    return out


def per_head(array, h, width):
    lane = lax.broadcasted_iota(jnp.int32, array.shape, 1)
    inside = (lane >= h * width) & (lane < (h + 1) * width)
    return jnp.where(inside, array, jnp.zeros_like(array))


def split_low(value):
    high = value.astype(LOW).astype(F32)
    return high, value - high


def column_of(row, size):
    return jnp.transpose(jnp.broadcast_to(row, (128, size)))


def sigmoid(v):
    return 0.5 * jnp.tanh(0.5 * v) + 0.5


def pick(flag, a, b):
    return jnp.where(flag, a, b)


class Sizes:
    def __init__(self, blocks, width, channels, heads, states, taps, head_axis, inner):
        self.blocks = blocks
        self.width = width
        self.channels = channels
        self.heads = heads
        self.head_width = channels // heads
        self.states = states
        self.lin = channels + 2 * states
        self.taps = taps
        self.head_axis = head_axis
        self.chunk = width // head_axis
        self.rows = blocks * HALF
        self.tokens = blocks * BLOCK
        self.inner = inner


def weight_copies(sz, layer, c, h, given, dst, sems):
    ch = sz.channels
    cols = aligned(c * ch, ch)
    places = [dst.at[:, :ch], dst.at[:, ch : 2 * ch], dst.at[:, 2 * ch :]]
    own = [given[0].at[0, :, cols], given[1].at[0, :, cols], given[2].at[0]]
    return copies_for(layer, c, own, given[3:], places, sems)


def out_copies(sz, layer, c, h, given, dst, sems):
    rows = aligned((h * 2 + c) * sz.channels, sz.channels)
    return copies_for(layer, c, [given[0].at[0, rows, :]], given[1:], [dst], sems)


def copies_for(layer, c, own, sent, places, sems):
    both = []
    for flag, sources in ((c == layer, own), (c != layer, sent)):
        copies = [
            pltpu.make_async_copy(p, q, sems.at[i]) for i, (p, q) in enumerate(zip(sources, places))
        ]
        both.append((flag, copies))
    return both


def run_copies(choices, start, wait):
    for flag, copies in choices:

        @pl.when(flag)
        def _(copies=copies):
            if start:
                for copy in copies:
                    copy.start()
            if wait:
                for copy in copies:
                    copy.wait()


def put_ordered(sz, dst, c, k, b, own, other):
    for r in range(len(own)):

        @pl.when(lax.rem(k - b + len(own), len(own)) == r)
        def _(r=r):
            put_pair(dst, c, own[r][:HALF, :], other[r][:HALF, :])


def put_pair(dst, c, own, other):
    dst[aligned(c * HALF, HALF), :] = own
    dst[aligned((1 - c) * HALF, HALF), :] = other


def far_first(count):
    return [0] + list(range(count - 1, 0, -1))


def put_pieces(sz, dst, c, h, own, other):
    own, other = (dict(zip(far_first(sz.head_axis), side)) for side in (own, other))
    for d in range(sz.head_axis):
        cols = aligned((h ^ d) * sz.chunk, sz.chunk)
        dst[aligned(c * HALF, HALF), cols] = own[d]
        dst[aligned((1 - c) * HALF, HALF), cols] = other[d]


def line_of(table, at):
    line = lax.broadcasted_iota(jnp.int32, table.shape, 0)
    return jnp.sum(jnp.where(line == at, table, 0.0), axis=0, keepdims=True)


def conv_forward(sz, ext, taps):
    pre = taps[0:1] * ext[5 : 5 + BLOCK, :]
    for j in range(1, sz.taps):
        pre = pre + taps[j : j + 1] * ext[5 + j : 5 + j + BLOCK, :]
    return pre


def decay_of(sz, cols, rp, h, mask):
    rows = cols[:, h : h + 1] + rp[12 + h : 13 + h, :]
    return jnp.exp(jnp.where(mask, rows, HIDDEN))


def lower_mask():
    t = lax.broadcasted_iota(jnp.int32, (BLOCK, BLOCK), 0)
    s = lax.broadcasted_iota(jnp.int32, (BLOCK, BLOCK), 1)
    return t >= s


def forward_kernel(sz, layer, slots, sc, *refs):
    n = sz.head_axis
    sources = 2 * slots if layer == 0 else 2 * n + 2 * slots
    src, refs = refs[:sources], refs[sources:]
    if layer == 1:
        table, refs = refs[0], refs[1:]
    gains, given, halo, begin = refs[0:2], refs[2:8], refs[8], refs[9]
    refs = refs[10:]
    if layer == 1:
        ov, refs = refs[0], refs[1:]
    normed_o, gl_o, lin_o, ssd_o, inc_o, inv_o, part_o, unit_o, fin_o, sc_o, base_o = refs[:11]
    refs = refs[11:]
    if layer == 1:
        mixed_o, refs = refs[0], refs[1:]
    else:
        tables_o, refs = refs[0:2], refs[2:]
    xs, ms, wv, ext, state, sems = refs
    b = pl.program_id(0)
    c, h, k = sc[0], sc[1], sc[3]
    ch, st = sz.channels, sz.states
    copies = weight_copies(sz, layer, c, h, given, wv, sems)

    @pl.when(b == 0)
    def _():
        run_copies(copies, True, False)
        ext[0:8, :] = halo[...]
        state[...] = begin[...]
        for i in range(4):
            sc_o[i] = sc[i]

    mine = aligned(c * HALF, HALF)
    cols = aligned(h * sz.chunk, sz.chunk)
    if layer == 0:
        put_ordered(sz, xs, c, k, b, src[:slots], src[slots:])
        base_o[...] = xs[mine, cols]
        for r in range(slots):

            @pl.when(lax.rem(k - b + slots, slots) == r)
            def _(r=r):
                own = decay_table(rates_of(src[r]), c, sz.heads)
                other = decay_table(rates_of(src[slots + r]), c, sz.heads)
                tables_o[0][...] = pick(c == 0, own, other)
                tables_o[1][...] = pick(c == 0, other, own)

        rp = tables_o[0][...]
    else:
        put_pieces(sz, xs, c, h, [r[...] for r in src[:n]], [r[...] for r in src[n : 2 * n]])
        put_ordered(sz, ms, c, k, b, src[2 * n : 2 * n + slots], src[2 * n + slots :])
        base_o[...] = ms[mine, cols]
        mixed_o[...] = ms[...]
        rp = table[...]

    pv = pick(c == layer, gains[0][...], gains[1][...])
    x = xs[...].astype(F32)
    inv_in = lax.rsqrt(jnp.mean(x * x, axis=1, keepdims=True) + EPS)
    normed = (x * inv_in * pv[0:1, : sz.width]).astype(LOW)
    normed_o[...] = normed

    @pl.when(b == 0)
    def _():
        run_copies(copies, False, True)

    proj = dot(normed, wv[...], NN)
    gl = proj[:, :ch]
    gl_o[...] = gl
    lin = proj[:, ch:].astype(LOW)
    lin_o[...] = lin
    ext[8 : 8 + BLOCK, :] = lin.astype(F32)
    pre = conv_forward(sz, ext, pv[1:5, : sz.lin])
    ext[0:8, :] = ext[BLOCK : BLOCK + 8, :]
    act = (pre * sigmoid(pre)).astype(LOW)
    values, bm, cm = act[:, :ch], act[:, ch : ch + st], act[:, ch + st :]

    cols = jnp.transpose(rp)
    mask = lower_mask()
    gram = dot(cm, bm, NT)
    mixes, parts = [], []
    for i in range(sz.heads):
        mixes.append((gram * decay_of(sz, cols, rp, i, mask)).astype(LOW))
        parts.append(per_head(values, i, sz.head_width))
    intra = dot(jnp.concatenate(mixes, axis=1), jnp.concatenate(parts, axis=0), NN)

    low_state = state[...].astype(LOW)
    inc_o[0] = low_state
    ecum = spread(cols, sz.heads, sz.heads, sz.head_width)
    inter = dot(cm, low_state, NT) * ecum
    vf = values.astype(F32)
    carried = (vf * spread(cols, 2 * sz.heads, sz.heads, sz.head_width)).astype(LOW)
    local = dot(carried, bm, TN)
    for i in range(sz.heads):
        rows = slice(i * sz.head_width, (i + 1) * sz.head_width)
        total = cols[BLOCK - 1 : BLOCK, sz.heads + i : sz.heads + i + 1]
        state[rows, :] = total * state[rows, :] + local[rows]
    ssd = intra + inter + pv[6:7, :ch] * vf
    ssd_o[...] = ssd
    gated = ssd * (gl * sigmoid(gl))
    weighty = gated * pv[5:6, :ch]
    unit_o[...] = weighty.astype(LOW)

    lane = lax.broadcasted_iota(jnp.int32, (BLOCK, 128), 1)
    square = jnp.sum(gated * gated, axis=1, keepdims=True)
    if layer == 0:
        project = jnp.zeros_like(square)
    else:
        scaled_grad = dot(ms[...], ov[...], NN)
        project = jnp.sum(scaled_grad * weighty, axis=1, keepdims=True)
    stats = jnp.where(lane == 0, square, jnp.where(lane == 1, project, inv_in))
    stats = jnp.transpose(stats)
    part_o[...] = stats[0:2, :]
    inv_o[...] = stats[2:3, :]

    @pl.when(b == sz.blocks - 1)
    def _():
        fin_o[...] = state[...]


def scalar_lines(sz, lines):
    fill = [jnp.zeros((8 - sz.blocks, HALF), F32)] if sz.blocks < 8 else []
    high, low = split_low(jnp.concatenate(lines + fill, axis=0))
    table = jnp.concatenate([high, low], axis=0).astype(LOW)
    return jnp.concatenate([table] * (sz.chunk // HALF), axis=1)


def own_rows(sz, ref, which):
    blocks = [ref[aligned(b * BLOCK + which * HALF, HALF), :] for b in range(sz.blocks)]
    return jnp.concatenate(blocks, axis=0)


def project_kernel(sz, layer, deps, sc, unit_r, stats_r, *refs):
    given, refs = refs[:2], refs[2 + deps :]
    keep, send, sc_o, weights, sems = refs
    c, h = sc[0], sc[1]
    copies = out_copies(sz, layer, c, h, given, weights, sems)
    run_copies(copies, True, False)
    for i in range(4):
        sc_o[i] = sc[i]
    sides = []
    for which, out in ((c, keep), (1 - c, send)):
        sides.append((out, own_rows(sz, unit_r, which)))
        lines = [
            stats_r[0:1, aligned(b * BLOCK + which * HALF, HALF)] for b in range(sz.blocks)
        ]
        table = scalar_lines(sz, lines)
        for d in range(sz.head_axis):
            out[d, sz.rows :, :] = table
    run_copies(copies, False, True)
    for out, rows in sides:
        for d in range(sz.head_axis):
            chunk = weights[:, aligned((h ^ d) * sz.chunk, sz.chunk)]
            out[d, : sz.rows, :] = dot(rows, chunk, NN).astype(LOW)


def turn_kernel(sz, sc, *refs):
    given, given_out, refs = refs[:6], refs[6:8], refs[8:]
    wide_o, out_o, wv, ov, sems = refs[:2], refs[2:4], refs[4], refs[5], refs[6]
    for layer in range(2):
        copies = weight_copies(sz, layer, sc[0], sc[1], given, wv, sems)
        run_copies(copies, True, True)
        copies = out_copies(sz, layer, sc[0], sc[1], given_out, ov, sems)
        run_copies(copies, True, True)
        wide_o[layer][...] = jnp.transpose(wv[...])
        out_o[layer][...] = jnp.transpose(ov[...])


def out_at(out, d):
    return out[d] if isinstance(out, tuple) else out.at[d]


def lift_kernel(sz, layer, deps, sc, cat_r, normed_r, zero_gains, one_gains, small_r, *refs):
    weights, refs = refs[0], refs[1 + deps :]
    keep, send, sc_o, common_o, wide = refs[0], refs[1:-3], *refs[-3:]
    c, h = sc[0], sc[1]
    for i in range(4):
        sc_o[i] = sc[i]
    wide[...] = jnp.zeros_like(wide)
    for which, out in ((c, keep), (1 - c, send)):
        rows = own_rows(sz, cat_r, which)
        along = jnp.zeros((sz.rows, 1), F32)
        for d in range(sz.head_axis):
            cols = aligned((h ^ d) * sz.chunk, sz.chunk)
            product = dot(rows, weights[:, cols], NN)
            out_at(out, d)[: sz.rows, :] = product.astype(LOW)
            blocks = [
                normed_r[aligned(b * BLOCK + which * HALF, HALF), cols] for b in range(sz.blocks)
            ]
            product = product * jnp.concatenate(blocks, axis=0).astype(F32)
            wide[0:1, cols] += jnp.sum(product, axis=0, keepdims=True)
            along = along + jnp.sum(product, axis=1, keepdims=True)
        lines = [
            jnp.transpose(jnp.broadcast_to(along[b * HALF : (b + 1) * HALF], (HALF, 128)))[0:1, :]
            for b in range(sz.blocks)
        ]
        table = scalar_lines(sz, lines)
        for d in range(sz.head_axis):
            out_at(out, d)[sz.rows :, :] = table
    gain_grad = wide[0:1, :] / pick(c == layer, zero_gains[0:1, :], one_gains[0:1, :])
    flat = [small_r[j : j + 1, sz.channels :] for j in range(sz.taps)]
    flat += [gain_grad[:, q * sz.chunk : (q + 1) * sz.chunk] for q in range(sz.head_axis)]
    high, low = split_low(jnp.concatenate(flat, axis=0))
    common_o[...] = jnp.concatenate([high, low], axis=0).astype(LOW)


def backward_kernel(sz, layer, deps, sc, *refs):
    n = sz.head_axis
    sources = 2 * n + 2 if layer == 0 else 1 + n
    src, refs = refs[:sources], refs[sources:]
    gl_r, lin_r, ssd_r, inc_r = refs[:4]
    table, gains, ov = refs[4], refs[5:7], refs[7]
    halo, halo_grad, begin = refs[8:11]
    refs = refs[11 + deps :]
    cat_o, scaled_o, small_o, sums_o, fin_o, rim_o, sc_o = refs[:7]
    refs = refs[7:]
    if layer == 0:
        mixed_o, refs = refs[0], refs[1:]
    ms, ext, back, state, heads_p, small = refs
    i_step = pl.program_id(0)
    b = sz.blocks - 1 - i_step
    c, h = sc[0], sc[1]
    ch, st = sz.channels, sz.states
    pv = pick(c == layer, gains[0][...], gains[1][...])
    rp = table[...]

    @pl.when(i_step == 0)
    def _():
        back[BLOCK : BLOCK + 8, :] = halo_grad[...]
        state[...] = begin[...]
        small[...] = jnp.zeros_like(small)
        for i in range(4):
            sc_o[i] = sc[i]
        if layer == 0:
            for i in range(2):
                extra = src[i * n][sz.rows :, :].astype(F32)
                for d in range(1, n):
                    extra = extra + src[i * n + d][sz.rows :, :].astype(F32)
                heads_p[8 * i : 8 * i + 8, :] = extra[0:8, :HALF] + extra[8:16, :HALF]

    if layer == 0:
        rows = aligned(b * HALF, HALF)
        put_pieces(
            sz, ms, c, h, [r[rows, :] for r in src[:n]], [r[rows, :] for r in src[n : 2 * n]]
        )
        halves = []
        for k in range(2):
            alpha = lax.rsqrt(line_of(src[2 * n + k][...], b) / sz.inner + EPS)
            beta = alpha * alpha * line_of(heads_p[...], 8 * k + b) / sz.inner
            halves.append((alpha, beta))
        alpha, beta = (
            pick(
                c == 0,
                jnp.concatenate([halves[0][q], halves[1][q]], axis=1),
                jnp.concatenate([halves[1][q], halves[0][q]], axis=1),
            )
            for q in range(2)
        )
    else:
        stats = src[1][...]
        for d in range(1, n):
            stats = stats + src[1 + d][...]
        alpha = lax.rsqrt(stats[0:1, :] / sz.inner + EPS)
        beta = alpha * alpha * alpha * stats[1:2, :] / sz.inner

    sub = lax.broadcasted_iota(jnp.int32, rp.shape, 0)
    cols = jnp.transpose(jnp.where(sub == 12, alpha, jnp.where(sub == 13, beta, rp)))
    alpha, beta = cols[:, 12:13], cols[:, 13:14]

    gl = gl_r[...]
    ssd = ssd_r[...]
    sig = sigmoid(gl)
    swish = gl * sig
    slope = sig * (1.0 + gl * (1.0 - sig))
    gated = ssd * swish
    if layer == 0:
        mixed_grad = ms[...]
        mixed_o[...] = mixed_grad
    else:
        mixed_grad = src[0][...]
    scaled_grad = dot(mixed_grad, ov[...], NN)
    gain = pv[5:6, :ch]
    normal = gated * alpha
    small[4:5, :ch] += jnp.sum(scaled_grad * normal, axis=0, keepdims=True)
    scaled_o[...] = (normal * gain).astype(LOW)
    gated_grad = alpha * (scaled_grad * gain) - beta * gated
    ssd_grad = (gated_grad * swish).astype(LOW)
    gate_grad = (gated_grad * ssd * slope).astype(LOW)
    sgf = ssd_grad.astype(F32)

    before = lin_r[pl.ds(pl.multiple_of(jnp.maximum(b * BLOCK - 16, 0), 16), 16), :]
    ext[0:8, :] = pick(b > 0, before.astype(F32)[8:16, :], halo[...])
    ext[8 : 8 + BLOCK, :] = lin_r[aligned(b * BLOCK, BLOCK), :].astype(F32)
    taps = pv[1:5, : sz.lin]
    pre = conv_forward(sz, ext, taps)
    psig = sigmoid(pre)
    pact = pre * psig
    pslope = psig * (1.0 + pre * (1.0 - psig))
    act = pact.astype(LOW)
    values, bm, cm = act[:, :ch], act[:, ch : ch + st], act[:, ch + st :]
    vf = values.astype(F32)
    small[5:6, :ch] += jnp.sum(sgf * vf, axis=0, keepdims=True)

    mask = lower_mask()
    gram = dot(cm, bm, NT)
    gram_grad = jnp.zeros((BLOCK, BLOCK), F32)
    mixes, parts = [], []
    for i in range(sz.heads):
        decay = decay_of(sz, cols, rp, i, mask)
        mixes.append((gram * decay).astype(LOW))
        parts.append(per_head(ssd_grad, i, sz.head_width))
        gram_grad = gram_grad + dot(parts[-1], values, NT) * decay
    intra_grad = dot(jnp.concatenate(mixes, axis=0), jnp.concatenate(parts, axis=0), TN)

    ecum = spread(cols, sz.heads, sz.heads, sz.head_width)
    to_end = spread(cols, 2 * sz.heads, sz.heads, sz.head_width)
    inter_grad = (sgf * ecum).astype(LOW)
    low_state = state[...].astype(LOW)
    carried = (vf * to_end).astype(LOW)
    carried_grad = dot(bm, low_state, NT)
    gram_low = gram_grad.astype(LOW)
    b_grad = dot(gram_low, cm, TN) + dot(carried, low_state, NN)
    c_grad = dot(gram_low, bm, NN) + dot(inter_grad, inc_r[0], NN)
    value_grad = intra_grad + pv[6:7, :ch] * sgf + carried_grad * to_end
    entry = dot(inter_grad, cm, TN)
    for i in range(sz.heads):
        rows = slice(i * sz.head_width, (i + 1) * sz.head_width)
        total = cols[BLOCK - 1 : BLOCK, sz.heads + i : sz.heads + i + 1]
        state[rows, :] = total * state[rows, :] + entry[rows]

    pre_grad = jnp.concatenate([value_grad, b_grad, c_grad], axis=1) * pslope
    back[0:BLOCK, :] = pre_grad
    lin_grad = taps[0:1] * back[sz.taps - 1 : sz.taps - 1 + BLOCK, :]
    for j in range(1, sz.taps):
        at = sz.taps - 1 - j
        lin_grad = lin_grad + taps[j : j + 1] * back[at : at + BLOCK, :]
    for j in range(sz.taps):
        small[j : j + 1, :] += jnp.sum(pre_grad * ext[5 + j : 5 + j + BLOCK, :], axis=0, keepdims=True)
    back[BLOCK : BLOCK + 8, :] = back[0:8, :]
    cat_o[...] = jnp.concatenate([gate_grad, lin_grad.astype(LOW)], axis=1)

    @pl.when(i_step == sz.blocks - 1)
    def _():
        fin_o[...] = state[...]
        rim_o[...] = back[0:8, :]
        sums = small[...]
        flat = [sums[j : j + 1, :ch] for j in range(sz.taps + 2)]
        flat = [jnp.concatenate(flat[j : j + 3], axis=1) for j in range(0, len(flat), 3)]
        flat = flat + [jnp.zeros_like(flat[0])] * (4 - len(flat))
        high, low = split_low(jnp.concatenate(flat, axis=0))
        rest = jnp.zeros((PAD - 8, high.shape[1]), F32)
        small_o[...] = jnp.concatenate([high, low, rest], axis=0).astype(LOW)
        sums_o[...] = sums


def weights_kernel(sz, seq, deps, with_common, sc, normed, cat, mixed, scaled, small, *refs):
    if with_common:
        common, refs = refs[0], refs[1:]
    refs = refs[deps:]
    sc_o, outs, heads, full, wide = refs[0], refs[1 : seq + 1], refs[seq + 1 : -2], refs[-2], refs[-1]
    for i in range(4):
        sc_o[i] = sc[i]
    ch, st = sz.channels, sz.states
    step = sz.chunk
    for q in range(sz.head_axis):
        at = slice(q * step, (q + 1) * step)
        grads = dot(normed[:, at], cat[...], TN)
        full[at, : 2 * ch] = grads[:, : 2 * ch].astype(LOW)
        wide[at, :] = grads[:, 2 * ch :]
        full[at, 2 * ch :] = dot(mixed[:, at], scaled[...], TN).astype(LOW)
    rows = sz.width // seq
    part = rows // sz.head_axis
    for r, out in enumerate(outs):
        out[:rows, :] = full[aligned(lax.rem(sc[2] + r, seq) * rows, rows), :]
        out[rows:, :] = small[...]
    for d, out in enumerate(heads):
        lines = [
            wide[aligned(lax.rem(sc[2] + r, seq) * rows + (sc[1] ^ d) * part, part), :]
            for r in range(seq)
        ]
        if with_common:
            lines = [common[...].astype(F32)] + lines
        out[...] = jnp.concatenate(lines, axis=0).astype(LOW)


def resplit(extra):
    half = extra.shape[0] // 2
    high, low = split_low(extra[:half, :] + extra[half:, :])
    return jnp.concatenate([high, low], axis=0)


def join_kernel(sz, parts, riders, deps, sc, keep, *refs):
    n = sz.head_axis
    recv, refs = refs[0] if parts == 1 else refs[:parts], refs[parts:]
    more = [(refs[i * (n + 1)], refs[i * (n + 1) + 1 : (i + 1) * (n + 1)]) for i in range(riders)]
    refs = refs[riders * (n + 1) + deps :]
    sc_o, outs = refs[0], refs[1:]
    rows = sz.rows
    for i in range(4):
        sc_o[i] = sc[i]
    extra = resplit(keep[0, rows:, :].astype(F32) + out_at(recv, 0)[rows:, :].astype(F32))
    for d, out in enumerate(outs):
        both = keep[d, :rows, :].astype(F32) + out_at(recv, d)[:rows, :].astype(F32)
        out[:rows, :] = both.astype(out.dtype)
        out[rows : rows + PAD, :] = extra.astype(out.dtype)
        at = rows + PAD
        for common, rider in more:
            size = rider[d].shape[0]
            out[at : at + PAD, :] = common[...].astype(out.dtype)
            out[at + PAD : at + PAD + size, :] = rider[d][...].astype(out.dtype)
            at += PAD + size


def total_of(parts, rows):
    total = parts[0][rows, :].astype(F32)
    for p in parts[1:]:
        total = total + p[rows, :].astype(F32)
    return total


def output_kernel(sz, layer, sc, *refs):
    n = sz.head_axis
    parts, refs = refs[:n], refs[n:]
    resid = refs[0]
    res_o, low_o, mixed_o, square_o, sc_o = refs[-5:]
    for i in range(4):
        sc_o[i] = sc[i]
    extra = total_of(parts, slice(sz.rows, sz.rows + PAD))
    square = extra[0:8, :HALF] + extra[8:16, :HALF]
    square_o[...] = square
    inv = lax.rsqrt(square / sz.inner + EPS)
    for b in range(sz.blocks):
        rows = slice(b * HALF, (b + 1) * HALF)
        col = column_of(inv[b : b + 1, :], HALF)[:, 0:1]
        mixed = total_of(parts, rows) * col
        res = resid[rows, :].astype(F32) + mixed
        res_o[rows, :] = res
        low_o[rows, :] = res.astype(LOW)
        mixed_o[rows, :] = mixed


def input_kernel(sz, layer, sc, *refs):
    n = sz.head_axis
    parts, refs = refs[:n], refs[n:]
    resid, outg, inv_r, gains = refs[0], refs[1], refs[2], refs[3:5]
    refs = refs[5:]
    if layer == 1:
        mixed = refs[0]
        grad_o, low_o, sc_o = refs[-3:]
    else:
        one_low, one_heads = refs[0], refs[1 : 1 + n]
        low_o, swap_o, shared_o, sc_o = refs[-4:]
    for i in range(4):
        sc_o[i] = sc[i]
    c, h = sc[0], sc[1]
    first = c == 0
    mine = aligned(h * sz.chunk, sz.chunk)
    gain = pick(c == layer, gains[0][0:1, mine], gains[1][0:1, mine])
    extra = total_of(parts, slice(sz.rows, sz.rows + PAD))
    along = extra[0:8, :HALF] + extra[8:16, :HALF]
    tops, lows = [], []
    for b in range(sz.blocks):
        rows = slice(b * HALF, (b + 1) * HALF)
        at = b * BLOCK
        inv_row = pick(c == 0, inv_r[:, at : at + HALF], inv_r[:, at + HALF : at + BLOCK])
        inv = column_of(inv_row, HALF)[:, 0:1]
        share = column_of(along[b : b + 1, :] / sz.width, HALF)[:, 0:1]
        total = total_of(parts, rows)
        base = resid[rows, :].astype(F32)
        grad = outg[rows, :].astype(F32) + inv * (total * gain - base * (inv * share))
        low = grad.astype(LOW)
        low_o[rows, :] = low
        if layer == 0:
            swap_o[rows, :] = pick(first, one_low[rows, :], low)
        else:
            grad_o[rows, :] = grad
            dots = jnp.sum(low.astype(F32) * mixed[rows, :], axis=1, keepdims=True)
            row = jnp.transpose(jnp.broadcast_to(dots, (HALF, 128)))[0:1, :]
            high, rest = split_low(row)
            tops.append(high)
            lows.append(rest)
    if layer == 1:
        fill = [jnp.zeros((8 - sz.blocks, HALF), F32)] if sz.blocks < 8 else []
        extra = jnp.concatenate(tops + fill + lows + fill, axis=0)
        extra = jnp.concatenate([extra] * (sz.chunk // HALF), axis=1)
        low_o[sz.rows :, :] = extra.astype(LOW)
    else:
        size = shared_o.shape[0]
        at = sz.rows + PAD
        zero = total_of(parts, slice(at, at + size))
        one = total_of(one_heads, slice(None))
        zero, one = (jnp.concatenate([resplit(v[:PAD]), v[PAD:]], axis=0) for v in (zero, one))
        shared_o[...] = pick(first, zero, one)
        swap_o[sz.rows :, :] = pick(first, one, zero).astype(LOW)


def sum_kernel(sz, last, deps, sc, *refs):
    refs = refs[deps:]
    if last:
        parts, done, outs = refs[:-3], refs[-3], refs[-2:]
    else:
        parts, outs = refs[:-1], refs[-1:]
    rows = outs[0].shape[0] - PAD
    total = total_of(parts, slice(None))
    extra = total[rows:]
    high, low = split_low(extra[0:4, :] + extra[4:8, :])
    extra = jnp.concatenate([high, low, jnp.zeros((PAD - 8, extra.shape[1]), F32)], axis=0)
    sums = jnp.concatenate([total[:rows], extra], axis=0).astype(LOW)
    if last:
        outs[0][...] = pick(sc[0] == 0, sums, done[...])
        outs[1][...] = pick(sc[0] == 0, done[...], sums)
    else:
        outs[0][...] = sums


def final_kernel(sz, seq, sc, own, got, *refs):
    pieces, refs = refs[:-9], refs[-9:]
    gate_o, inner_o, out_o, conv_o, norm_o, skip_o, shared_o, taps_o, gain_o = refs
    c = sc[0]
    ch = sz.channels
    rows = own.shape[0] - PAD
    lane = lax.broadcasted_iota(jnp.int32, skip_o.shape, 1)
    skip = jnp.zeros(skip_o.shape, F32)
    for i in range(2):
        which = pick(i == 0, c, 1 - c)
        to = aligned(which * ch, ch)
        sums = (own if i == 0 else got)[...].astype(F32)
        gate_o[:, to] = sums[:rows, :ch]
        inner_o[:, to] = sums[:rows, ch : 2 * ch]
        out_o[to, :] = jnp.transpose(sums[:rows, 2 * ch :])
        lines = sums[rows : rows + 4, :] + sums[rows + 4 : rows + 8, :]
        for j in range(sz.taps):
            conv_o[j : j + 1, to] = lines[j // 3 : j // 3 + 1, (j % 3) * ch : (j % 3 + 1) * ch]
        norm_o[:, to] = lines[1:2, ch : 2 * ch]
        skips = lines[1:2, 2 * ch :]
        for q in range(sz.heads):
            part = jnp.sum(per_head(skips, q, sz.head_width), axis=1, keepdims=True)
            skip = jnp.where(lane == which * sz.heads + q, part, skip)
    skip_o[...] = skip
    total = total_of(pieces, slice(BLOCK, None))
    shared_o[...] = total[PAD:]
    common = total[: PAD // 2] + total[PAD // 2 : PAD]
    place = sc[2] * sz.head_axis + sc[1]
    span = common.shape[1]
    size = span // (seq * sz.head_axis)
    turned = pltpu.roll(common, lax.rem(span - place * size, span), 1)
    taps_o[...] = turned[: sz.taps, :size]
    size = sz.width // (seq * sz.head_axis)
    at = place * size
    line = jnp.broadcast_to(line_of(common, sz.taps + at // span), common.shape)
    turned = pltpu.roll(line, lax.rem(span - lax.rem(at, span), span), 1)
    gain_o[...] = turned[:1, :size]


def slice_kernel(sz, slots, sc, order, tokens, rates, *refs):
    outs, sc_o, sems = refs[:slots], refs[slots], refs[slots + 1]
    copies = []
    for r in range(slots):
        rows = tokens.at[order[lax.rem(sc[3] + r, slots)], aligned(sc[0] * HALF, HALF), :]
        copies.append(pltpu.make_async_copy(rows, outs[r].at[:HALF], sems.at[r]))
    for copy in copies:
        copy.start()
    for i in range(4):
        sc_o[i] = sc[i]
    for r in range(slots):
        first, rest = split_low(rates[0, order[lax.rem(sc[3] + r, slots)]])
        second, rest = split_low(rest)
        lines = jnp.concatenate([first, second, rest, jnp.zeros_like(rest)], axis=1)
        lines = jnp.concatenate([lines, jnp.zeros_like(lines)], axis=0)
        outs[r][HALF:, :] = lines.astype(LOW)
    for copy in copies:
        copy.wait()


def rates_of(piece):
    lines = piece[HALF:, :].astype(F32)[:8, :]
    return (lines[:, :BLOCK] + lines[:, BLOCK : 2 * BLOCK]) + lines[:, 2 * BLOCK : 3 * BLOCK]


def pack_kernel(sz, sc, order, grads, gate, inner, out, in_gain, conv_i, conv_s, skip, norm, *refs):
    gate_o, inner_o, o_o, mine_o, send_o, sems = *refs[:5], refs[-1]
    c, h = sc[0], sc[1]
    ch = sz.channels
    outs = refs[5:-1]
    slices = []
    for r, to in enumerate(outs):
        rows = grads.at[order[lax.rem(sc[3] + r, len(outs))], aligned(c * HALF, HALF), :]
        slices.append(pltpu.make_async_copy(rows, to, sems.at[3 + r]))
    cols = aligned((1 - c) * ch, ch)
    rows = aligned((h * 2 + 1 - c) * ch, ch)
    copies = [
        pltpu.make_async_copy(gate.at[0, :, cols], gate_o, sems.at[0]),
        pltpu.make_async_copy(inner.at[0, :, cols], inner_o, sems.at[1]),
        pltpu.make_async_copy(out.at[0, rows, :], o_o, sems.at[2]),
        *slices,
    ]
    for copy in copies:
        copy.start()
    for which, ref in ((c, mine_o), (1 - c, send_o)):
        at = aligned(which * ch, ch)
        ref[...] = jnp.zeros_like(ref)
        ref[0:1, :] = in_gain[...]
        ref[1 : 1 + sz.taps, :ch] = conv_i[0, :, at]
        ref[1 : 1 + sz.taps, ch : sz.lin] = conv_s[0]
        ref[5:6, :ch] = norm[:, at]
        low = spread(skip[...], 0, sz.heads, sz.head_width)
        high = spread(skip[...], sz.heads, sz.heads, sz.head_width)
        ref[6:7, :ch] = pick(which == 0, low, high)
    for copy in copies:
        copy.wait()


def decay_table(rate, c, n):
    lane = lax.broadcasted_iota(jnp.int32, rate.shape, 1)
    cum = rate
    step = 1
    while step < BLOCK:
        cum = cum + jnp.where(lane >= step, pltpu.roll(cum, step, 1), 0.0)
        step *= 2
    end = cum[:, BLOCK - 1 :]
    lines = [cum, jnp.exp(cum), jnp.exp(end - cum) * -rate, jnp.log(-rate) - cum]
    low = jnp.concatenate([v[:n] for v in lines], axis=0)
    high = jnp.concatenate([v[n:] for v in lines], axis=0)
    return pick(c == 0, low, high)


def leave_kernel(sz, slots, riders, sc, zero_own, zero_other, one_own, one_other, *refs):
    c = sc[0]
    if riders:
        shared, refs = refs[0], refs[1:]
        total = shared[...] + one_other[sz.rows :, :].astype(F32)
        extra = resplit(total[:PAD])
        part = (total.shape[0] - PAD) // riders
    outs = refs[:slots]
    for i in range(4):
        refs[slots][i] = sc[i]
    for r in range(slots):
        rows = aligned(lax.rem(sc[3] + r, slots) * HALF, HALF)
        own = pick(c == 0, zero_own[rows, :], one_own[rows, :])
        other = pick(c == 0, zero_other[rows, :], one_other[rows, :])
        put_pair(outs[r], c, own, other)
        if riders:
            lines = [extra, total[PAD + r * part : PAD + (r + 1) * part]]
            outs[r][BLOCK:, :] = jnp.concatenate(lines, axis=0).astype(LOW)


def home_kernel(slots, sc, *refs):
    early, late, out, grad = refs[:slots], refs[slots : 2 * slots], refs[-3], refs[-2]
    for i in range(4):
        refs[-1][i] = sc[i]
    first = sc[0] == 0
    for r in range(slots):
        at = lax.rem(sc[3] - r + slots, slots)
        out[at] = pick(first, early[r][...], late[r][:BLOCK, :]).astype(F32)
        grad[at] = pick(first, late[r][:BLOCK, :], early[r][...]).astype(F32)


def whole(shape):
    return pl.BlockSpec(shape, lambda *_: (0,) * len(shape))


def per_device(
    tokens,
    slot_order,
    log_decay,
    grad_out,
    in_gain,
    w_gate,
    w_inner,
    w_shared,
    conv_inner,
    conv_shared,
    d_skip,
    norm_gain,
    w_out,
):
    slots = tokens.shape[0]
    span = tokens.shape[1]
    width = tokens.shape[2]
    seq = lax.axis_size("seq")
    head_axis = lax.axis_size("head")
    cores = lax.axis_size("section")
    spans = seq // slots
    c = lax.axis_index("section")
    z = lax.axis_index("seq")
    h = lax.axis_index("head")
    k = lax.rem(z, slots)
    inner_dev = w_gate.shape[2]
    channels = inner_dev // cores
    shared = w_shared.shape[2]
    heads_dev = d_skip.shape[1]
    taps = conv_inner.shape[1]
    sz = Sizes(
        slots * span // BLOCK,
        width,
        channels,
        heads_dev // cores,
        shared // 2,
        taps,
        head_axis,
        inner_dev * head_axis,
    )
    first = c == 0
    swap = [(0, 1), (1, 0)]
    nb, tok, rows, chunk = sz.blocks, sz.tokens, sz.rows, sz.chunk

    def cross(x):
        return lax.ppermute(x, "section", swap)

    def turn(x, r):
        pairs = [(i, i // slots * slots + (i % slots + r) % slots) for i in range(seq)]
        return lax.ppermute(x, "seq", pairs) if r else x

    def over_heads(x, d):
        return x if d == 0 else lax.ppermute(x, "head", [(i, i ^ d) for i in range(head_axis)])

    def next_span(x, way):
        pairs = [(i, i + way * slots) for i in range(seq) if 0 <= i + way * slots < seq]
        return lax.ppermute(x, "seq", pairs)

    def shape(dims, dtype):
        return jax.ShapeDtypeStruct(dims, dtype)

    prefetch = functools.partial(pltpu.PrefetchScalarGridSpec, num_scalar_prefetch=1)
    options = pltpu.CompilerParams(vmem_limit_bytes=VMEM_BYTES)
    from_hbm = pltpu.CompilerParams(vmem_limit_bytes=ALL_VMEM_BYTES)
    anywhere = pl.BlockSpec(memory_space=pl.ANY)
    smem = pl.BlockSpec(memory_space=pltpu.SMEM)
    vmem = pl.BlockSpec(memory_space=pltpu.VMEM)
    index_shape = shape((4,), jnp.int32)

    def cost(flops, moved):
        return pl.CostEstimate(flops=int(flops), bytes_accessed=int(moved), transcendentals=0)

    def to_members(pieces):
        return [turn(x, r) for r, x in enumerate(pieces)]

    sc = jnp.stack([c, h, z, k]).astype(jnp.int32)
    *tok_slices, sc = pl.pallas_call(
        functools.partial(slice_kernel, sz, slots),
        in_specs=[smem, smem, anywhere, vmem],
        out_specs=[vmem] * slots + [smem],
        out_shape=[shape((HALF + PAD, width), LOW)] * slots + [index_shape],
        scratch_shapes=[pltpu.SemaphoreType.DMA((slots,))],
        compiler_params=from_hbm,
    )(sc, slot_order, tokens, log_decay)
    tok_pieces = to_members(tok_slices)
    tok_others = [cross(x) for x in tok_pieces]

    wide = 2 * channels + shared
    gate_sent, inner_sent, o_sent, pv_mine, pv_sent, *out_slices = pl.pallas_call(
        functools.partial(pack_kernel, sz),
        in_specs=[smem, smem] + [anywhere] * 4 + [vmem] * 5,
        out_specs=[vmem] * (5 + slots),
        out_shape=[
            shape((width, channels), LOW),
            shape((width, channels), LOW),
            shape((channels, width), LOW),
            shape((16, width), F32),
            shape((16, width), F32),
        ]
        + [shape((HALF, width), LOW)] * slots,
        scratch_shapes=[pltpu.SemaphoreType.DMA((3 + slots,))],
        compiler_params=from_hbm,
    )(
        sc, slot_order, grad_out, w_gate, w_inner, w_out,
        in_gain, conv_inner, conv_shared, d_skip, norm_gain,
    )
    sent = [cross(x) for x in (gate_sent, inner_sent, w_shared[0], o_sent)]
    gains = [pv_mine, cross(pv_sent)]

    def span_total(table):
        ends = table[: sz.heads, BLOCK - 1 :: BLOCK]
        return jnp.repeat(jnp.exp(jnp.sum(ends, axis=1)), sz.head_width)[:, None]

    parts_shape = shape((head_axis, rows + PAD, chunk), LOW)
    in_weights = [w_gate, w_inner, w_shared, *sent[:3]]
    last_weights = [w_out, sent[3]]
    wide_weights = pltpu.VMEM((width, wide), LOW)
    out_weights = pltpu.VMEM((channels, width), LOW)
    copy_sems = pltpu.SemaphoreType.DMA((4,))
    dense = 2 * tok * width * (wide + channels)

    def forward(layer, sc, sources):
        def at(b, _):
            return (b, 0)

        piece = pl.BlockSpec((HALF, chunk), at)
        table = pl.BlockSpec((16, BLOCK), lambda b, _: (0, b))
        if layer == 0:
            src_specs = [whole((HALF + PAD, width))] * (2 * slots)
            more_specs = [table, table]
            more_shapes = [shape((16, tok), F32)] * 2
        else:
            src_specs = [piece] * (2 * head_axis) + [whole((HALF, width))] * (2 * slots) + [table]
            more_specs = [pl.BlockSpec((BLOCK, width), at)]
            more_shapes = [shape((tok, width), LOW)]

        last = [] if layer == 0 else [turned[3]]

        def call(halo, begin):
            return pl.pallas_call(
                functools.partial(forward_kernel, sz, layer, slots),
                grid_spec=prefetch(
                    grid=(nb,),
                    in_specs=src_specs
                    + [whole((16, width)), whole((16, width))]
                    + [anywhere] * len(in_weights)
                    + [whole((8, sz.lin)), whole((channels, sz.states))]
                    + [whole(x.shape) for x in last],
                    out_specs=[
                        pl.BlockSpec((BLOCK, width), at),
                        pl.BlockSpec((BLOCK, channels), at),
                        pl.BlockSpec((BLOCK, sz.lin), at),
                        pl.BlockSpec((BLOCK, channels), at),
                        pl.BlockSpec((1, channels, sz.states), lambda b, _: (b, 0, 0)),
                        pl.BlockSpec((1, BLOCK), lambda b, _: (0, b)),
                        pl.BlockSpec((2, BLOCK), lambda b, _: (0, b)),
                        pl.BlockSpec((BLOCK, channels), at),
                        whole((channels, sz.states)),
                        smem,
                        piece,
                    ]
                    + more_specs,
                    scratch_shapes=[
                        pltpu.VMEM((BLOCK, width), LOW),
                        pltpu.VMEM((BLOCK, width), LOW),
                        wide_weights,
                        pltpu.VMEM((BLOCK + 8, sz.lin), F32),
                        pltpu.VMEM((channels, sz.states), F32),
                        copy_sems,
                    ],
                ),
                out_shape=[
                    shape((tok, width), LOW),
                    shape((tok, channels), F32),
                    shape((tok, sz.lin), LOW),
                    shape((tok, channels), F32),
                    shape((nb, channels, sz.states), LOW),
                    shape((1, tok), F32),
                    shape((2, tok), F32),
                    shape((tok, channels), LOW),
                    shape((channels, sz.states), F32),
                    index_shape,
                    shape((rows, chunk), LOW),
                ]
                + more_shapes,
                compiler_params=options,
                cost_estimate=cost(6 * dense, 16e6),
            )(sc, *sources, *gains, *in_weights, halo, begin, *last)

        halo = jnp.zeros((8, sz.lin), F32)
        begin = jnp.zeros((channels, sz.states), F32)
        if spans == 1:
            return call(halo, begin), halo
        trial = call(halo, begin)
        halo = next_span(trial[2][tok - 8 :].astype(F32), 1)
        local = call(halo, begin)[8]
        total = span_total(trial[11] if layer == 0 else sources[-1])
        for _ in range(spans - 1):
            begin = next_span(total * begin + local, 1)
        return call(halo, begin), halo

    def backward(layer, sc, sources, saved, decays, halo, deps):
        def at(i, _):
            return (nb - 1 - i, 0)

        if layer == 0:
            src_specs = [whole(s.shape) for s in sources]
        else:
            stat = pl.BlockSpec((2, BLOCK), lambda i, _: (0, nb - 1 - i))
            src_specs = [pl.BlockSpec((BLOCK, width), at)] + [stat] * head_axis
        gl, lin, ssd, inc = saved
        mixed_spec = [pl.BlockSpec((BLOCK, width), at)] if layer == 0 else []
        mixed_shape = [shape((tok, width), LOW)] if layer == 0 else []

        def call(halo_grad, begin):
            return pl.pallas_call(
                functools.partial(backward_kernel, sz, layer, len(deps)),
                grid_spec=prefetch(
                    grid=(nb,),
                    in_specs=src_specs
                    + [
                        pl.BlockSpec((BLOCK, channels), at),
                        whole(lin.shape),
                        pl.BlockSpec((BLOCK, channels), at),
                        pl.BlockSpec((1, channels, sz.states), lambda i, _: (nb - 1 - i, 0, 0)),
                        pl.BlockSpec((16, BLOCK), lambda i, _: (0, nb - 1 - i)),
                        whole((16, width)),
                        whole((16, width)),
                        whole((width, channels)),
                        whole((8, sz.lin)),
                        whole((8, sz.lin)),
                        whole((channels, sz.states)),
                    ]
                    + [anywhere] * len(deps),
                    out_specs=[
                        pl.BlockSpec((BLOCK, wide), at),
                        pl.BlockSpec((BLOCK, channels), at),
                        whole((PAD, 3 * channels)),
                        whole((8, sz.lin)),
                        whole((channels, sz.states)),
                        whole((8, sz.lin)),
                        smem,
                    ]
                    + mixed_spec,
                    scratch_shapes=[
                        pltpu.VMEM((BLOCK, width), LOW),
                        pltpu.VMEM((BLOCK + 8, sz.lin), F32),
                        pltpu.VMEM((BLOCK + 8, sz.lin), F32),
                        pltpu.VMEM((channels, sz.states), F32),
                        pltpu.VMEM((PAD, HALF), F32),
                        pltpu.VMEM((8, sz.lin), F32),
                    ],
                ),
                out_shape=[
                    shape((tok, wide), LOW),
                    shape((tok, channels), LOW),
                    shape((PAD, 3 * channels), LOW),
                    shape((8, sz.lin), F32),
                    shape((channels, sz.states), F32),
                    shape((8, sz.lin), F32),
                    index_shape,
                ]
                + mixed_shape,
                compiler_params=options,
                cost_estimate=cost(8 * dense, 16e6),
            )(
                sc, *sources, gl, lin, ssd, inc, decays, *gains, turned[2 + layer],
                halo, halo_grad, begin, *deps,
            )

        halo_grad = jnp.zeros((8, sz.lin), F32)
        begin = jnp.zeros((channels, sz.states), F32)
        if spans == 1:
            return call(halo_grad, begin)
        local = call(halo_grad, begin)[4]
        for _ in range(spans - 1):
            begin = next_span(span_total(decays) * begin + local, -1)
        halo_grad = next_span(call(halo_grad, begin)[5], -1)
        return call(halo_grad, begin)

    def project(layer, sc, unit, stats, deps):
        return pl.pallas_call(
            functools.partial(project_kernel, sz, layer, len(deps)),
            in_specs=[smem, vmem, vmem] + [anywhere] * (2 + len(deps)),
            out_specs=[vmem, vmem, smem],
            out_shape=[parts_shape, parts_shape, index_shape],
            scratch_shapes=[out_weights, copy_sems],
            compiler_params=options,
            cost_estimate=cost(dense / 4, 4e6),
        )(sc, unit, stats, *last_weights, *deps)

    def lift(layer, sc, cat, normed, small, deps):
        outs = pl.pallas_call(
            functools.partial(lift_kernel, sz, layer, len(deps)),
            in_specs=[smem] + [vmem] * 6 + [anywhere] * len(deps),
            out_specs=[vmem] * (1 + head_axis) + [smem, vmem],
            out_shape=[parts_shape]
            + [shape(parts_shape.shape[1:], LOW)] * head_axis
            + [index_shape, shape((PAD, chunk), LOW)],
            scratch_shapes=[pltpu.VMEM((8, width), F32)],
            compiler_params=options,
            cost_estimate=cost(dense, 8e6),
        )(sc, cat, normed, *gains, small, turned[layer], *deps)
        return outs[0], list(outs[1:-2]), outs[-2], outs[-1]

    def scatter(sc, keep, send, riders=(), deps=()):
        size = rows + PAD + sum(PAD + rider[1].shape[0] for rider in riders)
        flat = [x for rider in riders for x in rider]
        got = [cross(x) for x in (send if isinstance(send, list) else [send])]
        joined = pl.pallas_call(
            functools.partial(join_kernel, sz, len(got), len(riders), len(deps)),
            in_specs=[smem] + [vmem] * (1 + len(got) + len(flat)) + [anywhere] * len(deps),
            out_specs=[smem] + [vmem] * head_axis,
            out_shape=[index_shape, shape((size, chunk), F32)]
            + [shape((size, chunk), LOW)] * (head_axis - 1),
            compiler_params=options,
        )(sc, keep, *got, *flat, *deps)
        return [over_heads(joined[1 + d], d) for d in far_first(head_axis)], joined[0]

    def gather(low):
        own = [over_heads(low, d) for d in far_first(head_axis)]
        return own + [cross(x) for x in own]

    turned = pl.pallas_call(
        functools.partial(turn_kernel, sz),
        in_specs=[smem] + [anywhere] * 8,
        out_specs=[vmem] * 4,
        out_shape=[shape((wide, width), LOW)] * 2 + [shape((width, channels), LOW)] * 2,
        scratch_shapes=[wide_weights, out_weights, copy_sems],
        compiler_params=options,
        cost_estimate=cost(1e9, 8e6),
    )

    def section_output(layer, sc, parts, resid, deps=()):
        return pl.pallas_call(
            functools.partial(output_kernel, sz, layer),
            in_specs=[smem] + [vmem] * (head_axis + 1) + [anywhere] * len(deps),
            out_specs=[vmem] * 4 + [smem],
            out_shape=[
                shape((rows, chunk), F32),
                shape((rows, chunk), LOW),
                shape((rows, chunk), F32),
                shape((8, HALF), F32),
                index_shape,
            ],
            compiler_params=options,
        )(sc, *parts, resid, *deps)

    part = width // seq
    columns = 3 * channels
    share = part // head_axis
    shared_size = seq * share + PAD

    def section_input(layer, sc, parts, *others, deps=()):
        if layer == 0:
            outs = [
                shape((rows + PAD, chunk), LOW),
                shape((rows + shared_size, chunk), LOW),
                shape((shared_size, chunk), F32),
            ]
        else:
            outs = [shape((rows, chunk), F32), shape((rows + PAD, chunk), LOW)]
        return pl.pallas_call(
            functools.partial(input_kernel, sz, layer),
            in_specs=[smem] + [vmem] * (head_axis + len(others)) + [anywhere] * len(deps),
            out_specs=[vmem] * len(outs) + [smem],
            out_shape=outs + [index_shape],
            compiler_params=options,
        )(sc, *parts, *others, *deps)

    def weight_grads(sc, normed, cat, mixed, scaled, small, deps=(), common=None):
        more = [] if common is None else [common]
        size = seq * share + PAD * len(more)
        outs = pl.pallas_call(
            functools.partial(weights_kernel, sz, seq, len(deps), bool(more)),
            in_specs=[smem] + [vmem] * (5 + len(more)) + [anywhere] * len(deps),
            out_specs=[smem] + [vmem] * (seq + head_axis),
            out_shape=[index_shape]
            + [shape((part + PAD, columns), LOW)] * seq
            + [shape((size, shared), LOW)] * head_axis,
            scratch_shapes=[pltpu.VMEM((width, columns), LOW), pltpu.VMEM((width, shared), F32)],
            compiler_params=options,
            cost_estimate=cost(4 * dense, 12e6),
        )(sc, normed, cat, mixed, scaled, small, *more, *deps)
        return over_seq(outs[1 : 1 + seq]), outs[1 + seq :], outs[0]

    def shifted(x, r):
        return lax.ppermute(x, "seq", [(i, (i + r) % seq) for i in range(seq)]) if r else x

    def over_seq(chunks):
        return [shifted(x, r) for r, x in enumerate(chunks)]

    def leave(sc, *arrays, riders=0):
        size = BLOCK + (share + PAD if riders else 0)
        pieces = pl.pallas_call(
            functools.partial(leave_kernel, sz, slots, riders),
            in_specs=[smem] + [vmem] * len(arrays),
            out_specs=[vmem] * slots + [smem],
            out_shape=[shape((size, chunk), LOW)] * slots + [index_shape],
            compiler_params=options,
        )(sc, *arrays)
        return to_members(pieces[:slots]), pieces[slots]

    out_pieces = to_members(out_slices)
    fw0, halo0 = forward(0, sc, tok_pieces + tok_others)
    base0, decays = fw0[10], fw0[11:13]
    pr0 = project(0, fw0[9], fw0[7], fw0[6], [out_pieces[1], out_pieces[-1]])
    out_others = [cross(x) for x in out_pieces]
    parts, sc_join = scatter(sc, pr0[0], pr0[1])
    turned = turned(sc_join, *in_weights, *last_weights)
    res1, low1, mixed0, square0, unused = section_output(0, sc, parts, base0, turned)
    pieces1 = gather(low1)
    square_other = cross(square0)

    fw1, halo1 = forward(1, sc, pieces1 + out_pieces + out_others + [decays[1]])
    stat = fw1[6] + cross(fw1[6])
    stats = [stat] + [over_heads(stat, d) for d in range(1, head_axis)]
    pr1 = project(1, fw1[9], fw1[7], fw1[6], [])
    parts_out, sc_out = scatter(sc, pr1[0], pr1[1])
    bw1 = backward(1, sc_out, [fw1[11]] + stats, fw1[1:5], decays[1], halo1, [])
    lf1 = lift(1, bw1[6], bw1[0], fw1[0], bw1[3], parts_out[1:])
    weights1, heads1, sc_weights = weight_grads(
        lf1[2], fw1[0], bw1[0], fw1[11], bw1[1], bw1[2], common=lf1[3]
    )
    parts, sc_join = scatter(sc_weights, lf1[0], lf1[1])
    igrad1, glow1, sc_in = section_input(
        1, sc_join, parts, res1, fw1[10], fw1[5], *gains, mixed0,
        deps=weights1[2:-1],
    )
    piecesg = gather(glow1)

    heads1 = [over_heads(heads1[d], d) for d in far_first(head_axis)]

    early, unused = leave(sc_in, low1, pieces1[head_axis], glow1, piecesg[head_axis])
    bw0 = backward(
        0, sc, piecesg + [square0, square_other], fw0[1:5], decays[0], halo0,
        weights1[1:2],
    )
    weights0, heads0, sc_weights = weight_grads(
        bw0[6], fw0[0], bw0[0], bw0[7], bw0[1], bw0[2], deps=early[1:] + weights1[-1:],
    )
    lf0 = lift(0, sc_weights, bw0[0], fw0[0], bw0[3], heads1[1:])
    parts, sc_join = scatter(lf0[2], lf0[0], lf0[1], [[lf0[3], *heads0]], weights0[1:2])

    def summed(sc, pieces, *done, deps=()):
        return pl.pallas_call(
            functools.partial(sum_kernel, sz, bool(done), len(deps)),
            in_specs=[smem] + [anywhere] * len(deps) + [vmem] * (len(pieces) + len(done)),
            out_shape=[shape((part + PAD, columns), LOW)] * (1 + len(done)),
            compiler_params=options,
        )(sc, *deps, *pieces, *done)

    sums1 = summed(sc_in, weights1)
    unused, low2, unused_mixed, unused_square, sc_out = section_output(1, sc_in, parts_out, res1)
    glow0, to_other, shared_own, sc_end = section_input(
        0, sc_out, parts, base0, igrad1, fw0[5], *gains, low2, *heads1,
        deps=[*weights0[2:], *sums1],
    )
    got = cross(to_other)
    if spans == 1:
        late, sc_end = leave(sc_end, glow0, got, low2, got, shared_own, riders=seq)
        shared_parts = late
    else:
        late, sc_end = leave(sc_end, glow0, got, low2, got)
        total = shared_own + got[rows:].astype(F32)
        extra = resplit(total[:PAD])
        fill = jnp.zeros((BLOCK, shared), F32)
        chunks = [
            jnp.concatenate([fill, extra, total[PAD + r * share : PAD + (r + 1) * share]])
            for r in range(seq)
        ]
        shared_parts = over_seq([x.astype(LOW) for x in chunks])
    own_sums, other_sums = summed(sc_end, weights0, *sums1)
    final = pl.pallas_call(
        functools.partial(final_kernel, sz, seq),
        in_specs=[smem] + [vmem] * (2 + seq),
        out_shape=[
            shape((part, inner_dev), F32),
            shape((part, inner_dev), F32),
            shape((inner_dev, part), F32),
            shape((taps, inner_dev), F32),
            shape((1, inner_dev), F32),
            shape((1, heads_dev), F32),
            shape((share, shared), F32),
            shape((taps, shared // (seq * head_axis)), F32),
            shape((1, width // (seq * head_axis)), F32),
        ],
        compiler_params=options,
    )(sc, own_sums, cross(other_sums), *shared_parts)
    section_out, input_grad, unused = pl.pallas_call(
        functools.partial(home_kernel, slots),
        in_specs=[smem] + [vmem] * (2 * slots),
        out_specs=[vmem, vmem, smem],
        out_shape=[shape((slots, BLOCK, chunk), F32)] * 2 + [index_shape],
        compiler_params=options,
    )(sc, *early, *late)

    return (
        section_out[None],
        input_grad[None],
        final[8],
        final[0][None],
        final[1][None],
        final[6][None],
        final[3][None],
        final[7][None],
        final[5],
        final[4],
        final[2][None],
    )


def solution(mesh):
    placed = (
        P(None, "seq", None),
        P(),
        P("section", None, "head", "seq"),
        P(None, "seq", None),
        P("section", None),
        P("section", None, "head"),
        P("section", None, "head"),
        P("section", None, None),
        P("section", None, "head"),
        P("section", None, None),
        P("section", "head"),
        P("section", "head"),
        P("section", None, None),
    )
    return jax.shard_map(
        per_device,
        mesh=mesh,
        in_specs=placed,
        out_specs=(
            P("section", None, "seq", "head"),
            P("section", None, "seq", "head"),
            P("section", ("seq", "head")),
            P("section", "seq", "head"),
            P("section", "seq", "head"),
            P("section", ("seq", "head"), None),
            P("section", None, "head"),
            P("section", None, ("seq", "head")),
            P("section", "head"),
            P("section", "head"),
            P("section", "head", "seq"),
        ),
        check_vma=False,
    )
```

```python
import functools

import jax
import jax.numpy as jnp
from jax import lax
from jax.experimental import pallas as pl
from jax.experimental.pallas import tpu as pltpu
from jax.sharding import PartitionSpec as P

BLOCK = 256
HALF = BLOCK // 2
PAD = 16
EPS = 1e-05
F32 = jnp.float32
LOW = jnp.bfloat16
HIDDEN = -1e30
NN = ((1,), (0,))
NT = ((1,), (1,))
TN = ((0,), (0,))
VMEM_BYTES = 22 * 1024 * 1024
ALL_VMEM_BYTES = 63 * 1024 * 1024


def dot(a, b, dims):
    return lax.dot_general(a, b, (dims, ((), ())), preferred_element_type=F32)


def aligned(start, size):
    return pl.ds(pl.multiple_of(start, size), size)


def spread(cols, first, count, width):
    rows = cols.shape[0]
    lane = lax.broadcasted_iota(jnp.int32, (rows, count * width), 1)
    out = jnp.broadcast_to(cols[:, first : first + 1], (rows, count * width))
    for h in range(1, count):
        out = jnp.where(lane >= h * width, cols[:, first + h : first + h + 1], out)
    return out


def per_head(array, h, width):
    lane = lax.broadcasted_iota(jnp.int32, array.shape, 1)
    inside = (lane >= h * width) & (lane < (h + 1) * width)
    return jnp.where(inside, array, jnp.zeros_like(array))


def split_low(value):
    high = value.astype(LOW).astype(F32)
    return high, value - high


def column_of(row, size):
    return jnp.transpose(jnp.broadcast_to(row, (128, size)))


def sigmoid(v):
    return 0.5 * jnp.tanh(0.5 * v) + 0.5


def pick(flag, a, b):
    return jnp.where(flag, a, b)


class Sizes:
    def __init__(self, blocks, width, channels, heads, states, taps, head_axis, inner):
        self.blocks = blocks
        self.width = width
        self.channels = channels
        self.heads = heads
        self.head_width = channels // heads
        self.states = states
        self.lin = channels + 2 * states
        self.taps = taps
        self.head_axis = head_axis
        self.chunk = width // head_axis
        self.rows = blocks * HALF
        self.tokens = blocks * BLOCK
        self.inner = inner


def weight_copies(sz, layer, c, h, given, dst, sems):
    ch = sz.channels
    cols = aligned(c * ch, ch)
    places = [dst.at[:, :ch], dst.at[:, ch : 2 * ch], dst.at[:, 2 * ch :]]
    own = [given[0].at[0, :, cols], given[1].at[0, :, cols], given[2].at[0]]
    return copies_for(layer, c, own, given[3:], places, sems)


def out_copies(sz, layer, c, h, given, dst, sems):
    rows = aligned((h * 2 + c) * sz.channels, sz.channels)
    return copies_for(layer, c, [given[0].at[0, rows, :]], given[1:], [dst], sems)


def copies_for(layer, c, own, sent, places, sems):
    both = []
    for flag, sources in ((c == layer, own), (c != layer, sent)):
        copies = [
            pltpu.make_async_copy(p, q, sems.at[i]) for i, (p, q) in enumerate(zip(sources, places))
        ]
        both.append((flag, copies))
    return both


def run_copies(choices, start, wait):
    for flag, copies in choices:

        @pl.when(flag)
        def _(copies=copies):
            if start:
                for copy in copies:
                    copy.start()
            if wait:
                for copy in copies:
                    copy.wait()


def put_ordered(sz, dst, c, k, b, own, other):
    for r in range(len(own)):

        @pl.when(lax.rem(k - b + len(own), len(own)) == r)
        def _(r=r):
            put_pair(dst, c, own[r][:HALF, :], other[r][:HALF, :])


def put_pair(dst, c, own, other):
    dst[aligned(c * HALF, HALF), :] = own
    dst[aligned((1 - c) * HALF, HALF), :] = other


def far_first(count):
    return [0] + list(range(count - 1, 0, -1))


def put_pieces(sz, dst, c, h, own, other):
    own, other = (dict(zip(far_first(sz.head_axis), side)) for side in (own, other))
    for d in range(sz.head_axis):
        cols = aligned((h ^ d) * sz.chunk, sz.chunk)
        dst[aligned(c * HALF, HALF), cols] = own[d]
        dst[aligned((1 - c) * HALF, HALF), cols] = other[d]


def line_of(table, at):
    line = lax.broadcasted_iota(jnp.int32, table.shape, 0)
    return jnp.sum(jnp.where(line == at, table, 0.0), axis=0, keepdims=True)


def conv_forward(sz, ext, taps):
    pre = taps[0:1] * ext[5 : 5 + BLOCK, :]
    for j in range(1, sz.taps):
        pre = pre + taps[j : j + 1] * ext[5 + j : 5 + j + BLOCK, :]
    return pre


def decay_of(sz, cols, rp, h, mask):
    rows = cols[:, h : h + 1] + rp[12 + h : 13 + h, :]
    return jnp.exp(jnp.where(mask, rows, HIDDEN))


def lower_mask():
    t = lax.broadcasted_iota(jnp.int32, (BLOCK, BLOCK), 0)
    s = lax.broadcasted_iota(jnp.int32, (BLOCK, BLOCK), 1)
    return t >= s


def forward_kernel(sz, layer, slots, sc, *refs):
    n = sz.head_axis
    sources = 2 * slots if layer == 0 else 2 * n + 2 * slots
    src, refs = refs[:sources], refs[sources:]
    if layer == 1:
        table, refs = refs[0], refs[1:]
    gains, given, halo, begin = refs[0:2], refs[2:8], refs[8], refs[9]
    refs = refs[10:]
    if layer == 1:
        ov, refs = refs[0], refs[1:]
    normed_o, gl_o, lin_o, ssd_o, inc_o, inv_o, part_o, unit_o, fin_o, sc_o, base_o = refs[:11]
    refs = refs[11:]
    if layer == 1:
        mixed_o, refs = refs[0], refs[1:]
    else:
        tables_o, refs = refs[0:2], refs[2:]
    xs, ms, wv, ext, state, sems = refs
    b = pl.program_id(0)
    c, h, k = sc[0], sc[1], sc[3]
    ch, st = sz.channels, sz.states
    copies = weight_copies(sz, layer, c, h, given, wv, sems)

    @pl.when(b == 0)
    def _():
        run_copies(copies, True, False)
        ext[0:8, :] = halo[...]
        state[...] = begin[...]
        for i in range(4):
            sc_o[i] = sc[i]

    mine = aligned(c * HALF, HALF)
    cols = aligned(h * sz.chunk, sz.chunk)
    if layer == 0:
        put_ordered(sz, xs, c, k, b, src[:slots], src[slots:])
        base_o[...] = xs[mine, cols]
        for r in range(slots):

            @pl.when(lax.rem(k - b + slots, slots) == r)
            def _(r=r):
                own = decay_table(rates_of(src[r]), c, sz.heads)
                other = decay_table(rates_of(src[slots + r]), c, sz.heads)
                tables_o[0][...] = pick(c == 0, own, other)
                tables_o[1][...] = pick(c == 0, other, own)

        rp = tables_o[0][...]
    else:
        put_pieces(sz, xs, c, h, [r[...] for r in src[:n]], [r[...] for r in src[n : 2 * n]])
        put_ordered(sz, ms, c, k, b, src[2 * n : 2 * n + slots], src[2 * n + slots :])
        base_o[...] = ms[mine, cols]
        mixed_o[...] = ms[...]
        rp = table[...]

    pv = pick(c == layer, gains[0][...], gains[1][...])
    x = xs[...].astype(F32)
    inv_in = lax.rsqrt(jnp.mean(x * x, axis=1, keepdims=True) + EPS)
    normed = (x * inv_in * pv[0:1, : sz.width]).astype(LOW)
    normed_o[...] = normed

    @pl.when(b == 0)
    def _():
        run_copies(copies, False, True)

    proj = dot(normed, wv[...], NN)
    gl = proj[:, :ch]
    gl_o[...] = gl
    lin = proj[:, ch:].astype(LOW)
    lin_o[...] = lin
    ext[8 : 8 + BLOCK, :] = lin.astype(F32)
    pre = conv_forward(sz, ext, pv[1:5, : sz.lin])
    ext[0:8, :] = ext[BLOCK : BLOCK + 8, :]
    act = (pre * sigmoid(pre)).astype(LOW)
    values, bm, cm = act[:, :ch], act[:, ch : ch + st], act[:, ch + st :]

    cols = jnp.transpose(rp)
    mask = lower_mask()
    gram = dot(cm, bm, NT)
    mixes, parts = [], []
    for i in range(sz.heads):
        mixes.append((gram * decay_of(sz, cols, rp, i, mask)).astype(LOW))
        parts.append(per_head(values, i, sz.head_width))
    intra = dot(jnp.concatenate(mixes, axis=1), jnp.concatenate(parts, axis=0), NN)

    low_state = state[...].astype(LOW)
    inc_o[0] = low_state
    ecum = spread(cols, sz.heads, sz.heads, sz.head_width)
    inter = dot(cm, low_state, NT) * ecum
    vf = values.astype(F32)
    carried = (vf * spread(cols, 2 * sz.heads, sz.heads, sz.head_width)).astype(LOW)
    local = dot(carried, bm, TN)
    for i in range(sz.heads):
        rows = slice(i * sz.head_width, (i + 1) * sz.head_width)
        total = cols[BLOCK - 1 : BLOCK, sz.heads + i : sz.heads + i + 1]
        state[rows, :] = total * state[rows, :] + local[rows]
    ssd = intra + inter + pv[6:7, :ch] * vf
    ssd_o[...] = ssd
    gated = ssd * (gl * sigmoid(gl))
    weighty = gated * pv[5:6, :ch]
    unit_o[...] = weighty.astype(LOW)

    lane = lax.broadcasted_iota(jnp.int32, (BLOCK, 128), 1)
    square = jnp.sum(gated * gated, axis=1, keepdims=True)
    if layer == 0:
        project = jnp.zeros_like(square)
    else:
        scaled_grad = dot(ms[...], ov[...], NN)
        project = jnp.sum(scaled_grad * weighty, axis=1, keepdims=True)
    stats = jnp.where(lane == 0, square, jnp.where(lane == 1, project, inv_in))
    stats = jnp.transpose(stats)
    part_o[...] = stats[0:2, :]
    inv_o[...] = stats[2:3, :]

    @pl.when(b == sz.blocks - 1)
    def _():
        fin_o[...] = state[...]


def scalar_lines(sz, lines):
    fill = [jnp.zeros((8 - sz.blocks, HALF), F32)] if sz.blocks < 8 else []
    high, low = split_low(jnp.concatenate(lines + fill, axis=0))
    table = jnp.concatenate([high, low], axis=0).astype(LOW)
    return jnp.concatenate([table] * (sz.chunk // HALF), axis=1)


def own_rows(sz, ref, which):
    blocks = [ref[aligned(b * BLOCK + which * HALF, HALF), :] for b in range(sz.blocks)]
    return jnp.concatenate(blocks, axis=0)


def project_kernel(sz, layer, deps, sc, unit_r, stats_r, *refs):
    given, refs = refs[:2], refs[2 + deps :]
    keep, send, sc_o, weights, sems = refs
    c, h = sc[0], sc[1]
    copies = out_copies(sz, layer, c, h, given, weights, sems)
    run_copies(copies, True, False)
    for i in range(4):
        sc_o[i] = sc[i]
    sides = []
    for which, out in ((c, keep), (1 - c, send)):
        sides.append((out, own_rows(sz, unit_r, which)))
        lines = [
            stats_r[0:1, aligned(b * BLOCK + which * HALF, HALF)] for b in range(sz.blocks)
        ]
        table = scalar_lines(sz, lines)
        for d in range(sz.head_axis):
            out[d, sz.rows :, :] = table
    run_copies(copies, False, True)
    for out, rows in sides:
        for d in range(sz.head_axis):
            chunk = weights[:, aligned((h ^ d) * sz.chunk, sz.chunk)]
            out[d, : sz.rows, :] = dot(rows, chunk, NN).astype(LOW)


def turn_kernel(sz, sc, *refs):
    given, given_out, refs = refs[:6], refs[6:8], refs[8:]
    wide_o, out_o, wv, ov, sems = refs[:2], refs[2:4], refs[4], refs[5], refs[6]
    for layer in range(2):
        copies = weight_copies(sz, layer, sc[0], sc[1], given, wv, sems)
        run_copies(copies, True, True)
        copies = out_copies(sz, layer, sc[0], sc[1], given_out, ov, sems)
        run_copies(copies, True, True)
        wide_o[layer][...] = jnp.transpose(wv[...])
        out_o[layer][...] = jnp.transpose(ov[...])


def out_at(out, d):
    return out[d] if isinstance(out, tuple) else out.at[d]


def lift_kernel(sz, layer, deps, sc, cat_r, normed_r, zero_gains, one_gains, small_r, *refs):
    weights, refs = refs[0], refs[1 + deps :]
    keep, send, sc_o, common_o, wide = refs[0], refs[1:-3], *refs[-3:]
    c, h = sc[0], sc[1]
    for i in range(4):
        sc_o[i] = sc[i]
    wide[...] = jnp.zeros_like(wide)
    for which, out in ((c, keep), (1 - c, send)):
        rows = own_rows(sz, cat_r, which)
        along = jnp.zeros((sz.rows, 1), F32)
        for d in range(sz.head_axis):
            cols = aligned((h ^ d) * sz.chunk, sz.chunk)
            product = dot(rows, weights[:, cols], NN)
            out_at(out, d)[: sz.rows, :] = product.astype(LOW)
            blocks = [
                normed_r[aligned(b * BLOCK + which * HALF, HALF), cols] for b in range(sz.blocks)
            ]
            product = product * jnp.concatenate(blocks, axis=0).astype(F32)
            wide[0:1, cols] += jnp.sum(product, axis=0, keepdims=True)
            along = along + jnp.sum(product, axis=1, keepdims=True)
        lines = [
            jnp.transpose(jnp.broadcast_to(along[b * HALF : (b + 1) * HALF], (HALF, 128)))[0:1, :]
            for b in range(sz.blocks)
        ]
        table = scalar_lines(sz, lines)
        for d in range(sz.head_axis):
            out_at(out, d)[sz.rows :, :] = table
    gain_grad = wide[0:1, :] / pick(c == layer, zero_gains[0:1, :], one_gains[0:1, :])
    flat = [small_r[j : j + 1, sz.channels :] for j in range(sz.taps)]
    flat += [gain_grad[:, q * sz.chunk : (q + 1) * sz.chunk] for q in range(sz.head_axis)]
    high, low = split_low(jnp.concatenate(flat, axis=0))
    common_o[...] = jnp.concatenate([high, low], axis=0).astype(LOW)


def backward_kernel(sz, layer, deps, sc, *refs):
    n = sz.head_axis
    sources = 2 * n + 2 if layer == 0 else 1 + n
    src, refs = refs[:sources], refs[sources:]
    gl_r, lin_r, ssd_r, inc_r = refs[:4]
    table, gains, ov = refs[4], refs[5:7], refs[7]
    halo, halo_grad, begin = refs[8:11]
    refs = refs[11 + deps :]
    cat_o, scaled_o, small_o, sums_o, fin_o, rim_o, sc_o = refs[:7]
    refs = refs[7:]
    if layer == 0:
        mixed_o, refs = refs[0], refs[1:]
    ms, ext, back, state, heads_p, small = refs
    i_step = pl.program_id(0)
    b = sz.blocks - 1 - i_step
    c, h = sc[0], sc[1]
    ch, st = sz.channels, sz.states
    pv = pick(c == layer, gains[0][...], gains[1][...])
    rp = table[...]

    @pl.when(i_step == 0)
    def _():
        back[BLOCK : BLOCK + 8, :] = halo_grad[...]
        state[...] = begin[...]
        small[...] = jnp.zeros_like(small)
        for i in range(4):
            sc_o[i] = sc[i]
        if layer == 0:
            for i in range(2):
                extra = src[i * n][sz.rows :, :].astype(F32)
                for d in range(1, n):
                    extra = extra + src[i * n + d][sz.rows :, :].astype(F32)
                heads_p[8 * i : 8 * i + 8, :] = extra[0:8, :HALF] + extra[8:16, :HALF]

    if layer == 0:
        rows = aligned(b * HALF, HALF)
        put_pieces(
            sz, ms, c, h, [r[rows, :] for r in src[:n]], [r[rows, :] for r in src[n : 2 * n]]
        )
        halves = []
        for k in range(2):
            alpha = lax.rsqrt(line_of(src[2 * n + k][...], b) / sz.inner + EPS)
            beta = alpha * alpha * line_of(heads_p[...], 8 * k + b) / sz.inner
            halves.append((alpha, beta))
        alpha, beta = (
            pick(
                c == 0,
                jnp.concatenate([halves[0][q], halves[1][q]], axis=1),
                jnp.concatenate([halves[1][q], halves[0][q]], axis=1),
            )
            for q in range(2)
        )
    else:
        stats = src[1][...]
        for d in range(1, n):
            stats = stats + src[1 + d][...]
        alpha = lax.rsqrt(stats[0:1, :] / sz.inner + EPS)
        beta = alpha * alpha * alpha * stats[1:2, :] / sz.inner

    sub = lax.broadcasted_iota(jnp.int32, rp.shape, 0)
    cols = jnp.transpose(jnp.where(sub == 12, alpha, jnp.where(sub == 13, beta, rp)))
    alpha, beta = cols[:, 12:13], cols[:, 13:14]

    gl = gl_r[...]
    ssd = ssd_r[...]
    sig = sigmoid(gl)
    swish = gl * sig
    slope = sig * (1.0 + gl * (1.0 - sig))
    gated = ssd * swish
    if layer == 0:
        mixed_grad = ms[...]
        mixed_o[...] = mixed_grad
    else:
        mixed_grad = src[0][...]
    scaled_grad = dot(mixed_grad, ov[...], NN)
    gain = pv[5:6, :ch]
    normal = gated * alpha
    small[4:5, :ch] += jnp.sum(scaled_grad * normal, axis=0, keepdims=True)
    scaled_o[...] = (normal * gain).astype(LOW)
    gated_grad = alpha * (scaled_grad * gain) - beta * gated
    ssd_grad = (gated_grad * swish).astype(LOW)
    gate_grad = (gated_grad * ssd * slope).astype(LOW)
    sgf = ssd_grad.astype(F32)

    before = lin_r[pl.ds(pl.multiple_of(jnp.maximum(b * BLOCK - 16, 0), 16), 16), :]
    ext[0:8, :] = pick(b > 0, before.astype(F32)[8:16, :], halo[...])
    ext[8 : 8 + BLOCK, :] = lin_r[aligned(b * BLOCK, BLOCK), :].astype(F32)
    taps = pv[1:5, : sz.lin]
    pre = conv_forward(sz, ext, taps)
    psig = sigmoid(pre)
    pact = pre * psig
    pslope = psig * (1.0 + pre * (1.0 - psig))
    act = pact.astype(LOW)
    values, bm, cm = act[:, :ch], act[:, ch : ch + st], act[:, ch + st :]
    vf = values.astype(F32)
    small[5:6, :ch] += jnp.sum(sgf * vf, axis=0, keepdims=True)

    mask = lower_mask()
    gram = dot(cm, bm, NT)
    gram_grad = jnp.zeros((BLOCK, BLOCK), F32)
    mixes, parts = [], []
    for i in range(sz.heads):
        decay = decay_of(sz, cols, rp, i, mask)
        mixes.append((gram * decay).astype(LOW))
        parts.append(per_head(ssd_grad, i, sz.head_width))
        gram_grad = gram_grad + dot(parts[-1], values, NT) * decay
    intra_grad = dot(jnp.concatenate(mixes, axis=0), jnp.concatenate(parts, axis=0), TN)

    ecum = spread(cols, sz.heads, sz.heads, sz.head_width)
    to_end = spread(cols, 2 * sz.heads, sz.heads, sz.head_width)
    inter_grad = (sgf * ecum).astype(LOW)
    low_state = state[...].astype(LOW)
    carried = (vf * to_end).astype(LOW)
    carried_grad = dot(bm, low_state, NT)
    gram_low = gram_grad.astype(LOW)
    b_grad = dot(gram_low, cm, TN) + dot(carried, low_state, NN)
    c_grad = dot(gram_low, bm, NN) + dot(inter_grad, inc_r[0], NN)
    value_grad = intra_grad + pv[6:7, :ch] * sgf + carried_grad * to_end
    entry = dot(inter_grad, cm, TN)
    for i in range(sz.heads):
        rows = slice(i * sz.head_width, (i + 1) * sz.head_width)
        total = cols[BLOCK - 1 : BLOCK, sz.heads + i : sz.heads + i + 1]
        state[rows, :] = total * state[rows, :] + entry[rows]

    pre_grad = jnp.concatenate([value_grad, b_grad, c_grad], axis=1) * pslope
    back[0:BLOCK, :] = pre_grad
    lin_grad = taps[0:1] * back[sz.taps - 1 : sz.taps - 1 + BLOCK, :]
    for j in range(1, sz.taps):
        at = sz.taps - 1 - j
        lin_grad = lin_grad + taps[j : j + 1] * back[at : at + BLOCK, :]
    for j in range(sz.taps):
        small[j : j + 1, :] += jnp.sum(pre_grad * ext[5 + j : 5 + j + BLOCK, :], axis=0, keepdims=True)
    back[BLOCK : BLOCK + 8, :] = back[0:8, :]
    cat_o[...] = jnp.concatenate([gate_grad, lin_grad.astype(LOW)], axis=1)

    @pl.when(i_step == sz.blocks - 1)
    def _():
        fin_o[...] = state[...]
        rim_o[...] = back[0:8, :]
        sums = small[...]
        flat = [sums[j : j + 1, :ch] for j in range(sz.taps + 2)]
        flat = [jnp.concatenate(flat[j : j + 3], axis=1) for j in range(0, len(flat), 3)]
        flat = flat + [jnp.zeros_like(flat[0])] * (4 - len(flat))
        high, low = split_low(jnp.concatenate(flat, axis=0))
        rest = jnp.zeros((PAD - 8, high.shape[1]), F32)
        small_o[...] = jnp.concatenate([high, low, rest], axis=0).astype(LOW)
        sums_o[...] = sums


def weights_kernel(sz, seq, deps, with_common, sc, normed, cat, mixed, scaled, small, *refs):
    if with_common:
        common, refs = refs[0], refs[1:]
    refs = refs[deps:]
    sc_o, outs, heads, full, wide = refs[0], refs[1 : seq + 1], refs[seq + 1 : -2], refs[-2], refs[-1]
    for i in range(4):
        sc_o[i] = sc[i]
    ch, st = sz.channels, sz.states
    step = sz.chunk
    for q in range(sz.head_axis):
        at = slice(q * step, (q + 1) * step)
        grads = dot(normed[:, at], cat[...], TN)
        full[at, : 2 * ch] = grads[:, : 2 * ch].astype(LOW)
        wide[at, :] = grads[:, 2 * ch :]
        full[at, 2 * ch :] = dot(mixed[:, at], scaled[...], TN).astype(LOW)
    rows = sz.width // seq
    part = rows // sz.head_axis
    for r, out in enumerate(outs):
        out[:rows, :] = full[aligned(lax.rem(sc[2] + r, seq) * rows, rows), :]
        out[rows:, :] = small[...]
    for d, out in enumerate(heads):
        lines = [
            wide[aligned(lax.rem(sc[2] + r, seq) * rows + (sc[1] ^ d) * part, part), :]
            for r in range(seq)
        ]
        if with_common:
            lines = [common[...].astype(F32)] + lines
        out[...] = jnp.concatenate(lines, axis=0).astype(LOW)


def resplit(extra):
    half = extra.shape[0] // 2
    high, low = split_low(extra[:half, :] + extra[half:, :])
    return jnp.concatenate([high, low], axis=0)


def join_kernel(sz, parts, riders, deps, sc, keep, *refs):
    n = sz.head_axis
    recv, refs = refs[0] if parts == 1 else refs[:parts], refs[parts:]
    more = [(refs[i * (n + 1)], refs[i * (n + 1) + 1 : (i + 1) * (n + 1)]) for i in range(riders)]
    refs = refs[riders * (n + 1) + deps :]
    sc_o, outs = refs[0], refs[1:]
    rows = sz.rows
    for i in range(4):
        sc_o[i] = sc[i]
    extra = resplit(keep[0, rows:, :].astype(F32) + out_at(recv, 0)[rows:, :].astype(F32))
    for d, out in enumerate(outs):
        both = keep[d, :rows, :].astype(F32) + out_at(recv, d)[:rows, :].astype(F32)
        out[:rows, :] = both.astype(out.dtype)
        out[rows : rows + PAD, :] = extra.astype(out.dtype)
        at = rows + PAD
        for common, rider in more:
            size = rider[d].shape[0]
            out[at : at + PAD, :] = common[...].astype(out.dtype)
            out[at + PAD : at + PAD + size, :] = rider[d][...].astype(out.dtype)
            at += PAD + size


def total_of(parts, rows):
    total = parts[0][rows, :].astype(F32)
    for p in parts[1:]:
        total = total + p[rows, :].astype(F32)
    return total


def output_kernel(sz, layer, sc, *refs):
    n = sz.head_axis
    parts, refs = refs[:n], refs[n:]
    resid = refs[0]
    res_o, low_o, mixed_o, square_o, sc_o = refs[-5:]
    for i in range(4):
        sc_o[i] = sc[i]
    extra = total_of(parts, slice(sz.rows, sz.rows + PAD))
    square = extra[0:8, :HALF] + extra[8:16, :HALF]
    square_o[...] = square
    inv = lax.rsqrt(square / sz.inner + EPS)
    for b in range(sz.blocks):
        rows = slice(b * HALF, (b + 1) * HALF)
        col = column_of(inv[b : b + 1, :], HALF)[:, 0:1]
        mixed = total_of(parts, rows) * col
        res = resid[rows, :].astype(F32) + mixed
        res_o[rows, :] = res
        low_o[rows, :] = res.astype(LOW)
        mixed_o[rows, :] = mixed


def input_kernel(sz, layer, sc, *refs):
    n = sz.head_axis
    parts, refs = refs[:n], refs[n:]
    resid, outg, inv_r, gains = refs[0], refs[1], refs[2], refs[3:5]
    refs = refs[5:]
    if layer == 1:
        mixed = refs[0]
        grad_o, low_o, sc_o = refs[-3:]
    else:
        one_low, one_heads = refs[0], refs[1 : 1 + n]
        low_o, swap_o, shared_o, sc_o = refs[-4:]
    for i in range(4):
        sc_o[i] = sc[i]
    c, h = sc[0], sc[1]
    first = c == 0
    mine = aligned(h * sz.chunk, sz.chunk)
    gain = pick(c == layer, gains[0][0:1, mine], gains[1][0:1, mine])
    extra = total_of(parts, slice(sz.rows, sz.rows + PAD))
    along = extra[0:8, :HALF] + extra[8:16, :HALF]
    tops, lows = [], []
    for b in range(sz.blocks):
        rows = slice(b * HALF, (b + 1) * HALF)
        at = b * BLOCK
        inv_row = pick(c == 0, inv_r[:, at : at + HALF], inv_r[:, at + HALF : at + BLOCK])
        inv = column_of(inv_row, HALF)[:, 0:1]
        share = column_of(along[b : b + 1, :] / sz.width, HALF)[:, 0:1]
        total = total_of(parts, rows)
        base = resid[rows, :].astype(F32)
        grad = outg[rows, :].astype(F32) + inv * (total * gain - base * (inv * share))
        low = grad.astype(LOW)
        low_o[rows, :] = low
        if layer == 0:
            swap_o[rows, :] = pick(first, one_low[rows, :], low)
        else:
            grad_o[rows, :] = grad
            dots = jnp.sum(low.astype(F32) * mixed[rows, :], axis=1, keepdims=True)
            row = jnp.transpose(jnp.broadcast_to(dots, (HALF, 128)))[0:1, :]
            high, rest = split_low(row)
            tops.append(high)
            lows.append(rest)
    if layer == 1:
        fill = [jnp.zeros((8 - sz.blocks, HALF), F32)] if sz.blocks < 8 else []
        extra = jnp.concatenate(tops + fill + lows + fill, axis=0)
        extra = jnp.concatenate([extra] * (sz.chunk // HALF), axis=1)
        low_o[sz.rows :, :] = extra.astype(LOW)
    else:
        size = shared_o.shape[0]
        at = sz.rows + PAD
        zero = total_of(parts, slice(at, at + size))
        one = total_of(one_heads, slice(None))
        zero, one = (jnp.concatenate([resplit(v[:PAD]), v[PAD:]], axis=0) for v in (zero, one))
        shared_o[...] = pick(first, zero, one)
        swap_o[sz.rows :, :] = pick(first, one, zero).astype(LOW)


def sum_kernel(sz, last, deps, sc, *refs):
    refs = refs[deps:]
    if last:
        parts, done, outs = refs[:-3], refs[-3], refs[-2:]
    else:
        parts, outs = refs[:-1], refs[-1:]
    rows = outs[0].shape[0] - PAD
    total = total_of(parts, slice(None))
    extra = total[rows:]
    high, low = split_low(extra[0:4, :] + extra[4:8, :])
    extra = jnp.concatenate([high, low, jnp.zeros((PAD - 8, extra.shape[1]), F32)], axis=0)
    sums = jnp.concatenate([total[:rows], extra], axis=0).astype(LOW)
    if last:
        outs[0][...] = pick(sc[0] == 0, sums, done[...])
        outs[1][...] = pick(sc[0] == 0, done[...], sums)
    else:
        outs[0][...] = sums


def final_kernel(sz, seq, sc, own, got, *refs):
    pieces, refs = refs[:-9], refs[-9:]
    gate_o, inner_o, out_o, conv_o, norm_o, skip_o, shared_o, taps_o, gain_o = refs
    c = sc[0]
    ch = sz.channels
    rows = own.shape[0] - PAD
    lane = lax.broadcasted_iota(jnp.int32, skip_o.shape, 1)
    skip = jnp.zeros(skip_o.shape, F32)
    for i in range(2):
        which = pick(i == 0, c, 1 - c)
        to = aligned(which * ch, ch)
        sums = (own if i == 0 else got)[...].astype(F32)
        gate_o[:, to] = sums[:rows, :ch]
        inner_o[:, to] = sums[:rows, ch : 2 * ch]
        out_o[to, :] = jnp.transpose(sums[:rows, 2 * ch :])
        lines = sums[rows : rows + 4, :] + sums[rows + 4 : rows + 8, :]
        for j in range(sz.taps):
            conv_o[j : j + 1, to] = lines[j // 3 : j // 3 + 1, (j % 3) * ch : (j % 3 + 1) * ch]
        norm_o[:, to] = lines[1:2, ch : 2 * ch]
        skips = lines[1:2, 2 * ch :]
        for q in range(sz.heads):
            part = jnp.sum(per_head(skips, q, sz.head_width), axis=1, keepdims=True)
            skip = jnp.where(lane == which * sz.heads + q, part, skip)
    skip_o[...] = skip
    total = total_of(pieces, slice(BLOCK, None))
    shared_o[...] = total[PAD:]
    common = total[: PAD // 2] + total[PAD // 2 : PAD]
    place = sc[2] * sz.head_axis + sc[1]
    span = common.shape[1]
    size = span // (seq * sz.head_axis)
    turned = pltpu.roll(common, lax.rem(span - place * size, span), 1)
    taps_o[...] = turned[: sz.taps, :size]
    size = sz.width // (seq * sz.head_axis)
    at = place * size
    line = jnp.broadcast_to(line_of(common, sz.taps + at // span), common.shape)
    turned = pltpu.roll(line, lax.rem(span - lax.rem(at, span), span), 1)
    gain_o[...] = turned[:1, :size]


def slice_kernel(sz, slots, sc, order, tokens, rates, *refs):
    outs, sc_o, sems = refs[:slots], refs[slots], refs[slots + 1]
    copies = []
    for r in range(slots):
        rows = tokens.at[order[lax.rem(sc[3] + r, slots)], aligned(sc[0] * HALF, HALF), :]
        copies.append(pltpu.make_async_copy(rows, outs[r].at[:HALF], sems.at[r]))
    for copy in copies:
        copy.start()
    for i in range(4):
        sc_o[i] = sc[i]
    for r in range(slots):
        first, rest = split_low(rates[0, order[lax.rem(sc[3] + r, slots)]])
        second, rest = split_low(rest)
        lines = jnp.concatenate([first, second, rest, jnp.zeros_like(rest)], axis=1)
        lines = jnp.concatenate([lines, jnp.zeros_like(lines)], axis=0)
        outs[r][HALF:, :] = lines.astype(LOW)
    for copy in copies:
        copy.wait()


def rates_of(piece):
    lines = piece[HALF:, :].astype(F32)[:8, :]
    return (lines[:, :BLOCK] + lines[:, BLOCK : 2 * BLOCK]) + lines[:, 2 * BLOCK : 3 * BLOCK]


def pack_kernel(sz, sc, order, grads, gate, inner, out, in_gain, conv_i, conv_s, skip, norm, *refs):
    gate_o, inner_o, o_o, mine_o, send_o, sems = *refs[:5], refs[-1]
    c, h = sc[0], sc[1]
    ch = sz.channels
    outs = refs[5:-1]
    slices = []
    for r, to in enumerate(outs):
        rows = grads.at[order[lax.rem(sc[3] + r, len(outs))], aligned(c * HALF, HALF), :]
        slices.append(pltpu.make_async_copy(rows, to, sems.at[3 + r]))
    cols = aligned((1 - c) * ch, ch)
    rows = aligned((h * 2 + 1 - c) * ch, ch)
    copies = [
        pltpu.make_async_copy(gate.at[0, :, cols], gate_o, sems.at[0]),
        pltpu.make_async_copy(inner.at[0, :, cols], inner_o, sems.at[1]),
        pltpu.make_async_copy(out.at[0, rows, :], o_o, sems.at[2]),
        *slices,
    ]
    for copy in copies:
        copy.start()
    for which, ref in ((c, mine_o), (1 - c, send_o)):
        at = aligned(which * ch, ch)
        ref[...] = jnp.zeros_like(ref)
        ref[0:1, :] = in_gain[...]
        ref[1 : 1 + sz.taps, :ch] = conv_i[0, :, at]
        ref[1 : 1 + sz.taps, ch : sz.lin] = conv_s[0]
        ref[5:6, :ch] = norm[:, at]
        low = spread(skip[...], 0, sz.heads, sz.head_width)
        high = spread(skip[...], sz.heads, sz.heads, sz.head_width)
        ref[6:7, :ch] = pick(which == 0, low, high)
    for copy in copies:
        copy.wait()


def decay_table(rate, c, n):
    lane = lax.broadcasted_iota(jnp.int32, rate.shape, 1)
    cum = rate
    step = 1
    while step < BLOCK:
        cum = cum + jnp.where(lane >= step, pltpu.roll(cum, step, 1), 0.0)
        step *= 2
    end = cum[:, BLOCK - 1 :]
    lines = [cum, jnp.exp(cum), jnp.exp(end - cum) * -rate, jnp.log(-rate) - cum]
    low = jnp.concatenate([v[:n] for v in lines], axis=0)
    high = jnp.concatenate([v[n:] for v in lines], axis=0)
    return pick(c == 0, low, high)


def leave_kernel(sz, slots, riders, sc, zero_own, zero_other, one_own, one_other, *refs):
    c = sc[0]
    if riders:
        shared, refs = refs[0], refs[1:]
        total = shared[...] + one_other[sz.rows :, :].astype(F32)
        extra = resplit(total[:PAD])
        part = (total.shape[0] - PAD) // riders
    outs = refs[:slots]
    for i in range(4):
        refs[slots][i] = sc[i]
    for r in range(slots):
        rows = aligned(lax.rem(sc[3] + r, slots) * HALF, HALF)
        own = pick(c == 0, zero_own[rows, :], one_own[rows, :])
        other = pick(c == 0, zero_other[rows, :], one_other[rows, :])
        put_pair(outs[r], c, own, other)
        if riders:
            lines = [extra, total[PAD + r * part : PAD + (r + 1) * part]]
            outs[r][BLOCK:, :] = jnp.concatenate(lines, axis=0).astype(LOW)


def home_kernel(slots, sc, *refs):
    early, late, out, grad = refs[:slots], refs[slots : 2 * slots], refs[-3], refs[-2]
    for i in range(4):
        refs[-1][i] = sc[i]
    first = sc[0] == 0
    for r in range(slots):
        at = lax.rem(sc[3] - r + slots, slots)
        out[at] = pick(first, early[r][...], late[r][:BLOCK, :]).astype(F32)
        grad[at] = pick(first, late[r][:BLOCK, :], early[r][...]).astype(F32)


def whole(shape):
    return pl.BlockSpec(shape, lambda *_: (0,) * len(shape))


def per_device(
    tokens,
    slot_order,
    log_decay,
    grad_out,
    in_gain,
    w_gate,
    w_inner,
    w_shared,
    conv_inner,
    conv_shared,
    d_skip,
    norm_gain,
    w_out,
):
    slots = tokens.shape[0]
    span = tokens.shape[1]
    width = tokens.shape[2]
    seq = lax.axis_size("seq")
    head_axis = lax.axis_size("head")
    cores = lax.axis_size("section")
    spans = seq // slots
    c = lax.axis_index("section")
    z = lax.axis_index("seq")
    h = lax.axis_index("head")
    k = lax.rem(z, slots)
    inner_dev = w_gate.shape[2]
    channels = inner_dev // cores
    shared = w_shared.shape[2]
    heads_dev = d_skip.shape[1]
    taps = conv_inner.shape[1]
    sz = Sizes(
        slots * span // BLOCK,
        width,
        channels,
        heads_dev // cores,
        shared // 2,
        taps,
        head_axis,
        inner_dev * head_axis,
    )
    first = c == 0
    swap = [(0, 1), (1, 0)]
    nb, tok, rows, chunk = sz.blocks, sz.tokens, sz.rows, sz.chunk

    def cross(x):
        return lax.ppermute(x, "section", swap)

    def turn(x, r):
        pairs = [(i, i // slots * slots + (i % slots + r) % slots) for i in range(seq)]
        return lax.ppermute(x, "seq", pairs) if r else x

    def over_heads(x, d):
        return x if d == 0 else lax.ppermute(x, "head", [(i, i ^ d) for i in range(head_axis)])

    def next_span(x, way):
        pairs = [(i, i + way * slots) for i in range(seq) if 0 <= i + way * slots < seq]
        return lax.ppermute(x, "seq", pairs)

    def shape(dims, dtype):
        return jax.ShapeDtypeStruct(dims, dtype)

    prefetch = functools.partial(pltpu.PrefetchScalarGridSpec, num_scalar_prefetch=1)
    options = pltpu.CompilerParams(vmem_limit_bytes=VMEM_BYTES)
    from_hbm = pltpu.CompilerParams(vmem_limit_bytes=ALL_VMEM_BYTES)
    anywhere = pl.BlockSpec(memory_space=pl.ANY)
    smem = pl.BlockSpec(memory_space=pltpu.SMEM)
    vmem = pl.BlockSpec(memory_space=pltpu.VMEM)
    index_shape = shape((4,), jnp.int32)

    def cost(flops, moved):
        return pl.CostEstimate(flops=int(flops), bytes_accessed=int(moved), transcendentals=0)

    def to_members(pieces):
        return [turn(x, r) for r, x in enumerate(pieces)]

    sc = jnp.stack([c, h, z, k]).astype(jnp.int32)
    *tok_slices, sc = pl.pallas_call(
        functools.partial(slice_kernel, sz, slots),
        in_specs=[smem, smem, anywhere, vmem],
        out_specs=[vmem] * slots + [smem],
        out_shape=[shape((HALF + PAD, width), LOW)] * slots + [index_shape],
        scratch_shapes=[pltpu.SemaphoreType.DMA((slots,))],
        compiler_params=from_hbm,
    )(sc, slot_order, tokens, log_decay)
    tok_pieces = to_members(tok_slices)
    tok_others = [cross(x) for x in tok_pieces]

    wide = 2 * channels + shared
    gate_sent, inner_sent, o_sent, pv_mine, pv_sent, *out_slices = pl.pallas_call(
        functools.partial(pack_kernel, sz),
        in_specs=[smem, smem] + [anywhere] * 4 + [vmem] * 5,
        out_specs=[vmem] * (5 + slots),
        out_shape=[
            shape((width, channels), LOW),
            shape((width, channels), LOW),
            shape((channels, width), LOW),
            shape((16, width), F32),
            shape((16, width), F32),
        ]
        + [shape((HALF, width), LOW)] * slots,
        scratch_shapes=[pltpu.SemaphoreType.DMA((3 + slots,))],
        compiler_params=from_hbm,
    )(
        sc, slot_order, grad_out, w_gate, w_inner, w_out,
        in_gain, conv_inner, conv_shared, d_skip, norm_gain,
    )
    sent = [cross(x) for x in (gate_sent, inner_sent, w_shared[0], o_sent)]
    gains = [pv_mine, cross(pv_sent)]

    def span_total(table):
        ends = table[: sz.heads, BLOCK - 1 :: BLOCK]
        return jnp.repeat(jnp.exp(jnp.sum(ends, axis=1)), sz.head_width)[:, None]

    parts_shape = shape((head_axis, rows + PAD, chunk), LOW)
    in_weights = [w_gate, w_inner, w_shared, *sent[:3]]
    last_weights = [w_out, sent[3]]
    wide_weights = pltpu.VMEM((width, wide), LOW)
    out_weights = pltpu.VMEM((channels, width), LOW)
    copy_sems = pltpu.SemaphoreType.DMA((4,))
    dense = 2 * tok * width * (wide + channels)

    def forward(layer, sc, sources):
        def at(b, _):
            return (b, 0)

        piece = pl.BlockSpec((HALF, chunk), at)
        table = pl.BlockSpec((16, BLOCK), lambda b, _: (0, b))
        if layer == 0:
            src_specs = [whole((HALF + PAD, width))] * (2 * slots)
            more_specs = [table, table]
            more_shapes = [shape((16, tok), F32)] * 2
        else:
            src_specs = [piece] * (2 * head_axis) + [whole((HALF, width))] * (2 * slots) + [table]
            more_specs = [pl.BlockSpec((BLOCK, width), at)]
            more_shapes = [shape((tok, width), LOW)]

        last = [] if layer == 0 else [turned[3]]

        def call(halo, begin):
            return pl.pallas_call(
                functools.partial(forward_kernel, sz, layer, slots),
                grid_spec=prefetch(
                    grid=(nb,),
                    in_specs=src_specs
                    + [whole((16, width)), whole((16, width))]
                    + [anywhere] * len(in_weights)
                    + [whole((8, sz.lin)), whole((channels, sz.states))]
                    + [whole(x.shape) for x in last],
                    out_specs=[
                        pl.BlockSpec((BLOCK, width), at),
                        pl.BlockSpec((BLOCK, channels), at),
                        pl.BlockSpec((BLOCK, sz.lin), at),
                        pl.BlockSpec((BLOCK, channels), at),
                        pl.BlockSpec((1, channels, sz.states), lambda b, _: (b, 0, 0)),
                        pl.BlockSpec((1, BLOCK), lambda b, _: (0, b)),
                        pl.BlockSpec((2, BLOCK), lambda b, _: (0, b)),
                        pl.BlockSpec((BLOCK, channels), at),
                        whole((channels, sz.states)),
                        smem,
                        piece,
                    ]
                    + more_specs,
                    scratch_shapes=[
                        pltpu.VMEM((BLOCK, width), LOW),
                        pltpu.VMEM((BLOCK, width), LOW),
                        wide_weights,
                        pltpu.VMEM((BLOCK + 8, sz.lin), F32),
                        pltpu.VMEM((channels, sz.states), F32),
                        copy_sems,
                    ],
                ),
                out_shape=[
                    shape((tok, width), LOW),
                    shape((tok, channels), F32),
                    shape((tok, sz.lin), LOW),
                    shape((tok, channels), F32),
                    shape((nb, channels, sz.states), LOW),
                    shape((1, tok), F32),
                    shape((2, tok), F32),
                    shape((tok, channels), LOW),
                    shape((channels, sz.states), F32),
                    index_shape,
                    shape((rows, chunk), LOW),
                ]
                + more_shapes,
                compiler_params=options,
                cost_estimate=cost(6 * dense, 16e6),
            )(sc, *sources, *gains, *in_weights, halo, begin, *last)

        halo = jnp.zeros((8, sz.lin), F32)
        begin = jnp.zeros((channels, sz.states), F32)
        if spans == 1:
            return call(halo, begin), halo
        trial = call(halo, begin)
        halo = next_span(trial[2][tok - 8 :].astype(F32), 1)
        local = call(halo, begin)[8]
        total = span_total(trial[11] if layer == 0 else sources[-1])
        for _ in range(spans - 1):
            begin = next_span(total * begin + local, 1)
        return call(halo, begin), halo

    def backward(layer, sc, sources, saved, decays, halo, deps):
        def at(i, _):
            return (nb - 1 - i, 0)

        if layer == 0:
            src_specs = [whole(s.shape) for s in sources]
        else:
            stat = pl.BlockSpec((2, BLOCK), lambda i, _: (0, nb - 1 - i))
            src_specs = [pl.BlockSpec((BLOCK, width), at)] + [stat] * head_axis
        gl, lin, ssd, inc = saved
        mixed_spec = [pl.BlockSpec((BLOCK, width), at)] if layer == 0 else []
        mixed_shape = [shape((tok, width), LOW)] if layer == 0 else []

        def call(halo_grad, begin):
            return pl.pallas_call(
                functools.partial(backward_kernel, sz, layer, len(deps)),
                grid_spec=prefetch(
                    grid=(nb,),
                    in_specs=src_specs
                    + [
                        pl.BlockSpec((BLOCK, channels), at),
                        whole(lin.shape),
                        pl.BlockSpec((BLOCK, channels), at),
                        pl.BlockSpec((1, channels, sz.states), lambda i, _: (nb - 1 - i, 0, 0)),
                        pl.BlockSpec((16, BLOCK), lambda i, _: (0, nb - 1 - i)),
                        whole((16, width)),
                        whole((16, width)),
                        whole((width, channels)),
                        whole((8, sz.lin)),
                        whole((8, sz.lin)),
                        whole((channels, sz.states)),
                    ]
                    + [anywhere] * len(deps),
                    out_specs=[
                        pl.BlockSpec((BLOCK, wide), at),
                        pl.BlockSpec((BLOCK, channels), at),
                        whole((PAD, 3 * channels)),
                        whole((8, sz.lin)),
                        whole((channels, sz.states)),
                        whole((8, sz.lin)),
                        smem,
                    ]
                    + mixed_spec,
                    scratch_shapes=[
                        pltpu.VMEM((BLOCK, width), LOW),
                        pltpu.VMEM((BLOCK + 8, sz.lin), F32),
                        pltpu.VMEM((BLOCK + 8, sz.lin), F32),
                        pltpu.VMEM((channels, sz.states), F32),
                        pltpu.VMEM((PAD, HALF), F32),
                        pltpu.VMEM((8, sz.lin), F32),
                    ],
                ),
                out_shape=[
                    shape((tok, wide), LOW),
                    shape((tok, channels), LOW),
                    shape((PAD, 3 * channels), LOW),
                    shape((8, sz.lin), F32),
                    shape((channels, sz.states), F32),
                    shape((8, sz.lin), F32),
                    index_shape,
                ]
                + mixed_shape,
                compiler_params=options,
                cost_estimate=cost(8 * dense, 16e6),
            )(
                sc, *sources, gl, lin, ssd, inc, decays, *gains, turned[2 + layer],
                halo, halo_grad, begin, *deps,
            )

        halo_grad = jnp.zeros((8, sz.lin), F32)
        begin = jnp.zeros((channels, sz.states), F32)
        if spans == 1:
            return call(halo_grad, begin)
        local = call(halo_grad, begin)[4]
        for _ in range(spans - 1):
            begin = next_span(span_total(decays) * begin + local, -1)
        halo_grad = next_span(call(halo_grad, begin)[5], -1)
        return call(halo_grad, begin)

    def project(layer, sc, unit, stats, deps):
        return pl.pallas_call(
            functools.partial(project_kernel, sz, layer, len(deps)),
            in_specs=[smem, vmem, vmem] + [anywhere] * (2 + len(deps)),
            out_specs=[vmem, vmem, smem],
            out_shape=[parts_shape, parts_shape, index_shape],
            scratch_shapes=[out_weights, copy_sems],
            compiler_params=options,
            cost_estimate=cost(dense / 4, 4e6),
        )(sc, unit, stats, *last_weights, *deps)

    def lift(layer, sc, cat, normed, small, deps):
        outs = pl.pallas_call(
            functools.partial(lift_kernel, sz, layer, len(deps)),
            in_specs=[smem] + [vmem] * 6 + [anywhere] * len(deps),
            out_specs=[vmem] * (1 + head_axis) + [smem, vmem],
            out_shape=[parts_shape]
            + [shape(parts_shape.shape[1:], LOW)] * head_axis
            + [index_shape, shape((PAD, chunk), LOW)],
            scratch_shapes=[pltpu.VMEM((8, width), F32)],
            compiler_params=options,
            cost_estimate=cost(dense, 8e6),
        )(sc, cat, normed, *gains, small, turned[layer], *deps)
        return outs[0], list(outs[1:-2]), outs[-2], outs[-1]

    def scatter(sc, keep, send, riders=(), deps=()):
        size = rows + PAD + sum(PAD + rider[1].shape[0] for rider in riders)
        flat = [x for rider in riders for x in rider]
        got = [cross(x) for x in (send if isinstance(send, list) else [send])]
        joined = pl.pallas_call(
            functools.partial(join_kernel, sz, len(got), len(riders), len(deps)),
            in_specs=[smem] + [vmem] * (1 + len(got) + len(flat)) + [anywhere] * len(deps),
            out_specs=[smem] + [vmem] * head_axis,
            out_shape=[index_shape, shape((size, chunk), F32)]
            + [shape((size, chunk), LOW)] * (head_axis - 1),
            compiler_params=options,
        )(sc, keep, *got, *flat, *deps)
        return [over_heads(joined[1 + d], d) for d in far_first(head_axis)], joined[0]

    def gather(low):
        own = [over_heads(low, d) for d in far_first(head_axis)]
        return own + [cross(x) for x in own]

    turned = pl.pallas_call(
        functools.partial(turn_kernel, sz),
        in_specs=[smem] + [anywhere] * 8,
        out_specs=[vmem] * 4,
        out_shape=[shape((wide, width), LOW)] * 2 + [shape((width, channels), LOW)] * 2,
        scratch_shapes=[wide_weights, out_weights, copy_sems],
        compiler_params=options,
        cost_estimate=cost(1e9, 8e6),
    )

    def section_output(layer, sc, parts, resid, deps=()):
        return pl.pallas_call(
            functools.partial(output_kernel, sz, layer),
            in_specs=[smem] + [vmem] * (head_axis + 1) + [anywhere] * len(deps),
            out_specs=[vmem] * 4 + [smem],
            out_shape=[
                shape((rows, chunk), F32),
                shape((rows, chunk), LOW),
                shape((rows, chunk), F32),
                shape((8, HALF), F32),
                index_shape,
            ],
            compiler_params=options,
        )(sc, *parts, resid, *deps)

    part = width // seq
    columns = 3 * channels
    share = part // head_axis
    shared_size = seq * share + PAD

    def section_input(layer, sc, parts, *others, deps=()):
        if layer == 0:
            outs = [
                shape((rows + PAD, chunk), LOW),
                shape((rows + shared_size, chunk), LOW),
                shape((shared_size, chunk), F32),
            ]
        else:
            outs = [shape((rows, chunk), F32), shape((rows + PAD, chunk), LOW)]
        return pl.pallas_call(
            functools.partial(input_kernel, sz, layer),
            in_specs=[smem] + [vmem] * (head_axis + len(others)) + [anywhere] * len(deps),
            out_specs=[vmem] * len(outs) + [smem],
            out_shape=outs + [index_shape],
            compiler_params=options,
        )(sc, *parts, *others, *deps)

    def weight_grads(sc, normed, cat, mixed, scaled, small, deps=(), common=None):
        more = [] if common is None else [common]
        size = seq * share + PAD * len(more)
        outs = pl.pallas_call(
            functools.partial(weights_kernel, sz, seq, len(deps), bool(more)),
            in_specs=[smem] + [vmem] * (5 + len(more)) + [anywhere] * len(deps),
            out_specs=[smem] + [vmem] * (seq + head_axis),
            out_shape=[index_shape]
            + [shape((part + PAD, columns), LOW)] * seq
            + [shape((size, shared), LOW)] * head_axis,
            scratch_shapes=[pltpu.VMEM((width, columns), LOW), pltpu.VMEM((width, shared), F32)],
            compiler_params=options,
            cost_estimate=cost(4 * dense, 12e6),
        )(sc, normed, cat, mixed, scaled, small, *more, *deps)
        return over_seq(outs[1 : 1 + seq]), outs[1 + seq :], outs[0]

    def shifted(x, r):
        return lax.ppermute(x, "seq", [(i, (i + r) % seq) for i in range(seq)]) if r else x

    def over_seq(chunks):
        return [shifted(x, r) for r, x in enumerate(chunks)]

    def leave(sc, *arrays, riders=0):
        size = BLOCK + (share + PAD if riders else 0)
        pieces = pl.pallas_call(
            functools.partial(leave_kernel, sz, slots, riders),
            in_specs=[smem] + [vmem] * len(arrays),
            out_specs=[vmem] * slots + [smem],
            out_shape=[shape((size, chunk), LOW)] * slots + [index_shape],
            compiler_params=options,
        )(sc, *arrays)
        return to_members(pieces[:slots]), pieces[slots]

    out_pieces = to_members(out_slices)
    fw0, halo0 = forward(0, sc, tok_pieces + tok_others)
    base0, decays = fw0[10], fw0[11:13]
    pr0 = project(0, fw0[9], fw0[7], fw0[6], [out_pieces[1], out_pieces[-1]])
    out_others = [cross(x) for x in out_pieces]
    parts, sc_join = scatter(sc, pr0[0], pr0[1])
    turned = turned(sc_join, *in_weights, *last_weights)
    res1, low1, mixed0, square0, unused = section_output(0, sc, parts, base0, turned)
    pieces1 = gather(low1)
    square_other = cross(square0)

    fw1, halo1 = forward(1, sc, pieces1 + out_pieces + out_others + [decays[1]])
    stat = fw1[6] + cross(fw1[6])
    stats = [stat] + [over_heads(stat, d) for d in range(1, head_axis)]
    pr1 = project(1, fw1[9], fw1[7], fw1[6], [])
    parts_out, sc_out = scatter(sc, pr1[0], pr1[1])
    bw1 = backward(1, sc_out, [fw1[11]] + stats, fw1[1:5], decays[1], halo1, [])
    lf1 = lift(1, bw1[6], bw1[0], fw1[0], bw1[3], parts_out[1:])
    weights1, heads1, sc_weights = weight_grads(
        lf1[2], fw1[0], bw1[0], fw1[11], bw1[1], bw1[2], common=lf1[3]
    )
    parts, sc_join = scatter(sc_weights, lf1[0], lf1[1])
    igrad1, glow1, sc_in = section_input(
        1, sc_join, parts, res1, fw1[10], fw1[5], *gains, mixed0,
        deps=weights1[2:-1],
    )
    piecesg = gather(glow1)

    heads1 = [over_heads(heads1[d], d) for d in far_first(head_axis)]

    early, unused = leave(sc_in, low1, pieces1[head_axis], glow1, piecesg[head_axis])
    bw0 = backward(
        0, sc, piecesg + [square0, square_other], fw0[1:5], decays[0], halo0,
        weights1[1:2],
    )
    weights0, heads0, sc_weights = weight_grads(
        bw0[6], fw0[0], bw0[0], bw0[7], bw0[1], bw0[2], deps=early[1:] + weights1[-1:],
    )
    lf0 = lift(0, sc_weights, bw0[0], fw0[0], bw0[3], heads1[1:])
    parts, sc_join = scatter(lf0[2], lf0[0], lf0[1], [[lf0[3], *heads0]], weights0[1:2])

    def summed(sc, pieces, *done, deps=()):
        return pl.pallas_call(
            functools.partial(sum_kernel, sz, bool(done), len(deps)),
            in_specs=[smem] + [anywhere] * len(deps) + [vmem] * (len(pieces) + len(done)),
            out_shape=[shape((part + PAD, columns), LOW)] * (1 + len(done)),
            compiler_params=options,
        )(sc, *deps, *pieces, *done)

    sums1 = summed(sc_in, weights1)
    unused, low2, unused_mixed, unused_square, sc_out = section_output(1, sc_in, parts_out, res1)
    glow0, to_other, shared_own, sc_end = section_input(
        0, sc_out, parts, base0, igrad1, fw0[5], *gains, low2, *heads1,
        deps=[*weights0[2:], *sums1],
    )
    got = cross(to_other)
    if spans == 1:
        late, sc_end = leave(sc_end, glow0, got, low2, got, shared_own, riders=seq)
        shared_parts = late
    else:
        late, sc_end = leave(sc_end, glow0, got, low2, got)
        total = shared_own + got[rows:].astype(F32)
        extra = resplit(total[:PAD])
        fill = jnp.zeros((BLOCK, shared), F32)
        chunks = [
            jnp.concatenate([fill, extra, total[PAD + r * share : PAD + (r + 1) * share]])
            for r in range(seq)
        ]
        shared_parts = over_seq([x.astype(LOW) for x in chunks])
    own_sums, other_sums = summed(sc_end, weights0, *sums1)
    final = pl.pallas_call(
        functools.partial(final_kernel, sz, seq),
        in_specs=[smem] + [vmem] * (2 + seq),
        out_shape=[
            shape((part, inner_dev), F32),
            shape((part, inner_dev), F32),
            shape((inner_dev, part), F32),
            shape((taps, inner_dev), F32),
            shape((1, inner_dev), F32),
            shape((1, heads_dev), F32),
            shape((share, shared), F32),
            shape((taps, shared // (seq * head_axis)), F32),
            shape((1, width // (seq * head_axis)), F32),
        ],
        compiler_params=options,
    )(sc, own_sums, cross(other_sums), *shared_parts)
    section_out, input_grad, unused = pl.pallas_call(
        functools.partial(home_kernel, slots),
        in_specs=[smem] + [vmem] * (2 * slots),
        out_specs=[vmem, vmem, smem],
        out_shape=[shape((slots, BLOCK, chunk), F32)] * 2 + [index_shape],
        compiler_params=options,
    )(sc, *early, *late)

    return (
        section_out[None],
        input_grad[None],
        final[8],
        final[0][None],
        final[1][None],
        final[6][None],
        final[3][None],
        final[7][None],
        final[5],
        final[4],
        final[2][None],
    )


def solution(mesh):
    placed = (
        P(None, "seq", None),
        P(),
        P("section", None, "head", "seq"),
        P(None, "seq", None),
        P("section", None),
        P("section", None, "head"),
        P("section", None, "head"),
        P("section", None, None),
        P("section", None, "head"),
        P("section", None, None),
        P("section", "head"),
        P("section", "head"),
        P("section", None, None),
    )
    return jax.shard_map(
        per_device,
        mesh=mesh,
        in_specs=placed,
        out_specs=(
            P("section", None, "seq", "head"),
            P("section", None, "seq", "head"),
            P("section", ("seq", "head")),
            P("section", "seq", "head"),
            P("section", "seq", "head"),
            P("section", ("seq", "head"), None),
            P("section", None, "head"),
            P("section", None, ("seq", "head")),
            P("section", "head"),
            P("section", "head"),
            P("section", "head", "seq"),
        ),
        check_vma=False,
    )
```
